32 devices in a mesh: ctx: 8 (over z, y), fsdp: 4 (over x, core).
Axes of the slice: x: 2, y: 2, z: 4, core: 2. Of those that a mesh axis runs over, the one named last changes fastest.
Arguments:
- inputs: float32 [4, 2, 1024, 1024], P('fsdp', None, 'ctx'), may hold values from -6 to 6
- cotangent: float32 [4, 2, 1024, 1024], P('fsdp', None, 'ctx'), may hold values from -6 to 6
- doc_lengths: int32 [4, 4], P('fsdp'), may hold values from 4 to 1536, as said below
- routes: int32 [4, 2, 1024, 8], P('fsdp', None, 'ctx'), may hold values from 0 to 31, all different within a row
- attn_gain: bfloat16 [1024], P('fsdp'), may hold values from 0.5 to 1.5
- ffn_gain: bfloat16 [1024], P('fsdp'), may hold values from 0.5 to 1.5
- w_query: bfloat16 [1024, 1024], P('fsdp'), may hold values from -0.75 to 0.75
- key_weight: bfloat16 [1024, 512], P('fsdp'), may hold values from -0.75 to 0.75
- value_weight: bfloat16 [1024, 512], P('fsdp'), may hold values from -0.1875 to 0.1875
- w_out: bfloat16 [1024, 1024], P('fsdp'), may hold values from -12 to 12
- w_router: bfloat16 [1024, 32], P('fsdp'), may hold values from -0.095703125 to 0.095703125
- w_gate: bfloat16 [32, 1024, 512], P('fsdp'), may hold values from -0.1875 to 0.1875
- w_up: bfloat16 [32, 1024, 512], P('fsdp'), may hold values from -0.1875 to 0.1875
- w_down: bfloat16 [32, 512, 1024], P('fsdp'), may hold values from -21 to 21
Outputs:
- mixed: float32 [4, 2, 1024, 1024], P('fsdp', None, 'ctx')
- grad_inputs: float32 [4, 2, 1024, 1024], P('fsdp', None, 'ctx')
- grad_attn_gain: float32 [1024], P('fsdp')
- grad_ffn_gain: float32 [1024], P('fsdp')
- grad_w_query: float32 [1024, 1024], P('fsdp')
- grad_w_key: float32 [1024, 512], P('fsdp')
- grad_w_value: float32 [1024, 512], P('fsdp')
- grad_w_out: float32 [1024, 1024], P('fsdp')
- grad_w_router: float32 [1024, 32], P('fsdp')
- grad_w_gate: float32 [32, 1024, 512], P('fsdp')
- grad_w_up: float32 [32, 1024, 512], P('fsdp')
- grad_w_down: float32 [32, 512, 1024], P('fsdp')
The draws below stay inside these ranges and needn't reach their ends.
Inputs may be any that keep to these rules, and one draw needn't show every extreme that they name: `doc_lengths`: each row's lengths sum to 2048; the first document of every sequence covers at least its first half. `routes`: each token names 8 different experts.
All inputs are finite; a program needn't handle non-finite values.
Results may differ from the reference program's by a relative error of at most 0.024.
Values may be sent and summed in bfloat16 or wider, within the bound.
A program may use at most 576 MiB of HBM per device.

```python
import jax
import jax.numpy as jnp
from jax import lax

MODEL_DIMENSION = 1024
QUERY_HEADS = 16
KEY_VALUE_HEADS = 8
HEAD_DIMENSION = 64
EXPERTS = 32
FF = 512
TOP = 8
SEQ = 2048
DOCS = 4
SEQS = 4
HALF = 1024
CAP = 80
N_CTX = 8


MIN_DOC = 4


def draw_doc_lengths(key, part):
    key = jax.random.fold_in(key, 11)
    first_key, pick_key, share_key = jax.random.split(key, 3)
    quarter = SEQ // 4
    surplus = jax.random.randint(first_key, (SEQS,), 0, quarter + 1)
    chosen = jax.random.randint(pick_key, (), 0, SEQS)
    picked = jnp.arange(SEQS) == chosen
    surplus = jnp.where(picked, quarter, surplus)
    leading = SEQ // 2 + surplus
    remaining = SEQ - leading
    spare = remaining - (DOCS - 1) * MIN_DOC
    shares = jax.random.randint(share_key, (SEQS, DOCS - 1), 1, 9)
    first_column = jnp.arange(DOCS - 1) == 0
    shares = jnp.where(picked[:, None] & first_column[None, :], 0, shares)
    pieces = MIN_DOC + spare[:, None] * shares // jnp.sum(shares, -1, keepdims=True)
    pieces = pieces.at[:, -1].set(remaining - jnp.sum(pieces[:, :-1], -1))
    return jnp.concatenate([leading[:, None], pieces], -1).astype(jnp.int32)


def levels(own_key, shape, cuts, low, top_value):
    def one(position, blocks):
        steps = jax.random.uniform(jax.random.fold_in(jax.random.fold_in(own_key, 6), position), (blocks,), jnp.float32, low / len(cuts), top_value / len(cuts))
        return jnp.repeat(jnp.exp(steps), shape[position] // blocks).reshape((-1,) + (1,) * (len(shape) - position - 1))

    gain = one(*cuts[0])
    for cut in cuts[1:]:
        gain = gain * one(*cut)
    return gain


def choose_distinct(rng, rows, number_of, top, lift):
    ranking = jax.random.permutation(jax.random.fold_in(rng, 1), number_of)
    pull = ranking
    for power in range(3):
        pull = pull * pull // number_of
    pull = pull * lift // number_of
    lots = jax.random.randint(jax.random.fold_in(rng, 2), (rows, number_of), 0, 4096) + pull
    fixed_rows = jax.random.permutation(jax.random.fold_in(rng, 3), rows)[jnp.arange(number_of) % rows]
    lots = jnp.where(jnp.arange(rows)[:, None] == fixed_rows[None, :], 1 << 14, lots)
    score = lots * number_of + jnp.arange(number_of)
    return lax.top_k(score.astype(jnp.int32), top)[1].astype(jnp.int32)


def centred(key, extent, spread, bound, cuts=(), held_as=jnp.bfloat16):
    array = spread * jax.random.normal(key, extent, jnp.float32)
    if cuts:
        array = array * levels(key, extent, cuts, -0.22, 0.18)
    return jnp.clip(array, -bound, bound).astype(held_as)


def setup_inputs(seed: int = 0) -> dict:
    key_list = jax.random.split(jax.random.key(seed), 15)
    return {
        "inputs": centred(key_list[0], (SEQS, 2, HALF, MODEL_DIMENSION), 1.0, 6.0, ((0, 4), (2, 8)), jnp.float32),
        "cotangent": centred(key_list[1], (SEQS, 2, HALF, MODEL_DIMENSION), 1.0, 6.0, ((0, 4), (2, 8)), jnp.float32),
        "doc_lengths": draw_doc_lengths(jax.random.fold_in(key_list[14], 71), 0),
        "routes": choose_distinct(key_list[3], SEQS * 2 * HALF, EXPERTS, TOP, 2048).reshape((SEQS, 2, HALF, TOP)),
        "attn_gain": jnp.clip(1.0 + 0.1 * jax.random.normal(key_list[4], (MODEL_DIMENSION,), jnp.float32), 0.5, 1.5).astype(jnp.bfloat16),
        "ffn_gain": jnp.clip(1.0 + 0.1 * jax.random.normal(key_list[5], (MODEL_DIMENSION,), jnp.float32), 0.5, 1.5).astype(jnp.bfloat16),
        "w_query": centred(key_list[6], (MODEL_DIMENSION, QUERY_HEADS * HEAD_DIMENSION), 0.125, 0.75, ((0, 4),)),
        "key_weight": centred(key_list[7], (MODEL_DIMENSION, KEY_VALUE_HEADS * HEAD_DIMENSION), 0.125, 0.75, ((0, 4),)),
        "value_weight": centred(key_list[8], (MODEL_DIMENSION, KEY_VALUE_HEADS * HEAD_DIMENSION), MODEL_DIMENSION ** -0.5, 0.1875, ((0, 4),)),
        "w_out": centred(key_list[9], (QUERY_HEADS * HEAD_DIMENSION, MODEL_DIMENSION), 2.0, 12.0, ((0, 4),)),
        "w_router": centred(key_list[10], (MODEL_DIMENSION, EXPERTS), 0.016, 0.095703125, ((0, 4),)),
        "w_gate": centred(key_list[11], (EXPERTS, MODEL_DIMENSION, FF), MODEL_DIMENSION ** -0.5, 0.1875, ((0, 4),)),
        "w_up": centred(key_list[12], (EXPERTS, MODEL_DIMENSION, FF), MODEL_DIMENSION ** -0.5, 0.1875, ((0, 4),)),
        "w_down": centred(key_list[13], (EXPERTS, FF, MODEL_DIMENSION), 3.5, 21.0, ((0, 4),)),
    }


ATTN_SCALE = 0.015625
RESIDUAL = 0.22
NORM_EPS = 1e-06
ROPE_BASE = 10000.0
MASKED = -1e+30
PRECISE = lax.Precision.HIGHEST

@jax.custom_vjp
def reduced_precision(v):
    return lax.optimization_barrier(v.astype(jnp.bfloat16)).astype(jnp.float32)

@jax.custom_vjp
def low_back(v):
    return v

def low_keep(v):
    return (reduced_precision(v), None)

def low_pass(kept, grad):
    return (grad,)

def back_keep(v):
    return (v, None)

def back_low(kept, grad):
    return (reduced_precision(grad),)
reduced_precision.defvjp(low_keep, low_pass)
low_back.defvjp(back_keep, back_low)

def product(matrix_one, matrix_two):
    return jnp.matmul(matrix_one, matrix_two, precision=PRECISE)

def rotation(positions, head_size):
    indices = jnp.arange(head_size // 2, dtype=jnp.float32)
    frequency = ROPE_BASE ** (-2.0 * indices / head_size)
    angles = positions.astype(jnp.float32)[:, None] * frequency[None, :]
    return (jnp.cos(angles), jnp.sin(angles))

def apply_rotary(values, cosine_table, sine_values, head_count, direction):
    shaped = values.reshape(values.shape[:-1] + (head_count, values.shape[-1] // head_count))
    middle = shaped.shape[-1] // 2
    first_half = shaped[..., :middle]
    second_half = shaped[..., middle:]
    cos_rows = cosine_table[:, None, :]
    sin_rows = direction * sine_values[:, None, :]
    turned = jnp.concatenate([first_half * cos_rows - second_half * sin_rows, second_half * cos_rows + first_half * sin_rows], -1)
    return turned.reshape(values.shape)

def normalize(values):
    return values * lax.rsqrt(lax.optimization_barrier(jnp.mean(values * values, -1, keepdims=True)) + NORM_EPS)

def softmax_rows(scores):
    peak_score = lax.optimization_barrier(jnp.max(scores, -1, keepdims=True))
    weights = jnp.exp(scores - peak_score)
    return weights / lax.optimization_barrier(jnp.sum(weights, -1, keepdims=True))

def head_attention(query_head, key_head, value_head, allowed):
    scores = low_back(jnp.einsum('rqd,sd->qrs', query_head, key_head, precision=PRECISE) * ATTN_SCALE)
    scores = jnp.where(allowed[None], scores, MASKED)
    attn_probs = softmax_rows(scores)
    return jnp.einsum('qrs,sd->rqd', reduced_precision(attn_probs), value_head, precision=PRECISE)

def reference(inputs, cotangent, doc_lengths, routes, attn_gain, ffn_gain, w_query, key_weight, value_weight, w_out, w_router, w_gate, w_up, w_down):
    sequence_count = inputs.shape[0]
    half_len = inputs.shape[2]
    model_width = inputs.shape[3]
    sequence_length = 2 * half_len
    token_count = sequence_count * sequence_length
    query_group_size = QUERY_HEADS // KEY_VALUE_HEADS
    indices = jnp.arange(half_len, dtype=jnp.int32)
    positions = jnp.concatenate([indices, sequence_length - 1 - indices])
    doc_ends = jnp.cumsum(doc_lengths, axis=-1)[:, :-1]
    doc_ids = lax.optimization_barrier(jnp.sum((positions[None, :, None] >= doc_ends[:, None, :]).astype(jnp.int32), -1))
    cosine_table, sine_values = rotation(positions, HEAD_DIMENSION)
    block_len = half_len // N_CTX
    block_count = sequence_count * N_CTX
    block_tokens = 2 * block_len
    token_ids = jnp.arange(token_count, dtype=jnp.int32).reshape(sequence_count, 2, N_CTX, block_len)
    token_ids = jnp.transpose(token_ids, (0, 2, 1, 3)).reshape(block_count, block_tokens)
    block_routes = jnp.transpose(routes.reshape(sequence_count, 2, N_CTX, block_len, TOP), (0, 2, 1, 3, 4)).reshape(block_count, block_tokens, TOP)
    choose = (block_routes[..., None] == jnp.arange(EXPERTS, dtype=jnp.int32)).astype(jnp.int32)
    ordered = jnp.transpose(choose, (0, 2, 1, 3)).reshape(block_count, TOP * block_tokens, EXPERTS)
    before = jnp.cumsum(ordered, axis=1) - ordered
    slot_index = jnp.transpose(lax.optimization_barrier(jnp.sum(before * ordered, -1)).reshape(block_count, TOP, block_tokens), (0, 2, 1))
    target = jnp.where(slot_index < CAP, block_routes * CAP + slot_index, EXPERTS * CAP)
    sources = jnp.repeat(token_ids, TOP, axis=1)

    def fill_table(places, entries):
        return jnp.full((EXPERTS * CAP,), token_count, jnp.int32).at[places].set(entries, mode='drop')
    token_table = jax.vmap(fill_table)(target.reshape(block_count, -1), sources)
    token_table = jnp.transpose(token_table.reshape(block_count, EXPERTS, CAP), (1, 0, 2)).reshape(EXPERTS, block_count * CAP)
    expert_ids = jnp.arange(EXPERTS, dtype=jnp.int32)[:, None]

    def attend_sequence(pieces):
        query_matrix_rows, key_matrix_rows, value_matrix_rows, doc_row = pieces
        allowed = (positions[None, :] <= positions[:, None]) & (doc_row[None, :] == doc_row[:, None])
        query_head_rows = jnp.transpose(query_matrix_rows.reshape(sequence_length, KEY_VALUE_HEADS, query_group_size, HEAD_DIMENSION), (1, 0, 2, 3))
        key_head_rows = jnp.transpose(key_matrix_rows.reshape(sequence_length, KEY_VALUE_HEADS, HEAD_DIMENSION), (1, 0, 2))
        value_head_rows = jnp.transpose(value_matrix_rows.reshape(sequence_length, KEY_VALUE_HEADS, HEAD_DIMENSION), (1, 0, 2))

        def one_head(head_pieces):
            return head_attention(head_pieces[0], head_pieces[1], head_pieces[2], allowed)
        attended = lax.map(jax.checkpoint(one_head), (query_head_rows, key_head_rows, value_head_rows))
        return jnp.transpose(attended, (1, 0, 2, 3)).reshape(sequence_length, QUERY_HEADS * HEAD_DIMENSION)

    def forward(inputs_f, attn_gain_f, ffn_gain_f, query_w, key_w, value_w, out_w, router_w, gate_w, up_w, down_w):
        flat_in = inputs_f.reshape(token_count, model_width)
        h_attn = reduced_precision(normalize(flat_in) * attn_gain_f)
        q_pre = low_back(product(h_attn, query_w))
        key_unrotated = low_back(product(h_attn, key_w))
        value_all = reduced_precision(low_back(product(h_attn, value_w)))
        query_rot = reduced_precision(apply_rotary(q_pre.reshape(sequence_count, sequence_length, -1), cosine_table, sine_values, QUERY_HEADS, 1.0))
        key_rotated = reduced_precision(apply_rotary(key_unrotated.reshape(sequence_count, sequence_length, -1), cosine_table, sine_values, KEY_VALUE_HEADS, 1.0))
        attended = lax.map(jax.checkpoint(attend_sequence), (query_rot, key_rotated, value_all.reshape(sequence_count, sequence_length, -1), doc_ids))
        attended = low_back(reduced_precision(attended.reshape(token_count, -1)))
        branch = low_back(product(attended, out_w))
        middle = flat_in + RESIDUAL * branch
        h_ffn = reduced_precision(normalize(middle) * ffn_gain_f)
        logits = low_back(product(h_ffn, router_w))
        router = softmax_rows(logits)
        router_pad = jnp.concatenate([router, jnp.zeros((1, EXPERTS), router.dtype)], 0)
        slot_gate = router_pad[token_table, expert_ids]

        def one_expert(pieces):
            row_ids, slot_gates, gate_matrix, up_matrix, down_matrix = pieces
            rows_in = low_back(jnp.take(h_ffn, row_ids, axis=0, mode='fill', fill_value=0.0))
            pre_gate = low_back(product(rows_in, gate_matrix))
            pre_up = low_back(product(rows_in, up_matrix))
            hidden = reduced_precision(jax.nn.silu(pre_gate) * pre_up)
            expert_out = reduced_precision(low_back(product(hidden, down_matrix)))
            return slot_gates[:, None] * expert_out
        weighted = lax.map(jax.checkpoint(one_expert), (token_table, slot_gate, gate_w, up_w, down_w))
        ffn_sum = jnp.zeros((token_count, model_width), middle.dtype).at[token_table.reshape(-1)].add(weighted.reshape(-1, model_width), mode='drop')
        return (middle + RESIDUAL * ffn_sum).reshape(inputs_f.shape)
    mixed, pullback = jax.vjp(forward, inputs.astype(jnp.float32), attn_gain.astype(jnp.float32), ffn_gain.astype(jnp.float32), w_query.astype(jnp.float32), key_weight.astype(jnp.float32), value_weight.astype(jnp.float32), w_out.astype(jnp.float32), w_router.astype(jnp.float32), w_gate.astype(jnp.float32), w_up.astype(jnp.float32), w_down.astype(jnp.float32))
    grads = pullback(cotangent.astype(jnp.float32))
    return (mixed, grads[0], grads[1], grads[2], grads[3], grads[4], grads[5], grads[6], grads[7], grads[8], grads[9], grads[10])
```

```python
import functools

import jax
import jax.numpy as jnp
import numpy as np
from jax import lax
from jax.experimental import pallas as pl
from jax.experimental.pallas import tpu as pltpu
from jax.sharding import PartitionSpec as P

QUERY_HEADS = 16
KEY_VALUE_HEADS = 8
HEAD_DIMENSION = 64
EXPERTS = 32
TOP = 8

ATTN_SCALE = 0.015625
RESIDUAL = 0.22
NORM_EPS = 1e-06
ROPE_BASE = 10000.0
MASKED = -1e30

F32 = jnp.float32
BF16 = jnp.bfloat16
MIB = 1 << 20
NT = (((1,), (1,)), ((), ()))
TN = (((0,), (0,)), ((), ()))
BLK = 256
PACK = 256


def dot(a, b, dims=None):
    if dims is None:
        return jnp.dot(a, b, preferred_element_type=F32)
    return lax.dot_general(a, b, dims, preferred_element_type=F32)


def params(limit=56, **kw):
    return pltpu.CompilerParams(vmem_limit_bytes=limit * MIB, **kw)


def cost(flops, bytes_accessed):
    return pl.CostEstimate(flops=int(flops), bytes_accessed=int(bytes_accessed), transcendentals=0)


def lane_iota(shape):
    return lax.broadcasted_iota(jnp.int32, shape, len(shape) - 1)


def row_iota(shape):
    return lax.broadcasted_iota(jnp.int32, shape, len(shape) - 2)


def rotary_table(length):
    half = length // 2
    order = np.arange(half, dtype=np.float32)
    positions = np.concatenate([order, length - 1 - order]).astype(np.float32)
    m = np.arange(HEAD_DIMENSION // 2, dtype=np.float64)
    frequency = (ROPE_BASE ** (-2.0 * m / HEAD_DIMENSION)).astype(np.float32)
    angles = (positions[:, None] * frequency[None, :]).astype(np.float64)
    cosine, sine = np.cos(angles), np.sin(angles)
    cos_head = np.concatenate([cosine, cosine], -1)
    sin_head = np.concatenate([-sine, sine], -1)
    return np.concatenate([cos_head, cos_head, sin_head, sin_head], -1).astype(np.float32)


def turn(v, table, direction):
    lanes = lane_iota(v.shape)
    cosine = jnp.concatenate([table[:, :128], table[:, :128]], -1)
    sine = jnp.concatenate([table[:, 128:], table[:, 128:]], -1)
    turned = lanes < 3 * HEAD_DIMENSION
    swapped = jnp.where(lanes % HEAD_DIMENSION < HEAD_DIMENSION // 2, pltpu.roll(v, PACK - 32, 1), pltpu.roll(v, 32, 1))
    return jnp.where(turned, v * cosine + direction * (swapped * sine), v)


def norm_parts(values):
    inv_rms = lax.rsqrt(jnp.mean(values * values, -1, keepdims=True) + NORM_EPS)
    return values * inv_rms, inv_rms


def norm_back(grad_normed, normed, inv_rms):
    return inv_rms * (grad_normed - normed * jnp.mean(grad_normed * normed, -1, keepdims=True))


def prep_kernel(cap, routes_ref, cot_ref, out_ref):
    tokens, width = cot_ref.shape
    routes = routes_ref[...]
    earlier = (lane_iota((tokens, tokens)) < row_iota((tokens, tokens))).astype(BF16)
    experts = lane_iota((tokens, 128))
    base = jnp.zeros((1, 128), F32)
    plus = jnp.zeros((tokens, 128), F32)
    for k in range(TOP):
        chosen = experts == routes[:, k : k + 1]
        ones = chosen.astype(F32)
        slot = dot(earlier, ones.astype(BF16)) + base
        plus = plus + jnp.where(chosen & (slot < cap), slot + 1.0, 0.0)
        base = base + jnp.sum(ones, 0, keepdims=True)
    out_ref[:tokens, :] = cot_ref[...].astype(BF16)
    slots = (jnp.transpose(plus) - 1.0)[:EXPERTS, :]
    out_ref[tokens:, :] = jnp.concatenate([slots, jnp.zeros((EXPERTS, width - tokens), F32)], -1).astype(BF16)


def prep(routes, cot, cap):
    tokens, width = cot.shape
    return pl.pallas_call(
        functools.partial(prep_kernel, cap),
        out_shape=jax.ShapeDtypeStruct((tokens + EXPERTS, width), BF16),
        compiler_params=params(),
        cost_estimate=cost(1e9, 2e6),
        name="prep",
    )(routes, cot)


def qkv_kernel(shard, x_ref, gain_ref, w_ref, table_ref, out_ref, h_ref):
    @pl.when(pl.program_id(0) == 0)
    def _():
        normed, _ = norm_parts(x_ref[...])
        h_ref[...] = (normed * gain_ref[...]).astype(BF16)

    total = None
    for f in range(w_ref.shape[0]):
        part = dot(h_ref[:, f * shard : (f + 1) * shard], w_ref[f, :shard, :])
        total = part if total is None else total + part
    for d in range(out_ref.shape[0]):
        out_ref[d] = turn(total[:, d * PACK : (d + 1) * PACK], table_ref[...], 1.0).astype(BF16)


def qkv(x, gain, weights, table, shard, n):
    tokens, width = x.shape
    fsdp, padded, _ = weights.shape
    return pl.pallas_call(
        functools.partial(qkv_kernel, shard),
        grid=(n // 2,),
        in_specs=[
            pl.BlockSpec((tokens, width), lambda i: (0, 0)),
            pl.BlockSpec((1, width), lambda i: (0, 0)),
            pl.BlockSpec((fsdp, padded, 2 * PACK), lambda i: (0, 0, i)),
            pl.BlockSpec((tokens, 256), lambda i: (0, 0)),
        ],
        out_specs=[
            pl.BlockSpec((2, tokens, PACK), lambda i: (i, 0, 0)),
            pl.BlockSpec((tokens, width), lambda i: (0, 0)),
        ],
        out_shape=[
            jax.ShapeDtypeStruct((n, tokens, PACK), BF16),
            jax.ShapeDtypeStruct((tokens, width), BF16),
        ],
        compiler_params=params(),
        cost_estimate=cost(2 * tokens * width * n * PACK, 8e6),
        name="qkv",
    )(x, gain, weights, table)


def pair_keys(kv):
    other = pltpu.roll(kv, 64, 1)
    low = lane_iota(kv.shape) < 64
    return jnp.where(low, kv, other), jnp.where(low, other, kv)


def stack_heads(q):
    low = lane_iota(q.shape) < 64
    zero = jnp.zeros_like(q)
    return jnp.concatenate([jnp.where(low, q, zero), jnp.where(low, zero, q)], 0)


def fold_heads(stacked):
    rows = stacked.shape[0] // 2
    return jnp.where(lane_iota((rows, 128)) < 64, stacked[:rows], stacked[rows:])


def query_rows(ends_ref, block, length):
    half = length // 2
    lanes = lane_iota((1, 2 * BLK))
    index = block * BLK + jnp.where(lanes < BLK, lanes, lanes - BLK)
    position = jnp.where(index < half, index, length + half - 1 - index)
    start = jnp.zeros_like(position)
    for j in range(3):
        end = ends_ref[j]
        start = jnp.where(position >= end, jnp.maximum(start, end), start)
    return position, start


def key_position(kb, length):
    half = length // 2
    index = kb * BLK + row_iota((BLK, 1))
    return jnp.where(index < half, index, length + half - 1 - index)


def block_loop(block, per_half, body, init):
    late = block >= per_half
    inner = jnp.where(late, block - per_half, block)
    count = jnp.where(late, 2 * per_half - inner, inner + 1)

    def step(j, carry):
        kb = jnp.where(late & (j >= per_half), inner + j, j)
        return body(kb, carry)

    return lax.fori_loop(0, count, step, init)


def load_package(pack_ref, c, h):
    return pack_ref[c, h].astype(F32)


def attn_forward_kernel(length, ends_ref, q_ref, pack_ref, out_ref, lse_ref, full_ref, keys, values_t, acc):
    block = pl.program_id(0)
    half = length // 2
    n, _, rows, _ = pack_ref.shape

    @pl.when(block == 0)
    def _():
        for h in range(2):
            for c in range(n):
                kk, vv = pair_keys(pack_ref[c, h, :, 128:256].astype(F32))
                at = h * half + c * rows
                keys[at : at + rows, :] = kk.astype(BF16)
                if rows % 128 == 0:
                    values_t[:, at : at + rows] = jnp.transpose(vv).astype(BF16)
        if rows % 128 != 0:
            for h in range(2):
                for c in range(0, n, 2):
                    pair = jnp.concatenate([pack_ref[c, h, :, 128:256], pack_ref[c + 1, h, :, 128:256]], 0)
                    _, vv = pair_keys(pair.astype(F32))
                    at = h * half + c * rows
                    values_t[:, at : at + 2 * rows] = jnp.transpose(vv).astype(BF16)

    q = q_ref[...].reshape(BLK, PACK)[:, :128]
    q2 = stack_heads(q)
    position, start = query_rows(ends_ref, block, length)
    acc[...] = jnp.zeros_like(acc)

    def body(kb, carry):
        peak, total = carry
        at = pl.multiple_of(kb * BLK, BLK)
        scores = dot(keys[pl.ds(at, BLK), :], q2, NT) * ATTN_SCALE
        where = key_position(kb, length)
        scores = jnp.where((where <= position) & (where >= start), scores, MASKED)
        new_peak = jnp.maximum(peak, jnp.max(scores, 0, keepdims=True))
        weights = jnp.exp(scores - new_peak)
        fade = jnp.exp(peak - new_peak)
        total = total * fade + jnp.sum(weights, 0, keepdims=True)
        acc[...] = acc[...] * fade + dot(values_t[:, pl.ds(at, BLK)], weights.astype(BF16))
        return new_peak, total

    init = (jnp.full((1, 2 * BLK), MASKED, F32), jnp.zeros((1, 2 * BLK), F32))
    peak, total = block_loop(block, half // BLK, body, init)
    result = acc[...] / total
    full_ref[0] = result
    lse_ref[0] = peak + jnp.log(total)
    folded = fold_heads(jnp.transpose(result)).astype(BF16)
    out_ref[...] = folded.reshape(out_ref.shape)


def attn_forward(ends, packs, length):
    n, _, rows, _ = packs.shape
    blocks, per = length // BLK, BLK // rows
    per_half = blocks // 2
    tiles = lambda i, ends: (lax.rem(i, per_half), i // per_half, 0, 0)
    return pl.pallas_call(
        functools.partial(attn_forward_kernel, length),
        grid_spec=pltpu.PrefetchScalarGridSpec(
            num_scalar_prefetch=1,
            grid=(blocks,),
            in_specs=[
                pl.BlockSpec((per, 1, rows, PACK), tiles),
                pl.BlockSpec(packs.shape, lambda i, ends: (0, 0, 0, 0)),
            ],
            out_specs=[
                pl.BlockSpec((per, 1, rows, 128), tiles),
                pl.BlockSpec((1, 1, 2 * BLK), lambda i, ends: (i, 0, 0)),
                pl.BlockSpec((1, 128, 2 * BLK), lambda i, ends: (i, 0, 0)),
            ],
            scratch_shapes=[
                pltpu.VMEM((length, 128), BF16),
                pltpu.VMEM((128, length), BF16),
                pltpu.VMEM((128, 2 * BLK), F32),
            ],
        ),
        out_shape=[
            jax.ShapeDtypeStruct((n, 2, rows, 128), BF16),
            jax.ShapeDtypeStruct((blocks, 1, 2 * BLK), F32),
            jax.ShapeDtypeStruct((blocks, 128, 2 * BLK), F32),
        ],
        compiler_params=params(),
        cost_estimate=cost(1.5e10, 6e6),
        name="attn_forward",
    )(ends, packs, packs)


def attn_backward_kernel(length, ends_ref, q_ref, g_ref, pack_ref, lse_ref, full_ref, table_ref, out_ref, keys, values, keys_t, grad_q, grad_k, grad_v, acc):
    block = pl.program_id(0)
    half = length // 2
    n, _, rows, _ = pack_ref.shape

    @pl.when(block == 0)
    def _():
        for h in range(2):
            for c in range(n):
                kk, vv = pair_keys(pack_ref[c, h, :, 128:256].astype(F32))
                at = h * half + c * rows
                keys[at : at + rows, :] = kk.astype(BF16)
                values[at : at + rows, :] = vv.astype(BF16)
        for b in range(length // BLK):
            keys_t[:, b * BLK : (b + 1) * BLK] = jnp.transpose(keys[b * BLK : (b + 1) * BLK, :].astype(F32)).astype(BF16)
        grad_k[...] = jnp.zeros_like(grad_k)
        grad_v[...] = jnp.zeros_like(grad_v)

    q2 = stack_heads(q_ref[...].reshape(BLK, PACK)[:, :128])
    g2 = stack_heads(g_ref[...].reshape(BLK, 128))
    position, start = query_rows(ends_ref, block, length)
    lse = lse_ref[0]
    delta = jnp.sum(jnp.transpose(g2.astype(F32)) * full_ref[0], 0, keepdims=True)
    acc[...] = jnp.zeros_like(acc)

    def body(kb, carry):
        at = pl.multiple_of(kb * BLK, BLK)
        scores = dot(keys[pl.ds(at, BLK), :], q2, NT) * ATTN_SCALE
        where = key_position(kb, length)
        probs = jnp.where((where <= position) & (where >= start), jnp.exp(scores - lse), 0.0)
        grad_probs = dot(values[pl.ds(at, BLK), :], g2, NT)
        grad_scores = (probs * (grad_probs - delta)).astype(BF16)
        acc[...] += dot(keys_t[:, pl.ds(at, BLK)], grad_scores)
        grad_k[pl.ds(at, BLK), :] += dot(grad_scores, q2)
        grad_v[pl.ds(at, BLK), :] += dot(probs.astype(BF16), g2)
        return carry

    block_loop(block, half // BLK, body, 0)
    grad_q[pl.ds(pl.multiple_of(block * BLK, BLK), BLK), :] = fold_heads(jnp.transpose(acc[...]))

    @pl.when(block == length // BLK - 1)
    def _():
        for h in range(2):
            for c in range(n):
                at = slice(h * half + c * rows, h * half + (c + 1) * rows)
                kk = grad_k[at, :]
                vv = grad_v[at, :]
                kk = (kk + pltpu.roll(kk, 64, 1)) * ATTN_SCALE
                vv = vv + pltpu.roll(vv, 64, 1)
                both = jnp.where(lane_iota(kk.shape) < 64, kk, vv)
                package = jnp.concatenate([grad_q[at, :] * ATTN_SCALE, both], -1)
                out_ref[c, h] = turn(package, table_ref[at, :], -1.0).astype(BF16)


def attn_backward(ends, packs, grads, lse, full, table, length):
    n, _, rows, _ = packs.shape
    blocks, per = length // BLK, BLK // rows
    per_half = blocks // 2
    tiles = lambda i, ends: (lax.rem(i, per_half), i // per_half, 0, 0)
    return pl.pallas_call(
        functools.partial(attn_backward_kernel, length),
        grid_spec=pltpu.PrefetchScalarGridSpec(
            num_scalar_prefetch=1,
            grid=(blocks,),
            in_specs=[
                pl.BlockSpec((per, 1, rows, PACK), tiles),
                pl.BlockSpec((per, 1, rows, 128), tiles),
                pl.BlockSpec(packs.shape, lambda i, ends: (0, 0, 0, 0)),
                pl.BlockSpec((1, 1, 2 * BLK), lambda i, ends: (i, 0, 0)),
                pl.BlockSpec((1, 128, 2 * BLK), lambda i, ends: (i, 0, 0)),
                pl.BlockSpec(table.shape, lambda i, ends: (0, 0)),
            ],
            out_specs=pl.BlockSpec(packs.shape, lambda i, ends: (0, 0, 0, 0)),
            scratch_shapes=[
                pltpu.VMEM((length, 128), BF16),
                pltpu.VMEM((length, 128), BF16),
                pltpu.VMEM((128, length), BF16),
                pltpu.VMEM((length, 128), F32),
                pltpu.VMEM((length, 128), F32),
                pltpu.VMEM((length, 128), F32),
                pltpu.VMEM((128, 2 * BLK), F32),
            ],
        ),
        out_shape=jax.ShapeDtypeStruct(packs.shape, BF16),
        compiler_params=params(),
        cost_estimate=cost(3e10, 8e6),
        name="attn_backward",
    )(ends, packs, grads, packs, lse, full, table)


def middle_kernel(attn_ref, wo_ref, x_ref, gain_ref, middle_ref, h_ref):
    total = None
    for c in range(attn_ref.shape[0]):
        part = dot(attn_ref[c], wo_ref[c])
        total = part if total is None else total + part
    middle = x_ref[...] + RESIDUAL * total
    middle_ref[...] = middle
    normed, _ = norm_parts(middle)
    h_ref[...] = (normed * gain_ref[...]).astype(BF16)


def middle_step(attn, wo, x, gain):
    tokens, width = x.shape
    return pl.pallas_call(
        middle_kernel,
        out_shape=[jax.ShapeDtypeStruct((tokens, width), F32), jax.ShapeDtypeStruct((tokens, width), BF16)],
        compiler_params=params(),
        cost_estimate=cost(2 * tokens * width * width, 5e6),
        name="middle",
    )(attn, wo, x, gain)


def own_row(table, row):
    return jnp.sum(jnp.where(row_iota(table.shape) == row, table, 0.0), 0, keepdims=True)


def one_hot(slots, first, number, capp):
    tokens = slots.shape[1]
    order = row_iota((capp, tokens)).astype(F32)
    return [(order == own_row(slots, first + j)).astype(F32) for j in range(number)]


def gather_kernel(number, capp, first_ref, h_ref, cx_ref, wrt_ref, x_ref, g_ref, gate_ref):
    tokens = h_ref.shape[1]
    first = first_ref[0]
    h = h_ref[0]
    slots = cx_ref[0, tokens:, :tokens].astype(F32)
    logits = dot(wrt_ref[...], h, NT)[:EXPERTS, :]
    raw = jnp.exp(logits - jnp.max(logits, 0, keepdims=True))
    router = raw / jnp.sum(raw, 0, keepdims=True)
    hots = one_hot(slots, first, number, capp)
    places = jnp.concatenate(hots, 0).astype(BF16)
    rows = dot(places, h).astype(BF16)
    grads = dot(places, cx_ref[0, :tokens, :]).astype(BF16)
    for j in range(number):
        at = slice(j * capp, (j + 1) * capp)
        x_ref[j, 0] = rows[at]
        g_ref[j, 0] = grads[at]
        gate = jnp.sum(hots[j] * own_row(router, first + j), 1, keepdims=True)
        gate_ref[j, 0] = jnp.broadcast_to(gate, (capp, 128))


def gather_rows(first, hs, cxs, wrt, number, capp):
    nb, tokens, width = hs.shape
    return pl.pallas_call(
        functools.partial(gather_kernel, number, capp),
        grid_spec=pltpu.PrefetchScalarGridSpec(
            num_scalar_prefetch=1,
            grid=(nb,),
            in_specs=[
                pl.BlockSpec((1, tokens, width), lambda b, f: (b, 0, 0)),
                pl.BlockSpec((1, tokens + EXPERTS, width), lambda b, f: (b, 0, 0)),
                pl.BlockSpec(wrt.shape, lambda b, f: (0, 0)),
            ],
            out_specs=[
                pl.BlockSpec((number, 1, capp, width), lambda b, f: (0, b, 0, 0)),
                pl.BlockSpec((number, 1, capp, width), lambda b, f: (0, b, 0, 0)),
                pl.BlockSpec((number, 1, capp, 128), lambda b, f: (0, b, 0, 0)),
            ],
        ),
        out_shape=[
            jax.ShapeDtypeStruct((number, nb, capp, width), BF16),
            jax.ShapeDtypeStruct((number, nb, capp, width), BF16),
            jax.ShapeDtypeStruct((number, nb, capp, 128), F32),
        ],
        compiler_params=params(),
        cost_estimate=cost(4 * nb * number * capp * tokens * width, 2e7),
        name="gather_rows",
    )(first, hs, cxs, wrt)


def expert_kernel(base_ref, x_ref, g_ref, gate_ref, wg_ref, wu_ref, wd_ref, dwg_ref, dwu_ref, dwd_ref, out_ref, rows_ref, dg_ref, out_acc, row_acc, go_ref):
    chunk = pl.program_id(1)
    last = pl.num_programs(1) - 1
    x = x_ref[0]
    gate = gate_ref[0][:, :1]

    @pl.when(chunk == 0)
    def _():
        go_ref[...] = (gate * (RESIDUAL * g_ref[0].astype(F32))).astype(BF16)

    go = go_ref[...]
    wg, wu, wd = wg_ref[0], wu_ref[0], wd_ref[0]
    pre_gate = dot(x, wg)
    pre_up = dot(x, wu)
    sig = jax.nn.sigmoid(pre_gate)
    hidden = (pre_gate * sig * pre_up).astype(BF16)
    out_part = dot(hidden, wd)
    grad_hidden = dot(go, wd, NT)
    grad_gate = (grad_hidden * pre_up * sig * (1.0 + pre_gate * (1.0 - sig))).astype(BF16)
    grad_up = (grad_hidden * pre_gate * sig).astype(BF16)
    row_part = dot(grad_gate, wg, NT) + dot(grad_up, wu, NT)
    dwg_ref[0] = dot(x, grad_gate, TN).astype(BF16)
    dwu_ref[0] = dot(x, grad_up, TN).astype(BF16)
    dwd_ref[0] = dot(hidden, go, TN).astype(BF16)

    @pl.when(chunk == 0)
    def _():
        out_acc[...] = out_part
        row_acc[...] = row_part

    @pl.when(chunk > 0)
    def _():
        out_acc[...] += out_part
        row_acc[...] += row_part

    @pl.when(chunk == last)
    def _():
        out = out_acc[...].astype(BF16).astype(F32)
        out_ref[0] = (gate * out).astype(BF16)
        rows_ref[0] = row_acc[...].astype(BF16)
        grad = jnp.sum(RESIDUAL * g_ref[0].astype(F32) * out, 1, keepdims=True)
        dg_ref[0] = jnp.broadcast_to(grad, dg_ref.shape[1:])


def expert_step(base, xs, gs, gates, w_gate, w_up, w_down, start, number):
    _, rows, width = xs.shape
    ff = w_gate.shape[2]
    chunks = 2
    part = ff // chunks
    row = lambda e, c, b: (start + e, 0, 0)
    back = lambda e, c, b: (e, 0, 0)
    return pl.pallas_call(
        expert_kernel,
        grid_spec=pltpu.PrefetchScalarGridSpec(
            num_scalar_prefetch=1,
            grid=(number, chunks),
            in_specs=[
                pl.BlockSpec((1, rows, width), row),
                pl.BlockSpec((1, rows, width), row),
                pl.BlockSpec((1, rows, 128), row),
                pl.BlockSpec((1, width, part), lambda e, c, b: (b[0] + start + e, 0, c)),
                pl.BlockSpec((1, width, part), lambda e, c, b: (b[0] + start + e, 0, c)),
                pl.BlockSpec((1, part, width), lambda e, c, b: (b[0] + start + e, c, 0)),
            ],
            out_specs=[
                pl.BlockSpec((1, width, part), lambda e, c, b: (e, 0, c)),
                pl.BlockSpec((1, width, part), lambda e, c, b: (e, 0, c)),
                pl.BlockSpec((1, part, width), lambda e, c, b: (e, c, 0)),
                pl.BlockSpec((1, rows, width), back),
                pl.BlockSpec((1, rows, width), back),
                pl.BlockSpec((1, rows, 128), back),
            ],
            scratch_shapes=[
                pltpu.VMEM((rows, width), F32),
                pltpu.VMEM((rows, width), F32),
                pltpu.VMEM((rows, width), BF16),
            ],
        ),
        out_shape=[
            jax.ShapeDtypeStruct((number, width, ff), BF16),
            jax.ShapeDtypeStruct((number, width, ff), BF16),
            jax.ShapeDtypeStruct((number, ff, width), BF16),
            jax.ShapeDtypeStruct((number, rows, width), BF16),
            jax.ShapeDtypeStruct((number, rows, width), BF16),
            jax.ShapeDtypeStruct((number, rows, 128), F32),
        ],
        compiler_params=params(60),
        cost_estimate=cost(18 * number * rows * width * ff, 2e7),
        name="expert_step",
    )(base, xs, gs, gates, w_gate, w_up, w_down)


def combine_kernel(number, capp, first_ref, slot_ref, *refs):
    outs, rows, grads = refs[:number], refs[number : 2 * number], refs[2 * number : 3 * number]
    y_ref, gx_ref = refs[3 * number :]
    tokens = y_ref.shape[1]
    width = y_ref.shape[2]
    first = first_ref[0]
    slots = slot_ref[0][:, :tokens].astype(F32)
    hots = one_hot(slots, first, number, capp)
    places = jnp.concatenate(hots, 0).astype(BF16)
    y_ref[0] = dot(places, jnp.concatenate([r[0, 0] for r in outs], 0), TN).astype(BF16)
    gx_ref[0, :tokens] = dot(places, jnp.concatenate([r[0, 0] for r in rows], 0), TN).astype(BF16)
    extra = jnp.zeros((EXPERTS, 2 * tokens), F32)
    for j in range(number):
        grad = jnp.sum(hots[j] * grads[j][0, 0][:, :1], 0, keepdims=True)
        high = grad.astype(BF16).astype(F32)
        both = jnp.concatenate([high, grad - high], 1)
        extra = jnp.where(row_iota(extra.shape) == first + j, both, extra)
    rest = jnp.zeros((EXPERTS, width - 2 * tokens), F32)
    gx_ref[0, tokens:] = jnp.concatenate([extra, rest], 1).astype(BF16)


def combine(first, cxs, outs, rows, grads, tokens, capp):
    number = len(outs)
    nb, _, width = cxs.shape
    split = lambda a: a.reshape(1, nb, capp, a.shape[-1])
    wide = pl.BlockSpec((1, 1, capp, width), lambda b, f: (0, b, 0, 0))
    thin = pl.BlockSpec((1, 1, capp, 128), lambda b, f: (0, b, 0, 0))
    return pl.pallas_call(
        functools.partial(combine_kernel, number, capp),
        grid_spec=pltpu.PrefetchScalarGridSpec(
            num_scalar_prefetch=1,
            grid=(nb,),
            in_specs=[pl.BlockSpec((1, EXPERTS, width), lambda b, f: (b, tokens // EXPERTS, 0))]
            + [wide] * (2 * number)
            + [thin] * number,
            out_specs=[
                pl.BlockSpec((1, tokens, width), lambda b, f: (b, 0, 0)),
                pl.BlockSpec((1, tokens + EXPERTS, width), lambda b, f: (b, 0, 0)),
            ],
        ),
        out_shape=[
            jax.ShapeDtypeStruct((nb, tokens, width), BF16),
            jax.ShapeDtypeStruct((nb, tokens + EXPERTS, width), BF16),
        ],
        compiler_params=params(),
        cost_estimate=cost(4 * nb * number * capp * tokens * width, 2e7),
        name="combine",
    )(first, cxs, *[split(a) for a in outs], *[split(a) for a in rows], *[split(a) for a in grads])


def home_kernel(gx_ref, h_ref, middle_ref, cot_ref, wr_ref, wo_ref, gain_ref, attn_ref, grad_middle_ref, dwo_ref, ga_ref, dwr_ref, dgain_ref):
    tokens, width = h_ref.shape
    h = h_ref[...]
    gain = gain_ref[...]
    extra = gx_ref[tokens:, :].astype(F32)
    grad_router = extra[:, :tokens] + extra[:, tokens : 2 * tokens]
    grad_router = jnp.transpose(jnp.concatenate([grad_router, jnp.zeros((128 - EXPERTS, tokens), F32)], 0))
    logits = dot(h, wr_ref[...])
    logits = jnp.where(lane_iota(logits.shape) < EXPERTS, logits, MASKED)
    raw = jnp.exp(logits - jnp.max(logits, -1, keepdims=True))
    router = raw / jnp.sum(raw, -1, keepdims=True)
    grad_logits = (router * (grad_router - jnp.sum(router * grad_router, -1, keepdims=True))).astype(BF16)
    dwr_ref[...] = dot(h, grad_logits, TN).astype(BF16)
    grad_h = gx_ref[:tokens, :].astype(F32) + dot(grad_logits, wr_ref[...], NT)
    normed, scale = norm_parts(middle_ref[...])
    dgain_ref[...] = jnp.sum(grad_h * normed, 0, keepdims=True)
    grad_middle = cot_ref[...] + norm_back(grad_h * gain, normed, scale)
    grad_middle_ref[...] = grad_middle
    grad_branch = (RESIDUAL * grad_middle).astype(BF16)
    for c in range(attn_ref.shape[0]):
        dwo_ref[c] = dot(attn_ref[c], grad_branch, TN).astype(BF16)
        ga_ref[c] = dot(grad_branch, wo_ref[c], NT).astype(BF16)


def home_step(gx, h, middle, cot, wr, wo, gain, attn):
    tokens, width = h.shape
    n = attn.shape[0]
    return pl.pallas_call(
        home_kernel,
        out_shape=[
            jax.ShapeDtypeStruct((tokens, width), F32),
            jax.ShapeDtypeStruct((n, 128, width), BF16),
            jax.ShapeDtypeStruct((n, tokens, 128), BF16),
            jax.ShapeDtypeStruct((width, 128), BF16),
            jax.ShapeDtypeStruct((1, width), F32),
        ],
        compiler_params=params(),
        cost_estimate=cost(4 * tokens * width * width, 1e7),
        name="home_step",
    )(gx, h, middle, cot, wr, wo, gain, attn)


def final_kernel(shard, grads_ref, w_ref, h_ref, x_ref, gain_ref, grad_middle_ref, dw_ref, grad_x_ref, dgain_ref, total):
    c = pl.program_id(0)
    g = grads_ref[0]
    dw_ref[...] = dot(h_ref[...], g, TN).astype(BF16)

    @pl.when(c == 0)
    def _():
        total[...] = jnp.zeros_like(total)

    for f in range(w_ref.shape[0]):
        total[:, f * shard : (f + 1) * shard] += dot(g, w_ref[f, :shard, :], NT)

    @pl.when(c == pl.num_programs(0) - 1)
    def _():
        normed, scale = norm_parts(x_ref[...])
        grad_h = total[...]
        dgain_ref[...] = jnp.sum(grad_h * normed, 0, keepdims=True)
        grad_x_ref[...] = grad_middle_ref[...] + norm_back(grad_h * gain_ref[...], normed, scale)


def final_step(grads, weights, h, x, gain, grad_middle, shard):
    n, tokens, _ = grads.shape
    width = x.shape[1]
    fsdp, padded, _ = weights.shape
    same = lambda c: (0, 0)
    return pl.pallas_call(
        functools.partial(final_kernel, shard),
        grid=(n,),
        in_specs=[
            pl.BlockSpec((1, tokens, PACK), lambda c: (c, 0, 0)),
            pl.BlockSpec((fsdp, padded, PACK), lambda c: (0, 0, c)),
            pl.BlockSpec((tokens, width), same),
            pl.BlockSpec((tokens, width), same),
            pl.BlockSpec((1, width), same),
            pl.BlockSpec((tokens, width), same),
        ],
        out_specs=[
            pl.BlockSpec((width, PACK), lambda c: (0, c)),
            pl.BlockSpec((tokens, width), same),
            pl.BlockSpec((1, width), same),
        ],
        out_shape=[
            jax.ShapeDtypeStruct((width, n * PACK), BF16),
            jax.ShapeDtypeStruct((tokens, width), F32),
            jax.ShapeDtypeStruct((1, width), F32),
        ],
        scratch_shapes=[pltpu.VMEM((tokens, width), F32)],
        compiler_params=params(),
        cost_estimate=cost(4 * tokens * width * n * PACK, 1.2e7),
        name="final_step",
    )(grads, weights, h, x, gain, grad_middle)


def place_kernel(index_ref, own_ref, other_ref, *refs):
    out_ref = refs[-1]

    @pl.when(pl.program_id(0) == 0)
    def _():
        out_ref[0] = own_ref[0].astype(F32)

    @pl.when(pl.program_id(0) == 1)
    def _():
        out_ref[0] = other_ref[0].astype(F32)


def place(index, own, other, number, buffer):
    _, rows, columns = own.shape
    block = pl.BlockSpec((1, rows, columns), lambda i, at: (0, 0, 0))
    extra = [] if buffer is None else [buffer]
    return pl.pallas_call(
        place_kernel,
        grid_spec=pltpu.PrefetchScalarGridSpec(
            num_scalar_prefetch=1,
            grid=(2,),
            in_specs=[block, block] + [pl.BlockSpec(memory_space=pl.ANY)] * len(extra),
            out_specs=pl.BlockSpec((1, rows, columns), lambda i, at: (at[i], 0, 0)),
        ),
        out_shape=jax.ShapeDtypeStruct((number, rows, columns), F32),
        input_output_aliases={3: 0} if extra else {},
        compiler_params=params(),
        cost_estimate=cost(0, 12 * rows * columns),
        name="place",
    )(index, own, other, *extra)


def swap(value, axis, bit):
    size = lax.axis_size(axis)
    return lax.ppermute(value, axis, [(i, i ^ bit) for i in range(size)])


def group_bits(fsdp):
    bits = [("fsdp", 1 << b) for b in range(1, fsdp.bit_length() - 1)]
    return bits + [("ctx", 1), ("fsdp", 1)]


def group_gather(value, bits):
    stacked = value[None]
    for axis, bit in bits:
        stacked = jnp.concatenate([stacked, swap(stacked, axis, bit)], 0)
    return stacked


def group_reduce(stacked, bits):
    for axis, bit in reversed(bits):
        half = stacked.shape[0] // 2
        arrived = swap(stacked[half:], axis, bit)
        stacked = (stacked[:half].astype(F32) + arrived.astype(F32)).astype(stacked.dtype)
    return stacked[0]


def line_sum(value, ctx):
    pairs = ctx // 2
    if pairs != 4:
        bit = 2
        while bit < ctx:
            value = value + swap(value, "ctx", bit)
            bit *= 2
        return value
    at = lambda z, y: 2 * z + y
    inward = [(at(0, y), at(1, y)) for y in range(2)] + [(at(3, y), at(2, y)) for y in range(2)]
    across = [(at(1, y), at(2, y)) for y in range(2)] + [(at(2, y), at(1, y)) for y in range(2)]
    outward = [(b, a) for a, b in inward]
    value = value + lax.ppermute(value, "ctx", inward)
    value = value + lax.ppermute(value, "ctx", across)
    arrived = lax.ppermute(value, "ctx", outward)
    z = lax.axis_index("ctx") // 2
    return jnp.where((z == 0) | (z == 3), arrived, value)


def local(
    inputs,
    cotangent,
    doc_lengths,
    routes,
    attn_gain,
    ffn_gain,
    w_query,
    key_weight,
    value_weight,
    w_out,
    w_router,
    w_gate,
    w_up,
    w_down,
):
    rows = inputs.shape[2]
    width = inputs.shape[3]
    n = lax.axis_size("ctx")
    fsdp = lax.axis_size("fsdp")
    me, mine = lax.axis_index("ctx"), lax.axis_index("fsdp")
    tokens = 2 * rows
    length = tokens * n
    experts_here = w_gate.shape[0]
    number = experts_here // 2
    capacity = 5 * tokens * TOP // (4 * EXPERTS)
    capp = -(-capacity // 16) * 16
    shard = width // fsdp
    heads = QUERY_HEADS // n
    head_lanes = heads * HEAD_DIMENSION
    copies = n // KEY_VALUE_HEADS
    bits = group_bits(fsdp)

    x = inputs.reshape(tokens, width)
    cot = cotangent.reshape(tokens, width)
    side = me % 2
    base = (side * number).astype(jnp.int32).reshape(1)
    first = (mine * experts_here + side * number).astype(jnp.int32).reshape(1)
    index = jnp.stack([side * number, (1 - side) * number]).astype(jnp.int32)
    ends = jnp.cumsum(doc_lengths[0])[:3].astype(jnp.int32)
    table = jnp.asarray(rotary_table(length))
    own_table = lax.dynamic_slice_in_dim(table.reshape(2, n, rows, 256), me, 1, 1).reshape(tokens, 256)

    query_part = w_query.reshape(shard, n, head_lanes)
    if head_lanes < 128:
        query_part = jnp.pad(query_part, ((0, 0), (0, 0), (0, 128 - head_lanes)))
    key_part = jnp.repeat(key_weight.reshape(shard, KEY_VALUE_HEADS, HEAD_DIMENSION), copies, 1)
    value_part = jnp.repeat(value_weight.reshape(shard, KEY_VALUE_HEADS, HEAD_DIMENSION), copies, 1)
    packed = jnp.concatenate([query_part, key_part, value_part], -1).reshape(shard, n * PACK)
    gains = jnp.pad(jnp.stack([attn_gain, ffn_gain]), ((0, 14), (0, n * PACK - shard)))
    weights = lax.all_gather(jnp.concatenate([packed, gains], 0), "fsdp", axis=0)
    gain_one = weights[:, shard, :shard].reshape(1, width).astype(F32)
    gain_two = weights[:, shard + 1, :shard].reshape(1, width).astype(F32)
    out_part = w_out.reshape(shard // head_lanes, head_lanes, width)
    if head_lanes < 128:
        out_part = jnp.pad(out_part, ((0, 0), (0, 128 - head_lanes), (0, 0)))
    wo = lax.all_gather(out_part, "fsdp", axis=0, tiled=True)
    wr = lax.all_gather(jnp.pad(w_router, ((0, 0), (0, 128 - EXPERTS))), "fsdp", axis=0, tiled=True)
    wrt = jnp.transpose(wr)

    cxs = group_gather(prep(routes.reshape(tokens, TOP), cot, capacity), bits)

    packs, h_attn = qkv(x, gain_one, weights, own_table, shard, n)
    packs = lax.all_to_all(packs, "ctx", split_axis=0, concat_axis=0, tiled=True).reshape(n, 2, rows, PACK)
    attn, lse, full = attn_forward(ends, packs, length)
    attn = lax.all_to_all(attn.reshape(n, tokens, 128), "ctx", split_axis=0, concat_axis=0, tiled=True)
    middle, h_ffn = middle_step(attn, wo, x, gain_two)
    hs = group_gather(h_ffn, bits)

    xs, gs, gates = gather_rows(first, hs, cxs, wrt, number, capp)
    nb = hs.shape[0]
    merge = lambda a: a.reshape(number, nb * capp, a.shape[-1])
    xs, gs, gates = merge(xs), merge(gs), merge(gates)
    steps = [expert_step(base, xs, gs, gates, w_gate, w_up, w_down, j, 1) for j in range(number)]
    y_part, gx_part = combine(first, cxs, [s[3] for s in steps], [s[4] for s in steps], [s[5] for s in steps], tokens, capp)
    gx = group_reduce(gx_part, bits)
    grad_middle, dwo, grad_attn, dwr, dgain_two = home_step(gx, h_ffn, middle, cot, wr, wo, gain_two, attn)
    grad_attn = lax.all_to_all(grad_attn, "ctx", split_axis=0, concat_axis=0, tiled=True).reshape(n, 2, rows, 128)
    grads = attn_backward(ends, packs, grad_attn, lse, full, table, length)
    grads = lax.all_to_all(grads.reshape(n, tokens, PACK), "ctx", split_axis=0, concat_axis=0, tiled=True)
    dw, grad_x, dgain_one = final_step(grads, weights, h_attn, x, gain_one, grad_middle, shard)
    mixed = middle + RESIDUAL * group_reduce(y_part, bits).astype(F32)

    outs = [None, None, None]
    for j, step in enumerate(steps):
        for m in range(3):
            total = line_sum(step[m], n)
            outs[m] = place(index + j, total, swap(total, "ctx", 1), experts_here, outs[m])

    scatter = lambda a: lax.psum(lax.psum_scatter(a, "fsdp", scatter_dimension=0, tiled=True), "ctx").astype(F32)
    dwo = scatter(dwo)[:, :head_lanes, :].reshape(shard, width)
    small = jnp.concatenate([dwr[:, :EXPERTS], dgain_two.reshape(width, 1).astype(BF16)], 1)
    small = scatter(jnp.pad(small, ((0, 0), (0, 127 - EXPERTS))))
    dw = scatter(dw).reshape(shard, n, PACK)
    dgain_one = scatter(dgain_one.reshape(width).astype(BF16))
    fold = lambda a: a.reshape(shard, KEY_VALUE_HEADS, copies, HEAD_DIMENSION).sum(2).reshape(shard, -1)
    return (
        mixed.reshape(inputs.shape),
        grad_x.reshape(inputs.shape),
        dgain_one,
        small[:, EXPERTS],
        dw[:, :, :head_lanes].reshape(shard, -1),
        fold(dw[:, :, 128:192]),
        fold(dw[:, :, 192:256]),
        dwo,
        small[:, :EXPERTS],
        outs[0],
        outs[1],
        outs[2],
    )


def solution(mesh):
    tokens = P("fsdp", None, "ctx", None)
    one, two, three = P("fsdp"), P("fsdp", None), P("fsdp", None, None)
    return jax.shard_map(
        local,
        mesh=mesh,
        in_specs=(tokens, tokens, two, tokens, one, one, two, two, two, two, two, three, three, three),
        out_specs=(tokens, tokens, one, one, two, two, two, two, two, three, three, three),
        check_vma=False,
    )
```

```python
import functools

import jax
import jax.numpy as jnp
import numpy as np
from jax import lax
from jax.experimental import pallas as pl
from jax.experimental.pallas import tpu as pltpu
from jax.sharding import PartitionSpec as P

QUERY_HEADS = 16
KEY_VALUE_HEADS = 8
HEAD_DIMENSION = 64
EXPERTS = 32
TOP = 8

ATTN_SCALE = 0.015625
RESIDUAL = 0.22
NORM_EPS = 1e-06
ROPE_BASE = 10000.0
MASKED = -1e30

F32 = jnp.float32
BF16 = jnp.bfloat16
MIB = 1 << 20
NT = (((1,), (1,)), ((), ()))
TN = (((0,), (0,)), ((), ()))
BLK = 256
PACK = 256


def dot(a, b, dims=None):
    if dims is None:
        return jnp.dot(a, b, preferred_element_type=F32)
    return lax.dot_general(a, b, dims, preferred_element_type=F32)


def params(limit=56, **kw):
    return pltpu.CompilerParams(vmem_limit_bytes=limit * MIB, **kw)


def cost(flops, bytes_accessed):
    return pl.CostEstimate(flops=int(flops), bytes_accessed=int(bytes_accessed), transcendentals=0)


def lane_iota(shape):
    return lax.broadcasted_iota(jnp.int32, shape, len(shape) - 1)


def row_iota(shape):
    return lax.broadcasted_iota(jnp.int32, shape, len(shape) - 2)


def rotary_table(length):
    half = length // 2
    order = np.arange(half, dtype=np.float32)
    positions = np.concatenate([order, length - 1 - order]).astype(np.float32)
    m = np.arange(HEAD_DIMENSION // 2, dtype=np.float64)
    frequency = (ROPE_BASE ** (-2.0 * m / HEAD_DIMENSION)).astype(np.float32)
    angles = (positions[:, None] * frequency[None, :]).astype(np.float64)
    cosine, sine = np.cos(angles), np.sin(angles)
    cos_head = np.concatenate([cosine, cosine], -1)
    sin_head = np.concatenate([-sine, sine], -1)
    return np.concatenate([cos_head, cos_head, sin_head, sin_head], -1).astype(np.float32)


def turn(v, table, direction):
    lanes = lane_iota(v.shape)
    cosine = jnp.concatenate([table[:, :128], table[:, :128]], -1)
    sine = jnp.concatenate([table[:, 128:], table[:, 128:]], -1)
    turned = lanes < 3 * HEAD_DIMENSION
    swapped = jnp.where(lanes % HEAD_DIMENSION < HEAD_DIMENSION // 2, pltpu.roll(v, PACK - 32, 1), pltpu.roll(v, 32, 1))
    return jnp.where(turned, v * cosine + direction * (swapped * sine), v)


def norm_parts(values):
    inv_rms = lax.rsqrt(jnp.mean(values * values, -1, keepdims=True) + NORM_EPS)
    return values * inv_rms, inv_rms


def norm_back(grad_normed, normed, inv_rms):
    return inv_rms * (grad_normed - normed * jnp.mean(grad_normed * normed, -1, keepdims=True))


def prep_kernel(cap, routes_ref, cot_ref, out_ref):
    tokens, width = cot_ref.shape
    routes = routes_ref[...]
    earlier = (lane_iota((tokens, tokens)) < row_iota((tokens, tokens))).astype(BF16)
    experts = lane_iota((tokens, 128))
    base = jnp.zeros((1, 128), F32)
    plus = jnp.zeros((tokens, 128), F32)
    for k in range(TOP):
        chosen = experts == routes[:, k : k + 1]
        ones = chosen.astype(F32)
        slot = dot(earlier, ones.astype(BF16)) + base
        plus = plus + jnp.where(chosen & (slot < cap), slot + 1.0, 0.0)
        base = base + jnp.sum(ones, 0, keepdims=True)
    out_ref[:tokens, :] = cot_ref[...].astype(BF16)
    slots = (jnp.transpose(plus) - 1.0)[:EXPERTS, :]
    out_ref[tokens:, :] = jnp.concatenate([slots, jnp.zeros((EXPERTS, width - tokens), F32)], -1).astype(BF16)


def prep(routes, cot, cap):
    tokens, width = cot.shape
    return pl.pallas_call(
        functools.partial(prep_kernel, cap),
        out_shape=jax.ShapeDtypeStruct((tokens + EXPERTS, width), BF16),
        compiler_params=params(),
        cost_estimate=cost(1e9, 2e6),
        name="prep",
    )(routes, cot)


def qkv_kernel(shard, x_ref, gain_ref, w_ref, table_ref, out_ref, h_ref):
    @pl.when(pl.program_id(0) == 0)
    def _():
        normed, _ = norm_parts(x_ref[...])
        h_ref[...] = (normed * gain_ref[...]).astype(BF16)

    total = None
    for f in range(w_ref.shape[0]):
        part = dot(h_ref[:, f * shard : (f + 1) * shard], w_ref[f, :shard, :])
        total = part if total is None else total + part
    for d in range(out_ref.shape[0]):
        out_ref[d] = turn(total[:, d * PACK : (d + 1) * PACK], table_ref[...], 1.0).astype(BF16)


def qkv(x, gain, weights, table, shard, n):
    tokens, width = x.shape
    fsdp, padded, _ = weights.shape
    return pl.pallas_call(
        functools.partial(qkv_kernel, shard),
        grid=(n // 2,),
        in_specs=[
            pl.BlockSpec((tokens, width), lambda i: (0, 0)),
            pl.BlockSpec((1, width), lambda i: (0, 0)),
            pl.BlockSpec((fsdp, padded, 2 * PACK), lambda i: (0, 0, i)),
            pl.BlockSpec((tokens, 256), lambda i: (0, 0)),
        ],
        out_specs=[
            pl.BlockSpec((2, tokens, PACK), lambda i: (i, 0, 0)),
            pl.BlockSpec((tokens, width), lambda i: (0, 0)),
        ],
        out_shape=[
            jax.ShapeDtypeStruct((n, tokens, PACK), BF16),
            jax.ShapeDtypeStruct((tokens, width), BF16),
        ],
        compiler_params=params(),
        cost_estimate=cost(2 * tokens * width * n * PACK, 8e6),
        name="qkv",
    )(x, gain, weights, table)


def pair_keys(kv):
    other = pltpu.roll(kv, 64, 1)
    low = lane_iota(kv.shape) < 64
    return jnp.where(low, kv, other), jnp.where(low, other, kv)


def stack_heads(q):
    low = lane_iota(q.shape) < 64
    zero = jnp.zeros_like(q)
    return jnp.concatenate([jnp.where(low, q, zero), jnp.where(low, zero, q)], 0)


def fold_heads(stacked):
    rows = stacked.shape[0] // 2
    return jnp.where(lane_iota((rows, 128)) < 64, stacked[:rows], stacked[rows:])


def query_rows(ends_ref, block, length):
    half = length // 2
    lanes = lane_iota((1, 2 * BLK))
    index = block * BLK + jnp.where(lanes < BLK, lanes, lanes - BLK)
    position = jnp.where(index < half, index, length + half - 1 - index)
    start = jnp.zeros_like(position)
    for j in range(3):
        end = ends_ref[j]
        start = jnp.where(position >= end, jnp.maximum(start, end), start)
    return position, start


def key_position(kb, length):
    half = length // 2
    index = kb * BLK + row_iota((BLK, 1))
    return jnp.where(index < half, index, length + half - 1 - index)


def block_loop(block, per_half, body, init):
    late = block >= per_half
    inner = jnp.where(late, block - per_half, block)
    count = jnp.where(late, 2 * per_half - inner, inner + 1)

    def step(j, carry):
        kb = jnp.where(late & (j >= per_half), inner + j, j)
        return body(kb, carry)

    return lax.fori_loop(0, count, step, init)


def load_package(pack_ref, c, h):
    return pack_ref[c, h].astype(F32)


def attn_forward_kernel(length, ends_ref, q_ref, pack_ref, out_ref, lse_ref, full_ref, keys, values_t, acc):
    block = pl.program_id(0)
    half = length // 2
    n, _, rows, _ = pack_ref.shape

    @pl.when(block == 0)
    def _():
        for h in range(2):
            for c in range(n):
                kk, vv = pair_keys(pack_ref[c, h, :, 128:256].astype(F32))
                at = h * half + c * rows
                keys[at : at + rows, :] = kk.astype(BF16)
                if rows % 128 == 0:
                    values_t[:, at : at + rows] = jnp.transpose(vv).astype(BF16)
        if rows % 128 != 0:
            for h in range(2):
                for c in range(0, n, 2):
                    pair = jnp.concatenate([pack_ref[c, h, :, 128:256], pack_ref[c + 1, h, :, 128:256]], 0)
                    _, vv = pair_keys(pair.astype(F32))
                    at = h * half + c * rows
                    values_t[:, at : at + 2 * rows] = jnp.transpose(vv).astype(BF16)

    q = q_ref[...].reshape(BLK, PACK)[:, :128]
    q2 = stack_heads(q)
    position, start = query_rows(ends_ref, block, length)
    acc[...] = jnp.zeros_like(acc)

    def body(kb, carry):
        peak, total = carry
        at = pl.multiple_of(kb * BLK, BLK)
        scores = dot(keys[pl.ds(at, BLK), :], q2, NT) * ATTN_SCALE
        where = key_position(kb, length)
        scores = jnp.where((where <= position) & (where >= start), scores, MASKED)
        new_peak = jnp.maximum(peak, jnp.max(scores, 0, keepdims=True))
        weights = jnp.exp(scores - new_peak)
        fade = jnp.exp(peak - new_peak)
        total = total * fade + jnp.sum(weights, 0, keepdims=True)
        acc[...] = acc[...] * fade + dot(values_t[:, pl.ds(at, BLK)], weights.astype(BF16))
        return new_peak, total

    init = (jnp.full((1, 2 * BLK), MASKED, F32), jnp.zeros((1, 2 * BLK), F32))
    peak, total = block_loop(block, half // BLK, body, init)
    result = acc[...] / total
    full_ref[0] = result
    lse_ref[0] = peak + jnp.log(total)
    folded = fold_heads(jnp.transpose(result)).astype(BF16)
    out_ref[...] = folded.reshape(out_ref.shape)


def attn_forward(ends, packs, length):
    n, _, rows, _ = packs.shape
    blocks, per = length // BLK, BLK // rows
    per_half = blocks // 2
    tiles = lambda i, ends: (lax.rem(i, per_half), i // per_half, 0, 0)
    return pl.pallas_call(
        functools.partial(attn_forward_kernel, length),
        grid_spec=pltpu.PrefetchScalarGridSpec(
            num_scalar_prefetch=1,
            grid=(blocks,),
            in_specs=[
                pl.BlockSpec((per, 1, rows, PACK), tiles),
                pl.BlockSpec(packs.shape, lambda i, ends: (0, 0, 0, 0)),
            ],
            out_specs=[
                pl.BlockSpec((per, 1, rows, 128), tiles),
                pl.BlockSpec((1, 1, 2 * BLK), lambda i, ends: (i, 0, 0)),
                pl.BlockSpec((1, 128, 2 * BLK), lambda i, ends: (i, 0, 0)),
            ],
            scratch_shapes=[
                pltpu.VMEM((length, 128), BF16),
                pltpu.VMEM((128, length), BF16),
                pltpu.VMEM((128, 2 * BLK), F32),
            ],
        ),
        out_shape=[
            jax.ShapeDtypeStruct((n, 2, rows, 128), BF16),
            jax.ShapeDtypeStruct((blocks, 1, 2 * BLK), F32),
            jax.ShapeDtypeStruct((blocks, 128, 2 * BLK), F32),
        ],
        compiler_params=params(),
        cost_estimate=cost(1.5e10, 6e6),
        name="attn_forward",
    )(ends, packs, packs)


def attn_backward_kernel(length, ends_ref, q_ref, g_ref, pack_ref, lse_ref, full_ref, table_ref, out_ref, keys, values, keys_t, grad_q, grad_k, grad_v, acc):
    block = pl.program_id(0)
    half = length // 2
    n, _, rows, _ = pack_ref.shape

    @pl.when(block == 0)
    def _():
        for h in range(2):
            for c in range(n):
                kk, vv = pair_keys(pack_ref[c, h, :, 128:256].astype(F32))
                at = h * half + c * rows
                keys[at : at + rows, :] = kk.astype(BF16)
                values[at : at + rows, :] = vv.astype(BF16)
        for b in range(length // BLK):
            keys_t[:, b * BLK : (b + 1) * BLK] = jnp.transpose(keys[b * BLK : (b + 1) * BLK, :].astype(F32)).astype(BF16)
        grad_k[...] = jnp.zeros_like(grad_k)
        grad_v[...] = jnp.zeros_like(grad_v)

    q2 = stack_heads(q_ref[...].reshape(BLK, PACK)[:, :128])
    g2 = stack_heads(g_ref[...].reshape(BLK, 128))
    position, start = query_rows(ends_ref, block, length)
    lse = lse_ref[0]
    delta = jnp.sum(jnp.transpose(g2.astype(F32)) * full_ref[0], 0, keepdims=True)
    acc[...] = jnp.zeros_like(acc)

    def body(kb, carry):
        at = pl.multiple_of(kb * BLK, BLK)
        scores = dot(keys[pl.ds(at, BLK), :], q2, NT) * ATTN_SCALE
        where = key_position(kb, length)
        probs = jnp.where((where <= position) & (where >= start), jnp.exp(scores - lse), 0.0)
        grad_probs = dot(values[pl.ds(at, BLK), :], g2, NT)
        grad_scores = (probs * (grad_probs - delta)).astype(BF16)
        acc[...] += dot(keys_t[:, pl.ds(at, BLK)], grad_scores)
        grad_k[pl.ds(at, BLK), :] += dot(grad_scores, q2)
        grad_v[pl.ds(at, BLK), :] += dot(probs.astype(BF16), g2)
        return carry

    block_loop(block, half // BLK, body, 0)
    grad_q[pl.ds(pl.multiple_of(block * BLK, BLK), BLK), :] = fold_heads(jnp.transpose(acc[...]))

    @pl.when(block == length // BLK - 1)
    def _():
        for h in range(2):
            for c in range(n):
                at = slice(h * half + c * rows, h * half + (c + 1) * rows)
                kk = grad_k[at, :]
                vv = grad_v[at, :]
                kk = (kk + pltpu.roll(kk, 64, 1)) * ATTN_SCALE
                vv = vv + pltpu.roll(vv, 64, 1)
                both = jnp.where(lane_iota(kk.shape) < 64, kk, vv)
                package = jnp.concatenate([grad_q[at, :] * ATTN_SCALE, both], -1)
                out_ref[c, h] = turn(package, table_ref[at, :], -1.0).astype(BF16)


def attn_backward(ends, packs, grads, lse, full, table, length):
    n, _, rows, _ = packs.shape
    blocks, per = length // BLK, BLK // rows
    per_half = blocks // 2
    tiles = lambda i, ends: (lax.rem(i, per_half), i // per_half, 0, 0)
    return pl.pallas_call(
        functools.partial(attn_backward_kernel, length),
        grid_spec=pltpu.PrefetchScalarGridSpec(
            num_scalar_prefetch=1,
            grid=(blocks,),
            in_specs=[
                pl.BlockSpec((per, 1, rows, PACK), tiles),
                pl.BlockSpec((per, 1, rows, 128), tiles),
                pl.BlockSpec(packs.shape, lambda i, ends: (0, 0, 0, 0)),
                pl.BlockSpec((1, 1, 2 * BLK), lambda i, ends: (i, 0, 0)),
                pl.BlockSpec((1, 128, 2 * BLK), lambda i, ends: (i, 0, 0)),
                pl.BlockSpec(table.shape, lambda i, ends: (0, 0)),
            ],
            out_specs=pl.BlockSpec(packs.shape, lambda i, ends: (0, 0, 0, 0)),
            scratch_shapes=[
                pltpu.VMEM((length, 128), BF16),
                pltpu.VMEM((length, 128), BF16),
                pltpu.VMEM((128, length), BF16),
                pltpu.VMEM((length, 128), F32),
                pltpu.VMEM((length, 128), F32),
                pltpu.VMEM((length, 128), F32),
                pltpu.VMEM((128, 2 * BLK), F32),
            ],
        ),
        out_shape=jax.ShapeDtypeStruct(packs.shape, BF16),
        compiler_params=params(),
        cost_estimate=cost(3e10, 8e6),
        name="attn_backward",
    )(ends, packs, grads, packs, lse, full, table)


def middle_kernel(attn_ref, wo_ref, x_ref, gain_ref, middle_ref, h_ref):
    total = None
    for c in range(attn_ref.shape[0]):
        part = dot(attn_ref[c], wo_ref[c])
        total = part if total is None else total + part
    middle = x_ref[...] + RESIDUAL * total
    middle_ref[...] = middle
    normed, _ = norm_parts(middle)
    h_ref[...] = (normed * gain_ref[...]).astype(BF16)


def middle_step(attn, wo, x, gain):
    tokens, width = x.shape
    return pl.pallas_call(
        middle_kernel,
        out_shape=[jax.ShapeDtypeStruct((tokens, width), F32), jax.ShapeDtypeStruct((tokens, width), BF16)],
        compiler_params=params(),
        cost_estimate=cost(2 * tokens * width * width, 5e6),
        name="middle",
    )(attn, wo, x, gain)


def own_row(table, row):
    return jnp.sum(jnp.where(row_iota(table.shape) == row, table, 0.0), 0, keepdims=True)


def one_hot(slots, first, number, capp):
    tokens = slots.shape[1]
    order = row_iota((capp, tokens)).astype(F32)
    return [(order == own_row(slots, first + j)).astype(F32) for j in range(number)]


def gather_kernel(number, capp, first_ref, h_ref, cx_ref, wrt_ref, x_ref, g_ref, gate_ref):
    tokens = h_ref.shape[1]
    first = first_ref[0]
    h = h_ref[0]
    slots = cx_ref[0, tokens:, :tokens].astype(F32)
    logits = dot(wrt_ref[...], h, NT)[:EXPERTS, :]
    raw = jnp.exp(logits - jnp.max(logits, 0, keepdims=True))
    router = raw / jnp.sum(raw, 0, keepdims=True)
    hots = one_hot(slots, first, number, capp)
    places = jnp.concatenate(hots, 0).astype(BF16)
    rows = dot(places, h).astype(BF16)
    grads = dot(places, cx_ref[0, :tokens, :]).astype(BF16)
    for j in range(number):
        at = slice(j * capp, (j + 1) * capp)
        x_ref[j, 0] = rows[at]
        g_ref[j, 0] = grads[at]
        gate = jnp.sum(hots[j] * own_row(router, first + j), 1, keepdims=True)
        gate_ref[j, 0] = jnp.broadcast_to(gate, (capp, 128))


def gather_rows(first, hs, cxs, wrt, number, capp):
    nb, tokens, width = hs.shape
    return pl.pallas_call(
        functools.partial(gather_kernel, number, capp),
        grid_spec=pltpu.PrefetchScalarGridSpec(
            num_scalar_prefetch=1,
            grid=(nb,),
            in_specs=[
                pl.BlockSpec((1, tokens, width), lambda b, f: (b, 0, 0)),
                pl.BlockSpec((1, tokens + EXPERTS, width), lambda b, f: (b, 0, 0)),
                pl.BlockSpec(wrt.shape, lambda b, f: (0, 0)),
            ],
            out_specs=[
                pl.BlockSpec((number, 1, capp, width), lambda b, f: (0, b, 0, 0)),
                pl.BlockSpec((number, 1, capp, width), lambda b, f: (0, b, 0, 0)),
                pl.BlockSpec((number, 1, capp, 128), lambda b, f: (0, b, 0, 0)),
            ],
        ),
        out_shape=[
            jax.ShapeDtypeStruct((number, nb, capp, width), BF16),
            jax.ShapeDtypeStruct((number, nb, capp, width), BF16),
            jax.ShapeDtypeStruct((number, nb, capp, 128), F32),
        ],
        compiler_params=params(),
        cost_estimate=cost(4 * nb * number * capp * tokens * width, 2e7),
        name="gather_rows",
    )(first, hs, cxs, wrt)


PIECE = 512


def expert_kernel(base_ref, x_ref, g_ref, gate_ref, wg_ref, wu_ref, wd_ref, piece_ref, out_ref, rows_ref, dg_ref):
    x = x_ref[0]
    gate = gate_ref[0][:, :1]
    grad_ffn = RESIDUAL * g_ref[0].astype(F32)
    go = (gate * grad_ffn).astype(BF16)
    part = wg_ref.shape[2] // 2
    out = rows = None
    for chunk in range(2):
        at = slice(chunk * part, (chunk + 1) * part)
        wg, wu, wd = wg_ref[0, :, at], wu_ref[0, :, at], wd_ref[0, at, :]
        pre_gate = dot(x, wg)
        pre_up = dot(x, wu)
        sig = jax.nn.sigmoid(pre_gate)
        hidden = (pre_gate * sig * pre_up).astype(BF16)
        out_part = dot(hidden, wd)
        grad_hidden = dot(go, wd, NT)
        grad_gate = (grad_hidden * pre_up * sig * (1.0 + pre_gate * (1.0 - sig))).astype(BF16)
        grad_up = (grad_hidden * pre_gate * sig).astype(BF16)
        row_part = dot(grad_gate, wg, NT) + dot(grad_up, wu, NT)
        dwg = dot(x, grad_gate, TN).astype(BF16)
        dwu = dot(x, grad_up, TN).astype(BF16)
        dwd = dot(hidden, go, TN).astype(BF16)
        for half in range(2):
            side = slice(half * PIECE, (half + 1) * PIECE)
            piece_ref[0, half, :, at] = dwg[side]
            piece_ref[0, 2 + half, :, at] = dwu[side]
            piece_ref[0, 4 + half, at, :] = dwd[:, side]
        out = out_part if out is None else out + out_part
        rows = row_part if rows is None else rows + row_part
    out = out.astype(BF16).astype(F32)
    out_ref[0] = (gate * out).astype(BF16)
    rows_ref[0] = rows.astype(BF16)
    grad = jnp.sum(grad_ffn * out, 1, keepdims=True)
    dg_ref[0] = jnp.broadcast_to(grad, dg_ref.shape[1:])


def expert_step(base, xs, gs, gates, w_gate, w_up, w_down):
    number, rows, width = xs.shape
    ff = w_gate.shape[2]
    row = lambda e, b: (e, 0, 0)
    weight = lambda e, b: (b[0] + e, 0, 0)
    return pl.pallas_call(
        expert_kernel,
        grid_spec=pltpu.PrefetchScalarGridSpec(
            num_scalar_prefetch=1,
            grid=(number,),
            in_specs=[
                pl.BlockSpec((1, rows, width), row),
                pl.BlockSpec((1, rows, width), row),
                pl.BlockSpec((1, rows, 128), row),
                pl.BlockSpec((1, width, ff), weight),
                pl.BlockSpec((1, width, ff), weight),
                pl.BlockSpec((1, ff, width), weight),
            ],
            out_specs=[
                pl.BlockSpec((1, 6, PIECE, PIECE), lambda e, b: (e, 0, 0, 0)),
                pl.BlockSpec((1, rows, width), row),
                pl.BlockSpec((1, rows, width), row),
                pl.BlockSpec((1, rows, 128), row),
            ],
        ),
        out_shape=[
            jax.ShapeDtypeStruct((number, 6, PIECE, PIECE), BF16),
            jax.ShapeDtypeStruct((number, rows, width), BF16),
            jax.ShapeDtypeStruct((number, rows, width), BF16),
            jax.ShapeDtypeStruct((number, rows, 128), F32),
        ],
        compiler_params=params(60),
        cost_estimate=cost(18 * number * rows * width * ff, 5e7),
        name="expert_step",
    )(base, xs, gs, gates, w_gate, w_up, w_down)


def combine_kernel(number, capp, first_ref, slot_ref, outs, rows, grads, y_ref, gx_ref):
    tokens = y_ref.shape[1]
    width = y_ref.shape[2]
    first = first_ref[0]
    slots = slot_ref[0][:, :tokens].astype(F32)
    hots = one_hot(slots, first, number, capp)
    places = jnp.concatenate(hots, 0).astype(BF16)
    y_ref[0] = dot(places, outs[:, 0].reshape(number * capp, width), TN).astype(BF16)
    gx_ref[0, :tokens] = dot(places, rows[:, 0].reshape(number * capp, width), TN).astype(BF16)
    extra = jnp.zeros((EXPERTS, 2 * tokens), F32)
    for j in range(number):
        grad = jnp.sum(hots[j] * grads[j, 0][:, :1], 0, keepdims=True)
        high = grad.astype(BF16).astype(F32)
        both = jnp.concatenate([high, grad - high], 1)
        extra = jnp.where(row_iota(extra.shape) == first + j, both, extra)
    rest = jnp.zeros((EXPERTS, width - 2 * tokens), F32)
    gx_ref[0, tokens:] = jnp.concatenate([extra, rest], 1).astype(BF16)


def combine(first, cxs, outs, rows, grads, tokens, capp):
    number = outs.shape[0]
    nb, _, width = cxs.shape
    split = lambda a: a.reshape(number, nb, capp, a.shape[-1])
    wide = pl.BlockSpec((number, 1, capp, width), lambda b, f: (0, b, 0, 0))
    thin = pl.BlockSpec((number, 1, capp, 128), lambda b, f: (0, b, 0, 0))
    return pl.pallas_call(
        functools.partial(combine_kernel, number, capp),
        grid_spec=pltpu.PrefetchScalarGridSpec(
            num_scalar_prefetch=1,
            grid=(nb,),
            in_specs=[pl.BlockSpec((1, EXPERTS, width), lambda b, f: (b, tokens // EXPERTS, 0))] + [wide, wide, thin],
            out_specs=[
                pl.BlockSpec((1, tokens, width), lambda b, f: (b, 0, 0)),
                pl.BlockSpec((1, tokens + EXPERTS, width), lambda b, f: (b, 0, 0)),
            ],
        ),
        out_shape=[
            jax.ShapeDtypeStruct((nb, tokens, width), BF16),
            jax.ShapeDtypeStruct((nb, tokens + EXPERTS, width), BF16),
        ],
        compiler_params=params(),
        cost_estimate=cost(4 * nb * number * capp * tokens * width, 2e7),
        name="combine",
    )(first, cxs, split(outs), split(rows), split(grads))


def home_kernel(gx_ref, h_ref, middle_ref, cot_ref, wr_ref, wo_ref, gain_ref, attn_ref, grad_middle_ref, dwo_ref, ga_ref, dwr_ref, dgain_ref):
    tokens, width = h_ref.shape
    h = h_ref[...]
    gain = gain_ref[...]
    extra = gx_ref[tokens:, :].astype(F32)
    grad_router = extra[:, :tokens] + extra[:, tokens : 2 * tokens]
    grad_router = jnp.transpose(jnp.concatenate([grad_router, jnp.zeros((128 - EXPERTS, tokens), F32)], 0))
    logits = dot(h, wr_ref[...])
    logits = jnp.where(lane_iota(logits.shape) < EXPERTS, logits, MASKED)
    raw = jnp.exp(logits - jnp.max(logits, -1, keepdims=True))
    router = raw / jnp.sum(raw, -1, keepdims=True)
    grad_logits = (router * (grad_router - jnp.sum(router * grad_router, -1, keepdims=True))).astype(BF16)
    dwr_ref[...] = dot(h, grad_logits, TN).astype(BF16)
    grad_h = gx_ref[:tokens, :].astype(F32) + dot(grad_logits, wr_ref[...], NT)
    normed, scale = norm_parts(middle_ref[...])
    dgain_ref[...] = jnp.sum(grad_h * normed, 0, keepdims=True)
    grad_middle = cot_ref[...] + norm_back(grad_h * gain, normed, scale)
    grad_middle_ref[...] = grad_middle
    grad_branch = (RESIDUAL * grad_middle).astype(BF16)
    for c in range(attn_ref.shape[0]):
        dwo_ref[c] = dot(attn_ref[c], grad_branch, TN).astype(BF16)
        ga_ref[c] = dot(grad_branch, wo_ref[c], NT).astype(BF16)


def home_step(gx, h, middle, cot, wr, wo, gain, attn):
    tokens, width = h.shape
    n = attn.shape[0]
    return pl.pallas_call(
        home_kernel,
        out_shape=[
            jax.ShapeDtypeStruct((tokens, width), F32),
            jax.ShapeDtypeStruct((n, 128, width), BF16),
            jax.ShapeDtypeStruct((n, tokens, 128), BF16),
            jax.ShapeDtypeStruct((width, 128), BF16),
            jax.ShapeDtypeStruct((1, width), F32),
        ],
        compiler_params=params(),
        cost_estimate=cost(4 * tokens * width * width, 1e7),
        name="home_step",
    )(gx, h, middle, cot, wr, wo, gain, attn)


def final_kernel(shard, grads_ref, w_ref, h_ref, x_ref, gain_ref, grad_middle_ref, dw_ref, grad_x_ref, dgain_ref, total):
    c = pl.program_id(0)
    g = grads_ref[0]
    dw_ref[...] = dot(h_ref[...], g, TN).astype(BF16)

    @pl.when(c == 0)
    def _():
        total[...] = jnp.zeros_like(total)

    for f in range(w_ref.shape[0]):
        total[:, f * shard : (f + 1) * shard] += dot(g, w_ref[f, :shard, :], NT)

    @pl.when(c == pl.num_programs(0) - 1)
    def _():
        normed, scale = norm_parts(x_ref[...])
        grad_h = total[...]
        dgain_ref[...] = jnp.sum(grad_h * normed, 0, keepdims=True)
        grad_x_ref[...] = grad_middle_ref[...] + norm_back(grad_h * gain_ref[...], normed, scale)


def final_step(grads, weights, h, x, gain, grad_middle, shard):
    n, tokens, _ = grads.shape
    width = x.shape[1]
    fsdp, padded, _ = weights.shape
    same = lambda c: (0, 0)
    return pl.pallas_call(
        functools.partial(final_kernel, shard),
        grid=(n,),
        in_specs=[
            pl.BlockSpec((1, tokens, PACK), lambda c: (c, 0, 0)),
            pl.BlockSpec((fsdp, padded, PACK), lambda c: (0, 0, c)),
            pl.BlockSpec((tokens, width), same),
            pl.BlockSpec((tokens, width), same),
            pl.BlockSpec((1, width), same),
            pl.BlockSpec((tokens, width), same),
        ],
        out_specs=[
            pl.BlockSpec((width, PACK), lambda c: (0, c)),
            pl.BlockSpec((tokens, width), same),
            pl.BlockSpec((1, width), same),
        ],
        out_shape=[
            jax.ShapeDtypeStruct((width, n * PACK), BF16),
            jax.ShapeDtypeStruct((tokens, width), F32),
            jax.ShapeDtypeStruct((1, width), F32),
        ],
        scratch_shapes=[pltpu.VMEM((tokens, width), F32)],
        compiler_params=params(),
        cost_estimate=cost(4 * tokens * width * n * PACK, 1.2e7),
        name="final_step",
    )(grads, weights, h, x, gain, grad_middle)


def widen_kernel(index_ref, own_ref, other_ref, out_ref):
    @pl.when(pl.program_id(0) == 0)
    def _():
        out_ref[0] = own_ref[0].astype(F32)

    @pl.when(pl.program_id(0) == 1)
    def _():
        out_ref[0] = other_ref[0].astype(F32)


def widen(index, own, other, matrix, shape):
    number = own.shape[0] // 6
    rows_cut = shape[1] == 2 * PIECE
    piece = lambda e, h: 6 * e + 2 * matrix + h
    return pl.pallas_call(
        widen_kernel,
        grid_spec=pltpu.PrefetchScalarGridSpec(
            num_scalar_prefetch=1,
            grid=(2, number, 2),
            in_specs=[
                pl.BlockSpec((1, PIECE, PIECE), lambda s, e, h, at: (jnp.where(s == 0, piece(e, h), piece(number - 1, 1)), 0, 0)),
                pl.BlockSpec((1, PIECE, PIECE), lambda s, e, h, at: (jnp.where(s == 0, piece(0, 0), piece(e, h)), 0, 0)),
            ],
            out_specs=pl.BlockSpec(
                (1, PIECE, PIECE),
                lambda s, e, h, at: (at[s] + e, h, 0) if rows_cut else (at[s] + e, 0, h),
            ),
        ),
        out_shape=jax.ShapeDtypeStruct(shape, F32),
        compiler_params=params(),
        cost_estimate=cost(0, 6 * shape[0] * shape[1] * shape[2]),
        name="widen",
    )(index, own, other)


def swap(value, axis, bit):
    size = lax.axis_size(axis)
    return lax.ppermute(value, axis, [(i, i ^ bit) for i in range(size)])


def group_bits(fsdp):
    bits = [("fsdp", 1 << b) for b in range(1, fsdp.bit_length() - 1)]
    return bits + [("ctx", 1), ("fsdp", 1)]


def group_gather(value, bits):
    stacked = value[None]
    for axis, bit in bits:
        stacked = jnp.concatenate([stacked, swap(stacked, axis, bit)], 0)
    return stacked


def group_reduce(stacked, bits):
    for axis, bit in reversed(bits):
        half = stacked.shape[0] // 2
        arrived = swap(stacked[half:], axis, bit)
        stacked = (stacked[:half].astype(F32) + arrived.astype(F32)).astype(stacked.dtype)
    return stacked[0]


def line_sum(value, ctx):
    pairs = ctx // 2
    if pairs != 4:
        bit = 2
        while bit < ctx:
            value = value + swap(value, "ctx", bit)
            bit *= 2
        return value
    at = lambda z, y: 2 * z + y
    inward = [(at(0, y), at(1, y)) for y in range(2)] + [(at(3, y), at(2, y)) for y in range(2)]
    across = [(at(1, y), at(2, y)) for y in range(2)] + [(at(2, y), at(1, y)) for y in range(2)]
    outward = [(b, a) for a, b in inward]
    value = value + lax.ppermute(value, "ctx", inward)
    value = value + lax.ppermute(value, "ctx", across)
    arrived = lax.ppermute(value, "ctx", outward)
    z = lax.axis_index("ctx") // 2
    return jnp.where((z == 0) | (z == 3), arrived, value)


def reduce_kernel(piece_ref, own_ref, other_ref, inbox, across, mine, line_send, line_recv, mid_send, mid_recv, side_send, side_recv, load, store):
    count = piece_ref.shape[0]
    ctx = lax.axis_index("ctx")
    z = ctx // 2
    middle = (z == 1) | (z == 2)
    line = {"ctx": jnp.where(z % 2 == 0, ctx + 2, ctx - 2)}
    peer = {"ctx": jnp.where(z == 1, ctx + 2, ctx - 2)}
    side = {"ctx": jnp.where(ctx % 2 == 0, ctx + 1, ctx - 1)}
    mesh_ids = pl.DeviceIdType.MESH

    def remote(src, dst, send, recv, device):
        return pltpu.make_async_remote_copy(src_ref=src, dst_ref=dst, send_sem=send, recv_sem=recv, device_id=device, device_id_type=mesh_ids)

    def send_line(src, i):
        return remote(src, inbox.at[i], line_send.at[i], line_recv.at[i], line)

    def send_mid(i):
        return remote(inbox.at[i], across.at[i], mid_send.at[i], mid_recv.at[i], peer)

    def send_side(src, i):
        return remote(src, other_ref.at[i], side_send.at[i], side_recv.at[i], side)

    def fetch(i):
        return pltpu.make_async_copy(piece_ref.at[i], mine.at[i % 2], load.at[i % 2])

    def keep(src, i):
        return pltpu.make_async_copy(src, own_ref.at[i], store.at[i])

    barrier = pltpu.get_barrier_semaphore()
    pl.semaphore_signal(barrier, inc=1, device_id=line, device_id_type=mesh_ids)
    pl.semaphore_signal(barrier, inc=1, device_id=side, device_id_type=mesh_ids)

    @pl.when(middle)
    def _():
        pl.semaphore_signal(barrier, inc=1, device_id=peer, device_id_type=mesh_ids)
        pl.semaphore_wait(barrier, 3)
        fetch(0).start()

        def tick(t, carry):
            @pl.when(t < count)
            def _():
                @pl.when(t + 1 < count)
                def _():
                    fetch(t + 1).start()

                fetch(t).wait()
                send_line(inbox.at[t], t).wait_recv()
                inbox[t] = inbox[t] + mine[t % 2]
                send_mid(t).start()

            @pl.when(t >= 1)
            def _():
                i = t - 1
                send_mid(i).wait_recv()
                across[i] = across[i] + inbox[i]
                send_line(across.at[i], i).start()
                send_side(across.at[i], i).start()
                keep(across.at[i], i).start()

            return carry

        lax.fori_loop(0, count + 1, tick, 0)

        def finish(i, carry):
            send_mid(i).wait_send()
            send_line(across.at[i], i).wait_send()
            send_side(across.at[i], i).wait()
            keep(across.at[i], i).wait()
            return carry

        lax.fori_loop(0, count, finish, 0)

    @pl.when(jnp.logical_not(middle))
    def _():
        pl.semaphore_wait(barrier, 2)

        def tick(t, carry):
            @pl.when(t < count)
            def _():
                @pl.when(t >= 2)
                def _():
                    send_line(piece_ref.at[t - 2], t - 2).wait_send()

                send_line(piece_ref.at[t], t).start()

            @pl.when(t >= 4)
            def _():
                i = t - 4
                send_line(inbox.at[i], i).wait_recv()
                send_side(inbox.at[i], i).start()
                keep(inbox.at[i], i).start()

            return carry

        lax.fori_loop(0, count + 4, tick, 0)
        for i in range(max(count - 2, 0), count):
            send_line(piece_ref.at[i], i).wait_send()

        def finish(i, carry):
            send_side(inbox.at[i], i).wait()
            keep(inbox.at[i], i).wait()
            return carry

        lax.fori_loop(0, count, finish, 0)


def reduce_pieces(pieces, n):
    if n != 8:
        total = line_sum(pieces, n)
        return total, swap(total, "ctx", 1)
    count = pieces.shape[0]
    shape = jax.ShapeDtypeStruct(pieces.shape, BF16)
    hbm = pl.BlockSpec(memory_space=pl.ANY)
    dma = pltpu.SemaphoreType.DMA((count,))
    return pl.pallas_call(
        reduce_kernel,
        out_shape=[shape, shape],
        in_specs=[hbm],
        out_specs=[hbm, hbm],
        scratch_shapes=[
            pltpu.VMEM(pieces.shape, BF16),
            pltpu.VMEM(pieces.shape, BF16),
            pltpu.VMEM((2,) + pieces.shape[1:], BF16),
            dma,
            dma,
            dma,
            dma,
            dma,
            dma,
            pltpu.SemaphoreType.DMA((2,)),
            dma,
        ],
        compiler_params=params(collective_id=0, has_side_effects=True),
        cost_estimate=cost(1e8, 1e9),
        name="reduce_pieces",
    )(pieces)


def local(
    inputs,
    cotangent,
    doc_lengths,
    routes,
    attn_gain,
    ffn_gain,
    w_query,
    key_weight,
    value_weight,
    w_out,
    w_router,
    w_gate,
    w_up,
    w_down,
):
    rows = inputs.shape[2]
    width = inputs.shape[3]
    n = lax.axis_size("ctx")
    fsdp = lax.axis_size("fsdp")
    me, mine = lax.axis_index("ctx"), lax.axis_index("fsdp")
    tokens = 2 * rows
    length = tokens * n
    experts_here = w_gate.shape[0]
    number = experts_here // 2
    capacity = 5 * tokens * TOP // (4 * EXPERTS)
    capp = -(-capacity // 16) * 16
    shard = width // fsdp
    heads = QUERY_HEADS // n
    head_lanes = heads * HEAD_DIMENSION
    copies = n // KEY_VALUE_HEADS
    bits = group_bits(fsdp)

    x = inputs.reshape(tokens, width)
    cot = cotangent.reshape(tokens, width)
    side = me % 2
    base = (side * number).astype(jnp.int32).reshape(1)
    first = (mine * experts_here + side * number).astype(jnp.int32).reshape(1)
    index = jnp.stack([side * number, (1 - side) * number]).astype(jnp.int32)
    ends = jnp.cumsum(doc_lengths[0])[:3].astype(jnp.int32)
    table = jnp.asarray(rotary_table(length))
    own_table = lax.dynamic_slice_in_dim(table.reshape(2, n, rows, 256), me, 1, 1).reshape(tokens, 256)

    query_part = w_query.reshape(shard, n, head_lanes)
    if head_lanes < 128:
        query_part = jnp.pad(query_part, ((0, 0), (0, 0), (0, 128 - head_lanes)))
    key_part = jnp.repeat(key_weight.reshape(shard, KEY_VALUE_HEADS, HEAD_DIMENSION), copies, 1)
    value_part = jnp.repeat(value_weight.reshape(shard, KEY_VALUE_HEADS, HEAD_DIMENSION), copies, 1)
    packed = jnp.concatenate([query_part, key_part, value_part], -1).reshape(shard, n * PACK)
    gains = jnp.pad(jnp.stack([attn_gain, ffn_gain]), ((0, 14), (0, n * PACK - shard)))
    weights = lax.all_gather(jnp.concatenate([packed, gains], 0), "fsdp", axis=0)
    gain_one = weights[:, shard, :shard].reshape(1, width).astype(F32)
    gain_two = weights[:, shard + 1, :shard].reshape(1, width).astype(F32)
    out_part = w_out.reshape(shard // head_lanes, head_lanes, width)
    if head_lanes < 128:
        out_part = jnp.pad(out_part, ((0, 0), (0, 128 - head_lanes), (0, 0)))
    wo = lax.all_gather(out_part, "fsdp", axis=0, tiled=True)
    wr = lax.all_gather(jnp.pad(w_router, ((0, 0), (0, 128 - EXPERTS))), "fsdp", axis=0, tiled=True)
    wrt = jnp.transpose(wr)

    cxs = group_gather(prep(routes.reshape(tokens, TOP), cot, capacity), bits)

    packs, h_attn = qkv(x, gain_one, weights, own_table, shard, n)
    packs = lax.all_to_all(packs, "ctx", split_axis=0, concat_axis=0, tiled=True).reshape(n, 2, rows, PACK)
    attn, lse, full = attn_forward(ends, packs, length)
    attn = lax.all_to_all(attn.reshape(n, tokens, 128), "ctx", split_axis=0, concat_axis=0, tiled=True)
    middle, h_ffn = middle_step(attn, wo, x, gain_two)
    hs = group_gather(h_ffn, bits)

    xs, gs, gates = gather_rows(first, hs, cxs, wrt, number, capp)
    nb = hs.shape[0]
    merge = lambda a: a.reshape(number, nb * capp, a.shape[-1])
    xs, gs, gates = merge(xs), merge(gs), merge(gates)
    pieces, outs, back, dgates = expert_step(base, xs, gs, gates, w_gate, w_up, w_down)
    y_part, gx_part = combine(first, cxs, outs, back, dgates, tokens, capp)
    gx = group_reduce(gx_part, bits)
    grad_middle, dwo, grad_attn, dwr, dgain_two = home_step(gx, h_ffn, middle, cot, wr, wo, gain_two, attn)
    grad_attn = lax.all_to_all(grad_attn, "ctx", split_axis=0, concat_axis=0, tiled=True).reshape(n, 2, rows, 128)
    grads = attn_backward(ends, packs, grad_attn, lse, full, table, length)
    grads = lax.all_to_all(grads.reshape(n, tokens, PACK), "ctx", split_axis=0, concat_axis=0, tiled=True)
    dw, grad_x, dgain_one = final_step(grads, weights, h_attn, x, gain_one, grad_middle, shard)
    mixed = middle + RESIDUAL * group_reduce(y_part, bits).astype(F32)

    own, other = reduce_pieces(pieces.reshape(number * 6, PIECE, PIECE), n)
    outs = [widen(index, own, other, m, w.shape) for m, w in enumerate((w_gate, w_up, w_down))]

    scatter = lambda a: lax.psum(lax.psum_scatter(a, "fsdp", scatter_dimension=0, tiled=True), "ctx").astype(F32)
    dwo = scatter(dwo)[:, :head_lanes, :].reshape(shard, width)
    small = jnp.concatenate([dwr[:, :EXPERTS], dgain_two.reshape(width, 1).astype(BF16)], 1)
    small = scatter(jnp.pad(small, ((0, 0), (0, 127 - EXPERTS))))
    dw = scatter(dw).reshape(shard, n, PACK)
    dgain_one = scatter(dgain_one.reshape(width).astype(BF16))
    fold = lambda a: a.reshape(shard, KEY_VALUE_HEADS, copies, HEAD_DIMENSION).sum(2).reshape(shard, -1)
    return (
        mixed.reshape(inputs.shape),
        grad_x.reshape(inputs.shape),
        dgain_one,
        small[:, EXPERTS],
        dw[:, :, :head_lanes].reshape(shard, -1),
        fold(dw[:, :, 128:192]),
        fold(dw[:, :, 192:256]),
        dwo,
        small[:, :EXPERTS],
        outs[0],
        outs[1],
        outs[2],
    )


def solution(mesh):
    tokens = P("fsdp", None, "ctx", None)
    one, two, three = P("fsdp"), P("fsdp", None), P("fsdp", None, None)
    return jax.shard_map(
        local,
        mesh=mesh,
        in_specs=(tokens, tokens, two, tokens, one, one, two, two, two, two, two, three, three, three),
        out_specs=(tokens, tokens, one, one, two, two, two, two, two, three, three, three),
        check_vma=False,
    )
```

```python
import functools

import jax
import jax.numpy as jnp
import numpy as np
from jax import lax
from jax.experimental import pallas as pl
from jax.experimental.pallas import tpu as pltpu
from jax.sharding import PartitionSpec as P

QUERY_HEADS = 16
KEY_VALUE_HEADS = 8
HEAD_DIMENSION = 64
EXPERTS = 32
TOP = 8

ATTN_SCALE = 0.015625
RESIDUAL = 0.22
NORM_EPS = 1e-06
ROPE_BASE = 10000.0
MASKED = -1e30

F32 = jnp.float32
BF16 = jnp.bfloat16
MIB = 1 << 20
NT = (((1,), (1,)), ((), ()))
TN = (((0,), (0,)), ((), ()))
BLK = 256
PACK = 256


def dot(a, b, dims=None):
    if dims is None:
        return jnp.dot(a, b, preferred_element_type=F32)
    return lax.dot_general(a, b, dims, preferred_element_type=F32)


def params(limit=56, **kw):
    return pltpu.CompilerParams(vmem_limit_bytes=limit * MIB, **kw)


def cost(flops, bytes_accessed):
    return pl.CostEstimate(flops=int(flops), bytes_accessed=int(bytes_accessed), transcendentals=0)


def lane_iota(shape):
    return lax.broadcasted_iota(jnp.int32, shape, len(shape) - 1)


def row_iota(shape):
    return lax.broadcasted_iota(jnp.int32, shape, len(shape) - 2)


def rotary_table(length):
    half = length // 2
    order = np.arange(half, dtype=np.float32)
    positions = np.concatenate([order, length - 1 - order]).astype(np.float32)
    m = np.arange(HEAD_DIMENSION // 2, dtype=np.float64)
    frequency = (ROPE_BASE ** (-2.0 * m / HEAD_DIMENSION)).astype(np.float32)
    angles = (positions[:, None] * frequency[None, :]).astype(np.float64)
    cosine, sine = np.cos(angles), np.sin(angles)
    cos_head = np.concatenate([cosine, cosine], -1)
    sin_head = np.concatenate([-sine, sine], -1)
    return np.concatenate([cos_head, cos_head, sin_head, sin_head], -1).astype(np.float32)


def turn(v, table, direction):
    lanes = lane_iota(v.shape)
    cosine = jnp.concatenate([table[:, :128], table[:, :128]], -1)
    sine = jnp.concatenate([table[:, 128:], table[:, 128:]], -1)
    turned = lanes < 3 * HEAD_DIMENSION
    swapped = jnp.where(lanes % HEAD_DIMENSION < HEAD_DIMENSION // 2, pltpu.roll(v, PACK - 32, 1), pltpu.roll(v, 32, 1))
    return jnp.where(turned, v * cosine + direction * (swapped * sine), v)


def norm_parts(values):
    inv_rms = lax.rsqrt(jnp.mean(values * values, -1, keepdims=True) + NORM_EPS)
    return values * inv_rms, inv_rms


def norm_back(grad_normed, normed, inv_rms):
    return inv_rms * (grad_normed - normed * jnp.mean(grad_normed * normed, -1, keepdims=True))


def prep_kernel(cap, routes_ref, cot_ref, out_ref):
    tokens, width = cot_ref.shape
    routes = routes_ref[...]
    earlier = (lane_iota((tokens, tokens)) < row_iota((tokens, tokens))).astype(BF16)
    experts = lane_iota((tokens, 128))
    base = jnp.zeros((1, 128), F32)
    plus = jnp.zeros((tokens, 128), F32)
    for k in range(TOP):
        chosen = experts == routes[:, k : k + 1]
        ones = chosen.astype(F32)
        slot = dot(earlier, ones.astype(BF16)) + base
        plus = plus + jnp.where(chosen & (slot < cap), slot + 1.0, 0.0)
        base = base + jnp.sum(ones, 0, keepdims=True)
    out_ref[:tokens, :] = cot_ref[...].astype(BF16)
    slots = (jnp.transpose(plus) - 1.0)[:EXPERTS, :]
    out_ref[tokens:, :] = jnp.concatenate([slots, jnp.zeros((EXPERTS, width - tokens), F32)], -1).astype(BF16)


def prep(routes, cot, cap):
    tokens, width = cot.shape
    return pl.pallas_call(
        functools.partial(prep_kernel, cap),
        out_shape=jax.ShapeDtypeStruct((tokens + EXPERTS, width), BF16),
        compiler_params=params(),
        cost_estimate=cost(1e9, 2e6),
        name="prep",
    )(routes, cot)


def qkv_kernel(shard, x_ref, gain_ref, w_ref, table_ref, out_ref, h_ref):
    @pl.when(pl.program_id(0) == 0)
    def _():
        normed, _ = norm_parts(x_ref[...])
        h_ref[...] = (normed * gain_ref[...]).astype(BF16)

    total = None
    for f in range(w_ref.shape[0]):
        part = dot(h_ref[:, f * shard : (f + 1) * shard], w_ref[f, :shard, :])
        total = part if total is None else total + part
    for d in range(out_ref.shape[0]):
        out_ref[d] = turn(total[:, d * PACK : (d + 1) * PACK], table_ref[...], 1.0).astype(BF16)


def qkv(x, gain, weights, table, shard, n):
    tokens, width = x.shape
    fsdp, padded, _ = weights.shape
    return pl.pallas_call(
        functools.partial(qkv_kernel, shard),
        grid=(n // 2,),
        in_specs=[
            pl.BlockSpec((tokens, width), lambda i: (0, 0)),
            pl.BlockSpec((1, width), lambda i: (0, 0)),
            pl.BlockSpec((fsdp, padded, 2 * PACK), lambda i: (0, 0, i)),
            pl.BlockSpec((tokens, 256), lambda i: (0, 0)),
        ],
        out_specs=[
            pl.BlockSpec((2, tokens, PACK), lambda i: (i, 0, 0)),
            pl.BlockSpec((tokens, width), lambda i: (0, 0)),
        ],
        out_shape=[
            jax.ShapeDtypeStruct((n, tokens, PACK), BF16),
            jax.ShapeDtypeStruct((tokens, width), BF16),
        ],
        compiler_params=params(),
        cost_estimate=cost(2 * tokens * width * n * PACK, 8e6),
        name="qkv",
    )(x, gain, weights, table)


def pair_keys(kv):
    other = pltpu.roll(kv, 64, 1)
    low = lane_iota(kv.shape) < 64
    return jnp.where(low, kv, other), jnp.where(low, other, kv)


def stack_heads(q):
    low = lane_iota(q.shape) < 64
    zero = jnp.zeros_like(q)
    return jnp.concatenate([jnp.where(low, q, zero), jnp.where(low, zero, q)], 0)


def fold_heads(stacked):
    rows = stacked.shape[0] // 2
    return jnp.where(lane_iota((rows, 128)) < 64, stacked[:rows], stacked[rows:])


def query_rows(ends_ref, block, length):
    half = length // 2
    lanes = lane_iota((1, 2 * BLK))
    index = block * BLK + jnp.where(lanes < BLK, lanes, lanes - BLK)
    position = jnp.where(index < half, index, length + half - 1 - index)
    start = jnp.zeros_like(position)
    for j in range(3):
        end = ends_ref[j]
        start = jnp.where(position >= end, jnp.maximum(start, end), start)
    return position, start


def key_position(kb, length):
    half = length // 2
    index = kb * BLK + row_iota((BLK, 1))
    return jnp.where(index < half, index, length + half - 1 - index)


def block_loop(block, per_half, body, init):
    late = block >= per_half
    inner = jnp.where(late, block - per_half, block)
    count = jnp.where(late, 2 * per_half - inner, inner + 1)

    def step(j, carry):
        kb = jnp.where(late & (j >= per_half), inner + j, j)
        return body(kb, carry)

    return lax.fori_loop(0, count, step, init)


def load_package(pack_ref, c, h):
    return pack_ref[c, h].astype(F32)


def attn_forward_kernel(length, ends_ref, q_ref, pack_ref, out_ref, lse_ref, full_ref, keys, values_t, acc):
    block = pl.program_id(0)
    half = length // 2
    n, _, rows, _ = pack_ref.shape

    @pl.when(block == 0)
    def _():
        for h in range(2):
            for c in range(n):
                kk, vv = pair_keys(pack_ref[c, h, :, 128:256].astype(F32))
                at = h * half + c * rows
                keys[at : at + rows, :] = kk.astype(BF16)
                if rows % 128 == 0:
                    values_t[:, at : at + rows] = jnp.transpose(vv).astype(BF16)
        if rows % 128 != 0:
            for h in range(2):
                for c in range(0, n, 2):
                    pair = jnp.concatenate([pack_ref[c, h, :, 128:256], pack_ref[c + 1, h, :, 128:256]], 0)
                    _, vv = pair_keys(pair.astype(F32))
                    at = h * half + c * rows
                    values_t[:, at : at + 2 * rows] = jnp.transpose(vv).astype(BF16)

    q = q_ref[...].reshape(BLK, PACK)[:, :128]
    q2 = stack_heads(q)
    position, start = query_rows(ends_ref, block, length)
    acc[...] = jnp.zeros_like(acc)

    def body(kb, carry):
        peak, total = carry
        at = pl.multiple_of(kb * BLK, BLK)
        scores = dot(keys[pl.ds(at, BLK), :], q2, NT) * ATTN_SCALE
        where = key_position(kb, length)
        scores = jnp.where((where <= position) & (where >= start), scores, MASKED)
        new_peak = jnp.maximum(peak, jnp.max(scores, 0, keepdims=True))
        weights = jnp.exp(scores - new_peak)
        fade = jnp.exp(peak - new_peak)
        total = total * fade + jnp.sum(weights, 0, keepdims=True)
        acc[...] = acc[...] * fade + dot(values_t[:, pl.ds(at, BLK)], weights.astype(BF16))
        return new_peak, total

    init = (jnp.full((1, 2 * BLK), MASKED, F32), jnp.zeros((1, 2 * BLK), F32))
    peak, total = block_loop(block, half // BLK, body, init)
    result = acc[...] / total
    full_ref[0] = result
    lse_ref[0] = peak + jnp.log(total)
    folded = fold_heads(jnp.transpose(result)).astype(BF16)
    out_ref[...] = folded.reshape(out_ref.shape)


def attn_forward(ends, packs, length):
    n, _, rows, _ = packs.shape
    blocks, per = length // BLK, BLK // rows
    per_half = blocks // 2
    tiles = lambda i, ends: (lax.rem(i, per_half), i // per_half, 0, 0)
    return pl.pallas_call(
        functools.partial(attn_forward_kernel, length),
        grid_spec=pltpu.PrefetchScalarGridSpec(
            num_scalar_prefetch=1,
            grid=(blocks,),
            in_specs=[
                pl.BlockSpec((per, 1, rows, PACK), tiles),
                pl.BlockSpec(packs.shape, lambda i, ends: (0, 0, 0, 0)),
            ],
            out_specs=[
                pl.BlockSpec((per, 1, rows, 128), tiles),
                pl.BlockSpec((1, 1, 2 * BLK), lambda i, ends: (i, 0, 0)),
                pl.BlockSpec((1, 128, 2 * BLK), lambda i, ends: (i, 0, 0)),
            ],
            scratch_shapes=[
                pltpu.VMEM((length, 128), BF16),
                pltpu.VMEM((128, length), BF16),
                pltpu.VMEM((128, 2 * BLK), F32),
            ],
        ),
        out_shape=[
            jax.ShapeDtypeStruct((n, 2, rows, 128), BF16),
            jax.ShapeDtypeStruct((blocks, 1, 2 * BLK), F32),
            jax.ShapeDtypeStruct((blocks, 128, 2 * BLK), F32),
        ],
        compiler_params=params(),
        cost_estimate=cost(1.5e10, 6e6),
        name="attn_forward",
    )(ends, packs, packs)


def attn_backward_kernel(length, ends_ref, q_ref, g_ref, pack_ref, lse_ref, full_ref, table_ref, out_ref, keys, values, keys_t, grad_q, grad_k, grad_v, acc):
    block = pl.program_id(0)
    half = length // 2
    n, _, rows, _ = pack_ref.shape

    @pl.when(block == 0)
    def _():
        for h in range(2):
            for c in range(n):
                kk, vv = pair_keys(pack_ref[c, h, :, 128:256].astype(F32))
                at = h * half + c * rows
                keys[at : at + rows, :] = kk.astype(BF16)
                values[at : at + rows, :] = vv.astype(BF16)
        for b in range(length // BLK):
            keys_t[:, b * BLK : (b + 1) * BLK] = jnp.transpose(keys[b * BLK : (b + 1) * BLK, :].astype(F32)).astype(BF16)
        grad_k[...] = jnp.zeros_like(grad_k)
        grad_v[...] = jnp.zeros_like(grad_v)

    q2 = stack_heads(q_ref[...].reshape(BLK, PACK)[:, :128])
    g2 = stack_heads(g_ref[...].reshape(BLK, 128))
    position, start = query_rows(ends_ref, block, length)
    lse = lse_ref[0]
    delta = jnp.sum(jnp.transpose(g2.astype(F32)) * full_ref[0], 0, keepdims=True)
    acc[...] = jnp.zeros_like(acc)

    def body(kb, carry):
        at = pl.multiple_of(kb * BLK, BLK)
        scores = dot(keys[pl.ds(at, BLK), :], q2, NT) * ATTN_SCALE
        where = key_position(kb, length)
        probs = jnp.where((where <= position) & (where >= start), jnp.exp(scores - lse), 0.0)
        grad_probs = dot(values[pl.ds(at, BLK), :], g2, NT)
        grad_scores = (probs * (grad_probs - delta)).astype(BF16)
        acc[...] += dot(keys_t[:, pl.ds(at, BLK)], grad_scores)
        grad_k[pl.ds(at, BLK), :] += dot(grad_scores, q2)
        grad_v[pl.ds(at, BLK), :] += dot(probs.astype(BF16), g2)
        return carry

    block_loop(block, half // BLK, body, 0)
    grad_q[pl.ds(pl.multiple_of(block * BLK, BLK), BLK), :] = fold_heads(jnp.transpose(acc[...]))

    @pl.when(block == length // BLK - 1)
    def _():
        for h in range(2):
            for c in range(n):
                at = slice(h * half + c * rows, h * half + (c + 1) * rows)
                kk = grad_k[at, :]
                vv = grad_v[at, :]
                kk = (kk + pltpu.roll(kk, 64, 1)) * ATTN_SCALE
                vv = vv + pltpu.roll(vv, 64, 1)
                both = jnp.where(lane_iota(kk.shape) < 64, kk, vv)
                package = jnp.concatenate([grad_q[at, :] * ATTN_SCALE, both], -1)
                out_ref[c, h] = turn(package, table_ref[at, :], -1.0).astype(BF16)


def attn_backward(ends, packs, grads, lse, full, table, length):
    n, _, rows, _ = packs.shape
    blocks, per = length // BLK, BLK // rows
    per_half = blocks // 2
    tiles = lambda i, ends: (lax.rem(i, per_half), i // per_half, 0, 0)
    return pl.pallas_call(
        functools.partial(attn_backward_kernel, length),
        grid_spec=pltpu.PrefetchScalarGridSpec(
            num_scalar_prefetch=1,
            grid=(blocks,),
            in_specs=[
                pl.BlockSpec((per, 1, rows, PACK), tiles),
                pl.BlockSpec((per, 1, rows, 128), tiles),
                pl.BlockSpec(packs.shape, lambda i, ends: (0, 0, 0, 0)),
                pl.BlockSpec((1, 1, 2 * BLK), lambda i, ends: (i, 0, 0)),
                pl.BlockSpec((1, 128, 2 * BLK), lambda i, ends: (i, 0, 0)),
                pl.BlockSpec(table.shape, lambda i, ends: (0, 0)),
            ],
            out_specs=pl.BlockSpec(packs.shape, lambda i, ends: (0, 0, 0, 0)),
            scratch_shapes=[
                pltpu.VMEM((length, 128), BF16),
                pltpu.VMEM((length, 128), BF16),
                pltpu.VMEM((128, length), BF16),
                pltpu.VMEM((length, 128), F32),
                pltpu.VMEM((length, 128), F32),
                pltpu.VMEM((length, 128), F32),
                pltpu.VMEM((128, 2 * BLK), F32),
            ],
        ),
        out_shape=jax.ShapeDtypeStruct(packs.shape, BF16),
        compiler_params=params(),
        cost_estimate=cost(3e10, 8e6),
        name="attn_backward",
    )(ends, packs, grads, packs, lse, full, table)


def middle_kernel(attn_ref, wo_ref, x_ref, gain_ref, middle_ref, h_ref):
    total = None
    for c in range(attn_ref.shape[0]):
        part = dot(attn_ref[c], wo_ref[c])
        total = part if total is None else total + part
    middle = x_ref[...] + RESIDUAL * total
    middle_ref[...] = middle
    normed, _ = norm_parts(middle)
    h_ref[...] = (normed * gain_ref[...]).astype(BF16)


def middle_step(attn, wo, x, gain):
    tokens, width = x.shape
    return pl.pallas_call(
        middle_kernel,
        out_shape=[jax.ShapeDtypeStruct((tokens, width), F32), jax.ShapeDtypeStruct((tokens, width), BF16)],
        compiler_params=params(),
        cost_estimate=cost(2 * tokens * width * width, 5e6),
        name="middle",
    )(attn, wo, x, gain)


def own_row(table, row):
    return jnp.sum(jnp.where(row_iota(table.shape) == row, table, 0.0), 0, keepdims=True)


def one_hot(slots, first, number, capp):
    tokens = slots.shape[1]
    order = row_iota((capp, tokens)).astype(F32)
    return [(order == own_row(slots, first + j)).astype(F32) for j in range(number)]


def gather_kernel(number, capp, first_ref, h_ref, cx_ref, wrt_ref, x_ref, g_ref, gate_ref):
    tokens = h_ref.shape[1]
    first = first_ref[0]
    h = h_ref[0]
    slots = cx_ref[0, tokens:, :tokens].astype(F32)
    logits = dot(wrt_ref[...], h, NT)[:EXPERTS, :]
    raw = jnp.exp(logits - jnp.max(logits, 0, keepdims=True))
    router = raw / jnp.sum(raw, 0, keepdims=True)
    hots = one_hot(slots, first, number, capp)
    places = jnp.concatenate(hots, 0).astype(BF16)
    rows = dot(places, h).astype(BF16)
    grads = dot(places, cx_ref[0, :tokens, :]).astype(BF16)
    for j in range(number):
        at = slice(j * capp, (j + 1) * capp)
        x_ref[j, 0] = rows[at]
        g_ref[j, 0] = grads[at]
        gate = jnp.sum(hots[j] * own_row(router, first + j), 1, keepdims=True)
        gate_ref[j, 0] = jnp.broadcast_to(gate, (capp, 128))


def gather_rows(first, hs, cxs, wrt, number, capp):
    nb, tokens, width = hs.shape
    return pl.pallas_call(
        functools.partial(gather_kernel, number, capp),
        grid_spec=pltpu.PrefetchScalarGridSpec(
            num_scalar_prefetch=1,
            grid=(nb,),
            in_specs=[
                pl.BlockSpec((1, tokens, width), lambda b, f: (b, 0, 0)),
                pl.BlockSpec((1, tokens + EXPERTS, width), lambda b, f: (b, 0, 0)),
                pl.BlockSpec(wrt.shape, lambda b, f: (0, 0)),
            ],
            out_specs=[
                pl.BlockSpec((number, 1, capp, width), lambda b, f: (0, b, 0, 0)),
                pl.BlockSpec((number, 1, capp, width), lambda b, f: (0, b, 0, 0)),
                pl.BlockSpec((number, 1, capp, 128), lambda b, f: (0, b, 0, 0)),
            ],
        ),
        out_shape=[
            jax.ShapeDtypeStruct((number, nb, capp, width), BF16),
            jax.ShapeDtypeStruct((number, nb, capp, width), BF16),
            jax.ShapeDtypeStruct((number, nb, capp, 128), F32),
        ],
        compiler_params=params(),
        cost_estimate=cost(4 * nb * number * capp * tokens * width, 2e7),
        name="gather_rows",
    )(first, hs, cxs, wrt)


PIECE = 512


def expert_kernel(base_ref, x_ref, g_ref, gate_ref, wg_ref, wu_ref, wd_ref, piece_ref, out_ref, rows_ref, dg_ref):
    x = x_ref[0]
    gate = gate_ref[0][:, :1]
    grad_ffn = RESIDUAL * g_ref[0].astype(F32)
    go = (gate * grad_ffn).astype(BF16)
    part = wg_ref.shape[2] // 2
    out = rows = None
    for chunk in range(2):
        at = slice(chunk * part, (chunk + 1) * part)
        wg, wu, wd = wg_ref[0, :, at], wu_ref[0, :, at], wd_ref[0, at, :]
        pre_gate = dot(x, wg)
        pre_up = dot(x, wu)
        sig = jax.nn.sigmoid(pre_gate)
        hidden = (pre_gate * sig * pre_up).astype(BF16)
        out_part = dot(hidden, wd)
        grad_hidden = dot(go, wd, NT)
        grad_gate = (grad_hidden * pre_up * sig * (1.0 + pre_gate * (1.0 - sig))).astype(BF16)
        grad_up = (grad_hidden * pre_gate * sig).astype(BF16)
        row_part = dot(grad_gate, wg, NT) + dot(grad_up, wu, NT)
        dwg = dot(x, grad_gate, TN).astype(BF16)
        dwu = dot(x, grad_up, TN).astype(BF16)
        dwd = dot(hidden, go, TN).astype(BF16)
        for half in range(2):
            side = slice(half * PIECE, (half + 1) * PIECE)
            piece_ref[0, half, :, at] = dwg[side]
            piece_ref[0, 2 + half, :, at] = dwu[side]
            piece_ref[0, 4 + half, at, :] = dwd[:, side]
        out = out_part if out is None else out + out_part
        rows = row_part if rows is None else rows + row_part
    out = out.astype(BF16).astype(F32)
    out_ref[0] = (gate * out).astype(BF16)
    rows_ref[0] = rows.astype(BF16)
    grad = jnp.sum(grad_ffn * out, 1, keepdims=True)
    dg_ref[0] = jnp.broadcast_to(grad, dg_ref.shape[1:])


def expert_step(base, xs, gs, gates, w_gate, w_up, w_down):
    number, rows, width = xs.shape
    ff = w_gate.shape[2]
    row = lambda e, b: (e, 0, 0)
    weight = lambda e, b: (b[0] + e, 0, 0)
    return pl.pallas_call(
        expert_kernel,
        grid_spec=pltpu.PrefetchScalarGridSpec(
            num_scalar_prefetch=1,
            grid=(number,),
            in_specs=[
                pl.BlockSpec((1, rows, width), row),
                pl.BlockSpec((1, rows, width), row),
                pl.BlockSpec((1, rows, 128), row),
                pl.BlockSpec((1, width, ff), weight),
                pl.BlockSpec((1, width, ff), weight),
                pl.BlockSpec((1, ff, width), weight),
            ],
            out_specs=[
                pl.BlockSpec((1, 6, PIECE, PIECE), lambda e, b: (e, 0, 0, 0)),
                pl.BlockSpec((1, rows, width), row),
                pl.BlockSpec((1, rows, width), row),
                pl.BlockSpec((1, rows, 128), row),
            ],
        ),
        out_shape=[
            jax.ShapeDtypeStruct((number, 6, PIECE, PIECE), BF16),
            jax.ShapeDtypeStruct((number, rows, width), BF16),
            jax.ShapeDtypeStruct((number, rows, width), BF16),
            jax.ShapeDtypeStruct((number, rows, 128), F32),
        ],
        compiler_params=params(60),
        cost_estimate=cost(18 * number * rows * width * ff, 5e7),
        name="expert_step",
    )(base, xs, gs, gates, w_gate, w_up, w_down)


def combine_kernel(number, capp, first_ref, slot_ref, outs, rows, grads, y_ref, gx_ref):
    tokens = y_ref.shape[1]
    width = y_ref.shape[2]
    first = first_ref[0]
    slots = slot_ref[0][:, :tokens].astype(F32)
    hots = one_hot(slots, first, number, capp)
    places = jnp.concatenate(hots, 0).astype(BF16)
    y_ref[0] = dot(places, outs[:, 0].reshape(number * capp, width), TN).astype(BF16)
    gx_ref[0, :tokens] = dot(places, rows[:, 0].reshape(number * capp, width), TN).astype(BF16)
    extra = jnp.zeros((EXPERTS, 2 * tokens), F32)
    for j in range(number):
        grad = jnp.sum(hots[j] * grads[j, 0][:, :1], 0, keepdims=True)
        high = grad.astype(BF16).astype(F32)
        both = jnp.concatenate([high, grad - high], 1)
        extra = jnp.where(row_iota(extra.shape) == first + j, both, extra)
    rest = jnp.zeros((EXPERTS, width - 2 * tokens), F32)
    gx_ref[0, tokens:] = jnp.concatenate([extra, rest], 1).astype(BF16)


def combine(first, cxs, outs, rows, grads, tokens, capp):
    number = outs.shape[0]
    nb, _, width = cxs.shape
    split = lambda a: a.reshape(number, nb, capp, a.shape[-1])
    wide = pl.BlockSpec((number, 1, capp, width), lambda b, f: (0, b, 0, 0))
    thin = pl.BlockSpec((number, 1, capp, 128), lambda b, f: (0, b, 0, 0))
    return pl.pallas_call(
        functools.partial(combine_kernel, number, capp),
        grid_spec=pltpu.PrefetchScalarGridSpec(
            num_scalar_prefetch=1,
            grid=(nb,),
            in_specs=[pl.BlockSpec((1, EXPERTS, width), lambda b, f: (b, tokens // EXPERTS, 0))] + [wide, wide, thin],
            out_specs=[
                pl.BlockSpec((1, tokens, width), lambda b, f: (b, 0, 0)),
                pl.BlockSpec((1, tokens + EXPERTS, width), lambda b, f: (b, 0, 0)),
            ],
        ),
        out_shape=[
            jax.ShapeDtypeStruct((nb, tokens, width), BF16),
            jax.ShapeDtypeStruct((nb, tokens + EXPERTS, width), BF16),
        ],
        compiler_params=params(),
        cost_estimate=cost(4 * nb * number * capp * tokens * width, 2e7),
        name="combine",
    )(first, cxs, split(outs), split(rows), split(grads))


def home_kernel(gx_ref, h_ref, middle_ref, cot_ref, wr_ref, wo_ref, gain_ref, attn_ref, grad_middle_ref, dwo_ref, ga_ref, dwr_ref, dgain_ref):
    tokens, width = h_ref.shape
    h = h_ref[...]
    gain = gain_ref[...]
    extra = gx_ref[tokens:, :].astype(F32)
    grad_router = extra[:, :tokens] + extra[:, tokens : 2 * tokens]
    grad_router = jnp.transpose(jnp.concatenate([grad_router, jnp.zeros((128 - EXPERTS, tokens), F32)], 0))
    logits = dot(h, wr_ref[...])
    logits = jnp.where(lane_iota(logits.shape) < EXPERTS, logits, MASKED)
    raw = jnp.exp(logits - jnp.max(logits, -1, keepdims=True))
    router = raw / jnp.sum(raw, -1, keepdims=True)
    grad_logits = (router * (grad_router - jnp.sum(router * grad_router, -1, keepdims=True))).astype(BF16)
    dwr_ref[...] = dot(h, grad_logits, TN).astype(BF16)
    grad_h = gx_ref[:tokens, :].astype(F32) + dot(grad_logits, wr_ref[...], NT)
    normed, scale = norm_parts(middle_ref[...])
    dgain_ref[...] = jnp.sum(grad_h * normed, 0, keepdims=True)
    grad_middle = cot_ref[...] + norm_back(grad_h * gain, normed, scale)
    grad_middle_ref[...] = grad_middle
    grad_branch = (RESIDUAL * grad_middle).astype(BF16)
    for c in range(attn_ref.shape[0]):
        dwo_ref[c] = dot(attn_ref[c], grad_branch, TN).astype(BF16)
        ga_ref[c] = dot(grad_branch, wo_ref[c], NT).astype(BF16)


def home_step(gx, h, middle, cot, wr, wo, gain, attn):
    tokens, width = h.shape
    n = attn.shape[0]
    return pl.pallas_call(
        home_kernel,
        out_shape=[
            jax.ShapeDtypeStruct((tokens, width), F32),
            jax.ShapeDtypeStruct((n, 128, width), BF16),
            jax.ShapeDtypeStruct((n, tokens, 128), BF16),
            jax.ShapeDtypeStruct((width, 128), BF16),
            jax.ShapeDtypeStruct((1, width), F32),
        ],
        compiler_params=params(),
        cost_estimate=cost(4 * tokens * width * width, 1e7),
        name="home_step",
    )(gx, h, middle, cot, wr, wo, gain, attn)


def final_kernel(shard, grads_ref, w_ref, h_ref, x_ref, gain_ref, grad_middle_ref, dw_ref, grad_x_ref, dgain_ref, total):
    c = pl.program_id(0)
    g = grads_ref[0]
    dw_ref[...] = dot(h_ref[...], g, TN).astype(BF16)

    @pl.when(c == 0)
    def _():
        total[...] = jnp.zeros_like(total)

    for f in range(w_ref.shape[0]):
        total[:, f * shard : (f + 1) * shard] += dot(g, w_ref[f, :shard, :], NT)

    @pl.when(c == pl.num_programs(0) - 1)
    def _():
        normed, scale = norm_parts(x_ref[...])
        grad_h = total[...]
        dgain_ref[...] = jnp.sum(grad_h * normed, 0, keepdims=True)
        grad_x_ref[...] = grad_middle_ref[...] + norm_back(grad_h * gain_ref[...], normed, scale)


def final_step(grads, weights, h, x, gain, grad_middle, shard):
    n, tokens, _ = grads.shape
    width = x.shape[1]
    fsdp, padded, _ = weights.shape
    same = lambda c: (0, 0)
    return pl.pallas_call(
        functools.partial(final_kernel, shard),
        grid=(n,),
        in_specs=[
            pl.BlockSpec((1, tokens, PACK), lambda c: (c, 0, 0)),
            pl.BlockSpec((fsdp, padded, PACK), lambda c: (0, 0, c)),
            pl.BlockSpec((tokens, width), same),
            pl.BlockSpec((tokens, width), same),
            pl.BlockSpec((1, width), same),
            pl.BlockSpec((tokens, width), same),
        ],
        out_specs=[
            pl.BlockSpec((width, PACK), lambda c: (0, c)),
            pl.BlockSpec((tokens, width), same),
            pl.BlockSpec((1, width), same),
        ],
        out_shape=[
            jax.ShapeDtypeStruct((width, n * PACK), BF16),
            jax.ShapeDtypeStruct((tokens, width), F32),
            jax.ShapeDtypeStruct((1, width), F32),
        ],
        scratch_shapes=[pltpu.VMEM((tokens, width), F32)],
        compiler_params=params(),
        cost_estimate=cost(4 * tokens * width * n * PACK, 1.2e7),
        name="final_step",
    )(grads, weights, h, x, gain, grad_middle)


def widen_kernel(by_rows, index_ref, own_ref, other_ref, out_ref):
    def write(ref):
        for half in range(2):
            at = slice(half * PIECE, (half + 1) * PIECE)
            if by_rows:
                out_ref[0, at, :] = ref[half].astype(F32)
            else:
                out_ref[0, :, at] = ref[half].astype(F32)

    @pl.when(pl.program_id(0) == 0)
    def _():
        write(own_ref)

    @pl.when(pl.program_id(0) == 1)
    def _():
        write(other_ref)


def widen(index, own, other, matrix, shape):
    number = own.shape[0] // 6
    by_rows = shape[1] == 2 * PIECE
    piece = lambda e: 3 * e + matrix
    return pl.pallas_call(
        functools.partial(widen_kernel, by_rows),
        grid_spec=pltpu.PrefetchScalarGridSpec(
            num_scalar_prefetch=1,
            grid=(2, number),
            in_specs=[
                pl.BlockSpec((2, PIECE, PIECE), lambda s, e, at: (jnp.where(s == 0, piece(e), piece(number - 1)), 0, 0)),
                pl.BlockSpec((2, PIECE, PIECE), lambda s, e, at: (jnp.where(s == 0, piece(0), piece(e)), 0, 0)),
            ],
            out_specs=pl.BlockSpec((1,) + tuple(shape[1:]), lambda s, e, at: (at[s] + e, 0, 0)),
        ),
        out_shape=jax.ShapeDtypeStruct(shape, F32),
        compiler_params=params(),
        cost_estimate=cost(0, 6 * shape[0] * shape[1] * shape[2]),
        name="widen",
    )(index, own, other)


def swap(value, axis, bit):
    size = lax.axis_size(axis)
    return lax.ppermute(value, axis, [(i, i ^ bit) for i in range(size)])


def group_bits(fsdp):
    bits = [("fsdp", 1 << b) for b in range(1, fsdp.bit_length() - 1)]
    return bits + [("ctx", 1), ("fsdp", 1)]


def group_gather(value, bits):
    stacked = value[None]
    for axis, bit in bits:
        stacked = jnp.concatenate([stacked, swap(stacked, axis, bit)], 0)
    return stacked


def group_reduce(stacked, bits):
    for axis, bit in reversed(bits):
        half = stacked.shape[0] // 2
        arrived = swap(stacked[half:], axis, bit)
        stacked = (stacked[:half].astype(F32) + arrived.astype(F32)).astype(stacked.dtype)
    return stacked[0]


def line_sum(value, ctx):
    pairs = ctx // 2
    if pairs != 4:
        bit = 2
        while bit < ctx:
            value = value + swap(value, "ctx", bit)
            bit *= 2
        return value
    at = lambda z, y: 2 * z + y
    inward = [(at(0, y), at(1, y)) for y in range(2)] + [(at(3, y), at(2, y)) for y in range(2)]
    across = [(at(1, y), at(2, y)) for y in range(2)] + [(at(2, y), at(1, y)) for y in range(2)]
    outward = [(b, a) for a, b in inward]
    value = value + lax.ppermute(value, "ctx", inward)
    value = value + lax.ppermute(value, "ctx", across)
    arrived = lax.ppermute(value, "ctx", outward)
    z = lax.axis_index("ctx") // 2
    return jnp.where((z == 0) | (z == 3), arrived, value)


MESH = pl.DeviceIdType.MESH


def flip(index, bit):
    return jnp.where((index // bit) % 2 == 0, index + bit, index - bit)


def send(src, dst, send_sem, recv_sem, device):
    return pltpu.make_async_remote_copy(src_ref=src, dst_ref=dst, send_sem=send_sem, recv_sem=recv_sem, device_id=device, device_id_type=MESH)


def neighbours():
    ctx, fsdp = lax.axis_index("ctx"), lax.axis_index("fsdp")
    side, across = flip(ctx, 1), flip(fsdp, 2)
    core = {"fsdp": flip(fsdp, 1)}
    return core, [{"fsdp": across}, {"ctx": side}, {"ctx": side, "fsdp": across}]


def greet(devices):
    barrier = pltpu.get_barrier_semaphore()
    for device in devices:
        pl.semaphore_signal(barrier, inc=1, device_id=device, device_id_type=MESH)
    pl.semaphore_wait(barrier, len(devices))


def others(n):
    ctx = lax.axis_index("ctx")
    return [lax.rem(ctx + d, n) for d in range(1, n)]


def exchange_start(src, dst, send_sems, recv_sems, local_sem, n):
    ctx = lax.axis_index("ctx")
    for d, c in enumerate(others(n)):
        send(src.at[c], dst.at[ctx], send_sems.at[d], recv_sems.at[d], {"ctx": c}).start()
    pltpu.make_async_copy(src.at[ctx], dst.at[ctx], local_sem).start()


def exchange_wait(src, dst, send_sems, recv_sems, local_sem, n, arrived=None):
    ctx = lax.axis_index("ctx")
    pltpu.make_async_copy(src.at[ctx], dst.at[ctx], local_sem).wait()
    if arrived is not None:
        arrived(ctx)
    for d in range(n - 1):
        source = lax.rem(ctx + n - 1 - d, n)
        send(src.at[source], dst.at[source], send_sems.at[d], recv_sems.at[d], {"ctx": source}).wait_recv()
        if arrived is not None:
            arrived(source)
    for d, c in enumerate(others(n)):
        send(src.at[c], dst.at[ctx], send_sems.at[d], recv_sems.at[d], {"ctx": c}).wait_send()


def front_kernel(n, cap, packed_ref, wo_part_ref, wr_part_ref, x_ref, table_ref, routes_ref, cot_ref, packs_ref, h_ref, weights_ref, wo_ref, wr_ref, cxs_ref, gains_ref, wall, cx, normed_ref, total, out, exch_send, exch_recv, full_send, full_recv, x_send, x_recv, y_send, y_recv, xs_send, xs_recv, ys_send, ys_recv, cx_send, cx_recv, fwd_send, fwd_recv, local_sems):
    width = x_ref.shape[1]
    shard = width // 4
    ctx, fsdp = lax.axis_index("ctx"), lax.axis_index("fsdp")
    parity = lax.rem(ctx, 2)
    core, group = neighbours()
    far, near = group[0], group[1]
    sibling, distant = flip(fsdp, 1), flip(fsdp, 2)
    other = flip(distant, 1)
    greet([core, far, group[2]] + [{"ctx": c} for c in others(n)])

    half_rows = packed_ref.shape[0] // 2
    low_rows = half_rows // 32 * 16

    def cut(k, part):
        if k == 0:
            return pl.ds(pl.multiple_of(part * half_rows, 16), low_rows)
        if k == 1:
            return pl.ds(pl.multiple_of(part * half_rows + low_rows, 16), half_rows - low_rows)
        if k == 2:
            return pl.ds(part, 1)
        return pl.ds(pl.multiple_of(part * (shard // 2), 16), shard // 2)

    sources = [packed_ref, packed_ref, wo_part_ref, wr_part_ref]
    targets = [wall, wall, wo_ref, wr_ref]
    wholes = [(packed_ref, wall), (wo_part_ref, wo_ref), (wr_part_ref, wr_ref)]

    def whole(i):
        src, dst = wholes[i]
        return send(src, dst.at[fsdp], full_send.at[i], full_recv.at[i], core)

    def own(i):
        src, dst = wholes[i]
        return pltpu.make_async_copy(src, dst.at[fsdp], local_sems.at[i])

    def to_far(k):
        return send(sources[k].at[cut(k, parity)], targets[k].at[fsdp, cut(k, parity)], x_send.at[k], x_recv.at[k], far)

    def pass_on(k, part, sems, device):
        ref = targets[k].at[distant, cut(k, part)]
        return send(ref, ref, sems[0].at[k], sems[1].at[k], device)

    def far_arrived(k):
        ref = targets[k].at[distant, cut(k, parity)]
        send(ref, ref, x_send.at[k], x_recv.at[k], far).wait_recv()
        pass_on(k, parity, (y_send, y_recv), near).start()
        pass_on(k, parity, (xs_send, xs_recv), core).start()

    def near_arrived(k):
        pass_on(k, 1 - parity, (y_send, y_recv), near).wait_recv()
        pass_on(k, 1 - parity, (ys_send, ys_recv), core).start()

    def core_arrived(k):
        for part, sems in ((parity, (xs_send, xs_recv)), (1 - parity, (ys_send, ys_recv))):
            ref = targets[k].at[other, cut(k, part)]
            send(ref, ref, sems[0].at[k], sems[1].at[k], core).wait_recv()

    own(0).start()
    to_far(0).start()
    to_far(1).start()
    whole(0).start()

    prep_kernel(cap, routes_ref, cot_ref, cx)
    send(cx, cxs_ref.at[2], cx_send.at[1], cx_recv.at[1], near).start()
    send(cx, cxs_ref.at[4], cx_send.at[3], cx_recv.at[3], core).start()
    pltpu.make_async_copy(cx, cxs_ref.at[0], local_sems.at[3]).start()
    normed, _ = norm_parts(x_ref[...])
    normed_ref[...] = normed

    def project(block, begin):
        at = pl.ds(pl.multiple_of(block * shard, shard), shard)
        gain = wall[block, shard : shard + 16, :shard].astype(F32)
        gains_ref[:, at] = gain
        h = (normed_ref[:, at] * gain[:1]).astype(BF16)
        h_ref[:, at] = h
        part = dot(h, wall[block, :shard, :])
        total[...] = part if begin else total[...] + part

    own(0).wait()
    project(fsdp, True)
    ref = wall.at[sibling]
    send(ref, ref, full_send.at[0], full_recv.at[0], core).wait_recv()
    project(sibling, False)
    far_arrived(0)
    far_arrived(1)
    for i in (1, 2):
        own(i).start()
        whole(i).start()
        to_far(i + 1).start()
    send(cx, cxs_ref.at[1], cx_send.at[0], cx_recv.at[0], far).start()
    send(cx, cxs_ref.at[3], cx_send.at[2], cx_recv.at[2], group[2]).start()
    near_arrived(0)
    near_arrived(1)
    project(distant, False)
    core_arrived(0)
    core_arrived(1)
    project(other, False)
    keep = pltpu.make_async_copy(wall, weights_ref, local_sems.at[4])
    keep.start()
    for c in range(n):
        out[c] = turn(total[:, c * PACK : (c + 1) * PACK], table_ref[...], 1.0).astype(BF16)
    exchange = (out, packs_ref, exch_send, exch_recv, local_sems.at[5], n)
    exchange_start(*exchange)

    def forward(i):
        return send(cxs_ref.at[1 + i], cxs_ref.at[5 + i], fwd_send.at[i], fwd_recv.at[i], core)

    for k in (2, 3):
        far_arrived(k)
    for i, device in ((1, near), (0, far), (2, group[2])):
        send(cx, cxs_ref.at[1 + i], cx_send.at[i], cx_recv.at[i], device).wait_recv()
        forward(i).start()
    for k in (2, 3):
        near_arrived(k)
    for k in (2, 3):
        core_arrived(k)
    for i in (1, 2):
        src, dst = wholes[i]
        ref = dst.at[sibling]
        send(ref, ref, full_send.at[i], full_recv.at[i], core).wait_recv()
        own(i).wait()
    send(cx, cxs_ref.at[4], cx_send.at[3], cx_recv.at[3], core).wait_recv()
    for i in range(3):
        forward(i).wait_recv()
    exchange_wait(*exchange)
    for i in range(3):
        whole(i).wait_send()
        forward(i).wait_send()
    for k in range(4):
        to_far(k).wait_send()
        pass_on(k, parity, (y_send, y_recv), near).wait_send()
        pass_on(k, parity, (xs_send, xs_recv), core).wait_send()
        pass_on(k, 1 - parity, (ys_send, ys_recv), core).wait_send()
    for i, (slot, device) in enumerate(((1, far), (2, near), (3, group[2]), (4, core))):
        send(cx, cxs_ref.at[slot], cx_send.at[i], cx_recv.at[i], device).wait_send()
    pltpu.make_async_copy(cx, cxs_ref.at[0], local_sems.at[3]).wait()
    keep.wait()


def front(packed, wo_part, wr_part, x, table, routes, cot, cap, n):
    tokens, width = x.shape
    hbm, vmem = pl.BlockSpec(memory_space=pl.ANY), pl.BlockSpec(memory_space=pltpu.VMEM)
    dma = lambda k: pltpu.SemaphoreType.DMA((k,))
    shaped = lambda shape, dtype=BF16: jax.ShapeDtypeStruct(shape, dtype)
    cx_shape = (tokens + EXPERTS, width)
    return pl.pallas_call(
        functools.partial(front_kernel, n, cap),
        in_specs=[hbm, hbm, hbm, vmem, vmem, vmem, vmem],
        out_specs=[hbm, vmem, hbm, hbm, hbm, hbm, vmem],
        out_shape=[
            shaped((n, tokens, PACK)),
            shaped((tokens, width)),
            shaped((4,) + packed.shape),
            shaped((4,) + wo_part.shape),
            shaped((4,) + wr_part.shape),
            shaped((8,) + cx_shape),
            shaped((16, width), F32),
        ],
        scratch_shapes=[
            pltpu.VMEM((4,) + packed.shape, BF16),
            pltpu.VMEM(cx_shape, BF16),
            pltpu.VMEM((tokens, width), F32),
            pltpu.VMEM((tokens, n * PACK), F32),
            pltpu.VMEM((n, tokens, PACK), BF16),
            dma(n - 1),
            dma(n - 1),
            dma(3),
            dma(3),
        ]
        + [dma(4)] * 10
        + [dma(3), dma(3), dma(6)],
        compiler_params=params(collective_id=1, has_side_effects=True),
        cost_estimate=cost(2e9, 5e7),
        name="front",
    )(packed, wo_part, wr_part, x, table, routes, cot)


def mid_kernel(n, number, capp, attn_ref, cxs_ref, wo_ref, wr_ref, x_ref, gain_ref, middle_ref, h_ref, kept_ref, xs_ref, gs_ref, gates_ref, arrived, hs, total, exch_send, exch_recv, hop_send, hop_recv, fwd_send, fwd_recv, local_sems):
    tokens, width = x_ref.shape
    ctx, fsdp = lax.axis_index("ctx"), lax.axis_index("fsdp")
    first = (fsdp * 2 + lax.rem(ctx, 2)) * number
    core, group = neighbours()
    greet([core, group[0], group[2]] + [{"ctx": c} for c in others(n)])
    exchange = (attn_ref, arrived, exch_send, exch_recv, local_sems.at[0], n)
    exchange_start(*exchange)
    total[...] = jnp.zeros_like(total)

    def take(c):
        total[...] += dot(arrived[c], wo_ref[c])

    exchange_wait(*exchange, take)
    keep = pltpu.make_async_copy(arrived, kept_ref, local_sems.at[1])
    keep.start()
    middle = x_ref[...] + RESIDUAL * total[...]
    middle_ref[...] = middle
    normed, _ = norm_parts(middle)
    h = (normed * gain_ref[...]).astype(BF16)
    h_ref[...] = h
    hs[0] = h

    def hop(i):
        return send(hs.at[0], hs.at[1 + i], hop_send.at[i], hop_recv.at[i], (group + [core])[i])

    def forward(i):
        return send(hs.at[1 + i], hs.at[5 + i], fwd_send.at[i], fwd_recv.at[i], core)

    for i in (2, 0, 1, 3):
        hop(i).start()

    def place(b):
        h = hs[b]
        logits = jnp.transpose(dot(h, wr_ref[...]))[:EXPERTS, :]
        raw = jnp.exp(logits - jnp.max(logits, 0, keepdims=True))
        router = raw / jnp.sum(raw, 0, keepdims=True)
        slots = cxs_ref[b, tokens:, :tokens].astype(F32)
        hots = one_hot(slots, first, number, capp)
        places = jnp.concatenate(hots, 0).astype(BF16)
        rows = dot(places, h).astype(BF16)
        grads = dot(places, cxs_ref[b, :tokens, :]).astype(BF16)
        for j in range(number):
            at = slice(j * capp, (j + 1) * capp)
            xs_ref[j, b] = rows[at]
            gs_ref[j, b] = grads[at]
            gate = jnp.sum(hots[j] * own_row(router, first + j), 1, keepdims=True)
            gates_ref[j, b] = jnp.broadcast_to(gate, (capp, 128))

    place(0)
    hop(3).wait_recv()
    place(4)
    for i in (0, 1, 2):
        hop(i).wait_recv()
        forward(i).start()
        place(1 + i)
    for i in (0, 1, 2):
        forward(i).wait_recv()
        place(5 + i)
    for i in range(4):
        hop(i).wait_send()
    for i in range(3):
        forward(i).wait_send()
    keep.wait()


def mid_step(attn, cxs, wo, wr, x, gain, number, capp, n):
    tokens, width = x.shape
    hbm, vmem = pl.BlockSpec(memory_space=pl.ANY), pl.BlockSpec(memory_space=pltpu.VMEM)
    dma = lambda k: pltpu.SemaphoreType.DMA((k,))
    shaped = lambda shape, dtype=BF16: jax.ShapeDtypeStruct(shape, dtype)
    return pl.pallas_call(
        functools.partial(mid_kernel, n, number, capp),
        in_specs=[hbm, vmem, vmem, vmem, vmem, vmem],
        out_specs=[vmem, vmem, hbm, vmem, vmem, vmem],
        out_shape=[
            shaped((tokens, width), F32),
            shaped((tokens, width)),
            shaped(attn.shape),
            shaped((number, 8, capp, width)),
            shaped((number, 8, capp, width)),
            shaped((number, 8, capp, 128), F32),
        ],
        scratch_shapes=[
            pltpu.VMEM(attn.shape, BF16),
            pltpu.VMEM((8, tokens, width), BF16),
            pltpu.VMEM((tokens, width), F32),
            dma(n - 1),
            dma(n - 1),
            dma(4),
            dma(4),
            dma(3),
            dma(3),
            dma(2),
        ],
        compiler_params=params(collective_id=2, has_side_effects=True),
        cost_estimate=cost(4e9, 5e7),
        name="mid_step",
    )(attn, cxs, wo, wr, x, gain)


def reduce_kernel(piece_ref, own_ref, other_ref, inbox, across, mine, line_send, line_recv, mid_send, mid_recv, side_send, side_recv, load, store):
    count = piece_ref.shape[0]
    ctx = lax.axis_index("ctx")
    z = ctx // 2
    middle = (z == 1) | (z == 2)
    line = {"ctx": jnp.where(z % 2 == 0, ctx + 2, ctx - 2)}
    peer = {"ctx": jnp.where(z == 1, ctx + 2, ctx - 2)}
    side = {"ctx": jnp.where(ctx % 2 == 0, ctx + 1, ctx - 1)}
    mesh_ids = pl.DeviceIdType.MESH

    def remote(src, dst, send, recv, device):
        return pltpu.make_async_remote_copy(src_ref=src, dst_ref=dst, send_sem=send, recv_sem=recv, device_id=device, device_id_type=mesh_ids)

    def send_line(src, i):
        return remote(src, inbox.at[i], line_send.at[i], line_recv.at[i], line)

    def send_mid(i):
        return remote(inbox.at[i], across.at[i], mid_send.at[i], mid_recv.at[i], peer)

    def send_side(src, i):
        return remote(src, other_ref.at[i], side_send.at[i], side_recv.at[i], side)

    def fetch(i):
        return pltpu.make_async_copy(piece_ref.at[i], mine.at[i % 2], load.at[i % 2])

    def keep(src, i):
        return pltpu.make_async_copy(src, own_ref.at[i], store.at[i])

    barrier = pltpu.get_barrier_semaphore()
    pl.semaphore_signal(barrier, inc=1, device_id=line, device_id_type=mesh_ids)
    pl.semaphore_signal(barrier, inc=1, device_id=side, device_id_type=mesh_ids)

    @pl.when(middle)
    def _():
        pl.semaphore_signal(barrier, inc=1, device_id=peer, device_id_type=mesh_ids)
        pl.semaphore_wait(barrier, 3)
        fetch(0).start()

        def tick(t, carry):
            @pl.when(t < count)
            def _():
                @pl.when(t + 1 < count)
                def _():
                    fetch(t + 1).start()

                fetch(t).wait()
                send_line(inbox.at[t], t).wait_recv()
                inbox[t] = inbox[t] + mine[t % 2]
                send_mid(t).start()

            @pl.when(t >= 1)
            def _():
                i = t - 1
                send_mid(i).wait_recv()
                across[i] = across[i] + inbox[i]
                send_line(across.at[i], i).start()
                send_side(across.at[i], i).start()
                keep(across.at[i], i).start()

            return carry

        lax.fori_loop(0, count + 1, tick, 0)

        def finish(i, carry):
            send_mid(i).wait_send()
            send_line(across.at[i], i).wait_send()
            send_side(across.at[i], i).wait()
            keep(across.at[i], i).wait()
            return carry

        lax.fori_loop(0, count, finish, 0)

    @pl.when(jnp.logical_not(middle))
    def _():
        pl.semaphore_wait(barrier, 2)

        def tick(t, carry):
            @pl.when(t < count)
            def _():
                @pl.when(t >= 2)
                def _():
                    send_line(piece_ref.at[t - 2], t - 2).wait_send()

                send_line(piece_ref.at[t], t).start()

            @pl.when(t >= 4)
            def _():
                i = t - 4
                send_line(inbox.at[i], i).wait_recv()
                send_side(inbox.at[i], i).start()
                keep(inbox.at[i], i).start()

            return carry

        lax.fori_loop(0, count + 4, tick, 0)
        for i in range(max(count - 2, 0), count):
            send_line(piece_ref.at[i], i).wait_send()

        def finish(i, carry):
            send_side(inbox.at[i], i).wait()
            keep(inbox.at[i], i).wait()
            return carry

        lax.fori_loop(0, count, finish, 0)


def reduce_pieces(pieces, n):
    if n != 8:
        total = line_sum(pieces, n)
        return total, swap(total, "ctx", 1)
    count = pieces.shape[0]
    shape = jax.ShapeDtypeStruct(pieces.shape, BF16)
    hbm = pl.BlockSpec(memory_space=pl.ANY)
    dma = pltpu.SemaphoreType.DMA((count,))
    return pl.pallas_call(
        reduce_kernel,
        out_shape=[shape, shape],
        in_specs=[hbm],
        out_specs=[hbm, hbm],
        scratch_shapes=[
            pltpu.VMEM(pieces.shape, BF16),
            pltpu.VMEM(pieces.shape, BF16),
            pltpu.VMEM((2,) + pieces.shape[1:], BF16),
            dma,
            dma,
            dma,
            dma,
            dma,
            dma,
            pltpu.SemaphoreType.DMA((2,)),
            dma,
        ],
        compiler_params=params(collective_id=0, has_side_effects=True),
        cost_estimate=cost(1e8, 1e9),
        name="reduce_pieces",
    )(pieces)


def local(
    inputs,
    cotangent,
    doc_lengths,
    routes,
    attn_gain,
    ffn_gain,
    w_query,
    key_weight,
    value_weight,
    w_out,
    w_router,
    w_gate,
    w_up,
    w_down,
):
    rows = inputs.shape[2]
    width = inputs.shape[3]
    n = lax.axis_size("ctx")
    fsdp = lax.axis_size("fsdp")
    me, mine = lax.axis_index("ctx"), lax.axis_index("fsdp")
    tokens = 2 * rows
    length = tokens * n
    experts_here = w_gate.shape[0]
    number = experts_here // 2
    capacity = 5 * tokens * TOP // (4 * EXPERTS)
    capp = -(-capacity // 16) * 16
    shard = width // fsdp
    heads = QUERY_HEADS // n
    head_lanes = heads * HEAD_DIMENSION
    copies = n // KEY_VALUE_HEADS
    bits = group_bits(fsdp)

    x = inputs.reshape(tokens, width)
    cot = cotangent.reshape(tokens, width)
    side = me % 2
    base = (side * number).astype(jnp.int32).reshape(1)
    first = (mine * experts_here + side * number).astype(jnp.int32).reshape(1)
    index = jnp.stack([side * number, (1 - side) * number]).astype(jnp.int32)
    ends = jnp.cumsum(doc_lengths[0])[:3].astype(jnp.int32)
    table = jnp.asarray(rotary_table(length))
    own_table = lax.dynamic_slice_in_dim(table.reshape(2, n, rows, 256), me, 1, 1).reshape(tokens, 256)

    query_part = w_query.reshape(shard, n, head_lanes)
    if head_lanes < 128:
        query_part = jnp.pad(query_part, ((0, 0), (0, 0), (0, 128 - head_lanes)))
    key_part = jnp.repeat(key_weight.reshape(shard, KEY_VALUE_HEADS, HEAD_DIMENSION), copies, 1)
    value_part = jnp.repeat(value_weight.reshape(shard, KEY_VALUE_HEADS, HEAD_DIMENSION), copies, 1)
    packed = jnp.concatenate([query_part, key_part, value_part], -1).reshape(shard, n * PACK)
    padding = 2 * 16 * (shard // 32 + 1) - shard
    gains = jnp.pad(jnp.stack([attn_gain, ffn_gain]), ((0, padding - 2), (0, n * PACK - shard)))
    packed = jnp.concatenate([packed, gains], 0)
    out_part = w_out.reshape(shard // head_lanes, head_lanes, width)
    if head_lanes < 128:
        out_part = jnp.pad(out_part, ((0, 0), (0, 128 - head_lanes), (0, 0)))
    router_part = jnp.pad(w_router, ((0, 0), (0, 128 - EXPERTS)))
    merge = lambda a: a.reshape(number, -1, a.shape[-1])

    if n == 8 and fsdp == 4:
        packs, h_attn, weights, wo, wr, cxs, gains = front(packed, out_part, router_part, x, own_table, routes.reshape(tokens, TOP), cot, capacity, n)
        gain_one, gain_two = gains[0:1], gains[1:2]
        wo, wr = wo.reshape(n, 128, width), wr.reshape(width, 128)
        packs = packs.reshape(n, 2, rows, PACK)
        attn, lse, full = attn_forward(ends, packs, length)
        middle, h_ffn, attn, xs, gs, gates = mid_step(attn.reshape(n, tokens, 128), cxs, wo, wr, x, gain_two, number, capp, n)
    else:
        weights = lax.all_gather(packed, "fsdp", axis=0)
        gain_one = weights[:, shard, :shard].reshape(1, width).astype(F32)
        gain_two = weights[:, shard + 1, :shard].reshape(1, width).astype(F32)
        wo = lax.all_gather(out_part, "fsdp", axis=0, tiled=True)
        wr = lax.all_gather(router_part, "fsdp", axis=0, tiled=True)
        cxs = group_gather(prep(routes.reshape(tokens, TOP), cot, capacity), bits)
        packs, h_attn = qkv(x, gain_one, weights, own_table, shard, n)
        packs = lax.all_to_all(packs, "ctx", split_axis=0, concat_axis=0, tiled=True).reshape(n, 2, rows, PACK)
        attn, lse, full = attn_forward(ends, packs, length)
        attn = lax.all_to_all(attn.reshape(n, tokens, 128), "ctx", split_axis=0, concat_axis=0, tiled=True)
        middle, h_ffn = middle_step(attn, wo, x, gain_two)
        xs, gs, gates = gather_rows(first, group_gather(h_ffn, bits), cxs, jnp.transpose(wr), number, capp)
    xs, gs, gates = merge(xs), merge(gs), merge(gates)
    pieces, outs, back, dgates = expert_step(base, xs, gs, gates, w_gate, w_up, w_down)
    y_part, gx_part = combine(first, cxs, outs, back, dgates, tokens, capp)
    gx = group_reduce(gx_part, bits)
    grad_middle, dwo, grad_attn, dwr, dgain_two = home_step(gx, h_ffn, middle, cot, wr, wo, gain_two, attn)
    grad_attn = lax.all_to_all(grad_attn, "ctx", split_axis=0, concat_axis=0, tiled=True).reshape(n, 2, rows, 128)
    grads = attn_backward(ends, packs, grad_attn, lse, full, table, length)
    grads = lax.all_to_all(grads.reshape(n, tokens, PACK), "ctx", split_axis=0, concat_axis=0, tiled=True)
    dw, grad_x, dgain_one = final_step(grads, weights, h_attn, x, gain_one, grad_middle, shard)
    mixed = middle + RESIDUAL * group_reduce(y_part, bits).astype(F32)

    own, other = reduce_pieces(pieces.reshape(number * 6, PIECE, PIECE), n)
    outs = [widen(index, own, other, m, w.shape) for m, w in enumerate((w_gate, w_up, w_down))]

    scatter = lambda a: lax.psum(lax.psum_scatter(a, "fsdp", scatter_dimension=0, tiled=True), "ctx").astype(F32)
    dwo = scatter(dwo)[:, :head_lanes, :].reshape(shard, width)
    small = jnp.concatenate([dwr[:, :EXPERTS], dgain_two.reshape(width, 1).astype(BF16)], 1)
    small = scatter(jnp.pad(small, ((0, 0), (0, 127 - EXPERTS))))
    dw = scatter(dw).reshape(shard, n, PACK)
    dgain_one = scatter(dgain_one.reshape(width).astype(BF16))
    fold = lambda a: a.reshape(shard, KEY_VALUE_HEADS, copies, HEAD_DIMENSION).sum(2).reshape(shard, -1)
    return (
        mixed.reshape(inputs.shape),
        grad_x.reshape(inputs.shape),
        dgain_one,
        small[:, EXPERTS],
        dw[:, :, :head_lanes].reshape(shard, -1),
        fold(dw[:, :, 128:192]),
        fold(dw[:, :, 192:256]),
        dwo,
        small[:, :EXPERTS],
        outs[0],
        outs[1],
        outs[2],
    )


def solution(mesh):
    tokens = P("fsdp", None, "ctx", None)
    one, two, three = P("fsdp"), P("fsdp", None), P("fsdp", None, None)
    return jax.shard_map(
        local,
        mesh=mesh,
        in_specs=(tokens, tokens, two, tokens, one, one, two, two, two, two, two, three, three, three),
        out_specs=(tokens, tokens, one, one, two, two, two, two, two, three, three, three),
        check_vma=False,
    )
```

```python
import functools

import jax
import jax.numpy as jnp
import numpy as np
from jax import lax
from jax.experimental import pallas as pl
from jax.experimental.pallas import tpu as pltpu
from jax.sharding import PartitionSpec as P

QUERY_HEADS = 16
KEY_VALUE_HEADS = 8
HEAD_DIMENSION = 64
EXPERTS = 32
TOP = 8

ATTN_SCALE = 0.015625
RESIDUAL = 0.22
NORM_EPS = 1e-06
ROPE_BASE = 10000.0
MASKED = -1e30

F32 = jnp.float32
BF16 = jnp.bfloat16
MIB = 1 << 20
NT = (((1,), (1,)), ((), ()))
TN = (((0,), (0,)), ((), ()))
BLK = 256
PACK = 256


def dot(a, b, dims=None):
    if dims is None:
        return jnp.dot(a, b, preferred_element_type=F32)
    return lax.dot_general(a, b, dims, preferred_element_type=F32)


def params(limit=56, **kw):
    return pltpu.CompilerParams(vmem_limit_bytes=limit * MIB, **kw)


def cost(flops, bytes_accessed):
    return pl.CostEstimate(flops=int(flops), bytes_accessed=int(bytes_accessed), transcendentals=0)


def lane_iota(shape):
    return lax.broadcasted_iota(jnp.int32, shape, len(shape) - 1)


def row_iota(shape):
    return lax.broadcasted_iota(jnp.int32, shape, len(shape) - 2)


def rotary_table(length):
    half = length // 2
    order = np.arange(half, dtype=np.float32)
    positions = np.concatenate([order, length - 1 - order]).astype(np.float32)
    m = np.arange(HEAD_DIMENSION // 2, dtype=np.float64)
    frequency = (ROPE_BASE ** (-2.0 * m / HEAD_DIMENSION)).astype(np.float32)
    angles = (positions[:, None] * frequency[None, :]).astype(np.float64)
    cosine, sine = np.cos(angles), np.sin(angles)
    cos_head = np.concatenate([cosine, cosine], -1)
    sin_head = np.concatenate([-sine, sine], -1)
    return np.concatenate([cos_head, cos_head, sin_head, sin_head], -1).astype(np.float32)


def turn(v, table, direction):
    lanes = lane_iota(v.shape)
    cosine = jnp.concatenate([table[:, :128], table[:, :128]], -1)
    sine = jnp.concatenate([table[:, 128:], table[:, 128:]], -1)
    turned = lanes < 3 * HEAD_DIMENSION
    swapped = jnp.where(lanes % HEAD_DIMENSION < HEAD_DIMENSION // 2, pltpu.roll(v, PACK - 32, 1), pltpu.roll(v, 32, 1))
    return jnp.where(turned, v * cosine + direction * (swapped * sine), v)


def norm_parts(values):
    inv_rms = lax.rsqrt(jnp.mean(values * values, -1, keepdims=True) + NORM_EPS)
    return values * inv_rms, inv_rms


def norm_back(grad_normed, normed, inv_rms):
    return inv_rms * (grad_normed - normed * jnp.mean(grad_normed * normed, -1, keepdims=True))


def prep_kernel(cap, routes_ref, cot_ref, out_ref):
    tokens, width = cot_ref.shape
    routes = routes_ref[...]
    earlier = (lane_iota((tokens, tokens)) < row_iota((tokens, tokens))).astype(BF16)
    experts = lane_iota((tokens, 128))
    base = jnp.zeros((1, 128), F32)
    plus = jnp.zeros((tokens, 128), F32)
    for k in range(TOP):
        chosen = experts == routes[:, k : k + 1]
        ones = chosen.astype(F32)
        slot = dot(earlier, ones.astype(BF16)) + base
        plus = plus + jnp.where(chosen & (slot < cap), slot + 1.0, 0.0)
        base = base + jnp.sum(ones, 0, keepdims=True)
    out_ref[:tokens, :] = cot_ref[...].astype(BF16)
    slots = (jnp.transpose(plus) - 1.0)[:EXPERTS, :]
    out_ref[tokens:, :] = jnp.concatenate([slots, jnp.zeros((EXPERTS, width - tokens), F32)], -1).astype(BF16)


def prep(routes, cot, cap):
    tokens, width = cot.shape
    return pl.pallas_call(
        functools.partial(prep_kernel, cap),
        out_shape=jax.ShapeDtypeStruct((tokens + EXPERTS, width), BF16),
        compiler_params=params(),
        cost_estimate=cost(1e9, 2e6),
        name="prep",
    )(routes, cot)


def qkv_kernel(shard, x_ref, gain_ref, w_ref, table_ref, out_ref, h_ref):
    @pl.when(pl.program_id(0) == 0)
    def _():
        normed, _ = norm_parts(x_ref[...])
        h_ref[...] = (normed * gain_ref[...]).astype(BF16)

    total = None
    for f in range(w_ref.shape[0]):
        part = dot(h_ref[:, f * shard : (f + 1) * shard], w_ref[f, :shard, :])
        total = part if total is None else total + part
    for d in range(out_ref.shape[0]):
        out_ref[d] = turn(total[:, d * PACK : (d + 1) * PACK], table_ref[...], 1.0).astype(BF16)


def qkv(x, gain, weights, table, shard, n):
    tokens, width = x.shape
    fsdp, padded, _ = weights.shape
    return pl.pallas_call(
        functools.partial(qkv_kernel, shard),
        grid=(n // 2,),
        in_specs=[
            pl.BlockSpec((tokens, width), lambda i: (0, 0)),
            pl.BlockSpec((1, width), lambda i: (0, 0)),
            pl.BlockSpec((fsdp, padded, 2 * PACK), lambda i: (0, 0, i)),
            pl.BlockSpec((tokens, 256), lambda i: (0, 0)),
        ],
        out_specs=[
            pl.BlockSpec((2, tokens, PACK), lambda i: (i, 0, 0)),
            pl.BlockSpec((tokens, width), lambda i: (0, 0)),
        ],
        out_shape=[
            jax.ShapeDtypeStruct((n, tokens, PACK), BF16),
            jax.ShapeDtypeStruct((tokens, width), BF16),
        ],
        compiler_params=params(),
        cost_estimate=cost(2 * tokens * width * n * PACK, 8e6),
        name="qkv",
    )(x, gain, weights, table)


def pair_keys(kv):
    other = pltpu.roll(kv, 64, 1)
    low = lane_iota(kv.shape) < 64
    return jnp.where(low, kv, other), jnp.where(low, other, kv)


def stack_heads(q):
    low = lane_iota(q.shape) < 64
    zero = jnp.zeros_like(q)
    return jnp.concatenate([jnp.where(low, q, zero), jnp.where(low, zero, q)], 0)


def fold_heads(stacked):
    rows = stacked.shape[0] // 2
    return jnp.where(lane_iota((rows, 128)) < 64, stacked[:rows], stacked[rows:])


def query_rows(ends_ref, block, length):
    half = length // 2
    lanes = lane_iota((1, 2 * BLK))
    index = block * BLK + jnp.where(lanes < BLK, lanes, lanes - BLK)
    position = jnp.where(index < half, index, length + half - 1 - index)
    start = jnp.zeros_like(position)
    for j in range(3):
        end = ends_ref[j]
        start = jnp.where(position >= end, jnp.maximum(start, end), start)
    return position, start


def key_position(kb, length):
    half = length // 2
    index = kb * BLK + row_iota((BLK, 1))
    return jnp.where(index < half, index, length + half - 1 - index)


def block_loop(block, per_half, body, init):
    late = block >= per_half
    inner = jnp.where(late, block - per_half, block)
    count = jnp.where(late, 2 * per_half - inner, inner + 1)

    def step(j, carry):
        kb = jnp.where(late & (j >= per_half), inner + j, j)
        return body(kb, carry)

    return lax.fori_loop(0, count, step, init)


def load_package(pack_ref, c, h):
    return pack_ref[c, h].astype(F32)


def attn_forward_kernel(length, ends_ref, q_ref, pack_ref, out_ref, lse_ref, full_ref, keys, values_t, acc):
    block = pl.program_id(0)
    half = length // 2
    n, _, rows, _ = pack_ref.shape

    @pl.when(block == 0)
    def _():
        for h in range(2):
            for c in range(n):
                kk, vv = pair_keys(pack_ref[c, h, :, 128:256].astype(F32))
                at = h * half + c * rows
                keys[at : at + rows, :] = kk.astype(BF16)
                if rows % 128 == 0:
                    values_t[:, at : at + rows] = jnp.transpose(vv).astype(BF16)
        if rows % 128 != 0:
            for h in range(2):
                for c in range(0, n, 2):
                    pair = jnp.concatenate([pack_ref[c, h, :, 128:256], pack_ref[c + 1, h, :, 128:256]], 0)
                    _, vv = pair_keys(pair.astype(F32))
                    at = h * half + c * rows
                    values_t[:, at : at + 2 * rows] = jnp.transpose(vv).astype(BF16)

    q = q_ref[...].reshape(BLK, PACK)[:, :128]
    q2 = stack_heads(q)
    position, start = query_rows(ends_ref, block, length)
    acc[...] = jnp.zeros_like(acc)

    def body(kb, carry):
        peak, total = carry
        at = pl.multiple_of(kb * BLK, BLK)
        scores = dot(keys[pl.ds(at, BLK), :], q2, NT) * ATTN_SCALE
        where = key_position(kb, length)
        scores = jnp.where((where <= position) & (where >= start), scores, MASKED)
        new_peak = jnp.maximum(peak, jnp.max(scores, 0, keepdims=True))
        weights = jnp.exp(scores - new_peak)
        fade = jnp.exp(peak - new_peak)
        total = total * fade + jnp.sum(weights, 0, keepdims=True)
        acc[...] = acc[...] * fade + dot(values_t[:, pl.ds(at, BLK)], weights.astype(BF16))
        return new_peak, total

    init = (jnp.full((1, 2 * BLK), MASKED, F32), jnp.zeros((1, 2 * BLK), F32))
    peak, total = block_loop(block, half // BLK, body, init)
    result = acc[...] / total
    full_ref[0] = result
    lse_ref[0] = peak + jnp.log(total)
    folded = fold_heads(jnp.transpose(result)).astype(BF16)
    out_ref[...] = folded.reshape(out_ref.shape)


def attn_forward(ends, packs, length):
    n, _, rows, _ = packs.shape
    blocks, per = length // BLK, BLK // rows
    per_half = blocks // 2
    tiles = lambda i, ends: (lax.rem(i, per_half), i // per_half, 0, 0)
    return pl.pallas_call(
        functools.partial(attn_forward_kernel, length),
        grid_spec=pltpu.PrefetchScalarGridSpec(
            num_scalar_prefetch=1,
            grid=(blocks,),
            in_specs=[
                pl.BlockSpec((per, 1, rows, PACK), tiles),
                pl.BlockSpec(packs.shape, lambda i, ends: (0, 0, 0, 0)),
            ],
            out_specs=[
                pl.BlockSpec((per, 1, rows, 128), tiles),
                pl.BlockSpec((1, 1, 2 * BLK), lambda i, ends: (i, 0, 0)),
                pl.BlockSpec((1, 128, 2 * BLK), lambda i, ends: (i, 0, 0)),
            ],
            scratch_shapes=[
                pltpu.VMEM((length, 128), BF16),
                pltpu.VMEM((128, length), BF16),
                pltpu.VMEM((128, 2 * BLK), F32),
            ],
        ),
        out_shape=[
            jax.ShapeDtypeStruct((n, 2, rows, 128), BF16),
            jax.ShapeDtypeStruct((blocks, 1, 2 * BLK), F32),
            jax.ShapeDtypeStruct((blocks, 128, 2 * BLK), F32),
        ],
        compiler_params=params(),
        cost_estimate=cost(1.5e10, 6e6),
        name="attn_forward",
    )(ends, packs, packs)


def attn_backward_kernel(length, ends_ref, q_ref, g_ref, pack_ref, lse_ref, full_ref, table_ref, out_ref, keys, values, keys_t, grad_q, grad_k, grad_v, acc):
    block = pl.program_id(0)
    half = length // 2
    n, _, rows, _ = pack_ref.shape

    @pl.when(block == 0)
    def _():
        for h in range(2):
            for c in range(n):
                kk, vv = pair_keys(pack_ref[c, h, :, 128:256].astype(F32))
                at = h * half + c * rows
                keys[at : at + rows, :] = kk.astype(BF16)
                values[at : at + rows, :] = vv.astype(BF16)
        for b in range(length // BLK):
            keys_t[:, b * BLK : (b + 1) * BLK] = jnp.transpose(keys[b * BLK : (b + 1) * BLK, :].astype(F32)).astype(BF16)
        grad_k[...] = jnp.zeros_like(grad_k)
        grad_v[...] = jnp.zeros_like(grad_v)

    q2 = stack_heads(q_ref[...].reshape(BLK, PACK)[:, :128])
    g2 = stack_heads(g_ref[...].reshape(BLK, 128))
    position, start = query_rows(ends_ref, block, length)
    lse = lse_ref[0]
    delta = jnp.sum(jnp.transpose(g2.astype(F32)) * full_ref[0], 0, keepdims=True)
    acc[...] = jnp.zeros_like(acc)

    def body(kb, carry):
        at = pl.multiple_of(kb * BLK, BLK)
        scores = dot(keys[pl.ds(at, BLK), :], q2, NT) * ATTN_SCALE
        where = key_position(kb, length)
        probs = jnp.where((where <= position) & (where >= start), jnp.exp(scores - lse), 0.0)
        grad_probs = dot(values[pl.ds(at, BLK), :], g2, NT)
        grad_scores = (probs * (grad_probs - delta)).astype(BF16)
        acc[...] += dot(keys_t[:, pl.ds(at, BLK)], grad_scores)
        grad_k[pl.ds(at, BLK), :] += dot(grad_scores, q2)
        grad_v[pl.ds(at, BLK), :] += dot(probs.astype(BF16), g2)
        return carry

    block_loop(block, half // BLK, body, 0)
    grad_q[pl.ds(pl.multiple_of(block * BLK, BLK), BLK), :] = fold_heads(jnp.transpose(acc[...]))

    @pl.when(block == length // BLK - 1)
    def _():
        for h in range(2):
            for c in range(n):
                at = slice(h * half + c * rows, h * half + (c + 1) * rows)
                kk = grad_k[at, :]
                vv = grad_v[at, :]
                kk = (kk + pltpu.roll(kk, 64, 1)) * ATTN_SCALE
                vv = vv + pltpu.roll(vv, 64, 1)
                both = jnp.where(lane_iota(kk.shape) < 64, kk, vv)
                package = jnp.concatenate([grad_q[at, :] * ATTN_SCALE, both], -1)
                out_ref[c, h] = turn(package, table_ref[at, :], -1.0).astype(BF16)


def attn_backward(ends, packs, grads, lse, full, table, length):
    n, _, rows, _ = packs.shape
    blocks, per = length // BLK, BLK // rows
    per_half = blocks // 2
    tiles = lambda i, ends: (lax.rem(i, per_half), i // per_half, 0, 0)
    return pl.pallas_call(
        functools.partial(attn_backward_kernel, length),
        grid_spec=pltpu.PrefetchScalarGridSpec(
            num_scalar_prefetch=1,
            grid=(blocks,),
            in_specs=[
                pl.BlockSpec((per, 1, rows, PACK), tiles),
                pl.BlockSpec((per, 1, rows, 128), tiles),
                pl.BlockSpec(packs.shape, lambda i, ends: (0, 0, 0, 0)),
                pl.BlockSpec((1, 1, 2 * BLK), lambda i, ends: (i, 0, 0)),
                pl.BlockSpec((1, 128, 2 * BLK), lambda i, ends: (i, 0, 0)),
                pl.BlockSpec(table.shape, lambda i, ends: (0, 0)),
            ],
            out_specs=pl.BlockSpec(packs.shape, lambda i, ends: (0, 0, 0, 0)),
            scratch_shapes=[
                pltpu.VMEM((length, 128), BF16),
                pltpu.VMEM((length, 128), BF16),
                pltpu.VMEM((128, length), BF16),
                pltpu.VMEM((length, 128), F32),
                pltpu.VMEM((length, 128), F32),
                pltpu.VMEM((length, 128), F32),
                pltpu.VMEM((128, 2 * BLK), F32),
            ],
        ),
        out_shape=jax.ShapeDtypeStruct(packs.shape, BF16),
        compiler_params=params(),
        cost_estimate=cost(3e10, 8e6),
        name="attn_backward",
    )(ends, packs, grads, packs, lse, full, table)


def middle_kernel(attn_ref, wo_ref, x_ref, gain_ref, middle_ref, h_ref):
    total = None
    for c in range(attn_ref.shape[0]):
        part = dot(attn_ref[c], wo_ref[c])
        total = part if total is None else total + part
    middle = x_ref[...] + RESIDUAL * total
    middle_ref[...] = middle
    normed, _ = norm_parts(middle)
    h_ref[...] = (normed * gain_ref[...]).astype(BF16)


def middle_step(attn, wo, x, gain):
    tokens, width = x.shape
    return pl.pallas_call(
        middle_kernel,
        out_shape=[jax.ShapeDtypeStruct((tokens, width), F32), jax.ShapeDtypeStruct((tokens, width), BF16)],
        compiler_params=params(),
        cost_estimate=cost(2 * tokens * width * width, 5e6),
        name="middle",
    )(attn, wo, x, gain)


def own_row(table, row):
    return jnp.sum(jnp.where(row_iota(table.shape) == row, table, 0.0), 0, keepdims=True)


def one_hot(slots, first, number, capp):
    tokens = slots.shape[1]
    order = row_iota((capp, tokens)).astype(F32)
    return [(order == own_row(slots, first + j)).astype(F32) for j in range(number)]


def gather_kernel(number, capp, first_ref, h_ref, cx_ref, wrt_ref, x_ref, g_ref, gate_ref):
    tokens = h_ref.shape[1]
    first = first_ref[0]
    h = h_ref[0]
    slots = cx_ref[0, tokens:, :tokens].astype(F32)
    logits = dot(wrt_ref[...], h, NT)[:EXPERTS, :]
    raw = jnp.exp(logits - jnp.max(logits, 0, keepdims=True))
    router = raw / jnp.sum(raw, 0, keepdims=True)
    hots = one_hot(slots, first, number, capp)
    places = jnp.concatenate(hots, 0).astype(BF16)
    rows = dot(places, h).astype(BF16)
    grads = dot(places, cx_ref[0, :tokens, :]).astype(BF16)
    for j in range(number):
        at = slice(j * capp, (j + 1) * capp)
        x_ref[j, 0] = rows[at]
        g_ref[j, 0] = grads[at]
        gate = jnp.sum(hots[j] * own_row(router, first + j), 1, keepdims=True)
        gate_ref[j, 0] = jnp.broadcast_to(gate, (capp, 128))


def gather_rows(first, hs, cxs, wrt, number, capp):
    nb, tokens, width = hs.shape
    return pl.pallas_call(
        functools.partial(gather_kernel, number, capp),
        grid_spec=pltpu.PrefetchScalarGridSpec(
            num_scalar_prefetch=1,
            grid=(nb,),
            in_specs=[
                pl.BlockSpec((1, tokens, width), lambda b, f: (b, 0, 0)),
                pl.BlockSpec((1, tokens + EXPERTS, width), lambda b, f: (b, 0, 0)),
                pl.BlockSpec(wrt.shape, lambda b, f: (0, 0)),
            ],
            out_specs=[
                pl.BlockSpec((number, 1, capp, width), lambda b, f: (0, b, 0, 0)),
                pl.BlockSpec((number, 1, capp, width), lambda b, f: (0, b, 0, 0)),
                pl.BlockSpec((number, 1, capp, 128), lambda b, f: (0, b, 0, 0)),
            ],
        ),
        out_shape=[
            jax.ShapeDtypeStruct((number, nb, capp, width), BF16),
            jax.ShapeDtypeStruct((number, nb, capp, width), BF16),
            jax.ShapeDtypeStruct((number, nb, capp, 128), F32),
        ],
        compiler_params=params(),
        cost_estimate=cost(4 * nb * number * capp * tokens * width, 2e7),
        name="gather_rows",
    )(first, hs, cxs, wrt)


PIECE = 512


def expert_kernel(base_ref, x_ref, g_ref, gate_ref, wg_ref, wu_ref, wd_ref, piece_ref, out_ref, rows_ref, dg_ref):
    x = x_ref[0]
    gate = gate_ref[0][:, :1]
    grad_ffn = RESIDUAL * g_ref[0].astype(F32)
    go = (gate * grad_ffn).astype(BF16)
    part = wg_ref.shape[2] // 2
    out = rows = None
    for chunk in range(2):
        at = slice(chunk * part, (chunk + 1) * part)
        wg, wu, wd = wg_ref[0, :, at], wu_ref[0, :, at], wd_ref[0, at, :]
        pre_gate = dot(x, wg)
        pre_up = dot(x, wu)
        sig = jax.nn.sigmoid(pre_gate)
        hidden = (pre_gate * sig * pre_up).astype(BF16)
        out_part = dot(hidden, wd)
        grad_hidden = dot(go, wd, NT)
        grad_gate = (grad_hidden * pre_up * sig * (1.0 + pre_gate * (1.0 - sig))).astype(BF16)
        grad_up = (grad_hidden * pre_gate * sig).astype(BF16)
        row_part = dot(grad_gate, wg, NT) + dot(grad_up, wu, NT)
        dwg = dot(x, grad_gate, TN).astype(BF16)
        dwu = dot(x, grad_up, TN).astype(BF16)
        dwd = dot(hidden, go, TN).astype(BF16)
        for half in range(2):
            side = slice(half * PIECE, (half + 1) * PIECE)
            piece_ref[0, half, :, at] = dwg[side]
            piece_ref[0, 2 + half, :, at] = dwu[side]
            piece_ref[0, 4 + half, at, :] = dwd[:, side]
        out = out_part if out is None else out + out_part
        rows = row_part if rows is None else rows + row_part
    out = out.astype(BF16).astype(F32)
    out_ref[0] = (gate * out).astype(BF16)
    rows_ref[0] = rows.astype(BF16)
    grad = jnp.sum(grad_ffn * out, 1, keepdims=True)
    dg_ref[0] = jnp.broadcast_to(grad, dg_ref.shape[1:])


def expert_step(base, xs, gs, gates, w_gate, w_up, w_down):
    number, rows, width = xs.shape
    ff = w_gate.shape[2]
    row = lambda e, b: (e, 0, 0)
    weight = lambda e, b: (b[0] + e, 0, 0)
    return pl.pallas_call(
        expert_kernel,
        grid_spec=pltpu.PrefetchScalarGridSpec(
            num_scalar_prefetch=1,
            grid=(number,),
            in_specs=[
                pl.BlockSpec((1, rows, width), row),
                pl.BlockSpec((1, rows, width), row),
                pl.BlockSpec((1, rows, 128), row),
                pl.BlockSpec((1, width, ff), weight),
                pl.BlockSpec((1, width, ff), weight),
                pl.BlockSpec((1, ff, width), weight),
            ],
            out_specs=[
                pl.BlockSpec((1, 6, PIECE, PIECE), lambda e, b: (e, 0, 0, 0)),
                pl.BlockSpec((1, rows, width), row),
                pl.BlockSpec((1, rows, width), row),
                pl.BlockSpec((1, rows, 128), row),
            ],
        ),
        out_shape=[
            jax.ShapeDtypeStruct((number, 6, PIECE, PIECE), BF16),
            jax.ShapeDtypeStruct((number, rows, width), BF16),
            jax.ShapeDtypeStruct((number, rows, width), BF16),
            jax.ShapeDtypeStruct((number, rows, 128), F32),
        ],
        compiler_params=params(60),
        cost_estimate=cost(18 * number * rows * width * ff, 5e7),
        name="expert_step",
    )(base, xs, gs, gates, w_gate, w_up, w_down)


def combine_kernel(number, capp, first_ref, slot_ref, outs, rows, grads, y_ref, gx_ref):
    tokens = y_ref.shape[1]
    width = y_ref.shape[2]
    first = first_ref[0]
    slots = slot_ref[0][:, :tokens].astype(F32)
    hots = one_hot(slots, first, number, capp)
    places = jnp.concatenate(hots, 0).astype(BF16)
    y_ref[0] = dot(places, outs[:, 0].reshape(number * capp, width), TN).astype(BF16)
    gx_ref[0, :tokens] = dot(places, rows[:, 0].reshape(number * capp, width), TN).astype(BF16)
    extra = jnp.zeros((EXPERTS, 2 * tokens), F32)
    for j in range(number):
        grad = jnp.sum(hots[j] * grads[j, 0][:, :1], 0, keepdims=True)
        high = grad.astype(BF16).astype(F32)
        both = jnp.concatenate([high, grad - high], 1)
        extra = jnp.where(row_iota(extra.shape) == first + j, both, extra)
    rest = jnp.zeros((EXPERTS, width - 2 * tokens), F32)
    gx_ref[0, tokens:] = jnp.concatenate([extra, rest], 1).astype(BF16)


def combine(first, cxs, outs, rows, grads, tokens, capp):
    number = outs.shape[0]
    nb, _, width = cxs.shape
    split = lambda a: a.reshape(number, nb, capp, a.shape[-1])
    wide = pl.BlockSpec((number, 1, capp, width), lambda b, f: (0, b, 0, 0))
    thin = pl.BlockSpec((number, 1, capp, 128), lambda b, f: (0, b, 0, 0))
    return pl.pallas_call(
        functools.partial(combine_kernel, number, capp),
        grid_spec=pltpu.PrefetchScalarGridSpec(
            num_scalar_prefetch=1,
            grid=(nb,),
            in_specs=[pl.BlockSpec((1, EXPERTS, width), lambda b, f: (b, tokens // EXPERTS, 0))] + [wide, wide, thin],
            out_specs=[
                pl.BlockSpec((1, tokens, width), lambda b, f: (b, 0, 0)),
                pl.BlockSpec((1, tokens + EXPERTS, width), lambda b, f: (b, 0, 0)),
            ],
        ),
        out_shape=[
            jax.ShapeDtypeStruct((nb, tokens, width), BF16),
            jax.ShapeDtypeStruct((nb, tokens + EXPERTS, width), BF16),
        ],
        compiler_params=params(),
        cost_estimate=cost(4 * nb * number * capp * tokens * width, 2e7),
        name="combine",
    )(first, cxs, split(outs), split(rows), split(grads))


def home_kernel(gx_ref, h_ref, middle_ref, cot_ref, wr_ref, wo_ref, gain_ref, attn_ref, grad_middle_ref, dwo_ref, ga_ref, dwr_ref, dgain_ref):
    tokens, width = h_ref.shape
    h = h_ref[...]
    gain = gain_ref[...]
    extra = gx_ref[tokens:, :].astype(F32)
    grad_router = extra[:, :tokens] + extra[:, tokens : 2 * tokens]
    grad_router = jnp.transpose(jnp.concatenate([grad_router, jnp.zeros((128 - EXPERTS, tokens), F32)], 0))
    logits = dot(h, wr_ref[...])
    logits = jnp.where(lane_iota(logits.shape) < EXPERTS, logits, MASKED)
    raw = jnp.exp(logits - jnp.max(logits, -1, keepdims=True))
    router = raw / jnp.sum(raw, -1, keepdims=True)
    grad_logits = (router * (grad_router - jnp.sum(router * grad_router, -1, keepdims=True))).astype(BF16)
    dwr_ref[...] = dot(h, grad_logits, TN).astype(BF16)
    grad_h = gx_ref[:tokens, :].astype(F32) + dot(grad_logits, wr_ref[...], NT)
    normed, scale = norm_parts(middle_ref[...])
    dgain_ref[...] = jnp.sum(grad_h * normed, 0, keepdims=True)
    grad_middle = cot_ref[...] + norm_back(grad_h * gain, normed, scale)
    grad_middle_ref[...] = grad_middle
    grad_branch = (RESIDUAL * grad_middle).astype(BF16)
    for c in range(attn_ref.shape[0]):
        dwo_ref[c] = dot(attn_ref[c], grad_branch, TN).astype(BF16)
        ga_ref[c] = dot(grad_branch, wo_ref[c], NT).astype(BF16)


def home_step(gx, h, middle, cot, wr, wo, gain, attn):
    tokens, width = h.shape
    n = attn.shape[0]
    return pl.pallas_call(
        home_kernel,
        out_shape=[
            jax.ShapeDtypeStruct((tokens, width), F32),
            jax.ShapeDtypeStruct((n, 128, width), BF16),
            jax.ShapeDtypeStruct((n, tokens, 128), BF16),
            jax.ShapeDtypeStruct((width, 128), BF16),
            jax.ShapeDtypeStruct((1, width), F32),
        ],
        compiler_params=params(),
        cost_estimate=cost(4 * tokens * width * width, 1e7),
        name="home_step",
    )(gx, h, middle, cot, wr, wo, gain, attn)


def final_kernel(shard, grads_ref, w_ref, h_ref, x_ref, gain_ref, grad_middle_ref, dw_ref, grad_x_ref, dgain_ref, total):
    c = pl.program_id(0)
    g = grads_ref[0]
    dw_ref[...] = dot(h_ref[...], g, TN).astype(BF16)

    @pl.when(c == 0)
    def _():
        total[...] = jnp.zeros_like(total)

    for f in range(w_ref.shape[0]):
        total[:, f * shard : (f + 1) * shard] += dot(g, w_ref[f, :shard, :], NT)

    @pl.when(c == pl.num_programs(0) - 1)
    def _():
        normed, scale = norm_parts(x_ref[...])
        grad_h = total[...]
        dgain_ref[...] = jnp.sum(grad_h * normed, 0, keepdims=True)
        grad_x_ref[...] = grad_middle_ref[...] + norm_back(grad_h * gain_ref[...], normed, scale)


def final_step(grads, weights, h, x, gain, grad_middle, shard):
    n, tokens, _ = grads.shape
    width = x.shape[1]
    fsdp, padded, _ = weights.shape
    same = lambda c: (0, 0)
    return pl.pallas_call(
        functools.partial(final_kernel, shard),
        grid=(n,),
        in_specs=[
            pl.BlockSpec((1, tokens, PACK), lambda c: (c, 0, 0)),
            pl.BlockSpec((fsdp, padded, PACK), lambda c: (0, 0, c)),
            pl.BlockSpec((tokens, width), same),
            pl.BlockSpec((tokens, width), same),
            pl.BlockSpec((1, width), same),
            pl.BlockSpec((tokens, width), same),
        ],
        out_specs=[
            pl.BlockSpec((width, PACK), lambda c: (0, c)),
            pl.BlockSpec((tokens, width), same),
            pl.BlockSpec((1, width), same),
        ],
        out_shape=[
            jax.ShapeDtypeStruct((width, n * PACK), BF16),
            jax.ShapeDtypeStruct((tokens, width), F32),
            jax.ShapeDtypeStruct((1, width), F32),
        ],
        scratch_shapes=[pltpu.VMEM((tokens, width), F32)],
        compiler_params=params(),
        cost_estimate=cost(4 * tokens * width * n * PACK, 1.2e7),
        name="final_step",
    )(grads, weights, h, x, gain, grad_middle)


def widen_kernel(by_rows, index_ref, own_ref, other_ref, out_ref):
    def write(ref):
        for half in range(2):
            at = slice(half * PIECE, (half + 1) * PIECE)
            if by_rows:
                out_ref[0, at, :] = ref[half].astype(F32)
            else:
                out_ref[0, :, at] = ref[half].astype(F32)

    @pl.when(pl.program_id(0) == 0)
    def _():
        write(own_ref)

    @pl.when(pl.program_id(0) == 1)
    def _():
        write(other_ref)


def widen(index, own, other, matrix, shape):
    number = own.shape[0] // 6
    by_rows = shape[1] == 2 * PIECE
    piece = lambda e: 3 * e + matrix
    return pl.pallas_call(
        functools.partial(widen_kernel, by_rows),
        grid_spec=pltpu.PrefetchScalarGridSpec(
            num_scalar_prefetch=1,
            grid=(2, number),
            in_specs=[
                pl.BlockSpec((2, PIECE, PIECE), lambda s, e, at: (jnp.where(s == 0, piece(e), piece(number - 1)), 0, 0)),
                pl.BlockSpec((2, PIECE, PIECE), lambda s, e, at: (jnp.where(s == 0, piece(0), piece(e)), 0, 0)),
            ],
            out_specs=pl.BlockSpec((1,) + tuple(shape[1:]), lambda s, e, at: (at[s] + e, 0, 0)),
        ),
        out_shape=jax.ShapeDtypeStruct(shape, F32),
        compiler_params=params(),
        cost_estimate=cost(0, 6 * shape[0] * shape[1] * shape[2]),
        name="widen",
    )(index, own, other)


def swap(value, axis, bit):
    size = lax.axis_size(axis)
    return lax.ppermute(value, axis, [(i, i ^ bit) for i in range(size)])


def group_bits(fsdp):
    bits = [("fsdp", 1 << b) for b in range(1, fsdp.bit_length() - 1)]
    return bits + [("ctx", 1), ("fsdp", 1)]


def group_gather(value, bits):
    stacked = value[None]
    for axis, bit in bits:
        stacked = jnp.concatenate([stacked, swap(stacked, axis, bit)], 0)
    return stacked


def group_reduce(stacked, bits):
    for axis, bit in reversed(bits):
        half = stacked.shape[0] // 2
        arrived = swap(stacked[half:], axis, bit)
        stacked = (stacked[:half].astype(F32) + arrived.astype(F32)).astype(stacked.dtype)
    return stacked[0]


def line_sum(value, ctx):
    pairs = ctx // 2
    if pairs != 4:
        bit = 2
        while bit < ctx:
            value = value + swap(value, "ctx", bit)
            bit *= 2
        return value
    at = lambda z, y: 2 * z + y
    inward = [(at(0, y), at(1, y)) for y in range(2)] + [(at(3, y), at(2, y)) for y in range(2)]
    across = [(at(1, y), at(2, y)) for y in range(2)] + [(at(2, y), at(1, y)) for y in range(2)]
    outward = [(b, a) for a, b in inward]
    value = value + lax.ppermute(value, "ctx", inward)
    value = value + lax.ppermute(value, "ctx", across)
    arrived = lax.ppermute(value, "ctx", outward)
    z = lax.axis_index("ctx") // 2
    return jnp.where((z == 0) | (z == 3), arrived, value)


MESH = pl.DeviceIdType.MESH


def flip(index, bit):
    return jnp.where((index // bit) % 2 == 0, index + bit, index - bit)


def send(src, dst, send_sem, recv_sem, device):
    return pltpu.make_async_remote_copy(src_ref=src, dst_ref=dst, send_sem=send_sem, recv_sem=recv_sem, device_id=device, device_id_type=MESH)


def neighbours():
    ctx, fsdp = lax.axis_index("ctx"), lax.axis_index("fsdp")
    side, across = flip(ctx, 1), flip(fsdp, 2)
    core = {"fsdp": flip(fsdp, 1)}
    return core, [{"fsdp": across}, {"ctx": side}, {"ctx": side, "fsdp": across}]


def greet(devices):
    barrier = pltpu.get_barrier_semaphore()
    for device in devices:
        pl.semaphore_signal(barrier, inc=1, device_id=device, device_id_type=MESH)
    pl.semaphore_wait(barrier, len(devices))


def others(n):
    ctx = lax.axis_index("ctx")
    return [lax.rem(ctx + d, n) for d in range(1, n)]


def exchange_start(src, dst, send_sems, recv_sems, local_sem, n):
    ctx = lax.axis_index("ctx")
    for d, c in enumerate(others(n)):
        send(src.at[c], dst.at[ctx], send_sems.at[d], recv_sems.at[d], {"ctx": c}).start()
    pltpu.make_async_copy(src.at[ctx], dst.at[ctx], local_sem).start()


def exchange_wait(src, dst, send_sems, recv_sems, local_sem, n, arrived=None):
    ctx = lax.axis_index("ctx")
    pltpu.make_async_copy(src.at[ctx], dst.at[ctx], local_sem).wait()
    if arrived is not None:
        arrived(ctx)
    for d in range(n - 1):
        source = lax.rem(ctx + n - 1 - d, n)
        send(src.at[source], dst.at[source], send_sems.at[d], recv_sems.at[d], {"ctx": source}).wait_recv()
        if arrived is not None:
            arrived(source)
    for d, c in enumerate(others(n)):
        send(src.at[c], dst.at[ctx], send_sems.at[d], recv_sems.at[d], {"ctx": c}).wait_send()


def front_kernel(n, cap, packed_ref, wo_part_ref, wr_part_ref, x_ref, table_ref, routes_ref, cot_ref, packs_ref, h_ref, weights_ref, wo_ref, wr_ref, cxs_ref, gains_ref, wall, cx, normed_ref, total, out, exch_send, exch_recv, full_send, full_recv, x_send, x_recv, y_send, y_recv, xs_send, xs_recv, ys_send, ys_recv, cx_send, cx_recv, fwd_send, fwd_recv, local_sems):
    width = x_ref.shape[1]
    shard = width // 4
    ctx, fsdp = lax.axis_index("ctx"), lax.axis_index("fsdp")
    parity = lax.rem(ctx, 2)
    core, group = neighbours()
    far, near = group[0], group[1]
    sibling, distant = flip(fsdp, 1), flip(fsdp, 2)
    other = flip(distant, 1)
    greet([core, far, group[2]] + [{"ctx": c} for c in others(n)])

    half_rows = packed_ref.shape[0] // 2
    low_rows = half_rows // 32 * 16

    def cut(k, part):
        if k == 0:
            return pl.ds(pl.multiple_of(part * half_rows, 16), low_rows)
        if k == 1:
            return pl.ds(pl.multiple_of(part * half_rows + low_rows, 16), half_rows - low_rows)
        if k == 2:
            return pl.ds(part, 1)
        return pl.ds(pl.multiple_of(part * (shard // 2), 16), shard // 2)

    sources = [packed_ref, packed_ref, wo_part_ref, wr_part_ref]
    targets = [wall, wall, wo_ref, wr_ref]
    wholes = [(packed_ref, wall), (wo_part_ref, wo_ref), (wr_part_ref, wr_ref)]

    def whole(i):
        src, dst = wholes[i]
        return send(src, dst.at[fsdp], full_send.at[i], full_recv.at[i], core)

    def own(i):
        src, dst = wholes[i]
        return pltpu.make_async_copy(src, dst.at[fsdp], local_sems.at[i])

    def to_far(k):
        return send(sources[k].at[cut(k, parity)], targets[k].at[fsdp, cut(k, parity)], x_send.at[k], x_recv.at[k], far)

    def pass_on(k, part, sems, device):
        ref = targets[k].at[distant, cut(k, part)]
        return send(ref, ref, sems[0].at[k], sems[1].at[k], device)

    def far_arrived(k):
        ref = targets[k].at[distant, cut(k, parity)]
        send(ref, ref, x_send.at[k], x_recv.at[k], far).wait_recv()
        pass_on(k, parity, (y_send, y_recv), near).start()
        pass_on(k, parity, (xs_send, xs_recv), core).start()

    def near_arrived(k):
        pass_on(k, 1 - parity, (y_send, y_recv), near).wait_recv()
        pass_on(k, 1 - parity, (ys_send, ys_recv), core).start()

    def core_arrived(k):
        for part, sems in ((parity, (xs_send, xs_recv)), (1 - parity, (ys_send, ys_recv))):
            ref = targets[k].at[other, cut(k, part)]
            send(ref, ref, sems[0].at[k], sems[1].at[k], core).wait_recv()

    own(0).start()
    to_far(0).start()
    to_far(1).start()
    whole(0).start()

    prep_kernel(cap, routes_ref, cot_ref, cx)
    send(cx, cxs_ref.at[2], cx_send.at[1], cx_recv.at[1], near).start()
    send(cx, cxs_ref.at[4], cx_send.at[3], cx_recv.at[3], core).start()
    pltpu.make_async_copy(cx, cxs_ref.at[0], local_sems.at[3]).start()
    normed, _ = norm_parts(x_ref[...])
    normed_ref[...] = normed

    def project(block, begin):
        at = pl.ds(pl.multiple_of(block * shard, shard), shard)
        gain = wall[block, shard : shard + 16, :shard].astype(F32)
        gains_ref[:, at] = gain
        h = (normed_ref[:, at] * gain[:1]).astype(BF16)
        h_ref[:, at] = h
        part = dot(h, wall[block, :shard, :])
        total[...] = part if begin else total[...] + part

    own(0).wait()
    project(fsdp, True)
    ref = wall.at[sibling]
    send(ref, ref, full_send.at[0], full_recv.at[0], core).wait_recv()
    project(sibling, False)
    far_arrived(0)
    far_arrived(1)
    for i in (1, 2):
        own(i).start()
        whole(i).start()
        to_far(i + 1).start()
    send(cx, cxs_ref.at[1], cx_send.at[0], cx_recv.at[0], far).start()
    send(cx, cxs_ref.at[3], cx_send.at[2], cx_recv.at[2], group[2]).start()
    near_arrived(0)
    near_arrived(1)
    project(distant, False)
    core_arrived(0)
    core_arrived(1)
    project(other, False)
    keep = pltpu.make_async_copy(wall, weights_ref, local_sems.at[4])
    keep.start()
    for c in range(n):
        out[c] = turn(total[:, c * PACK : (c + 1) * PACK], table_ref[...], 1.0).astype(BF16)
    exchange = (out, packs_ref, exch_send, exch_recv, local_sems.at[5], n)
    exchange_start(*exchange)

    def forward(i):
        return send(cxs_ref.at[1 + i], cxs_ref.at[5 + i], fwd_send.at[i], fwd_recv.at[i], core)

    for k in (2, 3):
        far_arrived(k)
    for i, device in ((1, near), (0, far), (2, group[2])):
        send(cx, cxs_ref.at[1 + i], cx_send.at[i], cx_recv.at[i], device).wait_recv()
        forward(i).start()
    for k in (2, 3):
        near_arrived(k)
    for k in (2, 3):
        core_arrived(k)
    for i in (1, 2):
        src, dst = wholes[i]
        ref = dst.at[sibling]
        send(ref, ref, full_send.at[i], full_recv.at[i], core).wait_recv()
        own(i).wait()
    send(cx, cxs_ref.at[4], cx_send.at[3], cx_recv.at[3], core).wait_recv()
    for i in range(3):
        forward(i).wait_recv()
    exchange_wait(*exchange)
    for i in range(3):
        whole(i).wait_send()
        forward(i).wait_send()
    for k in range(4):
        to_far(k).wait_send()
        pass_on(k, parity, (y_send, y_recv), near).wait_send()
        pass_on(k, parity, (xs_send, xs_recv), core).wait_send()
        pass_on(k, 1 - parity, (ys_send, ys_recv), core).wait_send()
    for i, (slot, device) in enumerate(((1, far), (2, near), (3, group[2]), (4, core))):
        send(cx, cxs_ref.at[slot], cx_send.at[i], cx_recv.at[i], device).wait_send()
    pltpu.make_async_copy(cx, cxs_ref.at[0], local_sems.at[3]).wait()
    keep.wait()


def front(packed, wo_part, wr_part, x, table, routes, cot, cap, n):
    tokens, width = x.shape
    hbm, vmem = pl.BlockSpec(memory_space=pl.ANY), pl.BlockSpec(memory_space=pltpu.VMEM)
    dma = lambda k: pltpu.SemaphoreType.DMA((k,))
    shaped = lambda shape, dtype=BF16: jax.ShapeDtypeStruct(shape, dtype)
    cx_shape = (tokens + EXPERTS, width)
    return pl.pallas_call(
        functools.partial(front_kernel, n, cap),
        in_specs=[hbm, hbm, hbm, vmem, vmem, vmem, vmem],
        out_specs=[hbm, vmem, hbm, hbm, hbm, hbm, vmem],
        out_shape=[
            shaped((n, tokens, PACK)),
            shaped((tokens, width)),
            shaped((4,) + packed.shape),
            shaped((4,) + wo_part.shape),
            shaped((4,) + wr_part.shape),
            shaped((8,) + cx_shape),
            shaped((16, width), F32),
        ],
        scratch_shapes=[
            pltpu.VMEM((4,) + packed.shape, BF16),
            pltpu.VMEM(cx_shape, BF16),
            pltpu.VMEM((tokens, width), F32),
            pltpu.VMEM((tokens, n * PACK), F32),
            pltpu.VMEM((n, tokens, PACK), BF16),
            dma(n - 1),
            dma(n - 1),
            dma(3),
            dma(3),
        ]
        + [dma(4)] * 10
        + [dma(3), dma(3), dma(6)],
        compiler_params=params(collective_id=1, has_side_effects=True),
        cost_estimate=cost(2e9, 5e7),
        name="front",
    )(packed, wo_part, wr_part, x, table, routes, cot)


def mid_kernel(n, number, capp, attn_ref, cxs_ref, wo_ref, wr_ref, x_ref, gain_ref, middle_ref, h_ref, kept_ref, xs_ref, gs_ref, gates_ref, arrived, hs, total, exch_send, exch_recv, hop_send, hop_recv, fwd_send, fwd_recv, local_sems):
    tokens, width = x_ref.shape
    ctx, fsdp = lax.axis_index("ctx"), lax.axis_index("fsdp")
    first = (fsdp * 2 + lax.rem(ctx, 2)) * number
    core, group = neighbours()
    greet([core, group[0], group[2]] + [{"ctx": c} for c in others(n)])
    exchange = (attn_ref, arrived, exch_send, exch_recv, local_sems.at[0], n)
    exchange_start(*exchange)
    total[...] = jnp.zeros_like(total)

    def take(c):
        total[...] += dot(arrived[c], wo_ref[c])

    exchange_wait(*exchange, take)
    keep = pltpu.make_async_copy(arrived, kept_ref, local_sems.at[1])
    keep.start()
    middle = x_ref[...] + RESIDUAL * total[...]
    middle_ref[...] = middle
    normed, _ = norm_parts(middle)
    h = (normed * gain_ref[...]).astype(BF16)
    h_ref[...] = h
    hs[0] = h

    def hop(i):
        return send(hs.at[0], hs.at[1 + i], hop_send.at[i], hop_recv.at[i], (group + [core])[i])

    def forward(i):
        return send(hs.at[1 + i], hs.at[5 + i], fwd_send.at[i], fwd_recv.at[i], core)

    for i in (2, 0, 1, 3):
        hop(i).start()

    def place(b):
        h = hs[b]
        logits = jnp.transpose(dot(h, wr_ref[...]))[:EXPERTS, :]
        raw = jnp.exp(logits - jnp.max(logits, 0, keepdims=True))
        router = raw / jnp.sum(raw, 0, keepdims=True)
        slots = cxs_ref[b, tokens:, :tokens].astype(F32)
        hots = one_hot(slots, first, number, capp)
        places = jnp.concatenate(hots, 0).astype(BF16)
        rows = dot(places, h).astype(BF16)
        grads = dot(places, cxs_ref[b, :tokens, :]).astype(BF16)
        for j in range(number):
            at = slice(j * capp, (j + 1) * capp)
            xs_ref[j, b] = rows[at]
            gs_ref[j, b] = grads[at]
            gate = jnp.sum(hots[j] * own_row(router, first + j), 1, keepdims=True)
            gates_ref[j, b] = jnp.broadcast_to(gate, (capp, 128))

    place(0)
    hop(3).wait_recv()
    place(4)
    for i in (0, 1, 2):
        hop(i).wait_recv()
        forward(i).start()
        place(1 + i)
    for i in (0, 1, 2):
        forward(i).wait_recv()
        place(5 + i)
    for i in range(4):
        hop(i).wait_send()
    for i in range(3):
        forward(i).wait_send()
    keep.wait()


def mid_step(attn, cxs, wo, wr, x, gain, number, capp, n):
    tokens, width = x.shape
    hbm, vmem = pl.BlockSpec(memory_space=pl.ANY), pl.BlockSpec(memory_space=pltpu.VMEM)
    dma = lambda k: pltpu.SemaphoreType.DMA((k,))
    shaped = lambda shape, dtype=BF16: jax.ShapeDtypeStruct(shape, dtype)
    return pl.pallas_call(
        functools.partial(mid_kernel, n, number, capp),
        in_specs=[hbm, vmem, vmem, vmem, vmem, vmem],
        out_specs=[vmem, vmem, hbm, vmem, vmem, vmem],
        out_shape=[
            shaped((tokens, width), F32),
            shaped((tokens, width)),
            shaped(attn.shape),
            shaped((number, 8, capp, width)),
            shaped((number, 8, capp, width)),
            shaped((number, 8, capp, 128), F32),
        ],
        scratch_shapes=[
            pltpu.VMEM(attn.shape, BF16),
            pltpu.VMEM((8, tokens, width), BF16),
            pltpu.VMEM((tokens, width), F32),
            dma(n - 1),
            dma(n - 1),
            dma(4),
            dma(4),
            dma(3),
            dma(3),
            dma(2),
        ],
        compiler_params=params(collective_id=2, has_side_effects=True),
        cost_estimate=cost(4e9, 5e7),
        name="mid_step",
    )(attn, cxs, wo, wr, x, gain)


RING = 8
ORDER_X, ORDER_Y, ORDER_CORE = 1, 2, 4


class GroupSum:
    def __init__(self, part, land, land_x, land_y, own, sems, core, group):
        self.part, self.land, self.land_x, self.land_y, self.own = part, land, land_x, land_y, own
        self.core_send, self.core_recv, self.x_send, self.x_recv, self.y_send, self.y_recv, self.load = sems
        self.core, self.far, self.near = core, group[0], group[1]

    def to_core(self, i):
        return send(self.part.at[4 + i], self.land.at[i], self.core_send.at[i], self.core_recv.at[i], self.core)

    def to_far(self, k):
        return send(self.land.at[1 + 2 * k], self.land_x.at[k], self.x_send.at[k], self.x_recv.at[k], self.far)

    def to_near(self):
        return send(self.land.at[2], self.land_y, self.y_send.at[0], self.y_recv.at[0], self.near)

    def fetch(self, i):
        return pltpu.make_async_copy(self.part.at[i], self.own.at[i % 2], self.load.at[i % 2])

    def start(self):
        for i in (1, 3, 2, 0):
            self.to_core(i).start()

    def over_cores(self):
        order = (1, 3, 2, 0)
        if self.own is not None:
            self.fetch(1).start()
        for step, i in enumerate(order):
            if self.own is None:
                mine = self.part[i]
            else:
                self.fetch(i).wait()
                mine = self.own[i % 2]
            self.to_core(i).wait_recv()
            self.land[i] = (self.land[i].astype(F32) + mine.astype(F32)).astype(BF16)
            if self.own is not None and step < 3:
                self.fetch(order[step + 1]).start()
            if i % 2 == 1:
                self.to_far(i // 2).start()

    def over_x(self):
        for k in (1, 0):
            self.to_far(k).wait_recv()
            self.land[2 * k] = (self.land[2 * k].astype(F32) + self.land_x[k].astype(F32)).astype(BF16)
            if k == 1:
                self.to_near().start()

    def finish(self):
        self.to_near().wait_recv()
        for i in range(4):
            self.to_core(i).wait_send()
        for k in range(2):
            self.to_far(k).wait_send()
        self.to_near().wait_send()
        return self.land[0].astype(F32) + self.land_y[...].astype(F32)


class LineSum:
    def __init__(self, count, own_ref, other_ref, inbox, across, mine, sems):
        self.count, self.own_ref, self.other_ref = count, own_ref, other_ref
        self.inbox, self.across, self.mine = inbox, across, mine
        self.line_send, self.line_recv, self.mid_send, self.mid_recv, self.side_send, self.side_recv, self.store, self.load = sems
        ctx = lax.axis_index("ctx")
        z = ctx // 2
        self.middle = (z == 1) | (z == 2)
        self.line = {"ctx": jnp.where(z % 2 == 0, ctx + 2, ctx - 2)}
        self.peer = {"ctx": jnp.where(z == 1, ctx + 2, ctx - 2)}
        self.side = {"ctx": flip(ctx, 1)}

    def send_line(self, src, i):
        s = lax.rem(i, RING)
        return send(src, self.inbox.at[s], self.line_send.at[s], self.line_recv.at[s], self.line)

    def send_mid(self, i):
        s = lax.rem(i, RING)
        return send(self.inbox.at[s], self.across.at[s], self.mid_send.at[s], self.mid_recv.at[s], self.peer)

    def send_side(self, src, i):
        return send(src, self.other_ref.at[i], self.side_send.at[lax.rem(i, RING)], self.side_recv.at[i], self.side)

    def keep(self, src, i):
        return pltpu.make_async_copy(src, self.own_ref.at[i], self.store.at[lax.rem(i, RING)])

    def drain_middle(self, i):
        src = self.across.at[lax.rem(i, RING)]
        self.send_line(src, i).wait_send()
        self.send_side(src, i).wait_send()
        self.keep(src, i).wait()

    def drain_end(self, i):
        src = self.inbox.at[lax.rem(i, RING)]
        self.send_side(src, i).wait_send()
        self.keep(src, i).wait()

    def tick(self, t, source):
        count = self.count
        fixed = isinstance(t, int)

        def when(condition):
            if fixed:
                return (lambda f: f()) if condition else (lambda f: None)
            return pl.when(condition)

        i32 = (lambda v: jnp.int32(v)) if fixed else (lambda v: v)

        @pl.when(self.middle)
        def _():
            @when(t < count)
            def _():
                @when(t >= 6)
                def _():
                    self.drain_middle(i32(t - 6))

                s = lax.rem(i32(t), RING)
                fetch = pltpu.make_async_copy(source(t), self.mine, self.load.at[0])
                fetch.start()
                self.send_line(self.inbox.at[s], i32(t)).wait_recv()
                fetch.wait()
                self.inbox[s] = self.inbox[s] + self.mine[...]
                self.send_mid(i32(t)).start()

            @when((t >= 1) & (t <= count))
            def _():
                i = i32(t - 1)
                s = lax.rem(i, RING)
                self.send_mid(i).wait()
                self.across[s] = self.across[s] + self.inbox[s]
                self.send_line(self.across.at[s], i).start()
                self.send_side(self.across.at[s], i).start()
                self.keep(self.across.at[s], i).start()

        @pl.when(jnp.logical_not(self.middle))
        def _():
            @when(t < count)
            def _():
                @when(t >= 8)
                def _():
                    self.drain_end(i32(t - 8))

                @when(t >= 2)
                def _():
                    self.send_line(self.mine, i32(t - 2)).wait_send()

                self.send_line(source(t), i32(t)).start()

            @when(t >= 4)
            def _():
                i = i32(t - 4)
                s = lax.rem(i, RING)
                self.send_line(self.inbox.at[s], i).wait_recv()
                self.send_side(self.inbox.at[s], i).start()
                self.keep(self.inbox.at[s], i).start()

    def finish(self):
        count = self.count

        @pl.when(self.middle)
        def _():
            for i in range(count - 6, count):
                self.drain_middle(jnp.int32(i))

        @pl.when(jnp.logical_not(self.middle))
        def _():
            for i in range(count - 2, count):
                self.send_line(self.mine, jnp.int32(i)).wait_send()
            for i in range(count - 8, count):
                self.drain_end(jnp.int32(i))

        def arrived(i, carry):
            self.send_side(self.mine, i).wait_recv()
            return carry

        lax.fori_loop(0, count, arrived, 0)


def backward_kernel(
    n,
    length,
    ends_ref,
    pieces_ref,
    gx_ref,
    yp_ref,
    full_ref,
    weights_ref,
    packs_hbm,
    table_hbm,
    h_ref,
    middle_ref,
    cot_ref,
    wr_ref,
    wo_ref,
    gains_ref,
    attn_ref,
    lse_ref,
    x_ref,
    h_attn_ref,
    own_ref,
    other_ref,
    grad_x_ref,
    mixed_ref,
    inbox,
    across,
    mine,
    gx_land,
    gx_x,
    gx_y,
    gx_own,
    y_land,
    y_x,
    y_y,
    y_own,
    small,
    s_land,
    s_x,
    s_y,
    packs,
    table,
    keys,
    values,
    keys_t,
    grad_q,
    grad_k,
    grad_v,
    acc,
    full_buf,
    ga,
    ga_in,
    pack_out,
    grads_in,
    wbuf,
    total,
    grad_middle,
    dgain,
    col,
    line_send,
    line_recv,
    mid_send,
    mid_recv,
    side_send,
    side_recv,
    line_store,
    line_load,
    ga_send,
    ga_recv,
    gr_send,
    gr_recv,
    rs_sems,
    local_sems,
    full_sems,
    w_sems,
):
    tokens, width = h_ref.shape
    half = length // 2
    rows = tokens // 2
    shard = width // 4
    blocks = length // BLK
    ctx, fsdp = lax.axis_index("ctx"), lax.axis_index("fsdp")
    core, group = neighbours()
    experts = pieces_ref.shape[0]
    line = LineSum(experts + 2, own_ref, other_ref, inbox, across, mine, (line_send, line_recv, mid_send, mid_recv, side_send, side_recv, line_store, line_load))
    source = lambda t: pieces_ref.at[t]
    tick = lambda t: line.tick(t, source)
    sems = lambda k: [rs_sems.at[k, j] for j in range(7)]
    gx = GroupSum(gx_ref, gx_land, gx_x, gx_y, gx_own, sems(0), core, group)
    ys = GroupSum(yp_ref, y_land, y_x, y_y, y_own, sems(1), core, group)
    ws = GroupSum(small, s_land, s_x, s_y, None, sems(2), core, group)

    greet([core, group[0], group[2]] + [{"ctx": c} for c in others(n)])
    gx.start()
    load_packs = pltpu.make_async_copy(packs_hbm, packs, local_sems.at[0])
    load_table = pltpu.make_async_copy(table_hbm, table, local_sems.at[1])
    load_packs.start()
    load_table.start()
    small[:, PIECE // 2 : PIECE, :] = jnp.zeros((8, PIECE // 2, PIECE), BF16)

    def strip(r):
        f = fsdp
        if r & ORDER_X:
            f = flip(f, 2)
        if r & ORDER_CORE:
            f = flip(f, 1)
        y = lax.rem(ctx, 2)
        return 2 * f + (1 - y if r & ORDER_Y else y)

    tick(0)
    gx.over_cores()
    tick(1)
    gx.over_x()
    tick(2)
    arrived = gx.finish()
    ys.start()

    h = h_ref[...]
    gain = gains_ref[1:2]
    extra = arrived[tokens:, :]
    grad_router = extra[:, :tokens] + extra[:, tokens : 2 * tokens]
    grad_router = jnp.transpose(jnp.concatenate([grad_router, jnp.zeros((128 - EXPERTS, tokens), F32)], 0))
    logits = dot(h, wr_ref[...])
    logits = jnp.where(lane_iota(logits.shape) < EXPERTS, logits, MASKED)
    raw = jnp.exp(logits - jnp.max(logits, -1, keepdims=True))
    router = raw / jnp.sum(raw, -1, keepdims=True)
    grad_logits = (router * (grad_router - jnp.sum(router * grad_router, -1, keepdims=True))).astype(BF16)
    grad_h = arrived[:tokens, :] + dot(grad_logits, wr_ref[...], NT)
    normed, scale = norm_parts(middle_ref[...])
    dgain[1:2, :] = jnp.sum(grad_h * normed, 0, keepdims=True)
    grad_mid = cot_ref[...] + norm_back(grad_h * gain, normed, scale)
    grad_middle[...] = grad_mid
    grad_branch = (RESIDUAL * grad_mid).astype(BF16)
    for c in range(n):
        ga[c] = dot(grad_branch, wo_ref[c], NT).astype(BF16)
    ga_exchange = (ga, ga_in, ga_send, ga_recv, local_sems.at[2], n)
    exchange_start(*ga_exchange)
    tick(3)
    col[:, :128] = dot(h, grad_logits, TN).astype(BF16)
    for r in range(8):
        at = strip(r)
        dwo = dot(attn_ref[at], grad_branch, TN).astype(BF16)
        small[r, 0:128, :] = dwo[:, :PIECE]
        small[r, 128:256, :] = dwo[:, PIECE:]
        small[r, 256:384, 0:128] = col[pl.ds(pl.multiple_of(at * 128, 128), 128), 0:128]
    load_packs.wait()
    for hh in range(2):
        for c in range(n):
            kk, vv = pair_keys(packs[c, hh, :, 128:256].astype(F32))
            at = hh * half + c * rows
            keys[at : at + rows, :] = kk.astype(BF16)
            values[at : at + rows, :] = vv.astype(BF16)
            keys_t[:, at : at + rows] = jnp.transpose(kk).astype(BF16)
    grad_k[...] = jnp.zeros_like(grad_k)
    grad_v[...] = jnp.zeros_like(grad_v)
    ys.over_cores()
    tick(4)
    exchange_wait(*ga_exchange)

    per = BLK // rows
    per_half = blocks // 2

    def fetch_full(b):
        return pltpu.make_async_copy(full_ref.at[b], full_buf.at[lax.rem(b, 2)], full_sems.at[lax.rem(b, 2)])

    fetch_full(jnp.int32(0)).start()

    def attend(block, carry):
        late = block // per_half
        c0 = lax.rem(block, per_half) * per
        q2 = stack_heads(jnp.concatenate([packs[c0 + k, late, :, :128] for k in range(per)], 0))
        g2 = stack_heads(jnp.concatenate([ga_in[c0 + k, pl.ds(pl.multiple_of(late * rows, rows), rows), :] for k in range(per)], 0))
        position, start = query_rows(ends_ref, block, length)
        lse = lse_ref[block]

        @pl.when(block + 1 < blocks)
        def _():
            fetch_full(block + 1).start()

        fetch_full(block).wait()
        delta = jnp.sum(jnp.transpose(g2.astype(F32)) * full_buf[lax.rem(block, 2)], 0, keepdims=True)
        acc[...] = jnp.zeros_like(acc)

        def body(kb, carry):
            at = pl.multiple_of(kb * BLK, BLK)
            scores = dot(keys[pl.ds(at, BLK), :], q2, NT) * ATTN_SCALE
            where = key_position(kb, length)
            probs = jnp.where((where <= position) & (where >= start), jnp.exp(scores - lse), 0.0)
            grad_probs = dot(values[pl.ds(at, BLK), :], g2, NT)
            grad_scores = (probs * (grad_probs - delta)).astype(BF16)
            acc[...] += dot(keys_t[:, pl.ds(at, BLK)], grad_scores)
            grad_k[pl.ds(at, BLK), :] += dot(grad_scores, q2)
            grad_v[pl.ds(at, BLK), :] += dot(probs.astype(BF16), g2)
            return carry

        block_loop(block, per_half, body, 0)
        grad_q[pl.ds(pl.multiple_of(block * BLK, BLK), BLK), :] = fold_heads(jnp.transpose(acc[...]))

        @pl.when(lax.rem(block, 2) == 1)
        def _():
            tick(5 + block // 2)

        return carry

    lax.fori_loop(0, blocks, attend, 0)
    load_table.wait()
    for c in range(n):
        for hh in range(2):
            at = slice(hh * half + c * rows, hh * half + (c + 1) * rows)
            kk = grad_k[at, :]
            vv = grad_v[at, :]
            kk = (kk + pltpu.roll(kk, 64, 1)) * ATTN_SCALE
            vv = vv + pltpu.roll(vv, 64, 1)
            both = jnp.where(lane_iota(kk.shape) < 64, kk, vv)
            package = jnp.concatenate([grad_q[at, :] * ATTN_SCALE, both], -1)
            pack_out[c, hh * rows : (hh + 1) * rows, :] = turn(package, table[at, :], -1.0).astype(BF16)
    gr_exchange = (pack_out, grads_in, gr_send, gr_recv, local_sems.at[3], n)
    exchange_start(*gr_exchange)

    def fetch_w(c):
        slot = lax.rem(c, 2)
        return pltpu.make_async_copy(weights_ref.at[:, :, pl.ds(pl.multiple_of(c * PACK, PACK), PACK)], wbuf.at[slot], w_sems.at[slot])

    fetch_w(jnp.int32(0)).start()
    ys.over_x()
    tick(9)
    total[...] = jnp.zeros_like(total)
    mixed_ref[...] = middle_ref[...] + RESIDUAL * ys.finish()
    tick(10)
    exchange_wait(*gr_exchange)

    def finish_columns(c, carry):
        @pl.when(c + 1 < n)
        def _():
            fetch_w(c + 1).start()

        fetch_w(c).wait()
        slot = lax.rem(c, 2)
        g = grads_in[c]
        col[...] = dot(h_attn_ref[...], g, TN).astype(BF16)
        for r in range(8):
            at = pl.ds(pl.multiple_of(strip(r) * 128, 128), 128)
            small[r, pl.ds(pl.multiple_of(PIECE + c // 2 * 128, 128), 128), pl.ds(pl.multiple_of(lax.rem(c, 2) * PACK, PACK), PACK)] = col[at, :]
        for f in range(4):
            total[:, f * shard : (f + 1) * shard] += dot(g, wbuf[slot, f, :shard, :], NT)

        @pl.when(lax.rem(c, 4) == 3)
        def _():
            tick(11 + c // 4)

        return carry

    lax.fori_loop(0, n, finish_columns, 0)
    normed, scale = norm_parts(x_ref[...])
    grad_h = total[...]
    dgain[0:1, :] = jnp.sum(grad_h * normed, 0, keepdims=True)
    grad_x_ref[...] = grad_middle[...] + norm_back(grad_h * gains_ref[0:1], normed, scale)
    for r in range(8):
        at = pl.ds(pl.multiple_of(strip(r) * 128, 128), 128)
        row = row_iota((16, 128))
        both = jnp.where(row == 0, dgain[0:1, at], jnp.where(row == 1, dgain[1:2, at], 0.0))
        small[r, 384:400, 0:128] = both.astype(BF16)
    ws.start()
    tick(13)
    ws.over_cores()
    tick(14)
    ws.over_x()
    tick(15)
    tick(16)
    s_land[0] = ws.finish().astype(BF16)

    def rest(t, carry):
        tick(t)
        return carry

    lax.fori_loop(17, experts, rest, 0)
    late_source = lambda t: s_land.at[0, pl.ds((t - experts) * PIECE, PIECE)]
    for t in range(experts, experts + 6):
        line.tick(t, late_source)
    line.finish()


def backward_step(ends, pieces, gx, yp, full, weights, packs, table, h, middle, cot, wr, wo, gains, attn, lse, x, h_attn, n, length):
    tokens, width = x.shape
    hbm, vmem = pl.BlockSpec(memory_space=pl.ANY), pl.BlockSpec(memory_space=pltpu.VMEM)
    smem = pl.BlockSpec(memory_space=pltpu.SMEM)
    dma = lambda *k: pltpu.SemaphoreType.DMA(k)
    shaped = lambda shape, dtype=BF16: jax.ShapeDtypeStruct(shape, dtype)
    count = pieces.shape[0] + 2
    piece = (PIECE, PIECE)
    gx_shape, y_shape, s_shape = gx.shape[1:], yp.shape[1:], (2 * PIECE, PIECE)
    return pl.pallas_call(
        functools.partial(backward_kernel, n, length),
        in_specs=[smem] + [hbm] * 7 + [vmem] * 10,
        out_specs=[hbm, hbm, vmem, vmem],
        out_shape=[
            shaped((count,) + piece),
            shaped((count,) + piece),
            shaped((tokens, width), F32),
            shaped((tokens, width), F32),
        ],
        scratch_shapes=[
            pltpu.VMEM((RING,) + piece, BF16),
            pltpu.VMEM((RING,) + piece, BF16),
            pltpu.VMEM(piece, BF16),
            pltpu.VMEM((4,) + gx_shape, BF16),
            pltpu.VMEM((2,) + gx_shape, BF16),
            pltpu.VMEM(gx_shape, BF16),
            pltpu.VMEM((2,) + gx_shape, BF16),
            pltpu.VMEM((4,) + y_shape, BF16),
            pltpu.VMEM((2,) + y_shape, BF16),
            pltpu.VMEM(y_shape, BF16),
            pltpu.VMEM((2,) + y_shape, BF16),
            pltpu.VMEM((8,) + s_shape, BF16),
            pltpu.VMEM((4,) + s_shape, BF16),
            pltpu.VMEM((2,) + s_shape, BF16),
            pltpu.VMEM(s_shape, BF16),
            pltpu.VMEM(packs.shape, BF16),
            pltpu.VMEM(table.shape, F32),
            pltpu.VMEM((length, 128), BF16),
            pltpu.VMEM((length, 128), BF16),
            pltpu.VMEM((128, length), BF16),
            pltpu.VMEM((length, 128), F32),
            pltpu.VMEM((length, 128), F32),
            pltpu.VMEM((length, 128), F32),
            pltpu.VMEM((128, 2 * BLK), F32),
            pltpu.VMEM((2, 128, 2 * BLK), F32),
            pltpu.VMEM((n, tokens, 128), BF16),
            pltpu.VMEM((n, tokens, 128), BF16),
            pltpu.VMEM((n, tokens, PACK), BF16),
            pltpu.VMEM((n, tokens, PACK), BF16),
            pltpu.VMEM((2, 4, weights.shape[1], PACK), BF16),
            pltpu.VMEM((tokens, width), F32),
            pltpu.VMEM((tokens, width), F32),
            pltpu.VMEM((8, width), F32),
            pltpu.VMEM((width, PACK), BF16),
            dma(RING),
            dma(RING),
            dma(RING),
            dma(RING),
            dma(RING),
            dma(count),
            dma(RING),
            dma(1),
            dma(n - 1),
            dma(n - 1),
            dma(n - 1),
            dma(n - 1),
            dma(3, 7, 4),
            dma(4),
            dma(2),
            dma(2),
        ],
        compiler_params=params(63, collective_id=0, has_side_effects=True),
        cost_estimate=cost(4e10, 1e9),
        name="backward_step",
    )(ends, pieces, gx, yp, full, weights, packs, table, h, middle, cot, wr, wo, gains, attn, lse, x, h_attn)


def local(
    inputs,
    cotangent,
    doc_lengths,
    routes,
    attn_gain,
    ffn_gain,
    w_query,
    key_weight,
    value_weight,
    w_out,
    w_router,
    w_gate,
    w_up,
    w_down,
):
    rows = inputs.shape[2]
    width = inputs.shape[3]
    n = lax.axis_size("ctx")
    fsdp = lax.axis_size("fsdp")
    me, mine = lax.axis_index("ctx"), lax.axis_index("fsdp")
    tokens = 2 * rows
    length = tokens * n
    experts_here = w_gate.shape[0]
    number = experts_here // 2
    capacity = 5 * tokens * TOP // (4 * EXPERTS)
    capp = -(-capacity // 16) * 16
    shard = width // fsdp
    heads = QUERY_HEADS // n
    head_lanes = heads * HEAD_DIMENSION
    copies = n // KEY_VALUE_HEADS
    bits = group_bits(fsdp)

    x = inputs.reshape(tokens, width)
    cot = cotangent.reshape(tokens, width)
    side = me % 2
    base = (side * number).astype(jnp.int32).reshape(1)
    first = (mine * experts_here + side * number).astype(jnp.int32).reshape(1)
    index = jnp.stack([side * number, (1 - side) * number]).astype(jnp.int32)
    ends = jnp.cumsum(doc_lengths[0])[:3].astype(jnp.int32)
    table = jnp.asarray(rotary_table(length))
    own_table = lax.dynamic_slice_in_dim(table.reshape(2, n, rows, 256), me, 1, 1).reshape(tokens, 256)

    query_part = w_query.reshape(shard, n, head_lanes)
    if head_lanes < 128:
        query_part = jnp.pad(query_part, ((0, 0), (0, 0), (0, 128 - head_lanes)))
    key_part = jnp.repeat(key_weight.reshape(shard, KEY_VALUE_HEADS, HEAD_DIMENSION), copies, 1)
    value_part = jnp.repeat(value_weight.reshape(shard, KEY_VALUE_HEADS, HEAD_DIMENSION), copies, 1)
    packed = jnp.concatenate([query_part, key_part, value_part], -1).reshape(shard, n * PACK)
    padding = 2 * 16 * (shard // 32 + 1) - shard
    gains = jnp.pad(jnp.stack([attn_gain, ffn_gain]), ((0, padding - 2), (0, n * PACK - shard)))
    packed = jnp.concatenate([packed, gains], 0)
    out_part = w_out.reshape(shard // head_lanes, head_lanes, width)
    if head_lanes < 128:
        out_part = jnp.pad(out_part, ((0, 0), (0, 128 - head_lanes), (0, 0)))
    router_part = jnp.pad(w_router, ((0, 0), (0, 128 - EXPERTS)))
    merge = lambda a: a.reshape(number, -1, a.shape[-1])

    if n == 8 and fsdp == 4:
        packs, h_attn, weights, wo, wr, cxs, gains = front(packed, out_part, router_part, x, own_table, routes.reshape(tokens, TOP), cot, capacity, n)
        gain_one, gain_two = gains[0:1], gains[1:2]
        wo, wr = wo.reshape(n, 128, width), wr.reshape(width, 128)
        packs = packs.reshape(n, 2, rows, PACK)
        attn, lse, full = attn_forward(ends, packs, length)
        middle, h_ffn, attn, xs, gs, gates = mid_step(attn.reshape(n, tokens, 128), cxs, wo, wr, x, gain_two, number, capp, n)
    else:
        weights = lax.all_gather(packed, "fsdp", axis=0)
        gain_one = weights[:, shard, :shard].reshape(1, width).astype(F32)
        gain_two = weights[:, shard + 1, :shard].reshape(1, width).astype(F32)
        wo = lax.all_gather(out_part, "fsdp", axis=0, tiled=True)
        wr = lax.all_gather(router_part, "fsdp", axis=0, tiled=True)
        cxs = group_gather(prep(routes.reshape(tokens, TOP), cot, capacity), bits)
        packs, h_attn = qkv(x, gain_one, weights, own_table, shard, n)
        packs = lax.all_to_all(packs, "ctx", split_axis=0, concat_axis=0, tiled=True).reshape(n, 2, rows, PACK)
        attn, lse, full = attn_forward(ends, packs, length)
        attn = lax.all_to_all(attn.reshape(n, tokens, 128), "ctx", split_axis=0, concat_axis=0, tiled=True)
        middle, h_ffn = middle_step(attn, wo, x, gain_two)
        xs, gs, gates = gather_rows(first, group_gather(h_ffn, bits), cxs, jnp.transpose(wr), number, capp)
    xs, gs, gates = merge(xs), merge(gs), merge(gates)
    pieces, outs, back, dgates = expert_step(base, xs, gs, gates, w_gate, w_up, w_down)
    y_part, gx_part = combine(first, cxs, outs, back, dgates, tokens, capp)
    pieces = pieces.reshape(number * 6, PIECE, PIECE)
    if n == 8 and fsdp == 4:
        own, other, grad_x, mixed = backward_step(
            ends, pieces, gx_part, y_part, full, weights, packs, table, h_ffn, middle, cot, wr, wo, gains, attn, lse, x, h_attn, n, length
        )
        low = jnp.where(side == 0, own[number * 6 :], other[number * 6 :]).astype(F32)
        high = jnp.where(side == 0, other[number * 6 :], own[number * 6 :]).astype(F32)
        unfold = lambda a, k: jnp.transpose(a.reshape(k, shard // 2, PIECE), (1, 0, 2)).reshape(shard // 2, k * PIECE)
        stack = lambda f: jnp.concatenate([f(low), f(high)], 0)
        dwo = stack(lambda a: unfold(a[0, :256], 2))
        dwr = stack(lambda a: a[0, 256:384, :EXPERTS])
        dgain_one = stack(lambda a: a[0, 384, :128])
        dgain_two = stack(lambda a: a[0, 385, :128])
        dw = stack(lambda a: unfold(a[1], 4)).reshape(shard, n, PACK)
    else:
        gx = group_reduce(gx_part, bits)
        grad_middle, dwo, grad_attn, dwr, dgain_two = home_step(gx, h_ffn, middle, cot, wr, wo, gain_two, attn)
        grad_attn = lax.all_to_all(grad_attn, "ctx", split_axis=0, concat_axis=0, tiled=True).reshape(n, 2, rows, 128)
        grads = attn_backward(ends, packs, grad_attn, lse, full, table, length)
        grads = lax.all_to_all(grads.reshape(n, tokens, PACK), "ctx", split_axis=0, concat_axis=0, tiled=True)
        dw, grad_x, dgain_one = final_step(grads, weights, h_attn, x, gain_one, grad_middle, shard)
        mixed = middle + RESIDUAL * group_reduce(y_part, bits).astype(F32)
        own = line_sum(pieces, n)
        other = swap(own, "ctx", 1)
        scatter = lambda a: lax.psum(lax.psum_scatter(a, "fsdp", scatter_dimension=0, tiled=True), "ctx").astype(F32)
        dwo = scatter(dwo)[:, :head_lanes, :].reshape(shard, width)
        small = jnp.concatenate([dwr[:, :EXPERTS], dgain_two.reshape(width, 1).astype(BF16)], 1)
        small = scatter(jnp.pad(small, ((0, 0), (0, 127 - EXPERTS))))
        dwr, dgain_two = small[:, :EXPERTS], small[:, EXPERTS]
        dw = scatter(dw).reshape(shard, n, PACK)
        dgain_one = scatter(dgain_one.reshape(width).astype(BF16))

    outs = [widen(index, own, other, m, w.shape) for m, w in enumerate((w_gate, w_up, w_down))]
    fold = lambda a: a.reshape(shard, KEY_VALUE_HEADS, copies, HEAD_DIMENSION).sum(2).reshape(shard, -1)
    return (
        mixed.reshape(inputs.shape),
        grad_x.reshape(inputs.shape),
        dgain_one,
        dgain_two,
        dw[:, :, :head_lanes].reshape(shard, -1),
        fold(dw[:, :, 128:192]),
        fold(dw[:, :, 192:256]),
        dwo,
        dwr,
        outs[0],
        outs[1],
        outs[2],
    )


def solution(mesh):
    tokens = P("fsdp", None, "ctx", None)
    one, two, three = P("fsdp"), P("fsdp", None), P("fsdp", None, None)
    return jax.shard_map(
        local,
        mesh=mesh,
        in_specs=(tokens, tokens, two, tokens, one, one, two, two, two, two, two, three, three, three),
        out_specs=(tokens, tokens, one, one, two, two, two, two, two, three, three, three),
        check_vma=False,
    )
```

```python
import functools

import jax
import jax.numpy as jnp
import numpy as np
from jax import lax
from jax.experimental import pallas as pl
from jax.experimental.pallas import tpu as pltpu
from jax.sharding import PartitionSpec as P

QUERY_HEADS = 16
KEY_VALUE_HEADS = 8
HEAD_DIMENSION = 64
EXPERTS = 32
TOP = 8

ATTN_SCALE = 0.015625
RESIDUAL = 0.22
NORM_EPS = 1e-06
ROPE_BASE = 10000.0
MASKED = -1e30

F32 = jnp.float32
BF16 = jnp.bfloat16
MIB = 1 << 20
NT = (((1,), (1,)), ((), ()))
TN = (((0,), (0,)), ((), ()))
BLK = 256
PACK = 256


def dot(a, b, dims=None):
    if dims is None:
        return jnp.dot(a, b, preferred_element_type=F32)
    return lax.dot_general(a, b, dims, preferred_element_type=F32)


def params(limit=56, **kw):
    return pltpu.CompilerParams(vmem_limit_bytes=limit * MIB, **kw)


def cost(flops, bytes_accessed):
    return pl.CostEstimate(flops=int(flops), bytes_accessed=int(bytes_accessed), transcendentals=0)


def lane_iota(shape):
    return lax.broadcasted_iota(jnp.int32, shape, len(shape) - 1)


def row_iota(shape):
    return lax.broadcasted_iota(jnp.int32, shape, len(shape) - 2)


def rotary_table(length):
    half = length // 2
    order = np.arange(half, dtype=np.float32)
    positions = np.concatenate([order, length - 1 - order]).astype(np.float32)
    m = np.arange(HEAD_DIMENSION // 2, dtype=np.float64)
    frequency = (ROPE_BASE ** (-2.0 * m / HEAD_DIMENSION)).astype(np.float32)
    angles = (positions[:, None] * frequency[None, :]).astype(np.float64)
    cosine, sine = np.cos(angles), np.sin(angles)
    cos_head = np.concatenate([cosine, cosine], -1)
    sin_head = np.concatenate([-sine, sine], -1)
    return np.concatenate([cos_head, cos_head, sin_head, sin_head], -1).astype(np.float32)


def turn(v, table, direction):
    lanes = lane_iota(v.shape)
    cosine = jnp.concatenate([table[:, :128], table[:, :128]], -1)
    sine = jnp.concatenate([table[:, 128:], table[:, 128:]], -1)
    turned = lanes < 3 * HEAD_DIMENSION
    swapped = jnp.where(lanes % HEAD_DIMENSION < HEAD_DIMENSION // 2, pltpu.roll(v, PACK - 32, 1), pltpu.roll(v, 32, 1))
    return jnp.where(turned, v * cosine + direction * (swapped * sine), v)


def norm_parts(values):
    inv_rms = lax.rsqrt(jnp.mean(values * values, -1, keepdims=True) + NORM_EPS)
    return values * inv_rms, inv_rms


def norm_back(grad_normed, normed, inv_rms):
    return inv_rms * (grad_normed - normed * jnp.mean(grad_normed * normed, -1, keepdims=True))


def prep_kernel(cap, routes_ref, cot_ref, out_ref):
    tokens, width = cot_ref.shape
    routes = routes_ref[...]
    earlier = (lane_iota((tokens, tokens)) < row_iota((tokens, tokens))).astype(BF16)
    experts = lane_iota((tokens, 128))
    base = jnp.zeros((1, 128), F32)
    plus = jnp.zeros((tokens, 128), F32)
    for k in range(TOP):
        chosen = experts == routes[:, k : k + 1]
        ones = chosen.astype(F32)
        slot = dot(earlier, ones.astype(BF16)) + base
        plus = plus + jnp.where(chosen & (slot < cap), slot + 1.0, 0.0)
        base = base + jnp.sum(ones, 0, keepdims=True)
    out_ref[:tokens, :] = cot_ref[...].astype(BF16)
    slots = (jnp.transpose(plus) - 1.0)[:EXPERTS, :]
    out_ref[tokens:, :] = jnp.concatenate([slots, jnp.zeros((EXPERTS, width - tokens), F32)], -1).astype(BF16)


def prep(routes, cot, cap):
    tokens, width = cot.shape
    return pl.pallas_call(
        functools.partial(prep_kernel, cap),
        out_shape=jax.ShapeDtypeStruct((tokens + EXPERTS, width), BF16),
        compiler_params=params(),
        cost_estimate=cost(1e9, 2e6),
        name="prep",
    )(routes, cot)


def qkv_kernel(shard, x_ref, gain_ref, w_ref, table_ref, out_ref, h_ref):
    @pl.when(pl.program_id(0) == 0)
    def _():
        normed, _ = norm_parts(x_ref[...])
        h_ref[...] = (normed * gain_ref[...]).astype(BF16)

    total = None
    for f in range(w_ref.shape[0]):
        part = dot(h_ref[:, f * shard : (f + 1) * shard], w_ref[f, :shard, :])
        total = part if total is None else total + part
    for d in range(out_ref.shape[0]):
        out_ref[d] = turn(total[:, d * PACK : (d + 1) * PACK], table_ref[...], 1.0).astype(BF16)


def qkv(x, gain, weights, table, shard, n):
    tokens, width = x.shape
    fsdp, padded, _ = weights.shape
    return pl.pallas_call(
        functools.partial(qkv_kernel, shard),
        grid=(n // 2,),
        in_specs=[
            pl.BlockSpec((tokens, width), lambda i: (0, 0)),
            pl.BlockSpec((1, width), lambda i: (0, 0)),
            pl.BlockSpec((fsdp, padded, 2 * PACK), lambda i: (0, 0, i)),
            pl.BlockSpec((tokens, 256), lambda i: (0, 0)),
        ],
        out_specs=[
            pl.BlockSpec((2, tokens, PACK), lambda i: (i, 0, 0)),
            pl.BlockSpec((tokens, width), lambda i: (0, 0)),
        ],
        out_shape=[
            jax.ShapeDtypeStruct((n, tokens, PACK), BF16),
            jax.ShapeDtypeStruct((tokens, width), BF16),
        ],
        compiler_params=params(),
        cost_estimate=cost(2 * tokens * width * n * PACK, 8e6),
        name="qkv",
    )(x, gain, weights, table)


def pair_keys(kv):
    other = pltpu.roll(kv, 64, 1)
    low = lane_iota(kv.shape) < 64
    return jnp.where(low, kv, other), jnp.where(low, other, kv)


def stack_heads(q):
    low = lane_iota(q.shape) < 64
    zero = jnp.zeros_like(q)
    return jnp.concatenate([jnp.where(low, q, zero), jnp.where(low, zero, q)], 0)


def fold_heads(stacked):
    rows = stacked.shape[0] // 2
    return jnp.where(lane_iota((rows, 128)) < 64, stacked[:rows], stacked[rows:])


def query_rows(ends_ref, block, length):
    half = length // 2
    lanes = lane_iota((1, 2 * BLK))
    index = block * BLK + jnp.where(lanes < BLK, lanes, lanes - BLK)
    position = jnp.where(index < half, index, length + half - 1 - index)
    start = jnp.zeros_like(position)
    for j in range(3):
        end = ends_ref[j]
        start = jnp.where(position >= end, jnp.maximum(start, end), start)
    return position, start


def key_position(kb, length):
    half = length // 2
    index = kb * BLK + row_iota((BLK, 1))
    return jnp.where(index < half, index, length + half - 1 - index)


def block_loop(block, per_half, body, init):
    late = block >= per_half
    inner = jnp.where(late, block - per_half, block)
    count = jnp.where(late, 2 * per_half - inner, inner + 1)

    def step(j, carry):
        kb = jnp.where(late & (j >= per_half), inner + j, j)
        return body(kb, carry)

    return lax.fori_loop(0, count, step, init)


def load_package(pack_ref, c, h):
    return pack_ref[c, h].astype(F32)


def attn_forward_kernel(length, ends_ref, q_ref, pack_ref, out_ref, lse_ref, full_ref, keys, values_t, acc):
    block = pl.program_id(0)
    half = length // 2
    n, _, rows, _ = pack_ref.shape

    @pl.when(block == 0)
    def _():
        for h in range(2):
            for c in range(n):
                kk, vv = pair_keys(pack_ref[c, h, :, 128:256].astype(F32))
                at = h * half + c * rows
                keys[at : at + rows, :] = kk.astype(BF16)
                if rows % 128 == 0:
                    values_t[:, at : at + rows] = jnp.transpose(vv).astype(BF16)
        if rows % 128 != 0:
            for h in range(2):
                for c in range(0, n, 2):
                    pair = jnp.concatenate([pack_ref[c, h, :, 128:256], pack_ref[c + 1, h, :, 128:256]], 0)
                    _, vv = pair_keys(pair.astype(F32))
                    at = h * half + c * rows
                    values_t[:, at : at + 2 * rows] = jnp.transpose(vv).astype(BF16)

    q = q_ref[...].reshape(BLK, PACK)[:, :128]
    q2 = stack_heads(q)
    position, start = query_rows(ends_ref, block, length)
    acc[...] = jnp.zeros_like(acc)

    def body(kb, carry):
        peak, total = carry
        at = pl.multiple_of(kb * BLK, BLK)
        scores = dot(keys[pl.ds(at, BLK), :], q2, NT) * ATTN_SCALE
        where = key_position(kb, length)
        scores = jnp.where((where <= position) & (where >= start), scores, MASKED)
        new_peak = jnp.maximum(peak, jnp.max(scores, 0, keepdims=True))
        weights = jnp.exp(scores - new_peak)
        fade = jnp.exp(peak - new_peak)
        total = total * fade + jnp.sum(weights, 0, keepdims=True)
        acc[...] = acc[...] * fade + dot(values_t[:, pl.ds(at, BLK)], weights.astype(BF16))
        return new_peak, total

    init = (jnp.full((1, 2 * BLK), MASKED, F32), jnp.zeros((1, 2 * BLK), F32))
    peak, total = block_loop(block, half // BLK, body, init)
    result = acc[...] / total
    full_ref[0] = result
    lse_ref[0] = peak + jnp.log(total)
    folded = fold_heads(jnp.transpose(result)).astype(BF16)
    out_ref[...] = folded.reshape(out_ref.shape)


def attn_forward(ends, packs, length):
    n, _, rows, _ = packs.shape
    blocks, per = length // BLK, BLK // rows
    per_half = blocks // 2
    tiles = lambda i, ends: (lax.rem(i, per_half), i // per_half, 0, 0)
    return pl.pallas_call(
        functools.partial(attn_forward_kernel, length),
        grid_spec=pltpu.PrefetchScalarGridSpec(
            num_scalar_prefetch=1,
            grid=(blocks,),
            in_specs=[
                pl.BlockSpec((per, 1, rows, PACK), tiles),
                pl.BlockSpec(packs.shape, lambda i, ends: (0, 0, 0, 0)),
            ],
            out_specs=[
                pl.BlockSpec((per, 1, rows, 128), tiles),
                pl.BlockSpec((1, 1, 2 * BLK), lambda i, ends: (i, 0, 0)),
                pl.BlockSpec((1, 128, 2 * BLK), lambda i, ends: (i, 0, 0)),
            ],
            scratch_shapes=[
                pltpu.VMEM((length, 128), BF16),
                pltpu.VMEM((128, length), BF16),
                pltpu.VMEM((128, 2 * BLK), F32),
            ],
        ),
        out_shape=[
            jax.ShapeDtypeStruct((n, 2, rows, 128), BF16),
            jax.ShapeDtypeStruct((blocks, 1, 2 * BLK), F32),
            jax.ShapeDtypeStruct((blocks, 128, 2 * BLK), F32),
        ],
        compiler_params=params(),
        cost_estimate=cost(1.5e10, 6e6),
        name="attn_forward",
    )(ends, packs, packs)


def attn_backward_kernel(length, ends_ref, q_ref, g_ref, pack_ref, lse_ref, full_ref, table_ref, out_ref, keys, values, keys_t, grad_q, grad_k, grad_v, acc):
    block = pl.program_id(0)
    half = length // 2
    n, _, rows, _ = pack_ref.shape

    @pl.when(block == 0)
    def _():
        for h in range(2):
            for c in range(n):
                kk, vv = pair_keys(pack_ref[c, h, :, 128:256].astype(F32))
                at = h * half + c * rows
                keys[at : at + rows, :] = kk.astype(BF16)
                values[at : at + rows, :] = vv.astype(BF16)
        for b in range(length // BLK):
            keys_t[:, b * BLK : (b + 1) * BLK] = jnp.transpose(keys[b * BLK : (b + 1) * BLK, :].astype(F32)).astype(BF16)
        grad_k[...] = jnp.zeros_like(grad_k)
        grad_v[...] = jnp.zeros_like(grad_v)

    q2 = stack_heads(q_ref[...].reshape(BLK, PACK)[:, :128])
    g2 = stack_heads(g_ref[...].reshape(BLK, 128))
    position, start = query_rows(ends_ref, block, length)
    lse = lse_ref[0]
    delta = jnp.sum(jnp.transpose(g2.astype(F32)) * full_ref[0], 0, keepdims=True)
    acc[...] = jnp.zeros_like(acc)

    def body(kb, carry):
        at = pl.multiple_of(kb * BLK, BLK)
        scores = dot(keys[pl.ds(at, BLK), :], q2, NT) * ATTN_SCALE
        where = key_position(kb, length)
        probs = jnp.where((where <= position) & (where >= start), jnp.exp(scores - lse), 0.0)
        grad_probs = dot(values[pl.ds(at, BLK), :], g2, NT)
        grad_scores = (probs * (grad_probs - delta)).astype(BF16)
        acc[...] += dot(keys_t[:, pl.ds(at, BLK)], grad_scores)
        grad_k[pl.ds(at, BLK), :] += dot(grad_scores, q2)
        grad_v[pl.ds(at, BLK), :] += dot(probs.astype(BF16), g2)
        return carry

    block_loop(block, half // BLK, body, 0)
    grad_q[pl.ds(pl.multiple_of(block * BLK, BLK), BLK), :] = fold_heads(jnp.transpose(acc[...]))

    @pl.when(block == length // BLK - 1)
    def _():
        for h in range(2):
            for c in range(n):
                at = slice(h * half + c * rows, h * half + (c + 1) * rows)
                kk = grad_k[at, :]
                vv = grad_v[at, :]
                kk = (kk + pltpu.roll(kk, 64, 1)) * ATTN_SCALE
                vv = vv + pltpu.roll(vv, 64, 1)
                both = jnp.where(lane_iota(kk.shape) < 64, kk, vv)
                package = jnp.concatenate([grad_q[at, :] * ATTN_SCALE, both], -1)
                out_ref[c, h] = turn(package, table_ref[at, :], -1.0).astype(BF16)


def attn_backward(ends, packs, grads, lse, full, table, length):
    n, _, rows, _ = packs.shape
    blocks, per = length // BLK, BLK // rows
    per_half = blocks // 2
    tiles = lambda i, ends: (lax.rem(i, per_half), i // per_half, 0, 0)
    return pl.pallas_call(
        functools.partial(attn_backward_kernel, length),
        grid_spec=pltpu.PrefetchScalarGridSpec(
            num_scalar_prefetch=1,
            grid=(blocks,),
            in_specs=[
                pl.BlockSpec((per, 1, rows, PACK), tiles),
                pl.BlockSpec((per, 1, rows, 128), tiles),
                pl.BlockSpec(packs.shape, lambda i, ends: (0, 0, 0, 0)),
                pl.BlockSpec((1, 1, 2 * BLK), lambda i, ends: (i, 0, 0)),
                pl.BlockSpec((1, 128, 2 * BLK), lambda i, ends: (i, 0, 0)),
                pl.BlockSpec(table.shape, lambda i, ends: (0, 0)),
            ],
            out_specs=pl.BlockSpec(packs.shape, lambda i, ends: (0, 0, 0, 0)),
            scratch_shapes=[
                pltpu.VMEM((length, 128), BF16),
                pltpu.VMEM((length, 128), BF16),
                pltpu.VMEM((128, length), BF16),
                pltpu.VMEM((length, 128), F32),
                pltpu.VMEM((length, 128), F32),
                pltpu.VMEM((length, 128), F32),
                pltpu.VMEM((128, 2 * BLK), F32),
            ],
        ),
        out_shape=jax.ShapeDtypeStruct(packs.shape, BF16),
        compiler_params=params(),
        cost_estimate=cost(3e10, 8e6),
        name="attn_backward",
    )(ends, packs, grads, packs, lse, full, table)


def middle_kernel(attn_ref, wo_ref, x_ref, gain_ref, middle_ref, h_ref):
    total = None
    for c in range(attn_ref.shape[0]):
        part = dot(attn_ref[c], wo_ref[c])
        total = part if total is None else total + part
    middle = x_ref[...] + RESIDUAL * total
    middle_ref[...] = middle
    normed, _ = norm_parts(middle)
    h_ref[...] = (normed * gain_ref[...]).astype(BF16)


def middle_step(attn, wo, x, gain):
    tokens, width = x.shape
    return pl.pallas_call(
        middle_kernel,
        out_shape=[jax.ShapeDtypeStruct((tokens, width), F32), jax.ShapeDtypeStruct((tokens, width), BF16)],
        compiler_params=params(),
        cost_estimate=cost(2 * tokens * width * width, 5e6),
        name="middle",
    )(attn, wo, x, gain)


def own_row(table, row):
    return jnp.sum(jnp.where(row_iota(table.shape) == row, table, 0.0), 0, keepdims=True)


def one_hot(slots, first, number, capp):
    tokens = slots.shape[1]
    order = row_iota((capp, tokens)).astype(F32)
    return [(order == own_row(slots, first + j)).astype(F32) for j in range(number)]


def gather_kernel(number, capp, first_ref, h_ref, cx_ref, wrt_ref, x_ref, g_ref, gate_ref):
    tokens = h_ref.shape[1]
    first = first_ref[0]
    h = h_ref[0]
    slots = cx_ref[0, tokens:, :tokens].astype(F32)
    logits = dot(wrt_ref[...], h, NT)[:EXPERTS, :]
    raw = jnp.exp(logits - jnp.max(logits, 0, keepdims=True))
    router = raw / jnp.sum(raw, 0, keepdims=True)
    hots = one_hot(slots, first, number, capp)
    places = jnp.concatenate(hots, 0).astype(BF16)
    rows = dot(places, h).astype(BF16)
    grads = dot(places, cx_ref[0, :tokens, :]).astype(BF16)
    for j in range(number):
        at = slice(j * capp, (j + 1) * capp)
        x_ref[j, 0] = rows[at]
        g_ref[j, 0] = grads[at]
        gate = jnp.sum(hots[j] * own_row(router, first + j), 1, keepdims=True)
        gate_ref[j, 0] = jnp.broadcast_to(gate, (capp, 128))


def gather_rows(first, hs, cxs, wrt, number, capp):
    nb, tokens, width = hs.shape
    return pl.pallas_call(
        functools.partial(gather_kernel, number, capp),
        grid_spec=pltpu.PrefetchScalarGridSpec(
            num_scalar_prefetch=1,
            grid=(nb,),
            in_specs=[
                pl.BlockSpec((1, tokens, width), lambda b, f: (b, 0, 0)),
                pl.BlockSpec((1, tokens + EXPERTS, width), lambda b, f: (b, 0, 0)),
                pl.BlockSpec(wrt.shape, lambda b, f: (0, 0)),
            ],
            out_specs=[
                pl.BlockSpec((number, 1, capp, width), lambda b, f: (0, b, 0, 0)),
                pl.BlockSpec((number, 1, capp, width), lambda b, f: (0, b, 0, 0)),
                pl.BlockSpec((number, 1, capp, 128), lambda b, f: (0, b, 0, 0)),
            ],
        ),
        out_shape=[
            jax.ShapeDtypeStruct((number, nb, capp, width), BF16),
            jax.ShapeDtypeStruct((number, nb, capp, width), BF16),
            jax.ShapeDtypeStruct((number, nb, capp, 128), F32),
        ],
        compiler_params=params(),
        cost_estimate=cost(4 * nb * number * capp * tokens * width, 2e7),
        name="gather_rows",
    )(first, hs, cxs, wrt)


PIECE = 512


def expert_kernel(base_ref, x_ref, g_ref, gate_ref, wg_ref, wu_ref, wd_ref, piece_ref, out_ref, rows_ref, dg_ref):
    x = x_ref[0]
    gate = gate_ref[0][:, :1]
    grad_ffn = RESIDUAL * g_ref[0].astype(F32)
    go = (gate * grad_ffn).astype(BF16)
    part = wg_ref.shape[2] // 2
    out = rows = None
    for chunk in range(2):
        at = slice(chunk * part, (chunk + 1) * part)
        wg, wu, wd = wg_ref[0, :, at], wu_ref[0, :, at], wd_ref[0, at, :]
        pre_gate = dot(x, wg)
        pre_up = dot(x, wu)
        sig = jax.nn.sigmoid(pre_gate)
        hidden = (pre_gate * sig * pre_up).astype(BF16)
        out_part = dot(hidden, wd)
        grad_hidden = dot(go, wd, NT)
        grad_gate = (grad_hidden * pre_up * sig * (1.0 + pre_gate * (1.0 - sig))).astype(BF16)
        grad_up = (grad_hidden * pre_gate * sig).astype(BF16)
        row_part = dot(grad_gate, wg, NT) + dot(grad_up, wu, NT)
        dwg = dot(x, grad_gate, TN).astype(BF16)
        dwu = dot(x, grad_up, TN).astype(BF16)
        dwd = dot(hidden, go, TN).astype(BF16)
        for half in range(2):
            side = slice(half * PIECE, (half + 1) * PIECE)
            piece_ref[0, half, :, at] = dwg[side]
            piece_ref[0, 2 + half, :, at] = dwu[side]
            piece_ref[0, 4 + half, at, :] = dwd[:, side]
        out = out_part if out is None else out + out_part
        rows = row_part if rows is None else rows + row_part
    out = out.astype(BF16).astype(F32)
    out_ref[0] = (gate * out).astype(BF16)
    rows_ref[0] = rows.astype(BF16)
    grad = jnp.sum(grad_ffn * out, 1, keepdims=True)
    dg_ref[0] = jnp.broadcast_to(grad, dg_ref.shape[1:])


def expert_step(base, xs, gs, gates, w_gate, w_up, w_down):
    number, rows, width = xs.shape
    ff = w_gate.shape[2]
    row = lambda e, b: (e, 0, 0)
    weight = lambda e, b: (b[0] + e, 0, 0)
    return pl.pallas_call(
        expert_kernel,
        grid_spec=pltpu.PrefetchScalarGridSpec(
            num_scalar_prefetch=1,
            grid=(number,),
            in_specs=[
                pl.BlockSpec((1, rows, width), row),
                pl.BlockSpec((1, rows, width), row),
                pl.BlockSpec((1, rows, 128), row),
                pl.BlockSpec((1, width, ff), weight),
                pl.BlockSpec((1, width, ff), weight),
                pl.BlockSpec((1, ff, width), weight),
            ],
            out_specs=[
                pl.BlockSpec((1, 6, PIECE, PIECE), lambda e, b: (e, 0, 0, 0)),
                pl.BlockSpec((1, rows, width), row),
                pl.BlockSpec((1, rows, width), row),
                pl.BlockSpec((1, rows, 128), row),
            ],
        ),
        out_shape=[
            jax.ShapeDtypeStruct((number, 6, PIECE, PIECE), BF16),
            jax.ShapeDtypeStruct((number, rows, width), BF16),
            jax.ShapeDtypeStruct((number, rows, width), BF16),
            jax.ShapeDtypeStruct((number, rows, 128), F32),
        ],
        compiler_params=params(60),
        cost_estimate=cost(18 * number * rows * width * ff, 5e7),
        name="expert_step",
    )(base, xs, gs, gates, w_gate, w_up, w_down)


def combine_kernel(number, capp, first_ref, slot_ref, outs, rows, grads, y_ref, gx_ref):
    tokens = y_ref.shape[1]
    width = y_ref.shape[2]
    first = first_ref[0]
    slots = slot_ref[0][:, :tokens].astype(F32)
    hots = one_hot(slots, first, number, capp)
    places = jnp.concatenate(hots, 0).astype(BF16)
    y_ref[0] = dot(places, outs[:, 0].reshape(number * capp, width), TN).astype(BF16)
    gx_ref[0, :tokens] = dot(places, rows[:, 0].reshape(number * capp, width), TN).astype(BF16)
    extra = jnp.zeros((EXPERTS, 2 * tokens), F32)
    for j in range(number):
        grad = jnp.sum(hots[j] * grads[j, 0][:, :1], 0, keepdims=True)
        high = grad.astype(BF16).astype(F32)
        both = jnp.concatenate([high, grad - high], 1)
        extra = jnp.where(row_iota(extra.shape) == first + j, both, extra)
    rest = jnp.zeros((EXPERTS, width - 2 * tokens), F32)
    gx_ref[0, tokens:] = jnp.concatenate([extra, rest], 1).astype(BF16)


def combine(first, slots, outs, rows, grads, tokens, capp):
    number = outs.shape[0]
    nb, _, width = slots.shape
    split = lambda a: a.reshape(number, nb, capp, a.shape[-1])
    wide = pl.BlockSpec((number, 1, capp, width), lambda b, f: (0, b, 0, 0))
    thin = pl.BlockSpec((number, 1, capp, 128), lambda b, f: (0, b, 0, 0))
    return pl.pallas_call(
        functools.partial(combine_kernel, number, capp),
        grid_spec=pltpu.PrefetchScalarGridSpec(
            num_scalar_prefetch=1,
            grid=(nb,),
            in_specs=[pl.BlockSpec((1, EXPERTS, width), lambda b, f: (b, 0, 0))] + [wide, wide, thin],
            out_specs=[
                pl.BlockSpec((1, tokens, width), lambda b, f: (b, 0, 0)),
                pl.BlockSpec((1, tokens + EXPERTS, width), lambda b, f: (b, 0, 0)),
            ],
        ),
        out_shape=[
            jax.ShapeDtypeStruct((nb, tokens, width), BF16),
            jax.ShapeDtypeStruct((nb, tokens + EXPERTS, width), BF16),
        ],
        compiler_params=params(),
        cost_estimate=cost(4 * nb * number * capp * tokens * width, 2e7),
        name="combine",
    )(first, slots, split(outs), split(rows), split(grads))


def home_kernel(gx_ref, h_ref, middle_ref, cot_ref, wr_ref, wo_ref, gain_ref, attn_ref, grad_middle_ref, dwo_ref, ga_ref, dwr_ref, dgain_ref):
    tokens, width = h_ref.shape
    h = h_ref[...]
    gain = gain_ref[...]
    extra = gx_ref[tokens:, :].astype(F32)
    grad_router = extra[:, :tokens] + extra[:, tokens : 2 * tokens]
    grad_router = jnp.transpose(jnp.concatenate([grad_router, jnp.zeros((128 - EXPERTS, tokens), F32)], 0))
    logits = dot(h, wr_ref[...])
    logits = jnp.where(lane_iota(logits.shape) < EXPERTS, logits, MASKED)
    raw = jnp.exp(logits - jnp.max(logits, -1, keepdims=True))
    router = raw / jnp.sum(raw, -1, keepdims=True)
    grad_logits = (router * (grad_router - jnp.sum(router * grad_router, -1, keepdims=True))).astype(BF16)
    dwr_ref[...] = dot(h, grad_logits, TN).astype(BF16)
    grad_h = gx_ref[:tokens, :].astype(F32) + dot(grad_logits, wr_ref[...], NT)
    normed, scale = norm_parts(middle_ref[...])
    dgain_ref[...] = jnp.sum(grad_h * normed, 0, keepdims=True)
    grad_middle = cot_ref[...] + norm_back(grad_h * gain, normed, scale)
    grad_middle_ref[...] = grad_middle
    grad_branch = (RESIDUAL * grad_middle).astype(BF16)
    for c in range(attn_ref.shape[0]):
        dwo_ref[c] = dot(attn_ref[c], grad_branch, TN).astype(BF16)
        ga_ref[c] = dot(grad_branch, wo_ref[c], NT).astype(BF16)


def home_step(gx, h, middle, cot, wr, wo, gain, attn):
    tokens, width = h.shape
    n = attn.shape[0]
    return pl.pallas_call(
        home_kernel,
        out_shape=[
            jax.ShapeDtypeStruct((tokens, width), F32),
            jax.ShapeDtypeStruct((n, 128, width), BF16),
            jax.ShapeDtypeStruct((n, tokens, 128), BF16),
            jax.ShapeDtypeStruct((width, 128), BF16),
            jax.ShapeDtypeStruct((1, width), F32),
        ],
        compiler_params=params(),
        cost_estimate=cost(4 * tokens * width * width, 1e7),
        name="home_step",
    )(gx, h, middle, cot, wr, wo, gain, attn)


def final_kernel(shard, grads_ref, w_ref, h_ref, x_ref, gain_ref, grad_middle_ref, dw_ref, grad_x_ref, dgain_ref, total):
    c = pl.program_id(0)
    g = grads_ref[0]
    dw_ref[...] = dot(h_ref[...], g, TN).astype(BF16)

    @pl.when(c == 0)
    def _():
        total[...] = jnp.zeros_like(total)

    for f in range(w_ref.shape[0]):
        total[:, f * shard : (f + 1) * shard] += dot(g, w_ref[f, :shard, :], NT)

    @pl.when(c == pl.num_programs(0) - 1)
    def _():
        normed, scale = norm_parts(x_ref[...])
        grad_h = total[...]
        dgain_ref[...] = jnp.sum(grad_h * normed, 0, keepdims=True)
        grad_x_ref[...] = grad_middle_ref[...] + norm_back(grad_h * gain_ref[...], normed, scale)


def final_step(grads, weights, h, x, gain, grad_middle, shard):
    n, tokens, _ = grads.shape
    width = x.shape[1]
    fsdp, padded, _ = weights.shape
    same = lambda c: (0, 0)
    return pl.pallas_call(
        functools.partial(final_kernel, shard),
        grid=(n,),
        in_specs=[
            pl.BlockSpec((1, tokens, PACK), lambda c: (c, 0, 0)),
            pl.BlockSpec((fsdp, padded, PACK), lambda c: (0, 0, c)),
            pl.BlockSpec((tokens, width), same),
            pl.BlockSpec((tokens, width), same),
            pl.BlockSpec((1, width), same),
            pl.BlockSpec((tokens, width), same),
        ],
        out_specs=[
            pl.BlockSpec((width, PACK), lambda c: (0, c)),
            pl.BlockSpec((tokens, width), same),
            pl.BlockSpec((1, width), same),
        ],
        out_shape=[
            jax.ShapeDtypeStruct((width, n * PACK), BF16),
            jax.ShapeDtypeStruct((tokens, width), F32),
            jax.ShapeDtypeStruct((1, width), F32),
        ],
        scratch_shapes=[pltpu.VMEM((tokens, width), F32)],
        compiler_params=params(),
        cost_estimate=cost(4 * tokens * width * n * PACK, 1.2e7),
        name="final_step",
    )(grads, weights, h, x, gain, grad_middle)


def widen_kernel(number, index_ref, own_ref, other_ref, gate_ref, up_ref, down_ref):
    def write(ref):
        for half in range(2):
            at = slice(half * PIECE, (half + 1) * PIECE)
            gate_ref[0, at, :] = ref[half].astype(F32)
            up_ref[0, at, :] = ref[2 + half].astype(F32)
            down_ref[0, :, at] = ref[4 + half].astype(F32)

    @pl.when(pl.program_id(0) == 0)
    def _():
        write(own_ref)

    @pl.when(pl.program_id(0) == 1)
    def _():
        write(other_ref)


def tail_kernel(number, index_ref, own_ref, other_ref, own_small_ref, other_small_ref, mixed_in, grad_in, gate_ref, up_ref, down_ref, mixed_ref, grad_ref, dwq_ref, dwk_ref, dwv_ref, dwo_ref, dwr_ref, g1_ref, g2_ref):
    widen_kernel(number, index_ref, own_ref, other_ref, gate_ref, up_ref, down_ref)
    mixed_ref[...] = mixed_in[...]
    grad_ref[...] = grad_in[...]

    @pl.when((pl.program_id(0) == 0) & (pl.program_id(1) == 0))
    def _():
        for which, ref in enumerate((own_small_ref, other_small_ref)):
            part = index_ref[which] // number
            at = pl.ds(pl.multiple_of(part * 128, 128), 128)
            for q in range(4):
                block = ref[1, q * 128 : (q + 1) * 128, :].astype(F32)
                dwq_ref[at, q * 256 : q * 256 + 128] = block[:, :128]
                dwq_ref[at, q * 256 + 128 : (q + 1) * 256] = block[:, 256:384]
                one, two = block[:, 128:256], block[:, 384:]
                low = lane_iota(one.shape) < HEAD_DIMENSION
                dwk_ref[at, q * 128 : (q + 1) * 128] = jnp.where(low, one, pltpu.roll(two, 64, 1))
                dwv_ref[at, q * 128 : (q + 1) * 128] = jnp.where(low, pltpu.roll(one, 64, 1), two)
            dwo_ref[at, :PIECE] = ref[0, 0:128, :].astype(F32)
            dwo_ref[at, PIECE:] = ref[0, 128:256, :].astype(F32)
            dwr_ref[at, :] = ref[0, 256:384, :EXPERTS].astype(F32)
            gains = ref[0, 384:400, :128].astype(F32)
            g1_ref[pl.ds(part, 1), :] = gains[0:1]
            g2_ref[pl.ds(part, 1), :] = gains[1:2]


def expert_specs(number, shapes):
    last = number - 1
    ins = [
        pl.BlockSpec((6, PIECE, PIECE), lambda s, e, at: (jnp.where(s == 0, e, last), 0, 0)),
        pl.BlockSpec((6, PIECE, PIECE), lambda s, e, at: (jnp.where(s == 0, 0, e), 0, 0)),
    ]
    outs = [pl.BlockSpec((1,) + tuple(shape[1:]), lambda s, e, at: (at[s] + e, 0, 0)) for shape in shapes]
    return ins, outs, [jax.ShapeDtypeStruct(shape, F32) for shape in shapes]


def widen(index, own, other, shapes):
    number = shapes[0][0] // 2
    ins, outs, out_shapes = expert_specs(number, shapes)
    return pl.pallas_call(
        functools.partial(widen_kernel, number),
        grid_spec=pltpu.PrefetchScalarGridSpec(num_scalar_prefetch=1, grid=(2, number), in_specs=ins, out_specs=outs),
        out_shape=out_shapes,
        compiler_params=params(),
        cost_estimate=cost(0, 1e8),
        name="widen",
    )(index, own, other)


def tail(index, own, other, mixed, grad_x, shapes, shard):
    number = shapes[0][0] // 2
    tokens, width = mixed.shape
    ins, outs, out_shapes = expert_specs(number, shapes)
    small = pl.BlockSpec((2, PIECE, PIECE), lambda s, e, at: (3 * number, 0, 0))
    rows = pl.BlockSpec((tokens // (2 * number), width), lambda s, e, at: (s * number + e, 0))
    small_shapes = [(shard, width), (shard, width // 2), (shard, width // 2), (shard, width), (shard, EXPERTS), (2, 128), (2, 128)]
    whole = [pl.BlockSpec(shape, lambda s, e, at: (0, 0)) for shape in small_shapes]
    return pl.pallas_call(
        functools.partial(tail_kernel, number),
        grid_spec=pltpu.PrefetchScalarGridSpec(
            num_scalar_prefetch=1,
            grid=(2, number),
            in_specs=ins + [small, small, rows, rows],
            out_specs=outs + [rows, rows] + whole,
        ),
        out_shape=out_shapes
        + [jax.ShapeDtypeStruct((tokens, width), F32)] * 2
        + [jax.ShapeDtypeStruct(shape, F32) for shape in small_shapes],
        compiler_params=params(),
        cost_estimate=cost(0, 1e8),
        name="tail",
    )(index, own, other, own, other, mixed, grad_x)


def swap(value, axis, bit):
    size = lax.axis_size(axis)
    return lax.ppermute(value, axis, [(i, i ^ bit) for i in range(size)])


def group_bits(fsdp):
    bits = [("fsdp", 1 << b) for b in range(1, fsdp.bit_length() - 1)]
    return bits + [("ctx", 1), ("fsdp", 1)]


def group_gather(value, bits):
    stacked = value[None]
    for axis, bit in bits:
        stacked = jnp.concatenate([stacked, swap(stacked, axis, bit)], 0)
    return stacked


def group_reduce(stacked, bits):
    for axis, bit in reversed(bits):
        half = stacked.shape[0] // 2
        arrived = swap(stacked[half:], axis, bit)
        stacked = (stacked[:half].astype(F32) + arrived.astype(F32)).astype(stacked.dtype)
    return stacked[0]


def line_sum(value, ctx):
    pairs = ctx // 2
    if pairs != 4:
        bit = 2
        while bit < ctx:
            value = value + swap(value, "ctx", bit)
            bit *= 2
        return value
    at = lambda z, y: 2 * z + y
    inward = [(at(0, y), at(1, y)) for y in range(2)] + [(at(3, y), at(2, y)) for y in range(2)]
    across = [(at(1, y), at(2, y)) for y in range(2)] + [(at(2, y), at(1, y)) for y in range(2)]
    outward = [(b, a) for a, b in inward]
    value = value + lax.ppermute(value, "ctx", inward)
    value = value + lax.ppermute(value, "ctx", across)
    arrived = lax.ppermute(value, "ctx", outward)
    z = lax.axis_index("ctx") // 2
    return jnp.where((z == 0) | (z == 3), arrived, value)


MESH = pl.DeviceIdType.MESH


def flip(index, bit):
    return jnp.where((index // bit) % 2 == 0, index + bit, index - bit)


def send(src, dst, send_sem, recv_sem, device):
    return pltpu.make_async_remote_copy(src_ref=src, dst_ref=dst, send_sem=send_sem, recv_sem=recv_sem, device_id=device, device_id_type=MESH)


def neighbours():
    ctx, fsdp = lax.axis_index("ctx"), lax.axis_index("fsdp")
    side, across = flip(ctx, 1), flip(fsdp, 2)
    core = {"fsdp": flip(fsdp, 1)}
    return core, [{"fsdp": across}, {"ctx": side}, {"ctx": side, "fsdp": across}]


def greet(devices):
    barrier = pltpu.get_barrier_semaphore()
    for device in devices:
        pl.semaphore_signal(barrier, inc=1, device_id=device, device_id_type=MESH)
    pl.semaphore_wait(barrier, len(devices))


def others(n):
    ctx = lax.axis_index("ctx")
    return [lax.rem(ctx + d, n) for d in range(1, n)]


def exchange_start(src, dst, send_sems, recv_sems, local_sem, n):
    ctx = lax.axis_index("ctx")
    for d, c in enumerate(others(n)):
        send(src.at[c], dst.at[ctx], send_sems.at[d], recv_sems.at[d], {"ctx": c}).start()
    pltpu.make_async_copy(src.at[ctx], dst.at[ctx], local_sem).start()


def exchange_wait(src, dst, send_sems, recv_sems, local_sem, n, arrived=None):
    ctx = lax.axis_index("ctx")
    pltpu.make_async_copy(src.at[ctx], dst.at[ctx], local_sem).wait()
    if arrived is not None:
        arrived(ctx)
    for d in range(n - 1):
        source = lax.rem(ctx + n - 1 - d, n)
        send(src.at[source], dst.at[source], send_sems.at[d], recv_sems.at[d], {"ctx": source}).wait_recv()
        if arrived is not None:
            arrived(source)
    for d, c in enumerate(others(n)):
        send(src.at[c], dst.at[ctx], send_sems.at[d], recv_sems.at[d], {"ctx": c}).wait_send()


def front_kernel(n, cap, wq_ref, wk_ref, wv_ref, wo_part_ref, wr_raw_ref, g1_ref, g2_ref, x_ref, table_ref, routes_ref, cot_ref, packs_ref, h_ref, weights_ref, wo_ref, wr_ref, cxs_ref, gains_ref, wall, packed_ref, wr_part_ref, cx, table, normed_ref, total, out, exch_send, exch_recv, full_send, full_recv, x_send, x_recv, y_send, y_recv, xs_send, xs_recv, ys_send, ys_recv, cx_send, cx_recv, local_sems):
    width = x_ref.shape[1]
    shard = width // 4
    ctx, fsdp = lax.axis_index("ctx"), lax.axis_index("fsdp")
    parity = lax.rem(ctx, 2)
    core, group = neighbours()
    far, near = group[0], group[1]
    sibling, distant = flip(fsdp, 1), flip(fsdp, 2)
    other = flip(distant, 1)
    for k in range(2):
        pltpu.make_async_copy(table_ref.at[k, ctx], table.at[k], local_sems.at[6 + k]).start()

    pair = HEAD_DIMENSION * 2
    for c in range(0, n, 2):
        for k in range(2):
            packed_ref[:shard, (c + k) * PACK : (c + k) * PACK + 128] = wq_ref[:, (c + k) * 128 : (c + k + 1) * 128]
        keys, values = wk_ref[:, c // 2 * pair : (c // 2 + 1) * pair].astype(F32), wv_ref[:, c // 2 * pair : (c // 2 + 1) * pair].astype(F32)
        low = lane_iota(keys.shape) < HEAD_DIMENSION
        packed_ref[:shard, c * PACK + 128 : (c + 1) * PACK] = jnp.where(low, keys, pltpu.roll(values, 64, 1)).astype(BF16)
        packed_ref[:shard, (c + 1) * PACK + 128 : (c + 2) * PACK] = jnp.where(low, pltpu.roll(keys, 64, 1), values).astype(BF16)
    row = row_iota((16, shard))
    gain_rows = jnp.where(row == 0, g1_ref[...].astype(F32), jnp.where(row == 1, g2_ref[...].astype(F32), 0.0))
    packed_ref[shard:, :] = jnp.zeros((packed_ref.shape[0] - shard, n * PACK), BF16)
    packed_ref[shard : shard + 16, :shard] = gain_rows.astype(BF16)
    wr_part_ref[...] = jnp.concatenate([wr_raw_ref[...].astype(F32), jnp.zeros((shard, 128 - EXPERTS), F32)], 1).astype(BF16)
    greet([core, far] + [{"ctx": c} for c in others(n)])

    half_rows = packed_ref.shape[0] // 2
    low_rows = half_rows // 32 * 16

    def cut(k, part):
        if k == 0:
            return pl.ds(pl.multiple_of(part * half_rows, 16), low_rows)
        if k == 1:
            return pl.ds(pl.multiple_of(part * half_rows + low_rows, 16), half_rows - low_rows)
        if k == 2:
            return pl.ds(part, 1)
        return pl.ds(pl.multiple_of(part * (shard // 2), 16), shard // 2)

    sources = [packed_ref, packed_ref, wo_part_ref, wr_part_ref]
    targets = [wall, wall, wo_ref, wr_ref]
    wholes = [(packed_ref, wall), (wo_part_ref, wo_ref), (wr_part_ref, wr_ref)]

    def whole(i):
        src, dst = wholes[i]
        return send(src, dst.at[fsdp], full_send.at[i], full_recv.at[i], core)

    def own(i):
        src, dst = wholes[i]
        return pltpu.make_async_copy(src, dst.at[fsdp], local_sems.at[i])

    def to_far(k):
        return send(sources[k].at[cut(k, parity)], targets[k].at[fsdp, cut(k, parity)], x_send.at[k], x_recv.at[k], far)

    def pass_on(k, part, sems, device):
        ref = targets[k].at[distant, cut(k, part)]
        return send(ref, ref, sems[0].at[k], sems[1].at[k], device)

    def far_arrived(k):
        ref = targets[k].at[distant, cut(k, parity)]
        send(ref, ref, x_send.at[k], x_recv.at[k], far).wait_recv()
        pass_on(k, parity, (y_send, y_recv), near).start()
        pass_on(k, parity, (xs_send, xs_recv), core).start()

    def near_arrived(k):
        pass_on(k, 1 - parity, (y_send, y_recv), near).wait_recv()
        pass_on(k, 1 - parity, (ys_send, ys_recv), core).start()

    def core_arrived(k):
        for part, sems in ((parity, (xs_send, xs_recv)), (1 - parity, (ys_send, ys_recv))):
            ref = targets[k].at[other, cut(k, part)]
            send(ref, ref, sems[0].at[k], sems[1].at[k], core).wait_recv()

    own(0).start()
    to_far(0).start()
    to_far(1).start()
    whole(0).start()

    prep_kernel(cap, routes_ref, cot_ref, cx)
    pltpu.make_async_copy(cx, cxs_ref.at[0], local_sems.at[3]).start()
    normed, _ = norm_parts(x_ref[...])
    normed_ref[...] = normed

    def project(block, begin):
        at = pl.ds(pl.multiple_of(block * shard, shard), shard)
        gain = wall[block, shard : shard + 16, :shard].astype(F32)
        gains_ref[:, at] = gain
        h = (normed_ref[:, at] * gain[:1]).astype(BF16)
        h_ref[:, at] = h
        part = dot(h, wall[block, :shard, :])
        total[...] = part if begin else total[...] + part

    own(0).wait()
    project(fsdp, True)
    ref = wall.at[sibling]
    send(ref, ref, full_send.at[0], full_recv.at[0], core).wait_recv()
    project(sibling, False)
    far_arrived(0)
    far_arrived(1)
    for i in (1, 2):
        own(i).start()
        whole(i).start()
        to_far(i + 1).start()
    send(cx, cxs_ref.at[1], cx_send.at[0], cx_recv.at[0], far).start()
    near_arrived(0)
    near_arrived(1)
    project(distant, False)
    core_arrived(0)
    core_arrived(1)
    project(other, False)
    keep = pltpu.make_async_copy(wall, weights_ref, local_sems.at[4])
    keep.start()
    for k in range(2):
        pltpu.make_async_copy(table_ref.at[k, ctx], table.at[k], local_sems.at[6 + k]).wait()
    angles = table[...].reshape(x_ref.shape[0], 256)
    for c in range(n):
        out[c] = turn(total[:, c * PACK : (c + 1) * PACK], angles, 1.0).astype(BF16)
    exchange = (out, packs_ref, exch_send, exch_recv, local_sems.at[5], n)
    exchange_start(*exchange)

    for k in (2, 3):
        far_arrived(k)
    for k in (2, 3):
        near_arrived(k)
    for k in (2, 3):
        core_arrived(k)
    for i in (1, 2):
        src, dst = wholes[i]
        ref = dst.at[sibling]
        send(ref, ref, full_send.at[i], full_recv.at[i], core).wait_recv()
        own(i).wait()
    exchange_wait(*exchange)
    for i in range(3):
        whole(i).wait_send()
    for k in range(4):
        to_far(k).wait_send()
        pass_on(k, parity, (y_send, y_recv), near).wait_send()
        pass_on(k, parity, (xs_send, xs_recv), core).wait_send()
        pass_on(k, 1 - parity, (ys_send, ys_recv), core).wait_send()
    send(cx, cxs_ref.at[1], cx_send.at[0], cx_recv.at[0], far).wait()
    pltpu.make_async_copy(cx, cxs_ref.at[0], local_sems.at[3]).wait()
    keep.wait()


def front(wq, wk, wv, wo_part, wr, g1, g2, x, table, routes, cot, cap, n):
    tokens, width = x.shape
    shard = wq.shape[0]
    hbm, vmem = pl.BlockSpec(memory_space=pl.ANY), pl.BlockSpec(memory_space=pltpu.VMEM)
    dma = lambda k: pltpu.SemaphoreType.DMA((k,))
    shaped = lambda shape, dtype=BF16: jax.ShapeDtypeStruct(shape, dtype)
    cx_shape = (tokens + EXPERTS, width)
    packed = (2 * 16 * (shard // 32 + 1), n * PACK)
    return pl.pallas_call(
        functools.partial(front_kernel, n, cap),
        in_specs=[vmem, vmem, vmem, hbm, vmem, vmem, vmem, vmem, hbm, vmem, vmem],
        out_specs=[hbm, vmem, hbm, hbm, hbm, hbm, vmem],
        out_shape=[
            shaped((n, tokens, PACK)),
            shaped((tokens, width)),
            shaped((4,) + packed),
            shaped((4,) + wo_part.shape),
            shaped((4, shard, 128)),
            shaped((2,) + cx_shape),
            shaped((16, width), F32),
        ],
        scratch_shapes=[
            pltpu.VMEM((4,) + packed, BF16),
            pltpu.VMEM(packed, BF16),
            pltpu.VMEM((shard, 128), BF16),
            pltpu.VMEM(cx_shape, BF16),
            pltpu.VMEM((2, tokens // 2, 256), F32),
            pltpu.VMEM((tokens, width), F32),
            pltpu.VMEM((tokens, n * PACK), F32),
            pltpu.VMEM((n, tokens, PACK), BF16),
            dma(n - 1),
            dma(n - 1),
            dma(3),
            dma(3),
        ]
        + [dma(4)] * 8
        + [dma(1), dma(1), dma(8)],
        compiler_params=params(collective_id=1, has_side_effects=True),
        cost_estimate=cost(2e9, 5e7),
        name="front",
    )(wq, wk, wv, wo_part, wr, g1, g2, x, table, routes, cot)


def attend_kernel(length, n, ends_ref, q_ref, pack_ref, cxs_ref, out_ref, lse_ref, full_ref, rest_ref, keys, values_t, acc, near_send, near_recv, core_send, core_recv):
    block = pl.program_id(0)
    core, group = neighbours()
    near = group[1]

    def to_near(i):
        return send(cxs_ref.at[i], rest_ref.at[i], near_send.at[i], near_recv.at[i], near)

    def to_core(i):
        src = cxs_ref.at[i] if i < 2 else rest_ref.at[i - 2]
        return send(src, rest_ref.at[2 + i], core_send.at[i], core_recv.at[i], core)

    @pl.when(block == 0)
    def _():
        greet([core, near])
        for i in range(2):
            to_near(i).start()
        for i in range(2):
            to_core(i).start()

    attn_forward_kernel(length, ends_ref, q_ref, pack_ref, out_ref, lse_ref, full_ref, keys, values_t, acc)

    @pl.when(block == pl.num_programs(0) - 2)
    def _():
        to_near(0).wait_recv()
        to_core(2).start()

    @pl.when(block == pl.num_programs(0) - 1)
    def _():
        to_near(1).wait_recv()
        to_core(3).start()
        for i in range(4):
            to_core(i).wait()
        for i in range(2):
            to_near(i).wait_send()


def attend(ends, packs, cxs, length):
    n, _, rows, _ = packs.shape
    blocks, per = length // BLK, BLK // rows
    per_half = blocks // 2
    tiles = lambda i: (lax.rem(i, per_half), i // per_half, 0, 0)
    hbm = pl.BlockSpec(memory_space=pl.ANY)
    dma = lambda k: pltpu.SemaphoreType.DMA((k,))
    return pl.pallas_call(
        functools.partial(attend_kernel, length, n),
        grid=(blocks,),
        in_specs=[
            pl.BlockSpec(memory_space=pltpu.SMEM),
            pl.BlockSpec((per, 1, rows, PACK), tiles),
            pl.BlockSpec(packs.shape, lambda i: (0, 0, 0, 0)),
            hbm,
        ],
        out_specs=[
            pl.BlockSpec((per, 1, rows, 128), tiles),
            pl.BlockSpec((1, 1, 2 * BLK), lambda i: (i, 0, 0)),
            pl.BlockSpec((1, 128, 2 * BLK), lambda i: (i, 0, 0)),
            hbm,
        ],
        scratch_shapes=[
            pltpu.VMEM((length, 128), BF16),
            pltpu.VMEM((128, length), BF16),
            pltpu.VMEM((128, 2 * BLK), F32),
            dma(2),
            dma(2),
            dma(4),
            dma(4),
        ],
        out_shape=[
            jax.ShapeDtypeStruct((n, 2, rows, 128), BF16),
            jax.ShapeDtypeStruct((blocks, 1, 2 * BLK), F32),
            jax.ShapeDtypeStruct((blocks, 128, 2 * BLK), F32),
            jax.ShapeDtypeStruct((6,) + cxs.shape[1:], BF16),
        ],
        compiler_params=params(collective_id=3, has_side_effects=True),
        cost_estimate=cost(1.5e10, 2e7),
        name="attend",
    )(ends, packs, packs, cxs)


def mid_kernel(n, number, capp, attn_ref, cxs_ref, rest_ref, wo_ref, wr_ref, x_ref, gain_ref, middle_ref, h_ref, kept_ref, xs_ref, gs_ref, gates_ref, arrived, hs, total, exch_send, exch_recv, hop_send, hop_recv, fwd_send, fwd_recv, local_sems):
    tokens, width = x_ref.shape
    ctx, fsdp = lax.axis_index("ctx"), lax.axis_index("fsdp")
    first = (fsdp * 2 + lax.rem(ctx, 2)) * number
    core, group = neighbours()
    greet([core, group[0], group[2]] + [{"ctx": c} for c in others(n)])
    exchange = (attn_ref, arrived, exch_send, exch_recv, local_sems.at[0], n)
    exchange_start(*exchange)
    total[...] = jnp.zeros_like(total)

    def take(c):
        total[...] += dot(arrived[c], wo_ref[c])

    exchange_wait(*exchange, take)
    keep = pltpu.make_async_copy(arrived, kept_ref, local_sems.at[1])
    keep.start()
    middle = x_ref[...] + RESIDUAL * total[...]
    middle_ref[...] = middle
    normed, _ = norm_parts(middle)
    h = (normed * gain_ref[...]).astype(BF16)
    h_ref[...] = h
    hs[0] = h

    def hop(i):
        return send(hs.at[0], hs.at[1 + i], hop_send.at[i], hop_recv.at[i], (group + [core])[i])

    def forward(i):
        return send(hs.at[1 + i], hs.at[5 + i], fwd_send.at[i], fwd_recv.at[i], core)

    for i in (2, 0, 1, 3):
        hop(i).start()

    def place(b):
        h = hs[b]
        cx = (cxs_ref.at[b] if b < 2 else rest_ref.at[cx_slot[b]])
        logits = jnp.transpose(dot(h, wr_ref[...]))[:EXPERTS, :]
        raw = jnp.exp(logits - jnp.max(logits, 0, keepdims=True))
        router = raw / jnp.sum(raw, 0, keepdims=True)
        slots = cx[tokens:, :tokens].astype(F32)
        hots = one_hot(slots, first, number, capp)
        places = jnp.concatenate(hots, 0).astype(BF16)
        rows = dot(places, h).astype(BF16)
        grads = dot(places, cx[:tokens, :]).astype(BF16)
        for j in range(number):
            at = slice(j * capp, (j + 1) * capp)
            xs_ref[j, b] = rows[at]
            gs_ref[j, b] = grads[at]
            gate = jnp.sum(hots[j] * own_row(router, first + j), 1, keepdims=True)
            gates_ref[j, b] = jnp.broadcast_to(gate, (capp, 128))

    cx_slot = {2: 0, 3: 1, 4: 2, 5: 3, 6: 4, 7: 5}
    place(0)
    hop(3).wait_recv()
    place(4)
    for i in (0, 1, 2):
        hop(i).wait_recv()
        forward(i).start()
        place(1 + i)
    for i in (0, 1, 2):
        forward(i).wait_recv()
        place(5 + i)
    for i in range(4):
        hop(i).wait_send()
    for i in range(3):
        forward(i).wait_send()
    keep.wait()


def mid_step(attn, cxs, rest, wo, wr, x, gain, number, capp, n):
    tokens, width = x.shape
    hbm, vmem = pl.BlockSpec(memory_space=pl.ANY), pl.BlockSpec(memory_space=pltpu.VMEM)
    dma = lambda k: pltpu.SemaphoreType.DMA((k,))
    shaped = lambda shape, dtype=BF16: jax.ShapeDtypeStruct(shape, dtype)
    return pl.pallas_call(
        functools.partial(mid_kernel, n, number, capp),
        in_specs=[hbm, vmem, vmem, vmem, vmem, vmem, vmem],
        out_specs=[vmem, vmem, hbm, vmem, vmem, vmem],
        out_shape=[
            shaped((tokens, width), F32),
            shaped((tokens, width)),
            shaped(attn.shape),
            shaped((number, 8, capp, width)),
            shaped((number, 8, capp, width)),
            shaped((number, 8, capp, 128), F32),
        ],
        scratch_shapes=[
            pltpu.VMEM(attn.shape, BF16),
            pltpu.VMEM((8, tokens, width), BF16),
            pltpu.VMEM((tokens, width), F32),
            dma(n - 1),
            dma(n - 1),
            dma(4),
            dma(4),
            dma(3),
            dma(3),
            dma(2),
        ],
        compiler_params=params(collective_id=2, has_side_effects=True),
        cost_estimate=cost(4e9, 5e7),
        name="mid_step",
    )(attn, cxs, rest, wo, wr, x, gain)


RING = 8
ORDER_X, ORDER_Y, ORDER_CORE = 1, 2, 4


class GroupSum:
    def __init__(self, part, land, land_x, land_y, own, sems, core, group):
        self.part, self.land, self.land_x, self.land_y, self.own = part, land, land_x, land_y, own
        self.core_send, self.core_recv, self.x_send, self.x_recv, self.y_send, self.y_recv, self.load = sems
        self.core, self.far, self.near = core, group[0], group[1]

    def to_core(self, i):
        return send(self.part.at[4 + i], self.land.at[i], self.core_send.at[i], self.core_recv.at[i], self.core)

    def to_far(self, k):
        return send(self.land.at[1 + 2 * k], self.land_x.at[k], self.x_send.at[k], self.x_recv.at[k], self.far)

    def to_near(self):
        return send(self.land.at[2], self.land_y, self.y_send.at[0], self.y_recv.at[0], self.near)

    def fetch(self, i):
        return pltpu.make_async_copy(self.part.at[i], self.own.at[i % 2], self.load.at[i % 2])

    def start(self):
        for i in (1, 3, 2, 0):
            self.to_core(i).start()

    def over_cores(self):
        order = (1, 3, 2, 0)
        if self.own is not None:
            self.fetch(1).start()
        for step, i in enumerate(order):
            if self.own is None:
                mine = self.part[i]
            else:
                self.fetch(i).wait()
                mine = self.own[i % 2]
            self.to_core(i).wait_recv()
            self.land[i] = (self.land[i].astype(F32) + mine.astype(F32)).astype(BF16)
            if self.own is not None and step < 3:
                self.fetch(order[step + 1]).start()
            if i % 2 == 1:
                self.to_far(i // 2).start()

    def over_x(self):
        for k in (1, 0):
            self.to_far(k).wait_recv()
            self.land[2 * k] = (self.land[2 * k].astype(F32) + self.land_x[k].astype(F32)).astype(BF16)
            if k == 1:
                self.to_near().start()

    def finish(self):
        self.to_near().wait_recv()
        for i in range(4):
            self.to_core(i).wait_send()
        for k in range(2):
            self.to_far(k).wait_send()
        self.to_near().wait_send()
        return self.land[0].astype(F32) + self.land_y[...].astype(F32)


class LineSum:
    def __init__(self, count, own_ref, other_ref, inbox, across, mine, sems):
        self.count, self.own_ref, self.other_ref = count, own_ref, other_ref
        self.inbox, self.across, self.mine = inbox, across, mine
        self.line_send, self.line_recv, self.mid_send, self.mid_recv, self.side_send, self.side_recv, self.store, self.load = sems
        ctx = lax.axis_index("ctx")
        z = ctx // 2
        self.middle = (z == 1) | (z == 2)
        self.line = {"ctx": jnp.where(z % 2 == 0, ctx + 2, ctx - 2)}
        self.peer = {"ctx": jnp.where(z == 1, ctx + 2, ctx - 2)}
        self.side = {"ctx": flip(ctx, 1)}

    def send_line(self, src, i):
        s = lax.rem(i, RING)
        return send(src, self.inbox.at[s], self.line_send.at[s], self.line_recv.at[s], self.line)

    def send_mid(self, i):
        s = lax.rem(i, RING)
        return send(self.inbox.at[s], self.across.at[s], self.mid_send.at[s], self.mid_recv.at[s], self.peer)

    def send_side(self, src, i):
        return send(src, self.other_ref.at[i], self.side_send.at[lax.rem(i, RING)], self.side_recv.at[i], self.side)

    def keep(self, src, i):
        return pltpu.make_async_copy(src, self.own_ref.at[i], self.store.at[lax.rem(i, RING)])

    def drain_middle(self, i):
        src = self.across.at[lax.rem(i, RING)]
        self.send_line(src, i).wait_send()
        self.send_side(src, i).wait_send()
        self.keep(src, i).wait()

    def drain_end(self, i):
        src = self.inbox.at[lax.rem(i, RING)]
        self.send_side(src, i).wait_send()
        self.keep(src, i).wait()

    def tick(self, t, source):
        count = self.count
        fixed = isinstance(t, int)

        def when(condition):
            if fixed:
                return (lambda f: f()) if condition else (lambda f: None)
            return pl.when(condition)

        i32 = (lambda v: jnp.int32(v)) if fixed else (lambda v: v)

        @pl.when(self.middle)
        def _():
            @when(t < count)
            def _():
                @when(t >= 6)
                def _():
                    self.drain_middle(i32(t - 6))

                s = lax.rem(i32(t), RING)
                fetch = pltpu.make_async_copy(source(t), self.mine, self.load.at[0])
                fetch.start()
                self.send_line(self.inbox.at[s], i32(t)).wait_recv()
                fetch.wait()
                self.inbox[s] = self.inbox[s] + self.mine[...]
                self.send_mid(i32(t)).start()

            @when((t >= 1) & (t <= count))
            def _():
                i = i32(t - 1)
                s = lax.rem(i, RING)
                self.send_mid(i).wait()
                self.across[s] = self.across[s] + self.inbox[s]
                self.send_line(self.across.at[s], i).start()
                self.send_side(self.across.at[s], i).start()
                self.keep(self.across.at[s], i).start()

        @pl.when(jnp.logical_not(self.middle))
        def _():
            @when(t < count)
            def _():
                @when(t >= 8)
                def _():
                    self.drain_end(i32(t - 8))

                @when(t >= 2)
                def _():
                    self.send_line(self.mine, i32(t - 2)).wait_send()

                self.send_line(source(t), i32(t)).start()

            @when(t >= 4)
            def _():
                i = i32(t - 4)
                s = lax.rem(i, RING)
                self.send_line(self.inbox.at[s], i).wait_recv()
                self.send_side(self.inbox.at[s], i).start()
                self.keep(self.inbox.at[s], i).start()

    def finish(self):
        count = self.count

        @pl.when(self.middle)
        def _():
            for i in range(count - 6, count):
                self.drain_middle(jnp.int32(i))

        @pl.when(jnp.logical_not(self.middle))
        def _():
            for i in range(count - 2, count):
                self.send_line(self.mine, jnp.int32(i)).wait_send()
            for i in range(count - 8, count):
                self.drain_end(jnp.int32(i))

        def arrived(i, carry):
            self.send_side(self.mine, i).wait_recv()
            return carry

        lax.fori_loop(0, count, arrived, 0)


def backward_kernel(
    n,
    length,
    ends_ref,
    pieces_ref,
    gx_ref,
    yp_ref,
    full_ref,
    weights_ref,
    packs_hbm,
    table_hbm,
    h_ref,
    middle_ref,
    cot_ref,
    wr_ref,
    wo_ref,
    gains_ref,
    attn_ref,
    lse_ref,
    x_ref,
    h_attn_ref,
    own_ref,
    other_ref,
    grad_x_ref,
    mixed_ref,
    inbox,
    across,
    mine,
    gx_land,
    gx_x,
    gx_y,
    gx_own,
    y_land,
    y_x,
    y_y,
    y_own,
    small,
    s_land,
    s_x,
    s_y,
    packs,
    table,
    keys,
    values,
    keys_t,
    grad_q,
    grad_k,
    grad_v,
    acc,
    full_buf,
    ga,
    ga_in,
    pack_out,
    grads_in,
    wbuf,
    total,
    grad_middle,
    dgain,
    col,
    line_send,
    line_recv,
    mid_send,
    mid_recv,
    side_send,
    side_recv,
    line_store,
    line_load,
    ga_send,
    ga_recv,
    gr_send,
    gr_recv,
    rs_sems,
    local_sems,
    full_sems,
    w_sems,
):
    tokens, width = h_ref.shape
    half = length // 2
    rows = tokens // 2
    shard = width // 4
    blocks = length // BLK
    ctx, fsdp = lax.axis_index("ctx"), lax.axis_index("fsdp")
    core, group = neighbours()
    experts = pieces_ref.shape[0]
    line = LineSum(experts + 2, own_ref, other_ref, inbox, across, mine, (line_send, line_recv, mid_send, mid_recv, side_send, side_recv, line_store, line_load))
    source = lambda t: pieces_ref.at[t]
    tick = lambda t: line.tick(t, source)
    sems = lambda k: [rs_sems.at[k, j] for j in range(7)]
    gx = GroupSum(gx_ref, gx_land, gx_x, gx_y, gx_own, sems(0), core, group)
    ys = GroupSum(yp_ref, y_land, y_x, y_y, y_own, sems(1), core, group)
    ws = GroupSum(small, s_land, s_x, s_y, None, sems(2), core, group)

    greet([core, group[0], group[2]] + [{"ctx": c} for c in others(n)])
    gx.start()
    load_packs = pltpu.make_async_copy(packs_hbm, packs, local_sems.at[0])
    load_table = pltpu.make_async_copy(table_hbm, table, local_sems.at[1])
    load_packs.start()
    load_table.start()
    small[:, PIECE // 2 : PIECE, :] = jnp.zeros((8, PIECE // 2, PIECE), BF16)

    def strip(r):
        f = fsdp
        if r & ORDER_X:
            f = flip(f, 2)
        if r & ORDER_CORE:
            f = flip(f, 1)
        y = lax.rem(ctx, 2)
        return 2 * f + (1 - y if r & ORDER_Y else y)

    tick(0)
    gx.over_cores()
    tick(1)
    gx.over_x()
    tick(2)
    arrived = gx.finish()
    ys.start()

    h = h_ref[...]
    gain = gains_ref[1:2]
    extra = arrived[tokens:, :]
    grad_router = extra[:, :tokens] + extra[:, tokens : 2 * tokens]
    grad_router = jnp.transpose(jnp.concatenate([grad_router, jnp.zeros((128 - EXPERTS, tokens), F32)], 0))
    logits = dot(h, wr_ref[...])
    logits = jnp.where(lane_iota(logits.shape) < EXPERTS, logits, MASKED)
    raw = jnp.exp(logits - jnp.max(logits, -1, keepdims=True))
    router = raw / jnp.sum(raw, -1, keepdims=True)
    grad_logits = (router * (grad_router - jnp.sum(router * grad_router, -1, keepdims=True))).astype(BF16)
    grad_h = arrived[:tokens, :] + dot(grad_logits, wr_ref[...], NT)
    normed, scale = norm_parts(middle_ref[...])
    dgain[1:2, :] = jnp.sum(grad_h * normed, 0, keepdims=True)
    grad_mid = cot_ref[...] + norm_back(grad_h * gain, normed, scale)
    grad_middle[...] = grad_mid
    grad_branch = (RESIDUAL * grad_mid).astype(BF16)
    for c in range(n):
        ga[c] = dot(grad_branch, wo_ref[c], NT).astype(BF16)
    ga_exchange = (ga, ga_in, ga_send, ga_recv, local_sems.at[2], n)
    exchange_start(*ga_exchange)
    tick(3)
    col[:, :128] = dot(h, grad_logits, TN).astype(BF16)
    for r in range(8):
        at = strip(r)
        dwo = dot(attn_ref[at], grad_branch, TN).astype(BF16)
        small[r, 0:128, :] = dwo[:, :PIECE]
        small[r, 128:256, :] = dwo[:, PIECE:]
        small[r, 256:384, 0:128] = col[pl.ds(pl.multiple_of(at * 128, 128), 128), 0:128]
    load_packs.wait()
    for hh in range(2):
        for c in range(n):
            kk, vv = pair_keys(packs[c, hh, :, 128:256].astype(F32))
            at = hh * half + c * rows
            keys[at : at + rows, :] = kk.astype(BF16)
            values[at : at + rows, :] = vv.astype(BF16)
            keys_t[:, at : at + rows] = jnp.transpose(kk).astype(BF16)
    grad_k[...] = jnp.zeros_like(grad_k)
    grad_v[...] = jnp.zeros_like(grad_v)
    ys.over_cores()
    tick(4)
    exchange_wait(*ga_exchange)

    per = BLK // rows
    per_half = blocks // 2

    def fetch_full(b):
        return pltpu.make_async_copy(full_ref.at[b], full_buf.at[lax.rem(b, 2)], full_sems.at[lax.rem(b, 2)])

    fetch_full(jnp.int32(0)).start()

    def attend(block, carry):
        late = block // per_half
        c0 = lax.rem(block, per_half) * per
        q2 = stack_heads(jnp.concatenate([packs[c0 + k, late, :, :128] for k in range(per)], 0))
        g2 = stack_heads(jnp.concatenate([ga_in[c0 + k, pl.ds(pl.multiple_of(late * rows, rows), rows), :] for k in range(per)], 0))
        position, start = query_rows(ends_ref, block, length)
        lse = lse_ref[block]

        @pl.when(block + 1 < blocks)
        def _():
            fetch_full(block + 1).start()

        fetch_full(block).wait()
        delta = jnp.sum(jnp.transpose(g2.astype(F32)) * full_buf[lax.rem(block, 2)], 0, keepdims=True)
        acc[...] = jnp.zeros_like(acc)

        def body(kb, carry):
            at = pl.multiple_of(kb * BLK, BLK)
            scores = dot(keys[pl.ds(at, BLK), :], q2, NT) * ATTN_SCALE
            where = key_position(kb, length)
            probs = jnp.where((where <= position) & (where >= start), jnp.exp(scores - lse), 0.0)
            grad_probs = dot(values[pl.ds(at, BLK), :], g2, NT)
            grad_scores = (probs * (grad_probs - delta)).astype(BF16)
            acc[...] += dot(keys_t[:, pl.ds(at, BLK)], grad_scores)
            grad_k[pl.ds(at, BLK), :] += dot(grad_scores, q2)
            grad_v[pl.ds(at, BLK), :] += dot(probs.astype(BF16), g2)
            return carry

        block_loop(block, per_half, body, 0)
        grad_q[pl.ds(pl.multiple_of(block * BLK, BLK), BLK), :] = fold_heads(jnp.transpose(acc[...]))

        @pl.when(lax.rem(block, 2) == 1)
        def _():
            tick(5 + block // 2)

        return carry

    lax.fori_loop(0, blocks, attend, 0)
    load_table.wait()
    for c in range(n):
        for hh in range(2):
            at = slice(hh * half + c * rows, hh * half + (c + 1) * rows)
            kk = grad_k[at, :]
            vv = grad_v[at, :]
            kk = (kk + pltpu.roll(kk, 64, 1)) * ATTN_SCALE
            vv = vv + pltpu.roll(vv, 64, 1)
            both = jnp.where(lane_iota(kk.shape) < 64, kk, vv)
            package = jnp.concatenate([grad_q[at, :] * ATTN_SCALE, both], -1)
            pack_out[c, hh * rows : (hh + 1) * rows, :] = turn(package, table[at, :], -1.0).astype(BF16)
    gr_exchange = (pack_out, grads_in, gr_send, gr_recv, local_sems.at[3], n)
    exchange_start(*gr_exchange)

    def fetch_w(c):
        slot = lax.rem(c, 2)
        return pltpu.make_async_copy(weights_ref.at[:, :, pl.ds(pl.multiple_of(c * PACK, PACK), PACK)], wbuf.at[slot], w_sems.at[slot])

    fetch_w(jnp.int32(0)).start()
    ys.over_x()
    tick(9)
    total[...] = jnp.zeros_like(total)
    mixed_ref[...] = middle_ref[...] + RESIDUAL * ys.finish()
    tick(10)
    exchange_wait(*gr_exchange)

    def finish_columns(c, carry):
        @pl.when(c + 1 < n)
        def _():
            fetch_w(c + 1).start()

        fetch_w(c).wait()
        slot = lax.rem(c, 2)
        g = grads_in[c]
        col[...] = dot(h_attn_ref[...], g, TN).astype(BF16)
        for r in range(8):
            at = pl.ds(pl.multiple_of(strip(r) * 128, 128), 128)
            small[r, pl.ds(pl.multiple_of(PIECE + c // 2 * 128, 128), 128), pl.ds(pl.multiple_of(lax.rem(c, 2) * PACK, PACK), PACK)] = col[at, :]
        for f in range(4):
            total[:, f * shard : (f + 1) * shard] += dot(g, wbuf[slot, f, :shard, :], NT)

        @pl.when(lax.rem(c, 4) == 3)
        def _():
            tick(11 + c // 4)

        return carry

    lax.fori_loop(0, n, finish_columns, 0)
    normed, scale = norm_parts(x_ref[...])
    grad_h = total[...]
    dgain[0:1, :] = jnp.sum(grad_h * normed, 0, keepdims=True)
    grad_x_ref[...] = grad_middle[...] + norm_back(grad_h * gains_ref[0:1], normed, scale)
    for r in range(8):
        at = pl.ds(pl.multiple_of(strip(r) * 128, 128), 128)
        row = row_iota((16, 128))
        both = jnp.where(row == 0, dgain[0:1, at], jnp.where(row == 1, dgain[1:2, at], 0.0))
        small[r, 384:400, 0:128] = both.astype(BF16)
    ws.start()
    tick(13)
    ws.over_cores()
    tick(14)
    ws.over_x()
    tick(15)
    tick(16)
    s_land[0] = ws.finish().astype(BF16)

    def rest(t, carry):
        tick(t)
        return carry

    lax.fori_loop(17, experts, rest, 0)
    late_source = lambda t: s_land.at[0, pl.ds((t - experts) * PIECE, PIECE)]
    for t in range(experts, experts + 6):
        line.tick(t, late_source)
    line.finish()


def backward_step(ends, pieces, gx, yp, full, weights, packs, table, h, middle, cot, wr, wo, gains, attn, lse, x, h_attn, n, length):
    tokens, width = x.shape
    hbm, vmem = pl.BlockSpec(memory_space=pl.ANY), pl.BlockSpec(memory_space=pltpu.VMEM)
    smem = pl.BlockSpec(memory_space=pltpu.SMEM)
    dma = lambda *k: pltpu.SemaphoreType.DMA(k)
    shaped = lambda shape, dtype=BF16: jax.ShapeDtypeStruct(shape, dtype)
    count = pieces.shape[0] + 2
    piece = (PIECE, PIECE)
    gx_shape, y_shape, s_shape = gx.shape[1:], yp.shape[1:], (2 * PIECE, PIECE)
    return pl.pallas_call(
        functools.partial(backward_kernel, n, length),
        in_specs=[smem] + [hbm] * 7 + [vmem] * 10,
        out_specs=[hbm, hbm, vmem, vmem],
        out_shape=[
            shaped((count,) + piece),
            shaped((count,) + piece),
            shaped((tokens, width), F32),
            shaped((tokens, width), F32),
        ],
        scratch_shapes=[
            pltpu.VMEM((RING,) + piece, BF16),
            pltpu.VMEM((RING,) + piece, BF16),
            pltpu.VMEM(piece, BF16),
            pltpu.VMEM((4,) + gx_shape, BF16),
            pltpu.VMEM((2,) + gx_shape, BF16),
            pltpu.VMEM(gx_shape, BF16),
            pltpu.VMEM((2,) + gx_shape, BF16),
            pltpu.VMEM((4,) + y_shape, BF16),
            pltpu.VMEM((2,) + y_shape, BF16),
            pltpu.VMEM(y_shape, BF16),
            pltpu.VMEM((2,) + y_shape, BF16),
            pltpu.VMEM((8,) + s_shape, BF16),
            pltpu.VMEM((4,) + s_shape, BF16),
            pltpu.VMEM((2,) + s_shape, BF16),
            pltpu.VMEM(s_shape, BF16),
            pltpu.VMEM(packs.shape, BF16),
            pltpu.VMEM(table.shape, F32),
            pltpu.VMEM((length, 128), BF16),
            pltpu.VMEM((length, 128), BF16),
            pltpu.VMEM((128, length), BF16),
            pltpu.VMEM((length, 128), F32),
            pltpu.VMEM((length, 128), F32),
            pltpu.VMEM((length, 128), F32),
            pltpu.VMEM((128, 2 * BLK), F32),
            pltpu.VMEM((2, 128, 2 * BLK), F32),
            pltpu.VMEM((n, tokens, 128), BF16),
            pltpu.VMEM((n, tokens, 128), BF16),
            pltpu.VMEM((n, tokens, PACK), BF16),
            pltpu.VMEM((n, tokens, PACK), BF16),
            pltpu.VMEM((2, 4, weights.shape[1], PACK), BF16),
            pltpu.VMEM((tokens, width), F32),
            pltpu.VMEM((tokens, width), F32),
            pltpu.VMEM((8, width), F32),
            pltpu.VMEM((width, PACK), BF16),
            dma(RING),
            dma(RING),
            dma(RING),
            dma(RING),
            dma(RING),
            dma(count),
            dma(RING),
            dma(1),
            dma(n - 1),
            dma(n - 1),
            dma(n - 1),
            dma(n - 1),
            dma(3, 7, 4),
            dma(4),
            dma(2),
            dma(2),
        ],
        compiler_params=params(63, collective_id=0, has_side_effects=True),
        cost_estimate=cost(4e10, 1e9),
        name="backward_step",
    )(ends, pieces, gx, yp, full, weights, packs, table, h, middle, cot, wr, wo, gains, attn, lse, x, h_attn)


def local(
    inputs,
    cotangent,
    doc_lengths,
    routes,
    attn_gain,
    ffn_gain,
    w_query,
    key_weight,
    value_weight,
    w_out,
    w_router,
    w_gate,
    w_up,
    w_down,
):
    rows = inputs.shape[2]
    width = inputs.shape[3]
    n = lax.axis_size("ctx")
    fsdp = lax.axis_size("fsdp")
    me, mine = lax.axis_index("ctx"), lax.axis_index("fsdp")
    tokens = 2 * rows
    length = tokens * n
    experts_here = w_gate.shape[0]
    number = experts_here // 2
    capacity = 5 * tokens * TOP // (4 * EXPERTS)
    capp = -(-capacity // 16) * 16
    shard = width // fsdp
    heads = QUERY_HEADS // n
    head_lanes = heads * HEAD_DIMENSION
    copies = n // KEY_VALUE_HEADS
    bits = group_bits(fsdp)

    x = inputs.reshape(tokens, width)
    cot = cotangent.reshape(tokens, width)
    side = me % 2
    base = (side * number).astype(jnp.int32).reshape(1)
    first = (mine * experts_here + side * number).astype(jnp.int32).reshape(1)
    index = jnp.stack([side * number, (1 - side) * number]).astype(jnp.int32)
    ends = jnp.cumsum(doc_lengths[0])[:3].astype(jnp.int32)
    table = jnp.asarray(rotary_table(length))

    out_part = w_out.reshape(shard // head_lanes, head_lanes, width)
    if head_lanes < 128:
        out_part = jnp.pad(out_part, ((0, 0), (0, 128 - head_lanes), (0, 0)))
    merge = lambda a: a.reshape(number, -1, a.shape[-1])

    if n == 8 and fsdp == 4:
        packs, h_attn, weights, wo, wr, cxs, gains = front(
            w_query,
            key_weight,
            value_weight,
            out_part,
            w_router,
            attn_gain.reshape(1, shard),
            ffn_gain.reshape(1, shard),
            x,
            table.reshape(2, n, rows, 256),
            routes.reshape(tokens, TOP),
            cot,
            capacity,
            n,
        )
        wo, wr = wo.reshape(n, 128, width), wr.reshape(width, 128)
        packs = packs.reshape(n, 2, rows, PACK)
        attn, lse, full, cx_rest = attend(ends, packs, cxs, length)
        middle, h_ffn, attn, xs, gs, gates = mid_step(attn.reshape(n, tokens, 128), cxs, cx_rest, wo, wr, x, gains[1:2], number, capp, n)
        slots = jnp.concatenate([cxs[:, tokens:], cx_rest[:, tokens:]], 0)
    else:
        own_table = lax.dynamic_slice_in_dim(table.reshape(2, n, rows, 256), me, 1, 1).reshape(tokens, 256)
        query_part = w_query.reshape(shard, n, head_lanes)
        if head_lanes < 128:
            query_part = jnp.pad(query_part, ((0, 0), (0, 0), (0, 128 - head_lanes)))
        key_part = jnp.repeat(key_weight.reshape(shard, KEY_VALUE_HEADS, HEAD_DIMENSION), copies, 1)
        value_part = jnp.repeat(value_weight.reshape(shard, KEY_VALUE_HEADS, HEAD_DIMENSION), copies, 1)
        packed = jnp.concatenate([query_part, key_part, value_part], -1).reshape(shard, n * PACK)
        padding = 2 * 16 * (shard // 32 + 1) - shard
        gains = jnp.pad(jnp.stack([attn_gain, ffn_gain]), ((0, padding - 2), (0, n * PACK - shard)))
        packed = jnp.concatenate([packed, gains], 0)
        router_part = jnp.pad(w_router, ((0, 0), (0, 128 - EXPERTS)))
        weights = lax.all_gather(packed, "fsdp", axis=0)
        gain_one = weights[:, shard, :shard].reshape(1, width).astype(F32)
        gain_two = weights[:, shard + 1, :shard].reshape(1, width).astype(F32)
        wo = lax.all_gather(out_part, "fsdp", axis=0, tiled=True)
        wr = lax.all_gather(router_part, "fsdp", axis=0, tiled=True)
        cxs = group_gather(prep(routes.reshape(tokens, TOP), cot, capacity), bits)
        packs, h_attn = qkv(x, gain_one, weights, own_table, shard, n)
        packs = lax.all_to_all(packs, "ctx", split_axis=0, concat_axis=0, tiled=True).reshape(n, 2, rows, PACK)
        attn, lse, full = attn_forward(ends, packs, length)
        attn = lax.all_to_all(attn.reshape(n, tokens, 128), "ctx", split_axis=0, concat_axis=0, tiled=True)
        middle, h_ffn = middle_step(attn, wo, x, gain_two)
        xs, gs, gates = gather_rows(first, group_gather(h_ffn, bits), cxs, jnp.transpose(wr), number, capp)
        slots = cxs[:, tokens:]
    xs, gs, gates = merge(xs), merge(gs), merge(gates)
    pieces, outs, back, dgates = expert_step(base, xs, gs, gates, w_gate, w_up, w_down)
    y_part, gx_part = combine(first, slots, outs, back, dgates, tokens, capp)
    pieces = pieces.reshape(number * 6, PIECE, PIECE)
    if n == 8 and fsdp == 4:
        own, other, grad_x, mixed = backward_step(
            ends, pieces, gx_part, y_part, full, weights, packs, table, h_ffn, middle, cot, wr, wo, gains, attn, lse, x, h_attn, n, length
        )
        shapes = [w.shape for w in (w_gate, w_up, w_down)]
        outs = tail(index, own, other, mixed, grad_x, shapes, shard)
        return (
            outs[3].reshape(inputs.shape),
            outs[4].reshape(inputs.shape),
            outs[10].reshape(shard),
            outs[11].reshape(shard),
            outs[5],
            outs[6],
            outs[7],
            outs[8],
            outs[9],
            outs[0],
            outs[1],
            outs[2],
        )
    gx = group_reduce(gx_part, bits)
    grad_middle, dwo, grad_attn, dwr, dgain_two = home_step(gx, h_ffn, middle, cot, wr, wo, gain_two, attn)
    grad_attn = lax.all_to_all(grad_attn, "ctx", split_axis=0, concat_axis=0, tiled=True).reshape(n, 2, rows, 128)
    grads = attn_backward(ends, packs, grad_attn, lse, full, table, length)
    grads = lax.all_to_all(grads.reshape(n, tokens, PACK), "ctx", split_axis=0, concat_axis=0, tiled=True)
    dw, grad_x, dgain_one = final_step(grads, weights, h_attn, x, gain_one, grad_middle, shard)
    mixed = middle + RESIDUAL * group_reduce(y_part, bits).astype(F32)
    own = line_sum(pieces, n)
    other = swap(own, "ctx", 1)
    scatter = lambda a: lax.psum(lax.psum_scatter(a, "fsdp", scatter_dimension=0, tiled=True), "ctx").astype(F32)
    dwo = scatter(dwo)[:, :head_lanes, :].reshape(shard, width)
    small = jnp.concatenate([dwr[:, :EXPERTS], dgain_two.reshape(width, 1).astype(BF16)], 1)
    small = scatter(jnp.pad(small, ((0, 0), (0, 127 - EXPERTS))))
    dwr, dgain_two = small[:, :EXPERTS], small[:, EXPERTS]
    dw = scatter(dw).reshape(shard, n, PACK)
    dgain_one = scatter(dgain_one.reshape(width).astype(BF16))

    outs = widen(index, own, other, [w.shape for w in (w_gate, w_up, w_down)])
    fold = lambda a: a.reshape(shard, KEY_VALUE_HEADS, copies, HEAD_DIMENSION).sum(2).reshape(shard, -1)
    return (
        mixed.reshape(inputs.shape),
        grad_x.reshape(inputs.shape),
        dgain_one,
        dgain_two,
        dw[:, :, :head_lanes].reshape(shard, -1),
        fold(dw[:, :, 128:192]),
        fold(dw[:, :, 192:256]),
        dwo,
        dwr,
        outs[0],
        outs[1],
        outs[2],
    )


def solution(mesh):
    tokens = P("fsdp", None, "ctx", None)
    one, two, three = P("fsdp"), P("fsdp", None), P("fsdp", None, None)
    return jax.shard_map(
        local,
        mesh=mesh,
        in_specs=(tokens, tokens, two, tokens, one, one, two, two, two, two, two, three, three, three),
        out_specs=(tokens, tokens, one, one, two, two, two, two, two, three, three, three),
        check_vma=False,
    )
```

```python
import functools

import jax
import jax.numpy as jnp
import numpy as np
from jax import lax
from jax.experimental import pallas as pl
from jax.experimental.pallas import tpu as pltpu
from jax.sharding import PartitionSpec as P

QUERY_HEADS = 16
KEY_VALUE_HEADS = 8
HEAD_DIMENSION = 64
EXPERTS = 32
TOP = 8

ATTN_SCALE = 0.015625
RESIDUAL = 0.22
NORM_EPS = 1e-06
ROPE_BASE = 10000.0
MASKED = -1e30

F32 = jnp.float32
BF16 = jnp.bfloat16
MIB = 1 << 20
NT = (((1,), (1,)), ((), ()))
TN = (((0,), (0,)), ((), ()))
BLK = 256
PACK = 256


def dot(a, b, dims=None):
    if dims is None:
        return jnp.dot(a, b, preferred_element_type=F32)
    return lax.dot_general(a, b, dims, preferred_element_type=F32)


def params(limit=56, **kw):
    return pltpu.CompilerParams(vmem_limit_bytes=limit * MIB, **kw)


def cost(flops, bytes_accessed):
    return pl.CostEstimate(flops=int(flops), bytes_accessed=int(bytes_accessed), transcendentals=0)


def lane_iota(shape):
    return lax.broadcasted_iota(jnp.int32, shape, len(shape) - 1)


def row_iota(shape):
    return lax.broadcasted_iota(jnp.int32, shape, len(shape) - 2)


def rotary_table(length):
    half = length // 2
    order = np.arange(half, dtype=np.float32)
    positions = np.concatenate([order, length - 1 - order]).astype(np.float32)
    m = np.arange(HEAD_DIMENSION // 2, dtype=np.float64)
    frequency = (ROPE_BASE ** (-2.0 * m / HEAD_DIMENSION)).astype(np.float32)
    angles = (positions[:, None] * frequency[None, :]).astype(np.float64)
    cosine, sine = np.cos(angles), np.sin(angles)
    cos_head = np.concatenate([cosine, cosine], -1)
    sin_head = np.concatenate([-sine, sine], -1)
    return np.concatenate([cos_head, cos_head, sin_head, sin_head], -1).astype(np.float32)


def turn(v, table, direction):
    lanes = lane_iota(v.shape)
    cosine = jnp.concatenate([table[:, :128], table[:, :128]], -1)
    sine = jnp.concatenate([table[:, 128:], table[:, 128:]], -1)
    turned = lanes < 3 * HEAD_DIMENSION
    swapped = jnp.where(lanes % HEAD_DIMENSION < HEAD_DIMENSION // 2, pltpu.roll(v, PACK - 32, 1), pltpu.roll(v, 32, 1))
    return jnp.where(turned, v * cosine + direction * (swapped * sine), v)


def norm_parts(values):
    inv_rms = lax.rsqrt(jnp.mean(values * values, -1, keepdims=True) + NORM_EPS)
    return values * inv_rms, inv_rms


def norm_back(grad_normed, normed, inv_rms):
    return inv_rms * (grad_normed - normed * jnp.mean(grad_normed * normed, -1, keepdims=True))


def prep_kernel(cap, routes_ref, cot_ref, out_ref):
    tokens, width = cot_ref.shape
    routes = routes_ref[...]
    earlier = (lane_iota((tokens, tokens)) < row_iota((tokens, tokens))).astype(BF16)
    experts = lane_iota((tokens, 128))
    base = jnp.zeros((1, 128), F32)
    plus = jnp.zeros((tokens, 128), F32)
    for k in range(TOP):
        chosen = experts == routes[:, k : k + 1]
        ones = chosen.astype(F32)
        slot = dot(earlier, ones.astype(BF16)) + base
        plus = plus + jnp.where(chosen & (slot < cap), slot + 1.0, 0.0)
        base = base + jnp.sum(ones, 0, keepdims=True)
    out_ref[:tokens, :] = cot_ref[...].astype(BF16)
    slots = (jnp.transpose(plus) - 1.0)[:EXPERTS, :]
    out_ref[tokens:, :] = jnp.concatenate([slots, jnp.zeros((EXPERTS, width - tokens), F32)], -1).astype(BF16)


def prep(routes, cot, cap):
    tokens, width = cot.shape
    return pl.pallas_call(
        functools.partial(prep_kernel, cap),
        out_shape=jax.ShapeDtypeStruct((tokens + EXPERTS, width), BF16),
        compiler_params=params(),
        cost_estimate=cost(1e9, 2e6),
        name="prep",
    )(routes, cot)


def qkv_kernel(shard, x_ref, gain_ref, w_ref, table_ref, out_ref, h_ref):
    @pl.when(pl.program_id(0) == 0)
    def _():
        normed, _ = norm_parts(x_ref[...])
        h_ref[...] = (normed * gain_ref[...]).astype(BF16)

    total = None
    for f in range(w_ref.shape[0]):
        part = dot(h_ref[:, f * shard : (f + 1) * shard], w_ref[f, :shard, :])
        total = part if total is None else total + part
    for d in range(out_ref.shape[0]):
        out_ref[d] = turn(total[:, d * PACK : (d + 1) * PACK], table_ref[...], 1.0).astype(BF16)


def qkv(x, gain, weights, table, shard, n):
    tokens, width = x.shape
    fsdp, padded, _ = weights.shape
    return pl.pallas_call(
        functools.partial(qkv_kernel, shard),
        grid=(n // 2,),
        in_specs=[
            pl.BlockSpec((tokens, width), lambda i: (0, 0)),
            pl.BlockSpec((1, width), lambda i: (0, 0)),
            pl.BlockSpec((fsdp, padded, 2 * PACK), lambda i: (0, 0, i)),
            pl.BlockSpec((tokens, 256), lambda i: (0, 0)),
        ],
        out_specs=[
            pl.BlockSpec((2, tokens, PACK), lambda i: (i, 0, 0)),
            pl.BlockSpec((tokens, width), lambda i: (0, 0)),
        ],
        out_shape=[
            jax.ShapeDtypeStruct((n, tokens, PACK), BF16),
            jax.ShapeDtypeStruct((tokens, width), BF16),
        ],
        compiler_params=params(),
        cost_estimate=cost(2 * tokens * width * n * PACK, 8e6),
        name="qkv",
    )(x, gain, weights, table)


def pair_keys(kv):
    other = pltpu.roll(kv, 64, 1)
    low = lane_iota(kv.shape) < 64
    return jnp.where(low, kv, other), jnp.where(low, other, kv)


def stack_heads(q):
    low = lane_iota(q.shape) < 64
    zero = jnp.zeros_like(q)
    return jnp.concatenate([jnp.where(low, q, zero), jnp.where(low, zero, q)], 0)


def fold_heads(stacked):
    rows = stacked.shape[0] // 2
    return jnp.where(lane_iota((rows, 128)) < 64, stacked[:rows], stacked[rows:])


def query_rows(ends_ref, block, length):
    half = length // 2
    lanes = lane_iota((1, 2 * BLK))
    index = block * BLK + jnp.where(lanes < BLK, lanes, lanes - BLK)
    position = jnp.where(index < half, index, length + half - 1 - index)
    start = jnp.zeros_like(position)
    for j in range(3):
        end = ends_ref[j]
        start = jnp.where(position >= end, jnp.maximum(start, end), start)
    return position, start


def key_position(kb, length):
    half = length // 2
    index = kb * BLK + row_iota((BLK, 1))
    return jnp.where(index < half, index, length + half - 1 - index)


def block_loop(block, per_half, body, init):
    late = block >= per_half
    inner = jnp.where(late, block - per_half, block)
    count = jnp.where(late, 2 * per_half - inner, inner + 1)

    def step(j, carry):
        kb = jnp.where(late & (j >= per_half), inner + j, j)
        return body(kb, carry)

    return lax.fori_loop(0, count, step, init)


def load_package(pack_ref, c, h):
    return pack_ref[c, h].astype(F32)


def attn_forward_kernel(length, ends_ref, q_ref, pack_ref, out_ref, lse_ref, full_ref, keys, values_t, acc):
    block = pl.program_id(0)
    half = length // 2
    n, _, rows, _ = pack_ref.shape

    @pl.when(block == 0)
    def _():
        for h in range(2):
            for c in range(n):
                kk, vv = pair_keys(pack_ref[c, h, :, 128:256].astype(F32))
                at = h * half + c * rows
                keys[at : at + rows, :] = kk.astype(BF16)
                if rows % 128 == 0:
                    values_t[:, at : at + rows] = jnp.transpose(vv).astype(BF16)
        if rows % 128 != 0:
            for h in range(2):
                for c in range(0, n, 2):
                    pair = jnp.concatenate([pack_ref[c, h, :, 128:256], pack_ref[c + 1, h, :, 128:256]], 0)
                    _, vv = pair_keys(pair.astype(F32))
                    at = h * half + c * rows
                    values_t[:, at : at + 2 * rows] = jnp.transpose(vv).astype(BF16)

    q = q_ref[...].reshape(BLK, PACK)[:, :128]
    q2 = stack_heads(q)
    position, start = query_rows(ends_ref, block, length)
    acc[...] = jnp.zeros_like(acc)

    def body(kb, carry):
        peak, total = carry
        at = pl.multiple_of(kb * BLK, BLK)
        scores = dot(keys[pl.ds(at, BLK), :], q2, NT) * ATTN_SCALE
        where = key_position(kb, length)
        scores = jnp.where((where <= position) & (where >= start), scores, MASKED)
        new_peak = jnp.maximum(peak, jnp.max(scores, 0, keepdims=True))
        weights = jnp.exp(scores - new_peak)
        fade = jnp.exp(peak - new_peak)
        total = total * fade + jnp.sum(weights, 0, keepdims=True)
        acc[...] = acc[...] * fade + dot(values_t[:, pl.ds(at, BLK)], weights.astype(BF16))
        return new_peak, total

    init = (jnp.full((1, 2 * BLK), MASKED, F32), jnp.zeros((1, 2 * BLK), F32))
    peak, total = block_loop(block, half // BLK, body, init)
    result = acc[...] / total
    full_ref[0] = result
    lse_ref[0] = peak + jnp.log(total)
    folded = fold_heads(jnp.transpose(result)).astype(BF16)
    out_ref[...] = folded.reshape(out_ref.shape)


def attn_forward(ends, packs, length):
    n, _, rows, _ = packs.shape
    blocks, per = length // BLK, BLK // rows
    per_half = blocks // 2
    tiles = lambda i, ends: (lax.rem(i, per_half), i // per_half, 0, 0)
    return pl.pallas_call(
        functools.partial(attn_forward_kernel, length),
        grid_spec=pltpu.PrefetchScalarGridSpec(
            num_scalar_prefetch=1,
            grid=(blocks,),
            in_specs=[
                pl.BlockSpec((per, 1, rows, PACK), tiles),
                pl.BlockSpec(packs.shape, lambda i, ends: (0, 0, 0, 0)),
            ],
            out_specs=[
                pl.BlockSpec((per, 1, rows, 128), tiles),
                pl.BlockSpec((1, 1, 2 * BLK), lambda i, ends: (i, 0, 0)),
                pl.BlockSpec((1, 128, 2 * BLK), lambda i, ends: (i, 0, 0)),
            ],
            scratch_shapes=[
                pltpu.VMEM((length, 128), BF16),
                pltpu.VMEM((128, length), BF16),
                pltpu.VMEM((128, 2 * BLK), F32),
            ],
        ),
        out_shape=[
            jax.ShapeDtypeStruct((n, 2, rows, 128), BF16),
            jax.ShapeDtypeStruct((blocks, 1, 2 * BLK), F32),
            jax.ShapeDtypeStruct((blocks, 128, 2 * BLK), F32),
        ],
        compiler_params=params(),
        cost_estimate=cost(1.5e10, 6e6),
        name="attn_forward",
    )(ends, packs, packs)


def attn_backward_kernel(length, ends_ref, q_ref, g_ref, pack_ref, lse_ref, full_ref, table_ref, out_ref, keys, values, keys_t, grad_q, grad_k, grad_v, acc):
    block = pl.program_id(0)
    half = length // 2
    n, _, rows, _ = pack_ref.shape

    @pl.when(block == 0)
    def _():
        for h in range(2):
            for c in range(n):
                kk, vv = pair_keys(pack_ref[c, h, :, 128:256].astype(F32))
                at = h * half + c * rows
                keys[at : at + rows, :] = kk.astype(BF16)
                values[at : at + rows, :] = vv.astype(BF16)
        for b in range(length // BLK):
            keys_t[:, b * BLK : (b + 1) * BLK] = jnp.transpose(keys[b * BLK : (b + 1) * BLK, :].astype(F32)).astype(BF16)
        grad_k[...] = jnp.zeros_like(grad_k)
        grad_v[...] = jnp.zeros_like(grad_v)

    q2 = stack_heads(q_ref[...].reshape(BLK, PACK)[:, :128])
    g2 = stack_heads(g_ref[...].reshape(BLK, 128))
    position, start = query_rows(ends_ref, block, length)
    lse = lse_ref[0]
    delta = jnp.sum(jnp.transpose(g2.astype(F32)) * full_ref[0], 0, keepdims=True)
    acc[...] = jnp.zeros_like(acc)

    def body(kb, carry):
        at = pl.multiple_of(kb * BLK, BLK)
        scores = dot(keys[pl.ds(at, BLK), :], q2, NT) * ATTN_SCALE
        where = key_position(kb, length)
        probs = jnp.where((where <= position) & (where >= start), jnp.exp(scores - lse), 0.0)
        grad_probs = dot(values[pl.ds(at, BLK), :], g2, NT)
        grad_scores = (probs * (grad_probs - delta)).astype(BF16)
        acc[...] += dot(keys_t[:, pl.ds(at, BLK)], grad_scores)
        grad_k[pl.ds(at, BLK), :] += dot(grad_scores, q2)
        grad_v[pl.ds(at, BLK), :] += dot(probs.astype(BF16), g2)
        return carry

    block_loop(block, half // BLK, body, 0)
    grad_q[pl.ds(pl.multiple_of(block * BLK, BLK), BLK), :] = fold_heads(jnp.transpose(acc[...]))

    @pl.when(block == length // BLK - 1)
    def _():
        for h in range(2):
            for c in range(n):
                at = slice(h * half + c * rows, h * half + (c + 1) * rows)
                kk = grad_k[at, :]
                vv = grad_v[at, :]
                kk = (kk + pltpu.roll(kk, 64, 1)) * ATTN_SCALE
                vv = vv + pltpu.roll(vv, 64, 1)
                both = jnp.where(lane_iota(kk.shape) < 64, kk, vv)
                package = jnp.concatenate([grad_q[at, :] * ATTN_SCALE, both], -1)
                out_ref[c, h] = turn(package, table_ref[at, :], -1.0).astype(BF16)


def attn_backward(ends, packs, grads, lse, full, table, length):
    n, _, rows, _ = packs.shape
    blocks, per = length // BLK, BLK // rows
    per_half = blocks // 2
    tiles = lambda i, ends: (lax.rem(i, per_half), i // per_half, 0, 0)
    return pl.pallas_call(
        functools.partial(attn_backward_kernel, length),
        grid_spec=pltpu.PrefetchScalarGridSpec(
            num_scalar_prefetch=1,
            grid=(blocks,),
            in_specs=[
                pl.BlockSpec((per, 1, rows, PACK), tiles),
                pl.BlockSpec((per, 1, rows, 128), tiles),
                pl.BlockSpec(packs.shape, lambda i, ends: (0, 0, 0, 0)),
                pl.BlockSpec((1, 1, 2 * BLK), lambda i, ends: (i, 0, 0)),
                pl.BlockSpec((1, 128, 2 * BLK), lambda i, ends: (i, 0, 0)),
                pl.BlockSpec(table.shape, lambda i, ends: (0, 0)),
            ],
            out_specs=pl.BlockSpec(packs.shape, lambda i, ends: (0, 0, 0, 0)),
            scratch_shapes=[
                pltpu.VMEM((length, 128), BF16),
                pltpu.VMEM((length, 128), BF16),
                pltpu.VMEM((128, length), BF16),
                pltpu.VMEM((length, 128), F32),
                pltpu.VMEM((length, 128), F32),
                pltpu.VMEM((length, 128), F32),
                pltpu.VMEM((128, 2 * BLK), F32),
            ],
        ),
        out_shape=jax.ShapeDtypeStruct(packs.shape, BF16),
        compiler_params=params(),
        cost_estimate=cost(3e10, 8e6),
        name="attn_backward",
    )(ends, packs, grads, packs, lse, full, table)


def middle_kernel(attn_ref, wo_ref, x_ref, gain_ref, middle_ref, h_ref):
    total = None
    for c in range(attn_ref.shape[0]):
        part = dot(attn_ref[c], wo_ref[c])
        total = part if total is None else total + part
    middle = x_ref[...] + RESIDUAL * total
    middle_ref[...] = middle
    normed, _ = norm_parts(middle)
    h_ref[...] = (normed * gain_ref[...]).astype(BF16)


def middle_step(attn, wo, x, gain):
    tokens, width = x.shape
    return pl.pallas_call(
        middle_kernel,
        out_shape=[jax.ShapeDtypeStruct((tokens, width), F32), jax.ShapeDtypeStruct((tokens, width), BF16)],
        compiler_params=params(),
        cost_estimate=cost(2 * tokens * width * width, 5e6),
        name="middle",
    )(attn, wo, x, gain)


def own_row(table, row):
    return jnp.sum(jnp.where(row_iota(table.shape) == row, table, 0.0), 0, keepdims=True)


def one_hot(slots, first, number, capp):
    tokens = slots.shape[1]
    order = row_iota((capp, tokens)).astype(F32)
    return [(order == own_row(slots, first + j)).astype(F32) for j in range(number)]


def gather_kernel(number, capp, first_ref, h_ref, cx_ref, wrt_ref, x_ref, g_ref, gate_ref):
    tokens = h_ref.shape[1]
    first = first_ref[0]
    h = h_ref[0]
    slots = cx_ref[0, tokens:, :tokens].astype(F32)
    logits = dot(wrt_ref[...], h, NT)[:EXPERTS, :]
    raw = jnp.exp(logits - jnp.max(logits, 0, keepdims=True))
    router = raw / jnp.sum(raw, 0, keepdims=True)
    hots = one_hot(slots, first, number, capp)
    places = jnp.concatenate(hots, 0).astype(BF16)
    rows = dot(places, h).astype(BF16)
    grads = dot(places, cx_ref[0, :tokens, :]).astype(BF16)
    for j in range(number):
        at = slice(j * capp, (j + 1) * capp)
        x_ref[j, 0] = rows[at]
        g_ref[j, 0] = grads[at]
        gate = jnp.sum(hots[j] * own_row(router, first + j), 1, keepdims=True)
        gate_ref[j, 0] = jnp.broadcast_to(gate, (capp, 128))


def gather_rows(first, hs, cxs, wrt, number, capp):
    nb, tokens, width = hs.shape
    return pl.pallas_call(
        functools.partial(gather_kernel, number, capp),
        grid_spec=pltpu.PrefetchScalarGridSpec(
            num_scalar_prefetch=1,
            grid=(nb,),
            in_specs=[
                pl.BlockSpec((1, tokens, width), lambda b, f: (b, 0, 0)),
                pl.BlockSpec((1, tokens + EXPERTS, width), lambda b, f: (b, 0, 0)),
                pl.BlockSpec(wrt.shape, lambda b, f: (0, 0)),
            ],
            out_specs=[
                pl.BlockSpec((number, 1, capp, width), lambda b, f: (0, b, 0, 0)),
                pl.BlockSpec((number, 1, capp, width), lambda b, f: (0, b, 0, 0)),
                pl.BlockSpec((number, 1, capp, 128), lambda b, f: (0, b, 0, 0)),
            ],
        ),
        out_shape=[
            jax.ShapeDtypeStruct((number, nb, capp, width), BF16),
            jax.ShapeDtypeStruct((number, nb, capp, width), BF16),
            jax.ShapeDtypeStruct((number, nb, capp, 128), F32),
        ],
        compiler_params=params(),
        cost_estimate=cost(4 * nb * number * capp * tokens * width, 2e7),
        name="gather_rows",
    )(first, hs, cxs, wrt)


PIECE = 512


def expert_kernel(base_ref, x_ref, g_ref, gate_ref, wg_ref, wu_ref, wd_ref, piece_ref, out_ref, rows_ref, dg_ref):
    x = x_ref[0]
    gate = gate_ref[0][:, :1]
    grad_ffn = RESIDUAL * g_ref[0].astype(F32)
    go = (gate * grad_ffn).astype(BF16)
    part = wg_ref.shape[2] // 2
    out = rows = None
    for chunk in range(2):
        at = slice(chunk * part, (chunk + 1) * part)
        wg, wu, wd = wg_ref[0, :, at], wu_ref[0, :, at], wd_ref[0, at, :]
        pre_gate = dot(x, wg)
        pre_up = dot(x, wu)
        sig = jax.nn.sigmoid(pre_gate)
        hidden = (pre_gate * sig * pre_up).astype(BF16)
        out_part = dot(hidden, wd)
        grad_hidden = dot(go, wd, NT)
        grad_gate = (grad_hidden * pre_up * sig * (1.0 + pre_gate * (1.0 - sig))).astype(BF16)
        grad_up = (grad_hidden * pre_gate * sig).astype(BF16)
        row_part = dot(grad_gate, wg, NT) + dot(grad_up, wu, NT)
        dwg = dot(x, grad_gate, TN).astype(BF16)
        dwu = dot(x, grad_up, TN).astype(BF16)
        dwd = dot(hidden, go, TN).astype(BF16)
        for half in range(2):
            side = slice(half * PIECE, (half + 1) * PIECE)
            piece_ref[0, half, :, at] = dwg[side]
            piece_ref[0, 2 + half, :, at] = dwu[side]
            piece_ref[0, 4 + half, at, :] = dwd[:, side]
        out = out_part if out is None else out + out_part
        rows = row_part if rows is None else rows + row_part
    out = out.astype(BF16).astype(F32)
    out_ref[0] = (gate * out).astype(BF16)
    rows_ref[0] = rows.astype(BF16)
    grad = jnp.sum(grad_ffn * out, 1, keepdims=True)
    dg_ref[0] = jnp.broadcast_to(grad, dg_ref.shape[1:])


def expert_step(base, xs, gs, gates, w_gate, w_up, w_down):
    number, rows, width = xs.shape
    ff = w_gate.shape[2]
    row = lambda e, b: (e, 0, 0)
    weight = lambda e, b: (b[0] + e, 0, 0)
    return pl.pallas_call(
        expert_kernel,
        grid_spec=pltpu.PrefetchScalarGridSpec(
            num_scalar_prefetch=1,
            grid=(number,),
            in_specs=[
                pl.BlockSpec((1, rows, width), row),
                pl.BlockSpec((1, rows, width), row),
                pl.BlockSpec((1, rows, 128), row),
                pl.BlockSpec((1, width, ff), weight),
                pl.BlockSpec((1, width, ff), weight),
                pl.BlockSpec((1, ff, width), weight),
            ],
            out_specs=[
                pl.BlockSpec((1, 6, PIECE, PIECE), lambda e, b: (e, 0, 0, 0)),
                pl.BlockSpec((1, rows, width), row),
                pl.BlockSpec((1, rows, width), row),
                pl.BlockSpec((1, rows, 128), row),
            ],
        ),
        out_shape=[
            jax.ShapeDtypeStruct((number, 6, PIECE, PIECE), BF16),
            jax.ShapeDtypeStruct((number, rows, width), BF16),
            jax.ShapeDtypeStruct((number, rows, width), BF16),
            jax.ShapeDtypeStruct((number, rows, 128), F32),
        ],
        compiler_params=params(60),
        cost_estimate=cost(18 * number * rows * width * ff, 5e7),
        name="expert_step",
    )(base, xs, gs, gates, w_gate, w_up, w_down)


def combine_kernel(number, capp, first_ref, slot_ref, outs, rows, grads, y_ref, gx_ref):
    tokens = y_ref.shape[1]
    width = y_ref.shape[2]
    first = first_ref[0]
    slots = slot_ref[0][:, :tokens].astype(F32)
    hots = one_hot(slots, first, number, capp)
    places = jnp.concatenate(hots, 0).astype(BF16)
    y_ref[0] = dot(places, outs[:, 0].reshape(number * capp, width), TN).astype(BF16)
    gx_ref[0, :tokens] = dot(places, rows[:, 0].reshape(number * capp, width), TN).astype(BF16)
    extra = jnp.zeros((EXPERTS, 2 * tokens), F32)
    for j in range(number):
        grad = jnp.sum(hots[j] * grads[j, 0][:, :1], 0, keepdims=True)
        high = grad.astype(BF16).astype(F32)
        both = jnp.concatenate([high, grad - high], 1)
        extra = jnp.where(row_iota(extra.shape) == first + j, both, extra)
    rest = jnp.zeros((EXPERTS, width - 2 * tokens), F32)
    gx_ref[0, tokens:] = jnp.concatenate([extra, rest], 1).astype(BF16)


def combine(first, slots, outs, rows, grads, tokens, capp):
    number = outs.shape[0]
    nb, _, width = slots.shape
    split = lambda a: a.reshape(number, nb, capp, a.shape[-1])
    wide = pl.BlockSpec((number, 1, capp, width), lambda b, f: (0, b, 0, 0))
    thin = pl.BlockSpec((number, 1, capp, 128), lambda b, f: (0, b, 0, 0))
    return pl.pallas_call(
        functools.partial(combine_kernel, number, capp),
        grid_spec=pltpu.PrefetchScalarGridSpec(
            num_scalar_prefetch=1,
            grid=(nb,),
            in_specs=[pl.BlockSpec((1, EXPERTS, width), lambda b, f: (b, 0, 0))] + [wide, wide, thin],
            out_specs=[
                pl.BlockSpec((1, tokens, width), lambda b, f: (b, 0, 0)),
                pl.BlockSpec((1, tokens + EXPERTS, width), lambda b, f: (b, 0, 0)),
            ],
        ),
        out_shape=[
            jax.ShapeDtypeStruct((nb, tokens, width), BF16),
            jax.ShapeDtypeStruct((nb, tokens + EXPERTS, width), BF16),
        ],
        compiler_params=params(),
        cost_estimate=cost(4 * nb * number * capp * tokens * width, 2e7),
        name="combine",
    )(first, slots, split(outs), split(rows), split(grads))


def home_kernel(gx_ref, h_ref, middle_ref, cot_ref, wr_ref, wo_ref, gain_ref, attn_ref, grad_middle_ref, dwo_ref, ga_ref, dwr_ref, dgain_ref):
    tokens, width = h_ref.shape
    h = h_ref[...]
    gain = gain_ref[...]
    extra = gx_ref[tokens:, :].astype(F32)
    grad_router = extra[:, :tokens] + extra[:, tokens : 2 * tokens]
    grad_router = jnp.transpose(jnp.concatenate([grad_router, jnp.zeros((128 - EXPERTS, tokens), F32)], 0))
    logits = dot(h, wr_ref[...])
    logits = jnp.where(lane_iota(logits.shape) < EXPERTS, logits, MASKED)
    raw = jnp.exp(logits - jnp.max(logits, -1, keepdims=True))
    router = raw / jnp.sum(raw, -1, keepdims=True)
    grad_logits = (router * (grad_router - jnp.sum(router * grad_router, -1, keepdims=True))).astype(BF16)
    dwr_ref[...] = dot(h, grad_logits, TN).astype(BF16)
    grad_h = gx_ref[:tokens, :].astype(F32) + dot(grad_logits, wr_ref[...], NT)
    normed, scale = norm_parts(middle_ref[...])
    dgain_ref[...] = jnp.sum(grad_h * normed, 0, keepdims=True)
    grad_middle = cot_ref[...] + norm_back(grad_h * gain, normed, scale)
    grad_middle_ref[...] = grad_middle
    grad_branch = (RESIDUAL * grad_middle).astype(BF16)
    for c in range(attn_ref.shape[0]):
        dwo_ref[c] = dot(attn_ref[c], grad_branch, TN).astype(BF16)
        ga_ref[c] = dot(grad_branch, wo_ref[c], NT).astype(BF16)


def home_step(gx, h, middle, cot, wr, wo, gain, attn):
    tokens, width = h.shape
    n = attn.shape[0]
    return pl.pallas_call(
        home_kernel,
        out_shape=[
            jax.ShapeDtypeStruct((tokens, width), F32),
            jax.ShapeDtypeStruct((n, 128, width), BF16),
            jax.ShapeDtypeStruct((n, tokens, 128), BF16),
            jax.ShapeDtypeStruct((width, 128), BF16),
            jax.ShapeDtypeStruct((1, width), F32),
        ],
        compiler_params=params(),
        cost_estimate=cost(4 * tokens * width * width, 1e7),
        name="home_step",
    )(gx, h, middle, cot, wr, wo, gain, attn)


def final_kernel(shard, grads_ref, w_ref, h_ref, x_ref, gain_ref, grad_middle_ref, dw_ref, grad_x_ref, dgain_ref, total):
    c = pl.program_id(0)
    g = grads_ref[0]
    dw_ref[...] = dot(h_ref[...], g, TN).astype(BF16)

    @pl.when(c == 0)
    def _():
        total[...] = jnp.zeros_like(total)

    for f in range(w_ref.shape[0]):
        total[:, f * shard : (f + 1) * shard] += dot(g, w_ref[f, :shard, :], NT)

    @pl.when(c == pl.num_programs(0) - 1)
    def _():
        normed, scale = norm_parts(x_ref[...])
        grad_h = total[...]
        dgain_ref[...] = jnp.sum(grad_h * normed, 0, keepdims=True)
        grad_x_ref[...] = grad_middle_ref[...] + norm_back(grad_h * gain_ref[...], normed, scale)


def final_step(grads, weights, h, x, gain, grad_middle, shard):
    n, tokens, _ = grads.shape
    width = x.shape[1]
    fsdp, padded, _ = weights.shape
    same = lambda c: (0, 0)
    return pl.pallas_call(
        functools.partial(final_kernel, shard),
        grid=(n,),
        in_specs=[
            pl.BlockSpec((1, tokens, PACK), lambda c: (c, 0, 0)),
            pl.BlockSpec((fsdp, padded, PACK), lambda c: (0, 0, c)),
            pl.BlockSpec((tokens, width), same),
            pl.BlockSpec((tokens, width), same),
            pl.BlockSpec((1, width), same),
            pl.BlockSpec((tokens, width), same),
        ],
        out_specs=[
            pl.BlockSpec((width, PACK), lambda c: (0, c)),
            pl.BlockSpec((tokens, width), same),
            pl.BlockSpec((1, width), same),
        ],
        out_shape=[
            jax.ShapeDtypeStruct((width, n * PACK), BF16),
            jax.ShapeDtypeStruct((tokens, width), F32),
            jax.ShapeDtypeStruct((1, width), F32),
        ],
        scratch_shapes=[pltpu.VMEM((tokens, width), F32)],
        compiler_params=params(),
        cost_estimate=cost(4 * tokens * width * n * PACK, 1.2e7),
        name="final_step",
    )(grads, weights, h, x, gain, grad_middle)


def widen_kernel(number, index_ref, own_ref, other_ref, gate_ref, up_ref, down_ref):
    def write(ref):
        for half in range(2):
            at = slice(half * PIECE, (half + 1) * PIECE)
            gate_ref[0, at, :] = ref[half].astype(F32)
            up_ref[0, at, :] = ref[2 + half].astype(F32)
            down_ref[0, :, at] = ref[4 + half].astype(F32)

    @pl.when(pl.program_id(0) == 0)
    def _():
        write(own_ref)

    @pl.when(pl.program_id(0) == 1)
    def _():
        write(other_ref)


def tail_kernel(number, index_ref, own_ref, other_ref, own_small_ref, other_small_ref, mixed_in, grad_in, gate_ref, up_ref, down_ref, mixed_ref, grad_ref, dwq_ref, dwk_ref, dwv_ref, dwo_ref, dwr_ref, g1_ref, g2_ref):
    widen_kernel(number, index_ref, own_ref, other_ref, gate_ref, up_ref, down_ref)
    mixed_ref[...] = mixed_in[...]
    grad_ref[...] = grad_in[...]

    @pl.when((pl.program_id(0) == 0) & (pl.program_id(1) == 0))
    def _():
        for which, ref in enumerate((own_small_ref, other_small_ref)):
            part = index_ref[which] // number
            at = pl.ds(pl.multiple_of(part * 128, 128), 128)
            for q in range(4):
                block = ref[1, q * 128 : (q + 1) * 128, :].astype(F32)
                dwq_ref[at, q * 256 : q * 256 + 128] = block[:, :128]
                dwq_ref[at, q * 256 + 128 : (q + 1) * 256] = block[:, 256:384]
                one, two = block[:, 128:256], block[:, 384:]
                low = lane_iota(one.shape) < HEAD_DIMENSION
                dwk_ref[at, q * 128 : (q + 1) * 128] = jnp.where(low, one, pltpu.roll(two, 64, 1))
                dwv_ref[at, q * 128 : (q + 1) * 128] = jnp.where(low, pltpu.roll(one, 64, 1), two)
            dwo_ref[at, :PIECE] = ref[0, 0:128, :].astype(F32)
            dwo_ref[at, PIECE:] = ref[0, 128:256, :].astype(F32)
            dwr_ref[at, :] = ref[0, 256:384, :EXPERTS].astype(F32)
            gains = ref[0, 384:400, :128].astype(F32)
            g1_ref[pl.ds(part, 1), :] = gains[0:1]
            g2_ref[pl.ds(part, 1), :] = gains[1:2]


def expert_specs(number, shapes):
    last = number - 1
    ins = [
        pl.BlockSpec((6, PIECE, PIECE), lambda s, e, at: (jnp.where(s == 0, e, last), 0, 0)),
        pl.BlockSpec((6, PIECE, PIECE), lambda s, e, at: (jnp.where(s == 0, 0, e), 0, 0)),
    ]
    outs = [pl.BlockSpec((1,) + tuple(shape[1:]), lambda s, e, at: (at[s] + e, 0, 0)) for shape in shapes]
    return ins, outs, [jax.ShapeDtypeStruct(shape, F32) for shape in shapes]


def widen(index, own, other, shapes):
    number = shapes[0][0] // 2
    ins, outs, out_shapes = expert_specs(number, shapes)
    return pl.pallas_call(
        functools.partial(widen_kernel, number),
        grid_spec=pltpu.PrefetchScalarGridSpec(num_scalar_prefetch=1, grid=(2, number), in_specs=ins, out_specs=outs),
        out_shape=out_shapes,
        compiler_params=params(),
        cost_estimate=cost(0, 1e8),
        name="widen",
    )(index, own, other)


def tail(index, own, other, mixed, grad_x, shapes, shard):
    number = shapes[0][0] // 2
    tokens, width = mixed.shape
    ins, outs, out_shapes = expert_specs(number, shapes)
    small = pl.BlockSpec((2, PIECE, PIECE), lambda s, e, at: (3 * number, 0, 0))
    rows = pl.BlockSpec((tokens // (2 * number), width), lambda s, e, at: (s * number + e, 0))
    small_shapes = [(shard, width), (shard, width // 2), (shard, width // 2), (shard, width), (shard, EXPERTS), (2, 128), (2, 128)]
    whole = [pl.BlockSpec(shape, lambda s, e, at: (0, 0)) for shape in small_shapes]
    return pl.pallas_call(
        functools.partial(tail_kernel, number),
        grid_spec=pltpu.PrefetchScalarGridSpec(
            num_scalar_prefetch=1,
            grid=(2, number),
            in_specs=ins + [small, small, rows, rows],
            out_specs=outs + [rows, rows] + whole,
        ),
        out_shape=out_shapes
        + [jax.ShapeDtypeStruct((tokens, width), F32)] * 2
        + [jax.ShapeDtypeStruct(shape, F32) for shape in small_shapes],
        compiler_params=params(),
        cost_estimate=cost(0, 1e8),
        name="tail",
    )(index, own, other, own, other, mixed, grad_x)


def swap(value, axis, bit):
    size = lax.axis_size(axis)
    return lax.ppermute(value, axis, [(i, i ^ bit) for i in range(size)])


def group_bits(fsdp):
    bits = [("fsdp", 1 << b) for b in range(1, fsdp.bit_length() - 1)]
    return bits + [("ctx", 1), ("fsdp", 1)]


def group_gather(value, bits):
    stacked = value[None]
    for axis, bit in bits:
        stacked = jnp.concatenate([stacked, swap(stacked, axis, bit)], 0)
    return stacked


def group_reduce(stacked, bits):
    for axis, bit in reversed(bits):
        half = stacked.shape[0] // 2
        arrived = swap(stacked[half:], axis, bit)
        stacked = (stacked[:half].astype(F32) + arrived.astype(F32)).astype(stacked.dtype)
    return stacked[0]


def line_sum(value, ctx):
    pairs = ctx // 2
    if pairs != 4:
        bit = 2
        while bit < ctx:
            value = value + swap(value, "ctx", bit)
            bit *= 2
        return value
    at = lambda z, y: 2 * z + y
    inward = [(at(0, y), at(1, y)) for y in range(2)] + [(at(3, y), at(2, y)) for y in range(2)]
    across = [(at(1, y), at(2, y)) for y in range(2)] + [(at(2, y), at(1, y)) for y in range(2)]
    outward = [(b, a) for a, b in inward]
    value = value + lax.ppermute(value, "ctx", inward)
    value = value + lax.ppermute(value, "ctx", across)
    arrived = lax.ppermute(value, "ctx", outward)
    z = lax.axis_index("ctx") // 2
    return jnp.where((z == 0) | (z == 3), arrived, value)


MESH = pl.DeviceIdType.MESH


def flip(index, bit):
    return jnp.where((index // bit) % 2 == 0, index + bit, index - bit)


def send(src, dst, send_sem, recv_sem, device):
    return pltpu.make_async_remote_copy(src_ref=src, dst_ref=dst, send_sem=send_sem, recv_sem=recv_sem, device_id=device, device_id_type=MESH)


def neighbours():
    ctx, fsdp = lax.axis_index("ctx"), lax.axis_index("fsdp")
    side, across = flip(ctx, 1), flip(fsdp, 2)
    core = {"fsdp": flip(fsdp, 1)}
    return core, [{"fsdp": across}, {"ctx": side}, {"ctx": side, "fsdp": across}]


def greet(devices):
    barrier = pltpu.get_barrier_semaphore()
    for device in devices:
        pl.semaphore_signal(barrier, inc=1, device_id=device, device_id_type=MESH)
    pl.semaphore_wait(barrier, len(devices))


def others(n):
    ctx = lax.axis_index("ctx")
    return [lax.rem(ctx + d, n) for d in range(1, n)]


def exchange_start(src, dst, send_sems, recv_sems, local_sem, n):
    ctx = lax.axis_index("ctx")
    for d, c in enumerate(others(n)):
        send(src.at[c], dst.at[ctx], send_sems.at[d], recv_sems.at[d], {"ctx": c}).start()
    pltpu.make_async_copy(src.at[ctx], dst.at[ctx], local_sem).start()


def exchange_wait(src, dst, send_sems, recv_sems, local_sem, n, arrived=None):
    ctx = lax.axis_index("ctx")
    pltpu.make_async_copy(src.at[ctx], dst.at[ctx], local_sem).wait()
    if arrived is not None:
        arrived(ctx)
    for d in range(n - 1):
        source = lax.rem(ctx + n - 1 - d, n)
        send(src.at[source], dst.at[source], send_sems.at[d], recv_sems.at[d], {"ctx": source}).wait_recv()
        if arrived is not None:
            arrived(source)
    for d, c in enumerate(others(n)):
        send(src.at[c], dst.at[ctx], send_sems.at[d], recv_sems.at[d], {"ctx": c}).wait_send()


def front_kernel(n, cap, wq_ref, wk_ref, wv_ref, wo_part_ref, wr_raw_ref, g1_ref, g2_ref, x_ref, table_ref, routes_ref, cot_ref, packs_ref, h_ref, weights_ref, wo_ref, wr_ref, cxs_ref, gains_ref, wall, packed_ref, wr_part_ref, cx, table, normed_ref, total, out, exch_send, exch_recv, full_send, full_recv, x_send, x_recv, y_send, y_recv, xs_send, xs_recv, ys_send, ys_recv, cx_send, cx_recv, local_sems):
    width = x_ref.shape[1]
    shard = width // 4
    ctx, fsdp = lax.axis_index("ctx"), lax.axis_index("fsdp")
    parity = lax.rem(ctx, 2)
    core, group = neighbours()
    far, near = group[0], group[1]
    sibling, distant = flip(fsdp, 1), flip(fsdp, 2)
    other = flip(distant, 1)
    for k in range(2):
        pltpu.make_async_copy(table_ref.at[k, ctx], table.at[k], local_sems.at[6 + k]).start()

    pair = HEAD_DIMENSION * 2
    for c in range(0, n, 2):
        for k in range(2):
            packed_ref[:shard, (c + k) * PACK : (c + k) * PACK + 128] = wq_ref[:, (c + k) * 128 : (c + k + 1) * 128]
        keys, values = wk_ref[:, c // 2 * pair : (c // 2 + 1) * pair].astype(F32), wv_ref[:, c // 2 * pair : (c // 2 + 1) * pair].astype(F32)
        low = lane_iota(keys.shape) < HEAD_DIMENSION
        packed_ref[:shard, c * PACK + 128 : (c + 1) * PACK] = jnp.where(low, keys, pltpu.roll(values, 64, 1)).astype(BF16)
        packed_ref[:shard, (c + 1) * PACK + 128 : (c + 2) * PACK] = jnp.where(low, pltpu.roll(keys, 64, 1), values).astype(BF16)
    row = row_iota((16, shard))
    gain_rows = jnp.where(row == 0, g1_ref[...].astype(F32), jnp.where(row == 1, g2_ref[...].astype(F32), 0.0))
    packed_ref[shard:, :] = jnp.zeros((packed_ref.shape[0] - shard, n * PACK), BF16)
    packed_ref[shard : shard + 16, :shard] = gain_rows.astype(BF16)
    wr_part_ref[...] = jnp.concatenate([wr_raw_ref[...].astype(F32), jnp.zeros((shard, 128 - EXPERTS), F32)], 1).astype(BF16)
    greet([core, far] + [{"ctx": c} for c in others(n)])

    half_rows = packed_ref.shape[0] // 2
    low_rows = half_rows // 32 * 16

    def cut(k, part):
        if k == 0:
            return pl.ds(pl.multiple_of(part * half_rows, 16), low_rows)
        if k == 1:
            return pl.ds(pl.multiple_of(part * half_rows + low_rows, 16), half_rows - low_rows)
        if k == 2:
            return pl.ds(part, 1)
        return pl.ds(pl.multiple_of(part * (shard // 2), 16), shard // 2)

    sources = [packed_ref, packed_ref, wo_part_ref, wr_part_ref]
    targets = [wall, wall, wo_ref, wr_ref]
    wholes = [(packed_ref, wall), (wo_part_ref, wo_ref), (wr_part_ref, wr_ref)]

    def whole(i):
        src, dst = wholes[i]
        return send(src, dst.at[fsdp], full_send.at[i], full_recv.at[i], core)

    def own(i):
        src, dst = wholes[i]
        return pltpu.make_async_copy(src, dst.at[fsdp], local_sems.at[i])

    def to_far(k):
        return send(sources[k].at[cut(k, parity)], targets[k].at[fsdp, cut(k, parity)], x_send.at[k], x_recv.at[k], far)

    def pass_on(k, part, sems, device):
        ref = targets[k].at[distant, cut(k, part)]
        return send(ref, ref, sems[0].at[k], sems[1].at[k], device)

    def far_arrived(k):
        ref = targets[k].at[distant, cut(k, parity)]
        send(ref, ref, x_send.at[k], x_recv.at[k], far).wait_recv()
        pass_on(k, parity, (y_send, y_recv), near).start()
        pass_on(k, parity, (xs_send, xs_recv), core).start()

    def near_arrived(k):
        pass_on(k, 1 - parity, (y_send, y_recv), near).wait_recv()
        pass_on(k, 1 - parity, (ys_send, ys_recv), core).start()

    def core_arrived(k):
        for part, sems in ((parity, (xs_send, xs_recv)), (1 - parity, (ys_send, ys_recv))):
            ref = targets[k].at[other, cut(k, part)]
            send(ref, ref, sems[0].at[k], sems[1].at[k], core).wait_recv()

    own(0).start()
    to_far(0).start()
    to_far(1).start()
    whole(0).start()

    prep_kernel(cap, routes_ref, cot_ref, cx)
    pltpu.make_async_copy(cx, cxs_ref.at[0], local_sems.at[3]).start()
    normed, _ = norm_parts(x_ref[...])
    normed_ref[...] = normed

    def project(block, begin):
        at = pl.ds(pl.multiple_of(block * shard, shard), shard)
        gain = wall[block, shard : shard + 16, :shard].astype(F32)
        gains_ref[:, at] = gain
        h = (normed_ref[:, at] * gain[:1]).astype(BF16)
        h_ref[:, at] = h
        part = dot(h, wall[block, :shard, :])
        total[...] = part if begin else total[...] + part

    own(0).wait()
    project(fsdp, True)
    ref = wall.at[sibling]
    send(ref, ref, full_send.at[0], full_recv.at[0], core).wait_recv()
    project(sibling, False)
    far_arrived(0)
    far_arrived(1)
    for i in (1, 2):
        own(i).start()
        whole(i).start()
        to_far(i + 1).start()
    send(cx, cxs_ref.at[1], cx_send.at[0], cx_recv.at[0], far).start()
    near_arrived(0)
    near_arrived(1)
    project(distant, False)
    core_arrived(0)
    core_arrived(1)
    project(other, False)
    keep = pltpu.make_async_copy(wall, weights_ref, local_sems.at[4])
    keep.start()
    for k in range(2):
        pltpu.make_async_copy(table_ref.at[k, ctx], table.at[k], local_sems.at[6 + k]).wait()
    angles = table[...].reshape(x_ref.shape[0], 256)
    for c in range(n):
        out[c] = turn(total[:, c * PACK : (c + 1) * PACK], angles, 1.0).astype(BF16)
    exchange = (out, packs_ref, exch_send, exch_recv, local_sems.at[5], n)
    exchange_start(*exchange)

    for k in (2, 3):
        far_arrived(k)
    for k in (2, 3):
        near_arrived(k)
    for k in (2, 3):
        core_arrived(k)
    for i in (1, 2):
        src, dst = wholes[i]
        ref = dst.at[sibling]
        send(ref, ref, full_send.at[i], full_recv.at[i], core).wait_recv()
        own(i).wait()
    exchange_wait(*exchange)
    for i in range(3):
        whole(i).wait_send()
    for k in range(4):
        to_far(k).wait_send()
        pass_on(k, parity, (y_send, y_recv), near).wait_send()
        pass_on(k, parity, (xs_send, xs_recv), core).wait_send()
        pass_on(k, 1 - parity, (ys_send, ys_recv), core).wait_send()
    send(cx, cxs_ref.at[1], cx_send.at[0], cx_recv.at[0], far).wait()
    pltpu.make_async_copy(cx, cxs_ref.at[0], local_sems.at[3]).wait()
    keep.wait()


def front(wq, wk, wv, wo_part, wr, g1, g2, x, table, routes, cot, cap, n):
    tokens, width = x.shape
    shard = wq.shape[0]
    hbm, vmem = pl.BlockSpec(memory_space=pl.ANY), pl.BlockSpec(memory_space=pltpu.VMEM)
    dma = lambda k: pltpu.SemaphoreType.DMA((k,))
    shaped = lambda shape, dtype=BF16: jax.ShapeDtypeStruct(shape, dtype)
    cx_shape = (tokens + EXPERTS, width)
    packed = (2 * 16 * (shard // 32 + 1), n * PACK)
    return pl.pallas_call(
        functools.partial(front_kernel, n, cap),
        in_specs=[vmem, vmem, vmem, hbm, vmem, vmem, vmem, vmem, hbm, vmem, vmem],
        out_specs=[hbm, vmem, hbm, hbm, hbm, hbm, vmem],
        out_shape=[
            shaped((n, tokens, PACK)),
            shaped((tokens, width)),
            shaped((4,) + packed),
            shaped((4,) + wo_part.shape),
            shaped((4, shard, 128)),
            shaped((2,) + cx_shape),
            shaped((16, width), F32),
        ],
        scratch_shapes=[
            pltpu.VMEM((4,) + packed, BF16),
            pltpu.VMEM(packed, BF16),
            pltpu.VMEM((shard, 128), BF16),
            pltpu.VMEM(cx_shape, BF16),
            pltpu.VMEM((2, tokens // 2, 256), F32),
            pltpu.VMEM((tokens, width), F32),
            pltpu.VMEM((tokens, n * PACK), F32),
            pltpu.VMEM((n, tokens, PACK), BF16),
            dma(n - 1),
            dma(n - 1),
            dma(3),
            dma(3),
        ]
        + [dma(4)] * 8
        + [dma(1), dma(1), dma(8)],
        compiler_params=params(collective_id=1, has_side_effects=True),
        cost_estimate=cost(2e9, 5e7),
        name="front",
    )(wq, wk, wv, wo_part, wr, g1, g2, x, table, routes, cot)


def attend_kernel(length, n, ends_ref, q_ref, pack_ref, cxs_ref, out_ref, lse_ref, full_ref, rest_ref, keys, values_t, acc, near_send, near_recv, core_send, core_recv):
    block = pl.program_id(0)
    core, group = neighbours()
    near = group[1]

    def to_near(i):
        return send(cxs_ref.at[i], rest_ref.at[i], near_send.at[i], near_recv.at[i], near)

    def to_core(i):
        src = cxs_ref.at[i] if i < 2 else rest_ref.at[i - 2]
        return send(src, rest_ref.at[2 + i], core_send.at[i], core_recv.at[i], core)

    @pl.when(block == 0)
    def _():
        greet([core, near])
        for i in range(2):
            to_near(i).start()
        for i in range(2):
            to_core(i).start()

    attn_forward_kernel(length, ends_ref, q_ref, pack_ref, out_ref, lse_ref, full_ref, keys, values_t, acc)

    @pl.when(block == pl.num_programs(0) - 2)
    def _():
        to_near(0).wait_recv()
        to_core(2).start()

    @pl.when(block == pl.num_programs(0) - 1)
    def _():
        to_near(1).wait_recv()
        to_core(3).start()
        for i in range(4):
            to_core(i).wait()
        for i in range(2):
            to_near(i).wait_send()


def attend(ends, packs, cxs, length):
    n, _, rows, _ = packs.shape
    blocks, per = length // BLK, BLK // rows
    per_half = blocks // 2
    tiles = lambda i: (lax.rem(i, per_half), i // per_half, 0, 0)
    hbm = pl.BlockSpec(memory_space=pl.ANY)
    dma = lambda k: pltpu.SemaphoreType.DMA((k,))
    return pl.pallas_call(
        functools.partial(attend_kernel, length, n),
        grid=(blocks,),
        in_specs=[
            pl.BlockSpec(memory_space=pltpu.SMEM),
            pl.BlockSpec((per, 1, rows, PACK), tiles),
            pl.BlockSpec(packs.shape, lambda i: (0, 0, 0, 0)),
            hbm,
        ],
        out_specs=[
            pl.BlockSpec((per, 1, rows, 128), tiles),
            pl.BlockSpec((1, 1, 2 * BLK), lambda i: (i, 0, 0)),
            pl.BlockSpec((1, 128, 2 * BLK), lambda i: (i, 0, 0)),
            hbm,
        ],
        scratch_shapes=[
            pltpu.VMEM((length, 128), BF16),
            pltpu.VMEM((128, length), BF16),
            pltpu.VMEM((128, 2 * BLK), F32),
            dma(2),
            dma(2),
            dma(4),
            dma(4),
        ],
        out_shape=[
            jax.ShapeDtypeStruct((n, 2, rows, 128), BF16),
            jax.ShapeDtypeStruct((blocks, 1, 2 * BLK), F32),
            jax.ShapeDtypeStruct((blocks, 128, 2 * BLK), F32),
            jax.ShapeDtypeStruct((6,) + cxs.shape[1:], BF16),
        ],
        compiler_params=params(collective_id=3, has_side_effects=True),
        cost_estimate=cost(1.5e10, 2e7),
        name="attend",
    )(ends, packs, packs, cxs)


def mid_kernel(n, number, capp, attn_ref, cxs_ref, rest_ref, wo_ref, wr_ref, x_ref, gain_ref, middle_ref, h_ref, kept_ref, xs_ref, gs_ref, gates_ref, arrived, hs, total, exch_send, exch_recv, hop_send, hop_recv, fwd_send, fwd_recv, local_sems):
    tokens, width = x_ref.shape
    ctx, fsdp = lax.axis_index("ctx"), lax.axis_index("fsdp")
    first = (fsdp * 2 + lax.rem(ctx, 2)) * number
    core, group = neighbours()
    greet([core, group[0], group[2]] + [{"ctx": c} for c in others(n)])
    exchange = (attn_ref, arrived, exch_send, exch_recv, local_sems.at[0], n)
    exchange_start(*exchange)
    total[...] = jnp.zeros_like(total)

    def take(c):
        total[...] += dot(arrived[c], wo_ref[c])

    exchange_wait(*exchange, take)
    keep = pltpu.make_async_copy(arrived, kept_ref, local_sems.at[1])
    keep.start()
    middle = x_ref[...] + RESIDUAL * total[...]
    middle_ref[...] = middle
    normed, _ = norm_parts(middle)
    h = (normed * gain_ref[...]).astype(BF16)
    h_ref[...] = h
    hs[0] = h

    def hop(i):
        return send(hs.at[0], hs.at[1 + i], hop_send.at[i], hop_recv.at[i], (group + [core])[i])

    def forward(i):
        return send(hs.at[1 + i], hs.at[5 + i], fwd_send.at[i], fwd_recv.at[i], core)

    for i in (2, 0, 1, 3):
        hop(i).start()

    def place(b):
        h = hs[b]
        cx = (cxs_ref.at[b] if b < 2 else rest_ref.at[cx_slot[b]])
        logits = jnp.transpose(dot(h, wr_ref[...]))[:EXPERTS, :]
        raw = jnp.exp(logits - jnp.max(logits, 0, keepdims=True))
        router = raw / jnp.sum(raw, 0, keepdims=True)
        slots = cx[tokens:, :tokens].astype(F32)
        hots = one_hot(slots, first, number, capp)
        places = jnp.concatenate(hots, 0).astype(BF16)
        rows = dot(places, h).astype(BF16)
        grads = dot(places, cx[:tokens, :]).astype(BF16)
        for j in range(number):
            at = slice(j * capp, (j + 1) * capp)
            xs_ref[j, b] = rows[at]
            gs_ref[j, b] = grads[at]
            gate = jnp.sum(hots[j] * own_row(router, first + j), 1, keepdims=True)
            gates_ref[j, b] = jnp.broadcast_to(gate, (capp, 128))

    cx_slot = {2: 0, 3: 1, 4: 2, 5: 3, 6: 4, 7: 5}
    place(0)
    hop(3).wait_recv()
    place(4)
    for i in (0, 1, 2):
        hop(i).wait_recv()
        forward(i).start()
        place(1 + i)
    for i in (0, 1, 2):
        forward(i).wait_recv()
        place(5 + i)
    for i in range(4):
        hop(i).wait_send()
    for i in range(3):
        forward(i).wait_send()
    keep.wait()


def mid_step(attn, cxs, rest, wo, wr, x, gain, number, capp, n):
    tokens, width = x.shape
    hbm, vmem = pl.BlockSpec(memory_space=pl.ANY), pl.BlockSpec(memory_space=pltpu.VMEM)
    dma = lambda k: pltpu.SemaphoreType.DMA((k,))
    shaped = lambda shape, dtype=BF16: jax.ShapeDtypeStruct(shape, dtype)
    return pl.pallas_call(
        functools.partial(mid_kernel, n, number, capp),
        in_specs=[hbm, vmem, vmem, vmem, vmem, vmem, vmem],
        out_specs=[vmem, vmem, hbm, vmem, vmem, vmem],
        out_shape=[
            shaped((tokens, width), F32),
            shaped((tokens, width)),
            shaped(attn.shape),
            shaped((number, 8, capp, width)),
            shaped((number, 8, capp, width)),
            shaped((number, 8, capp, 128), F32),
        ],
        scratch_shapes=[
            pltpu.VMEM(attn.shape, BF16),
            pltpu.VMEM((8, tokens, width), BF16),
            pltpu.VMEM((tokens, width), F32),
            dma(n - 1),
            dma(n - 1),
            dma(4),
            dma(4),
            dma(3),
            dma(3),
            dma(2),
        ],
        compiler_params=params(collective_id=2, has_side_effects=True),
        cost_estimate=cost(4e9, 5e7),
        name="mid_step",
    )(attn, cxs, rest, wo, wr, x, gain)


RING = 8
ORDER_X, ORDER_Y, ORDER_CORE = 1, 2, 4


class GroupSum:
    def __init__(self, part, land, land_x, land_y, own, sems, core, group):
        self.part, self.land, self.land_x, self.land_y, self.own = part, land, land_x, land_y, own
        self.core_send, self.core_recv, self.x_send, self.x_recv, self.y_send, self.y_recv, self.load = sems
        self.core, self.far, self.near = core, group[0], group[1]

    def to_core(self, i):
        return send(self.part.at[4 + i], self.land.at[i], self.core_send.at[i], self.core_recv.at[i], self.core)

    def to_far(self, k):
        return send(self.land.at[1 + 2 * k], self.land_x.at[k], self.x_send.at[k], self.x_recv.at[k], self.far)

    def to_near(self):
        return send(self.land.at[2], self.land_y, self.y_send.at[0], self.y_recv.at[0], self.near)

    def fetch(self, i):
        return pltpu.make_async_copy(self.part.at[i], self.own.at[i % 2], self.load.at[i % 2])

    def start(self):
        for i in (1, 3, 2, 0):
            self.to_core(i).start()

    def over_cores(self):
        order = (1, 3, 2, 0)
        if self.own is not None:
            self.fetch(1).start()
        for step, i in enumerate(order):
            if self.own is None:
                mine = self.part[i]
            else:
                self.fetch(i).wait()
                mine = self.own[i % 2]
            self.to_core(i).wait_recv()
            self.land[i] = (self.land[i].astype(F32) + mine.astype(F32)).astype(BF16)
            if self.own is not None and step < 3:
                self.fetch(order[step + 1]).start()
            if i % 2 == 1:
                self.to_far(i // 2).start()

    def over_x(self):
        for k in (1, 0):
            self.to_far(k).wait_recv()
            self.land[2 * k] = (self.land[2 * k].astype(F32) + self.land_x[k].astype(F32)).astype(BF16)
            if k == 1:
                self.to_near().start()

    def finish(self):
        self.to_near().wait_recv()
        for i in range(4):
            self.to_core(i).wait_send()
        for k in range(2):
            self.to_far(k).wait_send()
        self.to_near().wait_send()
        return self.land[0].astype(F32) + self.land_y[...].astype(F32)


class LineSum:
    def __init__(self, count, own_ref, other_ref, inbox, across, mine, sems):
        self.count, self.own_ref, self.other_ref = count, own_ref, other_ref
        self.inbox, self.across, self.mine = inbox, across, mine
        self.line_send, self.line_recv, self.mid_send, self.mid_recv, self.side_send, self.side_recv, self.store, self.load = sems
        ctx = lax.axis_index("ctx")
        z = ctx // 2
        self.middle = (z == 1) | (z == 2)
        self.line = {"ctx": jnp.where(z % 2 == 0, ctx + 2, ctx - 2)}
        self.peer = {"ctx": jnp.where(z == 1, ctx + 2, ctx - 2)}
        self.side = {"ctx": flip(ctx, 1)}

    def send_line(self, src, i):
        s = lax.rem(i, RING)
        return send(src, self.inbox.at[s], self.line_send.at[s], self.line_recv.at[s], self.line)

    def send_mid(self, i):
        s = lax.rem(i, RING)
        return send(self.inbox.at[s], self.across.at[s], self.mid_send.at[s], self.mid_recv.at[s], self.peer)

    def send_side(self, src, i):
        return send(src, self.other_ref.at[i], self.side_send.at[lax.rem(i, RING)], self.side_recv.at[i], self.side)

    def keep(self, src, i):
        return pltpu.make_async_copy(src, self.own_ref.at[i], self.store.at[lax.rem(i, RING)])

    def fetch(self, src, i):
        s = lax.rem(i, 2)
        return pltpu.make_async_copy(src, self.mine.at[s], self.load.at[s])

    def drain_middle(self, i):
        src = self.across.at[lax.rem(i, RING)]
        self.send_line(src, i).wait_send()
        self.send_side(src, i).wait_send()
        self.keep(src, i).wait()

    def drain_end(self, i):
        src = self.inbox.at[lax.rem(i, RING)]
        self.send_side(src, i).wait_send()
        self.keep(src, i).wait()

    def tick(self, t, source):
        count = self.count
        fixed = isinstance(t, int)

        def when(condition):
            if fixed:
                return (lambda f: f()) if condition else (lambda f: None)
            return pl.when(condition)

        i32 = (lambda v: jnp.int32(v)) if fixed else (lambda v: v)

        @pl.when(self.middle)
        def _():
            @when((t >= 1) & (t <= count))
            def _():
                i = i32(t - 1)

                @when(t >= 7)
                def _():
                    self.drain_middle(i32(t - 7))

                s = lax.rem(i, RING)
                self.fetch(self.own_ref.at[i], i).wait()
                self.send_line(self.inbox.at[s], i).wait_recv()
                self.inbox[s] = self.inbox[s] + self.mine[lax.rem(i, 2)]
                self.send_mid(i).start()

            @when(t < count)
            def _():
                self.fetch(source(t), i32(t)).start()

            @when((t >= 2) & (t <= count + 1))
            def _():
                i = i32(t - 2)
                s = lax.rem(i, RING)
                self.send_mid(i).wait()
                self.across[s] = self.across[s] + self.inbox[s]
                self.send_line(self.across.at[s], i).start()
                self.send_side(self.across.at[s], i).start()
                self.keep(self.across.at[s], i).start()

        @pl.when(jnp.logical_not(self.middle))
        def _():
            @when(t < count)
            def _():
                @when(t >= 8)
                def _():
                    self.drain_end(i32(t - 8))

                @when(t >= 2)
                def _():
                    self.send_line(self.mine.at[0], i32(t - 2)).wait_send()

                self.send_line(source(t), i32(t)).start()

            @when(t >= 4)
            def _():
                i = i32(t - 4)
                s = lax.rem(i, RING)
                self.send_line(self.inbox.at[s], i).wait_recv()
                self.send_side(self.inbox.at[s], i).start()
                self.keep(self.inbox.at[s], i).start()

    def finish(self):
        count = self.count

        @pl.when(self.middle)
        def _():
            for i in range(count - 6, count):
                self.drain_middle(jnp.int32(i))

        @pl.when(jnp.logical_not(self.middle))
        def _():
            for i in range(count - 2, count):
                self.send_line(self.mine.at[0], jnp.int32(i)).wait_send()
            for i in range(count - 8, count):
                self.drain_end(jnp.int32(i))

        def arrived(i, carry):
            self.send_side(self.mine.at[0], i).wait_recv()
            return carry

        lax.fori_loop(0, count, arrived, 0)


def backward_kernel(
    n,
    length,
    ends_ref,
    pieces_ref,
    gx_ref,
    yp_ref,
    full_ref,
    weights_ref,
    packs_hbm,
    table_hbm,
    h_ref,
    middle_ref,
    cot_ref,
    wr_ref,
    wo_ref,
    gains_ref,
    attn_ref,
    lse_ref,
    x_ref,
    h_attn_ref,
    own_ref,
    other_ref,
    grad_x_ref,
    mixed_ref,
    inbox,
    across,
    mine,
    gx_land,
    gx_x,
    gx_y,
    gx_own,
    y_land,
    y_x,
    y_y,
    y_own,
    small,
    s_land,
    s_x,
    s_y,
    packs,
    table,
    keys,
    values,
    keys_t,
    grad_q,
    grad_k,
    grad_v,
    acc,
    full_buf,
    ga,
    ga_in,
    pack_out,
    grads_in,
    wbuf,
    total,
    grad_middle,
    dgain,
    col,
    line_send,
    line_recv,
    mid_send,
    mid_recv,
    side_send,
    side_recv,
    line_store,
    line_load,
    ga_send,
    ga_recv,
    gr_send,
    gr_recv,
    rs_sems,
    local_sems,
    full_sems,
    w_sems,
):
    tokens, width = h_ref.shape
    half = length // 2
    rows = tokens // 2
    shard = width // 4
    blocks = length // BLK
    ctx, fsdp = lax.axis_index("ctx"), lax.axis_index("fsdp")
    core, group = neighbours()
    experts = pieces_ref.shape[0]
    line = LineSum(experts + 2, own_ref, other_ref, inbox, across, mine, (line_send, line_recv, mid_send, mid_recv, side_send, side_recv, line_store, line_load))
    source = lambda t: pieces_ref.at[t]
    tick = lambda t: line.tick(t, source)
    sems = lambda k: [rs_sems.at[k, j] for j in range(7)]
    gx = GroupSum(gx_ref, gx_land, gx_x, gx_y, gx_own, sems(0), core, group)
    ys = GroupSum(yp_ref, y_land, y_x, y_y, y_own, sems(1), core, group)
    ws = GroupSum(small, s_land, s_x, s_y, None, sems(2), core, group)

    greet([core, group[0], group[2]] + [{"ctx": c} for c in others(n)])
    gx.start()
    load_packs = pltpu.make_async_copy(packs_hbm, packs, local_sems.at[0])
    load_table = pltpu.make_async_copy(table_hbm, table, local_sems.at[1])
    load_packs.start()
    load_table.start()
    small[:, PIECE // 2 : PIECE, :] = jnp.zeros((8, PIECE // 2, PIECE), BF16)

    def strip(r):
        f = fsdp
        if r & ORDER_X:
            f = flip(f, 2)
        if r & ORDER_CORE:
            f = flip(f, 1)
        y = lax.rem(ctx, 2)
        return 2 * f + (1 - y if r & ORDER_Y else y)

    tick(0)
    gx.over_cores()
    tick(1)
    gx.over_x()
    tick(2)
    arrived = gx.finish()
    ys.start()

    h = h_ref[...]
    gain = gains_ref[1:2]
    extra = arrived[tokens:, :]
    grad_router = extra[:, :tokens] + extra[:, tokens : 2 * tokens]
    grad_router = jnp.transpose(jnp.concatenate([grad_router, jnp.zeros((128 - EXPERTS, tokens), F32)], 0))
    logits = dot(h, wr_ref[...])
    logits = jnp.where(lane_iota(logits.shape) < EXPERTS, logits, MASKED)
    raw = jnp.exp(logits - jnp.max(logits, -1, keepdims=True))
    router = raw / jnp.sum(raw, -1, keepdims=True)
    grad_logits = (router * (grad_router - jnp.sum(router * grad_router, -1, keepdims=True))).astype(BF16)
    grad_h = arrived[:tokens, :] + dot(grad_logits, wr_ref[...], NT)
    normed, scale = norm_parts(middle_ref[...])
    dgain[1:2, :] = jnp.sum(grad_h * normed, 0, keepdims=True)
    grad_mid = cot_ref[...] + norm_back(grad_h * gain, normed, scale)
    grad_middle[...] = grad_mid
    grad_branch = (RESIDUAL * grad_mid).astype(BF16)
    for c in range(n):
        ga[c] = dot(grad_branch, wo_ref[c], NT).astype(BF16)
    ga_exchange = (ga, ga_in, ga_send, ga_recv, local_sems.at[2], n)
    exchange_start(*ga_exchange)
    tick(3)
    col[:, :128] = dot(h, grad_logits, TN).astype(BF16)
    for r in range(8):
        at = strip(r)
        dwo = dot(attn_ref[at], grad_branch, TN).astype(BF16)
        small[r, 0:128, :] = dwo[:, :PIECE]
        small[r, 128:256, :] = dwo[:, PIECE:]
        small[r, 256:384, 0:128] = col[pl.ds(pl.multiple_of(at * 128, 128), 128), 0:128]
    load_packs.wait()
    for hh in range(2):
        for c in range(n):
            kk, vv = pair_keys(packs[c, hh, :, 128:256].astype(F32))
            at = hh * half + c * rows
            keys[at : at + rows, :] = kk.astype(BF16)
            values[at : at + rows, :] = vv.astype(BF16)
            keys_t[:, at : at + rows] = jnp.transpose(kk).astype(BF16)
    grad_k[...] = jnp.zeros_like(grad_k)
    grad_v[...] = jnp.zeros_like(grad_v)
    ys.over_cores()
    tick(4)
    exchange_wait(*ga_exchange)

    per = BLK // rows
    per_half = blocks // 2

    def fetch_full(b):
        return pltpu.make_async_copy(full_ref.at[b], full_buf.at[lax.rem(b, 2)], full_sems.at[lax.rem(b, 2)])

    fetch_full(jnp.int32(0)).start()

    def attend(block, carry):
        late = block // per_half
        c0 = lax.rem(block, per_half) * per
        q2 = stack_heads(jnp.concatenate([packs[c0 + k, late, :, :128] for k in range(per)], 0))
        g2 = stack_heads(jnp.concatenate([ga_in[c0 + k, pl.ds(pl.multiple_of(late * rows, rows), rows), :] for k in range(per)], 0))
        position, start = query_rows(ends_ref, block, length)
        lse = lse_ref[block]

        @pl.when(block + 1 < blocks)
        def _():
            fetch_full(block + 1).start()

        fetch_full(block).wait()
        delta = jnp.sum(jnp.transpose(g2.astype(F32)) * full_buf[lax.rem(block, 2)], 0, keepdims=True)
        acc[...] = jnp.zeros_like(acc)

        def body(kb, carry):
            at = pl.multiple_of(kb * BLK, BLK)
            scores = dot(keys[pl.ds(at, BLK), :], q2, NT) * ATTN_SCALE
            where = key_position(kb, length)
            probs = jnp.where((where <= position) & (where >= start), jnp.exp(scores - lse), 0.0)
            grad_probs = dot(values[pl.ds(at, BLK), :], g2, NT)
            grad_scores = (probs * (grad_probs - delta)).astype(BF16)
            acc[...] += dot(keys_t[:, pl.ds(at, BLK)], grad_scores)
            grad_k[pl.ds(at, BLK), :] += dot(grad_scores, q2)
            grad_v[pl.ds(at, BLK), :] += dot(probs.astype(BF16), g2)
            return carry

        block_loop(block, per_half, body, 0)
        grad_q[pl.ds(pl.multiple_of(block * BLK, BLK), BLK), :] = fold_heads(jnp.transpose(acc[...]))

        @pl.when(lax.rem(block, 2) == 1)
        def _():
            tick(5 + block // 2)

        return carry

    lax.fori_loop(0, blocks, attend, 0)
    load_table.wait()
    for c in range(n):
        for hh in range(2):
            at = slice(hh * half + c * rows, hh * half + (c + 1) * rows)
            kk = grad_k[at, :]
            vv = grad_v[at, :]
            kk = (kk + pltpu.roll(kk, 64, 1)) * ATTN_SCALE
            vv = vv + pltpu.roll(vv, 64, 1)
            both = jnp.where(lane_iota(kk.shape) < 64, kk, vv)
            package = jnp.concatenate([grad_q[at, :] * ATTN_SCALE, both], -1)
            pack_out[c, hh * rows : (hh + 1) * rows, :] = turn(package, table[at, :], -1.0).astype(BF16)
    gr_exchange = (pack_out, grads_in, gr_send, gr_recv, local_sems.at[3], n)
    exchange_start(*gr_exchange)

    def fetch_w(c):
        slot = lax.rem(c, 2)
        return pltpu.make_async_copy(weights_ref.at[:, :, pl.ds(pl.multiple_of(c * PACK, PACK), PACK)], wbuf.at[slot], w_sems.at[slot])

    fetch_w(jnp.int32(0)).start()
    ys.over_x()
    tick(9)
    total[...] = jnp.zeros_like(total)
    mixed_ref[...] = middle_ref[...] + RESIDUAL * ys.finish()
    tick(10)
    exchange_wait(*gr_exchange)

    def finish_columns(c, carry):
        @pl.when(c + 1 < n)
        def _():
            fetch_w(c + 1).start()

        fetch_w(c).wait()
        slot = lax.rem(c, 2)
        g = grads_in[c]
        col[...] = dot(h_attn_ref[...], g, TN).astype(BF16)
        for r in range(8):
            at = pl.ds(pl.multiple_of(strip(r) * 128, 128), 128)
            small[r, pl.ds(pl.multiple_of(PIECE + c // 2 * 128, 128), 128), pl.ds(pl.multiple_of(lax.rem(c, 2) * PACK, PACK), PACK)] = col[at, :]
        for f in range(4):
            total[:, f * shard : (f + 1) * shard] += dot(g, wbuf[slot, f, :shard, :], NT)

        @pl.when(lax.rem(c, 4) == 3)
        def _():
            tick(11 + c // 4)

        return carry

    lax.fori_loop(0, n, finish_columns, 0)
    normed, scale = norm_parts(x_ref[...])
    grad_h = total[...]
    dgain[0:1, :] = jnp.sum(grad_h * normed, 0, keepdims=True)
    grad_x_ref[...] = grad_middle[...] + norm_back(grad_h * gains_ref[0:1], normed, scale)
    for r in range(8):
        at = pl.ds(pl.multiple_of(strip(r) * 128, 128), 128)
        row = row_iota((16, 128))
        both = jnp.where(row == 0, dgain[0:1, at], jnp.where(row == 1, dgain[1:2, at], 0.0))
        small[r, 384:400, 0:128] = both.astype(BF16)
    ws.start()
    tick(13)
    ws.over_cores()
    tick(14)
    ws.over_x()
    tick(15)
    tick(16)
    s_land[0] = ws.finish().astype(BF16)

    def rest(t, carry):
        tick(t)
        return carry

    lax.fori_loop(17, experts, rest, 0)
    late_source = lambda t: s_land.at[0, pl.ds((t - experts) * PIECE, PIECE)]
    for t in range(experts, experts + 6):
        line.tick(t, late_source)
    line.finish()


def backward_step(ends, pieces, gx, yp, full, weights, packs, table, h, middle, cot, wr, wo, gains, attn, lse, x, h_attn, n, length):
    tokens, width = x.shape
    hbm, vmem = pl.BlockSpec(memory_space=pl.ANY), pl.BlockSpec(memory_space=pltpu.VMEM)
    smem = pl.BlockSpec(memory_space=pltpu.SMEM)
    dma = lambda *k: pltpu.SemaphoreType.DMA(k)
    shaped = lambda shape, dtype=BF16: jax.ShapeDtypeStruct(shape, dtype)
    count = pieces.shape[0] + 2
    piece = (PIECE, PIECE)
    gx_shape, y_shape, s_shape = gx.shape[1:], yp.shape[1:], (2 * PIECE, PIECE)
    return pl.pallas_call(
        functools.partial(backward_kernel, n, length),
        in_specs=[smem] + [hbm] * 7 + [vmem] * 10,
        out_specs=[hbm, hbm, vmem, vmem],
        out_shape=[
            shaped((count,) + piece),
            shaped((count,) + piece),
            shaped((tokens, width), F32),
            shaped((tokens, width), F32),
        ],
        scratch_shapes=[
            pltpu.VMEM((RING,) + piece, BF16),
            pltpu.VMEM((RING,) + piece, BF16),
            pltpu.VMEM((2,) + piece, BF16),
            pltpu.VMEM((4,) + gx_shape, BF16),
            pltpu.VMEM((2,) + gx_shape, BF16),
            pltpu.VMEM(gx_shape, BF16),
            pltpu.VMEM((2,) + gx_shape, BF16),
            pltpu.VMEM((4,) + y_shape, BF16),
            pltpu.VMEM((2,) + y_shape, BF16),
            pltpu.VMEM(y_shape, BF16),
            pltpu.VMEM((2,) + y_shape, BF16),
            pltpu.VMEM((8,) + s_shape, BF16),
            pltpu.VMEM((4,) + s_shape, BF16),
            pltpu.VMEM((2,) + s_shape, BF16),
            pltpu.VMEM(s_shape, BF16),
            pltpu.VMEM(packs.shape, BF16),
            pltpu.VMEM(table.shape, F32),
            pltpu.VMEM((length, 128), BF16),
            pltpu.VMEM((length, 128), BF16),
            pltpu.VMEM((128, length), BF16),
            pltpu.VMEM((length, 128), F32),
            pltpu.VMEM((length, 128), F32),
            pltpu.VMEM((length, 128), F32),
            pltpu.VMEM((128, 2 * BLK), F32),
            pltpu.VMEM((2, 128, 2 * BLK), F32),
            pltpu.VMEM((n, tokens, 128), BF16),
            pltpu.VMEM((n, tokens, 128), BF16),
            pltpu.VMEM((n, tokens, PACK), BF16),
            pltpu.VMEM((n, tokens, PACK), BF16),
            pltpu.VMEM((2, 4, weights.shape[1], PACK), BF16),
            pltpu.VMEM((tokens, width), F32),
            pltpu.VMEM((tokens, width), F32),
            pltpu.VMEM((8, width), F32),
            pltpu.VMEM((width, PACK), BF16),
            dma(RING),
            dma(RING),
            dma(RING),
            dma(RING),
            dma(RING),
            dma(count),
            dma(RING),
            dma(2),
            dma(n - 1),
            dma(n - 1),
            dma(n - 1),
            dma(n - 1),
            dma(3, 7, 4),
            dma(4),
            dma(2),
            dma(2),
        ],
        compiler_params=params(63, collective_id=0, has_side_effects=True),
        cost_estimate=cost(4e10, 1e9),
        name="backward_step",
    )(ends, pieces, gx, yp, full, weights, packs, table, h, middle, cot, wr, wo, gains, attn, lse, x, h_attn)


def local(
    inputs,
    cotangent,
    doc_lengths,
    routes,
    attn_gain,
    ffn_gain,
    w_query,
    key_weight,
    value_weight,
    w_out,
    w_router,
    w_gate,
    w_up,
    w_down,
):
    rows = inputs.shape[2]
    width = inputs.shape[3]
    n = lax.axis_size("ctx")
    fsdp = lax.axis_size("fsdp")
    me, mine = lax.axis_index("ctx"), lax.axis_index("fsdp")
    tokens = 2 * rows
    length = tokens * n
    experts_here = w_gate.shape[0]
    number = experts_here // 2
    capacity = 5 * tokens * TOP // (4 * EXPERTS)
    capp = -(-capacity // 16) * 16
    shard = width // fsdp
    heads = QUERY_HEADS // n
    head_lanes = heads * HEAD_DIMENSION
    copies = n // KEY_VALUE_HEADS
    bits = group_bits(fsdp)

    x = inputs.reshape(tokens, width)
    cot = cotangent.reshape(tokens, width)
    side = me % 2
    base = (side * number).astype(jnp.int32).reshape(1)
    first = (mine * experts_here + side * number).astype(jnp.int32).reshape(1)
    index = jnp.stack([side * number, (1 - side) * number]).astype(jnp.int32)
    ends = jnp.cumsum(doc_lengths[0])[:3].astype(jnp.int32)
    table = jnp.asarray(rotary_table(length))

    out_part = w_out.reshape(shard // head_lanes, head_lanes, width)
    if head_lanes < 128:
        out_part = jnp.pad(out_part, ((0, 0), (0, 128 - head_lanes), (0, 0)))
    merge = lambda a: a.reshape(number, -1, a.shape[-1])

    if n == 8 and fsdp == 4:
        packs, h_attn, weights, wo, wr, cxs, gains = front(
            w_query,
            key_weight,
            value_weight,
            out_part,
            w_router,
            attn_gain.reshape(1, shard),
            ffn_gain.reshape(1, shard),
            x,
            table.reshape(2, n, rows, 256),
            routes.reshape(tokens, TOP),
            cot,
            capacity,
            n,
        )
        wo, wr = wo.reshape(n, 128, width), wr.reshape(width, 128)
        packs = packs.reshape(n, 2, rows, PACK)
        attn, lse, full, cx_rest = attend(ends, packs, cxs, length)
        middle, h_ffn, attn, xs, gs, gates = mid_step(attn.reshape(n, tokens, 128), cxs, cx_rest, wo, wr, x, gains[1:2], number, capp, n)
        slots = jnp.concatenate([cxs[:, tokens:], cx_rest[:, tokens:]], 0)
    else:
        own_table = lax.dynamic_slice_in_dim(table.reshape(2, n, rows, 256), me, 1, 1).reshape(tokens, 256)
        query_part = w_query.reshape(shard, n, head_lanes)
        if head_lanes < 128:
            query_part = jnp.pad(query_part, ((0, 0), (0, 0), (0, 128 - head_lanes)))
        key_part = jnp.repeat(key_weight.reshape(shard, KEY_VALUE_HEADS, HEAD_DIMENSION), copies, 1)
        value_part = jnp.repeat(value_weight.reshape(shard, KEY_VALUE_HEADS, HEAD_DIMENSION), copies, 1)
        packed = jnp.concatenate([query_part, key_part, value_part], -1).reshape(shard, n * PACK)
        padding = 2 * 16 * (shard // 32 + 1) - shard
        gains = jnp.pad(jnp.stack([attn_gain, ffn_gain]), ((0, padding - 2), (0, n * PACK - shard)))
        packed = jnp.concatenate([packed, gains], 0)
        router_part = jnp.pad(w_router, ((0, 0), (0, 128 - EXPERTS)))
        weights = lax.all_gather(packed, "fsdp", axis=0)
        gain_one = weights[:, shard, :shard].reshape(1, width).astype(F32)
        gain_two = weights[:, shard + 1, :shard].reshape(1, width).astype(F32)
        wo = lax.all_gather(out_part, "fsdp", axis=0, tiled=True)
        wr = lax.all_gather(router_part, "fsdp", axis=0, tiled=True)
        cxs = group_gather(prep(routes.reshape(tokens, TOP), cot, capacity), bits)
        packs, h_attn = qkv(x, gain_one, weights, own_table, shard, n)
        packs = lax.all_to_all(packs, "ctx", split_axis=0, concat_axis=0, tiled=True).reshape(n, 2, rows, PACK)
        attn, lse, full = attn_forward(ends, packs, length)
        attn = lax.all_to_all(attn.reshape(n, tokens, 128), "ctx", split_axis=0, concat_axis=0, tiled=True)
        middle, h_ffn = middle_step(attn, wo, x, gain_two)
        xs, gs, gates = gather_rows(first, group_gather(h_ffn, bits), cxs, jnp.transpose(wr), number, capp)
        slots = cxs[:, tokens:]
    xs, gs, gates = merge(xs), merge(gs), merge(gates)
    pieces, outs, back, dgates = expert_step(base, xs, gs, gates, w_gate, w_up, w_down)
    y_part, gx_part = combine(first, slots, outs, back, dgates, tokens, capp)
    pieces = pieces.reshape(number * 6, PIECE, PIECE)
    if n == 8 and fsdp == 4:
        own, other, grad_x, mixed = backward_step(
            ends, pieces, gx_part, y_part, full, weights, packs, table, h_ffn, middle, cot, wr, wo, gains, attn, lse, x, h_attn, n, length
        )
        shapes = [w.shape for w in (w_gate, w_up, w_down)]
        outs = tail(index, own, other, mixed, grad_x, shapes, shard)
        return (
            outs[3].reshape(inputs.shape),
            outs[4].reshape(inputs.shape),
            outs[10].reshape(shard),
            outs[11].reshape(shard),
            outs[5],
            outs[6],
            outs[7],
            outs[8],
            outs[9],
            outs[0],
            outs[1],
            outs[2],
        )
    gx = group_reduce(gx_part, bits)
    grad_middle, dwo, grad_attn, dwr, dgain_two = home_step(gx, h_ffn, middle, cot, wr, wo, gain_two, attn)
    grad_attn = lax.all_to_all(grad_attn, "ctx", split_axis=0, concat_axis=0, tiled=True).reshape(n, 2, rows, 128)
    grads = attn_backward(ends, packs, grad_attn, lse, full, table, length)
    grads = lax.all_to_all(grads.reshape(n, tokens, PACK), "ctx", split_axis=0, concat_axis=0, tiled=True)
    dw, grad_x, dgain_one = final_step(grads, weights, h_attn, x, gain_one, grad_middle, shard)
    mixed = middle + RESIDUAL * group_reduce(y_part, bits).astype(F32)
    own = line_sum(pieces, n)
    other = swap(own, "ctx", 1)
    scatter = lambda a: lax.psum(lax.psum_scatter(a, "fsdp", scatter_dimension=0, tiled=True), "ctx").astype(F32)
    dwo = scatter(dwo)[:, :head_lanes, :].reshape(shard, width)
    small = jnp.concatenate([dwr[:, :EXPERTS], dgain_two.reshape(width, 1).astype(BF16)], 1)
    small = scatter(jnp.pad(small, ((0, 0), (0, 127 - EXPERTS))))
    dwr, dgain_two = small[:, :EXPERTS], small[:, EXPERTS]
    dw = scatter(dw).reshape(shard, n, PACK)
    dgain_one = scatter(dgain_one.reshape(width).astype(BF16))

    outs = widen(index, own, other, [w.shape for w in (w_gate, w_up, w_down)])
    fold = lambda a: a.reshape(shard, KEY_VALUE_HEADS, copies, HEAD_DIMENSION).sum(2).reshape(shard, -1)
    return (
        mixed.reshape(inputs.shape),
        grad_x.reshape(inputs.shape),
        dgain_one,
        dgain_two,
        dw[:, :, :head_lanes].reshape(shard, -1),
        fold(dw[:, :, 128:192]),
        fold(dw[:, :, 192:256]),
        dwo,
        dwr,
        outs[0],
        outs[1],
        outs[2],
    )


def solution(mesh):
    tokens = P("fsdp", None, "ctx", None)
    one, two, three = P("fsdp"), P("fsdp", None), P("fsdp", None, None)
    return jax.shard_map(
        local,
        mesh=mesh,
        in_specs=(tokens, tokens, two, tokens, one, one, two, two, two, two, two, three, three, three),
        out_specs=(tokens, tokens, one, one, two, two, two, two, two, three, three, three),
        check_vma=False,
    )
```

```python
import functools

import jax
import jax.numpy as jnp
import numpy as np
from jax import lax
from jax.experimental import pallas as pl
from jax.experimental.pallas import tpu as pltpu
from jax.sharding import PartitionSpec as P

QUERY_HEADS = 16
KEY_VALUE_HEADS = 8
HEAD_DIMENSION = 64
EXPERTS = 32
TOP = 8

ATTN_SCALE = 0.015625
RESIDUAL = 0.22
NORM_EPS = 1e-06
ROPE_BASE = 10000.0
MASKED = -1e30

F32 = jnp.float32
BF16 = jnp.bfloat16
MIB = 1 << 20
NT = (((1,), (1,)), ((), ()))
TN = (((0,), (0,)), ((), ()))
BLK = 256
PACK = 256


def dot(a, b, dims=None):
    if dims is None:
        return jnp.dot(a, b, preferred_element_type=F32)
    return lax.dot_general(a, b, dims, preferred_element_type=F32)


def params(limit=56, **kw):
    return pltpu.CompilerParams(vmem_limit_bytes=limit * MIB, **kw)


def cost(flops, bytes_accessed):
    return pl.CostEstimate(flops=int(flops), bytes_accessed=int(bytes_accessed), transcendentals=0)


def lane_iota(shape):
    return lax.broadcasted_iota(jnp.int32, shape, len(shape) - 1)


def row_iota(shape):
    return lax.broadcasted_iota(jnp.int32, shape, len(shape) - 2)


def rotary_table(length):
    half = length // 2
    order = np.arange(half, dtype=np.float32)
    positions = np.concatenate([order, length - 1 - order]).astype(np.float32)
    m = np.arange(HEAD_DIMENSION // 2, dtype=np.float64)
    frequency = (ROPE_BASE ** (-2.0 * m / HEAD_DIMENSION)).astype(np.float32)
    angles = (positions[:, None] * frequency[None, :]).astype(np.float64)
    cosine, sine = np.cos(angles), np.sin(angles)
    cos_head = np.concatenate([cosine, cosine], -1)
    sin_head = np.concatenate([-sine, sine], -1)
    return np.concatenate([cos_head, cos_head, sin_head, sin_head], -1).astype(np.float32)


def turn(v, table, direction):
    lanes = lane_iota(v.shape)
    cosine = jnp.concatenate([table[:, :128], table[:, :128]], -1)
    sine = jnp.concatenate([table[:, 128:], table[:, 128:]], -1)
    turned = lanes < 3 * HEAD_DIMENSION
    swapped = jnp.where(lanes % HEAD_DIMENSION < HEAD_DIMENSION // 2, pltpu.roll(v, PACK - 32, 1), pltpu.roll(v, 32, 1))
    return jnp.where(turned, v * cosine + direction * (swapped * sine), v)


def norm_parts(values):
    inv_rms = lax.rsqrt(jnp.mean(values * values, -1, keepdims=True) + NORM_EPS)
    return values * inv_rms, inv_rms


def norm_back(grad_normed, normed, inv_rms):
    return inv_rms * (grad_normed - normed * jnp.mean(grad_normed * normed, -1, keepdims=True))


def prep_kernel(cap, routes_ref, cot_ref, out_ref):
    tokens, width = cot_ref.shape
    routes = routes_ref[...]
    earlier = (lane_iota((tokens, tokens)) < row_iota((tokens, tokens))).astype(BF16)
    experts = lane_iota((tokens, 128))
    base = jnp.zeros((1, 128), F32)
    plus = jnp.zeros((tokens, 128), F32)
    for k in range(TOP):
        chosen = experts == routes[:, k : k + 1]
        ones = chosen.astype(F32)
        slot = dot(earlier, ones.astype(BF16)) + base
        plus = plus + jnp.where(chosen & (slot < cap), slot + 1.0, 0.0)
        base = base + jnp.sum(ones, 0, keepdims=True)
    out_ref[:tokens, :] = cot_ref[...].astype(BF16)
    slots = (jnp.transpose(plus) - 1.0)[:EXPERTS, :]
    out_ref[tokens:, :] = jnp.concatenate([slots, jnp.zeros((EXPERTS, width - tokens), F32)], -1).astype(BF16)


def prep(routes, cot, cap):
    tokens, width = cot.shape
    return pl.pallas_call(
        functools.partial(prep_kernel, cap),
        out_shape=jax.ShapeDtypeStruct((tokens + EXPERTS, width), BF16),
        compiler_params=params(),
        cost_estimate=cost(1e9, 2e6),
        name="prep",
    )(routes, cot)


def qkv_kernel(shard, x_ref, gain_ref, w_ref, table_ref, out_ref, h_ref):
    @pl.when(pl.program_id(0) == 0)
    def _():
        normed, _ = norm_parts(x_ref[...])
        h_ref[...] = (normed * gain_ref[...]).astype(BF16)

    total = None
    for f in range(w_ref.shape[0]):
        part = dot(h_ref[:, f * shard : (f + 1) * shard], w_ref[f, :shard, :])
        total = part if total is None else total + part
    for d in range(out_ref.shape[0]):
        out_ref[d] = turn(total[:, d * PACK : (d + 1) * PACK], table_ref[...], 1.0).astype(BF16)


def qkv(x, gain, weights, table, shard, n):
    tokens, width = x.shape
    fsdp, padded, _ = weights.shape
    return pl.pallas_call(
        functools.partial(qkv_kernel, shard),
        grid=(n // 2,),
        in_specs=[
            pl.BlockSpec((tokens, width), lambda i: (0, 0)),
            pl.BlockSpec((1, width), lambda i: (0, 0)),
            pl.BlockSpec((fsdp, padded, 2 * PACK), lambda i: (0, 0, i)),
            pl.BlockSpec((tokens, 256), lambda i: (0, 0)),
        ],
        out_specs=[
            pl.BlockSpec((2, tokens, PACK), lambda i: (i, 0, 0)),
            pl.BlockSpec((tokens, width), lambda i: (0, 0)),
        ],
        out_shape=[
            jax.ShapeDtypeStruct((n, tokens, PACK), BF16),
            jax.ShapeDtypeStruct((tokens, width), BF16),
        ],
        compiler_params=params(),
        cost_estimate=cost(2 * tokens * width * n * PACK, 8e6),
        name="qkv",
    )(x, gain, weights, table)


def pair_keys(kv):
    other = pltpu.roll(kv, 64, 1)
    low = lane_iota(kv.shape) < 64
    return jnp.where(low, kv, other), jnp.where(low, other, kv)


def stack_heads(q):
    low = lane_iota(q.shape) < 64
    zero = jnp.zeros_like(q)
    return jnp.concatenate([jnp.where(low, q, zero), jnp.where(low, zero, q)], 0)


def fold_heads(stacked):
    rows = stacked.shape[0] // 2
    return jnp.where(lane_iota((rows, 128)) < 64, stacked[:rows], stacked[rows:])


def query_rows(ends_ref, block, length):
    half = length // 2
    lanes = lane_iota((1, 2 * BLK))
    index = block * BLK + jnp.where(lanes < BLK, lanes, lanes - BLK)
    position = jnp.where(index < half, index, length + half - 1 - index)
    start = jnp.zeros_like(position)
    for j in range(3):
        end = ends_ref[j]
        start = jnp.where(position >= end, jnp.maximum(start, end), start)
    return position, start


def key_position(kb, length):
    half = length // 2
    index = kb * BLK + row_iota((BLK, 1))
    return jnp.where(index < half, index, length + half - 1 - index)


def block_loop(block, per_half, body, init):
    late = block >= per_half
    inner = jnp.where(late, block - per_half, block)
    count = jnp.where(late, 2 * per_half - inner, inner + 1)

    def step(j, carry):
        kb = jnp.where(late & (j >= per_half), inner + j, j)
        return body(kb, carry)

    return lax.fori_loop(0, count, step, init)


def load_package(pack_ref, c, h):
    return pack_ref[c, h].astype(F32)


def attn_forward_kernel(length, ends_ref, q_ref, pack_ref, out_ref, lse_ref, full_ref, keys, values_t, acc):
    block = pl.program_id(0)
    half = length // 2
    n, _, rows, _ = pack_ref.shape

    @pl.when(block == 0)
    def _():
        for h in range(2):
            for c in range(n):
                kk, vv = pair_keys(pack_ref[c, h, :, 128:256].astype(F32))
                at = h * half + c * rows
                keys[at : at + rows, :] = kk.astype(BF16)
                if rows % 128 == 0:
                    values_t[:, at : at + rows] = jnp.transpose(vv).astype(BF16)
        if rows % 128 != 0:
            for h in range(2):
                for c in range(0, n, 2):
                    pair = jnp.concatenate([pack_ref[c, h, :, 128:256], pack_ref[c + 1, h, :, 128:256]], 0)
                    _, vv = pair_keys(pair.astype(F32))
                    at = h * half + c * rows
                    values_t[:, at : at + 2 * rows] = jnp.transpose(vv).astype(BF16)

    q = q_ref[...].reshape(BLK, PACK)[:, :128]
    q2 = stack_heads(q)
    position, start = query_rows(ends_ref, block, length)
    acc[...] = jnp.zeros_like(acc)

    def body(kb, carry):
        peak, total = carry
        at = pl.multiple_of(kb * BLK, BLK)
        scores = dot(keys[pl.ds(at, BLK), :], q2, NT) * ATTN_SCALE
        where = key_position(kb, length)
        scores = jnp.where((where <= position) & (where >= start), scores, MASKED)
        new_peak = jnp.maximum(peak, jnp.max(scores, 0, keepdims=True))
        weights = jnp.exp(scores - new_peak)
        fade = jnp.exp(peak - new_peak)
        total = total * fade + jnp.sum(weights, 0, keepdims=True)
        acc[...] = acc[...] * fade + dot(values_t[:, pl.ds(at, BLK)], weights.astype(BF16))
        return new_peak, total

    init = (jnp.full((1, 2 * BLK), MASKED, F32), jnp.zeros((1, 2 * BLK), F32))
    peak, total = block_loop(block, half // BLK, body, init)
    result = acc[...] / total
    full_ref[0] = result
    lse_ref[0] = peak + jnp.log(total)
    folded = fold_heads(jnp.transpose(result)).astype(BF16)
    out_ref[...] = folded.reshape(out_ref.shape)


def attn_forward(ends, packs, length):
    n, _, rows, _ = packs.shape
    blocks, per = length // BLK, BLK // rows
    per_half = blocks // 2
    tiles = lambda i, ends: (lax.rem(i, per_half), i // per_half, 0, 0)
    return pl.pallas_call(
        functools.partial(attn_forward_kernel, length),
        grid_spec=pltpu.PrefetchScalarGridSpec(
            num_scalar_prefetch=1,
            grid=(blocks,),
            in_specs=[
                pl.BlockSpec((per, 1, rows, PACK), tiles),
                pl.BlockSpec(packs.shape, lambda i, ends: (0, 0, 0, 0)),
            ],
            out_specs=[
                pl.BlockSpec((per, 1, rows, 128), tiles),
                pl.BlockSpec((1, 1, 2 * BLK), lambda i, ends: (i, 0, 0)),
                pl.BlockSpec((1, 128, 2 * BLK), lambda i, ends: (i, 0, 0)),
            ],
            scratch_shapes=[
                pltpu.VMEM((length, 128), BF16),
                pltpu.VMEM((128, length), BF16),
                pltpu.VMEM((128, 2 * BLK), F32),
            ],
        ),
        out_shape=[
            jax.ShapeDtypeStruct((n, 2, rows, 128), BF16),
            jax.ShapeDtypeStruct((blocks, 1, 2 * BLK), F32),
            jax.ShapeDtypeStruct((blocks, 128, 2 * BLK), F32),
        ],
        compiler_params=params(),
        cost_estimate=cost(1.5e10, 6e6),
        name="attn_forward",
    )(ends, packs, packs)


def attn_backward_kernel(length, ends_ref, q_ref, g_ref, pack_ref, lse_ref, full_ref, table_ref, out_ref, keys, values, keys_t, grad_q, grad_k, grad_v, acc):
    block = pl.program_id(0)
    half = length // 2
    n, _, rows, _ = pack_ref.shape

    @pl.when(block == 0)
    def _():
        for h in range(2):
            for c in range(n):
                kk, vv = pair_keys(pack_ref[c, h, :, 128:256].astype(F32))
                at = h * half + c * rows
                keys[at : at + rows, :] = kk.astype(BF16)
                values[at : at + rows, :] = vv.astype(BF16)
        for b in range(length // BLK):
            keys_t[:, b * BLK : (b + 1) * BLK] = jnp.transpose(keys[b * BLK : (b + 1) * BLK, :].astype(F32)).astype(BF16)
        grad_k[...] = jnp.zeros_like(grad_k)
        grad_v[...] = jnp.zeros_like(grad_v)

    q2 = stack_heads(q_ref[...].reshape(BLK, PACK)[:, :128])
    g2 = stack_heads(g_ref[...].reshape(BLK, 128))
    position, start = query_rows(ends_ref, block, length)
    lse = lse_ref[0]
    delta = jnp.sum(jnp.transpose(g2.astype(F32)) * full_ref[0], 0, keepdims=True)
    acc[...] = jnp.zeros_like(acc)

    def body(kb, carry):
        at = pl.multiple_of(kb * BLK, BLK)
        scores = dot(keys[pl.ds(at, BLK), :], q2, NT) * ATTN_SCALE
        where = key_position(kb, length)
        probs = jnp.where((where <= position) & (where >= start), jnp.exp(scores - lse), 0.0)
        grad_probs = dot(values[pl.ds(at, BLK), :], g2, NT)
        grad_scores = (probs * (grad_probs - delta)).astype(BF16)
        acc[...] += dot(keys_t[:, pl.ds(at, BLK)], grad_scores)
        grad_k[pl.ds(at, BLK), :] += dot(grad_scores, q2)
        grad_v[pl.ds(at, BLK), :] += dot(probs.astype(BF16), g2)
        return carry

    block_loop(block, half // BLK, body, 0)
    grad_q[pl.ds(pl.multiple_of(block * BLK, BLK), BLK), :] = fold_heads(jnp.transpose(acc[...]))

    @pl.when(block == length // BLK - 1)
    def _():
        for h in range(2):
            for c in range(n):
                at = slice(h * half + c * rows, h * half + (c + 1) * rows)
                kk = grad_k[at, :]
                vv = grad_v[at, :]
                kk = (kk + pltpu.roll(kk, 64, 1)) * ATTN_SCALE
                vv = vv + pltpu.roll(vv, 64, 1)
                both = jnp.where(lane_iota(kk.shape) < 64, kk, vv)
                package = jnp.concatenate([grad_q[at, :] * ATTN_SCALE, both], -1)
                out_ref[c, h] = turn(package, table_ref[at, :], -1.0).astype(BF16)


def attn_backward(ends, packs, grads, lse, full, table, length):
    n, _, rows, _ = packs.shape
    blocks, per = length // BLK, BLK // rows
    per_half = blocks // 2
    tiles = lambda i, ends: (lax.rem(i, per_half), i // per_half, 0, 0)
    return pl.pallas_call(
        functools.partial(attn_backward_kernel, length),
        grid_spec=pltpu.PrefetchScalarGridSpec(
            num_scalar_prefetch=1,
            grid=(blocks,),
            in_specs=[
                pl.BlockSpec((per, 1, rows, PACK), tiles),
                pl.BlockSpec((per, 1, rows, 128), tiles),
                pl.BlockSpec(packs.shape, lambda i, ends: (0, 0, 0, 0)),
                pl.BlockSpec((1, 1, 2 * BLK), lambda i, ends: (i, 0, 0)),
                pl.BlockSpec((1, 128, 2 * BLK), lambda i, ends: (i, 0, 0)),
                pl.BlockSpec(table.shape, lambda i, ends: (0, 0)),
            ],
            out_specs=pl.BlockSpec(packs.shape, lambda i, ends: (0, 0, 0, 0)),
            scratch_shapes=[
                pltpu.VMEM((length, 128), BF16),
                pltpu.VMEM((length, 128), BF16),
                pltpu.VMEM((128, length), BF16),
                pltpu.VMEM((length, 128), F32),
                pltpu.VMEM((length, 128), F32),
                pltpu.VMEM((length, 128), F32),
                pltpu.VMEM((128, 2 * BLK), F32),
            ],
        ),
        out_shape=jax.ShapeDtypeStruct(packs.shape, BF16),
        compiler_params=params(),
        cost_estimate=cost(3e10, 8e6),
        name="attn_backward",
    )(ends, packs, grads, packs, lse, full, table)


def middle_kernel(attn_ref, wo_ref, x_ref, gain_ref, middle_ref, h_ref):
    total = None
    for c in range(attn_ref.shape[0]):
        part = dot(attn_ref[c], wo_ref[c])
        total = part if total is None else total + part
    middle = x_ref[...] + RESIDUAL * total
    middle_ref[...] = middle
    normed, _ = norm_parts(middle)
    h_ref[...] = (normed * gain_ref[...]).astype(BF16)


def middle_step(attn, wo, x, gain):
    tokens, width = x.shape
    return pl.pallas_call(
        middle_kernel,
        out_shape=[jax.ShapeDtypeStruct((tokens, width), F32), jax.ShapeDtypeStruct((tokens, width), BF16)],
        compiler_params=params(),
        cost_estimate=cost(2 * tokens * width * width, 5e6),
        name="middle",
    )(attn, wo, x, gain)


def own_row(table, row):
    return jnp.sum(jnp.where(row_iota(table.shape) == row, table, 0.0), 0, keepdims=True)


def one_hot(slots, first, number, capp):
    tokens = slots.shape[1]
    order = row_iota((capp, tokens)).astype(F32)
    return [(order == own_row(slots, first + j)).astype(F32) for j in range(number)]


def gather_kernel(number, capp, first_ref, h_ref, cx_ref, wrt_ref, x_ref, g_ref, gate_ref):
    tokens = h_ref.shape[1]
    first = first_ref[0]
    h = h_ref[0]
    slots = cx_ref[0, tokens:, :tokens].astype(F32)
    logits = dot(wrt_ref[...], h, NT)[:EXPERTS, :]
    raw = jnp.exp(logits - jnp.max(logits, 0, keepdims=True))
    router = raw / jnp.sum(raw, 0, keepdims=True)
    hots = one_hot(slots, first, number, capp)
    places = jnp.concatenate(hots, 0).astype(BF16)
    rows = dot(places, h).astype(BF16)
    grads = dot(places, cx_ref[0, :tokens, :]).astype(BF16)
    for j in range(number):
        at = slice(j * capp, (j + 1) * capp)
        x_ref[j, 0] = rows[at]
        g_ref[j, 0] = grads[at]
        gate = jnp.sum(hots[j] * own_row(router, first + j), 1, keepdims=True)
        gate_ref[j, 0] = jnp.broadcast_to(gate, (capp, 128))


def gather_rows(first, hs, cxs, wrt, number, capp):
    nb, tokens, width = hs.shape
    return pl.pallas_call(
        functools.partial(gather_kernel, number, capp),
        grid_spec=pltpu.PrefetchScalarGridSpec(
            num_scalar_prefetch=1,
            grid=(nb,),
            in_specs=[
                pl.BlockSpec((1, tokens, width), lambda b, f: (b, 0, 0)),
                pl.BlockSpec((1, tokens + EXPERTS, width), lambda b, f: (b, 0, 0)),
                pl.BlockSpec(wrt.shape, lambda b, f: (0, 0)),
            ],
            out_specs=[
                pl.BlockSpec((number, 1, capp, width), lambda b, f: (0, b, 0, 0)),
                pl.BlockSpec((number, 1, capp, width), lambda b, f: (0, b, 0, 0)),
                pl.BlockSpec((number, 1, capp, 128), lambda b, f: (0, b, 0, 0)),
            ],
        ),
        out_shape=[
            jax.ShapeDtypeStruct((number, nb, capp, width), BF16),
            jax.ShapeDtypeStruct((number, nb, capp, width), BF16),
            jax.ShapeDtypeStruct((number, nb, capp, 128), F32),
        ],
        compiler_params=params(),
        cost_estimate=cost(4 * nb * number * capp * tokens * width, 2e7),
        name="gather_rows",
    )(first, hs, cxs, wrt)


PIECE = 512


def expert_kernel(base_ref, x_ref, g_ref, gate_ref, wg_ref, wu_ref, wd_ref, piece_ref, out_ref, rows_ref, dg_ref):
    x = x_ref[0]
    gate = gate_ref[0][:, :1]
    grad_ffn = RESIDUAL * g_ref[0].astype(F32)
    go = (gate * grad_ffn).astype(BF16)
    part = wg_ref.shape[2] // 2
    out = rows = None
    for chunk in range(2):
        at = slice(chunk * part, (chunk + 1) * part)
        wg, wu, wd = wg_ref[0, :, at], wu_ref[0, :, at], wd_ref[0, at, :]
        pre_gate = dot(x, wg)
        pre_up = dot(x, wu)
        sig = jax.nn.sigmoid(pre_gate)
        hidden = (pre_gate * sig * pre_up).astype(BF16)
        out_part = dot(hidden, wd)
        grad_hidden = dot(go, wd, NT)
        grad_gate = (grad_hidden * pre_up * sig * (1.0 + pre_gate * (1.0 - sig))).astype(BF16)
        grad_up = (grad_hidden * pre_gate * sig).astype(BF16)
        row_part = dot(grad_gate, wg, NT) + dot(grad_up, wu, NT)
        dwg = dot(x, grad_gate, TN).astype(BF16)
        dwu = dot(x, grad_up, TN).astype(BF16)
        dwd = dot(hidden, go, TN).astype(BF16)
        for half in range(2):
            side = slice(half * PIECE, (half + 1) * PIECE)
            piece_ref[0, half, :, at] = dwg[side]
            piece_ref[0, 2 + half, :, at] = dwu[side]
            piece_ref[0, 4 + half, at, :] = dwd[:, side]
        out = out_part if out is None else out + out_part
        rows = row_part if rows is None else rows + row_part
    out = out.astype(BF16).astype(F32)
    out_ref[0] = (gate * out).astype(BF16)
    rows_ref[0] = rows.astype(BF16)
    grad = jnp.sum(grad_ffn * out, 1, keepdims=True)
    dg_ref[0] = jnp.broadcast_to(grad, dg_ref.shape[1:])


def expert_step(base, xs, gs, gates, w_gate, w_up, w_down):
    number, rows, width = xs.shape
    ff = w_gate.shape[2]
    row = lambda e, b: (e, 0, 0)
    weight = lambda e, b: (b[0] + e, 0, 0)
    return pl.pallas_call(
        expert_kernel,
        grid_spec=pltpu.PrefetchScalarGridSpec(
            num_scalar_prefetch=1,
            grid=(number,),
            in_specs=[
                pl.BlockSpec((1, rows, width), row),
                pl.BlockSpec((1, rows, width), row),
                pl.BlockSpec((1, rows, 128), row),
                pl.BlockSpec((1, width, ff), weight),
                pl.BlockSpec((1, width, ff), weight),
                pl.BlockSpec((1, ff, width), weight),
            ],
            out_specs=[
                pl.BlockSpec((1, 6, PIECE, PIECE), lambda e, b: (e, 0, 0, 0)),
                pl.BlockSpec((1, rows, width), row),
                pl.BlockSpec((1, rows, width), row),
                pl.BlockSpec((1, rows, 128), row),
            ],
        ),
        out_shape=[
            jax.ShapeDtypeStruct((number, 6, PIECE, PIECE), BF16),
            jax.ShapeDtypeStruct((number, rows, width), BF16),
            jax.ShapeDtypeStruct((number, rows, width), BF16),
            jax.ShapeDtypeStruct((number, rows, 128), F32),
        ],
        compiler_params=params(60),
        cost_estimate=cost(18 * number * rows * width * ff, 5e7),
        name="expert_step",
    )(base, xs, gs, gates, w_gate, w_up, w_down)


def combine_kernel(number, capp, first_ref, slot_ref, outs, rows, grads, y_ref, gx_ref):
    tokens = y_ref.shape[1]
    width = y_ref.shape[2]
    first = first_ref[0]
    slots = slot_ref[0][:, :tokens].astype(F32)
    hots = one_hot(slots, first, number, capp)
    places = jnp.concatenate(hots, 0).astype(BF16)
    y_ref[0] = dot(places, outs[:, 0].reshape(number * capp, width), TN).astype(BF16)
    gx_ref[0, :tokens] = dot(places, rows[:, 0].reshape(number * capp, width), TN).astype(BF16)
    extra = jnp.zeros((EXPERTS, 2 * tokens), F32)
    for j in range(number):
        grad = jnp.sum(hots[j] * grads[j, 0][:, :1], 0, keepdims=True)
        high = grad.astype(BF16).astype(F32)
        both = jnp.concatenate([high, grad - high], 1)
        extra = jnp.where(row_iota(extra.shape) == first + j, both, extra)
    rest = jnp.zeros((EXPERTS, width - 2 * tokens), F32)
    gx_ref[0, tokens:] = jnp.concatenate([extra, rest], 1).astype(BF16)


def combine(first, slots, outs, rows, grads, tokens, capp):
    number = outs.shape[0]
    nb, _, width = slots.shape
    split = lambda a: a.reshape(number, nb, capp, a.shape[-1])
    wide = pl.BlockSpec((number, 1, capp, width), lambda b, f: (0, b, 0, 0))
    thin = pl.BlockSpec((number, 1, capp, 128), lambda b, f: (0, b, 0, 0))
    return pl.pallas_call(
        functools.partial(combine_kernel, number, capp),
        grid_spec=pltpu.PrefetchScalarGridSpec(
            num_scalar_prefetch=1,
            grid=(nb,),
            in_specs=[pl.BlockSpec((1, EXPERTS, width), lambda b, f: (b, 0, 0))] + [wide, wide, thin],
            out_specs=[
                pl.BlockSpec((1, tokens, width), lambda b, f: (b, 0, 0)),
                pl.BlockSpec((1, tokens + EXPERTS, width), lambda b, f: (b, 0, 0)),
            ],
        ),
        out_shape=[
            jax.ShapeDtypeStruct((nb, tokens, width), BF16),
            jax.ShapeDtypeStruct((nb, tokens + EXPERTS, width), BF16),
        ],
        compiler_params=params(),
        cost_estimate=cost(4 * nb * number * capp * tokens * width, 2e7),
        name="combine",
    )(first, slots, split(outs), split(rows), split(grads))


def home_kernel(gx_ref, h_ref, middle_ref, cot_ref, wr_ref, wo_ref, gain_ref, attn_ref, grad_middle_ref, dwo_ref, ga_ref, dwr_ref, dgain_ref):
    tokens, width = h_ref.shape
    h = h_ref[...]
    gain = gain_ref[...]
    extra = gx_ref[tokens:, :].astype(F32)
    grad_router = extra[:, :tokens] + extra[:, tokens : 2 * tokens]
    grad_router = jnp.transpose(jnp.concatenate([grad_router, jnp.zeros((128 - EXPERTS, tokens), F32)], 0))
    logits = dot(h, wr_ref[...])
    logits = jnp.where(lane_iota(logits.shape) < EXPERTS, logits, MASKED)
    raw = jnp.exp(logits - jnp.max(logits, -1, keepdims=True))
    router = raw / jnp.sum(raw, -1, keepdims=True)
    grad_logits = (router * (grad_router - jnp.sum(router * grad_router, -1, keepdims=True))).astype(BF16)
    dwr_ref[...] = dot(h, grad_logits, TN).astype(BF16)
    grad_h = gx_ref[:tokens, :].astype(F32) + dot(grad_logits, wr_ref[...], NT)
    normed, scale = norm_parts(middle_ref[...])
    dgain_ref[...] = jnp.sum(grad_h * normed, 0, keepdims=True)
    grad_middle = cot_ref[...] + norm_back(grad_h * gain, normed, scale)
    grad_middle_ref[...] = grad_middle
    grad_branch = (RESIDUAL * grad_middle).astype(BF16)
    for c in range(attn_ref.shape[0]):
        dwo_ref[c] = dot(attn_ref[c], grad_branch, TN).astype(BF16)
        ga_ref[c] = dot(grad_branch, wo_ref[c], NT).astype(BF16)


def home_step(gx, h, middle, cot, wr, wo, gain, attn):
    tokens, width = h.shape
    n = attn.shape[0]
    return pl.pallas_call(
        home_kernel,
        out_shape=[
            jax.ShapeDtypeStruct((tokens, width), F32),
            jax.ShapeDtypeStruct((n, 128, width), BF16),
            jax.ShapeDtypeStruct((n, tokens, 128), BF16),
            jax.ShapeDtypeStruct((width, 128), BF16),
            jax.ShapeDtypeStruct((1, width), F32),
        ],
        compiler_params=params(),
        cost_estimate=cost(4 * tokens * width * width, 1e7),
        name="home_step",
    )(gx, h, middle, cot, wr, wo, gain, attn)


def final_kernel(shard, grads_ref, w_ref, h_ref, x_ref, gain_ref, grad_middle_ref, dw_ref, grad_x_ref, dgain_ref, total):
    c = pl.program_id(0)
    g = grads_ref[0]
    dw_ref[...] = dot(h_ref[...], g, TN).astype(BF16)

    @pl.when(c == 0)
    def _():
        total[...] = jnp.zeros_like(total)

    for f in range(w_ref.shape[0]):
        total[:, f * shard : (f + 1) * shard] += dot(g, w_ref[f, :shard, :], NT)

    @pl.when(c == pl.num_programs(0) - 1)
    def _():
        normed, scale = norm_parts(x_ref[...])
        grad_h = total[...]
        dgain_ref[...] = jnp.sum(grad_h * normed, 0, keepdims=True)
        grad_x_ref[...] = grad_middle_ref[...] + norm_back(grad_h * gain_ref[...], normed, scale)


def final_step(grads, weights, h, x, gain, grad_middle, shard):
    n, tokens, _ = grads.shape
    width = x.shape[1]
    fsdp, padded, _ = weights.shape
    same = lambda c: (0, 0)
    return pl.pallas_call(
        functools.partial(final_kernel, shard),
        grid=(n,),
        in_specs=[
            pl.BlockSpec((1, tokens, PACK), lambda c: (c, 0, 0)),
            pl.BlockSpec((fsdp, padded, PACK), lambda c: (0, 0, c)),
            pl.BlockSpec((tokens, width), same),
            pl.BlockSpec((tokens, width), same),
            pl.BlockSpec((1, width), same),
            pl.BlockSpec((tokens, width), same),
        ],
        out_specs=[
            pl.BlockSpec((width, PACK), lambda c: (0, c)),
            pl.BlockSpec((tokens, width), same),
            pl.BlockSpec((1, width), same),
        ],
        out_shape=[
            jax.ShapeDtypeStruct((width, n * PACK), BF16),
            jax.ShapeDtypeStruct((tokens, width), F32),
            jax.ShapeDtypeStruct((1, width), F32),
        ],
        scratch_shapes=[pltpu.VMEM((tokens, width), F32)],
        compiler_params=params(),
        cost_estimate=cost(4 * tokens * width * n * PACK, 1.2e7),
        name="final_step",
    )(grads, weights, h, x, gain, grad_middle)


def widen_kernel(number, index_ref, own_ref, other_ref, gate_ref, up_ref, down_ref):
    def write(ref):
        for half in range(2):
            at = slice(half * PIECE, (half + 1) * PIECE)
            gate_ref[0, at, :] = ref[half].astype(F32)
            up_ref[0, at, :] = ref[2 + half].astype(F32)
            down_ref[0, :, at] = ref[4 + half].astype(F32)

    @pl.when(pl.program_id(0) == 0)
    def _():
        write(own_ref)

    @pl.when(pl.program_id(0) == 1)
    def _():
        write(other_ref)


def tail_kernel(number, index_ref, own_ref, other_ref, own_small_ref, other_small_ref, mixed_in, grad_in, gate_ref, up_ref, down_ref, mixed_ref, grad_ref, dwq_ref, dwk_ref, dwv_ref, dwo_ref, dwr_ref, g1_ref, g2_ref):
    widen_kernel(number, index_ref, own_ref, other_ref, gate_ref, up_ref, down_ref)
    mixed_ref[...] = mixed_in[...]
    grad_ref[...] = grad_in[...]

    @pl.when((pl.program_id(0) == 0) & (pl.program_id(1) == 0))
    def _():
        for which, ref in enumerate((own_small_ref, other_small_ref)):
            part = index_ref[which] // number
            at = pl.ds(pl.multiple_of(part * 128, 128), 128)
            for q in range(4):
                block = ref[1, q * 128 : (q + 1) * 128, :].astype(F32)
                dwq_ref[at, q * 256 : q * 256 + 128] = block[:, :128]
                dwq_ref[at, q * 256 + 128 : (q + 1) * 256] = block[:, 256:384]
                one, two = block[:, 128:256], block[:, 384:]
                low = lane_iota(one.shape) < HEAD_DIMENSION
                dwk_ref[at, q * 128 : (q + 1) * 128] = jnp.where(low, one, pltpu.roll(two, 64, 1))
                dwv_ref[at, q * 128 : (q + 1) * 128] = jnp.where(low, pltpu.roll(one, 64, 1), two)
            dwo_ref[at, :PIECE] = ref[0, 0:128, :].astype(F32)
            dwo_ref[at, PIECE:] = ref[0, 128:256, :].astype(F32)
            dwr_ref[at, :] = ref[0, 256:384, :EXPERTS].astype(F32)
            gains = ref[0, 384:400, :128].astype(F32)
            g1_ref[pl.ds(part, 1), :] = gains[0:1]
            g2_ref[pl.ds(part, 1), :] = gains[1:2]


def expert_specs(number, shapes):
    last = number - 1
    ins = [
        pl.BlockSpec((6, PIECE, PIECE), lambda s, e, at: (jnp.where(s == 0, e, last), 0, 0)),
        pl.BlockSpec((6, PIECE, PIECE), lambda s, e, at: (jnp.where(s == 0, 0, e), 0, 0)),
    ]
    outs = [pl.BlockSpec((1,) + tuple(shape[1:]), lambda s, e, at: (at[s] + e, 0, 0)) for shape in shapes]
    return ins, outs, [jax.ShapeDtypeStruct(shape, F32) for shape in shapes]


def widen(index, own, other, shapes):
    number = shapes[0][0] // 2
    ins, outs, out_shapes = expert_specs(number, shapes)
    return pl.pallas_call(
        functools.partial(widen_kernel, number),
        grid_spec=pltpu.PrefetchScalarGridSpec(num_scalar_prefetch=1, grid=(2, number), in_specs=ins, out_specs=outs),
        out_shape=out_shapes,
        compiler_params=params(),
        cost_estimate=cost(0, 1e8),
        name="widen",
    )(index, own, other)


def tail(index, own, other, mixed, grad_x, shapes, shard):
    number = shapes[0][0] // 2
    tokens, width = mixed.shape
    ins, outs, out_shapes = expert_specs(number, shapes)
    small = pl.BlockSpec((2, PIECE, PIECE), lambda s, e, at: (3 * number, 0, 0))
    rows = pl.BlockSpec((tokens // (2 * number), width), lambda s, e, at: (s * number + e, 0))
    small_shapes = [(shard, width), (shard, width // 2), (shard, width // 2), (shard, width), (shard, EXPERTS), (2, 128), (2, 128)]
    whole = [pl.BlockSpec(shape, lambda s, e, at: (0, 0)) for shape in small_shapes]
    return pl.pallas_call(
        functools.partial(tail_kernel, number),
        grid_spec=pltpu.PrefetchScalarGridSpec(
            num_scalar_prefetch=1,
            grid=(2, number),
            in_specs=ins + [small, small, rows, rows],
            out_specs=outs + [rows, rows] + whole,
        ),
        out_shape=out_shapes
        + [jax.ShapeDtypeStruct((tokens, width), F32)] * 2
        + [jax.ShapeDtypeStruct(shape, F32) for shape in small_shapes],
        compiler_params=params(),
        cost_estimate=cost(0, 1e8),
        name="tail",
    )(index, own, other, own, other, mixed, grad_x)


def swap(value, axis, bit):
    size = lax.axis_size(axis)
    return lax.ppermute(value, axis, [(i, i ^ bit) for i in range(size)])


def group_bits(fsdp):
    bits = [("fsdp", 1 << b) for b in range(1, fsdp.bit_length() - 1)]
    return bits + [("ctx", 1), ("fsdp", 1)]


def group_gather(value, bits):
    stacked = value[None]
    for axis, bit in bits:
        stacked = jnp.concatenate([stacked, swap(stacked, axis, bit)], 0)
    return stacked


def group_reduce(stacked, bits):
    for axis, bit in reversed(bits):
        half = stacked.shape[0] // 2
        arrived = swap(stacked[half:], axis, bit)
        stacked = (stacked[:half].astype(F32) + arrived.astype(F32)).astype(stacked.dtype)
    return stacked[0]


def line_sum(value, ctx):
    pairs = ctx // 2
    if pairs != 4:
        bit = 2
        while bit < ctx:
            value = value + swap(value, "ctx", bit)
            bit *= 2
        return value
    at = lambda z, y: 2 * z + y
    inward = [(at(0, y), at(1, y)) for y in range(2)] + [(at(3, y), at(2, y)) for y in range(2)]
    across = [(at(1, y), at(2, y)) for y in range(2)] + [(at(2, y), at(1, y)) for y in range(2)]
    outward = [(b, a) for a, b in inward]
    value = value + lax.ppermute(value, "ctx", inward)
    value = value + lax.ppermute(value, "ctx", across)
    arrived = lax.ppermute(value, "ctx", outward)
    z = lax.axis_index("ctx") // 2
    return jnp.where((z == 0) | (z == 3), arrived, value)


MESH = pl.DeviceIdType.MESH


def flip(index, bit):
    return jnp.where((index // bit) % 2 == 0, index + bit, index - bit)


def send(src, dst, send_sem, recv_sem, device):
    return pltpu.make_async_remote_copy(src_ref=src, dst_ref=dst, send_sem=send_sem, recv_sem=recv_sem, device_id=device, device_id_type=MESH)


def neighbours():
    ctx, fsdp = lax.axis_index("ctx"), lax.axis_index("fsdp")
    side, across = flip(ctx, 1), flip(fsdp, 2)
    core = {"fsdp": flip(fsdp, 1)}
    return core, [{"fsdp": across}, {"ctx": side}, {"ctx": side, "fsdp": across}]


def greet(devices):
    barrier = pltpu.get_barrier_semaphore()
    for device in devices:
        pl.semaphore_signal(barrier, inc=1, device_id=device, device_id_type=MESH)
    pl.semaphore_wait(barrier, len(devices))


def others(n):
    ctx = lax.axis_index("ctx")
    return [lax.rem(ctx + d, n) for d in range(1, n)]


def exchange_start(src, dst, send_sems, recv_sems, local_sem, n):
    ctx = lax.axis_index("ctx")
    for d, c in enumerate(others(n)):
        send(src.at[c], dst.at[ctx], send_sems.at[d], recv_sems.at[d], {"ctx": c}).start()
    pltpu.make_async_copy(src.at[ctx], dst.at[ctx], local_sem).start()


def exchange_wait(src, dst, send_sems, recv_sems, local_sem, n, arrived=None):
    ctx = lax.axis_index("ctx")
    pltpu.make_async_copy(src.at[ctx], dst.at[ctx], local_sem).wait()
    if arrived is not None:
        arrived(ctx)
    for d in range(n - 1):
        source = lax.rem(ctx + n - 1 - d, n)
        send(src.at[source], dst.at[source], send_sems.at[d], recv_sems.at[d], {"ctx": source}).wait_recv()
        if arrived is not None:
            arrived(source)
    for d, c in enumerate(others(n)):
        send(src.at[c], dst.at[ctx], send_sems.at[d], recv_sems.at[d], {"ctx": c}).wait_send()


def front_kernel(n, cap, wq_ref, wk_ref, wv_ref, wo_part_ref, wr_raw_ref, g1_ref, g2_ref, x_ref, table_ref, routes_ref, cot_ref, packs_ref, h_ref, weights_ref, wo_ref, wr_ref, cxs_ref, gains_ref, wall, packed_ref, wr_part_ref, cx, table, normed_ref, total, out, exch_send, exch_recv, full_send, full_recv, x_send, x_recv, y_send, y_recv, xs_send, xs_recv, ys_send, ys_recv, cx_send, cx_recv, local_sems):
    width = x_ref.shape[1]
    shard = width // 4
    ctx, fsdp = lax.axis_index("ctx"), lax.axis_index("fsdp")
    parity = lax.rem(ctx, 2)
    core, group = neighbours()
    far, near = group[0], group[1]
    sibling, distant = flip(fsdp, 1), flip(fsdp, 2)
    other = flip(distant, 1)
    for k in range(2):
        pltpu.make_async_copy(table_ref.at[k, ctx], table.at[k], local_sems.at[6 + k]).start()

    pair = HEAD_DIMENSION * 2
    for c in range(0, n, 2):
        for k in range(2):
            packed_ref[:shard, (c + k) * PACK : (c + k) * PACK + 128] = wq_ref[:, (c + k) * 128 : (c + k + 1) * 128]
        keys, values = wk_ref[:, c // 2 * pair : (c // 2 + 1) * pair].astype(F32), wv_ref[:, c // 2 * pair : (c // 2 + 1) * pair].astype(F32)
        low = lane_iota(keys.shape) < HEAD_DIMENSION
        packed_ref[:shard, c * PACK + 128 : (c + 1) * PACK] = jnp.where(low, keys, pltpu.roll(values, 64, 1)).astype(BF16)
        packed_ref[:shard, (c + 1) * PACK + 128 : (c + 2) * PACK] = jnp.where(low, pltpu.roll(keys, 64, 1), values).astype(BF16)
    row = row_iota((16, shard))
    gain_rows = jnp.where(row == 0, g1_ref[...].astype(F32), jnp.where(row == 1, g2_ref[...].astype(F32), 0.0))
    packed_ref[shard:, :] = jnp.zeros((packed_ref.shape[0] - shard, n * PACK), BF16)
    packed_ref[shard : shard + 16, :shard] = gain_rows.astype(BF16)
    wr_part_ref[...] = jnp.concatenate([wr_raw_ref[...].astype(F32), jnp.zeros((shard, 128 - EXPERTS), F32)], 1).astype(BF16)
    greet([core, far] + [{"ctx": c} for c in others(n)])

    half_rows = packed_ref.shape[0] // 2
    low_rows = half_rows // 32 * 16

    def cut(k, part):
        if k == 0:
            return pl.ds(pl.multiple_of(part * half_rows, 16), low_rows)
        if k == 1:
            return pl.ds(pl.multiple_of(part * half_rows + low_rows, 16), half_rows - low_rows)
        if k == 2:
            return pl.ds(part, 1)
        return pl.ds(pl.multiple_of(part * (shard // 2), 16), shard // 2)

    sources = [packed_ref, packed_ref, wo_part_ref, wr_part_ref]
    targets = [wall, wall, wo_ref, wr_ref]
    wholes = [(packed_ref, wall), (wo_part_ref, wo_ref), (wr_part_ref, wr_ref)]

    def whole(i):
        src, dst = wholes[i]
        return send(src, dst.at[fsdp], full_send.at[i], full_recv.at[i], core)

    def own(i):
        src, dst = wholes[i]
        return pltpu.make_async_copy(src, dst.at[fsdp], local_sems.at[i])

    def to_far(k):
        return send(sources[k].at[cut(k, parity)], targets[k].at[fsdp, cut(k, parity)], x_send.at[k], x_recv.at[k], far)

    def pass_on(k, part, sems, device):
        ref = targets[k].at[distant, cut(k, part)]
        return send(ref, ref, sems[0].at[k], sems[1].at[k], device)

    def far_arrived(k):
        ref = targets[k].at[distant, cut(k, parity)]
        send(ref, ref, x_send.at[k], x_recv.at[k], far).wait_recv()
        pass_on(k, parity, (y_send, y_recv), near).start()
        pass_on(k, parity, (xs_send, xs_recv), core).start()

    def near_arrived(k):
        pass_on(k, 1 - parity, (y_send, y_recv), near).wait_recv()
        pass_on(k, 1 - parity, (ys_send, ys_recv), core).start()

    def core_arrived(k):
        for part, sems in ((parity, (xs_send, xs_recv)), (1 - parity, (ys_send, ys_recv))):
            ref = targets[k].at[other, cut(k, part)]
            send(ref, ref, sems[0].at[k], sems[1].at[k], core).wait_recv()

    own(0).start()
    to_far(0).start()
    to_far(1).start()
    whole(0).start()

    prep_kernel(cap, routes_ref, cot_ref, cx)
    pltpu.make_async_copy(cx, cxs_ref.at[0], local_sems.at[3]).start()
    normed, _ = norm_parts(x_ref[...])
    normed_ref[...] = normed

    def project(block, begin):
        at = pl.ds(pl.multiple_of(block * shard, shard), shard)
        gain = wall[block, shard : shard + 16, :shard].astype(F32)
        gains_ref[:, at] = gain
        h = (normed_ref[:, at] * gain[:1]).astype(BF16)
        h_ref[:, at] = h
        part = dot(h, wall[block, :shard, :])
        total[...] = part if begin else total[...] + part

    own(0).wait()
    project(fsdp, True)
    ref = wall.at[sibling]
    send(ref, ref, full_send.at[0], full_recv.at[0], core).wait_recv()
    project(sibling, False)
    far_arrived(0)
    far_arrived(1)
    for i in (1, 2):
        own(i).start()
        whole(i).start()
        to_far(i + 1).start()
    send(cx, cxs_ref.at[1], cx_send.at[0], cx_recv.at[0], far).start()
    near_arrived(0)
    near_arrived(1)
    project(distant, False)
    core_arrived(0)
    core_arrived(1)
    project(other, False)
    keep = pltpu.make_async_copy(wall, weights_ref, local_sems.at[4])
    keep.start()
    for k in range(2):
        pltpu.make_async_copy(table_ref.at[k, ctx], table.at[k], local_sems.at[6 + k]).wait()
    angles = table[...].reshape(x_ref.shape[0], 256)
    for c in range(n):
        out[c] = turn(total[:, c * PACK : (c + 1) * PACK], angles, 1.0).astype(BF16)
    exchange = (out, packs_ref, exch_send, exch_recv, local_sems.at[5], n)
    exchange_start(*exchange)

    for k in (2, 3):
        far_arrived(k)
    for k in (2, 3):
        near_arrived(k)
    for k in (2, 3):
        core_arrived(k)
    for i in (1, 2):
        src, dst = wholes[i]
        ref = dst.at[sibling]
        send(ref, ref, full_send.at[i], full_recv.at[i], core).wait_recv()
        own(i).wait()
    exchange_wait(*exchange)
    for i in range(3):
        whole(i).wait_send()
    for k in range(4):
        to_far(k).wait_send()
        pass_on(k, parity, (y_send, y_recv), near).wait_send()
        pass_on(k, parity, (xs_send, xs_recv), core).wait_send()
        pass_on(k, 1 - parity, (ys_send, ys_recv), core).wait_send()
    send(cx, cxs_ref.at[1], cx_send.at[0], cx_recv.at[0], far).wait()
    pltpu.make_async_copy(cx, cxs_ref.at[0], local_sems.at[3]).wait()
    keep.wait()


def front(wq, wk, wv, wo_part, wr, g1, g2, x, table, routes, cot, cap, n):
    tokens, width = x.shape
    shard = wq.shape[0]
    hbm, vmem = pl.BlockSpec(memory_space=pl.ANY), pl.BlockSpec(memory_space=pltpu.VMEM)
    dma = lambda k: pltpu.SemaphoreType.DMA((k,))
    shaped = lambda shape, dtype=BF16: jax.ShapeDtypeStruct(shape, dtype)
    cx_shape = (tokens + EXPERTS, width)
    packed = (2 * 16 * (shard // 32 + 1), n * PACK)
    return pl.pallas_call(
        functools.partial(front_kernel, n, cap),
        in_specs=[vmem, vmem, vmem, hbm, vmem, vmem, vmem, vmem, hbm, vmem, vmem],
        out_specs=[hbm, vmem, hbm, hbm, hbm, hbm, vmem],
        out_shape=[
            shaped((n, tokens, PACK)),
            shaped((tokens, width)),
            shaped((4,) + packed),
            shaped((4,) + wo_part.shape),
            shaped((4, shard, 128)),
            shaped((2,) + cx_shape),
            shaped((16, width), F32),
        ],
        scratch_shapes=[
            pltpu.VMEM((4,) + packed, BF16),
            pltpu.VMEM(packed, BF16),
            pltpu.VMEM((shard, 128), BF16),
            pltpu.VMEM(cx_shape, BF16),
            pltpu.VMEM((2, tokens // 2, 256), F32),
            pltpu.VMEM((tokens, width), F32),
            pltpu.VMEM((tokens, n * PACK), F32),
            pltpu.VMEM((n, tokens, PACK), BF16),
            dma(n - 1),
            dma(n - 1),
            dma(3),
            dma(3),
        ]
        + [dma(4)] * 8
        + [dma(1), dma(1), dma(8)],
        compiler_params=params(collective_id=1, has_side_effects=True),
        cost_estimate=cost(2e9, 5e7),
        name="front",
    )(wq, wk, wv, wo_part, wr, g1, g2, x, table, routes, cot)


def attend_kernel(length, n, ends_ref, q_ref, pack_ref, cxs_ref, out_ref, lse_ref, full_ref, rest_ref, keys, values_t, acc, near_send, near_recv, core_send, core_recv):
    block = pl.program_id(0)
    core, group = neighbours()
    near = group[1]

    def to_near(i):
        return send(cxs_ref.at[i], rest_ref.at[i], near_send.at[i], near_recv.at[i], near)

    def to_core(i):
        src = cxs_ref.at[i] if i < 2 else rest_ref.at[i - 2]
        return send(src, rest_ref.at[2 + i], core_send.at[i], core_recv.at[i], core)

    @pl.when(block == 0)
    def _():
        greet([core, near])
        for i in range(2):
            to_near(i).start()
        for i in range(2):
            to_core(i).start()

    attn_forward_kernel(length, ends_ref, q_ref, pack_ref, out_ref, lse_ref, full_ref, keys, values_t, acc)

    @pl.when(block == pl.num_programs(0) - 2)
    def _():
        to_near(0).wait_recv()
        to_core(2).start()

    @pl.when(block == pl.num_programs(0) - 1)
    def _():
        to_near(1).wait_recv()
        to_core(3).start()
        for i in range(4):
            to_core(i).wait()
        for i in range(2):
            to_near(i).wait_send()


def attend(ends, packs, cxs, length):
    n, _, rows, _ = packs.shape
    blocks, per = length // BLK, BLK // rows
    per_half = blocks // 2
    tiles = lambda i: (lax.rem(i, per_half), i // per_half, 0, 0)
    hbm = pl.BlockSpec(memory_space=pl.ANY)
    dma = lambda k: pltpu.SemaphoreType.DMA((k,))
    return pl.pallas_call(
        functools.partial(attend_kernel, length, n),
        grid=(blocks,),
        in_specs=[
            pl.BlockSpec(memory_space=pltpu.SMEM),
            pl.BlockSpec((per, 1, rows, PACK), tiles),
            pl.BlockSpec(packs.shape, lambda i: (0, 0, 0, 0)),
            hbm,
        ],
        out_specs=[
            pl.BlockSpec((per, 1, rows, 128), tiles),
            pl.BlockSpec((1, 1, 2 * BLK), lambda i: (i, 0, 0)),
            pl.BlockSpec((1, 128, 2 * BLK), lambda i: (i, 0, 0)),
            hbm,
        ],
        scratch_shapes=[
            pltpu.VMEM((length, 128), BF16),
            pltpu.VMEM((128, length), BF16),
            pltpu.VMEM((128, 2 * BLK), F32),
            dma(2),
            dma(2),
            dma(4),
            dma(4),
        ],
        out_shape=[
            jax.ShapeDtypeStruct((n, 2, rows, 128), BF16),
            jax.ShapeDtypeStruct((blocks, 1, 2 * BLK), F32),
            jax.ShapeDtypeStruct((blocks, 128, 2 * BLK), F32),
            jax.ShapeDtypeStruct((6,) + cxs.shape[1:], BF16),
        ],
        compiler_params=params(collective_id=3, has_side_effects=True),
        cost_estimate=cost(1.5e10, 2e7),
        name="attend",
    )(ends, packs, packs, cxs)


def mid_kernel(n, number, capp, attn_ref, cxs_ref, rest_ref, wo_ref, wr_ref, x_ref, gain_ref, middle_ref, h_ref, kept_ref, xs_ref, gs_ref, gates_ref, arrived, hs, total, exch_send, exch_recv, hop_send, hop_recv, fwd_send, fwd_recv, local_sems):
    tokens, width = x_ref.shape
    ctx, fsdp = lax.axis_index("ctx"), lax.axis_index("fsdp")
    first = (fsdp * 2 + lax.rem(ctx, 2)) * number
    core, group = neighbours()
    greet([core, group[0], group[2]] + [{"ctx": c} for c in others(n)])
    exchange = (attn_ref, arrived, exch_send, exch_recv, local_sems.at[0], n)
    exchange_start(*exchange)
    total[...] = jnp.zeros_like(total)

    def take(c):
        total[...] += dot(arrived[c], wo_ref[c])

    exchange_wait(*exchange, take)
    keep = pltpu.make_async_copy(arrived, kept_ref, local_sems.at[1])
    keep.start()
    middle = x_ref[...] + RESIDUAL * total[...]
    middle_ref[...] = middle
    normed, _ = norm_parts(middle)
    h = (normed * gain_ref[...]).astype(BF16)
    h_ref[...] = h
    hs[0] = h

    def hop(i):
        return send(hs.at[0], hs.at[1 + i], hop_send.at[i], hop_recv.at[i], (group + [core])[i])

    def forward(i):
        return send(hs.at[1 + i], hs.at[5 + i], fwd_send.at[i], fwd_recv.at[i], core)

    for i in (2, 0, 1, 3):
        hop(i).start()

    def place(b):
        h = hs[b]
        cx = (cxs_ref.at[b] if b < 2 else rest_ref.at[cx_slot[b]])
        logits = jnp.transpose(dot(h, wr_ref[...]))[:EXPERTS, :]
        raw = jnp.exp(logits - jnp.max(logits, 0, keepdims=True))
        router = raw / jnp.sum(raw, 0, keepdims=True)
        slots = cx[tokens:, :tokens].astype(F32)
        hots = one_hot(slots, first, number, capp)
        places = jnp.concatenate(hots, 0).astype(BF16)
        rows = dot(places, h).astype(BF16)
        grads = dot(places, cx[:tokens, :]).astype(BF16)
        for j in range(number):
            at = slice(j * capp, (j + 1) * capp)
            xs_ref[j, b] = rows[at]
            gs_ref[j, b] = grads[at]
            gate = jnp.sum(hots[j] * own_row(router, first + j), 1, keepdims=True)
            gates_ref[j, b] = jnp.broadcast_to(gate, (capp, 128))

    cx_slot = {2: 0, 3: 1, 4: 2, 5: 3, 6: 4, 7: 5}
    place(0)
    hop(3).wait_recv()
    place(4)
    for i in (0, 1, 2):
        hop(i).wait_recv()
        forward(i).start()
        place(1 + i)
    for i in (0, 1, 2):
        forward(i).wait_recv()
        place(5 + i)
    for i in range(4):
        hop(i).wait_send()
    for i in range(3):
        forward(i).wait_send()
    keep.wait()


def mid_step(attn, cxs, rest, wo, wr, x, gain, number, capp, n):
    tokens, width = x.shape
    hbm, vmem = pl.BlockSpec(memory_space=pl.ANY), pl.BlockSpec(memory_space=pltpu.VMEM)
    dma = lambda k: pltpu.SemaphoreType.DMA((k,))
    shaped = lambda shape, dtype=BF16: jax.ShapeDtypeStruct(shape, dtype)
    return pl.pallas_call(
        functools.partial(mid_kernel, n, number, capp),
        in_specs=[hbm, vmem, vmem, vmem, vmem, vmem, vmem],
        out_specs=[vmem, vmem, hbm, vmem, vmem, vmem],
        out_shape=[
            shaped((tokens, width), F32),
            shaped((tokens, width)),
            shaped(attn.shape),
            shaped((number, 8, capp, width)),
            shaped((number, 8, capp, width)),
            shaped((number, 8, capp, 128), F32),
        ],
        scratch_shapes=[
            pltpu.VMEM(attn.shape, BF16),
            pltpu.VMEM((8, tokens, width), BF16),
            pltpu.VMEM((tokens, width), F32),
            dma(n - 1),
            dma(n - 1),
            dma(4),
            dma(4),
            dma(3),
            dma(3),
            dma(2),
        ],
        compiler_params=params(collective_id=2, has_side_effects=True),
        cost_estimate=cost(4e9, 5e7),
        name="mid_step",
    )(attn, cxs, rest, wo, wr, x, gain)


RING = 8
ORDER_X, ORDER_Y, ORDER_CORE = 1, 2, 4


class GroupSum:
    def __init__(self, part, rows, lands, own, sems, load, free, first, core, group):
        self.part, self.rows, self.own, self.load, self.free, self.first = part, rows, own, load, free, first
        self.land, self.land_x, self.land_y = lands
        self.core_send, self.core_recv, self.x_send, self.x_recv, self.y_send, self.y_recv = sems
        self.core, self.far, self.near = core, group[0], group[1]

    def place(self, i):
        return self.land.at[i, pl.ds(0, self.rows)]

    def ready(self, which):
        if not self.first:
            pl.semaphore_wait(self.free.at[which], 1)

    def to_core(self, i):
        return send(self.part.at[4 + i], self.place(i), self.core_send.at[i], self.core_recv.at[i], self.core)

    def to_far(self, k):
        return send(self.place(1 + 2 * k), self.land_x.at[k, pl.ds(0, self.rows)], self.x_send.at[k], self.x_recv.at[k], self.far)

    def to_near(self):
        return send(self.place(2), self.land_y.at[pl.ds(0, self.rows)], self.y_send.at[0], self.y_recv.at[0], self.near)

    def fetch(self, i):
        return pltpu.make_async_copy(self.part.at[i], self.own.at[i % 2, pl.ds(0, self.rows)], self.load.at[i % 2])

    def start(self):
        self.ready(0)
        for i in (1, 3, 2, 0):
            self.to_core(i).start()

    def over_cores(self):
        order = (1, 3, 2, 0)
        if self.own is not None:
            self.fetch(1).start()
        for step, i in enumerate(order):
            if self.own is None:
                mine = self.part[i]
            else:
                self.fetch(i).wait()
                mine = self.own[i % 2, : self.rows]
            self.to_core(i).wait_recv()
            self.land[i, : self.rows] = (self.land[i, : self.rows].astype(F32) + mine.astype(F32)).astype(BF16)
            if self.own is not None and step < 3:
                self.fetch(order[step + 1]).start()
            if i % 2 == 1:
                if step == 0:
                    self.ready(1)
                self.to_far(i // 2).start()

    def over_x(self):
        for k in (1, 0):
            self.to_far(k).wait_recv()
            both = self.land[2 * k, : self.rows].astype(F32) + self.land_x[k, : self.rows].astype(F32)
            self.land[2 * k, : self.rows] = both.astype(BF16)
            if k == 1:
                self.ready(2)
                self.to_near().start()

    def finish(self):
        self.to_near().wait_recv()
        for i in range(4):
            self.to_core(i).wait_send()
        for k in range(2):
            self.to_far(k).wait_send()
        self.to_near().wait_send()
        return self.land[0, : self.rows].astype(F32) + self.land_y[: self.rows].astype(F32)

    def release(self):
        for which, device in enumerate((self.core, self.far, self.near)):
            pl.semaphore_signal(self.free.at[which], inc=1, device_id=device, device_id_type=MESH)


class LineSum:
    def __init__(self, count, own_ref, other_ref, inbox, across, mine, sems):
        self.count, self.own_ref, self.other_ref = count, own_ref, other_ref
        self.inbox, self.across, self.mine = inbox, across, mine
        self.line_send, self.line_recv, self.mid_send, self.mid_recv, self.side_send, self.side_recv, self.store, self.load = sems
        ctx = lax.axis_index("ctx")
        z = ctx // 2
        self.middle = (z == 1) | (z == 2)
        self.line = {"ctx": jnp.where(z % 2 == 0, ctx + 2, ctx - 2)}
        self.peer = {"ctx": jnp.where(z == 1, ctx + 2, ctx - 2)}
        self.side = {"ctx": flip(ctx, 1)}

    def send_line(self, src, i):
        s = lax.rem(i, RING)
        return send(src, self.inbox.at[s], self.line_send.at[s], self.line_recv.at[s], self.line)

    def send_mid(self, i):
        s = lax.rem(i, RING)
        return send(self.inbox.at[s], self.across.at[s], self.mid_send.at[s], self.mid_recv.at[s], self.peer)

    def send_side(self, src, i):
        return send(src, self.other_ref.at[i], self.side_send.at[lax.rem(i, RING)], self.side_recv.at[i], self.side)

    def keep(self, src, i):
        return pltpu.make_async_copy(src, self.own_ref.at[i], self.store.at[lax.rem(i, RING)])

    def fetch(self, src, i):
        s = lax.rem(i, 2)
        return pltpu.make_async_copy(src, self.mine.at[s], self.load.at[s])

    def drain_middle(self, i):
        src = self.across.at[lax.rem(i, RING)]
        self.send_line(src, i).wait_send()
        self.send_side(src, i).wait_send()
        self.keep(src, i).wait()

    def drain_end(self, i):
        src = self.inbox.at[lax.rem(i, RING)]
        self.send_side(src, i).wait_send()
        self.keep(src, i).wait()

    def tick(self, t, source):
        count = self.count
        fixed = isinstance(t, int)

        def when(condition):
            if fixed:
                return (lambda f: f()) if condition else (lambda f: None)
            return pl.when(condition)

        i32 = (lambda v: jnp.int32(v)) if fixed else (lambda v: v)

        @pl.when(self.middle)
        def _():
            @when((t >= 1) & (t <= count))
            def _():
                i = i32(t - 1)

                @when(t >= 7)
                def _():
                    self.drain_middle(i32(t - 7))

                s = lax.rem(i, RING)
                self.fetch(self.own_ref.at[i], i).wait()
                self.send_line(self.inbox.at[s], i).wait_recv()
                self.inbox[s] = self.inbox[s] + self.mine[lax.rem(i, 2)]
                self.send_mid(i).start()

            @when(t < count)
            def _():
                self.fetch(source(t), i32(t)).start()

            @when((t >= 2) & (t <= count + 1))
            def _():
                i = i32(t - 2)
                s = lax.rem(i, RING)
                self.send_mid(i).wait()
                self.across[s] = self.across[s] + self.inbox[s]
                self.send_line(self.across.at[s], i).start()
                self.send_side(self.across.at[s], i).start()
                self.keep(self.across.at[s], i).start()

        @pl.when(jnp.logical_not(self.middle))
        def _():
            @when(t < count)
            def _():
                @when(t >= 8)
                def _():
                    self.drain_end(i32(t - 8))

                @when(t >= 2)
                def _():
                    self.send_line(self.mine.at[0], i32(t - 2)).wait_send()

                self.send_line(source(t), i32(t)).start()

            @when(t >= 4)
            def _():
                i = i32(t - 4)
                s = lax.rem(i, RING)
                self.send_line(self.inbox.at[s], i).wait_recv()
                self.send_side(self.inbox.at[s], i).start()
                self.keep(self.inbox.at[s], i).start()

    def finish(self):
        count = self.count

        @pl.when(self.middle)
        def _():
            for i in range(count - 6, count):
                self.drain_middle(jnp.int32(i))

        @pl.when(jnp.logical_not(self.middle))
        def _():
            for i in range(count - 2, count):
                self.send_line(self.mine.at[0], jnp.int32(i)).wait_send()
            for i in range(count - 8, count):
                self.drain_end(jnp.int32(i))

        def arrived(i, carry):
            self.send_side(self.mine.at[0], i).wait_recv()
            return carry

        lax.fori_loop(0, count, arrived, 0)


def backward_kernel(
    n,
    length,
    capp,
    ends_ref,
    xs_ref,
    gs_ref,
    gates_ref,
    wg_ref,
    wu_ref,
    wd_ref,
    cxs_ref,
    rest_ref,
    full_ref,
    weights_ref,
    packs_hbm,
    table_hbm,
    cot_hbm,
    wo_hbm,
    attn_hbm,
    x_hbm,
    h_attn_hbm,
    h_ref,
    middle_ref,
    wr_ref,
    gains_ref,
    lse_ref,
    own_ref,
    other_ref,
    pieces_ref,
    outs_ref,
    backs_ref,
    gx_ref,
    yp_ref,
    grad_x_ref,
    mixed_ref,
    inbox,
    across,
    mine,
    land,
    land_x,
    land_y,
    own_buf,
    ga_in,
    grads_in,
    line_send,
    line_recv,
    mid_send,
    mid_recv,
    side_send,
    side_recv,
    line_store,
    line_load,
    ga_send,
    ga_recv,
    gr_send,
    gr_recv,
    group_sems,
    group_load,
    free,
    local_sems,
    full_sems,
    w_sems,
    load_sems,
    store_sems,
    comb_sems,
    part_sems,
):
    tokens, width = h_ref.shape
    half = length // 2
    rows = tokens // 2
    shard = width // 4
    blocks = length // BLK
    number = xs_ref.shape[0]
    ff = wg_ref.shape[2]
    ctx, fsdp = lax.axis_index("ctx"), lax.axis_index("fsdp")
    side = lax.rem(ctx, 2)
    first = (fsdp * 2 + side) * number
    core, group = neighbours()
    sub = own_ref.shape[1]
    cuts = PIECE // sub
    early = number * 6 * cuts
    line = LineSum(early + 2 * cuts, own_ref, other_ref, inbox, across, mine, (line_send, line_recv, mid_send, mid_recv, side_send, side_recv, line_store, line_load))

    def source(t):
        return pieces_ref.at[t // cuts, pl.ds(pl.multiple_of(lax.rem(t, cuts) * sub, sub), sub)]

    def tick(t):
        line.tick(jnp.int32(t) if isinstance(t, int) else t, source)

    sems = lambda k: [group_sems.at[k, j] for j in range(6)]
    lands = (land, land_x, land_y)
    ext = tokens + EXPERTS
    gx = GroupSum(gx_ref, 2 * ext, lands, own_buf, sems(0), group_load.at[0], free, True, core, group)
    ys = GroupSum(yp_ref, 2 * tokens, lands, own_buf, sems(1), group_load.at[1], free, False, core, group)

    greet([core, group[0]] + [{"ctx": c} for c in others(n)])

    def strip(r):
        f = fsdp
        if r & ORDER_X:
            f = flip(f, 2)
        if r & ORDER_CORE:
            f = flip(f, 1)
        return 2 * f + (1 - side if r & ORDER_Y else side)

    def experts(wg, wu, wd, xb, gb, gateb, stage, out_acc, back_acc, outb, backb, go, dgate, comb_o, comb_b, gst, yst, slots):
        def loads(e):
            s = lax.rem(e, 2)
            at = side * number + e
            pairs = ((wg_ref.at[at], wg), (wu_ref.at[at], wu), (wd_ref.at[at], wd), (xs_ref.at[e], xb), (gs_ref.at[e], gb), (gates_ref.at[e], gateb))
            return [pltpu.make_async_copy(src, dst.at[s], load_sems.at[s, k]) for k, (src, dst) in enumerate(pairs)]

        def slot_copy(b):
            src = cxs_ref.at[b] if b < 2 else rest_ref.at[b - 2]
            return pltpu.make_async_copy(src.at[pl.ds(tokens, EXPERTS), pl.ds(0, tokens)], slots.at[b], part_sems.at[0, b])

        def stores(e):
            pairs = ((stage, pieces_ref.at[pl.ds(6 * e, 6)]), (outb, outs_ref.at[e]), (backb, backs_ref.at[e]))
            return [pltpu.make_async_copy(src, dst, store_sems.at[k]) for k, (src, dst) in enumerate(pairs)]

        for copy in loads(jnp.int32(0)):
            copy.start()
        for b in range(8):
            slot_copy(b).start()

        def one(e, carry):
            s = lax.rem(e, 2)

            @pl.when(e + 1 < number)
            def _():
                for copy in loads(e + 1):
                    copy.start()

            for copy in loads(e):
                copy.wait()

            @pl.when(e > 0)
            def _():
                for copy in stores(e - 1)[1:]:
                    copy.wait()

            x = xb[s]
            gate = gateb[s][:, :1]
            go[...] = (gate * (RESIDUAL * gb[s].astype(F32))).astype(BF16)
            part = ff // 2
            for chunk in range(2):
                at = slice(chunk * part, (chunk + 1) * part)
                wgc, wuc, wdc = wg[s, :, at], wu[s, :, at], wd[s, at, :]
                pre_gate = dot(x, wgc)
                pre_up = dot(x, wuc)
                sig = jax.nn.sigmoid(pre_gate)
                hidden = (pre_gate * sig * pre_up).astype(BF16)
                out_part = dot(hidden, wdc)
                grad_hidden = dot(go[...], wdc, NT)
                grad_gate = (grad_hidden * pre_up * sig * (1.0 + pre_gate * (1.0 - sig))).astype(BF16)
                grad_up = (grad_hidden * pre_gate * sig).astype(BF16)
                row_part = dot(grad_gate, wgc, NT) + dot(grad_up, wuc, NT)
                dwg = dot(x, grad_gate, TN).astype(BF16)
                dwu = dot(x, grad_up, TN).astype(BF16)
                dwd = dot(hidden, go[...], TN).astype(BF16)
                for k in range(2):
                    cut = slice(k * PIECE, (k + 1) * PIECE)
                    stage[k, :, at] = dwg[cut]
                    stage[2 + k, :, at] = dwu[cut]
                    stage[4 + k, at, :] = dwd[:, cut]
                if chunk == 0:
                    out_acc[...] = out_part
                    back_acc[...] = row_part

                    @pl.when(e > 0)
                    def _():
                        tick(2 * e - 1)

                else:
                    out = (out_acc[...] + out_part).astype(BF16).astype(F32)
                    outb[...] = (gate * out).astype(BF16)
                    backb[...] = (back_acc[...] + row_part).astype(BF16)
                    grad = jnp.sum(RESIDUAL * gb[s].astype(F32) * out, 1, keepdims=True)
                    dgate[e] = jnp.broadcast_to(grad, dgate.shape[1:])
            for copy in stores(e):
                copy.start()
            stores(e)[0].wait()
            tick(2 * e)
            return carry

        lax.fori_loop(0, number, one, 0)
        for copy in stores(jnp.int32(number - 1))[1:]:
            copy.wait()
        for b in range(8):
            slot_copy(b).wait()

        def which(s):
            k = lax.rem(s, 4)
            i = jnp.where(k == 0, 1, jnp.where(k == 1, 3, jnp.where(k == 2, 2, 0)))
            return jnp.where(s < 4, 4 + i, i), i

        def comb(s):
            k = lax.rem(s, 2)
            at = pl.ds(pl.multiple_of(which(s)[0] * capp, 16), capp)
            return [
                pltpu.make_async_copy(outs_ref.at[:, at], comb_o.at[k], comb_sems.at[0, k]),
                pltpu.make_async_copy(backs_ref.at[:, at], comb_b.at[k], comb_sems.at[1, k]),
            ]

        def put(s):
            k = lax.rem(s, 2)
            r, _ = which(s)
            return [
                pltpu.make_async_copy(gst.at[k], gx_ref.at[r], part_sems.at[1, k]),
                pltpu.make_async_copy(yst.at[k], yp_ref.at[r], part_sems.at[1, 2 + k]),
            ]

        for copy in comb(jnp.int32(0)):
            copy.start()

        def join(s, carry):
            k = lax.rem(s, 2)
            r, i = which(s)

            @pl.when(s + 1 < 8)
            def _():
                for copy in comb(s + 1):
                    copy.start()

            for copy in comb(s):
                copy.wait()

            @pl.when(s >= 6)
            def _():
                put(s - 2)[0].wait()

            @pl.when(s >= 2)
            def _():
                put(s - 2)[1].wait()

            hots = one_hot(slots[r].astype(F32), first, number, capp)
            places = jnp.concatenate(hots, 0).astype(BF16)
            y = dot(places, comb_o[k].reshape(number * capp, width), TN).astype(BF16)
            back = dot(places, comb_b[k].reshape(number * capp, width), TN).astype(BF16)
            extra = jnp.zeros((EXPERTS, 2 * tokens), F32)
            for j in range(number):
                grads = dgate[j, pl.ds(pl.multiple_of(r * capp, 16), capp), :][:, :1]
                grad = jnp.sum(hots[j] * grads, 0, keepdims=True)
                high = grad.astype(BF16).astype(F32)
                extra = jnp.where(row_iota(extra.shape) == first + j, jnp.concatenate([high, grad - high], 1), extra)
            for q in range(2):
                yst[k, q * tokens : (q + 1) * tokens, :] = y[:, q * PIECE : (q + 1) * PIECE]
                gst[k, q * ext : q * ext + tokens, :] = back[:, q * PIECE : (q + 1) * PIECE]
            gst[k, tokens:ext, :] = extra.astype(BF16)
            gst[k, ext + tokens :, :] = jnp.zeros((EXPERTS, PIECE), BF16)
            for copy in put(s):
                copy.start()

            @pl.when(s < 4)
            def _():
                put(s)[0].wait()
                gx.to_core(i).start()

            @pl.when(lax.rem(s, 3) == 2)
            def _():
                tick(2 * number - 1 + s // 3)

            return carry

        lax.fori_loop(0, 8, join, 0)
        for s in range(6, 8):
            for copy in put(jnp.int32(s)):
                copy.wait()

    slots_rows = xs_ref.shape[1]
    pl.run_scoped(
        experts,
        pltpu.VMEM((2, width, ff), BF16),
        pltpu.VMEM((2, width, ff), BF16),
        pltpu.VMEM((2, ff, width), BF16),
        pltpu.VMEM((2, slots_rows, width), BF16),
        pltpu.VMEM((2, slots_rows, width), BF16),
        pltpu.VMEM((2, slots_rows, 128), F32),
        pltpu.VMEM((6, PIECE, PIECE), BF16),
        pltpu.VMEM((slots_rows, width), F32),
        pltpu.VMEM((slots_rows, width), F32),
        pltpu.VMEM((slots_rows, width), BF16),
        pltpu.VMEM((slots_rows, width), BF16),
        pltpu.VMEM((slots_rows, width), BF16),
        pltpu.VMEM((number, slots_rows, 128), F32),
        pltpu.VMEM((2, number, capp, width), BF16),
        pltpu.VMEM((2, number, capp, width), BF16),
        pltpu.VMEM((2, 2 * ext, PIECE), BF16),
        pltpu.VMEM((2, 2 * tokens, PIECE), BF16),
        pltpu.VMEM((8, EXPERTS, tokens), BF16),
    )
    at_tick = [2 * number + 1]

    def go_on(k=1):
        for _ in range(k):
            tick(at_tick[0])
            at_tick[0] += 1

    def backward(packs, table, keys, values, keys_t, grad_q, grad_k, grad_v, acc, full_buf, ga, pack_out, wbuf, total, grad_middle, dgain, col, small, cot, wo, attn, x_in, h_attn):
        ws = GroupSum(small, 2 * PIECE, lands, None, sems(2), None, free, False, core, group)
        copies = [
            pltpu.make_async_copy(src, dst, local_sems.at[4 + k])
            for k, (src, dst) in enumerate(
                ((cot_hbm, cot), (wo_hbm, wo), (attn_hbm, attn), (packs_hbm, packs), (table_hbm, table), (x_hbm, x_in), (h_attn_hbm, h_attn))
            )
        ]
        for copy in copies:
            copy.start()
        small[:, PIECE // 2 : PIECE, :] = jnp.zeros((8, PIECE // 2, PIECE), BF16)
        gx.over_cores()
        go_on()
        gx.over_x()
        go_on()
        arrived = gx.finish()
        arrived = jnp.concatenate([arrived[:ext], arrived[ext:]], 1)
        gx.release()

        h = h_ref[...]
        gain = gains_ref[1:2]
        extra = arrived[tokens:, :]
        grad_router = extra[:, :tokens] + extra[:, tokens : 2 * tokens]
        grad_router = jnp.transpose(jnp.concatenate([grad_router, jnp.zeros((128 - EXPERTS, tokens), F32)], 0))
        logits = dot(h, wr_ref[...])
        logits = jnp.where(lane_iota(logits.shape) < EXPERTS, logits, MASKED)
        raw = jnp.exp(logits - jnp.max(logits, -1, keepdims=True))
        router = raw / jnp.sum(raw, -1, keepdims=True)
        grad_logits = (router * (grad_router - jnp.sum(router * grad_router, -1, keepdims=True))).astype(BF16)
        grad_h = arrived[:tokens, :] + dot(grad_logits, wr_ref[...], NT)
        normed, scale = norm_parts(middle_ref[...])
        dgain[1:2, :] = jnp.sum(grad_h * normed, 0, keepdims=True)
        for copy in copies[:3]:
            copy.wait()
        grad_mid = cot[...] + norm_back(grad_h * gain, normed, scale)
        grad_middle[...] = grad_mid
        grad_branch = (RESIDUAL * grad_mid).astype(BF16)
        for c in range(n):
            ga[c] = dot(grad_branch, wo[c], NT).astype(BF16)
        ga_exchange = (ga, ga_in, ga_send, ga_recv, local_sems.at[2], n)
        exchange_start(*ga_exchange)
        go_on()
        ys.start()
        col[:, :128] = dot(h, grad_logits, TN).astype(BF16)
        for r in range(8):
            at = strip(r)
            dwo = dot(attn[at], grad_branch, TN).astype(BF16)
            small[r, 0:128, :] = dwo[:, :PIECE]
            small[r, 128:256, :] = dwo[:, PIECE:]
            small[r, 256:384, 0:128] = col[pl.ds(pl.multiple_of(at * 128, 128), 128), 0:128]
        go_on()
        copies[3].wait()
        for hh in range(2):
            for c in range(n):
                kk, vv = pair_keys(packs[c, hh, :, 128:256].astype(F32))
                at = hh * half + c * rows
                keys[at : at + rows, :] = kk.astype(BF16)
                values[at : at + rows, :] = vv.astype(BF16)
                keys_t[:, at : at + rows] = jnp.transpose(kk).astype(BF16)
        grad_k[...] = jnp.zeros_like(grad_k)
        grad_v[...] = jnp.zeros_like(grad_v)
        ys.over_cores()
        go_on()
        exchange_wait(*ga_exchange)
        go_on()

        per = BLK // rows
        per_half = blocks // 2

        def fetch_full(b):
            return pltpu.make_async_copy(full_ref.at[b], full_buf.at[lax.rem(b, 2)], full_sems.at[lax.rem(b, 2)])

        fetch_full(jnp.int32(0)).start()
        attend_tick = at_tick[0]

        def attend(block, carry):
            late = block // per_half
            c0 = lax.rem(block, per_half) * per
            q2 = stack_heads(jnp.concatenate([packs[c0 + k, late, :, :128] for k in range(per)], 0))
            g2 = stack_heads(jnp.concatenate([ga_in[c0 + k, pl.ds(pl.multiple_of(late * rows, rows), rows), :] for k in range(per)], 0))
            position, start = query_rows(ends_ref, block, length)
            lse = lse_ref[block]

            @pl.when(block + 1 < blocks)
            def _():
                fetch_full(block + 1).start()

            fetch_full(block).wait()
            delta = jnp.sum(jnp.transpose(g2.astype(F32)) * full_buf[lax.rem(block, 2)], 0, keepdims=True)
            acc[...] = jnp.zeros_like(acc)

            def body(kb, carry):
                at = pl.multiple_of(kb * BLK, BLK)
                scores = dot(keys[pl.ds(at, BLK), :], q2, NT) * ATTN_SCALE
                where = key_position(kb, length)
                probs = jnp.where((where <= position) & (where >= start), jnp.exp(scores - lse), 0.0)
                grad_probs = dot(values[pl.ds(at, BLK), :], g2, NT)
                grad_scores = (probs * (grad_probs - delta)).astype(BF16)
                acc[...] += dot(keys_t[:, pl.ds(at, BLK)], grad_scores)
                grad_k[pl.ds(at, BLK), :] += dot(grad_scores, q2)
                grad_v[pl.ds(at, BLK), :] += dot(probs.astype(BF16), g2)
                return carry

            block_loop(block, per_half, body, 0)
            grad_q[pl.ds(pl.multiple_of(block * BLK, BLK), BLK), :] = fold_heads(jnp.transpose(acc[...]))
            tick(attend_tick + block)
            return carry

        lax.fori_loop(0, blocks, attend, 0)
        at_tick[0] += blocks
        copies[4].wait()
        for c in range(n):
            for hh in range(2):
                at = slice(hh * half + c * rows, hh * half + (c + 1) * rows)
                kk = grad_k[at, :]
                vv = grad_v[at, :]
                kk = (kk + pltpu.roll(kk, 64, 1)) * ATTN_SCALE
                vv = vv + pltpu.roll(vv, 64, 1)
                both = jnp.where(lane_iota(kk.shape) < 64, kk, vv)
                package = jnp.concatenate([grad_q[at, :] * ATTN_SCALE, both], -1)
                pack_out[c, hh * rows : (hh + 1) * rows, :] = turn(package, table[at, :], -1.0).astype(BF16)
        gr_exchange = (pack_out, grads_in, gr_send, gr_recv, local_sems.at[3], n)
        exchange_start(*gr_exchange)

        def fetch_w(c):
            slot = lax.rem(c, 2)
            return pltpu.make_async_copy(weights_ref.at[:, :, pl.ds(pl.multiple_of(c * PACK, PACK), PACK)], wbuf.at[slot], w_sems.at[slot])

        fetch_w(jnp.int32(0)).start()
        go_on()
        ys.over_x()
        go_on()
        total[...] = jnp.zeros_like(total)
        ffn = ys.finish()
        mixed_ref[...] = middle_ref[...] + RESIDUAL * jnp.concatenate([ffn[:tokens], ffn[tokens:]], 1)
        ys.release()
        go_on(2)
        exchange_wait(*gr_exchange)
        copies[5].wait()
        copies[6].wait()

        columns_tick = at_tick[0]

        def finish_columns(c, carry):
            @pl.when(c + 1 < n)
            def _():
                fetch_w(c + 1).start()

            fetch_w(c).wait()
            slot = lax.rem(c, 2)
            g = grads_in[c]
            col[...] = dot(h_attn[...], g, TN).astype(BF16)
            for r in range(8):
                at = pl.ds(pl.multiple_of(strip(r) * 128, 128), 128)
                small[r, pl.ds(pl.multiple_of(PIECE + c // 2 * 128, 128), 128), pl.ds(pl.multiple_of(lax.rem(c, 2) * PACK, PACK), PACK)] = col[at, :]
            for f in range(4):
                total[:, f * shard : (f + 1) * shard] += dot(g, wbuf[slot, f, :shard, :], NT)

            @pl.when(lax.rem(c, 2) == 1)
            def _():
                tick(columns_tick + c // 2)

            return carry

        lax.fori_loop(0, n, finish_columns, 0)
        at_tick[0] += n // 2
        normed, scale = norm_parts(x_in[...])
        grad_h = total[...]
        dgain[0:1, :] = jnp.sum(grad_h * normed, 0, keepdims=True)
        grad_x_ref[...] = grad_middle[...] + norm_back(grad_h * gains_ref[0:1], normed, scale)
        for r in range(8):
            at = pl.ds(pl.multiple_of(strip(r) * 128, 128), 128)
            row = row_iota((16, 128))
            both = jnp.where(row == 0, dgain[0:1, at], jnp.where(row == 1, dgain[1:2, at], 0.0))
            small[r, 384:400, 0:128] = both.astype(BF16)
        ws.start()
        go_on(2)
        ws.over_cores()
        go_on(3)
        ws.over_x()
        go_on(3)
        land[0] = ws.finish().astype(BF16)

    f32, bf = (lambda *shape: pltpu.VMEM(shape, F32)), (lambda *shape: pltpu.VMEM(shape, BF16))
    pl.run_scoped(
        backward,
        bf(*packs_hbm.shape),
        f32(*table_hbm.shape),
        bf(length, 128),
        bf(length, 128),
        bf(128, length),
        f32(length, 128),
        f32(length, 128),
        f32(length, 128),
        f32(128, 2 * BLK),
        f32(2, 128, 2 * BLK),
        bf(n, tokens, 128),
        bf(n, tokens, PACK),
        bf(2, 4, weights_ref.shape[1], PACK),
        f32(tokens, width),
        f32(tokens, width),
        f32(8, width),
        bf(width, PACK),
        bf(8, 2 * PIECE, PIECE),
        f32(tokens, width),
        bf(*wo_hbm.shape),
        bf(*attn_hbm.shape),
        f32(tokens, width),
        bf(tokens, width),
    )

    def rest(t, carry):
        tick(t)
        return carry

    lax.fori_loop(at_tick[0], early, rest, 0)

    def late_source(t):
        return land.at[0, pl.ds(pl.multiple_of((t - early) * sub, sub), sub)]

    def late(t, carry):
        line.tick(t, late_source)
        return carry

    lax.fori_loop(early, line.count + 4, late, 0)
    line.finish()


def backward_step(ends, xs, gs, gates, w_gate, w_up, w_down, cxs, rest, full, weights, packs, table, cot, wo, attn, x, h_attn, h, middle, wr, gains, lse, n, length, capp):
    tokens, width = x.shape
    number, slots_rows, _ = xs.shape
    hbm, vmem = pl.BlockSpec(memory_space=pl.ANY), pl.BlockSpec(memory_space=pltpu.VMEM)
    smem = pl.BlockSpec(memory_space=pltpu.SMEM)
    dma = lambda *k: pltpu.SemaphoreType.DMA(k)
    shaped = lambda shape, dtype=BF16: jax.ShapeDtypeStruct(shape, dtype)
    sub = PIECE // 2
    piece = (sub, PIECE)
    count = (number * 6 + 2) * 2
    return pl.pallas_call(
        functools.partial(backward_kernel, n, length, capp),
        in_specs=[smem] + [hbm] * 17 + [vmem] * 5,
        out_specs=[hbm] * 7 + [vmem, vmem],
        out_shape=[
            shaped((count,) + piece),
            shaped((count,) + piece),
            shaped((number * 6, PIECE, PIECE)),
            shaped(xs.shape),
            shaped(xs.shape),
            shaped((8, 2 * (tokens + EXPERTS), PIECE)),
            shaped((8, 2 * tokens, PIECE)),
            shaped((tokens, width), F32),
            shaped((tokens, width), F32),
        ],
        scratch_shapes=[
            pltpu.VMEM((RING,) + piece, BF16),
            pltpu.VMEM((RING,) + piece, BF16),
            pltpu.VMEM((2,) + piece, BF16),
            pltpu.VMEM((4, 2 * PIECE, PIECE), BF16),
            pltpu.VMEM((2, 2 * PIECE, PIECE), BF16),
            pltpu.VMEM((2 * PIECE, PIECE), BF16),
            pltpu.VMEM((2, 2 * PIECE, PIECE), BF16),
            pltpu.VMEM((n, tokens, 128), BF16),
            pltpu.VMEM((n, tokens, PACK), BF16),
            dma(RING),
            dma(RING),
            dma(RING),
            dma(RING),
            dma(RING),
            dma(count),
            dma(RING),
            dma(2),
            dma(n - 1),
            dma(n - 1),
            dma(n - 1),
            dma(n - 1),
            dma(3, 6, 4),
            dma(2, 2),
            pltpu.SemaphoreType.REGULAR((3,)),
            dma(11),
            dma(2),
            dma(2),
            dma(2, 6),
            dma(3),
            dma(2, 2),
            dma(2, 8),
        ],
        compiler_params=params(63, collective_id=0, has_side_effects=True),
        cost_estimate=cost(6e10, 1e9),
        name="backward_step",
    )(ends, xs, gs, gates, w_gate, w_up, w_down, cxs, rest, full, weights, packs, table, cot, wo, attn, x, h_attn, h, middle, wr, gains, lse)


def local(
    inputs,
    cotangent,
    doc_lengths,
    routes,
    attn_gain,
    ffn_gain,
    w_query,
    key_weight,
    value_weight,
    w_out,
    w_router,
    w_gate,
    w_up,
    w_down,
):
    rows = inputs.shape[2]
    width = inputs.shape[3]
    n = lax.axis_size("ctx")
    fsdp = lax.axis_size("fsdp")
    me, mine = lax.axis_index("ctx"), lax.axis_index("fsdp")
    tokens = 2 * rows
    length = tokens * n
    experts_here = w_gate.shape[0]
    number = experts_here // 2
    capacity = 5 * tokens * TOP // (4 * EXPERTS)
    capp = -(-capacity // 16) * 16
    shard = width // fsdp
    heads = QUERY_HEADS // n
    head_lanes = heads * HEAD_DIMENSION
    copies = n // KEY_VALUE_HEADS
    bits = group_bits(fsdp)

    x = inputs.reshape(tokens, width)
    cot = cotangent.reshape(tokens, width)
    side = me % 2
    base = (side * number).astype(jnp.int32).reshape(1)
    first = (mine * experts_here + side * number).astype(jnp.int32).reshape(1)
    index = jnp.stack([side * number, (1 - side) * number]).astype(jnp.int32)
    ends = jnp.cumsum(doc_lengths[0])[:3].astype(jnp.int32)
    table = jnp.asarray(rotary_table(length))

    out_part = w_out.reshape(shard // head_lanes, head_lanes, width)
    if head_lanes < 128:
        out_part = jnp.pad(out_part, ((0, 0), (0, 128 - head_lanes), (0, 0)))
    merge = lambda a: a.reshape(number, -1, a.shape[-1])

    if n == 8 and fsdp == 4:
        packs, h_attn, weights, wo, wr, cxs, gains = front(
            w_query,
            key_weight,
            value_weight,
            out_part,
            w_router,
            attn_gain.reshape(1, shard),
            ffn_gain.reshape(1, shard),
            x,
            table.reshape(2, n, rows, 256),
            routes.reshape(tokens, TOP),
            cot,
            capacity,
            n,
        )
        wo, wr = wo.reshape(n, 128, width), wr.reshape(width, 128)
        packs = packs.reshape(n, 2, rows, PACK)
        attn, lse, full, cx_rest = attend(ends, packs, cxs, length)
        middle, h_ffn, attn, xs, gs, gates = mid_step(attn.reshape(n, tokens, 128), cxs, cx_rest, wo, wr, x, gains[1:2], number, capp, n)
        own, other, _, _, _, _, _, grad_x, mixed = backward_step(
            ends,
            merge(xs),
            merge(gs),
            merge(gates),
            w_gate,
            w_up,
            w_down,
            cxs,
            cx_rest,
            full,
            weights,
            packs,
            table,
            cot,
            wo,
            attn,
            x,
            h_attn,
            h_ffn,
            middle,
            wr,
            gains,
            lse,
            n,
            length,
            capp,
        )
        own, other = own.reshape(-1, PIECE, PIECE), other.reshape(-1, PIECE, PIECE)
        shapes = [w.shape for w in (w_gate, w_up, w_down)]
        outs = tail(index, own, other, mixed, grad_x, shapes, shard)
        return (
            outs[3].reshape(inputs.shape),
            outs[4].reshape(inputs.shape),
            outs[10].reshape(shard),
            outs[11].reshape(shard),
            outs[5],
            outs[6],
            outs[7],
            outs[8],
            outs[9],
            outs[0],
            outs[1],
            outs[2],
        )

    else:
        own_table = lax.dynamic_slice_in_dim(table.reshape(2, n, rows, 256), me, 1, 1).reshape(tokens, 256)
        query_part = w_query.reshape(shard, n, head_lanes)
        if head_lanes < 128:
            query_part = jnp.pad(query_part, ((0, 0), (0, 0), (0, 128 - head_lanes)))
        key_part = jnp.repeat(key_weight.reshape(shard, KEY_VALUE_HEADS, HEAD_DIMENSION), copies, 1)
        value_part = jnp.repeat(value_weight.reshape(shard, KEY_VALUE_HEADS, HEAD_DIMENSION), copies, 1)
        packed = jnp.concatenate([query_part, key_part, value_part], -1).reshape(shard, n * PACK)
        padding = 2 * 16 * (shard // 32 + 1) - shard
        gains = jnp.pad(jnp.stack([attn_gain, ffn_gain]), ((0, padding - 2), (0, n * PACK - shard)))
        packed = jnp.concatenate([packed, gains], 0)
        router_part = jnp.pad(w_router, ((0, 0), (0, 128 - EXPERTS)))
        weights = lax.all_gather(packed, "fsdp", axis=0)
        gain_one = weights[:, shard, :shard].reshape(1, width).astype(F32)
        gain_two = weights[:, shard + 1, :shard].reshape(1, width).astype(F32)
        wo = lax.all_gather(out_part, "fsdp", axis=0, tiled=True)
        wr = lax.all_gather(router_part, "fsdp", axis=0, tiled=True)
        cxs = group_gather(prep(routes.reshape(tokens, TOP), cot, capacity), bits)
        packs, h_attn = qkv(x, gain_one, weights, own_table, shard, n)
        packs = lax.all_to_all(packs, "ctx", split_axis=0, concat_axis=0, tiled=True).reshape(n, 2, rows, PACK)
        attn, lse, full = attn_forward(ends, packs, length)
        attn = lax.all_to_all(attn.reshape(n, tokens, 128), "ctx", split_axis=0, concat_axis=0, tiled=True)
        middle, h_ffn = middle_step(attn, wo, x, gain_two)
        xs, gs, gates = gather_rows(first, group_gather(h_ffn, bits), cxs, jnp.transpose(wr), number, capp)
        slots = cxs[:, tokens:]
    xs, gs, gates = merge(xs), merge(gs), merge(gates)
    pieces, outs, back, dgates = expert_step(base, xs, gs, gates, w_gate, w_up, w_down)
    y_part, gx_part = combine(first, slots, outs, back, dgates, tokens, capp)
    pieces = pieces.reshape(number * 6, PIECE, PIECE)
    gx = group_reduce(gx_part, bits)
    grad_middle, dwo, grad_attn, dwr, dgain_two = home_step(gx, h_ffn, middle, cot, wr, wo, gain_two, attn)
    grad_attn = lax.all_to_all(grad_attn, "ctx", split_axis=0, concat_axis=0, tiled=True).reshape(n, 2, rows, 128)
    grads = attn_backward(ends, packs, grad_attn, lse, full, table, length)
    grads = lax.all_to_all(grads.reshape(n, tokens, PACK), "ctx", split_axis=0, concat_axis=0, tiled=True)
    dw, grad_x, dgain_one = final_step(grads, weights, h_attn, x, gain_one, grad_middle, shard)
    mixed = middle + RESIDUAL * group_reduce(y_part, bits).astype(F32)
    own = line_sum(pieces, n)
    other = swap(own, "ctx", 1)
    scatter = lambda a: lax.psum(lax.psum_scatter(a, "fsdp", scatter_dimension=0, tiled=True), "ctx").astype(F32)
    dwo = scatter(dwo)[:, :head_lanes, :].reshape(shard, width)
    small = jnp.concatenate([dwr[:, :EXPERTS], dgain_two.reshape(width, 1).astype(BF16)], 1)
    small = scatter(jnp.pad(small, ((0, 0), (0, 127 - EXPERTS))))
    dwr, dgain_two = small[:, :EXPERTS], small[:, EXPERTS]
    dw = scatter(dw).reshape(shard, n, PACK)
    dgain_one = scatter(dgain_one.reshape(width).astype(BF16))

    outs = widen(index, own, other, [w.shape for w in (w_gate, w_up, w_down)])
    fold = lambda a: a.reshape(shard, KEY_VALUE_HEADS, copies, HEAD_DIMENSION).sum(2).reshape(shard, -1)
    return (
        mixed.reshape(inputs.shape),
        grad_x.reshape(inputs.shape),
        dgain_one,
        dgain_two,
        dw[:, :, :head_lanes].reshape(shard, -1),
        fold(dw[:, :, 128:192]),
        fold(dw[:, :, 192:256]),
        dwo,
        dwr,
        outs[0],
        outs[1],
        outs[2],
    )


def solution(mesh):
    tokens = P("fsdp", None, "ctx", None)
    one, two, three = P("fsdp"), P("fsdp", None), P("fsdp", None, None)
    return jax.shard_map(
        local,
        mesh=mesh,
        in_specs=(tokens, tokens, two, tokens, one, one, two, two, two, two, two, three, three, three),
        out_specs=(tokens, tokens, one, one, two, two, two, two, two, three, three, three),
        check_vma=False,
    )
```

```python
import functools

import jax
import jax.numpy as jnp
import numpy as np
from jax import lax
from jax.experimental import pallas as pl
from jax.experimental.pallas import tpu as pltpu
from jax.sharding import PartitionSpec as P

QUERY_HEADS = 16
KEY_VALUE_HEADS = 8
HEAD_DIMENSION = 64
EXPERTS = 32
TOP = 8

ATTN_SCALE = 0.015625
RESIDUAL = 0.22
NORM_EPS = 1e-06
ROPE_BASE = 10000.0
MASKED = -1e30

F32 = jnp.float32
BF16 = jnp.bfloat16
MIB = 1 << 20
NT = (((1,), (1,)), ((), ()))
TN = (((0,), (0,)), ((), ()))
BLK = 256
PACK = 256


def dot(a, b, dims=None):
    if dims is None:
        return jnp.dot(a, b, preferred_element_type=F32)
    return lax.dot_general(a, b, dims, preferred_element_type=F32)


def params(limit=56, **kw):
    return pltpu.CompilerParams(vmem_limit_bytes=limit * MIB, **kw)


def cost(flops, bytes_accessed):
    return pl.CostEstimate(flops=int(flops), bytes_accessed=int(bytes_accessed), transcendentals=0)


def lane_iota(shape):
    return lax.broadcasted_iota(jnp.int32, shape, len(shape) - 1)


def row_iota(shape):
    return lax.broadcasted_iota(jnp.int32, shape, len(shape) - 2)


def rotary_table(length):
    half = length // 2
    order = np.arange(half, dtype=np.float32)
    positions = np.concatenate([order, length - 1 - order]).astype(np.float32)
    m = np.arange(HEAD_DIMENSION // 2, dtype=np.float64)
    frequency = (ROPE_BASE ** (-2.0 * m / HEAD_DIMENSION)).astype(np.float32)
    angles = (positions[:, None] * frequency[None, :]).astype(np.float64)
    cosine, sine = np.cos(angles), np.sin(angles)
    cos_head = np.concatenate([cosine, cosine], -1)
    sin_head = np.concatenate([-sine, sine], -1)
    return np.concatenate([cos_head, cos_head, sin_head, sin_head], -1).astype(np.float32)


def turn(v, table, direction):
    lanes = lane_iota(v.shape)
    cosine = jnp.concatenate([table[:, :128], table[:, :128]], -1)
    sine = jnp.concatenate([table[:, 128:], table[:, 128:]], -1)
    turned = lanes < 3 * HEAD_DIMENSION
    swapped = jnp.where(lanes % HEAD_DIMENSION < HEAD_DIMENSION // 2, pltpu.roll(v, PACK - 32, 1), pltpu.roll(v, 32, 1))
    return jnp.where(turned, v * cosine + direction * (swapped * sine), v)


def norm_parts(values):
    inv_rms = lax.rsqrt(jnp.mean(values * values, -1, keepdims=True) + NORM_EPS)
    return values * inv_rms, inv_rms


def norm_back(grad_normed, normed, inv_rms):
    return inv_rms * (grad_normed - normed * jnp.mean(grad_normed * normed, -1, keepdims=True))


def prep_kernel(cap, routes_ref, cot_ref, out_ref):
    tokens, width = cot_ref.shape
    routes = routes_ref[...]
    earlier = (lane_iota((tokens, tokens)) < row_iota((tokens, tokens))).astype(BF16)
    experts = lane_iota((tokens, 128))
    base = jnp.zeros((1, 128), F32)
    plus = jnp.zeros((tokens, 128), F32)
    for k in range(TOP):
        chosen = experts == routes[:, k : k + 1]
        ones = chosen.astype(F32)
        slot = dot(earlier, ones.astype(BF16)) + base
        plus = plus + jnp.where(chosen & (slot < cap), slot + 1.0, 0.0)
        base = base + jnp.sum(ones, 0, keepdims=True)
    out_ref[:tokens, :] = cot_ref[...].astype(BF16)
    slots = (jnp.transpose(plus) - 1.0)[:EXPERTS, :]
    out_ref[tokens:, :] = jnp.concatenate([slots, jnp.zeros((EXPERTS, width - tokens), F32)], -1).astype(BF16)


def prep(routes, cot, cap):
    tokens, width = cot.shape
    return pl.pallas_call(
        functools.partial(prep_kernel, cap),
        out_shape=jax.ShapeDtypeStruct((tokens + EXPERTS, width), BF16),
        compiler_params=params(),
        cost_estimate=cost(1e9, 2e6),
        name="prep",
    )(routes, cot)


def qkv_kernel(shard, x_ref, gain_ref, w_ref, table_ref, out_ref, h_ref):
    @pl.when(pl.program_id(0) == 0)
    def _():
        normed, _ = norm_parts(x_ref[...])
        h_ref[...] = (normed * gain_ref[...]).astype(BF16)

    total = None
    for f in range(w_ref.shape[0]):
        part = dot(h_ref[:, f * shard : (f + 1) * shard], w_ref[f, :shard, :])
        total = part if total is None else total + part
    for d in range(out_ref.shape[0]):
        out_ref[d] = turn(total[:, d * PACK : (d + 1) * PACK], table_ref[...], 1.0).astype(BF16)


def qkv(x, gain, weights, table, shard, n):
    tokens, width = x.shape
    fsdp, padded, _ = weights.shape
    return pl.pallas_call(
        functools.partial(qkv_kernel, shard),
        grid=(n // 2,),
        in_specs=[
            pl.BlockSpec((tokens, width), lambda i: (0, 0)),
            pl.BlockSpec((1, width), lambda i: (0, 0)),
            pl.BlockSpec((fsdp, padded, 2 * PACK), lambda i: (0, 0, i)),
            pl.BlockSpec((tokens, 256), lambda i: (0, 0)),
        ],
        out_specs=[
            pl.BlockSpec((2, tokens, PACK), lambda i: (i, 0, 0)),
            pl.BlockSpec((tokens, width), lambda i: (0, 0)),
        ],
        out_shape=[
            jax.ShapeDtypeStruct((n, tokens, PACK), BF16),
            jax.ShapeDtypeStruct((tokens, width), BF16),
        ],
        compiler_params=params(),
        cost_estimate=cost(2 * tokens * width * n * PACK, 8e6),
        name="qkv",
    )(x, gain, weights, table)


def pair_keys(kv):
    other = pltpu.roll(kv, 64, 1)
    low = lane_iota(kv.shape) < 64
    return jnp.where(low, kv, other), jnp.where(low, other, kv)


def stack_heads(q):
    low = lane_iota(q.shape) < 64
    zero = jnp.zeros_like(q)
    return jnp.concatenate([jnp.where(low, q, zero), jnp.where(low, zero, q)], 0)


def fold_heads(stacked):
    rows = stacked.shape[0] // 2
    return jnp.where(lane_iota((rows, 128)) < 64, stacked[:rows], stacked[rows:])


def query_rows(ends_ref, block, length):
    half = length // 2
    lanes = lane_iota((1, 2 * BLK))
    index = block * BLK + jnp.where(lanes < BLK, lanes, lanes - BLK)
    position = jnp.where(index < half, index, length + half - 1 - index)
    start = jnp.zeros_like(position)
    for j in range(3):
        end = ends_ref[j]
        start = jnp.where(position >= end, jnp.maximum(start, end), start)
    return position, start


def key_position(kb, length):
    half = length // 2
    index = kb * BLK + row_iota((BLK, 1))
    return jnp.where(index < half, index, length + half - 1 - index)


def block_loop(block, per_half, body, init):
    late = block >= per_half
    inner = jnp.where(late, block - per_half, block)
    count = jnp.where(late, 2 * per_half - inner, inner + 1)

    def step(j, carry):
        kb = jnp.where(late & (j >= per_half), inner + j, j)
        return body(kb, carry)

    return lax.fori_loop(0, count, step, init)


def load_package(pack_ref, c, h):
    return pack_ref[c, h].astype(F32)


def attn_forward_kernel(length, ends_ref, q_ref, pack_ref, out_ref, lse_ref, full_ref, keys, values_t, acc):
    block = pl.program_id(0)
    half = length // 2
    n, _, rows, _ = pack_ref.shape

    @pl.when(block == 0)
    def _():
        for h in range(2):
            for c in range(n):
                kk, vv = pair_keys(pack_ref[c, h, :, 128:256].astype(F32))
                at = h * half + c * rows
                keys[at : at + rows, :] = kk.astype(BF16)
                if rows % 128 == 0:
                    values_t[:, at : at + rows] = jnp.transpose(vv).astype(BF16)
        if rows % 128 != 0:
            for h in range(2):
                for c in range(0, n, 2):
                    pair = jnp.concatenate([pack_ref[c, h, :, 128:256], pack_ref[c + 1, h, :, 128:256]], 0)
                    _, vv = pair_keys(pair.astype(F32))
                    at = h * half + c * rows
                    values_t[:, at : at + 2 * rows] = jnp.transpose(vv).astype(BF16)

    q = q_ref[...].reshape(BLK, PACK)[:, :128]
    q2 = stack_heads(q)
    position, start = query_rows(ends_ref, block, length)
    acc[...] = jnp.zeros_like(acc)

    def body(kb, carry):
        peak, total = carry
        at = pl.multiple_of(kb * BLK, BLK)
        scores = dot(keys[pl.ds(at, BLK), :], q2, NT) * ATTN_SCALE
        where = key_position(kb, length)
        scores = jnp.where((where <= position) & (where >= start), scores, MASKED)
        new_peak = jnp.maximum(peak, jnp.max(scores, 0, keepdims=True))
        weights = jnp.exp(scores - new_peak)
        fade = jnp.exp(peak - new_peak)
        total = total * fade + jnp.sum(weights, 0, keepdims=True)
        acc[...] = acc[...] * fade + dot(values_t[:, pl.ds(at, BLK)], weights.astype(BF16))
        return new_peak, total

    init = (jnp.full((1, 2 * BLK), MASKED, F32), jnp.zeros((1, 2 * BLK), F32))
    peak, total = block_loop(block, half // BLK, body, init)
    result = acc[...] / total
    full_ref[0] = result
    lse_ref[0] = peak + jnp.log(total)
    folded = fold_heads(jnp.transpose(result)).astype(BF16)
    out_ref[...] = folded.reshape(out_ref.shape)


def attn_forward(ends, packs, length):
    n, _, rows, _ = packs.shape
    blocks, per = length // BLK, BLK // rows
    per_half = blocks // 2
    tiles = lambda i, ends: (lax.rem(i, per_half), i // per_half, 0, 0)
    return pl.pallas_call(
        functools.partial(attn_forward_kernel, length),
        grid_spec=pltpu.PrefetchScalarGridSpec(
            num_scalar_prefetch=1,
            grid=(blocks,),
            in_specs=[
                pl.BlockSpec((per, 1, rows, PACK), tiles),
                pl.BlockSpec(packs.shape, lambda i, ends: (0, 0, 0, 0)),
            ],
            out_specs=[
                pl.BlockSpec((per, 1, rows, 128), tiles),
                pl.BlockSpec((1, 1, 2 * BLK), lambda i, ends: (i, 0, 0)),
                pl.BlockSpec((1, 128, 2 * BLK), lambda i, ends: (i, 0, 0)),
            ],
            scratch_shapes=[
                pltpu.VMEM((length, 128), BF16),
                pltpu.VMEM((128, length), BF16),
                pltpu.VMEM((128, 2 * BLK), F32),
            ],
        ),
        out_shape=[
            jax.ShapeDtypeStruct((n, 2, rows, 128), BF16),
            jax.ShapeDtypeStruct((blocks, 1, 2 * BLK), F32),
            jax.ShapeDtypeStruct((blocks, 128, 2 * BLK), F32),
        ],
        compiler_params=params(),
        cost_estimate=cost(1.5e10, 6e6),
        name="attn_forward",
    )(ends, packs, packs)


def attn_backward_kernel(length, ends_ref, q_ref, g_ref, pack_ref, lse_ref, full_ref, table_ref, out_ref, keys, values, keys_t, grad_q, grad_k, grad_v, acc):
    block = pl.program_id(0)
    half = length // 2
    n, _, rows, _ = pack_ref.shape

    @pl.when(block == 0)
    def _():
        for h in range(2):
            for c in range(n):
                kk, vv = pair_keys(pack_ref[c, h, :, 128:256].astype(F32))
                at = h * half + c * rows
                keys[at : at + rows, :] = kk.astype(BF16)
                values[at : at + rows, :] = vv.astype(BF16)
        for b in range(length // BLK):
            keys_t[:, b * BLK : (b + 1) * BLK] = jnp.transpose(keys[b * BLK : (b + 1) * BLK, :].astype(F32)).astype(BF16)
        grad_k[...] = jnp.zeros_like(grad_k)
        grad_v[...] = jnp.zeros_like(grad_v)

    q2 = stack_heads(q_ref[...].reshape(BLK, PACK)[:, :128])
    g2 = stack_heads(g_ref[...].reshape(BLK, 128))
    position, start = query_rows(ends_ref, block, length)
    lse = lse_ref[0]
    delta = jnp.sum(jnp.transpose(g2.astype(F32)) * full_ref[0], 0, keepdims=True)
    acc[...] = jnp.zeros_like(acc)

    def body(kb, carry):
        at = pl.multiple_of(kb * BLK, BLK)
        scores = dot(keys[pl.ds(at, BLK), :], q2, NT) * ATTN_SCALE
        where = key_position(kb, length)
        probs = jnp.where((where <= position) & (where >= start), jnp.exp(scores - lse), 0.0)
        grad_probs = dot(values[pl.ds(at, BLK), :], g2, NT)
        grad_scores = (probs * (grad_probs - delta)).astype(BF16)
        acc[...] += dot(keys_t[:, pl.ds(at, BLK)], grad_scores)
        grad_k[pl.ds(at, BLK), :] += dot(grad_scores, q2)
        grad_v[pl.ds(at, BLK), :] += dot(probs.astype(BF16), g2)
        return carry

    block_loop(block, half // BLK, body, 0)
    grad_q[pl.ds(pl.multiple_of(block * BLK, BLK), BLK), :] = fold_heads(jnp.transpose(acc[...]))

    @pl.when(block == length // BLK - 1)
    def _():
        for h in range(2):
            for c in range(n):
                at = slice(h * half + c * rows, h * half + (c + 1) * rows)
                kk = grad_k[at, :]
                vv = grad_v[at, :]
                kk = (kk + pltpu.roll(kk, 64, 1)) * ATTN_SCALE
                vv = vv + pltpu.roll(vv, 64, 1)
                both = jnp.where(lane_iota(kk.shape) < 64, kk, vv)
                package = jnp.concatenate([grad_q[at, :] * ATTN_SCALE, both], -1)
                out_ref[c, h] = turn(package, table_ref[at, :], -1.0).astype(BF16)


def attn_backward(ends, packs, grads, lse, full, table, length):
    n, _, rows, _ = packs.shape
    blocks, per = length // BLK, BLK // rows
    per_half = blocks // 2
    tiles = lambda i, ends: (lax.rem(i, per_half), i // per_half, 0, 0)
    return pl.pallas_call(
        functools.partial(attn_backward_kernel, length),
        grid_spec=pltpu.PrefetchScalarGridSpec(
            num_scalar_prefetch=1,
            grid=(blocks,),
            in_specs=[
                pl.BlockSpec((per, 1, rows, PACK), tiles),
                pl.BlockSpec((per, 1, rows, 128), tiles),
                pl.BlockSpec(packs.shape, lambda i, ends: (0, 0, 0, 0)),
                pl.BlockSpec((1, 1, 2 * BLK), lambda i, ends: (i, 0, 0)),
                pl.BlockSpec((1, 128, 2 * BLK), lambda i, ends: (i, 0, 0)),
                pl.BlockSpec(table.shape, lambda i, ends: (0, 0)),
            ],
            out_specs=pl.BlockSpec(packs.shape, lambda i, ends: (0, 0, 0, 0)),
            scratch_shapes=[
                pltpu.VMEM((length, 128), BF16),
                pltpu.VMEM((length, 128), BF16),
                pltpu.VMEM((128, length), BF16),
                pltpu.VMEM((length, 128), F32),
                pltpu.VMEM((length, 128), F32),
                pltpu.VMEM((length, 128), F32),
                pltpu.VMEM((128, 2 * BLK), F32),
            ],
        ),
        out_shape=jax.ShapeDtypeStruct(packs.shape, BF16),
        compiler_params=params(),
        cost_estimate=cost(3e10, 8e6),
        name="attn_backward",
    )(ends, packs, grads, packs, lse, full, table)


def middle_kernel(attn_ref, wo_ref, x_ref, gain_ref, middle_ref, h_ref):
    total = None
    for c in range(attn_ref.shape[0]):
        part = dot(attn_ref[c], wo_ref[c])
        total = part if total is None else total + part
    middle = x_ref[...] + RESIDUAL * total
    middle_ref[...] = middle
    normed, _ = norm_parts(middle)
    h_ref[...] = (normed * gain_ref[...]).astype(BF16)


def middle_step(attn, wo, x, gain):
    tokens, width = x.shape
    return pl.pallas_call(
        middle_kernel,
        out_shape=[jax.ShapeDtypeStruct((tokens, width), F32), jax.ShapeDtypeStruct((tokens, width), BF16)],
        compiler_params=params(),
        cost_estimate=cost(2 * tokens * width * width, 5e6),
        name="middle",
    )(attn, wo, x, gain)


def own_row(table, row):
    return jnp.sum(jnp.where(row_iota(table.shape) == row, table, 0.0), 0, keepdims=True)


def one_hot(slots, first, number, capp):
    tokens = slots.shape[1]
    order = row_iota((capp, tokens)).astype(F32)
    return [(order == own_row(slots, first + j)).astype(F32) for j in range(number)]


def gather_kernel(number, capp, first_ref, h_ref, cx_ref, wrt_ref, x_ref, g_ref, gate_ref):
    tokens = h_ref.shape[1]
    first = first_ref[0]
    h = h_ref[0]
    slots = cx_ref[0, tokens:, :tokens].astype(F32)
    logits = dot(wrt_ref[...], h, NT)[:EXPERTS, :]
    raw = jnp.exp(logits - jnp.max(logits, 0, keepdims=True))
    router = raw / jnp.sum(raw, 0, keepdims=True)
    hots = one_hot(slots, first, number, capp)
    places = jnp.concatenate(hots, 0).astype(BF16)
    rows = dot(places, h).astype(BF16)
    grads = dot(places, cx_ref[0, :tokens, :]).astype(BF16)
    for j in range(number):
        at = slice(j * capp, (j + 1) * capp)
        x_ref[j, 0] = rows[at]
        g_ref[j, 0] = grads[at]
        gate = jnp.sum(hots[j] * own_row(router, first + j), 1, keepdims=True)
        gate_ref[j, 0] = jnp.broadcast_to(gate, (capp, 128))


def gather_rows(first, hs, cxs, wrt, number, capp):
    nb, tokens, width = hs.shape
    return pl.pallas_call(
        functools.partial(gather_kernel, number, capp),
        grid_spec=pltpu.PrefetchScalarGridSpec(
            num_scalar_prefetch=1,
            grid=(nb,),
            in_specs=[
                pl.BlockSpec((1, tokens, width), lambda b, f: (b, 0, 0)),
                pl.BlockSpec((1, tokens + EXPERTS, width), lambda b, f: (b, 0, 0)),
                pl.BlockSpec(wrt.shape, lambda b, f: (0, 0)),
            ],
            out_specs=[
                pl.BlockSpec((number, 1, capp, width), lambda b, f: (0, b, 0, 0)),
                pl.BlockSpec((number, 1, capp, width), lambda b, f: (0, b, 0, 0)),
                pl.BlockSpec((number, 1, capp, 128), lambda b, f: (0, b, 0, 0)),
            ],
        ),
        out_shape=[
            jax.ShapeDtypeStruct((number, nb, capp, width), BF16),
            jax.ShapeDtypeStruct((number, nb, capp, width), BF16),
            jax.ShapeDtypeStruct((number, nb, capp, 128), F32),
        ],
        compiler_params=params(),
        cost_estimate=cost(4 * nb * number * capp * tokens * width, 2e7),
        name="gather_rows",
    )(first, hs, cxs, wrt)


PIECE = 512


def expert_kernel(base_ref, x_ref, g_ref, gate_ref, wg_ref, wu_ref, wd_ref, piece_ref, out_ref, rows_ref, dg_ref):
    x = x_ref[0]
    gate = gate_ref[0][:, :1]
    grad_ffn = RESIDUAL * g_ref[0].astype(F32)
    go = (gate * grad_ffn).astype(BF16)
    part = wg_ref.shape[2] // 2
    out = rows = None
    for chunk in range(2):
        at = slice(chunk * part, (chunk + 1) * part)
        wg, wu, wd = wg_ref[0, :, at], wu_ref[0, :, at], wd_ref[0, at, :]
        pre_gate = dot(x, wg)
        pre_up = dot(x, wu)
        sig = jax.nn.sigmoid(pre_gate)
        hidden = (pre_gate * sig * pre_up).astype(BF16)
        out_part = dot(hidden, wd)
        grad_hidden = dot(go, wd, NT)
        grad_gate = (grad_hidden * pre_up * sig * (1.0 + pre_gate * (1.0 - sig))).astype(BF16)
        grad_up = (grad_hidden * pre_gate * sig).astype(BF16)
        row_part = dot(grad_gate, wg, NT) + dot(grad_up, wu, NT)
        dwg = dot(x, grad_gate, TN).astype(BF16)
        dwu = dot(x, grad_up, TN).astype(BF16)
        dwd = dot(hidden, go, TN).astype(BF16)
        for half in range(2):
            side = slice(half * PIECE, (half + 1) * PIECE)
            piece_ref[0, half, :, at] = dwg[side]
            piece_ref[0, 2 + half, :, at] = dwu[side]
            piece_ref[0, 4 + half, at, :] = dwd[:, side]
        out = out_part if out is None else out + out_part
        rows = row_part if rows is None else rows + row_part
    out = out.astype(BF16).astype(F32)
    out_ref[0] = (gate * out).astype(BF16)
    rows_ref[0] = rows.astype(BF16)
    grad = jnp.sum(grad_ffn * out, 1, keepdims=True)
    dg_ref[0] = jnp.broadcast_to(grad, dg_ref.shape[1:])


def expert_step(base, xs, gs, gates, w_gate, w_up, w_down):
    number, rows, width = xs.shape
    ff = w_gate.shape[2]
    row = lambda e, b: (e, 0, 0)
    weight = lambda e, b: (b[0] + e, 0, 0)
    return pl.pallas_call(
        expert_kernel,
        grid_spec=pltpu.PrefetchScalarGridSpec(
            num_scalar_prefetch=1,
            grid=(number,),
            in_specs=[
                pl.BlockSpec((1, rows, width), row),
                pl.BlockSpec((1, rows, width), row),
                pl.BlockSpec((1, rows, 128), row),
                pl.BlockSpec((1, width, ff), weight),
                pl.BlockSpec((1, width, ff), weight),
                pl.BlockSpec((1, ff, width), weight),
            ],
            out_specs=[
                pl.BlockSpec((1, 6, PIECE, PIECE), lambda e, b: (e, 0, 0, 0)),
                pl.BlockSpec((1, rows, width), row),
                pl.BlockSpec((1, rows, width), row),
                pl.BlockSpec((1, rows, 128), row),
            ],
        ),
        out_shape=[
            jax.ShapeDtypeStruct((number, 6, PIECE, PIECE), BF16),
            jax.ShapeDtypeStruct((number, rows, width), BF16),
            jax.ShapeDtypeStruct((number, rows, width), BF16),
            jax.ShapeDtypeStruct((number, rows, 128), F32),
        ],
        compiler_params=params(60),
        cost_estimate=cost(18 * number * rows * width * ff, 5e7),
        name="expert_step",
    )(base, xs, gs, gates, w_gate, w_up, w_down)


def combine_kernel(number, capp, first_ref, slot_ref, outs, rows, grads, y_ref, gx_ref):
    tokens = y_ref.shape[1]
    width = y_ref.shape[2]
    first = first_ref[0]
    slots = slot_ref[0][:, :tokens].astype(F32)
    hots = one_hot(slots, first, number, capp)
    places = jnp.concatenate(hots, 0).astype(BF16)
    y_ref[0] = dot(places, outs[:, 0].reshape(number * capp, width), TN).astype(BF16)
    gx_ref[0, :tokens] = dot(places, rows[:, 0].reshape(number * capp, width), TN).astype(BF16)
    extra = jnp.zeros((EXPERTS, 2 * tokens), F32)
    for j in range(number):
        grad = jnp.sum(hots[j] * grads[j, 0][:, :1], 0, keepdims=True)
        high = grad.astype(BF16).astype(F32)
        both = jnp.concatenate([high, grad - high], 1)
        extra = jnp.where(row_iota(extra.shape) == first + j, both, extra)
    rest = jnp.zeros((EXPERTS, width - 2 * tokens), F32)
    gx_ref[0, tokens:] = jnp.concatenate([extra, rest], 1).astype(BF16)


def combine(first, slots, outs, rows, grads, tokens, capp):
    number = outs.shape[0]
    nb, _, width = slots.shape
    split = lambda a: a.reshape(number, nb, capp, a.shape[-1])
    wide = pl.BlockSpec((number, 1, capp, width), lambda b, f: (0, b, 0, 0))
    thin = pl.BlockSpec((number, 1, capp, 128), lambda b, f: (0, b, 0, 0))
    return pl.pallas_call(
        functools.partial(combine_kernel, number, capp),
        grid_spec=pltpu.PrefetchScalarGridSpec(
            num_scalar_prefetch=1,
            grid=(nb,),
            in_specs=[pl.BlockSpec((1, EXPERTS, width), lambda b, f: (b, 0, 0))] + [wide, wide, thin],
            out_specs=[
                pl.BlockSpec((1, tokens, width), lambda b, f: (b, 0, 0)),
                pl.BlockSpec((1, tokens + EXPERTS, width), lambda b, f: (b, 0, 0)),
            ],
        ),
        out_shape=[
            jax.ShapeDtypeStruct((nb, tokens, width), BF16),
            jax.ShapeDtypeStruct((nb, tokens + EXPERTS, width), BF16),
        ],
        compiler_params=params(),
        cost_estimate=cost(4 * nb * number * capp * tokens * width, 2e7),
        name="combine",
    )(first, slots, split(outs), split(rows), split(grads))


def home_kernel(gx_ref, h_ref, middle_ref, cot_ref, wr_ref, wo_ref, gain_ref, attn_ref, grad_middle_ref, dwo_ref, ga_ref, dwr_ref, dgain_ref):
    tokens, width = h_ref.shape
    h = h_ref[...]
    gain = gain_ref[...]
    extra = gx_ref[tokens:, :].astype(F32)
    grad_router = extra[:, :tokens] + extra[:, tokens : 2 * tokens]
    grad_router = jnp.transpose(jnp.concatenate([grad_router, jnp.zeros((128 - EXPERTS, tokens), F32)], 0))
    logits = dot(h, wr_ref[...])
    logits = jnp.where(lane_iota(logits.shape) < EXPERTS, logits, MASKED)
    raw = jnp.exp(logits - jnp.max(logits, -1, keepdims=True))
    router = raw / jnp.sum(raw, -1, keepdims=True)
    grad_logits = (router * (grad_router - jnp.sum(router * grad_router, -1, keepdims=True))).astype(BF16)
    dwr_ref[...] = dot(h, grad_logits, TN).astype(BF16)
    grad_h = gx_ref[:tokens, :].astype(F32) + dot(grad_logits, wr_ref[...], NT)
    normed, scale = norm_parts(middle_ref[...])
    dgain_ref[...] = jnp.sum(grad_h * normed, 0, keepdims=True)
    grad_middle = cot_ref[...] + norm_back(grad_h * gain, normed, scale)
    grad_middle_ref[...] = grad_middle
    grad_branch = (RESIDUAL * grad_middle).astype(BF16)
    for c in range(attn_ref.shape[0]):
        dwo_ref[c] = dot(attn_ref[c], grad_branch, TN).astype(BF16)
        ga_ref[c] = dot(grad_branch, wo_ref[c], NT).astype(BF16)


def home_step(gx, h, middle, cot, wr, wo, gain, attn):
    tokens, width = h.shape
    n = attn.shape[0]
    return pl.pallas_call(
        home_kernel,
        out_shape=[
            jax.ShapeDtypeStruct((tokens, width), F32),
            jax.ShapeDtypeStruct((n, 128, width), BF16),
            jax.ShapeDtypeStruct((n, tokens, 128), BF16),
            jax.ShapeDtypeStruct((width, 128), BF16),
            jax.ShapeDtypeStruct((1, width), F32),
        ],
        compiler_params=params(),
        cost_estimate=cost(4 * tokens * width * width, 1e7),
        name="home_step",
    )(gx, h, middle, cot, wr, wo, gain, attn)


def final_kernel(shard, grads_ref, w_ref, h_ref, x_ref, gain_ref, grad_middle_ref, dw_ref, grad_x_ref, dgain_ref, total):
    c = pl.program_id(0)
    g = grads_ref[0]
    dw_ref[...] = dot(h_ref[...], g, TN).astype(BF16)

    @pl.when(c == 0)
    def _():
        total[...] = jnp.zeros_like(total)

    for f in range(w_ref.shape[0]):
        total[:, f * shard : (f + 1) * shard] += dot(g, w_ref[f, :shard, :], NT)

    @pl.when(c == pl.num_programs(0) - 1)
    def _():
        normed, scale = norm_parts(x_ref[...])
        grad_h = total[...]
        dgain_ref[...] = jnp.sum(grad_h * normed, 0, keepdims=True)
        grad_x_ref[...] = grad_middle_ref[...] + norm_back(grad_h * gain_ref[...], normed, scale)


def final_step(grads, weights, h, x, gain, grad_middle, shard):
    n, tokens, _ = grads.shape
    width = x.shape[1]
    fsdp, padded, _ = weights.shape
    same = lambda c: (0, 0)
    return pl.pallas_call(
        functools.partial(final_kernel, shard),
        grid=(n,),
        in_specs=[
            pl.BlockSpec((1, tokens, PACK), lambda c: (c, 0, 0)),
            pl.BlockSpec((fsdp, padded, PACK), lambda c: (0, 0, c)),
            pl.BlockSpec((tokens, width), same),
            pl.BlockSpec((tokens, width), same),
            pl.BlockSpec((1, width), same),
            pl.BlockSpec((tokens, width), same),
        ],
        out_specs=[
            pl.BlockSpec((width, PACK), lambda c: (0, c)),
            pl.BlockSpec((tokens, width), same),
            pl.BlockSpec((1, width), same),
        ],
        out_shape=[
            jax.ShapeDtypeStruct((width, n * PACK), BF16),
            jax.ShapeDtypeStruct((tokens, width), F32),
            jax.ShapeDtypeStruct((1, width), F32),
        ],
        scratch_shapes=[pltpu.VMEM((tokens, width), F32)],
        compiler_params=params(),
        cost_estimate=cost(4 * tokens * width * n * PACK, 1.2e7),
        name="final_step",
    )(grads, weights, h, x, gain, grad_middle)


def widen_kernel(number, index_ref, own_ref, other_ref, gate_ref, up_ref, down_ref):
    def write(ref):
        for half in range(2):
            at = slice(half * PIECE, (half + 1) * PIECE)
            gate_ref[0, at, :] = ref[half].astype(F32)
            up_ref[0, at, :] = ref[2 + half].astype(F32)
            down_ref[0, :, at] = ref[4 + half].astype(F32)

    @pl.when(pl.program_id(0) == 0)
    def _():
        write(own_ref)

    @pl.when(pl.program_id(0) == 1)
    def _():
        write(other_ref)


def tail_kernel(number, index_ref, own_ref, other_ref, own_small_ref, other_small_ref, mixed_in, grad_in, gate_ref, up_ref, down_ref, mixed_ref, grad_ref, dwq_ref, dwk_ref, dwv_ref, dwo_ref, dwr_ref, g1_ref, g2_ref):
    widen_kernel(number, index_ref, own_ref, other_ref, gate_ref, up_ref, down_ref)
    mixed_ref[...] = mixed_in[...]
    grad_ref[...] = grad_in[...]

    @pl.when((pl.program_id(0) == 0) & (pl.program_id(1) == 0))
    def _():
        for which, ref in enumerate((own_small_ref, other_small_ref)):
            part = index_ref[which] // number
            at = pl.ds(pl.multiple_of(part * 128, 128), 128)
            for q in range(4):
                block = ref[1, q * 128 : (q + 1) * 128, :].astype(F32)
                dwq_ref[at, q * 256 : q * 256 + 128] = block[:, :128]
                dwq_ref[at, q * 256 + 128 : (q + 1) * 256] = block[:, 256:384]
                one, two = block[:, 128:256], block[:, 384:]
                low = lane_iota(one.shape) < HEAD_DIMENSION
                dwk_ref[at, q * 128 : (q + 1) * 128] = jnp.where(low, one, pltpu.roll(two, 64, 1))
                dwv_ref[at, q * 128 : (q + 1) * 128] = jnp.where(low, pltpu.roll(one, 64, 1), two)
            dwo_ref[at, :PIECE] = ref[0, 0:128, :].astype(F32)
            dwo_ref[at, PIECE:] = ref[0, 128:256, :].astype(F32)
            dwr_ref[at, :] = ref[0, 256:384, :EXPERTS].astype(F32)
            gains = ref[0, 384:400, :128].astype(F32)
            g1_ref[pl.ds(part, 1), :] = gains[0:1]
            g2_ref[pl.ds(part, 1), :] = gains[1:2]


def expert_specs(number, shapes):
    last = number - 1
    ins = [
        pl.BlockSpec((6, PIECE, PIECE), lambda s, e, at: (jnp.where(s == 0, e, last), 0, 0)),
        pl.BlockSpec((6, PIECE, PIECE), lambda s, e, at: (jnp.where(s == 0, 0, e), 0, 0)),
    ]
    outs = [pl.BlockSpec((1,) + tuple(shape[1:]), lambda s, e, at: (at[s] + e, 0, 0)) for shape in shapes]
    return ins, outs, [jax.ShapeDtypeStruct(shape, F32) for shape in shapes]


def widen(index, own, other, shapes):
    number = shapes[0][0] // 2
    ins, outs, out_shapes = expert_specs(number, shapes)
    return pl.pallas_call(
        functools.partial(widen_kernel, number),
        grid_spec=pltpu.PrefetchScalarGridSpec(num_scalar_prefetch=1, grid=(2, number), in_specs=ins, out_specs=outs),
        out_shape=out_shapes,
        compiler_params=params(),
        cost_estimate=cost(0, 1e8),
        name="widen",
    )(index, own, other)


def tail(index, own, other, mixed, grad_x, shapes, shard):
    number = shapes[0][0] // 2
    tokens, width = mixed.shape
    ins, outs, out_shapes = expert_specs(number, shapes)
    small = pl.BlockSpec((2, PIECE, PIECE), lambda s, e, at: (3 * number, 0, 0))
    rows = pl.BlockSpec((tokens // (2 * number), width), lambda s, e, at: (s * number + e, 0))
    small_shapes = [(shard, width), (shard, width // 2), (shard, width // 2), (shard, width), (shard, EXPERTS), (2, 128), (2, 128)]
    whole = [pl.BlockSpec(shape, lambda s, e, at: (0, 0)) for shape in small_shapes]
    return pl.pallas_call(
        functools.partial(tail_kernel, number),
        grid_spec=pltpu.PrefetchScalarGridSpec(
            num_scalar_prefetch=1,
            grid=(2, number),
            in_specs=ins + [small, small, rows, rows],
            out_specs=outs + [rows, rows] + whole,
        ),
        out_shape=out_shapes
        + [jax.ShapeDtypeStruct((tokens, width), F32)] * 2
        + [jax.ShapeDtypeStruct(shape, F32) for shape in small_shapes],
        compiler_params=params(),
        cost_estimate=cost(0, 1e8),
        name="tail",
    )(index, own, other, own, other, mixed, grad_x)


def swap(value, axis, bit):
    size = lax.axis_size(axis)
    return lax.ppermute(value, axis, [(i, i ^ bit) for i in range(size)])


def group_bits(fsdp):
    bits = [("fsdp", 1 << b) for b in range(1, fsdp.bit_length() - 1)]
    return bits + [("ctx", 1), ("fsdp", 1)]


def group_gather(value, bits):
    stacked = value[None]
    for axis, bit in bits:
        stacked = jnp.concatenate([stacked, swap(stacked, axis, bit)], 0)
    return stacked


def group_reduce(stacked, bits):
    for axis, bit in reversed(bits):
        half = stacked.shape[0] // 2
        arrived = swap(stacked[half:], axis, bit)
        stacked = (stacked[:half].astype(F32) + arrived.astype(F32)).astype(stacked.dtype)
    return stacked[0]


def line_sum(value, ctx):
    pairs = ctx // 2
    if pairs != 4:
        bit = 2
        while bit < ctx:
            value = value + swap(value, "ctx", bit)
            bit *= 2
        return value
    at = lambda z, y: 2 * z + y
    inward = [(at(0, y), at(1, y)) for y in range(2)] + [(at(3, y), at(2, y)) for y in range(2)]
    across = [(at(1, y), at(2, y)) for y in range(2)] + [(at(2, y), at(1, y)) for y in range(2)]
    outward = [(b, a) for a, b in inward]
    value = value + lax.ppermute(value, "ctx", inward)
    value = value + lax.ppermute(value, "ctx", across)
    arrived = lax.ppermute(value, "ctx", outward)
    z = lax.axis_index("ctx") // 2
    return jnp.where((z == 0) | (z == 3), arrived, value)


MESH = pl.DeviceIdType.MESH


def flip(index, bit):
    return jnp.where((index // bit) % 2 == 0, index + bit, index - bit)


def send(src, dst, send_sem, recv_sem, device):
    return pltpu.make_async_remote_copy(src_ref=src, dst_ref=dst, send_sem=send_sem, recv_sem=recv_sem, device_id=device, device_id_type=MESH)


def neighbours():
    ctx, fsdp = lax.axis_index("ctx"), lax.axis_index("fsdp")
    side, across = flip(ctx, 1), flip(fsdp, 2)
    core = {"fsdp": flip(fsdp, 1)}
    return core, [{"fsdp": across}, {"ctx": side}, {"ctx": side, "fsdp": across}]


def greet(devices):
    barrier = pltpu.get_barrier_semaphore()
    for device in devices:
        pl.semaphore_signal(barrier, inc=1, device_id=device, device_id_type=MESH)
    pl.semaphore_wait(barrier, len(devices))


def others(n):
    ctx = lax.axis_index("ctx")
    return [lax.rem(ctx + d, n) for d in range(1, n)]


def exchange_start(src, dst, send_sems, recv_sems, local_sem, n):
    ctx = lax.axis_index("ctx")
    for d, c in enumerate(others(n)):
        send(src.at[c], dst.at[ctx], send_sems.at[d], recv_sems.at[d], {"ctx": c}).start()
    pltpu.make_async_copy(src.at[ctx], dst.at[ctx], local_sem).start()


def exchange_wait(src, dst, send_sems, recv_sems, local_sem, n, arrived=None):
    ctx = lax.axis_index("ctx")
    pltpu.make_async_copy(src.at[ctx], dst.at[ctx], local_sem).wait()
    if arrived is not None:
        arrived(ctx)
    for d in range(n - 1):
        source = lax.rem(ctx + n - 1 - d, n)
        send(src.at[source], dst.at[source], send_sems.at[d], recv_sems.at[d], {"ctx": source}).wait_recv()
        if arrived is not None:
            arrived(source)
    for d, c in enumerate(others(n)):
        send(src.at[c], dst.at[ctx], send_sems.at[d], recv_sems.at[d], {"ctx": c}).wait_send()


def front_kernel(n, cap, wq_ref, wk_ref, wv_ref, wo_part_ref, wr_raw_ref, g1_ref, g2_ref, x_ref, table_ref, routes_ref, cot_ref, packs_ref, h_ref, weights_ref, wo_ref, wr_ref, cxs_ref, gains_ref, wall, packed_ref, wr_part_ref, cx, table, normed_ref, total, out, exch_send, exch_recv, full_send, full_recv, x_send, x_recv, y_send, y_recv, xs_send, xs_recv, ys_send, ys_recv, cx_send, cx_recv, local_sems):
    width = x_ref.shape[1]
    shard = width // 4
    ctx, fsdp = lax.axis_index("ctx"), lax.axis_index("fsdp")
    parity = lax.rem(ctx, 2)
    core, group = neighbours()
    far, near = group[0], group[1]
    sibling, distant = flip(fsdp, 1), flip(fsdp, 2)
    other = flip(distant, 1)
    for k in range(2):
        pltpu.make_async_copy(table_ref.at[k, ctx], table.at[k], local_sems.at[6 + k]).start()

    pair = HEAD_DIMENSION * 2
    for c in range(0, n, 2):
        for k in range(2):
            packed_ref[:shard, (c + k) * PACK : (c + k) * PACK + 128] = wq_ref[:, (c + k) * 128 : (c + k + 1) * 128]
        keys, values = wk_ref[:, c // 2 * pair : (c // 2 + 1) * pair].astype(F32), wv_ref[:, c // 2 * pair : (c // 2 + 1) * pair].astype(F32)
        low = lane_iota(keys.shape) < HEAD_DIMENSION
        packed_ref[:shard, c * PACK + 128 : (c + 1) * PACK] = jnp.where(low, keys, pltpu.roll(values, 64, 1)).astype(BF16)
        packed_ref[:shard, (c + 1) * PACK + 128 : (c + 2) * PACK] = jnp.where(low, pltpu.roll(keys, 64, 1), values).astype(BF16)
    row = row_iota((16, shard))
    gain_rows = jnp.where(row == 0, g1_ref[...].astype(F32), jnp.where(row == 1, g2_ref[...].astype(F32), 0.0))
    packed_ref[shard:, :] = jnp.zeros((packed_ref.shape[0] - shard, n * PACK), BF16)
    packed_ref[shard : shard + 16, :shard] = gain_rows.astype(BF16)
    wr_part_ref[...] = jnp.concatenate([wr_raw_ref[...].astype(F32), jnp.zeros((shard, 128 - EXPERTS), F32)], 1).astype(BF16)
    greet([core, far] + [{"ctx": c} for c in others(n)])

    half_rows = packed_ref.shape[0] // 2
    low_rows = half_rows // 32 * 16

    def cut(k, part):
        if k == 0:
            return pl.ds(pl.multiple_of(part * half_rows, 16), low_rows)
        if k == 1:
            return pl.ds(pl.multiple_of(part * half_rows + low_rows, 16), half_rows - low_rows)
        if k == 2:
            return pl.ds(part, 1)
        return pl.ds(pl.multiple_of(part * (shard // 2), 16), shard // 2)

    sources = [packed_ref, packed_ref, wo_part_ref, wr_part_ref]
    targets = [wall, wall, wo_ref, wr_ref]
    wholes = [(packed_ref, wall), (wo_part_ref, wo_ref), (wr_part_ref, wr_ref)]

    def whole(i):
        src, dst = wholes[i]
        return send(src, dst.at[fsdp], full_send.at[i], full_recv.at[i], core)

    def own(i):
        src, dst = wholes[i]
        return pltpu.make_async_copy(src, dst.at[fsdp], local_sems.at[i])

    def to_far(k):
        return send(sources[k].at[cut(k, parity)], targets[k].at[fsdp, cut(k, parity)], x_send.at[k], x_recv.at[k], far)

    def pass_on(k, part, sems, device):
        ref = targets[k].at[distant, cut(k, part)]
        return send(ref, ref, sems[0].at[k], sems[1].at[k], device)

    def far_arrived(k):
        ref = targets[k].at[distant, cut(k, parity)]
        send(ref, ref, x_send.at[k], x_recv.at[k], far).wait_recv()
        pass_on(k, parity, (y_send, y_recv), near).start()
        pass_on(k, parity, (xs_send, xs_recv), core).start()

    def near_arrived(k):
        pass_on(k, 1 - parity, (y_send, y_recv), near).wait_recv()
        pass_on(k, 1 - parity, (ys_send, ys_recv), core).start()

    def core_arrived(k):
        for part, sems in ((parity, (xs_send, xs_recv)), (1 - parity, (ys_send, ys_recv))):
            ref = targets[k].at[other, cut(k, part)]
            send(ref, ref, sems[0].at[k], sems[1].at[k], core).wait_recv()

    own(0).start()
    to_far(0).start()
    to_far(1).start()
    whole(0).start()

    prep_kernel(cap, routes_ref, cot_ref, cx)
    pltpu.make_async_copy(cx, cxs_ref.at[0], local_sems.at[3]).start()
    normed, _ = norm_parts(x_ref[...])
    normed_ref[...] = normed

    def project(block, begin):
        at = pl.ds(pl.multiple_of(block * shard, shard), shard)
        gain = wall[block, shard : shard + 16, :shard].astype(F32)
        gains_ref[:, at] = gain
        h = (normed_ref[:, at] * gain[:1]).astype(BF16)
        h_ref[:, at] = h
        part = dot(h, wall[block, :shard, :])
        total[...] = part if begin else total[...] + part

    own(0).wait()
    project(fsdp, True)
    ref = wall.at[sibling]
    send(ref, ref, full_send.at[0], full_recv.at[0], core).wait_recv()
    project(sibling, False)
    far_arrived(0)
    far_arrived(1)
    for i in (1, 2):
        own(i).start()
        whole(i).start()
        to_far(i + 1).start()
    send(cx, cxs_ref.at[1], cx_send.at[0], cx_recv.at[0], far).start()
    near_arrived(0)
    near_arrived(1)
    project(distant, False)
    core_arrived(0)
    core_arrived(1)
    project(other, False)
    keep = pltpu.make_async_copy(wall, weights_ref, local_sems.at[4])
    keep.start()
    for k in range(2):
        pltpu.make_async_copy(table_ref.at[k, ctx], table.at[k], local_sems.at[6 + k]).wait()
    angles = table[...].reshape(x_ref.shape[0], 256)
    for c in range(n):
        out[c] = turn(total[:, c * PACK : (c + 1) * PACK], angles, 1.0).astype(BF16)
    exchange = (out, packs_ref, exch_send, exch_recv, local_sems.at[5], n)
    exchange_start(*exchange)

    for k in (2, 3):
        far_arrived(k)
    for k in (2, 3):
        near_arrived(k)
    for k in (2, 3):
        core_arrived(k)
    for i in (1, 2):
        src, dst = wholes[i]
        ref = dst.at[sibling]
        send(ref, ref, full_send.at[i], full_recv.at[i], core).wait_recv()
        own(i).wait()
    exchange_wait(*exchange)
    for i in range(3):
        whole(i).wait_send()
    for k in range(4):
        to_far(k).wait_send()
        pass_on(k, parity, (y_send, y_recv), near).wait_send()
        pass_on(k, parity, (xs_send, xs_recv), core).wait_send()
        pass_on(k, 1 - parity, (ys_send, ys_recv), core).wait_send()
    send(cx, cxs_ref.at[1], cx_send.at[0], cx_recv.at[0], far).wait()
    pltpu.make_async_copy(cx, cxs_ref.at[0], local_sems.at[3]).wait()
    keep.wait()


def front(wq, wk, wv, wo_part, wr, g1, g2, x, table, routes, cot, cap, n):
    tokens, width = x.shape
    shard = wq.shape[0]
    hbm, vmem = pl.BlockSpec(memory_space=pl.ANY), pl.BlockSpec(memory_space=pltpu.VMEM)
    dma = lambda k: pltpu.SemaphoreType.DMA((k,))
    shaped = lambda shape, dtype=BF16: jax.ShapeDtypeStruct(shape, dtype)
    cx_shape = (tokens + EXPERTS, width)
    packed = (2 * 16 * (shard // 32 + 1), n * PACK)
    return pl.pallas_call(
        functools.partial(front_kernel, n, cap),
        in_specs=[vmem, vmem, vmem, hbm, vmem, vmem, vmem, vmem, hbm, vmem, vmem],
        out_specs=[hbm, vmem, hbm, hbm, hbm, hbm, vmem],
        out_shape=[
            shaped((n, tokens, PACK)),
            shaped((tokens, width)),
            shaped((4,) + packed),
            shaped((4,) + wo_part.shape),
            shaped((4, shard, 128)),
            shaped((2,) + cx_shape),
            shaped((16, width), F32),
        ],
        scratch_shapes=[
            pltpu.VMEM((4,) + packed, BF16),
            pltpu.VMEM(packed, BF16),
            pltpu.VMEM((shard, 128), BF16),
            pltpu.VMEM(cx_shape, BF16),
            pltpu.VMEM((2, tokens // 2, 256), F32),
            pltpu.VMEM((tokens, width), F32),
            pltpu.VMEM((tokens, n * PACK), F32),
            pltpu.VMEM((n, tokens, PACK), BF16),
            dma(n - 1),
            dma(n - 1),
            dma(3),
            dma(3),
        ]
        + [dma(4)] * 8
        + [dma(1), dma(1), dma(8)],
        compiler_params=params(collective_id=1, has_side_effects=True),
        cost_estimate=cost(2e9, 5e7),
        name="front",
    )(wq, wk, wv, wo_part, wr, g1, g2, x, table, routes, cot)


def attend_kernel(length, n, ends_ref, q_ref, pack_ref, cxs_ref, out_ref, lse_ref, full_ref, rest_ref, keys, values_t, acc, near_send, near_recv, core_send, core_recv):
    block = pl.program_id(0)
    core, group = neighbours()
    near = group[1]

    def to_near(i):
        return send(cxs_ref.at[i], rest_ref.at[i], near_send.at[i], near_recv.at[i], near)

    def to_core(i):
        src = cxs_ref.at[i] if i < 2 else rest_ref.at[i - 2]
        return send(src, rest_ref.at[2 + i], core_send.at[i], core_recv.at[i], core)

    @pl.when(block == 0)
    def _():
        greet([core, near])
        for i in range(2):
            to_near(i).start()
        for i in range(2):
            to_core(i).start()

    attn_forward_kernel(length, ends_ref, q_ref, pack_ref, out_ref, lse_ref, full_ref, keys, values_t, acc)

    @pl.when(block == pl.num_programs(0) - 2)
    def _():
        to_near(0).wait_recv()
        to_core(2).start()

    @pl.when(block == pl.num_programs(0) - 1)
    def _():
        to_near(1).wait_recv()
        to_core(3).start()
        for i in range(4):
            to_core(i).wait()
        for i in range(2):
            to_near(i).wait_send()


def attend(ends, packs, cxs, length):
    n, _, rows, _ = packs.shape
    blocks, per = length // BLK, BLK // rows
    per_half = blocks // 2
    tiles = lambda i: (lax.rem(i, per_half), i // per_half, 0, 0)
    hbm = pl.BlockSpec(memory_space=pl.ANY)
    dma = lambda k: pltpu.SemaphoreType.DMA((k,))
    return pl.pallas_call(
        functools.partial(attend_kernel, length, n),
        grid=(blocks,),
        in_specs=[
            pl.BlockSpec(memory_space=pltpu.SMEM),
            pl.BlockSpec((per, 1, rows, PACK), tiles),
            pl.BlockSpec(packs.shape, lambda i: (0, 0, 0, 0)),
            hbm,
        ],
        out_specs=[
            pl.BlockSpec((per, 1, rows, 128), tiles),
            pl.BlockSpec((1, 1, 2 * BLK), lambda i: (i, 0, 0)),
            pl.BlockSpec((1, 128, 2 * BLK), lambda i: (i, 0, 0)),
            hbm,
        ],
        scratch_shapes=[
            pltpu.VMEM((length, 128), BF16),
            pltpu.VMEM((128, length), BF16),
            pltpu.VMEM((128, 2 * BLK), F32),
            dma(2),
            dma(2),
            dma(4),
            dma(4),
        ],
        out_shape=[
            jax.ShapeDtypeStruct((n, 2, rows, 128), BF16),
            jax.ShapeDtypeStruct((blocks, 1, 2 * BLK), F32),
            jax.ShapeDtypeStruct((blocks, 128, 2 * BLK), F32),
            jax.ShapeDtypeStruct((6,) + cxs.shape[1:], BF16),
        ],
        compiler_params=params(collective_id=3, has_side_effects=True),
        cost_estimate=cost(1.5e10, 2e7),
        name="attend",
    )(ends, packs, packs, cxs)


def mid_kernel(n, number, capp, attn_ref, cxs_ref, rest_ref, wo_ref, wr_ref, x_ref, gain_ref, middle_ref, h_ref, kept_ref, xs_ref, gs_ref, gates_ref, arrived, hs, total, exch_send, exch_recv, hop_send, hop_recv, fwd_send, fwd_recv, local_sems):
    tokens, width = x_ref.shape
    ctx, fsdp = lax.axis_index("ctx"), lax.axis_index("fsdp")
    first = (fsdp * 2 + lax.rem(ctx, 2)) * number
    core, group = neighbours()
    greet([core, group[0], group[2]] + [{"ctx": c} for c in others(n)])
    exchange = (attn_ref, arrived, exch_send, exch_recv, local_sems.at[0], n)
    exchange_start(*exchange)
    total[...] = jnp.zeros_like(total)

    def take(c):
        total[...] += dot(arrived[c], wo_ref[c])

    exchange_wait(*exchange, take)
    keep = pltpu.make_async_copy(arrived, kept_ref, local_sems.at[1])
    keep.start()
    middle = x_ref[...] + RESIDUAL * total[...]
    middle_ref[...] = middle
    normed, _ = norm_parts(middle)
    h = (normed * gain_ref[...]).astype(BF16)
    h_ref[...] = h
    hs[0] = h

    def hop(i):
        return send(hs.at[0], hs.at[1 + i], hop_send.at[i], hop_recv.at[i], (group + [core])[i])

    def forward(i):
        return send(hs.at[1 + i], hs.at[5 + i], fwd_send.at[i], fwd_recv.at[i], core)

    for i in (2, 0, 1, 3):
        hop(i).start()

    def place(b):
        h = hs[b]
        cx = (cxs_ref.at[b] if b < 2 else rest_ref.at[cx_slot[b]])
        logits = jnp.transpose(dot(h, wr_ref[...]))[:EXPERTS, :]
        raw = jnp.exp(logits - jnp.max(logits, 0, keepdims=True))
        router = raw / jnp.sum(raw, 0, keepdims=True)
        slots = cx[tokens:, :tokens].astype(F32)
        hots = one_hot(slots, first, number, capp)
        places = jnp.concatenate(hots, 0).astype(BF16)
        rows = dot(places, h).astype(BF16)
        grads = dot(places, cx[:tokens, :]).astype(BF16)
        for j in range(number):
            at = slice(j * capp, (j + 1) * capp)
            xs_ref[j, b] = rows[at]
            gs_ref[j, b] = grads[at]
            gate = jnp.sum(hots[j] * own_row(router, first + j), 1, keepdims=True)
            gates_ref[j, b] = jnp.broadcast_to(gate, (capp, 128))

    cx_slot = {2: 0, 3: 1, 4: 2, 5: 3, 6: 4, 7: 5}
    place(0)
    hop(3).wait_recv()
    place(4)
    for i in (0, 1, 2):
        hop(i).wait_recv()
        forward(i).start()
        place(1 + i)
    for i in (0, 1, 2):
        forward(i).wait_recv()
        place(5 + i)
    for i in range(4):
        hop(i).wait_send()
    for i in range(3):
        forward(i).wait_send()
    keep.wait()


def mid_step(attn, cxs, rest, wo, wr, x, gain, number, capp, n):
    tokens, width = x.shape
    hbm, vmem = pl.BlockSpec(memory_space=pl.ANY), pl.BlockSpec(memory_space=pltpu.VMEM)
    dma = lambda k: pltpu.SemaphoreType.DMA((k,))
    shaped = lambda shape, dtype=BF16: jax.ShapeDtypeStruct(shape, dtype)
    return pl.pallas_call(
        functools.partial(mid_kernel, n, number, capp),
        in_specs=[hbm, vmem, vmem, vmem, vmem, vmem, vmem],
        out_specs=[vmem, vmem, hbm, vmem, vmem, vmem],
        out_shape=[
            shaped((tokens, width), F32),
            shaped((tokens, width)),
            shaped(attn.shape),
            shaped((number, 8, capp, width)),
            shaped((number, 8, capp, width)),
            shaped((number, 8, capp, 128), F32),
        ],
        scratch_shapes=[
            pltpu.VMEM(attn.shape, BF16),
            pltpu.VMEM((8, tokens, width), BF16),
            pltpu.VMEM((tokens, width), F32),
            dma(n - 1),
            dma(n - 1),
            dma(4),
            dma(4),
            dma(3),
            dma(3),
            dma(2),
        ],
        compiler_params=params(collective_id=2, has_side_effects=True),
        cost_estimate=cost(4e9, 5e7),
        name="mid_step",
    )(attn, cxs, rest, wo, wr, x, gain)


RING = 8
ORDER_X, ORDER_Y, ORDER_CORE = 1, 2, 4


class GroupSum:
    def __init__(self, part, rows, lands, own, sems, load, free, first, core, group):
        self.part, self.rows, self.own, self.load, self.free, self.first = part, rows, own, load, free, first
        self.land, self.land_x, self.land_y = lands
        self.core_send, self.core_recv, self.x_send, self.x_recv, self.y_send, self.y_recv = sems
        self.core, self.far, self.near = core, group[0], group[1]

    def place(self, i):
        return self.land.at[i, pl.ds(0, self.rows)]

    def ready(self, which):
        if not self.first:
            pl.semaphore_wait(self.free.at[which], 1)

    def to_core(self, i):
        return send(self.part.at[4 + i], self.place(i), self.core_send.at[i], self.core_recv.at[i], self.core)

    def to_far(self, k):
        return send(self.place(1 + 2 * k), self.land_x.at[k, pl.ds(0, self.rows)], self.x_send.at[k], self.x_recv.at[k], self.far)

    def to_near(self):
        return send(self.place(2), self.land_y.at[pl.ds(0, self.rows)], self.y_send.at[0], self.y_recv.at[0], self.near)

    def fetch(self, i):
        return pltpu.make_async_copy(self.part.at[i], self.own.at[i % 2, pl.ds(0, self.rows)], self.load.at[i % 2])

    def start(self):
        self.ready(0)
        for i in (1, 3, 2, 0):
            self.to_core(i).start()

    def over_cores(self):
        order = (1, 3, 2, 0)
        if self.own is not None:
            self.fetch(1).start()
        for step, i in enumerate(order):
            if self.own is None:
                mine = self.part[i]
            else:
                self.fetch(i).wait()
                mine = self.own[i % 2, : self.rows]
            self.to_core(i).wait_recv()
            self.land[i, : self.rows] = (self.land[i, : self.rows].astype(F32) + mine.astype(F32)).astype(BF16)
            if self.own is not None and step < 3:
                self.fetch(order[step + 1]).start()
            if i % 2 == 1:
                if step == 0:
                    self.ready(1)
                self.to_far(i // 2).start()

    def over_x(self, between=None):
        for k in (1, 0):
            if k == 0 and between is not None:
                between()
            self.to_far(k).wait_recv()
            both = self.land[2 * k, : self.rows].astype(F32) + self.land_x[k, : self.rows].astype(F32)
            self.land[2 * k, : self.rows] = both.astype(BF16)
            if k == 1:
                self.ready(2)
                self.to_near().start()

    def finish(self):
        self.to_near().wait_recv()
        for i in range(4):
            self.to_core(i).wait_send()
        for k in range(2):
            self.to_far(k).wait_send()
        self.to_near().wait_send()
        return self.land[0, : self.rows].astype(F32) + self.land_y[: self.rows].astype(F32)

    def release(self):
        for which, device in enumerate((self.core, self.far, self.near)):
            pl.semaphore_signal(self.free.at[which], inc=1, device_id=device, device_id_type=MESH)


class LineSum:
    def __init__(self, count, own_ref, other_ref, inbox, across, mine, sems):
        self.count, self.own_ref, self.other_ref = count, own_ref, other_ref
        self.inbox, self.across, self.mine = inbox, across, mine
        self.line_send, self.line_recv, self.mid_send, self.mid_recv, self.side_send, self.side_recv, self.store, self.load = sems
        ctx = lax.axis_index("ctx")
        z = ctx // 2
        self.middle = (z == 1) | (z == 2)
        self.line = {"ctx": jnp.where(z % 2 == 0, ctx + 2, ctx - 2)}
        self.peer = {"ctx": jnp.where(z == 1, ctx + 2, ctx - 2)}
        self.side = {"ctx": flip(ctx, 1)}

    def send_line(self, src, i):
        s = lax.rem(i, RING)
        return send(src, self.inbox.at[s], self.line_send.at[s], self.line_recv.at[s], self.line)

    def send_mid(self, i):
        s = lax.rem(i, RING)
        return send(self.inbox.at[s], self.across.at[s], self.mid_send.at[s], self.mid_recv.at[s], self.peer)

    def send_side(self, src, i):
        return send(src, self.other_ref.at[i], self.side_send.at[lax.rem(i, RING)], self.side_recv.at[i], self.side)

    def keep(self, src, i):
        return pltpu.make_async_copy(src, self.own_ref.at[i], self.store.at[lax.rem(i, RING)])

    def fetch(self, src, i):
        s = lax.rem(i, 2)
        return pltpu.make_async_copy(src, self.mine.at[s], self.load.at[s])

    def drain_middle(self, i):
        src = self.across.at[lax.rem(i, RING)]
        self.send_line(src, i).wait_send()
        self.send_side(src, i).wait_send()
        self.keep(src, i).wait()

    def drain_end(self, i):
        src = self.inbox.at[lax.rem(i, RING)]
        self.send_side(src, i).wait_send()
        self.keep(src, i).wait()

    def tick(self, t, source):
        count = self.count
        fixed = isinstance(t, int)

        def when(condition):
            if fixed:
                return (lambda f: f()) if condition else (lambda f: None)
            return pl.when(condition)

        i32 = (lambda v: jnp.int32(v)) if fixed else (lambda v: v)

        @pl.when(self.middle)
        def _():
            @when((t >= 1) & (t <= count))
            def _():
                i = i32(t - 1)

                @when(t >= 7)
                def _():
                    self.drain_middle(i32(t - 7))

                s = lax.rem(i, RING)
                self.fetch(self.own_ref.at[i], i).wait()
                self.send_line(self.inbox.at[s], i).wait_recv()
                self.inbox[s] = self.inbox[s] + self.mine[lax.rem(i, 2)]
                self.send_mid(i).start()

            @when(t < count)
            def _():
                self.fetch(source(t), i32(t)).start()

            @when((t >= 2) & (t <= count + 1))
            def _():
                i = i32(t - 2)
                s = lax.rem(i, RING)
                self.send_mid(i).wait()
                self.across[s] = self.across[s] + self.inbox[s]
                self.send_line(self.across.at[s], i).start()
                self.send_side(self.across.at[s], i).start()
                self.keep(self.across.at[s], i).start()

        @pl.when(jnp.logical_not(self.middle))
        def _():
            @when(t < count)
            def _():
                @when(t >= 8)
                def _():
                    self.drain_end(i32(t - 8))

                @when(t >= 2)
                def _():
                    self.send_line(self.mine.at[0], i32(t - 2)).wait_send()

                self.send_line(source(t), i32(t)).start()

            @when(t >= 4)
            def _():
                i = i32(t - 4)
                s = lax.rem(i, RING)
                self.send_line(self.inbox.at[s], i).wait_recv()
                self.send_side(self.inbox.at[s], i).start()
                self.keep(self.inbox.at[s], i).start()

    def finish(self):
        count = self.count

        @pl.when(self.middle)
        def _():
            for i in range(count - 6, count):
                self.drain_middle(jnp.int32(i))

        @pl.when(jnp.logical_not(self.middle))
        def _():
            for i in range(count - 2, count):
                self.send_line(self.mine.at[0], jnp.int32(i)).wait_send()
            for i in range(count - 8, count):
                self.drain_end(jnp.int32(i))

        def arrived(i, carry):
            self.send_side(self.mine.at[0], i).wait_recv()
            return carry

        lax.fori_loop(0, count, arrived, 0)


def backward_kernel(
    n,
    length,
    capp,
    ends_ref,
    xs_ref,
    gs_ref,
    gates_ref,
    wg_ref,
    wu_ref,
    wd_ref,
    cxs_ref,
    rest_ref,
    full_ref,
    weights_ref,
    packs_hbm,
    table_hbm,
    cot_hbm,
    wo_hbm,
    attn_hbm,
    x_hbm,
    h_attn_hbm,
    h_ref,
    middle_ref,
    wr_ref,
    gains_ref,
    lse_ref,
    own_ref,
    other_ref,
    pieces_ref,
    outs_ref,
    backs_ref,
    gx_ref,
    yp_ref,
    grad_x_ref,
    mixed_ref,
    inbox,
    across,
    mine,
    land,
    land_x,
    land_y,
    y_land,
    y_land_x,
    y_land_y,
    own_buf,
    late_pieces,
    ga_in,
    grads_in,
    line_send,
    line_recv,
    mid_send,
    mid_recv,
    side_send,
    side_recv,
    line_store,
    line_load,
    ga_send,
    ga_recv,
    gr_send,
    gr_recv,
    group_sems,
    group_load,
    free,
    local_sems,
    full_sems,
    w_sems,
    load_sems,
    store_sems,
    comb_sems,
    part_sems,
):
    tokens, width = h_ref.shape
    half = length // 2
    rows = tokens // 2
    shard = width // 4
    blocks = length // BLK
    number = xs_ref.shape[0]
    ff = wg_ref.shape[2]
    ctx, fsdp = lax.axis_index("ctx"), lax.axis_index("fsdp")
    side = lax.rem(ctx, 2)
    first = (fsdp * 2 + side) * number
    core, group = neighbours()
    sub = own_ref.shape[1]
    cuts = PIECE // sub
    early = number * 6 * cuts
    line = LineSum(early + 2 * cuts, own_ref, other_ref, inbox, across, mine, (line_send, line_recv, mid_send, mid_recv, side_send, side_recv, line_store, line_load))

    def source(t):
        return pieces_ref.at[t // cuts, pl.ds(pl.multiple_of(lax.rem(t, cuts) * sub, sub), sub)]

    def tick(t):
        line.tick(jnp.int32(t) if isinstance(t, int) else t, source)

    sems = lambda k: [group_sems.at[k, j] for j in range(6)]
    lands = (land, land_x, land_y)
    ext = tokens + EXPERTS
    gx = GroupSum(gx_ref, 2 * ext, lands, None, sems(0), None, free, True, core, group)
    ys = GroupSum(yp_ref, 2 * tokens, (y_land, y_land_x, y_land_y), own_buf, sems(1), group_load, free, True, core, group)

    greet([core, group[0]] + [{"ctx": c} for c in others(n)])

    def strip(r):
        f = fsdp
        if r & ORDER_X:
            f = flip(f, 2)
        if r & ORDER_CORE:
            f = flip(f, 1)
        return 2 * f + (1 - side if r & ORDER_Y else side)

    def experts(wg, wu, wd, xb, gb, gateb, stage, out_acc, back_acc, outb, backb, go, dgate, comb_o, comb_b, gst, yst, slots):
        def loads(e):
            s = lax.rem(e, 2)
            at = side * number + e
            pairs = ((wg_ref.at[at], wg), (wu_ref.at[at], wu), (wd_ref.at[at], wd), (xs_ref.at[e], xb), (gs_ref.at[e], gb), (gates_ref.at[e], gateb))
            return [pltpu.make_async_copy(src, dst.at[s], load_sems.at[s, k]) for k, (src, dst) in enumerate(pairs)]

        def slot_copy(b):
            src = cxs_ref.at[b] if b < 2 else rest_ref.at[b - 2]
            return pltpu.make_async_copy(src.at[pl.ds(tokens, EXPERTS), pl.ds(0, tokens)], slots.at[b], part_sems.at[0, b])

        def stores(e):
            pairs = ((stage, pieces_ref.at[pl.ds(6 * e, 6)]), (outb, outs_ref.at[e]), (backb, backs_ref.at[e]))
            return [pltpu.make_async_copy(src, dst, store_sems.at[k]) for k, (src, dst) in enumerate(pairs)]

        for copy in loads(jnp.int32(0)):
            copy.start()
        for b in range(8):
            slot_copy(b).start()

        def one(e, carry):
            s = lax.rem(e, 2)

            @pl.when(e + 1 < number)
            def _():
                for copy in loads(e + 1):
                    copy.start()

            for copy in loads(e):
                copy.wait()

            @pl.when(e > 0)
            def _():
                for copy in stores(e - 1)[1:]:
                    copy.wait()

            x = xb[s]
            gate = gateb[s][:, :1]
            go[...] = (gate * (RESIDUAL * gb[s].astype(F32))).astype(BF16)
            part = ff // 2
            for chunk in range(2):
                at = slice(chunk * part, (chunk + 1) * part)
                wgc, wuc, wdc = wg[s, :, at], wu[s, :, at], wd[s, at, :]
                pre_gate = dot(x, wgc)
                pre_up = dot(x, wuc)
                sig = jax.nn.sigmoid(pre_gate)
                hidden = (pre_gate * sig * pre_up).astype(BF16)
                out_part = dot(hidden, wdc)
                grad_hidden = dot(go[...], wdc, NT)
                grad_gate = (grad_hidden * pre_up * sig * (1.0 + pre_gate * (1.0 - sig))).astype(BF16)
                grad_up = (grad_hidden * pre_gate * sig).astype(BF16)
                row_part = dot(grad_gate, wgc, NT) + dot(grad_up, wuc, NT)
                dwg = dot(x, grad_gate, TN).astype(BF16)
                dwu = dot(x, grad_up, TN).astype(BF16)
                dwd = dot(hidden, go[...], TN).astype(BF16)
                for k in range(2):
                    cut = slice(k * PIECE, (k + 1) * PIECE)
                    stage[k, :, at] = dwg[cut]
                    stage[2 + k, :, at] = dwu[cut]
                    stage[4 + k, at, :] = dwd[:, cut]
                if chunk == 0:
                    out_acc[...] = out_part
                    back_acc[...] = row_part

                    @pl.when(e > 0)
                    def _():
                        tick(2 * e - 1)

                else:
                    out = (out_acc[...] + out_part).astype(BF16).astype(F32)
                    outb[...] = (gate * out).astype(BF16)
                    backb[...] = (back_acc[...] + row_part).astype(BF16)
                    grad = jnp.sum(RESIDUAL * gb[s].astype(F32) * out, 1, keepdims=True)
                    dgate[e] = jnp.broadcast_to(grad, dgate.shape[1:])
            for copy in stores(e):
                copy.start()
            stores(e)[0].wait()
            tick(2 * e)
            return carry

        lax.fori_loop(0, number, one, 0)
        for copy in stores(jnp.int32(number - 1))[1:]:
            copy.wait()
        for b in range(8):
            slot_copy(b).wait()

        def which(s):
            k = lax.rem(s, 4)
            i = jnp.where(k == 0, 1, jnp.where(k == 1, 3, jnp.where(k == 2, 2, 0)))
            return jnp.where(s < 4, 4 + i, i), i

        def comb(s):
            k = lax.rem(s, 2)
            at = pl.ds(pl.multiple_of(which(s)[0] * capp, 16), capp)
            return [
                pltpu.make_async_copy(outs_ref.at[:, at], comb_o.at[k], comb_sems.at[0, k]),
                pltpu.make_async_copy(backs_ref.at[:, at], comb_b.at[k], comb_sems.at[1, k]),
            ]

        def put(s):
            k = lax.rem(s, 2)
            r, _ = which(s)
            return [
                pltpu.make_async_copy(gst.at[k], gx_ref.at[r], part_sems.at[1, k]),
                pltpu.make_async_copy(yst.at[k], yp_ref.at[r], part_sems.at[1, 2 + k]),
            ]

        for copy in comb(jnp.int32(0)):
            copy.start()

        def join(s, carry):
            k = lax.rem(s, 2)
            r, i = which(s)

            @pl.when(s + 1 < 8)
            def _():
                for copy in comb(s + 1):
                    copy.start()

            for copy in comb(s):
                copy.wait()

            @pl.when(s >= 2)
            def _():
                put(s - 2)[1].wait()

            hots = one_hot(slots[r].astype(F32), first, number, capp)
            places = jnp.concatenate(hots, 0).astype(BF16)
            y = dot(places, comb_o[k].reshape(number * capp, width), TN).astype(BF16)
            back = dot(places, comb_b[k].reshape(number * capp, width), TN).astype(BF16)
            extra = jnp.zeros((EXPERTS, 2 * tokens), F32)
            for j in range(number):
                grads = dgate[j, pl.ds(pl.multiple_of(r * capp, 16), capp), :][:, :1]
                grad = jnp.sum(hots[j] * grads, 0, keepdims=True)
                high = grad.astype(BF16).astype(F32)
                extra = jnp.where(row_iota(extra.shape) == first + j, jnp.concatenate([high, grad - high], 1), extra)
            for q in range(2):
                yst[k, q * tokens : (q + 1) * tokens, :] = y[:, q * PIECE : (q + 1) * PIECE]
                gst[k, q * ext : q * ext + tokens, :] = back[:, q * PIECE : (q + 1) * PIECE]
            gst[k, tokens:ext, :] = extra.astype(BF16)
            gst[k, ext + tokens :, :] = jnp.zeros((EXPERTS, PIECE), BF16)
            put(s)[1].start()

            @pl.when(s < 4)
            def _():
                put(s)[0].start()
                put(s)[0].wait()
                gx.to_core(i).start()

            @pl.when(s >= 4)
            def _():
                gx.to_core(i).wait_recv()
                land[i, : gx.rows] = (land[i, : gx.rows].astype(F32) + gst[k].astype(F32)).astype(BF16)

            @pl.when((s == 4) | (s == 5))
            def _():
                gx.to_far(s - 4).start()

            @pl.when(lax.rem(s, 2) == 1)
            def _():
                tick(2 * number - 1 + s // 2)

            return carry

        lax.fori_loop(0, 8, join, 0)
        for s in range(6, 8):
            put(jnp.int32(s))[1].wait()

    slots_rows = xs_ref.shape[1]
    pl.run_scoped(
        experts,
        pltpu.VMEM((2, width, ff), BF16),
        pltpu.VMEM((2, width, ff), BF16),
        pltpu.VMEM((2, ff, width), BF16),
        pltpu.VMEM((2, slots_rows, width), BF16),
        pltpu.VMEM((2, slots_rows, width), BF16),
        pltpu.VMEM((2, slots_rows, 128), F32),
        pltpu.VMEM((6, PIECE, PIECE), BF16),
        pltpu.VMEM((slots_rows, width), F32),
        pltpu.VMEM((slots_rows, width), F32),
        pltpu.VMEM((slots_rows, width), BF16),
        pltpu.VMEM((slots_rows, width), BF16),
        pltpu.VMEM((slots_rows, width), BF16),
        pltpu.VMEM((number, slots_rows, 128), F32),
        pltpu.VMEM((2, number, capp, width), BF16),
        pltpu.VMEM((2, number, capp, width), BF16),
        pltpu.VMEM((2, 2 * ext, PIECE), BF16),
        pltpu.VMEM((2, 2 * tokens, PIECE), BF16),
        pltpu.VMEM((8, EXPERTS, tokens), BF16),
    )
    at_tick = [2 * number + 3]

    def go_on(k=1):
        for _ in range(k):
            tick(at_tick[0])
            at_tick[0] += 1

    def backward(packs, table, keys, values, keys_t, grad_q, grad_k, grad_v, acc, full_buf, ga, pack_out, wbuf, total, grad_middle, dgain, col, small, columns, cot, wo, attn, x_in, h_attn):
        ws = GroupSum(small, PIECE, lands, None, sems(2), None, free, False, core, group)
        cs = GroupSum(columns, PIECE + 16, lands, None, sems(3), None, free, False, core, group)
        copies = [
            pltpu.make_async_copy(src, dst, local_sems.at[4 + k])
            for k, (src, dst) in enumerate(
                ((cot_hbm, cot), (wo_hbm, wo), (attn_hbm, attn), (packs_hbm, packs), (table_hbm, table), (x_hbm, x_in), (h_attn_hbm, h_attn))
            )
        ]
        for copy in copies:
            copy.start()
        small[:, PIECE // 2 : PIECE, :] = jnp.zeros((8, PIECE // 2, PIECE), BF16)
        columns[:, PIECE:, :] = jnp.zeros((8, 16, PIECE), BF16)
        go_on(2)
        gx.over_x(go_on)
        go_on(2)
        arrived = gx.finish()
        arrived = jnp.concatenate([arrived[:ext], arrived[ext:]], 1)
        gx.release()

        h = h_ref[...]
        gain = gains_ref[1:2]
        extra = arrived[tokens:, :]
        grad_router = extra[:, :tokens] + extra[:, tokens : 2 * tokens]
        grad_router = jnp.transpose(jnp.concatenate([grad_router, jnp.zeros((128 - EXPERTS, tokens), F32)], 0))
        logits = dot(h, wr_ref[...])
        logits = jnp.where(lane_iota(logits.shape) < EXPERTS, logits, MASKED)
        raw = jnp.exp(logits - jnp.max(logits, -1, keepdims=True))
        router = raw / jnp.sum(raw, -1, keepdims=True)
        grad_logits = (router * (grad_router - jnp.sum(router * grad_router, -1, keepdims=True))).astype(BF16)
        grad_h = arrived[:tokens, :] + dot(grad_logits, wr_ref[...], NT)
        normed, scale = norm_parts(middle_ref[...])
        dgain[1:2, :] = jnp.sum(grad_h * normed, 0, keepdims=True)
        for copy in copies[:3]:
            copy.wait()
        grad_mid = cot[...] + norm_back(grad_h * gain, normed, scale)
        grad_middle[...] = grad_mid
        grad_branch = (RESIDUAL * grad_mid).astype(BF16)
        for c in range(n):
            ga[c] = dot(grad_branch, wo[c], NT).astype(BF16)
        ga_exchange = (ga, ga_in, ga_send, ga_recv, local_sems.at[2], n)
        exchange_start(*ga_exchange)
        go_on()
        col[:, :128] = dot(h, grad_logits, TN).astype(BF16)
        for r in range(8):
            at = strip(r)
            dwo = dot(attn[at], grad_branch, TN).astype(BF16)
            small[r, 0:128, :] = dwo[:, :PIECE]
            small[r, 128:256, :] = dwo[:, PIECE:]
            small[r, 256:384, 0:128] = col[pl.ds(pl.multiple_of(at * 128, 128), 128), 0:128]
        ws.start()
        ys.start()
        go_on()
        copies[3].wait()
        for hh in range(2):
            for c in range(n):
                kk, vv = pair_keys(packs[c, hh, :, 128:256].astype(F32))
                at = hh * half + c * rows
                keys[at : at + rows, :] = kk.astype(BF16)
                values[at : at + rows, :] = vv.astype(BF16)
                keys_t[:, at : at + rows] = jnp.transpose(kk).astype(BF16)
        grad_k[...] = jnp.zeros_like(grad_k)
        grad_v[...] = jnp.zeros_like(grad_v)
        go_on()
        ws.over_cores()
        ys.over_cores()
        go_on()
        exchange_wait(*ga_exchange)

        per = BLK // rows
        per_half = blocks // 2

        def fetch_full(b):
            return pltpu.make_async_copy(full_ref.at[b], full_buf.at[lax.rem(b, 2)], full_sems.at[lax.rem(b, 2)])

        fetch_full(jnp.int32(0)).start()
        attend_tick = at_tick[0]

        def attend(block, carry):
            late = block // per_half
            c0 = lax.rem(block, per_half) * per
            q2 = stack_heads(jnp.concatenate([packs[c0 + k, late, :, :128] for k in range(per)], 0))
            g2 = stack_heads(jnp.concatenate([ga_in[c0 + k, pl.ds(pl.multiple_of(late * rows, rows), rows), :] for k in range(per)], 0))
            position, start = query_rows(ends_ref, block, length)
            lse = lse_ref[block]

            @pl.when(block + 1 < blocks)
            def _():
                fetch_full(block + 1).start()

            fetch_full(block).wait()
            delta = jnp.sum(jnp.transpose(g2.astype(F32)) * full_buf[lax.rem(block, 2)], 0, keepdims=True)
            acc[...] = jnp.zeros_like(acc)

            def body(kb, carry):
                at = pl.multiple_of(kb * BLK, BLK)
                scores = dot(keys[pl.ds(at, BLK), :], q2, NT) * ATTN_SCALE
                where = key_position(kb, length)
                probs = jnp.where((where <= position) & (where >= start), jnp.exp(scores - lse), 0.0)
                grad_probs = dot(values[pl.ds(at, BLK), :], g2, NT)
                grad_scores = (probs * (grad_probs - delta)).astype(BF16)
                acc[...] += dot(keys_t[:, pl.ds(at, BLK)], grad_scores)
                grad_k[pl.ds(at, BLK), :] += dot(grad_scores, q2)
                grad_v[pl.ds(at, BLK), :] += dot(probs.astype(BF16), g2)
                return carry

            block_loop(block, per_half, body, 0)
            grad_q[pl.ds(pl.multiple_of(block * BLK, BLK), BLK), :] = fold_heads(jnp.transpose(acc[...]))

            @pl.when((block == 1) | (block >= 3))
            def _():
                tick(attend_tick + jnp.where(block == 1, 0, block - 2))

            return carry

        lax.fori_loop(0, blocks, attend, 0)
        at_tick[0] += blocks - 2
        copies[4].wait()
        for c in range(n):
            for hh in range(2):
                at = slice(hh * half + c * rows, hh * half + (c + 1) * rows)
                kk = grad_k[at, :]
                vv = grad_v[at, :]
                kk = (kk + pltpu.roll(kk, 64, 1)) * ATTN_SCALE
                vv = vv + pltpu.roll(vv, 64, 1)
                both = jnp.where(lane_iota(kk.shape) < 64, kk, vv)
                package = jnp.concatenate([grad_q[at, :] * ATTN_SCALE, both], -1)
                pack_out[c, hh * rows : (hh + 1) * rows, :] = turn(package, table[at, :], -1.0).astype(BF16)
        gr_exchange = (pack_out, grads_in, gr_send, gr_recv, local_sems.at[3], n)
        exchange_start(*gr_exchange)

        def fetch_w(c):
            slot = lax.rem(c, 2)
            return pltpu.make_async_copy(weights_ref.at[:, :, pl.ds(pl.multiple_of(c * PACK, PACK), PACK)], wbuf.at[slot], w_sems.at[slot])

        fetch_w(jnp.int32(0)).start()
        go_on()
        ws.over_x()
        ys.over_x()
        go_on(2)
        total[...] = jnp.zeros_like(total)
        late_pieces[:PIECE] = ws.finish().astype(BF16)
        ws.release()
        ffn = ys.finish()
        mixed_ref[...] = middle_ref[...] + RESIDUAL * jnp.concatenate([ffn[:tokens], ffn[tokens:]], 1)
        go_on(4)
        exchange_wait(*gr_exchange)
        copies[5].wait()
        copies[6].wait()

        columns_tick = at_tick[0]

        def finish_columns(c, carry):
            @pl.when(c + 1 < n)
            def _():
                fetch_w(c + 1).start()

            fetch_w(c).wait()
            slot = lax.rem(c, 2)
            g = grads_in[c]
            col[...] = dot(h_attn[...], g, TN).astype(BF16)
            for r in range(8):
                at = pl.ds(pl.multiple_of(strip(r) * 128, 128), 128)
                columns[r, pl.ds(pl.multiple_of(c // 2 * 128, 128), 128), pl.ds(pl.multiple_of(lax.rem(c, 2) * PACK, PACK), PACK)] = col[at, :]
            for f in range(4):
                total[:, f * shard : (f + 1) * shard] += dot(g, wbuf[slot, f, :shard, :], NT)

            @pl.when(lax.rem(c, 4) == 3)
            def _():
                tick(columns_tick + c // 4)

            return carry

        lax.fori_loop(0, n, finish_columns, 0)
        at_tick[0] += n // 4
        normed, scale = norm_parts(x_in[...])
        grad_h = total[...]
        dgain[0:1, :] = jnp.sum(grad_h * normed, 0, keepdims=True)
        grad_x_ref[...] = grad_middle[...] + norm_back(grad_h * gains_ref[0:1], normed, scale)
        for r in range(8):
            at = pl.ds(pl.multiple_of(strip(r) * 128, 128), 128)
            row = row_iota((16, 128))
            both = jnp.where(row == 0, dgain[0:1, at], jnp.where(row == 1, dgain[1:2, at], 0.0))
            columns[r, PIECE:, 0:128] = both.astype(BF16)
        cs.start()
        go_on()
        cs.over_cores()
        go_on(3)
        cs.over_x(go_on)
        go_on(3)
        summed = cs.finish().astype(BF16)
        late_pieces[PIECE:] = summed[:PIECE]
        late_pieces[384:400] = summed[PIECE:]

    f32, bf = (lambda *shape: pltpu.VMEM(shape, F32)), (lambda *shape: pltpu.VMEM(shape, BF16))
    pl.run_scoped(
        backward,
        bf(*packs_hbm.shape),
        f32(*table_hbm.shape),
        bf(length, 128),
        bf(length, 128),
        bf(128, length),
        f32(length, 128),
        f32(length, 128),
        f32(length, 128),
        f32(128, 2 * BLK),
        f32(2, 128, 2 * BLK),
        bf(n, tokens, 128),
        bf(n, tokens, PACK),
        bf(2, 4, weights_ref.shape[1], PACK),
        f32(tokens, width),
        f32(tokens, width),
        f32(8, width),
        bf(width, PACK),
        bf(8, PIECE, PIECE),
        bf(8, PIECE + 16, PIECE),
        f32(tokens, width),
        bf(*wo_hbm.shape),
        bf(*attn_hbm.shape),
        f32(tokens, width),
        bf(tokens, width),
    )

    def rest(t, carry):
        tick(t)
        return carry

    lax.fori_loop(at_tick[0], early, rest, 0)

    def late_source(t):
        return late_pieces.at[pl.ds(pl.multiple_of((t - early) * sub, sub), sub)]

    def late(t, carry):
        line.tick(t, late_source)
        return carry

    lax.fori_loop(early, line.count + 4, late, 0)
    line.finish()


def backward_step(ends, xs, gs, gates, w_gate, w_up, w_down, cxs, rest, full, weights, packs, table, cot, wo, attn, x, h_attn, h, middle, wr, gains, lse, n, length, capp):
    tokens, width = x.shape
    number, slots_rows, _ = xs.shape
    hbm, vmem = pl.BlockSpec(memory_space=pl.ANY), pl.BlockSpec(memory_space=pltpu.VMEM)
    smem = pl.BlockSpec(memory_space=pltpu.SMEM)
    dma = lambda *k: pltpu.SemaphoreType.DMA(k)
    shaped = lambda shape, dtype=BF16: jax.ShapeDtypeStruct(shape, dtype)
    sub = PIECE // 2
    piece = (sub, PIECE)
    count = (number * 6 + 2) * 2
    land_rows = max(2 * (tokens + EXPERTS), PIECE + 16)
    return pl.pallas_call(
        functools.partial(backward_kernel, n, length, capp),
        in_specs=[smem] + [hbm] * 17 + [vmem] * 5,
        out_specs=[hbm] * 7 + [vmem, vmem],
        out_shape=[
            shaped((count,) + piece),
            shaped((count,) + piece),
            shaped((number * 6, PIECE, PIECE)),
            shaped(xs.shape),
            shaped(xs.shape),
            shaped((8, 2 * (tokens + EXPERTS), PIECE)),
            shaped((8, 2 * tokens, PIECE)),
            shaped((tokens, width), F32),
            shaped((tokens, width), F32),
        ],
        scratch_shapes=[
            pltpu.VMEM((RING,) + piece, BF16),
            pltpu.VMEM((RING,) + piece, BF16),
            pltpu.VMEM((2,) + piece, BF16),
            pltpu.VMEM((4, land_rows, PIECE), BF16),
            pltpu.VMEM((2, land_rows, PIECE), BF16),
            pltpu.VMEM((land_rows, PIECE), BF16),
            pltpu.VMEM((4, 2 * tokens, PIECE), BF16),
            pltpu.VMEM((2, 2 * tokens, PIECE), BF16),
            pltpu.VMEM((2 * tokens, PIECE), BF16),
            pltpu.VMEM((2, 2 * tokens, PIECE), BF16),
            pltpu.VMEM((2 * PIECE, PIECE), BF16),
            pltpu.VMEM((n, tokens, 128), BF16),
            pltpu.VMEM((n, tokens, PACK), BF16),
            dma(RING),
            dma(RING),
            dma(RING),
            dma(RING),
            dma(RING),
            dma(count),
            dma(RING),
            dma(2),
            dma(n - 1),
            dma(n - 1),
            dma(n - 1),
            dma(n - 1),
            dma(4, 6, 4),
            dma(2),
            pltpu.SemaphoreType.REGULAR((3,)),
            dma(11),
            dma(2),
            dma(2),
            dma(2, 6),
            dma(3),
            dma(2, 2),
            dma(2, 8),
        ],
        compiler_params=params(63, collective_id=0, has_side_effects=True),
        cost_estimate=cost(6e10, 1e9),
        name="backward_step",
    )(ends, xs, gs, gates, w_gate, w_up, w_down, cxs, rest, full, weights, packs, table, cot, wo, attn, x, h_attn, h, middle, wr, gains, lse)


def local(
    inputs,
    cotangent,
    doc_lengths,
    routes,
    attn_gain,
    ffn_gain,
    w_query,
    key_weight,
    value_weight,
    w_out,
    w_router,
    w_gate,
    w_up,
    w_down,
):
    rows = inputs.shape[2]
    width = inputs.shape[3]
    n = lax.axis_size("ctx")
    fsdp = lax.axis_size("fsdp")
    me, mine = lax.axis_index("ctx"), lax.axis_index("fsdp")
    tokens = 2 * rows
    length = tokens * n
    experts_here = w_gate.shape[0]
    number = experts_here // 2
    capacity = 5 * tokens * TOP // (4 * EXPERTS)
    capp = -(-capacity // 16) * 16
    shard = width // fsdp
    heads = QUERY_HEADS // n
    head_lanes = heads * HEAD_DIMENSION
    copies = n // KEY_VALUE_HEADS
    bits = group_bits(fsdp)

    x = inputs.reshape(tokens, width)
    cot = cotangent.reshape(tokens, width)
    side = me % 2
    base = (side * number).astype(jnp.int32).reshape(1)
    first = (mine * experts_here + side * number).astype(jnp.int32).reshape(1)
    index = jnp.stack([side * number, (1 - side) * number]).astype(jnp.int32)
    ends = jnp.cumsum(doc_lengths[0])[:3].astype(jnp.int32)
    table = jnp.asarray(rotary_table(length))

    out_part = w_out.reshape(shard // head_lanes, head_lanes, width)
    if head_lanes < 128:
        out_part = jnp.pad(out_part, ((0, 0), (0, 128 - head_lanes), (0, 0)))
    merge = lambda a: a.reshape(number, -1, a.shape[-1])

    if n == 8 and fsdp == 4:
        packs, h_attn, weights, wo, wr, cxs, gains = front(
            w_query,
            key_weight,
            value_weight,
            out_part,
            w_router,
            attn_gain.reshape(1, shard),
            ffn_gain.reshape(1, shard),
            x,
            table.reshape(2, n, rows, 256),
            routes.reshape(tokens, TOP),
            cot,
            capacity,
            n,
        )
        wo, wr = wo.reshape(n, 128, width), wr.reshape(width, 128)
        packs = packs.reshape(n, 2, rows, PACK)
        attn, lse, full, cx_rest = attend(ends, packs, cxs, length)
        middle, h_ffn, attn, xs, gs, gates = mid_step(attn.reshape(n, tokens, 128), cxs, cx_rest, wo, wr, x, gains[1:2], number, capp, n)
        own, other, _, _, _, _, _, grad_x, mixed = backward_step(
            ends,
            merge(xs),
            merge(gs),
            merge(gates),
            w_gate,
            w_up,
            w_down,
            cxs,
            cx_rest,
            full,
            weights,
            packs,
            table,
            cot,
            wo,
            attn,
            x,
            h_attn,
            h_ffn,
            middle,
            wr,
            gains,
            lse,
            n,
            length,
            capp,
        )
        own, other = own.reshape(-1, PIECE, PIECE), other.reshape(-1, PIECE, PIECE)
        shapes = [w.shape for w in (w_gate, w_up, w_down)]
        outs = tail(index, own, other, mixed, grad_x, shapes, shard)
        return (
            outs[3].reshape(inputs.shape),
            outs[4].reshape(inputs.shape),
            outs[10].reshape(shard),
            outs[11].reshape(shard),
            outs[5],
            outs[6],
            outs[7],
            outs[8],
            outs[9],
            outs[0],
            outs[1],
            outs[2],
        )

    else:
        own_table = lax.dynamic_slice_in_dim(table.reshape(2, n, rows, 256), me, 1, 1).reshape(tokens, 256)
        query_part = w_query.reshape(shard, n, head_lanes)
        if head_lanes < 128:
            query_part = jnp.pad(query_part, ((0, 0), (0, 0), (0, 128 - head_lanes)))
        key_part = jnp.repeat(key_weight.reshape(shard, KEY_VALUE_HEADS, HEAD_DIMENSION), copies, 1)
        value_part = jnp.repeat(value_weight.reshape(shard, KEY_VALUE_HEADS, HEAD_DIMENSION), copies, 1)
        packed = jnp.concatenate([query_part, key_part, value_part], -1).reshape(shard, n * PACK)
        padding = 2 * 16 * (shard // 32 + 1) - shard
        gains = jnp.pad(jnp.stack([attn_gain, ffn_gain]), ((0, padding - 2), (0, n * PACK - shard)))
        packed = jnp.concatenate([packed, gains], 0)
        router_part = jnp.pad(w_router, ((0, 0), (0, 128 - EXPERTS)))
        weights = lax.all_gather(packed, "fsdp", axis=0)
        gain_one = weights[:, shard, :shard].reshape(1, width).astype(F32)
        gain_two = weights[:, shard + 1, :shard].reshape(1, width).astype(F32)
        wo = lax.all_gather(out_part, "fsdp", axis=0, tiled=True)
        wr = lax.all_gather(router_part, "fsdp", axis=0, tiled=True)
        cxs = group_gather(prep(routes.reshape(tokens, TOP), cot, capacity), bits)
        packs, h_attn = qkv(x, gain_one, weights, own_table, shard, n)
        packs = lax.all_to_all(packs, "ctx", split_axis=0, concat_axis=0, tiled=True).reshape(n, 2, rows, PACK)
        attn, lse, full = attn_forward(ends, packs, length)
        attn = lax.all_to_all(attn.reshape(n, tokens, 128), "ctx", split_axis=0, concat_axis=0, tiled=True)
        middle, h_ffn = middle_step(attn, wo, x, gain_two)
        xs, gs, gates = gather_rows(first, group_gather(h_ffn, bits), cxs, jnp.transpose(wr), number, capp)
        slots = cxs[:, tokens:]
    xs, gs, gates = merge(xs), merge(gs), merge(gates)
    pieces, outs, back, dgates = expert_step(base, xs, gs, gates, w_gate, w_up, w_down)
    y_part, gx_part = combine(first, slots, outs, back, dgates, tokens, capp)
    pieces = pieces.reshape(number * 6, PIECE, PIECE)
    gx = group_reduce(gx_part, bits)
    grad_middle, dwo, grad_attn, dwr, dgain_two = home_step(gx, h_ffn, middle, cot, wr, wo, gain_two, attn)
    grad_attn = lax.all_to_all(grad_attn, "ctx", split_axis=0, concat_axis=0, tiled=True).reshape(n, 2, rows, 128)
    grads = attn_backward(ends, packs, grad_attn, lse, full, table, length)
    grads = lax.all_to_all(grads.reshape(n, tokens, PACK), "ctx", split_axis=0, concat_axis=0, tiled=True)
    dw, grad_x, dgain_one = final_step(grads, weights, h_attn, x, gain_one, grad_middle, shard)
    mixed = middle + RESIDUAL * group_reduce(y_part, bits).astype(F32)
    own = line_sum(pieces, n)
    other = swap(own, "ctx", 1)
    scatter = lambda a: lax.psum(lax.psum_scatter(a, "fsdp", scatter_dimension=0, tiled=True), "ctx").astype(F32)
    dwo = scatter(dwo)[:, :head_lanes, :].reshape(shard, width)
    small = jnp.concatenate([dwr[:, :EXPERTS], dgain_two.reshape(width, 1).astype(BF16)], 1)
    small = scatter(jnp.pad(small, ((0, 0), (0, 127 - EXPERTS))))
    dwr, dgain_two = small[:, :EXPERTS], small[:, EXPERTS]
    dw = scatter(dw).reshape(shard, n, PACK)
    dgain_one = scatter(dgain_one.reshape(width).astype(BF16))

    outs = widen(index, own, other, [w.shape for w in (w_gate, w_up, w_down)])
    fold = lambda a: a.reshape(shard, KEY_VALUE_HEADS, copies, HEAD_DIMENSION).sum(2).reshape(shard, -1)
    return (
        mixed.reshape(inputs.shape),
        grad_x.reshape(inputs.shape),
        dgain_one,
        dgain_two,
        dw[:, :, :head_lanes].reshape(shard, -1),
        fold(dw[:, :, 128:192]),
        fold(dw[:, :, 192:256]),
        dwo,
        dwr,
        outs[0],
        outs[1],
        outs[2],
    )


def solution(mesh):
    tokens = P("fsdp", None, "ctx", None)
    one, two, three = P("fsdp"), P("fsdp", None), P("fsdp", None, None)
    return jax.shard_map(
        local,
        mesh=mesh,
        in_specs=(tokens, tokens, two, tokens, one, one, two, two, two, two, two, three, three, three),
        out_specs=(tokens, tokens, one, one, two, two, two, two, two, three, three, three),
        check_vma=False,
    )
```

```python
import functools

import jax
import jax.numpy as jnp
import numpy as np
from jax import lax
from jax.experimental import pallas as pl
from jax.experimental.pallas import tpu as pltpu
from jax.sharding import PartitionSpec as P

QUERY_HEADS = 16
KEY_VALUE_HEADS = 8
HEAD_DIMENSION = 64
EXPERTS = 32
TOP = 8

ATTN_SCALE = 0.015625
RESIDUAL = 0.22
NORM_EPS = 1e-06
ROPE_BASE = 10000.0
MASKED = -1e30

F32 = jnp.float32
BF16 = jnp.bfloat16
MIB = 1 << 20
NT = (((1,), (1,)), ((), ()))
TN = (((0,), (0,)), ((), ()))
BLK = 256
PACK = 256


def dot(a, b, dims=None):
    if dims is None:
        return jnp.dot(a, b, preferred_element_type=F32)
    return lax.dot_general(a, b, dims, preferred_element_type=F32)


def params(limit=56, **kw):
    return pltpu.CompilerParams(vmem_limit_bytes=limit * MIB, **kw)


def cost(flops, bytes_accessed):
    return pl.CostEstimate(flops=int(flops), bytes_accessed=int(bytes_accessed), transcendentals=0)


def lane_iota(shape):
    return lax.broadcasted_iota(jnp.int32, shape, len(shape) - 1)


def row_iota(shape):
    return lax.broadcasted_iota(jnp.int32, shape, len(shape) - 2)


def rotary_table(length):
    half = length // 2
    order = np.arange(half, dtype=np.float32)
    positions = np.concatenate([order, length - 1 - order]).astype(np.float32)
    m = np.arange(HEAD_DIMENSION // 2, dtype=np.float64)
    frequency = (ROPE_BASE ** (-2.0 * m / HEAD_DIMENSION)).astype(np.float32)
    angles = (positions[:, None] * frequency[None, :]).astype(np.float64)
    cosine, sine = np.cos(angles), np.sin(angles)
    cos_head = np.concatenate([cosine, cosine], -1)
    sin_head = np.concatenate([-sine, sine], -1)
    return np.concatenate([cos_head, cos_head, sin_head, sin_head], -1).astype(np.float32)


def turn(v, table, direction):
    lanes = lane_iota(v.shape)
    cosine = jnp.concatenate([table[:, :128], table[:, :128]], -1)
    sine = jnp.concatenate([table[:, 128:], table[:, 128:]], -1)
    turned = lanes < 3 * HEAD_DIMENSION
    swapped = jnp.where(lanes % HEAD_DIMENSION < HEAD_DIMENSION // 2, pltpu.roll(v, PACK - 32, 1), pltpu.roll(v, 32, 1))
    return jnp.where(turned, v * cosine + direction * (swapped * sine), v)


def norm_parts(values):
    inv_rms = lax.rsqrt(jnp.mean(values * values, -1, keepdims=True) + NORM_EPS)
    return values * inv_rms, inv_rms


def norm_back(grad_normed, normed, inv_rms):
    return inv_rms * (grad_normed - normed * jnp.mean(grad_normed * normed, -1, keepdims=True))


def prep_kernel(cap, routes_ref, cot_ref, out_ref):
    tokens, width = cot_ref.shape
    routes = routes_ref[...]
    earlier = (lane_iota((tokens, tokens)) < row_iota((tokens, tokens))).astype(BF16)
    experts = lane_iota((tokens, 128))
    base = jnp.zeros((1, 128), F32)
    plus = jnp.zeros((tokens, 128), F32)
    for k in range(TOP):
        chosen = experts == routes[:, k : k + 1]
        ones = chosen.astype(F32)
        slot = dot(earlier, ones.astype(BF16)) + base
        plus = plus + jnp.where(chosen & (slot < cap), slot + 1.0, 0.0)
        base = base + jnp.sum(ones, 0, keepdims=True)
    out_ref[:tokens, :] = cot_ref[...].astype(BF16)
    slots = (jnp.transpose(plus) - 1.0)[:EXPERTS, :]
    out_ref[tokens:, :] = jnp.concatenate([slots, jnp.zeros((EXPERTS, width - tokens), F32)], -1).astype(BF16)


def prep(routes, cot, cap):
    tokens, width = cot.shape
    return pl.pallas_call(
        functools.partial(prep_kernel, cap),
        out_shape=jax.ShapeDtypeStruct((tokens + EXPERTS, width), BF16),
        compiler_params=params(),
        cost_estimate=cost(1e9, 2e6),
        name="prep",
    )(routes, cot)


def qkv_kernel(shard, x_ref, gain_ref, w_ref, table_ref, out_ref, h_ref):
    @pl.when(pl.program_id(0) == 0)
    def _():
        normed, _ = norm_parts(x_ref[...])
        h_ref[...] = (normed * gain_ref[...]).astype(BF16)

    total = None
    for f in range(w_ref.shape[0]):
        part = dot(h_ref[:, f * shard : (f + 1) * shard], w_ref[f, :shard, :])
        total = part if total is None else total + part
    for d in range(out_ref.shape[0]):
        out_ref[d] = turn(total[:, d * PACK : (d + 1) * PACK], table_ref[...], 1.0).astype(BF16)


def qkv(x, gain, weights, table, shard, n):
    tokens, width = x.shape
    fsdp, padded, _ = weights.shape
    return pl.pallas_call(
        functools.partial(qkv_kernel, shard),
        grid=(n // 2,),
        in_specs=[
            pl.BlockSpec((tokens, width), lambda i: (0, 0)),
            pl.BlockSpec((1, width), lambda i: (0, 0)),
            pl.BlockSpec((fsdp, padded, 2 * PACK), lambda i: (0, 0, i)),
            pl.BlockSpec((tokens, 256), lambda i: (0, 0)),
        ],
        out_specs=[
            pl.BlockSpec((2, tokens, PACK), lambda i: (i, 0, 0)),
            pl.BlockSpec((tokens, width), lambda i: (0, 0)),
        ],
        out_shape=[
            jax.ShapeDtypeStruct((n, tokens, PACK), BF16),
            jax.ShapeDtypeStruct((tokens, width), BF16),
        ],
        compiler_params=params(),
        cost_estimate=cost(2 * tokens * width * n * PACK, 8e6),
        name="qkv",
    )(x, gain, weights, table)


def pair_keys(kv):
    other = pltpu.roll(kv, 64, 1)
    low = lane_iota(kv.shape) < 64
    return jnp.where(low, kv, other), jnp.where(low, other, kv)


def stack_heads(q):
    low = lane_iota(q.shape) < 64
    zero = jnp.zeros_like(q)
    return jnp.concatenate([jnp.where(low, q, zero), jnp.where(low, zero, q)], 0)


def fold_heads(stacked):
    rows = stacked.shape[0] // 2
    return jnp.where(lane_iota((rows, 128)) < 64, stacked[:rows], stacked[rows:])


def query_rows(ends_ref, block, length):
    half = length // 2
    lanes = lane_iota((1, 2 * BLK))
    index = block * BLK + jnp.where(lanes < BLK, lanes, lanes - BLK)
    position = jnp.where(index < half, index, length + half - 1 - index)
    start = jnp.zeros_like(position)
    for j in range(3):
        end = ends_ref[j]
        start = jnp.where(position >= end, jnp.maximum(start, end), start)
    return position, start


def key_position(kb, length):
    half = length // 2
    index = kb * BLK + row_iota((BLK, 1))
    return jnp.where(index < half, index, length + half - 1 - index)


def block_loop(block, per_half, body, init):
    late = block >= per_half
    inner = jnp.where(late, block - per_half, block)
    count = jnp.where(late, 2 * per_half - inner, inner + 1)

    def step(j, carry):
        kb = jnp.where(late & (j >= per_half), inner + j, j)
        return body(kb, carry)

    return lax.fori_loop(0, count, step, init)


def load_package(pack_ref, c, h):
    return pack_ref[c, h].astype(F32)


def attn_forward_kernel(length, ends_ref, q_ref, pack_ref, out_ref, lse_ref, full_ref, keys, values_t, acc):
    block = pl.program_id(0)
    half = length // 2
    n, _, rows, _ = pack_ref.shape

    @pl.when(block == 0)
    def _():
        for h in range(2):
            for c in range(n):
                kk, vv = pair_keys(pack_ref[c, h, :, 128:256].astype(F32))
                at = h * half + c * rows
                keys[at : at + rows, :] = kk.astype(BF16)
                if rows % 128 == 0:
                    values_t[:, at : at + rows] = jnp.transpose(vv).astype(BF16)
        if rows % 128 != 0:
            for h in range(2):
                for c in range(0, n, 2):
                    pair = jnp.concatenate([pack_ref[c, h, :, 128:256], pack_ref[c + 1, h, :, 128:256]], 0)
                    _, vv = pair_keys(pair.astype(F32))
                    at = h * half + c * rows
                    values_t[:, at : at + 2 * rows] = jnp.transpose(vv).astype(BF16)

    q = q_ref[...].reshape(BLK, PACK)[:, :128]
    q2 = stack_heads(q)
    position, start = query_rows(ends_ref, block, length)
    acc[...] = jnp.zeros_like(acc)

    def body(kb, carry):
        peak, total = carry
        at = pl.multiple_of(kb * BLK, BLK)
        scores = dot(keys[pl.ds(at, BLK), :], q2, NT) * ATTN_SCALE
        where = key_position(kb, length)
        scores = jnp.where((where <= position) & (where >= start), scores, MASKED)
        new_peak = jnp.maximum(peak, jnp.max(scores, 0, keepdims=True))
        weights = jnp.exp(scores - new_peak)
        fade = jnp.exp(peak - new_peak)
        total = total * fade + jnp.sum(weights, 0, keepdims=True)
        acc[...] = acc[...] * fade + dot(values_t[:, pl.ds(at, BLK)], weights.astype(BF16))
        return new_peak, total

    init = (jnp.full((1, 2 * BLK), MASKED, F32), jnp.zeros((1, 2 * BLK), F32))
    peak, total = block_loop(block, half // BLK, body, init)
    result = acc[...] / total
    full_ref[0] = result
    lse_ref[0] = peak + jnp.log(total)
    folded = fold_heads(jnp.transpose(result)).astype(BF16)
    out_ref[...] = folded.reshape(out_ref.shape)


def attn_forward(ends, packs, length):
    n, _, rows, _ = packs.shape
    blocks, per = length // BLK, BLK // rows
    per_half = blocks // 2
    tiles = lambda i, ends: (lax.rem(i, per_half), i // per_half, 0, 0)
    return pl.pallas_call(
        functools.partial(attn_forward_kernel, length),
        grid_spec=pltpu.PrefetchScalarGridSpec(
            num_scalar_prefetch=1,
            grid=(blocks,),
            in_specs=[
                pl.BlockSpec((per, 1, rows, PACK), tiles),
                pl.BlockSpec(packs.shape, lambda i, ends: (0, 0, 0, 0)),
            ],
            out_specs=[
                pl.BlockSpec((per, 1, rows, 128), tiles),
                pl.BlockSpec((1, 1, 2 * BLK), lambda i, ends: (i, 0, 0)),
                pl.BlockSpec((1, 128, 2 * BLK), lambda i, ends: (i, 0, 0)),
            ],
            scratch_shapes=[
                pltpu.VMEM((length, 128), BF16),
                pltpu.VMEM((128, length), BF16),
                pltpu.VMEM((128, 2 * BLK), F32),
            ],
        ),
        out_shape=[
            jax.ShapeDtypeStruct((n, 2, rows, 128), BF16),
            jax.ShapeDtypeStruct((blocks, 1, 2 * BLK), F32),
            jax.ShapeDtypeStruct((blocks, 128, 2 * BLK), F32),
        ],
        compiler_params=params(),
        cost_estimate=cost(1.5e10, 6e6),
        name="attn_forward",
    )(ends, packs, packs)


def attn_backward_kernel(length, ends_ref, q_ref, g_ref, pack_ref, lse_ref, full_ref, table_ref, out_ref, keys, values, keys_t, grad_q, grad_k, grad_v, acc):
    block = pl.program_id(0)
    half = length // 2
    n, _, rows, _ = pack_ref.shape

    @pl.when(block == 0)
    def _():
        for h in range(2):
            for c in range(n):
                kk, vv = pair_keys(pack_ref[c, h, :, 128:256].astype(F32))
                at = h * half + c * rows
                keys[at : at + rows, :] = kk.astype(BF16)
                values[at : at + rows, :] = vv.astype(BF16)
        for b in range(length // BLK):
            keys_t[:, b * BLK : (b + 1) * BLK] = jnp.transpose(keys[b * BLK : (b + 1) * BLK, :].astype(F32)).astype(BF16)
        grad_k[...] = jnp.zeros_like(grad_k)
        grad_v[...] = jnp.zeros_like(grad_v)

    q2 = stack_heads(q_ref[...].reshape(BLK, PACK)[:, :128])
    g2 = stack_heads(g_ref[...].reshape(BLK, 128))
    position, start = query_rows(ends_ref, block, length)
    lse = lse_ref[0]
    delta = jnp.sum(jnp.transpose(g2.astype(F32)) * full_ref[0], 0, keepdims=True)
    acc[...] = jnp.zeros_like(acc)

    def body(kb, carry):
        at = pl.multiple_of(kb * BLK, BLK)
        scores = dot(keys[pl.ds(at, BLK), :], q2, NT) * ATTN_SCALE
        where = key_position(kb, length)
        probs = jnp.where((where <= position) & (where >= start), jnp.exp(scores - lse), 0.0)
        grad_probs = dot(values[pl.ds(at, BLK), :], g2, NT)
        grad_scores = (probs * (grad_probs - delta)).astype(BF16)
        acc[...] += dot(keys_t[:, pl.ds(at, BLK)], grad_scores)
        grad_k[pl.ds(at, BLK), :] += dot(grad_scores, q2)
        grad_v[pl.ds(at, BLK), :] += dot(probs.astype(BF16), g2)
        return carry

    block_loop(block, half // BLK, body, 0)
    grad_q[pl.ds(pl.multiple_of(block * BLK, BLK), BLK), :] = fold_heads(jnp.transpose(acc[...]))

    @pl.when(block == length // BLK - 1)
    def _():
        for h in range(2):
            for c in range(n):
                at = slice(h * half + c * rows, h * half + (c + 1) * rows)
                kk = grad_k[at, :]
                vv = grad_v[at, :]
                kk = (kk + pltpu.roll(kk, 64, 1)) * ATTN_SCALE
                vv = vv + pltpu.roll(vv, 64, 1)
                both = jnp.where(lane_iota(kk.shape) < 64, kk, vv)
                package = jnp.concatenate([grad_q[at, :] * ATTN_SCALE, both], -1)
                out_ref[c, h] = turn(package, table_ref[at, :], -1.0).astype(BF16)


def attn_backward(ends, packs, grads, lse, full, table, length):
    n, _, rows, _ = packs.shape
    blocks, per = length // BLK, BLK // rows
    per_half = blocks // 2
    tiles = lambda i, ends: (lax.rem(i, per_half), i // per_half, 0, 0)
    return pl.pallas_call(
        functools.partial(attn_backward_kernel, length),
        grid_spec=pltpu.PrefetchScalarGridSpec(
            num_scalar_prefetch=1,
            grid=(blocks,),
            in_specs=[
                pl.BlockSpec((per, 1, rows, PACK), tiles),
                pl.BlockSpec((per, 1, rows, 128), tiles),
                pl.BlockSpec(packs.shape, lambda i, ends: (0, 0, 0, 0)),
                pl.BlockSpec((1, 1, 2 * BLK), lambda i, ends: (i, 0, 0)),
                pl.BlockSpec((1, 128, 2 * BLK), lambda i, ends: (i, 0, 0)),
                pl.BlockSpec(table.shape, lambda i, ends: (0, 0)),
            ],
            out_specs=pl.BlockSpec(packs.shape, lambda i, ends: (0, 0, 0, 0)),
            scratch_shapes=[
                pltpu.VMEM((length, 128), BF16),
                pltpu.VMEM((length, 128), BF16),
                pltpu.VMEM((128, length), BF16),
                pltpu.VMEM((length, 128), F32),
                pltpu.VMEM((length, 128), F32),
                pltpu.VMEM((length, 128), F32),
                pltpu.VMEM((128, 2 * BLK), F32),
            ],
        ),
        out_shape=jax.ShapeDtypeStruct(packs.shape, BF16),
        compiler_params=params(),
        cost_estimate=cost(3e10, 8e6),
        name="attn_backward",
    )(ends, packs, grads, packs, lse, full, table)


def middle_kernel(attn_ref, wo_ref, x_ref, gain_ref, middle_ref, h_ref):
    total = None
    for c in range(attn_ref.shape[0]):
        part = dot(attn_ref[c], wo_ref[c])
        total = part if total is None else total + part
    middle = x_ref[...] + RESIDUAL * total
    middle_ref[...] = middle
    normed, _ = norm_parts(middle)
    h_ref[...] = (normed * gain_ref[...]).astype(BF16)


def middle_step(attn, wo, x, gain):
    tokens, width = x.shape
    return pl.pallas_call(
        middle_kernel,
        out_shape=[jax.ShapeDtypeStruct((tokens, width), F32), jax.ShapeDtypeStruct((tokens, width), BF16)],
        compiler_params=params(),
        cost_estimate=cost(2 * tokens * width * width, 5e6),
        name="middle",
    )(attn, wo, x, gain)


def own_row(table, row):
    return jnp.sum(jnp.where(row_iota(table.shape) == row, table, 0.0), 0, keepdims=True)


def one_hot(slots, first, number, capp):
    tokens = slots.shape[1]
    order = row_iota((capp, tokens)).astype(F32)
    return [(order == own_row(slots, first + j)).astype(F32) for j in range(number)]


def gather_kernel(number, capp, first_ref, h_ref, cx_ref, wrt_ref, x_ref, g_ref, gate_ref):
    tokens = h_ref.shape[1]
    first = first_ref[0]
    h = h_ref[0]
    slots = cx_ref[0, tokens:, :tokens].astype(F32)
    logits = dot(wrt_ref[...], h, NT)[:EXPERTS, :]
    raw = jnp.exp(logits - jnp.max(logits, 0, keepdims=True))
    router = raw / jnp.sum(raw, 0, keepdims=True)
    hots = one_hot(slots, first, number, capp)
    places = jnp.concatenate(hots, 0).astype(BF16)
    rows = dot(places, h).astype(BF16)
    grads = dot(places, cx_ref[0, :tokens, :]).astype(BF16)
    for j in range(number):
        at = slice(j * capp, (j + 1) * capp)
        x_ref[j, 0] = rows[at]
        g_ref[j, 0] = grads[at]
        gate = jnp.sum(hots[j] * own_row(router, first + j), 1, keepdims=True)
        gate_ref[j, 0] = jnp.broadcast_to(gate, (capp, 128))


def gather_rows(first, hs, cxs, wrt, number, capp):
    nb, tokens, width = hs.shape
    return pl.pallas_call(
        functools.partial(gather_kernel, number, capp),
        grid_spec=pltpu.PrefetchScalarGridSpec(
            num_scalar_prefetch=1,
            grid=(nb,),
            in_specs=[
                pl.BlockSpec((1, tokens, width), lambda b, f: (b, 0, 0)),
                pl.BlockSpec((1, tokens + EXPERTS, width), lambda b, f: (b, 0, 0)),
                pl.BlockSpec(wrt.shape, lambda b, f: (0, 0)),
            ],
            out_specs=[
                pl.BlockSpec((number, 1, capp, width), lambda b, f: (0, b, 0, 0)),
                pl.BlockSpec((number, 1, capp, width), lambda b, f: (0, b, 0, 0)),
                pl.BlockSpec((number, 1, capp, 128), lambda b, f: (0, b, 0, 0)),
            ],
        ),
        out_shape=[
            jax.ShapeDtypeStruct((number, nb, capp, width), BF16),
            jax.ShapeDtypeStruct((number, nb, capp, width), BF16),
            jax.ShapeDtypeStruct((number, nb, capp, 128), F32),
        ],
        compiler_params=params(),
        cost_estimate=cost(4 * nb * number * capp * tokens * width, 2e7),
        name="gather_rows",
    )(first, hs, cxs, wrt)


PIECE = 512


def expert_kernel(base_ref, x_ref, g_ref, gate_ref, wg_ref, wu_ref, wd_ref, piece_ref, out_ref, rows_ref, dg_ref):
    x = x_ref[0]
    gate = gate_ref[0][:, :1]
    grad_ffn = RESIDUAL * g_ref[0].astype(F32)
    go = (gate * grad_ffn).astype(BF16)
    part = wg_ref.shape[2] // 2
    out = rows = None
    for chunk in range(2):
        at = slice(chunk * part, (chunk + 1) * part)
        wg, wu, wd = wg_ref[0, :, at], wu_ref[0, :, at], wd_ref[0, at, :]
        pre_gate = dot(x, wg)
        pre_up = dot(x, wu)
        sig = jax.nn.sigmoid(pre_gate)
        hidden = (pre_gate * sig * pre_up).astype(BF16)
        out_part = dot(hidden, wd)
        grad_hidden = dot(go, wd, NT)
        grad_gate = (grad_hidden * pre_up * sig * (1.0 + pre_gate * (1.0 - sig))).astype(BF16)
        grad_up = (grad_hidden * pre_gate * sig).astype(BF16)
        row_part = dot(grad_gate, wg, NT) + dot(grad_up, wu, NT)
        dwg = dot(x, grad_gate, TN).astype(BF16)
        dwu = dot(x, grad_up, TN).astype(BF16)
        dwd = dot(hidden, go, TN).astype(BF16)
        for half in range(2):
            side = slice(half * PIECE, (half + 1) * PIECE)
            piece_ref[0, half, :, at] = dwg[side]
            piece_ref[0, 2 + half, :, at] = dwu[side]
            piece_ref[0, 4 + half, at, :] = dwd[:, side]
        out = out_part if out is None else out + out_part
        rows = row_part if rows is None else rows + row_part
    out = out.astype(BF16).astype(F32)
    out_ref[0] = (gate * out).astype(BF16)
    rows_ref[0] = rows.astype(BF16)
    grad = jnp.sum(grad_ffn * out, 1, keepdims=True)
    dg_ref[0] = jnp.broadcast_to(grad, dg_ref.shape[1:])


def expert_step(base, xs, gs, gates, w_gate, w_up, w_down):
    number, rows, width = xs.shape
    ff = w_gate.shape[2]
    row = lambda e, b: (e, 0, 0)
    weight = lambda e, b: (b[0] + e, 0, 0)
    return pl.pallas_call(
        expert_kernel,
        grid_spec=pltpu.PrefetchScalarGridSpec(
            num_scalar_prefetch=1,
            grid=(number,),
            in_specs=[
                pl.BlockSpec((1, rows, width), row),
                pl.BlockSpec((1, rows, width), row),
                pl.BlockSpec((1, rows, 128), row),
                pl.BlockSpec((1, width, ff), weight),
                pl.BlockSpec((1, width, ff), weight),
                pl.BlockSpec((1, ff, width), weight),
            ],
            out_specs=[
                pl.BlockSpec((1, 6, PIECE, PIECE), lambda e, b: (e, 0, 0, 0)),
                pl.BlockSpec((1, rows, width), row),
                pl.BlockSpec((1, rows, width), row),
                pl.BlockSpec((1, rows, 128), row),
            ],
        ),
        out_shape=[
            jax.ShapeDtypeStruct((number, 6, PIECE, PIECE), BF16),
            jax.ShapeDtypeStruct((number, rows, width), BF16),
            jax.ShapeDtypeStruct((number, rows, width), BF16),
            jax.ShapeDtypeStruct((number, rows, 128), F32),
        ],
        compiler_params=params(60),
        cost_estimate=cost(18 * number * rows * width * ff, 5e7),
        name="expert_step",
    )(base, xs, gs, gates, w_gate, w_up, w_down)


def combine_kernel(number, capp, first_ref, slot_ref, outs, rows, grads, y_ref, gx_ref):
    tokens = y_ref.shape[1]
    width = y_ref.shape[2]
    first = first_ref[0]
    slots = slot_ref[0][:, :tokens].astype(F32)
    hots = one_hot(slots, first, number, capp)
    places = jnp.concatenate(hots, 0).astype(BF16)
    y_ref[0] = dot(places, outs[:, 0].reshape(number * capp, width), TN).astype(BF16)
    gx_ref[0, :tokens] = dot(places, rows[:, 0].reshape(number * capp, width), TN).astype(BF16)
    extra = jnp.zeros((EXPERTS, 2 * tokens), F32)
    for j in range(number):
        grad = jnp.sum(hots[j] * grads[j, 0][:, :1], 0, keepdims=True)
        high = grad.astype(BF16).astype(F32)
        both = jnp.concatenate([high, grad - high], 1)
        extra = jnp.where(row_iota(extra.shape) == first + j, both, extra)
    rest = jnp.zeros((EXPERTS, width - 2 * tokens), F32)
    gx_ref[0, tokens:] = jnp.concatenate([extra, rest], 1).astype(BF16)


def combine(first, slots, outs, rows, grads, tokens, capp):
    number = outs.shape[0]
    nb, _, width = slots.shape
    split = lambda a: a.reshape(number, nb, capp, a.shape[-1])
    wide = pl.BlockSpec((number, 1, capp, width), lambda b, f: (0, b, 0, 0))
    thin = pl.BlockSpec((number, 1, capp, 128), lambda b, f: (0, b, 0, 0))
    return pl.pallas_call(
        functools.partial(combine_kernel, number, capp),
        grid_spec=pltpu.PrefetchScalarGridSpec(
            num_scalar_prefetch=1,
            grid=(nb,),
            in_specs=[pl.BlockSpec((1, EXPERTS, width), lambda b, f: (b, 0, 0))] + [wide, wide, thin],
            out_specs=[
                pl.BlockSpec((1, tokens, width), lambda b, f: (b, 0, 0)),
                pl.BlockSpec((1, tokens + EXPERTS, width), lambda b, f: (b, 0, 0)),
            ],
        ),
        out_shape=[
            jax.ShapeDtypeStruct((nb, tokens, width), BF16),
            jax.ShapeDtypeStruct((nb, tokens + EXPERTS, width), BF16),
        ],
        compiler_params=params(),
        cost_estimate=cost(4 * nb * number * capp * tokens * width, 2e7),
        name="combine",
    )(first, slots, split(outs), split(rows), split(grads))


def home_kernel(gx_ref, h_ref, middle_ref, cot_ref, wr_ref, wo_ref, gain_ref, attn_ref, grad_middle_ref, dwo_ref, ga_ref, dwr_ref, dgain_ref):
    tokens, width = h_ref.shape
    h = h_ref[...]
    gain = gain_ref[...]
    extra = gx_ref[tokens:, :].astype(F32)
    grad_router = extra[:, :tokens] + extra[:, tokens : 2 * tokens]
    grad_router = jnp.transpose(jnp.concatenate([grad_router, jnp.zeros((128 - EXPERTS, tokens), F32)], 0))
    logits = dot(h, wr_ref[...])
    logits = jnp.where(lane_iota(logits.shape) < EXPERTS, logits, MASKED)
    raw = jnp.exp(logits - jnp.max(logits, -1, keepdims=True))
    router = raw / jnp.sum(raw, -1, keepdims=True)
    grad_logits = (router * (grad_router - jnp.sum(router * grad_router, -1, keepdims=True))).astype(BF16)
    dwr_ref[...] = dot(h, grad_logits, TN).astype(BF16)
    grad_h = gx_ref[:tokens, :].astype(F32) + dot(grad_logits, wr_ref[...], NT)
    normed, scale = norm_parts(middle_ref[...])
    dgain_ref[...] = jnp.sum(grad_h * normed, 0, keepdims=True)
    grad_middle = cot_ref[...] + norm_back(grad_h * gain, normed, scale)
    grad_middle_ref[...] = grad_middle
    grad_branch = (RESIDUAL * grad_middle).astype(BF16)
    for c in range(attn_ref.shape[0]):
        dwo_ref[c] = dot(attn_ref[c], grad_branch, TN).astype(BF16)
        ga_ref[c] = dot(grad_branch, wo_ref[c], NT).astype(BF16)


def home_step(gx, h, middle, cot, wr, wo, gain, attn):
    tokens, width = h.shape
    n = attn.shape[0]
    return pl.pallas_call(
        home_kernel,
        out_shape=[
            jax.ShapeDtypeStruct((tokens, width), F32),
            jax.ShapeDtypeStruct((n, 128, width), BF16),
            jax.ShapeDtypeStruct((n, tokens, 128), BF16),
            jax.ShapeDtypeStruct((width, 128), BF16),
            jax.ShapeDtypeStruct((1, width), F32),
        ],
        compiler_params=params(),
        cost_estimate=cost(4 * tokens * width * width, 1e7),
        name="home_step",
    )(gx, h, middle, cot, wr, wo, gain, attn)


def final_kernel(shard, grads_ref, w_ref, h_ref, x_ref, gain_ref, grad_middle_ref, dw_ref, grad_x_ref, dgain_ref, total):
    c = pl.program_id(0)
    g = grads_ref[0]
    dw_ref[...] = dot(h_ref[...], g, TN).astype(BF16)

    @pl.when(c == 0)
    def _():
        total[...] = jnp.zeros_like(total)

    for f in range(w_ref.shape[0]):
        total[:, f * shard : (f + 1) * shard] += dot(g, w_ref[f, :shard, :], NT)

    @pl.when(c == pl.num_programs(0) - 1)
    def _():
        normed, scale = norm_parts(x_ref[...])
        grad_h = total[...]
        dgain_ref[...] = jnp.sum(grad_h * normed, 0, keepdims=True)
        grad_x_ref[...] = grad_middle_ref[...] + norm_back(grad_h * gain_ref[...], normed, scale)


def final_step(grads, weights, h, x, gain, grad_middle, shard):
    n, tokens, _ = grads.shape
    width = x.shape[1]
    fsdp, padded, _ = weights.shape
    same = lambda c: (0, 0)
    return pl.pallas_call(
        functools.partial(final_kernel, shard),
        grid=(n,),
        in_specs=[
            pl.BlockSpec((1, tokens, PACK), lambda c: (c, 0, 0)),
            pl.BlockSpec((fsdp, padded, PACK), lambda c: (0, 0, c)),
            pl.BlockSpec((tokens, width), same),
            pl.BlockSpec((tokens, width), same),
            pl.BlockSpec((1, width), same),
            pl.BlockSpec((tokens, width), same),
        ],
        out_specs=[
            pl.BlockSpec((width, PACK), lambda c: (0, c)),
            pl.BlockSpec((tokens, width), same),
            pl.BlockSpec((1, width), same),
        ],
        out_shape=[
            jax.ShapeDtypeStruct((width, n * PACK), BF16),
            jax.ShapeDtypeStruct((tokens, width), F32),
            jax.ShapeDtypeStruct((1, width), F32),
        ],
        scratch_shapes=[pltpu.VMEM((tokens, width), F32)],
        compiler_params=params(),
        cost_estimate=cost(4 * tokens * width * n * PACK, 1.2e7),
        name="final_step",
    )(grads, weights, h, x, gain, grad_middle)


def widen_kernel(number, index_ref, own_ref, other_ref, gate_ref, up_ref, down_ref):
    def write(ref):
        for half in range(2):
            at = slice(half * PIECE, (half + 1) * PIECE)
            gate_ref[0, at, :] = ref[half].astype(F32)
            up_ref[0, at, :] = ref[2 + half].astype(F32)
            down_ref[0, :, at] = ref[4 + half].astype(F32)

    @pl.when(pl.program_id(0) == 0)
    def _():
        write(own_ref)

    @pl.when(pl.program_id(0) == 1)
    def _():
        write(other_ref)


def tail_kernel(number, index_ref, own_ref, other_ref, own_small_ref, other_small_ref, mixed_in, grad_in, gate_ref, up_ref, down_ref, mixed_ref, grad_ref, dwq_ref, dwk_ref, dwv_ref, dwo_ref, dwr_ref, g1_ref, g2_ref):
    widen_kernel(number, index_ref, own_ref, other_ref, gate_ref, up_ref, down_ref)
    mixed_ref[...] = mixed_in[...]
    grad_ref[...] = grad_in[...]

    @pl.when((pl.program_id(0) == 0) & (pl.program_id(1) == 0))
    def _():
        for which, ref in enumerate((own_small_ref, other_small_ref)):
            part = index_ref[which] // number
            at = pl.ds(pl.multiple_of(part * 128, 128), 128)
            for q in range(4):
                block = ref[1, q * 128 : (q + 1) * 128, :].astype(F32)
                dwq_ref[at, q * 256 : q * 256 + 128] = block[:, :128]
                dwq_ref[at, q * 256 + 128 : (q + 1) * 256] = block[:, 256:384]
                one, two = block[:, 128:256], block[:, 384:]
                low = lane_iota(one.shape) < HEAD_DIMENSION
                dwk_ref[at, q * 128 : (q + 1) * 128] = jnp.where(low, one, pltpu.roll(two, 64, 1))
                dwv_ref[at, q * 128 : (q + 1) * 128] = jnp.where(low, pltpu.roll(one, 64, 1), two)
            dwo_ref[at, :PIECE] = ref[0, 0:128, :].astype(F32)
            dwo_ref[at, PIECE:] = ref[0, 128:256, :].astype(F32)
            dwr_ref[at, :] = ref[0, 256:384, :EXPERTS].astype(F32)
            gains = ref[0, 384:400, :128].astype(F32)
            g1_ref[pl.ds(part, 1), :] = gains[0:1]
            g2_ref[pl.ds(part, 1), :] = gains[1:2]


def expert_specs(number, shapes):
    last = number - 1
    ins = [
        pl.BlockSpec((6, PIECE, PIECE), lambda s, e, at: (jnp.where(s == 0, e, last), 0, 0)),
        pl.BlockSpec((6, PIECE, PIECE), lambda s, e, at: (jnp.where(s == 0, 0, e), 0, 0)),
    ]
    outs = [pl.BlockSpec((1,) + tuple(shape[1:]), lambda s, e, at: (at[s] + e, 0, 0)) for shape in shapes]
    return ins, outs, [jax.ShapeDtypeStruct(shape, F32) for shape in shapes]


def widen(index, own, other, shapes):
    number = shapes[0][0] // 2
    ins, outs, out_shapes = expert_specs(number, shapes)
    return pl.pallas_call(
        functools.partial(widen_kernel, number),
        grid_spec=pltpu.PrefetchScalarGridSpec(num_scalar_prefetch=1, grid=(2, number), in_specs=ins, out_specs=outs),
        out_shape=out_shapes,
        compiler_params=params(),
        cost_estimate=cost(0, 1e8),
        name="widen",
    )(index, own, other)


def tail(index, own, other, mixed, grad_x, shapes, shard):
    number = shapes[0][0] // 2
    tokens, width = mixed.shape
    ins, outs, out_shapes = expert_specs(number, shapes)
    small = pl.BlockSpec((2, PIECE, PIECE), lambda s, e, at: (3 * number, 0, 0))
    rows = pl.BlockSpec((tokens // (2 * number), width), lambda s, e, at: (s * number + e, 0))
    small_shapes = [(shard, width), (shard, width // 2), (shard, width // 2), (shard, width), (shard, EXPERTS), (2, 128), (2, 128)]
    whole = [pl.BlockSpec(shape, lambda s, e, at: (0, 0)) for shape in small_shapes]
    return pl.pallas_call(
        functools.partial(tail_kernel, number),
        grid_spec=pltpu.PrefetchScalarGridSpec(
            num_scalar_prefetch=1,
            grid=(2, number),
            in_specs=ins + [small, small, rows, rows],
            out_specs=outs + [rows, rows] + whole,
        ),
        out_shape=out_shapes
        + [jax.ShapeDtypeStruct((tokens, width), F32)] * 2
        + [jax.ShapeDtypeStruct(shape, F32) for shape in small_shapes],
        compiler_params=params(),
        cost_estimate=cost(0, 1e8),
        name="tail",
    )(index, own, other, own, other, mixed, grad_x)


def swap(value, axis, bit):
    size = lax.axis_size(axis)
    return lax.ppermute(value, axis, [(i, i ^ bit) for i in range(size)])


def group_bits(fsdp):
    bits = [("fsdp", 1 << b) for b in range(1, fsdp.bit_length() - 1)]
    return bits + [("ctx", 1), ("fsdp", 1)]


def group_gather(value, bits):
    stacked = value[None]
    for axis, bit in bits:
        stacked = jnp.concatenate([stacked, swap(stacked, axis, bit)], 0)
    return stacked


def group_reduce(stacked, bits):
    for axis, bit in reversed(bits):
        half = stacked.shape[0] // 2
        arrived = swap(stacked[half:], axis, bit)
        stacked = (stacked[:half].astype(F32) + arrived.astype(F32)).astype(stacked.dtype)
    return stacked[0]


def line_sum(value, ctx):
    pairs = ctx // 2
    if pairs != 4:
        bit = 2
        while bit < ctx:
            value = value + swap(value, "ctx", bit)
            bit *= 2
        return value
    at = lambda z, y: 2 * z + y
    inward = [(at(0, y), at(1, y)) for y in range(2)] + [(at(3, y), at(2, y)) for y in range(2)]
    across = [(at(1, y), at(2, y)) for y in range(2)] + [(at(2, y), at(1, y)) for y in range(2)]
    outward = [(b, a) for a, b in inward]
    value = value + lax.ppermute(value, "ctx", inward)
    value = value + lax.ppermute(value, "ctx", across)
    arrived = lax.ppermute(value, "ctx", outward)
    z = lax.axis_index("ctx") // 2
    return jnp.where((z == 0) | (z == 3), arrived, value)


MESH = pl.DeviceIdType.MESH


def flip(index, bit):
    return jnp.where((index // bit) % 2 == 0, index + bit, index - bit)


def send(src, dst, send_sem, recv_sem, device):
    return pltpu.make_async_remote_copy(src_ref=src, dst_ref=dst, send_sem=send_sem, recv_sem=recv_sem, device_id=device, device_id_type=MESH)


def neighbours():
    ctx, fsdp = lax.axis_index("ctx"), lax.axis_index("fsdp")
    side, across = flip(ctx, 1), flip(fsdp, 2)
    core = {"fsdp": flip(fsdp, 1)}
    return core, [{"fsdp": across}, {"ctx": side}, {"ctx": side, "fsdp": across}]


def greet(devices):
    barrier = pltpu.get_barrier_semaphore()
    for device in devices:
        pl.semaphore_signal(barrier, inc=1, device_id=device, device_id_type=MESH)
    pl.semaphore_wait(barrier, len(devices))


def others(n):
    ctx = lax.axis_index("ctx")
    return [lax.rem(ctx + d, n) for d in range(1, n)]


def exchange_start(src, dst, send_sems, recv_sems, local_sem, n):
    ctx = lax.axis_index("ctx")
    for d, c in enumerate(others(n)):
        send(src.at[c], dst.at[ctx], send_sems.at[d], recv_sems.at[d], {"ctx": c}).start()
    pltpu.make_async_copy(src.at[ctx], dst.at[ctx], local_sem).start()


def exchange_wait(src, dst, send_sems, recv_sems, local_sem, n, arrived=None):
    ctx = lax.axis_index("ctx")
    pltpu.make_async_copy(src.at[ctx], dst.at[ctx], local_sem).wait()
    if arrived is not None:
        arrived(ctx)
    for d in range(n - 1):
        source = lax.rem(ctx + n - 1 - d, n)
        send(src.at[source], dst.at[source], send_sems.at[d], recv_sems.at[d], {"ctx": source}).wait_recv()
        if arrived is not None:
            arrived(source)
    for d, c in enumerate(others(n)):
        send(src.at[c], dst.at[ctx], send_sems.at[d], recv_sems.at[d], {"ctx": c}).wait_send()


def front_kernel(n, cap, wq_ref, wk_ref, wv_ref, wo_part_ref, wr_raw_ref, g1_ref, g2_ref, x_ref, table_ref, routes_ref, cot_ref, packs_ref, h_ref, weights_ref, wo_ref, wr_ref, cxs_ref, gains_ref, wall, packed_ref, wr_part_ref, cx, table, normed_ref, total, out, exch_send, exch_recv, full_send, full_recv, x_send, x_recv, y_send, y_recv, xs_send, xs_recv, ys_send, ys_recv, cx_send, cx_recv, local_sems):
    width = x_ref.shape[1]
    shard = width // 4
    ctx, fsdp = lax.axis_index("ctx"), lax.axis_index("fsdp")
    parity = lax.rem(ctx, 2)
    core, group = neighbours()
    far, near = group[0], group[1]
    sibling, distant = flip(fsdp, 1), flip(fsdp, 2)
    other = flip(distant, 1)
    for k in range(2):
        pltpu.make_async_copy(table_ref.at[k, ctx], table.at[k], local_sems.at[6 + k]).start()

    pair = HEAD_DIMENSION * 2
    for c in range(0, n, 2):
        for k in range(2):
            packed_ref[:shard, (c + k) * PACK : (c + k) * PACK + 128] = wq_ref[:, (c + k) * 128 : (c + k + 1) * 128]
        keys, values = wk_ref[:, c // 2 * pair : (c // 2 + 1) * pair].astype(F32), wv_ref[:, c // 2 * pair : (c // 2 + 1) * pair].astype(F32)
        low = lane_iota(keys.shape) < HEAD_DIMENSION
        packed_ref[:shard, c * PACK + 128 : (c + 1) * PACK] = jnp.where(low, keys, pltpu.roll(values, 64, 1)).astype(BF16)
        packed_ref[:shard, (c + 1) * PACK + 128 : (c + 2) * PACK] = jnp.where(low, pltpu.roll(keys, 64, 1), values).astype(BF16)
    row = row_iota((16, shard))
    gain_rows = jnp.where(row == 0, g1_ref[...].astype(F32), jnp.where(row == 1, g2_ref[...].astype(F32), 0.0))
    packed_ref[shard:, :] = jnp.zeros((packed_ref.shape[0] - shard, n * PACK), BF16)
    packed_ref[shard : shard + 16, :shard] = gain_rows.astype(BF16)
    wr_part_ref[...] = jnp.concatenate([wr_raw_ref[...].astype(F32), jnp.zeros((shard, 128 - EXPERTS), F32)], 1).astype(BF16)
    greet([core, far] + [{"ctx": c} for c in others(n)])

    half_rows = packed_ref.shape[0] // 2
    low_rows = half_rows // 32 * 16

    def cut(k, part):
        if k == 0:
            return pl.ds(pl.multiple_of(part * half_rows, 16), low_rows)
        if k == 1:
            return pl.ds(pl.multiple_of(part * half_rows + low_rows, 16), half_rows - low_rows)
        if k == 2:
            return pl.ds(part, 1)
        return pl.ds(pl.multiple_of(part * (shard // 2), 16), shard // 2)

    sources = [packed_ref, packed_ref, wo_part_ref, wr_part_ref]
    targets = [wall, wall, wo_ref, wr_ref]
    wholes = [(packed_ref, wall), (wo_part_ref, wo_ref), (wr_part_ref, wr_ref)]

    def whole(i):
        src, dst = wholes[i]
        return send(src, dst.at[fsdp], full_send.at[i], full_recv.at[i], core)

    def own(i):
        src, dst = wholes[i]
        return pltpu.make_async_copy(src, dst.at[fsdp], local_sems.at[i])

    def to_far(k):
        return send(sources[k].at[cut(k, parity)], targets[k].at[fsdp, cut(k, parity)], x_send.at[k], x_recv.at[k], far)

    def pass_on(k, part, sems, device):
        ref = targets[k].at[distant, cut(k, part)]
        return send(ref, ref, sems[0].at[k], sems[1].at[k], device)

    def far_arrived(k):
        ref = targets[k].at[distant, cut(k, parity)]
        send(ref, ref, x_send.at[k], x_recv.at[k], far).wait_recv()
        pass_on(k, parity, (y_send, y_recv), near).start()
        pass_on(k, parity, (xs_send, xs_recv), core).start()

    def near_arrived(k):
        pass_on(k, 1 - parity, (y_send, y_recv), near).wait_recv()
        pass_on(k, 1 - parity, (ys_send, ys_recv), core).start()

    def core_arrived(k):
        for part, sems in ((parity, (xs_send, xs_recv)), (1 - parity, (ys_send, ys_recv))):
            ref = targets[k].at[other, cut(k, part)]
            send(ref, ref, sems[0].at[k], sems[1].at[k], core).wait_recv()

    own(0).start()
    to_far(0).start()
    to_far(1).start()
    whole(0).start()

    prep_kernel(cap, routes_ref, cot_ref, cx)
    pltpu.make_async_copy(cx, cxs_ref.at[0], local_sems.at[3]).start()
    normed, _ = norm_parts(x_ref[...])
    normed_ref[...] = normed

    def project(block, begin):
        at = pl.ds(pl.multiple_of(block * shard, shard), shard)
        gain = wall[block, shard : shard + 16, :shard].astype(F32)
        gains_ref[:, at] = gain
        h = (normed_ref[:, at] * gain[:1]).astype(BF16)
        h_ref[:, at] = h
        part = dot(h, wall[block, :shard, :])
        total[...] = part if begin else total[...] + part

    own(0).wait()
    project(fsdp, True)
    ref = wall.at[sibling]
    send(ref, ref, full_send.at[0], full_recv.at[0], core).wait_recv()
    project(sibling, False)
    far_arrived(0)
    far_arrived(1)
    for i in (1, 2):
        own(i).start()
        whole(i).start()
        to_far(i + 1).start()
    send(cx, cxs_ref.at[1], cx_send.at[0], cx_recv.at[0], far).start()
    near_arrived(0)
    near_arrived(1)
    project(distant, False)
    core_arrived(0)
    core_arrived(1)
    project(other, False)
    keep = pltpu.make_async_copy(wall, weights_ref, local_sems.at[4])
    keep.start()
    for k in range(2):
        pltpu.make_async_copy(table_ref.at[k, ctx], table.at[k], local_sems.at[6 + k]).wait()
    angles = table[...].reshape(x_ref.shape[0], 256)
    for c in range(n):
        out[c] = turn(total[:, c * PACK : (c + 1) * PACK], angles, 1.0).astype(BF16)
    exchange = (out, packs_ref, exch_send, exch_recv, local_sems.at[5], n)
    exchange_start(*exchange)

    for k in (2, 3):
        far_arrived(k)
    for k in (2, 3):
        near_arrived(k)
    for k in (2, 3):
        core_arrived(k)
    for i in (1, 2):
        src, dst = wholes[i]
        ref = dst.at[sibling]
        send(ref, ref, full_send.at[i], full_recv.at[i], core).wait_recv()
        own(i).wait()
    exchange_wait(*exchange)
    for i in range(3):
        whole(i).wait_send()
    for k in range(4):
        to_far(k).wait_send()
        pass_on(k, parity, (y_send, y_recv), near).wait_send()
        pass_on(k, parity, (xs_send, xs_recv), core).wait_send()
        pass_on(k, 1 - parity, (ys_send, ys_recv), core).wait_send()
    send(cx, cxs_ref.at[1], cx_send.at[0], cx_recv.at[0], far).wait()
    pltpu.make_async_copy(cx, cxs_ref.at[0], local_sems.at[3]).wait()
    keep.wait()


def front(wq, wk, wv, wo_part, wr, g1, g2, x, table, routes, cot, cap, n):
    tokens, width = x.shape
    shard = wq.shape[0]
    hbm, vmem = pl.BlockSpec(memory_space=pl.ANY), pl.BlockSpec(memory_space=pltpu.VMEM)
    dma = lambda k: pltpu.SemaphoreType.DMA((k,))
    shaped = lambda shape, dtype=BF16: jax.ShapeDtypeStruct(shape, dtype)
    cx_shape = (tokens + EXPERTS, width)
    packed = (2 * 16 * (shard // 32 + 1), n * PACK)
    return pl.pallas_call(
        functools.partial(front_kernel, n, cap),
        in_specs=[vmem, vmem, vmem, hbm, vmem, vmem, vmem, vmem, hbm, vmem, vmem],
        out_specs=[hbm, vmem, hbm, hbm, hbm, hbm, vmem],
        out_shape=[
            shaped((n, tokens, PACK)),
            shaped((tokens, width)),
            shaped((4,) + packed),
            shaped((4,) + wo_part.shape),
            shaped((4, shard, 128)),
            shaped((2,) + cx_shape),
            shaped((16, width), F32),
        ],
        scratch_shapes=[
            pltpu.VMEM((4,) + packed, BF16),
            pltpu.VMEM(packed, BF16),
            pltpu.VMEM((shard, 128), BF16),
            pltpu.VMEM(cx_shape, BF16),
            pltpu.VMEM((2, tokens // 2, 256), F32),
            pltpu.VMEM((tokens, width), F32),
            pltpu.VMEM((tokens, n * PACK), F32),
            pltpu.VMEM((n, tokens, PACK), BF16),
            dma(n - 1),
            dma(n - 1),
            dma(3),
            dma(3),
        ]
        + [dma(4)] * 8
        + [dma(1), dma(1), dma(8)],
        compiler_params=params(collective_id=1, has_side_effects=True),
        cost_estimate=cost(2e9, 5e7),
        name="front",
    )(wq, wk, wv, wo_part, wr, g1, g2, x, table, routes, cot)


def attend_kernel(length, n, ends_ref, q_ref, pack_ref, cxs_ref, out_ref, lse_ref, full_ref, rest_ref, keys, values_t, acc, near_send, near_recv, far_send, far_recv, core_send, core_recv):
    block = pl.program_id(0)
    core, group = neighbours()
    far, near = group[0], group[1]
    split = cxs_ref.shape[1] // 2

    def to_near(i):
        at = pl.ds(0, cxs_ref.shape[1] if i == 0 else split)
        return send(cxs_ref.at[i, at], rest_ref.at[i, at], near_send.at[i], near_recv.at[i], near)

    def to_far():
        at = pl.ds(split, split)
        return send(rest_ref.at[0, at], rest_ref.at[1, at], far_send.at[0], far_recv.at[0], far)

    def to_core(i):
        src = cxs_ref.at[i] if i < 2 else rest_ref.at[i - 2]
        return send(src, rest_ref.at[2 + i], core_send.at[i], core_recv.at[i], core)

    @pl.when(block == 0)
    def _():
        greet([core, far, near])
        for i in range(2):
            to_near(i).start()
        for i in range(2):
            to_core(i).start()

    attn_forward_kernel(length, ends_ref, q_ref, pack_ref, out_ref, lse_ref, full_ref, keys, values_t, acc)

    @pl.when(block == pl.num_programs(0) - 4)
    def _():
        to_near(0).wait_recv()
        to_far().start()
        to_core(2).start()

    @pl.when(block == pl.num_programs(0) - 1)
    def _():
        to_near(1).wait_recv()
        to_far().wait_recv()
        to_core(3).start()
        for i in range(4):
            to_core(i).wait()
        for i in range(2):
            to_near(i).wait_send()
        to_far().wait_send()


def attend(ends, packs, cxs, length):
    n, _, rows, _ = packs.shape
    blocks, per = length // BLK, BLK // rows
    per_half = blocks // 2
    tiles = lambda i: (lax.rem(i, per_half), i // per_half, 0, 0)
    hbm = pl.BlockSpec(memory_space=pl.ANY)
    dma = lambda k: pltpu.SemaphoreType.DMA((k,))
    return pl.pallas_call(
        functools.partial(attend_kernel, length, n),
        grid=(blocks,),
        in_specs=[
            pl.BlockSpec(memory_space=pltpu.SMEM),
            pl.BlockSpec((per, 1, rows, PACK), tiles),
            pl.BlockSpec(packs.shape, lambda i: (0, 0, 0, 0)),
            hbm,
        ],
        out_specs=[
            pl.BlockSpec((per, 1, rows, 128), tiles),
            pl.BlockSpec((1, 1, 2 * BLK), lambda i: (i, 0, 0)),
            pl.BlockSpec((1, 128, 2 * BLK), lambda i: (i, 0, 0)),
            hbm,
        ],
        scratch_shapes=[
            pltpu.VMEM((length, 128), BF16),
            pltpu.VMEM((128, length), BF16),
            pltpu.VMEM((128, 2 * BLK), F32),
            dma(2),
            dma(2),
            dma(1),
            dma(1),
            dma(4),
            dma(4),
        ],
        out_shape=[
            jax.ShapeDtypeStruct((n, 2, rows, 128), BF16),
            jax.ShapeDtypeStruct((blocks, 1, 2 * BLK), F32),
            jax.ShapeDtypeStruct((blocks, 128, 2 * BLK), F32),
            jax.ShapeDtypeStruct((6,) + cxs.shape[1:], BF16),
        ],
        compiler_params=params(collective_id=3, has_side_effects=True),
        cost_estimate=cost(1.5e10, 2e7),
        name="attend",
    )(ends, packs, packs, cxs)


def mid_kernel(n, number, capp, attn_ref, cxs_ref, rest_ref, wo_ref, wr_ref, x_ref, gain_ref, middle_ref, h_ref, kept_ref, xs_ref, gs_ref, gates_ref, arrived, hs, total, exch_send, exch_recv, hop_send, hop_recv, cross_send, cross_recv, fwd_send, fwd_recv, local_sems):
    tokens, width = x_ref.shape
    ctx, fsdp = lax.axis_index("ctx"), lax.axis_index("fsdp")
    first = (fsdp * 2 + lax.rem(ctx, 2)) * number
    core, group = neighbours()
    greet([core, group[0]] + [{"ctx": c} for c in others(n)])
    exchange = (attn_ref, arrived, exch_send, exch_recv, local_sems.at[0], n)
    exchange_start(*exchange)
    total[...] = jnp.zeros_like(total)

    def take(c):
        total[...] += dot(arrived[c], wo_ref[c])

    exchange_wait(*exchange, take)
    keep = pltpu.make_async_copy(arrived, kept_ref, local_sems.at[1])
    keep.start()
    middle = x_ref[...] + RESIDUAL * total[...]
    middle_ref[...] = middle
    normed, _ = norm_parts(middle)
    h = (normed * gain_ref[...]).astype(BF16)
    h_ref[...] = h
    hs[0] = h

    split = tokens // 2

    def hop(i):
        return send(hs.at[0], hs.at[(1, 2, 4)[i]], hop_send.at[i], hop_recv.at[i], (group[0], group[1], core)[i])

    def cross(i):
        at = pl.ds(i * split, split)
        return send(hs.at[1 + i, at], hs.at[3, at], cross_send.at[i], cross_recv.at[i], group[1 - i])

    def forward(i):
        return send(hs.at[1 + i], hs.at[5 + i], fwd_send.at[i], fwd_recv.at[i], core)

    for i in range(3):
        hop(i).start()

    def place(b):
        h = hs[b]
        cx = (cxs_ref.at[b] if b < 2 else rest_ref.at[cx_slot[b]])
        logits = jnp.transpose(dot(h, wr_ref[...]))[:EXPERTS, :]
        raw = jnp.exp(logits - jnp.max(logits, 0, keepdims=True))
        router = raw / jnp.sum(raw, 0, keepdims=True)
        slots = cx[tokens:, :tokens].astype(F32)
        hots = one_hot(slots, first, number, capp)
        places = jnp.concatenate(hots, 0).astype(BF16)
        rows = dot(places, h).astype(BF16)
        grads = dot(places, cx[:tokens, :]).astype(BF16)
        for j in range(number):
            at = slice(j * capp, (j + 1) * capp)
            xs_ref[j, b] = rows[at]
            gs_ref[j, b] = grads[at]
            gate = jnp.sum(hots[j] * own_row(router, first + j), 1, keepdims=True)
            gates_ref[j, b] = jnp.broadcast_to(gate, (capp, 128))

    cx_slot = {2: 0, 3: 1, 4: 2, 5: 3, 6: 4, 7: 5}
    place(0)
    hop(2).wait_recv()
    place(4)
    for i in range(2):
        hop(i).wait_recv()
        cross(i).start()
        forward(i).start()
    place(1)
    place(2)
    for i in range(2):
        cross(i).wait_recv()
    forward(2).start()
    place(3)
    for i in range(3):
        forward(i).wait_recv()
        place(5 + i)
    for i in range(2):
        cross(i).wait_send()
    for i in range(3):
        hop(i).wait_send()
        forward(i).wait_send()
    keep.wait()


def mid_step(attn, cxs, rest, wo, wr, x, gain, number, capp, n):
    tokens, width = x.shape
    hbm, vmem = pl.BlockSpec(memory_space=pl.ANY), pl.BlockSpec(memory_space=pltpu.VMEM)
    dma = lambda k: pltpu.SemaphoreType.DMA((k,))
    shaped = lambda shape, dtype=BF16: jax.ShapeDtypeStruct(shape, dtype)
    return pl.pallas_call(
        functools.partial(mid_kernel, n, number, capp),
        in_specs=[hbm, vmem, vmem, vmem, vmem, vmem, vmem],
        out_specs=[vmem, vmem, hbm, vmem, vmem, vmem],
        out_shape=[
            shaped((tokens, width), F32),
            shaped((tokens, width)),
            shaped(attn.shape),
            shaped((number, 8, capp, width)),
            shaped((number, 8, capp, width)),
            shaped((number, 8, capp, 128), F32),
        ],
        scratch_shapes=[
            pltpu.VMEM(attn.shape, BF16),
            pltpu.VMEM((8, tokens, width), BF16),
            pltpu.VMEM((tokens, width), F32),
            dma(n - 1),
            dma(n - 1),
            dma(3),
            dma(3),
            dma(2),
            dma(2),
            dma(3),
            dma(3),
            dma(2),
        ],
        compiler_params=params(collective_id=2, has_side_effects=True),
        cost_estimate=cost(4e9, 5e7),
        name="mid_step",
    )(attn, cxs, rest, wo, wr, x, gain)


RING = 12
LAG_MIDDLE, LAG_ACROSS, LAG_END = 2, 4, 7
ORDER_X, ORDER_Y, ORDER_CORE = 1, 2, 4


class GroupSum:
    def __init__(self, part, rows, lands, own, sems, load, free, first, core, group):
        self.part, self.rows, self.own, self.load, self.free, self.first = part, rows, own, load, free, first
        self.land, self.land_x, self.land_y = lands
        self.core_send, self.core_recv, self.x_send, self.x_recv, self.y_send, self.y_recv = sems
        self.core, self.far, self.near = core, group[0], group[1]

    def place(self, i):
        return self.land.at[i, pl.ds(0, self.rows)]

    def ready(self, which):
        if not self.first:
            pl.semaphore_wait(self.free.at[which], 1)

    def to_core(self, i):
        return send(self.part.at[4 + i], self.place(i), self.core_send.at[i], self.core_recv.at[i], self.core)

    def to_far(self, k):
        return send(self.place(1 + 2 * k), self.land_x.at[k, pl.ds(0, self.rows)], self.x_send.at[k], self.x_recv.at[k], self.far)

    def to_near(self):
        return send(self.place(2), self.land_y.at[pl.ds(0, self.rows)], self.y_send.at[0], self.y_recv.at[0], self.near)

    def fetch(self, i):
        return pltpu.make_async_copy(self.part.at[i], self.own.at[i % 2, pl.ds(0, self.rows)], self.load.at[i % 2])

    def start(self):
        self.ready(0)
        for i in (1, 3, 2, 0):
            self.to_core(i).start()

    def over_cores(self):
        order = (1, 3, 2, 0)
        if self.own is not None:
            self.fetch(1).start()
        for step, i in enumerate(order):
            if self.own is None:
                mine = self.part[i]
            else:
                self.fetch(i).wait()
                mine = self.own[i % 2, : self.rows]
            self.to_core(i).wait_recv()
            self.land[i, : self.rows] = (self.land[i, : self.rows].astype(F32) + mine.astype(F32)).astype(BF16)
            if self.own is not None and step < 3:
                self.fetch(order[step + 1]).start()
            if i % 2 == 1:
                if step == 0:
                    self.ready(1)
                self.to_far(i // 2).start()

    def over_x(self, between=None):
        for k in (1, 0):
            if k == 0 and between is not None:
                between()
            self.to_far(k).wait_recv()
            both = self.land[2 * k, : self.rows].astype(F32) + self.land_x[k, : self.rows].astype(F32)
            self.land[2 * k, : self.rows] = both.astype(BF16)
            if k == 1:
                self.ready(2)
                self.to_near().start()

    def finish(self):
        self.to_near().wait_recv()
        for i in range(4):
            self.to_core(i).wait_send()
        for k in range(2):
            self.to_far(k).wait_send()
        self.to_near().wait_send()
        return self.land[0, : self.rows].astype(F32) + self.land_y[: self.rows].astype(F32)

    def release(self):
        for which, device in enumerate((self.core, self.far, self.near)):
            pl.semaphore_signal(self.free.at[which], inc=1, device_id=device, device_id_type=MESH)


class LineSum:
    def __init__(self, count, own_ref, other_ref, inbox, across, mine, sems):
        self.count, self.own_ref, self.other_ref = count, own_ref, other_ref
        self.inbox, self.across, self.mine = inbox, across, mine
        self.line_send, self.line_recv, self.mid_send, self.mid_recv, self.side_send, self.side_recv, self.store, self.load = sems
        ctx = lax.axis_index("ctx")
        z = ctx // 2
        self.middle = (z == 1) | (z == 2)
        self.line = {"ctx": jnp.where(z % 2 == 0, ctx + 2, ctx - 2)}
        self.peer = {"ctx": jnp.where(z == 1, ctx + 2, ctx - 2)}
        self.side = {"ctx": flip(ctx, 1)}

    def send_line(self, src, i):
        s = lax.rem(i, RING)
        return send(src, self.inbox.at[s], self.line_send.at[s], self.line_recv.at[s], self.line)

    def send_mid(self, i):
        s = lax.rem(i, RING)
        return send(self.inbox.at[s], self.across.at[s], self.mid_send.at[s], self.mid_recv.at[s], self.peer)

    def send_side(self, src, i):
        return send(src, self.other_ref.at[i], self.side_send.at[lax.rem(i, RING)], self.side_recv.at[i], self.side)

    def keep(self, src, i):
        return pltpu.make_async_copy(src, self.own_ref.at[i], self.store.at[lax.rem(i, RING)])

    def fetch(self, src, i):
        s = lax.rem(i, 4)
        return pltpu.make_async_copy(src, self.mine.at[s], self.load.at[s])

    def drain_middle(self, i):
        src = self.across.at[lax.rem(i, RING)]
        self.send_line(src, i).wait_send()
        self.send_side(src, i).wait_send()
        self.keep(src, i).wait()

    def drain_end(self, i):
        src = self.inbox.at[lax.rem(i, RING)]
        self.send_side(src, i).wait_send()
        self.keep(src, i).wait()

    def tick(self, t, source):
        count = self.count
        fixed = isinstance(t, int)

        def when(condition):
            if fixed:
                return (lambda f: f()) if condition else (lambda f: None)
            return pl.when(condition)

        i32 = (lambda v: jnp.int32(v)) if fixed else (lambda v: v)

        @pl.when(self.middle)
        def _():
            @when((t >= LAG_MIDDLE) & (t < count + LAG_MIDDLE))
            def _():
                i = i32(t - LAG_MIDDLE)

                @when(t >= LAG_ACROSS + 4)
                def _():
                    self.drain_middle(i32(t - LAG_ACROSS - 4))

                s = lax.rem(i, RING)
                self.fetch(self.own_ref.at[i], i).wait()
                self.send_line(self.inbox.at[s], i).wait_recv()
                self.inbox[s] = self.inbox[s] + self.mine[lax.rem(i, 4)]
                self.send_mid(i).start()

            @when(t < count)
            def _():
                self.fetch(source(t), i32(t)).start()

            @when((t >= LAG_ACROSS) & (t < count + LAG_ACROSS))
            def _():
                i = i32(t - LAG_ACROSS)
                s = lax.rem(i, RING)
                self.send_mid(i).wait()
                self.across[s] = self.across[s] + self.inbox[s]
                self.send_line(self.across.at[s], i).start()
                self.send_side(self.across.at[s], i).start()
                self.keep(self.across.at[s], i).start()

        @pl.when(jnp.logical_not(self.middle))
        def _():
            @when(t < count)
            def _():
                @when(t >= LAG_END + 2)
                def _():
                    self.drain_end(i32(t - LAG_END - 2))

                @when(t >= 3)
                def _():
                    self.send_line(self.mine.at[0], i32(t - 3)).wait_send()

                self.send_line(source(t), i32(t)).start()

            @when(t >= LAG_END)
            def _():
                i = i32(t - LAG_END)
                s = lax.rem(i, RING)
                self.send_line(self.inbox.at[s], i).wait_recv()
                self.send_side(self.inbox.at[s], i).start()
                self.keep(self.inbox.at[s], i).start()

    def finish(self):
        count = self.count

        @pl.when(self.middle)
        def _():
            for i in range(count + LAG_MIDDLE - LAG_ACROSS - 4, count):
                self.drain_middle(jnp.int32(i))

        @pl.when(jnp.logical_not(self.middle))
        def _():
            for i in range(count - 3, count):
                self.send_line(self.mine.at[0], jnp.int32(i)).wait_send()
            for i in range(count - LAG_END - 2, count):
                self.drain_end(jnp.int32(i))

        def arrived(i, carry):
            self.send_side(self.mine.at[0], i).wait_recv()
            return carry

        lax.fori_loop(0, count, arrived, 0)


def backward_kernel(
    n,
    length,
    capp,
    ends_ref,
    xs_ref,
    gs_ref,
    gates_ref,
    wg_ref,
    wu_ref,
    wd_ref,
    cxs_ref,
    rest_ref,
    full_ref,
    weights_ref,
    packs_hbm,
    table_hbm,
    cot_hbm,
    wo_hbm,
    attn_hbm,
    x_hbm,
    h_attn_hbm,
    h_ref,
    middle_ref,
    wr_ref,
    gains_ref,
    lse_ref,
    own_ref,
    other_ref,
    pieces_ref,
    outs_ref,
    backs_ref,
    gx_ref,
    yp_ref,
    grad_x_ref,
    mixed_ref,
    inbox,
    across,
    mine,
    land,
    land_x,
    land_y,
    y_land,
    y_land_x,
    y_land_y,
    own_buf,
    late_pieces,
    ga_in,
    grads_in,
    line_send,
    line_recv,
    mid_send,
    mid_recv,
    side_send,
    side_recv,
    line_store,
    line_load,
    ga_send,
    ga_recv,
    gr_send,
    gr_recv,
    group_sems,
    group_load,
    free,
    local_sems,
    full_sems,
    w_sems,
    load_sems,
    store_sems,
    comb_sems,
    part_sems,
):
    tokens, width = h_ref.shape
    half = length // 2
    rows = tokens // 2
    shard = width // 4
    blocks = length // BLK
    number = xs_ref.shape[0]
    ff = wg_ref.shape[2]
    ctx, fsdp = lax.axis_index("ctx"), lax.axis_index("fsdp")
    side = lax.rem(ctx, 2)
    first = (fsdp * 2 + side) * number
    core, group = neighbours()
    sub = own_ref.shape[1]
    cuts = PIECE // sub
    early = number * 6 * cuts
    line = LineSum(early + 2 * cuts, own_ref, other_ref, inbox, across, mine, (line_send, line_recv, mid_send, mid_recv, side_send, side_recv, line_store, line_load))

    def source(t):
        return pieces_ref.at[t // cuts, pl.ds(pl.multiple_of(lax.rem(t, cuts) * sub, sub), sub)]

    def tick(t):
        line.tick(jnp.int32(t) if isinstance(t, int) else t, source)

    sems = lambda k: [group_sems.at[k, j] for j in range(6)]
    lands = (land, land_x, land_y)
    ext = tokens + EXPERTS
    gx = GroupSum(gx_ref, 2 * ext, lands, None, sems(0), None, free, True, core, group)
    ys = GroupSum(yp_ref, 2 * tokens, (y_land, y_land_x, y_land_y), own_buf, sems(1), group_load, free, True, core, group)

    greet([core, group[0]] + [{"ctx": c} for c in others(n)])

    def strip(r):
        f = fsdp
        if r & ORDER_X:
            f = flip(f, 2)
        if r & ORDER_CORE:
            f = flip(f, 1)
        return 2 * f + (1 - side if r & ORDER_Y else side)

    def experts(wg, wu, wd, xb, gb, gateb, stage, out_acc, back_acc, outb, backb, go, dgate, comb_o, comb_b, gst, yst, slots):
        def loads(e):
            s = lax.rem(e, 2)
            at = side * number + e
            pairs = ((wg_ref.at[at], wg), (wu_ref.at[at], wu), (wd_ref.at[at], wd), (xs_ref.at[e], xb), (gs_ref.at[e], gb), (gates_ref.at[e], gateb))
            return [pltpu.make_async_copy(src, dst.at[s], load_sems.at[s, k]) for k, (src, dst) in enumerate(pairs)]

        def slot_copy(b):
            src = cxs_ref.at[b] if b < 2 else rest_ref.at[b - 2]
            return pltpu.make_async_copy(src.at[pl.ds(tokens, EXPERTS), pl.ds(0, tokens)], slots.at[b], part_sems.at[0, b])

        def stores(e):
            pairs = ((stage, pieces_ref.at[pl.ds(6 * e, 6)]), (outb, outs_ref.at[e]), (backb, backs_ref.at[e]))
            return [pltpu.make_async_copy(src, dst, store_sems.at[k]) for k, (src, dst) in enumerate(pairs)]

        for copy in loads(jnp.int32(0)):
            copy.start()
        for b in range(8):
            slot_copy(b).start()

        def one(e, carry):
            s = lax.rem(e, 2)

            @pl.when(e + 1 < number)
            def _():
                for copy in loads(e + 1):
                    copy.start()

            for copy in loads(e):
                copy.wait()

            @pl.when(e > 0)
            def _():
                for copy in stores(e - 1)[1:]:
                    copy.wait()

            x = xb[s]
            gate = gateb[s][:, :1]
            go[...] = (gate * (RESIDUAL * gb[s].astype(F32))).astype(BF16)
            part = ff // 2
            for chunk in range(2):
                at = slice(chunk * part, (chunk + 1) * part)
                wgc, wuc, wdc = wg[s, :, at], wu[s, :, at], wd[s, at, :]
                pre_gate = dot(x, wgc)
                pre_up = dot(x, wuc)
                sig = jax.nn.sigmoid(pre_gate)
                hidden = (pre_gate * sig * pre_up).astype(BF16)
                out_part = dot(hidden, wdc)
                grad_hidden = dot(go[...], wdc, NT)
                grad_gate = (grad_hidden * pre_up * sig * (1.0 + pre_gate * (1.0 - sig))).astype(BF16)
                grad_up = (grad_hidden * pre_gate * sig).astype(BF16)
                row_part = dot(grad_gate, wgc, NT) + dot(grad_up, wuc, NT)
                dwg = dot(x, grad_gate, TN).astype(BF16)
                dwu = dot(x, grad_up, TN).astype(BF16)
                dwd = dot(hidden, go[...], TN).astype(BF16)
                for k in range(2):
                    cut = slice(k * PIECE, (k + 1) * PIECE)
                    stage[k, :, at] = dwg[cut]
                    stage[2 + k, :, at] = dwu[cut]
                    stage[4 + k, at, :] = dwd[:, cut]
                if chunk == 0:
                    out_acc[...] = out_part
                    back_acc[...] = row_part

                    @pl.when(e > 0)
                    def _():
                        tick(2 * e - 1)

                else:
                    out = (out_acc[...] + out_part).astype(BF16).astype(F32)
                    outb[...] = (gate * out).astype(BF16)
                    backb[...] = (back_acc[...] + row_part).astype(BF16)
                    grad = jnp.sum(RESIDUAL * gb[s].astype(F32) * out, 1, keepdims=True)
                    dgate[e] = jnp.broadcast_to(grad, dgate.shape[1:])
            for copy in stores(e):
                copy.start()
            stores(e)[0].wait()
            tick(2 * e)
            return carry

        lax.fori_loop(0, number, one, 0)
        for copy in stores(jnp.int32(number - 1))[1:]:
            copy.wait()
        for b in range(8):
            slot_copy(b).wait()

        def which(s):
            k = lax.rem(s, 4)
            i = jnp.where(k == 0, 1, jnp.where(k == 1, 3, jnp.where(k == 2, 2, 0)))
            return jnp.where(s < 4, 4 + i, i), i

        def comb(s):
            k = lax.rem(s, 2)
            at = pl.ds(pl.multiple_of(which(s)[0] * capp, 16), capp)
            return [
                pltpu.make_async_copy(outs_ref.at[:, at], comb_o.at[k], comb_sems.at[0, k]),
                pltpu.make_async_copy(backs_ref.at[:, at], comb_b.at[k], comb_sems.at[1, k]),
            ]

        def put(s):
            k = lax.rem(s, 2)
            r, _ = which(s)
            return [
                pltpu.make_async_copy(gst.at[k], gx_ref.at[r], part_sems.at[1, k]),
                pltpu.make_async_copy(yst.at[k], yp_ref.at[r], part_sems.at[1, 2 + k]),
            ]

        for copy in comb(jnp.int32(0)):
            copy.start()

        def join(s, carry):
            k = lax.rem(s, 2)
            r, i = which(s)

            @pl.when(s + 1 < 8)
            def _():
                for copy in comb(s + 1):
                    copy.start()

            for copy in comb(s):
                copy.wait()

            @pl.when(s >= 2)
            def _():
                put(s - 2)[1].wait()

            hots = one_hot(slots[r].astype(F32), first, number, capp)
            places = jnp.concatenate(hots, 0).astype(BF16)
            y = dot(places, comb_o[k].reshape(number * capp, width), TN).astype(BF16)
            back = dot(places, comb_b[k].reshape(number * capp, width), TN).astype(BF16)
            extra = jnp.zeros((EXPERTS, 2 * tokens), F32)
            for j in range(number):
                grads = dgate[j, pl.ds(pl.multiple_of(r * capp, 16), capp), :][:, :1]
                grad = jnp.sum(hots[j] * grads, 0, keepdims=True)
                high = grad.astype(BF16).astype(F32)
                extra = jnp.where(row_iota(extra.shape) == first + j, jnp.concatenate([high, grad - high], 1), extra)
            for q in range(2):
                yst[k, q * tokens : (q + 1) * tokens, :] = y[:, q * PIECE : (q + 1) * PIECE]
                gst[k, q * ext : q * ext + tokens, :] = back[:, q * PIECE : (q + 1) * PIECE]
            gst[k, tokens:ext, :] = extra.astype(BF16)
            gst[k, ext + tokens :, :] = jnp.zeros((EXPERTS, PIECE), BF16)
            put(s)[1].start()

            @pl.when(s < 4)
            def _():
                put(s)[0].start()
                put(s)[0].wait()
                gx.to_core(i).start()

            @pl.when(s >= 4)
            def _():
                gx.to_core(i).wait_recv()
                land[i, : gx.rows] = (land[i, : gx.rows].astype(F32) + gst[k].astype(F32)).astype(BF16)

            @pl.when((s == 4) | (s == 5))
            def _():
                gx.to_far(s - 4).start()

            @pl.when(lax.rem(s, 2) == 1)
            def _():
                tick(2 * number - 1 + s // 2)

            return carry

        lax.fori_loop(0, 8, join, 0)
        for s in range(6, 8):
            put(jnp.int32(s))[1].wait()

    slots_rows = xs_ref.shape[1]
    pl.run_scoped(
        experts,
        pltpu.VMEM((2, width, ff), BF16),
        pltpu.VMEM((2, width, ff), BF16),
        pltpu.VMEM((2, ff, width), BF16),
        pltpu.VMEM((2, slots_rows, width), BF16),
        pltpu.VMEM((2, slots_rows, width), BF16),
        pltpu.VMEM((2, slots_rows, 128), F32),
        pltpu.VMEM((6, PIECE, PIECE), BF16),
        pltpu.VMEM((slots_rows, width), F32),
        pltpu.VMEM((slots_rows, width), F32),
        pltpu.VMEM((slots_rows, width), BF16),
        pltpu.VMEM((slots_rows, width), BF16),
        pltpu.VMEM((slots_rows, width), BF16),
        pltpu.VMEM((number, slots_rows, 128), F32),
        pltpu.VMEM((2, number, capp, width), BF16),
        pltpu.VMEM((2, number, capp, width), BF16),
        pltpu.VMEM((2, 2 * ext, PIECE), BF16),
        pltpu.VMEM((2, 2 * tokens, PIECE), BF16),
        pltpu.VMEM((8, EXPERTS, tokens), BF16),
    )
    at_tick = [2 * number + 3]

    def go_on(k=1):
        for _ in range(k):
            tick(at_tick[0])
            at_tick[0] += 1

    def backward(packs, table, keys, values, keys_t, grad_q, grad_k, grad_v, acc, full_buf, ga, pack_out, wbuf, total, grad_middle, dgain, col, small, columns, cot, wo, attn, x_in, h_attn):
        ws = GroupSum(small, PIECE, lands, None, sems(2), None, free, False, core, group)
        cs = GroupSum(columns, PIECE + 16, lands, None, sems(3), None, free, False, core, group)
        copies = [
            pltpu.make_async_copy(src, dst, local_sems.at[4 + k])
            for k, (src, dst) in enumerate(
                ((cot_hbm, cot), (wo_hbm, wo), (attn_hbm, attn), (packs_hbm, packs), (table_hbm, table), (x_hbm, x_in), (h_attn_hbm, h_attn))
            )
        ]
        for copy in copies:
            copy.start()
        small[:, PIECE // 2 : PIECE, :] = jnp.zeros((8, PIECE // 2, PIECE), BF16)
        columns[:, PIECE:, :] = jnp.zeros((8, 16, PIECE), BF16)
        go_on(2)
        gx.over_x(go_on)
        go_on(2)
        arrived = gx.finish()
        arrived = jnp.concatenate([arrived[:ext], arrived[ext:]], 1)
        gx.release()

        h = h_ref[...]
        gain = gains_ref[1:2]
        extra = arrived[tokens:, :]
        grad_router = extra[:, :tokens] + extra[:, tokens : 2 * tokens]
        grad_router = jnp.transpose(jnp.concatenate([grad_router, jnp.zeros((128 - EXPERTS, tokens), F32)], 0))
        logits = dot(h, wr_ref[...])
        logits = jnp.where(lane_iota(logits.shape) < EXPERTS, logits, MASKED)
        raw = jnp.exp(logits - jnp.max(logits, -1, keepdims=True))
        router = raw / jnp.sum(raw, -1, keepdims=True)
        grad_logits = (router * (grad_router - jnp.sum(router * grad_router, -1, keepdims=True))).astype(BF16)
        grad_h = arrived[:tokens, :] + dot(grad_logits, wr_ref[...], NT)
        normed, scale = norm_parts(middle_ref[...])
        dgain[1:2, :] = jnp.sum(grad_h * normed, 0, keepdims=True)
        for copy in copies[:3]:
            copy.wait()
        grad_mid = cot[...] + norm_back(grad_h * gain, normed, scale)
        grad_middle[...] = grad_mid
        grad_branch = (RESIDUAL * grad_mid).astype(BF16)
        for c in range(n):
            ga[c] = dot(grad_branch, wo[c], NT).astype(BF16)
        ga_exchange = (ga, ga_in, ga_send, ga_recv, local_sems.at[2], n)
        exchange_start(*ga_exchange)
        go_on()
        col[:, :128] = dot(h, grad_logits, TN).astype(BF16)
        for r in range(8):
            at = strip(r)
            dwo = dot(attn[at], grad_branch, TN).astype(BF16)
            small[r, 0:128, :] = dwo[:, :PIECE]
            small[r, 128:256, :] = dwo[:, PIECE:]
            small[r, 256:384, 0:128] = col[pl.ds(pl.multiple_of(at * 128, 128), 128), 0:128]
        ws.start()
        ys.start()
        go_on()
        copies[3].wait()
        for hh in range(2):
            for c in range(n):
                kk, vv = pair_keys(packs[c, hh, :, 128:256].astype(F32))
                at = hh * half + c * rows
                keys[at : at + rows, :] = kk.astype(BF16)
                values[at : at + rows, :] = vv.astype(BF16)
                keys_t[:, at : at + rows] = jnp.transpose(kk).astype(BF16)
        grad_k[...] = jnp.zeros_like(grad_k)
        grad_v[...] = jnp.zeros_like(grad_v)
        go_on()
        ws.over_cores()
        ys.over_cores()
        go_on()
        exchange_wait(*ga_exchange)

        per = BLK // rows
        per_half = blocks // 2

        def fetch_full(b):
            return pltpu.make_async_copy(full_ref.at[b], full_buf.at[lax.rem(b, 2)], full_sems.at[lax.rem(b, 2)])

        fetch_full(jnp.int32(0)).start()
        attend_tick = at_tick[0]

        def attend(block, carry):
            late = block // per_half
            c0 = lax.rem(block, per_half) * per
            q2 = stack_heads(jnp.concatenate([packs[c0 + k, late, :, :128] for k in range(per)], 0))
            g2 = stack_heads(jnp.concatenate([ga_in[c0 + k, pl.ds(pl.multiple_of(late * rows, rows), rows), :] for k in range(per)], 0))
            position, start = query_rows(ends_ref, block, length)
            lse = lse_ref[block]

            @pl.when(block + 1 < blocks)
            def _():
                fetch_full(block + 1).start()

            fetch_full(block).wait()
            delta = jnp.sum(jnp.transpose(g2.astype(F32)) * full_buf[lax.rem(block, 2)], 0, keepdims=True)
            acc[...] = jnp.zeros_like(acc)

            def body(kb, carry):
                at = pl.multiple_of(kb * BLK, BLK)
                scores = dot(keys[pl.ds(at, BLK), :], q2, NT) * ATTN_SCALE
                where = key_position(kb, length)
                probs = jnp.where((where <= position) & (where >= start), jnp.exp(scores - lse), 0.0)
                grad_probs = dot(values[pl.ds(at, BLK), :], g2, NT)
                grad_scores = (probs * (grad_probs - delta)).astype(BF16)
                acc[...] += dot(keys_t[:, pl.ds(at, BLK)], grad_scores)
                grad_k[pl.ds(at, BLK), :] += dot(grad_scores, q2)
                grad_v[pl.ds(at, BLK), :] += dot(probs.astype(BF16), g2)
                return carry

            block_loop(block, per_half, body, 0)
            grad_q[pl.ds(pl.multiple_of(block * BLK, BLK), BLK), :] = fold_heads(jnp.transpose(acc[...]))

            @pl.when((block == 1) | (block >= 3))
            def _():
                tick(attend_tick + jnp.where(block == 1, 0, block - 2))

            return carry

        lax.fori_loop(0, blocks, attend, 0)
        at_tick[0] += blocks - 2
        copies[4].wait()
        for c in range(n):
            for hh in range(2):
                at = slice(hh * half + c * rows, hh * half + (c + 1) * rows)
                kk = grad_k[at, :]
                vv = grad_v[at, :]
                kk = (kk + pltpu.roll(kk, 64, 1)) * ATTN_SCALE
                vv = vv + pltpu.roll(vv, 64, 1)
                both = jnp.where(lane_iota(kk.shape) < 64, kk, vv)
                package = jnp.concatenate([grad_q[at, :] * ATTN_SCALE, both], -1)
                pack_out[c, hh * rows : (hh + 1) * rows, :] = turn(package, table[at, :], -1.0).astype(BF16)
        gr_exchange = (pack_out, grads_in, gr_send, gr_recv, local_sems.at[3], n)
        exchange_start(*gr_exchange)

        def fetch_w(c):
            slot = lax.rem(c, 2)
            return pltpu.make_async_copy(weights_ref.at[:, :, pl.ds(pl.multiple_of(c * PACK, PACK), PACK)], wbuf.at[slot], w_sems.at[slot])

        fetch_w(jnp.int32(0)).start()
        go_on()
        ws.over_x()
        ys.over_x()
        go_on(2)
        total[...] = jnp.zeros_like(total)
        late_pieces[:PIECE] = ws.finish().astype(BF16)
        ws.release()
        ffn = ys.finish()
        mixed_ref[...] = middle_ref[...] + RESIDUAL * jnp.concatenate([ffn[:tokens], ffn[tokens:]], 1)
        go_on(5)
        exchange_wait(*gr_exchange)
        copies[5].wait()
        copies[6].wait()

        columns_tick = at_tick[0]

        def finish_columns(c, carry):
            @pl.when(c + 1 < n)
            def _():
                fetch_w(c + 1).start()

            fetch_w(c).wait()
            slot = lax.rem(c, 2)
            g = grads_in[c]
            col[...] = dot(h_attn[...], g, TN).astype(BF16)
            for r in range(8):
                at = pl.ds(pl.multiple_of(strip(r) * 128, 128), 128)
                columns[r, pl.ds(pl.multiple_of(c // 2 * 128, 128), 128), pl.ds(pl.multiple_of(lax.rem(c, 2) * PACK, PACK), PACK)] = col[at, :]
            for f in range(4):
                total[:, f * shard : (f + 1) * shard] += dot(g, wbuf[slot, f, :shard, :], NT)

            @pl.when(lax.rem(c, 4) == 3)
            def _():
                tick(columns_tick + c // 4)

            return carry

        lax.fori_loop(0, n, finish_columns, 0)
        at_tick[0] += n // 4
        normed, scale = norm_parts(x_in[...])
        grad_h = total[...]
        dgain[0:1, :] = jnp.sum(grad_h * normed, 0, keepdims=True)
        grad_x_ref[...] = grad_middle[...] + norm_back(grad_h * gains_ref[0:1], normed, scale)
        for r in range(8):
            at = pl.ds(pl.multiple_of(strip(r) * 128, 128), 128)
            row = row_iota((16, 128))
            both = jnp.where(row == 0, dgain[0:1, at], jnp.where(row == 1, dgain[1:2, at], 0.0))
            columns[r, PIECE:, 0:128] = both.astype(BF16)
        cs.start()
        go_on()
        cs.over_cores()
        go_on(4)
        cs.over_x(go_on)
        go_on(4)
        summed = cs.finish().astype(BF16)
        late_pieces[PIECE:] = summed[:PIECE]
        late_pieces[384:400] = summed[PIECE:]

    f32, bf = (lambda *shape: pltpu.VMEM(shape, F32)), (lambda *shape: pltpu.VMEM(shape, BF16))
    pl.run_scoped(
        backward,
        bf(*packs_hbm.shape),
        f32(*table_hbm.shape),
        bf(length, 128),
        bf(length, 128),
        bf(128, length),
        f32(length, 128),
        f32(length, 128),
        f32(length, 128),
        f32(128, 2 * BLK),
        f32(2, 128, 2 * BLK),
        bf(n, tokens, 128),
        bf(n, tokens, PACK),
        bf(2, 4, weights_ref.shape[1], PACK),
        f32(tokens, width),
        f32(tokens, width),
        f32(8, width),
        bf(width, PACK),
        bf(8, PIECE, PIECE),
        bf(8, PIECE + 16, PIECE),
        f32(tokens, width),
        bf(*wo_hbm.shape),
        bf(*attn_hbm.shape),
        f32(tokens, width),
        bf(tokens, width),
    )

    def rest(t, carry):
        tick(t)
        return carry

    lax.fori_loop(at_tick[0], early, rest, 0)

    def late_source(t):
        return late_pieces.at[pl.ds(pl.multiple_of((t - early) * sub, sub), sub)]

    def late(t, carry):
        line.tick(t, late_source)
        return carry

    lax.fori_loop(early, line.count + LAG_END, late, 0)
    line.finish()


def backward_step(ends, xs, gs, gates, w_gate, w_up, w_down, cxs, rest, full, weights, packs, table, cot, wo, attn, x, h_attn, h, middle, wr, gains, lse, n, length, capp):
    tokens, width = x.shape
    number, slots_rows, _ = xs.shape
    hbm, vmem = pl.BlockSpec(memory_space=pl.ANY), pl.BlockSpec(memory_space=pltpu.VMEM)
    smem = pl.BlockSpec(memory_space=pltpu.SMEM)
    dma = lambda *k: pltpu.SemaphoreType.DMA(k)
    shaped = lambda shape, dtype=BF16: jax.ShapeDtypeStruct(shape, dtype)
    sub = PIECE // 2
    piece = (sub, PIECE)
    count = (number * 6 + 2) * 2
    land_rows = max(2 * (tokens + EXPERTS), PIECE + 16)
    return pl.pallas_call(
        functools.partial(backward_kernel, n, length, capp),
        in_specs=[smem] + [hbm] * 17 + [vmem] * 5,
        out_specs=[hbm] * 7 + [vmem, vmem],
        out_shape=[
            shaped((count,) + piece),
            shaped((count,) + piece),
            shaped((number * 6, PIECE, PIECE)),
            shaped(xs.shape),
            shaped(xs.shape),
            shaped((8, 2 * (tokens + EXPERTS), PIECE)),
            shaped((8, 2 * tokens, PIECE)),
            shaped((tokens, width), F32),
            shaped((tokens, width), F32),
        ],
        scratch_shapes=[
            pltpu.VMEM((RING,) + piece, BF16),
            pltpu.VMEM((RING,) + piece, BF16),
            pltpu.VMEM((4,) + piece, BF16),
            pltpu.VMEM((4, land_rows, PIECE), BF16),
            pltpu.VMEM((2, land_rows, PIECE), BF16),
            pltpu.VMEM((land_rows, PIECE), BF16),
            pltpu.VMEM((4, 2 * tokens, PIECE), BF16),
            pltpu.VMEM((2, 2 * tokens, PIECE), BF16),
            pltpu.VMEM((2 * tokens, PIECE), BF16),
            pltpu.VMEM((2, 2 * tokens, PIECE), BF16),
            pltpu.VMEM((2 * PIECE, PIECE), BF16),
            pltpu.VMEM((n, tokens, 128), BF16),
            pltpu.VMEM((n, tokens, PACK), BF16),
            dma(RING),
            dma(RING),
            dma(RING),
            dma(RING),
            dma(RING),
            dma(count),
            dma(RING),
            dma(4),
            dma(n - 1),
            dma(n - 1),
            dma(n - 1),
            dma(n - 1),
            dma(4, 6, 4),
            dma(2),
            pltpu.SemaphoreType.REGULAR((3,)),
            dma(11),
            dma(2),
            dma(2),
            dma(2, 6),
            dma(3),
            dma(2, 2),
            dma(2, 8),
        ],
        compiler_params=params(63, collective_id=0, has_side_effects=True),
        cost_estimate=cost(6e10, 1e9),
        name="backward_step",
    )(ends, xs, gs, gates, w_gate, w_up, w_down, cxs, rest, full, weights, packs, table, cot, wo, attn, x, h_attn, h, middle, wr, gains, lse)


def local(
    inputs,
    cotangent,
    doc_lengths,
    routes,
    attn_gain,
    ffn_gain,
    w_query,
    key_weight,
    value_weight,
    w_out,
    w_router,
    w_gate,
    w_up,
    w_down,
):
    rows = inputs.shape[2]
    width = inputs.shape[3]
    n = lax.axis_size("ctx")
    fsdp = lax.axis_size("fsdp")
    me, mine = lax.axis_index("ctx"), lax.axis_index("fsdp")
    tokens = 2 * rows
    length = tokens * n
    experts_here = w_gate.shape[0]
    number = experts_here // 2
    capacity = 5 * tokens * TOP // (4 * EXPERTS)
    capp = -(-capacity // 16) * 16
    shard = width // fsdp
    heads = QUERY_HEADS // n
    head_lanes = heads * HEAD_DIMENSION
    copies = n // KEY_VALUE_HEADS
    bits = group_bits(fsdp)

    x = inputs.reshape(tokens, width)
    cot = cotangent.reshape(tokens, width)
    side = me % 2
    base = (side * number).astype(jnp.int32).reshape(1)
    first = (mine * experts_here + side * number).astype(jnp.int32).reshape(1)
    index = jnp.stack([side * number, (1 - side) * number]).astype(jnp.int32)
    ends = jnp.cumsum(doc_lengths[0])[:3].astype(jnp.int32)
    table = jnp.asarray(rotary_table(length))

    out_part = w_out.reshape(shard // head_lanes, head_lanes, width)
    if head_lanes < 128:
        out_part = jnp.pad(out_part, ((0, 0), (0, 128 - head_lanes), (0, 0)))
    merge = lambda a: a.reshape(number, -1, a.shape[-1])

    if n == 8 and fsdp == 4:
        packs, h_attn, weights, wo, wr, cxs, gains = front(
            w_query,
            key_weight,
            value_weight,
            out_part,
            w_router,
            attn_gain.reshape(1, shard),
            ffn_gain.reshape(1, shard),
            x,
            table.reshape(2, n, rows, 256),
            routes.reshape(tokens, TOP),
            cot,
            capacity,
            n,
        )
        wo, wr = wo.reshape(n, 128, width), wr.reshape(width, 128)
        packs = packs.reshape(n, 2, rows, PACK)
        attn, lse, full, cx_rest = attend(ends, packs, cxs, length)
        middle, h_ffn, attn, xs, gs, gates = mid_step(attn.reshape(n, tokens, 128), cxs, cx_rest, wo, wr, x, gains[1:2], number, capp, n)
        own, other, _, _, _, _, _, grad_x, mixed = backward_step(
            ends,
            merge(xs),
            merge(gs),
            merge(gates),
            w_gate,
            w_up,
            w_down,
            cxs,
            cx_rest,
            full,
            weights,
            packs,
            table,
            cot,
            wo,
            attn,
            x,
            h_attn,
            h_ffn,
            middle,
            wr,
            gains,
            lse,
            n,
            length,
            capp,
        )
        own, other = own.reshape(-1, PIECE, PIECE), other.reshape(-1, PIECE, PIECE)
        shapes = [w.shape for w in (w_gate, w_up, w_down)]
        outs = tail(index, own, other, mixed, grad_x, shapes, shard)
        return (
            outs[3].reshape(inputs.shape),
            outs[4].reshape(inputs.shape),
            outs[10].reshape(shard),
            outs[11].reshape(shard),
            outs[5],
            outs[6],
            outs[7],
            outs[8],
            outs[9],
            outs[0],
            outs[1],
            outs[2],
        )

    else:
        own_table = lax.dynamic_slice_in_dim(table.reshape(2, n, rows, 256), me, 1, 1).reshape(tokens, 256)
        query_part = w_query.reshape(shard, n, head_lanes)
        if head_lanes < 128:
            query_part = jnp.pad(query_part, ((0, 0), (0, 0), (0, 128 - head_lanes)))
        key_part = jnp.repeat(key_weight.reshape(shard, KEY_VALUE_HEADS, HEAD_DIMENSION), copies, 1)
        value_part = jnp.repeat(value_weight.reshape(shard, KEY_VALUE_HEADS, HEAD_DIMENSION), copies, 1)
        packed = jnp.concatenate([query_part, key_part, value_part], -1).reshape(shard, n * PACK)
        padding = 2 * 16 * (shard // 32 + 1) - shard
        gains = jnp.pad(jnp.stack([attn_gain, ffn_gain]), ((0, padding - 2), (0, n * PACK - shard)))
        packed = jnp.concatenate([packed, gains], 0)
        router_part = jnp.pad(w_router, ((0, 0), (0, 128 - EXPERTS)))
        weights = lax.all_gather(packed, "fsdp", axis=0)
        gain_one = weights[:, shard, :shard].reshape(1, width).astype(F32)
        gain_two = weights[:, shard + 1, :shard].reshape(1, width).astype(F32)
        wo = lax.all_gather(out_part, "fsdp", axis=0, tiled=True)
        wr = lax.all_gather(router_part, "fsdp", axis=0, tiled=True)
        cxs = group_gather(prep(routes.reshape(tokens, TOP), cot, capacity), bits)
        packs, h_attn = qkv(x, gain_one, weights, own_table, shard, n)
        packs = lax.all_to_all(packs, "ctx", split_axis=0, concat_axis=0, tiled=True).reshape(n, 2, rows, PACK)
        attn, lse, full = attn_forward(ends, packs, length)
        attn = lax.all_to_all(attn.reshape(n, tokens, 128), "ctx", split_axis=0, concat_axis=0, tiled=True)
        middle, h_ffn = middle_step(attn, wo, x, gain_two)
        xs, gs, gates = gather_rows(first, group_gather(h_ffn, bits), cxs, jnp.transpose(wr), number, capp)
        slots = cxs[:, tokens:]
    xs, gs, gates = merge(xs), merge(gs), merge(gates)
    pieces, outs, back, dgates = expert_step(base, xs, gs, gates, w_gate, w_up, w_down)
    y_part, gx_part = combine(first, slots, outs, back, dgates, tokens, capp)
    pieces = pieces.reshape(number * 6, PIECE, PIECE)
    gx = group_reduce(gx_part, bits)
    grad_middle, dwo, grad_attn, dwr, dgain_two = home_step(gx, h_ffn, middle, cot, wr, wo, gain_two, attn)
    grad_attn = lax.all_to_all(grad_attn, "ctx", split_axis=0, concat_axis=0, tiled=True).reshape(n, 2, rows, 128)
    grads = attn_backward(ends, packs, grad_attn, lse, full, table, length)
    grads = lax.all_to_all(grads.reshape(n, tokens, PACK), "ctx", split_axis=0, concat_axis=0, tiled=True)
    dw, grad_x, dgain_one = final_step(grads, weights, h_attn, x, gain_one, grad_middle, shard)
    mixed = middle + RESIDUAL * group_reduce(y_part, bits).astype(F32)
    own = line_sum(pieces, n)
    other = swap(own, "ctx", 1)
    scatter = lambda a: lax.psum(lax.psum_scatter(a, "fsdp", scatter_dimension=0, tiled=True), "ctx").astype(F32)
    dwo = scatter(dwo)[:, :head_lanes, :].reshape(shard, width)
    small = jnp.concatenate([dwr[:, :EXPERTS], dgain_two.reshape(width, 1).astype(BF16)], 1)
    small = scatter(jnp.pad(small, ((0, 0), (0, 127 - EXPERTS))))
    dwr, dgain_two = small[:, :EXPERTS], small[:, EXPERTS]
    dw = scatter(dw).reshape(shard, n, PACK)
    dgain_one = scatter(dgain_one.reshape(width).astype(BF16))

    outs = widen(index, own, other, [w.shape for w in (w_gate, w_up, w_down)])
    fold = lambda a: a.reshape(shard, KEY_VALUE_HEADS, copies, HEAD_DIMENSION).sum(2).reshape(shard, -1)
    return (
        mixed.reshape(inputs.shape),
        grad_x.reshape(inputs.shape),
        dgain_one,
        dgain_two,
        dw[:, :, :head_lanes].reshape(shard, -1),
        fold(dw[:, :, 128:192]),
        fold(dw[:, :, 192:256]),
        dwo,
        dwr,
        outs[0],
        outs[1],
        outs[2],
    )


def solution(mesh):
    tokens = P("fsdp", None, "ctx", None)
    one, two, three = P("fsdp"), P("fsdp", None), P("fsdp", None, None)
    return jax.shard_map(
        local,
        mesh=mesh,
        in_specs=(tokens, tokens, two, tokens, one, one, two, two, two, two, two, three, three, three),
        out_specs=(tokens, tokens, one, one, two, two, two, two, two, three, three, three),
        check_vma=False,
    )
```

```python
import functools

import jax
import jax.numpy as jnp
import numpy as np
from jax import lax
from jax.experimental import pallas as pl
from jax.experimental.pallas import tpu as pltpu
from jax.sharding import PartitionSpec as P

QUERY_HEADS = 16
KEY_VALUE_HEADS = 8
HEAD_DIMENSION = 64
EXPERTS = 32
TOP = 8

ATTN_SCALE = 0.015625
RESIDUAL = 0.22
NORM_EPS = 1e-06
ROPE_BASE = 10000.0
MASKED = -1e30

F32 = jnp.float32
BF16 = jnp.bfloat16
MIB = 1 << 20
NT = (((1,), (1,)), ((), ()))
TN = (((0,), (0,)), ((), ()))
BLK = 256
PACK = 256


def dot(a, b, dims=None):
    if dims is None:
        return jnp.dot(a, b, preferred_element_type=F32)
    return lax.dot_general(a, b, dims, preferred_element_type=F32)


def params(limit=56, **kw):
    return pltpu.CompilerParams(vmem_limit_bytes=limit * MIB, **kw)


def cost(flops, bytes_accessed):
    return pl.CostEstimate(flops=int(flops), bytes_accessed=int(bytes_accessed), transcendentals=0)


def lane_iota(shape):
    return lax.broadcasted_iota(jnp.int32, shape, len(shape) - 1)


def row_iota(shape):
    return lax.broadcasted_iota(jnp.int32, shape, len(shape) - 2)


def rotary_table(length):
    half = length // 2
    order = np.arange(half, dtype=np.float32)
    positions = np.concatenate([order, length - 1 - order]).astype(np.float32)
    m = np.arange(HEAD_DIMENSION // 2, dtype=np.float64)
    frequency = (ROPE_BASE ** (-2.0 * m / HEAD_DIMENSION)).astype(np.float32)
    angles = (positions[:, None] * frequency[None, :]).astype(np.float64)
    cosine, sine = np.cos(angles), np.sin(angles)
    cos_head = np.concatenate([cosine, cosine], -1)
    sin_head = np.concatenate([-sine, sine], -1)
    return np.concatenate([cos_head, cos_head, sin_head, sin_head], -1).astype(np.float32)


def turn(v, table, direction):
    lanes = lane_iota(v.shape)
    cosine = jnp.concatenate([table[:, :128], table[:, :128]], -1)
    sine = jnp.concatenate([table[:, 128:], table[:, 128:]], -1)
    turned = lanes < 3 * HEAD_DIMENSION
    swapped = jnp.where(lanes % HEAD_DIMENSION < HEAD_DIMENSION // 2, pltpu.roll(v, PACK - 32, 1), pltpu.roll(v, 32, 1))
    return jnp.where(turned, v * cosine + direction * (swapped * sine), v)


def norm_parts(values):
    inv_rms = lax.rsqrt(jnp.mean(values * values, -1, keepdims=True) + NORM_EPS)
    return values * inv_rms, inv_rms


def norm_back(grad_normed, normed, inv_rms):
    return inv_rms * (grad_normed - normed * jnp.mean(grad_normed * normed, -1, keepdims=True))


def prep_kernel(cap, routes_ref, cot_ref, out_ref):
    tokens, width = cot_ref.shape
    earlier = (row_iota((tokens, tokens)) < lane_iota((tokens, tokens))).astype(BF16)
    experts = row_iota((EXPERTS, tokens))
    base = jnp.zeros((EXPERTS, 1), F32)
    plus = jnp.zeros((EXPERTS, tokens), F32)
    for k in range(TOP):
        row = jnp.concatenate([routes_ref[0, k : k + 1, :], routes_ref[1, k : k + 1, :]], 1)
        chosen = experts == row
        ones = chosen.astype(F32)
        slot = dot(ones.astype(BF16), earlier) + base
        plus = plus + jnp.where(chosen & (slot < cap), slot + 1.0, 0.0)
        base = base + jnp.sum(ones, 1, keepdims=True)
    out_ref[:tokens, :] = cot_ref[...].astype(BF16)
    out_ref[tokens:, :] = jnp.concatenate([plus - 1.0, jnp.zeros((EXPERTS, width - tokens), F32)], -1).astype(BF16)


def prep(routes, cot, cap):
    tokens, width = cot.shape
    return pl.pallas_call(
        functools.partial(prep_kernel, cap),
        out_shape=jax.ShapeDtypeStruct((tokens + EXPERTS, width), BF16),
        compiler_params=params(),
        cost_estimate=cost(1e9, 2e6),
        name="prep",
    )(routes, cot)


def qkv_kernel(shard, x_ref, gain_ref, w_ref, table_ref, out_ref, h_ref):
    @pl.when(pl.program_id(0) == 0)
    def _():
        normed, _ = norm_parts(x_ref[...])
        h_ref[...] = (normed * gain_ref[...]).astype(BF16)

    total = None
    for f in range(w_ref.shape[0]):
        part = dot(h_ref[:, f * shard : (f + 1) * shard], w_ref[f, :shard, :])
        total = part if total is None else total + part
    for d in range(out_ref.shape[0]):
        out_ref[d] = turn(total[:, d * PACK : (d + 1) * PACK], table_ref[...], 1.0).astype(BF16)


def qkv(x, gain, weights, table, shard, n):
    tokens, width = x.shape
    fsdp, padded, _ = weights.shape
    return pl.pallas_call(
        functools.partial(qkv_kernel, shard),
        grid=(n // 2,),
        in_specs=[
            pl.BlockSpec((tokens, width), lambda i: (0, 0)),
            pl.BlockSpec((1, width), lambda i: (0, 0)),
            pl.BlockSpec((fsdp, padded, 2 * PACK), lambda i: (0, 0, i)),
            pl.BlockSpec((tokens, 256), lambda i: (0, 0)),
        ],
        out_specs=[
            pl.BlockSpec((2, tokens, PACK), lambda i: (i, 0, 0)),
            pl.BlockSpec((tokens, width), lambda i: (0, 0)),
        ],
        out_shape=[
            jax.ShapeDtypeStruct((n, tokens, PACK), BF16),
            jax.ShapeDtypeStruct((tokens, width), BF16),
        ],
        compiler_params=params(),
        cost_estimate=cost(2 * tokens * width * n * PACK, 8e6),
        name="qkv",
    )(x, gain, weights, table)


def pair_keys(kv):
    other = pltpu.roll(kv, 64, 1)
    low = lane_iota(kv.shape) < 64
    return jnp.where(low, kv, other), jnp.where(low, other, kv)


def stack_heads(q):
    low = lane_iota(q.shape) < 64
    zero = jnp.zeros_like(q)
    return jnp.concatenate([jnp.where(low, q, zero), jnp.where(low, zero, q)], 0)


def fold_heads(stacked):
    rows = stacked.shape[0] // 2
    return jnp.where(lane_iota((rows, 128)) < 64, stacked[:rows], stacked[rows:])


def query_rows(ends_ref, block, length):
    half = length // 2
    lanes = lane_iota((1, 2 * BLK))
    index = block * BLK + jnp.where(lanes < BLK, lanes, lanes - BLK)
    position = jnp.where(index < half, index, length + half - 1 - index)
    start = jnp.zeros_like(position)
    end = 0
    for j in range(3):
        end = end + ends_ref[0, j]
        start = jnp.where(position >= end, jnp.maximum(start, end), start)
    return position, start


def key_position(kb, length):
    half = length // 2
    index = kb * BLK + row_iota((BLK, 1))
    return jnp.where(index < half, index, length + half - 1 - index)


def block_loop(block, per_half, body, init):
    late = block >= per_half
    inner = jnp.where(late, block - per_half, block)
    count = jnp.where(late, 2 * per_half - inner, inner + 1)

    def step(j, carry):
        kb = jnp.where(late & (j >= per_half), inner + j, j)
        return body(kb, carry)

    return lax.fori_loop(0, count, step, init)


def load_package(pack_ref, c, h):
    return pack_ref[c, h].astype(F32)


def attn_forward_kernel(length, ends_ref, q_ref, pack_ref, out_ref, lse_ref, full_ref, keys, values_t, acc):
    block = pl.program_id(0)
    half = length // 2
    n, _, rows, _ = pack_ref.shape

    @pl.when(block == 0)
    def _():
        for h in range(2):
            for c in range(n):
                kk, vv = pair_keys(pack_ref[c, h, :, 128:256].astype(F32))
                at = h * half + c * rows
                keys[at : at + rows, :] = kk.astype(BF16)
                if rows % 128 == 0:
                    values_t[:, at : at + rows] = jnp.transpose(vv).astype(BF16)
        if rows % 128 != 0:
            for h in range(2):
                for c in range(0, n, 2):
                    pair = jnp.concatenate([pack_ref[c, h, :, 128:256], pack_ref[c + 1, h, :, 128:256]], 0)
                    _, vv = pair_keys(pair.astype(F32))
                    at = h * half + c * rows
                    values_t[:, at : at + 2 * rows] = jnp.transpose(vv).astype(BF16)

    q = q_ref[...].reshape(BLK, PACK)[:, :128]
    q2 = stack_heads(q)
    position, start = query_rows(ends_ref, block, length)
    acc[...] = jnp.zeros_like(acc)

    def body(kb, carry):
        peak, total = carry
        at = pl.multiple_of(kb * BLK, BLK)
        scores = dot(keys[pl.ds(at, BLK), :], q2, NT) * ATTN_SCALE
        where = key_position(kb, length)
        scores = jnp.where((where <= position) & (where >= start), scores, MASKED)
        new_peak = jnp.maximum(peak, jnp.max(scores, 0, keepdims=True))
        weights = jnp.exp(scores - new_peak)
        fade = jnp.exp(peak - new_peak)
        total = total * fade + jnp.sum(weights, 0, keepdims=True)
        acc[...] = acc[...] * fade + dot(values_t[:, pl.ds(at, BLK)], weights.astype(BF16))
        return new_peak, total

    init = (jnp.full((1, 2 * BLK), MASKED, F32), jnp.zeros((1, 2 * BLK), F32))
    peak, total = block_loop(block, half // BLK, body, init)
    result = acc[...] / total
    full_ref[0] = result
    lse_ref[0] = peak + jnp.log(total)
    folded = fold_heads(jnp.transpose(result)).astype(BF16)
    out_ref[...] = folded.reshape(out_ref.shape)


def attn_forward(ends, packs, length):
    n, _, rows, _ = packs.shape
    blocks, per = length // BLK, BLK // rows
    per_half = blocks // 2
    tiles = lambda i, ends: (lax.rem(i, per_half), i // per_half, 0, 0)
    return pl.pallas_call(
        functools.partial(attn_forward_kernel, length),
        grid_spec=pltpu.PrefetchScalarGridSpec(
            num_scalar_prefetch=1,
            grid=(blocks,),
            in_specs=[
                pl.BlockSpec((per, 1, rows, PACK), tiles),
                pl.BlockSpec(packs.shape, lambda i, ends: (0, 0, 0, 0)),
            ],
            out_specs=[
                pl.BlockSpec((per, 1, rows, 128), tiles),
                pl.BlockSpec((1, 1, 2 * BLK), lambda i, ends: (i, 0, 0)),
                pl.BlockSpec((1, 128, 2 * BLK), lambda i, ends: (i, 0, 0)),
            ],
            scratch_shapes=[
                pltpu.VMEM((length, 128), BF16),
                pltpu.VMEM((128, length), BF16),
                pltpu.VMEM((128, 2 * BLK), F32),
            ],
        ),
        out_shape=[
            jax.ShapeDtypeStruct((n, 2, rows, 128), BF16),
            jax.ShapeDtypeStruct((blocks, 1, 2 * BLK), F32),
            jax.ShapeDtypeStruct((blocks, 128, 2 * BLK), F32),
        ],
        compiler_params=params(),
        cost_estimate=cost(1.5e10, 6e6),
        name="attn_forward",
    )(ends, packs, packs)


def attn_backward_kernel(length, ends_ref, q_ref, g_ref, pack_ref, lse_ref, full_ref, table_ref, out_ref, keys, values, keys_t, grad_q, grad_k, grad_v, acc):
    block = pl.program_id(0)
    half = length // 2
    n, _, rows, _ = pack_ref.shape

    @pl.when(block == 0)
    def _():
        for h in range(2):
            for c in range(n):
                kk, vv = pair_keys(pack_ref[c, h, :, 128:256].astype(F32))
                at = h * half + c * rows
                keys[at : at + rows, :] = kk.astype(BF16)
                values[at : at + rows, :] = vv.astype(BF16)
        for b in range(length // BLK):
            keys_t[:, b * BLK : (b + 1) * BLK] = jnp.transpose(keys[b * BLK : (b + 1) * BLK, :].astype(F32)).astype(BF16)
        grad_k[...] = jnp.zeros_like(grad_k)
        grad_v[...] = jnp.zeros_like(grad_v)

    q2 = stack_heads(q_ref[...].reshape(BLK, PACK)[:, :128])
    g2 = stack_heads(g_ref[...].reshape(BLK, 128))
    position, start = query_rows(ends_ref, block, length)
    lse = lse_ref[0]
    delta = jnp.sum(jnp.transpose(g2.astype(F32)) * full_ref[0], 0, keepdims=True)
    acc[...] = jnp.zeros_like(acc)

    def body(kb, carry):
        at = pl.multiple_of(kb * BLK, BLK)
        scores = dot(keys[pl.ds(at, BLK), :], q2, NT) * ATTN_SCALE
        where = key_position(kb, length)
        probs = jnp.where((where <= position) & (where >= start), jnp.exp(scores - lse), 0.0)
        grad_probs = dot(values[pl.ds(at, BLK), :], g2, NT)
        grad_scores = (probs * (grad_probs - delta)).astype(BF16)
        acc[...] += dot(keys_t[:, pl.ds(at, BLK)], grad_scores)
        grad_k[pl.ds(at, BLK), :] += dot(grad_scores, q2)
        grad_v[pl.ds(at, BLK), :] += dot(probs.astype(BF16), g2)
        return carry

    block_loop(block, half // BLK, body, 0)
    grad_q[pl.ds(pl.multiple_of(block * BLK, BLK), BLK), :] = fold_heads(jnp.transpose(acc[...]))

    @pl.when(block == length // BLK - 1)
    def _():
        for h in range(2):
            for c in range(n):
                at = slice(h * half + c * rows, h * half + (c + 1) * rows)
                kk = grad_k[at, :]
                vv = grad_v[at, :]
                kk = (kk + pltpu.roll(kk, 64, 1)) * ATTN_SCALE
                vv = vv + pltpu.roll(vv, 64, 1)
                both = jnp.where(lane_iota(kk.shape) < 64, kk, vv)
                package = jnp.concatenate([grad_q[at, :] * ATTN_SCALE, both], -1)
                out_ref[c, h] = turn(package, table_ref[at, :], -1.0).astype(BF16)


def attn_backward(ends, packs, grads, lse, full, table, length):
    n, _, rows, _ = packs.shape
    blocks, per = length // BLK, BLK // rows
    per_half = blocks // 2
    tiles = lambda i, ends: (lax.rem(i, per_half), i // per_half, 0, 0)
    return pl.pallas_call(
        functools.partial(attn_backward_kernel, length),
        grid_spec=pltpu.PrefetchScalarGridSpec(
            num_scalar_prefetch=1,
            grid=(blocks,),
            in_specs=[
                pl.BlockSpec((per, 1, rows, PACK), tiles),
                pl.BlockSpec((per, 1, rows, 128), tiles),
                pl.BlockSpec(packs.shape, lambda i, ends: (0, 0, 0, 0)),
                pl.BlockSpec((1, 1, 2 * BLK), lambda i, ends: (i, 0, 0)),
                pl.BlockSpec((1, 128, 2 * BLK), lambda i, ends: (i, 0, 0)),
                pl.BlockSpec(table.shape, lambda i, ends: (0, 0)),
            ],
            out_specs=pl.BlockSpec(packs.shape, lambda i, ends: (0, 0, 0, 0)),
            scratch_shapes=[
                pltpu.VMEM((length, 128), BF16),
                pltpu.VMEM((length, 128), BF16),
                pltpu.VMEM((128, length), BF16),
                pltpu.VMEM((length, 128), F32),
                pltpu.VMEM((length, 128), F32),
                pltpu.VMEM((length, 128), F32),
                pltpu.VMEM((128, 2 * BLK), F32),
            ],
        ),
        out_shape=jax.ShapeDtypeStruct(packs.shape, BF16),
        compiler_params=params(),
        cost_estimate=cost(3e10, 8e6),
        name="attn_backward",
    )(ends, packs, grads, packs, lse, full, table)


def middle_kernel(attn_ref, wo_ref, x_ref, gain_ref, middle_ref, h_ref):
    total = None
    for c in range(attn_ref.shape[0]):
        part = dot(attn_ref[c], wo_ref[c])
        total = part if total is None else total + part
    middle = x_ref[...] + RESIDUAL * total
    middle_ref[...] = middle
    normed, _ = norm_parts(middle)
    h_ref[...] = (normed * gain_ref[...]).astype(BF16)


def middle_step(attn, wo, x, gain):
    tokens, width = x.shape
    return pl.pallas_call(
        middle_kernel,
        out_shape=[jax.ShapeDtypeStruct((tokens, width), F32), jax.ShapeDtypeStruct((tokens, width), BF16)],
        compiler_params=params(),
        cost_estimate=cost(2 * tokens * width * width, 5e6),
        name="middle",
    )(attn, wo, x, gain)


def own_row(table, row):
    return jnp.sum(jnp.where(row_iota(table.shape) == row, table, 0.0), 0, keepdims=True)


def one_hot(slots, first, number, capp):
    tokens = slots.shape[1]
    order = row_iota((capp, tokens)).astype(F32)
    return [(order == own_row(slots, first + j)).astype(F32) for j in range(number)]


def gather_kernel(number, capp, first_ref, h_ref, cx_ref, wrt_ref, x_ref, g_ref, gate_ref):
    tokens = h_ref.shape[1]
    first = first_ref[0]
    h = h_ref[0]
    slots = cx_ref[0, tokens:, :tokens].astype(F32)
    logits = dot(wrt_ref[...], h, NT)[:EXPERTS, :]
    raw = jnp.exp(logits - jnp.max(logits, 0, keepdims=True))
    router = raw / jnp.sum(raw, 0, keepdims=True)
    hots = one_hot(slots, first, number, capp)
    places = jnp.concatenate(hots, 0).astype(BF16)
    rows = dot(places, h).astype(BF16)
    grads = dot(places, cx_ref[0, :tokens, :]).astype(BF16)
    for j in range(number):
        at = slice(j * capp, (j + 1) * capp)
        x_ref[j, 0] = rows[at]
        g_ref[j, 0] = grads[at]
        gate = jnp.sum(hots[j] * own_row(router, first + j), 1, keepdims=True)
        gate_ref[j, 0] = jnp.broadcast_to(gate, (capp, 128))


def gather_rows(first, hs, cxs, wrt, number, capp):
    nb, tokens, width = hs.shape
    return pl.pallas_call(
        functools.partial(gather_kernel, number, capp),
        grid_spec=pltpu.PrefetchScalarGridSpec(
            num_scalar_prefetch=1,
            grid=(nb,),
            in_specs=[
                pl.BlockSpec((1, tokens, width), lambda b, f: (b, 0, 0)),
                pl.BlockSpec((1, tokens + EXPERTS, width), lambda b, f: (b, 0, 0)),
                pl.BlockSpec(wrt.shape, lambda b, f: (0, 0)),
            ],
            out_specs=[
                pl.BlockSpec((number, 1, capp, width), lambda b, f: (0, b, 0, 0)),
                pl.BlockSpec((number, 1, capp, width), lambda b, f: (0, b, 0, 0)),
                pl.BlockSpec((number, 1, capp, 128), lambda b, f: (0, b, 0, 0)),
            ],
        ),
        out_shape=[
            jax.ShapeDtypeStruct((number, nb, capp, width), BF16),
            jax.ShapeDtypeStruct((number, nb, capp, width), BF16),
            jax.ShapeDtypeStruct((number, nb, capp, 128), F32),
        ],
        compiler_params=params(),
        cost_estimate=cost(4 * nb * number * capp * tokens * width, 2e7),
        name="gather_rows",
    )(first, hs, cxs, wrt)


PIECE = 512


def expert_kernel(base_ref, x_ref, g_ref, gate_ref, wg_ref, wu_ref, wd_ref, piece_ref, out_ref, rows_ref, dg_ref):
    x = x_ref[0]
    gate = gate_ref[0][:, :1]
    grad_ffn = RESIDUAL * g_ref[0].astype(F32)
    go = (gate * grad_ffn).astype(BF16)
    part = wg_ref.shape[2] // 2
    out = rows = None
    for chunk in range(2):
        at = slice(chunk * part, (chunk + 1) * part)
        wg, wu, wd = wg_ref[0, :, at], wu_ref[0, :, at], wd_ref[0, at, :]
        pre_gate = dot(x, wg)
        pre_up = dot(x, wu)
        sig = jax.nn.sigmoid(pre_gate)
        hidden = (pre_gate * sig * pre_up).astype(BF16)
        out_part = dot(hidden, wd)
        grad_hidden = dot(go, wd, NT)
        grad_gate = (grad_hidden * pre_up * sig * (1.0 + pre_gate * (1.0 - sig))).astype(BF16)
        grad_up = (grad_hidden * pre_gate * sig).astype(BF16)
        row_part = dot(grad_gate, wg, NT) + dot(grad_up, wu, NT)
        dwg = dot(x, grad_gate, TN).astype(BF16)
        dwu = dot(x, grad_up, TN).astype(BF16)
        dwd = dot(hidden, go, TN).astype(BF16)
        for half in range(2):
            side = slice(half * PIECE, (half + 1) * PIECE)
            piece_ref[0, 3 * chunk + half, :, :part] = dwg[side]
            piece_ref[0, 3 * chunk + half, :, part:] = dwu[side]
            piece_ref[0, 3 * chunk + 2, half * part : (half + 1) * part, :] = dwd[:, side]
        out = out_part if out is None else out + out_part
        rows = row_part if rows is None else rows + row_part
    out = out.astype(BF16).astype(F32)
    out_ref[0] = (gate * out).astype(BF16)
    rows_ref[0] = rows.astype(BF16)
    grad = jnp.sum(grad_ffn * out, 1, keepdims=True)
    dg_ref[0] = jnp.broadcast_to(grad, dg_ref.shape[1:])


def expert_step(base, xs, gs, gates, w_gate, w_up, w_down):
    number, rows, width = xs.shape
    ff = w_gate.shape[2]
    row = lambda e, b: (e, 0, 0)
    weight = lambda e, b: (b[0] + e, 0, 0)
    return pl.pallas_call(
        expert_kernel,
        grid_spec=pltpu.PrefetchScalarGridSpec(
            num_scalar_prefetch=1,
            grid=(number,),
            in_specs=[
                pl.BlockSpec((1, rows, width), row),
                pl.BlockSpec((1, rows, width), row),
                pl.BlockSpec((1, rows, 128), row),
                pl.BlockSpec((1, width, ff), weight),
                pl.BlockSpec((1, width, ff), weight),
                pl.BlockSpec((1, ff, width), weight),
            ],
            out_specs=[
                pl.BlockSpec((1, 6, PIECE, PIECE), lambda e, b: (e, 0, 0, 0)),
                pl.BlockSpec((1, rows, width), row),
                pl.BlockSpec((1, rows, width), row),
                pl.BlockSpec((1, rows, 128), row),
            ],
        ),
        out_shape=[
            jax.ShapeDtypeStruct((number, 6, PIECE, PIECE), BF16),
            jax.ShapeDtypeStruct((number, rows, width), BF16),
            jax.ShapeDtypeStruct((number, rows, width), BF16),
            jax.ShapeDtypeStruct((number, rows, 128), F32),
        ],
        compiler_params=params(60),
        cost_estimate=cost(18 * number * rows * width * ff, 5e7),
        name="expert_step",
    )(base, xs, gs, gates, w_gate, w_up, w_down)


def combine_kernel(number, capp, first_ref, slot_ref, outs, rows, grads, y_ref, gx_ref):
    tokens = y_ref.shape[1]
    width = y_ref.shape[2]
    first = first_ref[0]
    slots = slot_ref[0][:, :tokens].astype(F32)
    hots = one_hot(slots, first, number, capp)
    places = jnp.concatenate(hots, 0).astype(BF16)
    y_ref[0] = dot(places, outs[:, 0].reshape(number * capp, width), TN).astype(BF16)
    gx_ref[0, :tokens] = dot(places, rows[:, 0].reshape(number * capp, width), TN).astype(BF16)
    extra = jnp.zeros((EXPERTS, 2 * tokens), F32)
    for j in range(number):
        grad = jnp.sum(hots[j] * grads[j, 0][:, :1], 0, keepdims=True)
        high = grad.astype(BF16).astype(F32)
        both = jnp.concatenate([high, grad - high], 1)
        extra = jnp.where(row_iota(extra.shape) == first + j, both, extra)
    rest = jnp.zeros((EXPERTS, width - 2 * tokens), F32)
    gx_ref[0, tokens:] = jnp.concatenate([extra, rest], 1).astype(BF16)


def combine(first, slots, outs, rows, grads, tokens, capp):
    number = outs.shape[0]
    nb, _, width = slots.shape
    split = lambda a: a.reshape(number, nb, capp, a.shape[-1])
    wide = pl.BlockSpec((number, 1, capp, width), lambda b, f: (0, b, 0, 0))
    thin = pl.BlockSpec((number, 1, capp, 128), lambda b, f: (0, b, 0, 0))
    return pl.pallas_call(
        functools.partial(combine_kernel, number, capp),
        grid_spec=pltpu.PrefetchScalarGridSpec(
            num_scalar_prefetch=1,
            grid=(nb,),
            in_specs=[pl.BlockSpec((1, EXPERTS, width), lambda b, f: (b, 0, 0))] + [wide, wide, thin],
            out_specs=[
                pl.BlockSpec((1, tokens, width), lambda b, f: (b, 0, 0)),
                pl.BlockSpec((1, tokens + EXPERTS, width), lambda b, f: (b, 0, 0)),
            ],
        ),
        out_shape=[
            jax.ShapeDtypeStruct((nb, tokens, width), BF16),
            jax.ShapeDtypeStruct((nb, tokens + EXPERTS, width), BF16),
        ],
        compiler_params=params(),
        cost_estimate=cost(4 * nb * number * capp * tokens * width, 2e7),
        name="combine",
    )(first, slots, split(outs), split(rows), split(grads))


def home_kernel(gx_ref, h_ref, middle_ref, cot_ref, wr_ref, wo_ref, gain_ref, attn_ref, grad_middle_ref, dwo_ref, ga_ref, dwr_ref, dgain_ref):
    tokens, width = h_ref.shape
    h = h_ref[...]
    gain = gain_ref[...]
    extra = gx_ref[tokens:, :].astype(F32)
    grad_router = extra[:, :tokens] + extra[:, tokens : 2 * tokens]
    grad_router = jnp.transpose(jnp.concatenate([grad_router, jnp.zeros((128 - EXPERTS, tokens), F32)], 0))
    logits = dot(h, wr_ref[...])
    logits = jnp.where(lane_iota(logits.shape) < EXPERTS, logits, MASKED)
    raw = jnp.exp(logits - jnp.max(logits, -1, keepdims=True))
    router = raw / jnp.sum(raw, -1, keepdims=True)
    grad_logits = (router * (grad_router - jnp.sum(router * grad_router, -1, keepdims=True))).astype(BF16)
    dwr_ref[...] = dot(h, grad_logits, TN).astype(BF16)
    grad_h = gx_ref[:tokens, :].astype(F32) + dot(grad_logits, wr_ref[...], NT)
    normed, scale = norm_parts(middle_ref[...])
    dgain_ref[...] = jnp.sum(grad_h * normed, 0, keepdims=True)
    grad_middle = cot_ref[...] + norm_back(grad_h * gain, normed, scale)
    grad_middle_ref[...] = grad_middle
    grad_branch = (RESIDUAL * grad_middle).astype(BF16)
    for c in range(attn_ref.shape[0]):
        dwo_ref[c] = dot(attn_ref[c], grad_branch, TN).astype(BF16)
        ga_ref[c] = dot(grad_branch, wo_ref[c], NT).astype(BF16)


def home_step(gx, h, middle, cot, wr, wo, gain, attn):
    tokens, width = h.shape
    n = attn.shape[0]
    return pl.pallas_call(
        home_kernel,
        out_shape=[
            jax.ShapeDtypeStruct((tokens, width), F32),
            jax.ShapeDtypeStruct((n, 128, width), BF16),
            jax.ShapeDtypeStruct((n, tokens, 128), BF16),
            jax.ShapeDtypeStruct((width, 128), BF16),
            jax.ShapeDtypeStruct((1, width), F32),
        ],
        compiler_params=params(),
        cost_estimate=cost(4 * tokens * width * width, 1e7),
        name="home_step",
    )(gx, h, middle, cot, wr, wo, gain, attn)


def final_kernel(shard, grads_ref, w_ref, h_ref, x_ref, gain_ref, grad_middle_ref, dw_ref, grad_x_ref, dgain_ref, total):
    c = pl.program_id(0)
    g = grads_ref[0]
    dw_ref[...] = dot(h_ref[...], g, TN).astype(BF16)

    @pl.when(c == 0)
    def _():
        total[...] = jnp.zeros_like(total)

    for f in range(w_ref.shape[0]):
        total[:, f * shard : (f + 1) * shard] += dot(g, w_ref[f, :shard, :], NT)

    @pl.when(c == pl.num_programs(0) - 1)
    def _():
        normed, scale = norm_parts(x_ref[...])
        grad_h = total[...]
        dgain_ref[...] = jnp.sum(grad_h * normed, 0, keepdims=True)
        grad_x_ref[...] = grad_middle_ref[...] + norm_back(grad_h * gain_ref[...], normed, scale)


def final_step(grads, weights, h, x, gain, grad_middle, shard):
    n, tokens, _ = grads.shape
    width = x.shape[1]
    fsdp, padded, _ = weights.shape
    same = lambda c: (0, 0)
    return pl.pallas_call(
        functools.partial(final_kernel, shard),
        grid=(n,),
        in_specs=[
            pl.BlockSpec((1, tokens, PACK), lambda c: (c, 0, 0)),
            pl.BlockSpec((fsdp, padded, PACK), lambda c: (0, 0, c)),
            pl.BlockSpec((tokens, width), same),
            pl.BlockSpec((tokens, width), same),
            pl.BlockSpec((1, width), same),
            pl.BlockSpec((tokens, width), same),
        ],
        out_specs=[
            pl.BlockSpec((width, PACK), lambda c: (0, c)),
            pl.BlockSpec((tokens, width), same),
            pl.BlockSpec((1, width), same),
        ],
        out_shape=[
            jax.ShapeDtypeStruct((width, n * PACK), BF16),
            jax.ShapeDtypeStruct((tokens, width), F32),
            jax.ShapeDtypeStruct((1, width), F32),
        ],
        scratch_shapes=[pltpu.VMEM((tokens, width), F32)],
        compiler_params=params(),
        cost_estimate=cost(4 * tokens * width * n * PACK, 1.2e7),
        name="final_step",
    )(grads, weights, h, x, gain, grad_middle)


def widen_kernel(number, index_ref, own_ref, other_ref, gate_ref, up_ref, down_ref):
    part = gate_ref.shape[2]

    def write(ref):
        for half in range(2):
            at = slice(half * PIECE, (half + 1) * PIECE)
            gate_ref[0, at, :] = ref[half, :, :part].astype(F32)
            up_ref[0, at, :] = ref[half, :, part:].astype(F32)
            down_ref[0, :, at] = ref[2, half * part : (half + 1) * part, :].astype(F32)

    @pl.when(pl.program_id(0) == 0)
    def _():
        write(own_ref)

    @pl.when(pl.program_id(0) == 1)
    def _():
        write(other_ref)


def tail_kernel(number, index_ref, own_ref, other_ref, own_small_ref, other_small_ref, mixed_in, grad_in, gate_ref, up_ref, down_ref, mixed_ref, grad_ref, dwq_ref, dwk_ref, dwv_ref, dwo_ref, dwr_ref, g1_ref, g2_ref):
    widen_kernel(number, index_ref, own_ref, other_ref, gate_ref, up_ref, down_ref)
    mixed_ref[...] = mixed_in[...]
    grad_ref[...] = grad_in[...]

    @pl.when((pl.program_id(0) == 0) & (pl.program_id(1) == 0) & (pl.program_id(2) == 0))
    def _():
        for which, ref in enumerate((own_small_ref, other_small_ref)):
            part = index_ref[which] // number
            at = pl.ds(pl.multiple_of(part * 128, 128), 128)
            for q in range(4):
                block = ref[1, q * 128 : (q + 1) * 128, :].astype(F32)
                dwq_ref[at, q * 256 : q * 256 + 128] = block[:, :128]
                dwq_ref[at, q * 256 + 128 : (q + 1) * 256] = block[:, 256:384]
                one, two = block[:, 128:256], block[:, 384:]
                low = lane_iota(one.shape) < HEAD_DIMENSION
                dwk_ref[at, q * 128 : (q + 1) * 128] = jnp.where(low, one, pltpu.roll(two, 64, 1))
                dwv_ref[at, q * 128 : (q + 1) * 128] = jnp.where(low, pltpu.roll(one, 64, 1), two)
            dwo_ref[at, :PIECE] = ref[0, 0:128, :].astype(F32)
            dwo_ref[at, PIECE:] = ref[0, 128:256, :].astype(F32)
            dwr_ref[:, at] = jnp.transpose(ref[0, 256:384, :128].astype(F32))[:EXPERTS]
            gains = ref[0, 384:400, :128].astype(F32)
            g1_ref[pl.ds(part, 1), :] = gains[0:1]
            g2_ref[pl.ds(part, 1), :] = gains[1:2]


def expert_specs(number, shapes):
    last = 2 * number - 1
    ins = [
        pl.BlockSpec((3, PIECE, PIECE), lambda s, e, h, at: (jnp.where(s == 0, 2 * e + h, last), 0, 0)),
        pl.BlockSpec((3, PIECE, PIECE), lambda s, e, h, at: (jnp.where(s == 0, 0, 2 * e + h), 0, 0)),
    ]
    _, width, ff = shapes[0]
    columns = pl.BlockSpec((1, width, ff // 2), lambda s, e, h, at: (at[s] + e, 0, h))
    rows = pl.BlockSpec((1, ff // 2, width), lambda s, e, h, at: (at[s] + e, h, 0))
    return ins, [columns, columns, rows], [jax.ShapeDtypeStruct(shape, F32) for shape in shapes]


def widen(index, own, other, shapes):
    number = shapes[0][0] // 2
    ins, outs, out_shapes = expert_specs(number, shapes)
    return pl.pallas_call(
        functools.partial(widen_kernel, number),
        grid_spec=pltpu.PrefetchScalarGridSpec(num_scalar_prefetch=1, grid=(2, number, 2), in_specs=ins, out_specs=outs),
        out_shape=out_shapes,
        compiler_params=params(),
        cost_estimate=cost(0, 1e8),
        name="widen",
    )(index, own, other)


def tail(index, own, other, mixed, grad_x, shapes, shard):
    number = shapes[0][0] // 2
    tokens, width = mixed.shape
    ins, outs, out_shapes = expert_specs(number, shapes)
    small = pl.BlockSpec((2, PIECE, PIECE), lambda s, e, h, at: (3 * number, 0, 0))
    rows = pl.BlockSpec((tokens // (4 * number), width), lambda s, e, h, at: ((s * number + e) * 2 + h, 0))
    small_shapes = [(shard, width), (shard, width // 2), (shard, width // 2), (shard, width), (EXPERTS, shard), (2, 128), (2, 128)]
    whole = [pl.BlockSpec(shape, lambda s, e, h, at: (0, 0)) for shape in small_shapes]
    return pl.pallas_call(
        functools.partial(tail_kernel, number),
        grid_spec=pltpu.PrefetchScalarGridSpec(
            num_scalar_prefetch=1,
            grid=(2, number, 2),
            in_specs=ins + [small, small, rows, rows],
            out_specs=outs + [rows, rows] + whole,
        ),
        out_shape=out_shapes
        + [jax.ShapeDtypeStruct((tokens, width), F32)] * 2
        + [jax.ShapeDtypeStruct(shape, F32) for shape in small_shapes],
        compiler_params=params(),
        cost_estimate=cost(0, 1e8),
        name="tail",
    )(index, own, other, own, other, mixed, grad_x)


def swap(value, axis, bit):
    size = lax.axis_size(axis)
    return lax.ppermute(value, axis, [(i, i ^ bit) for i in range(size)])


def group_bits(fsdp):
    bits = [("fsdp", 1 << b) for b in range(1, fsdp.bit_length() - 1)]
    return bits + [("ctx", 1), ("fsdp", 1)]


def group_gather(value, bits):
    stacked = value[None]
    for axis, bit in bits:
        stacked = jnp.concatenate([stacked, swap(stacked, axis, bit)], 0)
    return stacked


def group_reduce(stacked, bits):
    for axis, bit in reversed(bits):
        half = stacked.shape[0] // 2
        arrived = swap(stacked[half:], axis, bit)
        stacked = (stacked[:half].astype(F32) + arrived.astype(F32)).astype(stacked.dtype)
    return stacked[0]


def line_sum(value, ctx):
    pairs = ctx // 2
    if pairs != 4:
        bit = 2
        while bit < ctx:
            value = value + swap(value, "ctx", bit)
            bit *= 2
        return value
    at = lambda z, y: 2 * z + y
    inward = [(at(0, y), at(1, y)) for y in range(2)] + [(at(3, y), at(2, y)) for y in range(2)]
    across = [(at(1, y), at(2, y)) for y in range(2)] + [(at(2, y), at(1, y)) for y in range(2)]
    outward = [(b, a) for a, b in inward]
    value = value + lax.ppermute(value, "ctx", inward)
    value = value + lax.ppermute(value, "ctx", across)
    arrived = lax.ppermute(value, "ctx", outward)
    z = lax.axis_index("ctx") // 2
    return jnp.where((z == 0) | (z == 3), arrived, value)


MESH = pl.DeviceIdType.MESH


def flip(index, bit):
    return jnp.where((index // bit) % 2 == 0, index + bit, index - bit)


def send(src, dst, send_sem, recv_sem, device):
    return pltpu.make_async_remote_copy(src_ref=src, dst_ref=dst, send_sem=send_sem, recv_sem=recv_sem, device_id=device, device_id_type=MESH)


def neighbours():
    ctx, fsdp = lax.axis_index("ctx"), lax.axis_index("fsdp")
    side, across = flip(ctx, 1), flip(fsdp, 2)
    core = {"fsdp": flip(fsdp, 1)}
    return core, [{"fsdp": across}, {"ctx": side}, {"ctx": side, "fsdp": across}]


def greet(devices):
    barrier = pltpu.get_barrier_semaphore()
    for device in devices:
        pl.semaphore_signal(barrier, inc=1, device_id=device, device_id_type=MESH)
    pl.semaphore_wait(barrier, len(devices))


def others(n):
    ctx = lax.axis_index("ctx")
    return [lax.rem(ctx + d, n) for d in range(1, n)]


def exchange_start(src, dst, send_sems, recv_sems, local_sem, n):
    ctx = lax.axis_index("ctx")
    for d, c in enumerate(others(n)):
        send(src.at[c], dst.at[ctx], send_sems.at[d], recv_sems.at[d], {"ctx": c}).start()
    pltpu.make_async_copy(src.at[ctx], dst.at[ctx], local_sem).start()


def exchange_wait(src, dst, send_sems, recv_sems, local_sem, n, arrived=None):
    ctx = lax.axis_index("ctx")
    pltpu.make_async_copy(src.at[ctx], dst.at[ctx], local_sem).wait()
    if arrived is not None:
        arrived(ctx)
    for d in range(n - 1):
        source = lax.rem(ctx + n - 1 - d, n)
        send(src.at[source], dst.at[source], send_sems.at[d], recv_sems.at[d], {"ctx": source}).wait_recv()
        if arrived is not None:
            arrived(source)
    for d, c in enumerate(others(n)):
        send(src.at[c], dst.at[ctx], send_sems.at[d], recv_sems.at[d], {"ctx": c}).wait_send()


def turn_half(v, table, direction, lanes_turned):
    lanes = lane_iota(v.shape)
    swapped = jnp.where(lanes % HEAD_DIMENSION < HEAD_DIMENSION // 2, pltpu.roll(v, 96, 1), pltpu.roll(v, 32, 1))
    return jnp.where(lanes < lanes_turned, v * table[:, :128] + direction * (swapped * table[:, 128:]), v)


def front_kernel(n, cap, wq_ref, wk_ref, wv_ref, wo_part_ref, wr_raw_ref, gain_ref, x_ref, table_ref, routes_ref, cot_ref, packs_ref, h_ref, weights_ref, wo_ref, wr_ref, cxs_ref, gains_ref, wall, packed_ref, wr_part_ref, cx, table, normed_ref, total, out, exch_send, exch_recv, full_send, full_recv, x_send, x_recv, y_send, y_recv, xs_send, xs_recv, ys_send, ys_recv, cx_send, cx_recv, local_sems):
    tokens, width = x_ref.shape
    shard = width // 4
    ctx, fsdp = lax.axis_index("ctx"), lax.axis_index("fsdp")
    parity = lax.rem(ctx, 2)
    core, group = neighbours()
    far, near = group[0], group[1]
    sibling, distant = flip(fsdp, 1), flip(fsdp, 2)
    other = flip(distant, 1)
    for k in range(2):
        pltpu.make_async_copy(table_ref.at[k, ctx], table.at[k], local_sems.at[6 + k]).start()

    pair = HEAD_DIMENSION * 2
    for c in range(0, n, 2):
        keys, values = wk_ref[:, c // 2 * pair : (c // 2 + 1) * pair].astype(F32), wv_ref[:, c // 2 * pair : (c // 2 + 1) * pair].astype(F32)
        low = lane_iota(keys.shape) < HEAD_DIMENSION
        packed_ref[0, :shard, c * 128 : (c + 1) * 128] = jnp.where(low, keys, pltpu.roll(values, 64, 1)).astype(BF16)
        packed_ref[0, :shard, (c + 1) * 128 : (c + 2) * 128] = jnp.where(low, pltpu.roll(keys, 64, 1), values).astype(BF16)
    below = packed_ref.shape[1] - shard
    packed_ref[0, shard:, :] = jnp.zeros((below, width), BF16)
    row = row_iota((16, shard))
    gains = gain_ref[...].astype(F32)
    gain_rows = jnp.where(row == 0, gains[0:1], jnp.where(row == 1, gains[1:2], 0.0))
    packed_ref[0, shard : shard + 16, :shard] = gain_rows.astype(BF16)
    packed_ref[1, :shard, :] = wq_ref[...]
    packed_ref[1, shard:, :] = jnp.zeros((below, width), BF16)
    router = jnp.concatenate([wr_raw_ref[...].astype(F32), jnp.zeros((128 - EXPERTS, shard), F32)], 0)
    wr_part_ref[...] = jnp.transpose(router).astype(BF16)
    greet([core, far] + [{"ctx": c} for c in others(n)])

    half_rows = packed_ref.shape[1] // 2

    def cut(k, part):
        if k < 2:
            return pl.ds(pl.multiple_of(part * half_rows, 16), half_rows)
        if k == 2:
            return pl.ds(part, 1)
        return pl.ds(pl.multiple_of(part * (shard // 2), 16), shard // 2)

    sources = [packed_ref.at[0], packed_ref.at[1], wo_part_ref, wr_part_ref]
    targets = [wall.at[0], wall.at[1], wo_ref, wr_ref]

    def whole(k):
        return send(sources[k], targets[k].at[fsdp], full_send.at[k], full_recv.at[k], core)

    def own(k):
        return pltpu.make_async_copy(sources[k], targets[k].at[fsdp], local_sems.at[k])

    def to_far(k):
        return send(sources[k].at[cut(k, parity)], targets[k].at[fsdp, cut(k, parity)], x_send.at[k], x_recv.at[k], far)

    def pass_on(k, part, sems, device):
        ref = targets[k].at[distant, cut(k, part)]
        return send(ref, ref, sems[0].at[k], sems[1].at[k], device)

    def sibling_arrived(k):
        ref = targets[k].at[sibling]
        send(ref, ref, full_send.at[k], full_recv.at[k], core).wait_recv()

    def far_arrived(k):
        ref = targets[k].at[distant, cut(k, parity)]
        send(ref, ref, x_send.at[k], x_recv.at[k], far).wait_recv()
        pass_on(k, parity, (y_send, y_recv), near).start()
        pass_on(k, parity, (xs_send, xs_recv), core).start()

    def near_arrived(k):
        pass_on(k, 1 - parity, (y_send, y_recv), near).wait_recv()
        pass_on(k, 1 - parity, (ys_send, ys_recv), core).start()

    def core_arrived(k):
        for part, sems in ((parity, (xs_send, xs_recv)), (1 - parity, (ys_send, ys_recv))):
            ref = targets[k].at[other, cut(k, part)]
            send(ref, ref, sems[0].at[k], sems[1].at[k], core).wait_recv()

    for k in range(2):
        to_far(k).start()
    for k in range(2):
        whole(k).start()
        own(k).start()

    prep_kernel(cap, routes_ref, cot_ref, cx)
    pltpu.make_async_copy(cx, cxs_ref.at[0], local_sems.at[4]).start()
    normed, _ = norm_parts(x_ref[...])
    normed_ref[...] = normed

    def project(k, block, begin):
        at = pl.ds(pl.multiple_of(block * shard, shard), shard)
        if k == 0:
            gain = wall[0, block, shard : shard + 16, :shard].astype(F32)
            gains_ref[:, at] = gain
            h_ref[:, at] = (normed_ref[:, at] * gain[:1]).astype(BF16)
        part = dot(h_ref[:, at], wall[k, block, :shard, :])
        total[k] = part if begin else total[k] + part

    for k in range(2):
        own(k).wait()
        project(k, fsdp, True)
        sibling_arrived(k)
        project(k, sibling, False)
        if k == 0:
            far_arrived(0)

    exchanges = []

    def emit(k):
        lanes = slice(128, 256) if k == 0 else slice(0, 128)
        for c in range(n):
            out[c, :, lanes] = turn_half(total[k, :, c * 128 : (c + 1) * 128], angles, 1.0, 64 if k == 0 else 128).astype(BF16)
        cut_lanes = pl.ds(128 if k == 0 else 0, 128)
        source, target = out.at[:, :, cut_lanes], packs_ref.at[:, :, cut_lanes]
        exchanges.append((source, target, exch_send.at[k], exch_recv.at[k], local_sems.at[8 + k], n))
        exchange_start(*exchanges[-1])

    near_arrived(0)
    project(0, distant, False)
    core_arrived(0)
    project(0, other, False)
    for k in range(2):
        pltpu.make_async_copy(table_ref.at[k, ctx], table.at[k], local_sems.at[6 + k]).wait()
    angles = table[...].reshape(tokens, 256)
    emit(0)
    far_arrived(1)
    for k in (2, 3):
        own(k).start()
        whole(k).start()
        to_far(k).start()
    send(cx, cxs_ref.at[1], cx_send.at[0], cx_recv.at[0], far).start()
    near_arrived(1)
    project(1, distant, False)
    core_arrived(1)
    project(1, other, False)
    emit(1)
    keep = pltpu.make_async_copy(wall, weights_ref, local_sems.at[5])
    keep.start()
    for k in (2, 3):
        far_arrived(k)
    for k in (2, 3):
        near_arrived(k)
    for k in (2, 3):
        core_arrived(k)
        sibling_arrived(k)
        own(k).wait()
    for exchange in exchanges:
        exchange_wait(*exchange)
    for k in range(4):
        whole(k).wait_send()
        to_far(k).wait_send()
        pass_on(k, parity, (y_send, y_recv), near).wait_send()
        pass_on(k, parity, (xs_send, xs_recv), core).wait_send()
        pass_on(k, 1 - parity, (ys_send, ys_recv), core).wait_send()
    send(cx, cxs_ref.at[1], cx_send.at[0], cx_recv.at[0], far).wait()
    pltpu.make_async_copy(cx, cxs_ref.at[0], local_sems.at[4]).wait()
    keep.wait()


def front(wq, wk, wv, wo_part, wr, gains, x, table, routes, cot, cap, n):
    tokens, width = x.shape
    shard = wq.shape[0]
    hbm, vmem = pl.BlockSpec(memory_space=pl.ANY), pl.BlockSpec(memory_space=pltpu.VMEM)
    dma = lambda *k: pltpu.SemaphoreType.DMA(k)
    shaped = lambda shape, dtype=BF16: jax.ShapeDtypeStruct(shape, dtype)
    cx_shape = (tokens + EXPERTS, width)
    padded = 2 * 16 * (shard // 32 + 1)
    return pl.pallas_call(
        functools.partial(front_kernel, n, cap),
        in_specs=[vmem, vmem, vmem, hbm, vmem, vmem, vmem, hbm, vmem, vmem],
        out_specs=[hbm, vmem, hbm, hbm, hbm, hbm, vmem],
        out_shape=[
            shaped((n, tokens, PACK)),
            shaped((tokens, width)),
            shaped((2, 4, padded, width)),
            shaped((4,) + wo_part.shape),
            shaped((4, shard, 128)),
            shaped((2,) + cx_shape),
            shaped((16, width), F32),
        ],
        scratch_shapes=[
            pltpu.VMEM((2, 4, padded, width), BF16),
            pltpu.VMEM((2, padded, width), BF16),
            pltpu.VMEM((shard, 128), BF16),
            pltpu.VMEM(cx_shape, BF16),
            pltpu.VMEM((2, tokens // 2, 256), F32),
            pltpu.VMEM((tokens, width), F32),
            pltpu.VMEM((2, tokens, width), F32),
            pltpu.VMEM((n, tokens, PACK), BF16),
            dma(2, n - 1),
            dma(2, n - 1),
        ]
        + [dma(4)] * 10
        + [dma(1), dma(1), dma(10)],
        compiler_params=params(collective_id=1, has_side_effects=True),
        cost_estimate=cost(2e9, 5e7),
        name="front",
    )(wq, wk, wv, wo_part, wr, gains, x, table, routes, cot)


def attend_kernel(length, n, ends_ref, q_ref, pack_ref, cxs_ref, out_ref, lse_ref, full_ref, rest_ref, keys, values_t, acc, near_send, near_recv, far_send, far_recv, core_send, core_recv):
    block = pl.program_id(0)
    core, group = neighbours()
    far, near = group[0], group[1]
    split = cxs_ref.shape[1] // 2

    def to_near(i):
        at = pl.ds(0, cxs_ref.shape[1] if i == 0 else split)
        return send(cxs_ref.at[i, at], rest_ref.at[i, at], near_send.at[i], near_recv.at[i], near)

    def to_far():
        at = pl.ds(split, split)
        return send(rest_ref.at[0, at], rest_ref.at[1, at], far_send.at[0], far_recv.at[0], far)

    def to_core(i):
        src = cxs_ref.at[i] if i < 2 else rest_ref.at[i - 2]
        return send(src, rest_ref.at[2 + i], core_send.at[i], core_recv.at[i], core)

    @pl.when(block == 0)
    def _():
        greet([core, far, near])
        for i in range(2):
            to_near(i).start()
        for i in range(2):
            to_core(i).start()

    attn_forward_kernel(length, ends_ref, q_ref, pack_ref, out_ref, lse_ref, full_ref, keys, values_t, acc)

    @pl.when(block == pl.num_programs(0) - 4)
    def _():
        to_near(0).wait_recv()
        to_far().start()
        to_core(2).start()

    @pl.when(block == pl.num_programs(0) - 1)
    def _():
        to_near(1).wait_recv()
        to_far().wait_recv()
        to_core(3).start()
        for i in range(4):
            to_core(i).wait()
        for i in range(2):
            to_near(i).wait_send()
        to_far().wait_send()


def attend(ends, packs, cxs, length):
    n, _, rows, _ = packs.shape
    blocks, per = length // BLK, BLK // rows
    per_half = blocks // 2
    tiles = lambda i: (lax.rem(i, per_half), i // per_half, 0, 0)
    hbm = pl.BlockSpec(memory_space=pl.ANY)
    dma = lambda k: pltpu.SemaphoreType.DMA((k,))
    return pl.pallas_call(
        functools.partial(attend_kernel, length, n),
        grid=(blocks,),
        in_specs=[
            pl.BlockSpec(memory_space=pltpu.SMEM),
            pl.BlockSpec((per, 1, rows, PACK), tiles),
            pl.BlockSpec(packs.shape, lambda i: (0, 0, 0, 0)),
            hbm,
        ],
        out_specs=[
            pl.BlockSpec((per, 1, rows, 128), tiles),
            pl.BlockSpec((1, 1, 2 * BLK), lambda i: (i, 0, 0)),
            pl.BlockSpec((1, 128, 2 * BLK), lambda i: (i, 0, 0)),
            hbm,
        ],
        scratch_shapes=[
            pltpu.VMEM((length, 128), BF16),
            pltpu.VMEM((128, length), BF16),
            pltpu.VMEM((128, 2 * BLK), F32),
            dma(2),
            dma(2),
            dma(1),
            dma(1),
            dma(4),
            dma(4),
        ],
        out_shape=[
            jax.ShapeDtypeStruct((n, 2, rows, 128), BF16),
            jax.ShapeDtypeStruct((blocks, 1, 2 * BLK), F32),
            jax.ShapeDtypeStruct((blocks, 128, 2 * BLK), F32),
            jax.ShapeDtypeStruct((6,) + cxs.shape[1:], BF16),
        ],
        compiler_params=params(collective_id=3, has_side_effects=True),
        cost_estimate=cost(1.5e10, 2e7),
        name="attend",
    )(ends, packs, packs, cxs)


def mid_kernel(n, number, capp, attn_ref, cxs_ref, rest_ref, wo_ref, wr_ref, x_ref, gain_ref, middle_ref, h_ref, kept_ref, xs_ref, gs_ref, gates_ref, arrived, hs, total, exch_send, exch_recv, hop_send, hop_recv, cross_send, cross_recv, fwd_send, fwd_recv, local_sems):
    tokens, width = x_ref.shape
    ctx, fsdp = lax.axis_index("ctx"), lax.axis_index("fsdp")
    first = (fsdp * 2 + lax.rem(ctx, 2)) * number
    core, group = neighbours()
    greet([core, group[0]] + [{"ctx": c} for c in others(n)])
    exchange = (attn_ref, arrived, exch_send, exch_recv, local_sems.at[0], n)
    exchange_start(*exchange)
    total[...] = jnp.zeros_like(total)

    def take(c):
        total[...] += dot(arrived[c], wo_ref[c])

    exchange_wait(*exchange, take)
    keep = pltpu.make_async_copy(arrived, kept_ref, local_sems.at[1])
    keep.start()
    middle = x_ref[...] + RESIDUAL * total[...]
    middle_ref[...] = middle
    normed, _ = norm_parts(middle)
    h = (normed * gain_ref[1:2]).astype(BF16)
    h_ref[...] = h
    hs[0] = h

    split = tokens // 2

    def hop(i):
        return send(hs.at[0], hs.at[(1, 2, 4)[i]], hop_send.at[i], hop_recv.at[i], (group[0], group[1], core)[i])

    def cross(i):
        at = pl.ds(i * split, split)
        return send(hs.at[1 + i, at], hs.at[3, at], cross_send.at[i], cross_recv.at[i], group[1 - i])

    def forward(i):
        return send(hs.at[1 + i], hs.at[5 + i], fwd_send.at[i], fwd_recv.at[i], core)

    for i in range(3):
        hop(i).start()

    def place(b):
        h = hs[b]
        cx = (cxs_ref.at[b] if b < 2 else rest_ref.at[cx_slot[b]])
        logits = jnp.transpose(dot(h, wr_ref[...]))[:EXPERTS, :]
        raw = jnp.exp(logits - jnp.max(logits, 0, keepdims=True))
        router = raw / jnp.sum(raw, 0, keepdims=True)
        slots = cx[tokens:, :tokens].astype(F32)
        hots = one_hot(slots, first, number, capp)
        places = jnp.concatenate(hots, 0).astype(BF16)
        rows = dot(places, h).astype(BF16)
        grads = dot(places, cx[:tokens, :]).astype(BF16)
        for j in range(number):
            at = slice(j * capp, (j + 1) * capp)
            xs_ref[j, b] = rows[at]
            gs_ref[j, b] = grads[at]
            gate = jnp.sum(hots[j] * own_row(router, first + j), 1, keepdims=True)
            gates_ref[j, b] = jnp.broadcast_to(gate, (capp, 128))

    cx_slot = {2: 0, 3: 1, 4: 2, 5: 3, 6: 4, 7: 5}
    place(0)
    hop(2).wait_recv()
    place(4)
    for i in range(2):
        hop(i).wait_recv()
        cross(i).start()
        forward(i).start()
    place(1)
    place(2)
    for i in range(2):
        cross(i).wait_recv()
    forward(2).start()
    place(3)
    for i in range(3):
        forward(i).wait_recv()
        place(5 + i)
    for i in range(2):
        cross(i).wait_send()
    for i in range(3):
        hop(i).wait_send()
        forward(i).wait_send()
    keep.wait()


def mid_step(attn, cxs, rest, wo, wr, x, gain, number, capp, n):
    tokens, width = x.shape
    hbm, vmem = pl.BlockSpec(memory_space=pl.ANY), pl.BlockSpec(memory_space=pltpu.VMEM)
    dma = lambda k: pltpu.SemaphoreType.DMA((k,))
    shaped = lambda shape, dtype=BF16: jax.ShapeDtypeStruct(shape, dtype)
    return pl.pallas_call(
        functools.partial(mid_kernel, n, number, capp),
        in_specs=[hbm, vmem, vmem, vmem, vmem, vmem, vmem],
        out_specs=[vmem, vmem, hbm, vmem, vmem, vmem],
        out_shape=[
            shaped((tokens, width), F32),
            shaped((tokens, width)),
            shaped(attn.shape),
            shaped((number, 8, capp, width)),
            shaped((number, 8, capp, width)),
            shaped((number, 8, capp, 128), F32),
        ],
        scratch_shapes=[
            pltpu.VMEM(attn.shape, BF16),
            pltpu.VMEM((8, tokens, width), BF16),
            pltpu.VMEM((tokens, width), F32),
            dma(n - 1),
            dma(n - 1),
            dma(3),
            dma(3),
            dma(2),
            dma(2),
            dma(3),
            dma(3),
            dma(2),
        ],
        compiler_params=params(collective_id=2, has_side_effects=True),
        cost_estimate=cost(4e9, 5e7),
        name="mid_step",
    )(attn, cxs, rest, wo, wr, x, gain)


RING = 12
LAG_MIDDLE, LAG_ACROSS, LAG_END = 1, 2, 4
ORDER_X, ORDER_Y, ORDER_CORE = 1, 2, 4


class GroupSum:
    def __init__(self, part, rows, lands, own, sems, load, free, first, core, group):
        self.part, self.rows, self.own, self.load, self.free, self.first = part, rows, own, load, free, first
        self.land, self.land_x, self.land_y = lands
        self.core_send, self.core_recv, self.x_send, self.x_recv, self.y_send, self.y_recv = sems
        self.core, self.far, self.near = core, group[0], group[1]

    def place(self, i):
        return self.land.at[i, pl.ds(0, self.rows)]

    def ready(self, which):
        if not self.first:
            pl.semaphore_wait(self.free.at[which], 1)

    def to_core(self, i):
        return send(self.part.at[4 + i], self.place(i), self.core_send.at[i], self.core_recv.at[i], self.core)

    def to_far(self, k):
        return send(self.place(1 + 2 * k), self.land_x.at[k, pl.ds(0, self.rows)], self.x_send.at[k], self.x_recv.at[k], self.far)

    def to_near(self):
        return send(self.place(2), self.land_y.at[pl.ds(0, self.rows)], self.y_send.at[0], self.y_recv.at[0], self.near)

    def fetch(self, i):
        return pltpu.make_async_copy(self.part.at[i], self.own.at[i % 2, pl.ds(0, self.rows)], self.load.at[i % 2])

    def start(self):
        self.ready(0)
        for i in (1, 3, 2, 0):
            self.to_core(i).start()

    def over_cores(self):
        order = (1, 3, 2, 0)
        if self.own is not None:
            self.fetch(1).start()
        for step, i in enumerate(order):
            if self.own is None:
                mine = self.part[i]
            else:
                self.fetch(i).wait()
                mine = self.own[i % 2, : self.rows]
            self.to_core(i).wait_recv()
            self.land[i, : self.rows] = (self.land[i, : self.rows].astype(F32) + mine.astype(F32)).astype(BF16)
            if self.own is not None and step < 3:
                self.fetch(order[step + 1]).start()
            if i % 2 == 1:
                if step == 0:
                    self.ready(1)
                self.to_far(i // 2).start()

    def over_x(self, between=None):
        for k in (1, 0):
            if k == 0 and between is not None:
                between()
            self.to_far(k).wait_recv()
            both = self.land[2 * k, : self.rows].astype(F32) + self.land_x[k, : self.rows].astype(F32)
            self.land[2 * k, : self.rows] = both.astype(BF16)
            if k == 1:
                self.ready(2)
                self.to_near().start()

    def finish(self):
        self.to_near().wait_recv()
        for i in range(4):
            self.to_core(i).wait_send()
        for k in range(2):
            self.to_far(k).wait_send()
        self.to_near().wait_send()
        return self.land[0, : self.rows].astype(F32) + self.land_y[: self.rows].astype(F32)

    def release(self):
        for which, device in enumerate((self.core, self.far, self.near)):
            pl.semaphore_signal(self.free.at[which], inc=1, device_id=device, device_id_type=MESH)


class LineSum:
    def __init__(self, count, own_ref, other_ref, inbox, across, mine, sems):
        self.count, self.own_ref, self.other_ref = count, own_ref, other_ref
        self.inbox, self.across, self.mine = inbox, across, mine
        self.line_send, self.line_recv, self.mid_send, self.mid_recv, self.side_send, self.side_recv, self.store, self.load = sems
        ctx = lax.axis_index("ctx")
        z = ctx // 2
        self.middle = (z == 1) | (z == 2)
        self.line = {"ctx": jnp.where(z % 2 == 0, ctx + 2, ctx - 2)}
        self.peer = {"ctx": jnp.where(z == 1, ctx + 2, ctx - 2)}
        self.side = {"ctx": flip(ctx, 1)}

    def send_line(self, src, i):
        s = lax.rem(i, RING)
        return send(src, self.inbox.at[s], self.line_send.at[s], self.line_recv.at[s], self.line)

    def send_mid(self, i):
        s = lax.rem(i, RING)
        return send(self.inbox.at[s], self.across.at[s], self.mid_send.at[s], self.mid_recv.at[s], self.peer)

    def send_side(self, src, i):
        return send(src, self.other_ref.at[i], self.side_send.at[lax.rem(i, RING)], self.side_recv.at[i], self.side)

    def keep(self, src, i):
        return pltpu.make_async_copy(src, self.own_ref.at[i], self.store.at[lax.rem(i, RING)])

    def fetch(self, src, i):
        s = lax.rem(i, 4)
        return pltpu.make_async_copy(src, self.mine.at[s], self.load.at[s])

    def drain_middle(self, i):
        src = self.across.at[lax.rem(i, RING)]
        self.send_line(src, i).wait_send()
        self.send_side(src, i).wait_send()
        self.keep(src, i).wait()

    def drain_end(self, i):
        src = self.inbox.at[lax.rem(i, RING)]
        self.send_side(src, i).wait_send()
        self.keep(src, i).wait()

    def tick(self, t, source):
        count = self.count
        fixed = isinstance(t, int)

        def when(condition):
            if fixed:
                return (lambda f: f()) if condition else (lambda f: None)
            return pl.when(condition)

        i32 = (lambda v: jnp.int32(v)) if fixed else (lambda v: v)

        @pl.when(self.middle)
        def _():
            @when((t >= LAG_MIDDLE) & (t < count + LAG_MIDDLE))
            def _():
                i = i32(t - LAG_MIDDLE)

                @when(t >= LAG_ACROSS + 4)
                def _():
                    self.drain_middle(i32(t - LAG_ACROSS - 4))

                s = lax.rem(i, RING)
                self.fetch(self.own_ref.at[i], i).wait()
                self.send_line(self.inbox.at[s], i).wait_recv()
                self.inbox[s] = self.inbox[s] + self.mine[lax.rem(i, 4)]
                self.send_mid(i).start()

            @when(t < count)
            def _():
                self.fetch(source(t), i32(t)).start()

            @when((t >= LAG_ACROSS) & (t < count + LAG_ACROSS))
            def _():
                i = i32(t - LAG_ACROSS)
                s = lax.rem(i, RING)
                self.send_mid(i).wait()
                self.across[s] = self.across[s] + self.inbox[s]
                self.send_line(self.across.at[s], i).start()
                self.send_side(self.across.at[s], i).start()
                self.keep(self.across.at[s], i).start()

        @pl.when(jnp.logical_not(self.middle))
        def _():
            @when(t < count)
            def _():
                @when(t >= LAG_END + 2)
                def _():
                    self.drain_end(i32(t - LAG_END - 2))

                @when(t >= 3)
                def _():
                    self.send_line(self.mine.at[0], i32(t - 3)).wait_send()

                self.send_line(source(t), i32(t)).start()

            @when(t >= LAG_END)
            def _():
                i = i32(t - LAG_END)
                s = lax.rem(i, RING)
                self.send_line(self.inbox.at[s], i).wait_recv()
                self.send_side(self.inbox.at[s], i).start()
                self.keep(self.inbox.at[s], i).start()

    def finish(self):
        count = self.count

        @pl.when(self.middle)
        def _():
            for i in range(count + LAG_MIDDLE - LAG_ACROSS - 4, count):
                self.drain_middle(jnp.int32(i))

        @pl.when(jnp.logical_not(self.middle))
        def _():
            for i in range(count - 3, count):
                self.send_line(self.mine.at[0], jnp.int32(i)).wait_send()
            for i in range(count - LAG_END - 2, count):
                self.drain_end(jnp.int32(i))

        def arrived(i, carry):
            self.send_side(self.mine.at[0], i).wait_recv()
            return carry

        lax.fori_loop(0, count, arrived, 0)


def backward_kernel(
    n,
    length,
    capp,
    ends_ref,
    xs_ref,
    gs_ref,
    gates_ref,
    wg_ref,
    wu_ref,
    wd_ref,
    cxs_ref,
    rest_ref,
    full_ref,
    weights_ref,
    packs_hbm,
    table_hbm,
    cot_hbm,
    wo_hbm,
    attn_hbm,
    x_hbm,
    h_attn_hbm,
    h_ref,
    middle_ref,
    wr_ref,
    gains_ref,
    lse_ref,
    own_ref,
    other_ref,
    pieces_ref,
    outs_ref,
    backs_ref,
    gx_ref,
    yp_ref,
    grad_x_ref,
    mixed_ref,
    inbox,
    across,
    mine,
    land,
    land_x,
    land_y,
    y_land,
    y_land_x,
    y_land_y,
    own_buf,
    late_pieces,
    ga_in,
    grads_in,
    line_send,
    line_recv,
    mid_send,
    mid_recv,
    side_send,
    side_recv,
    line_store,
    line_load,
    ga_send,
    ga_recv,
    gr_send,
    gr_recv,
    group_sems,
    group_load,
    free,
    local_sems,
    full_sems,
    w_sems,
    load_sems,
    store_sems,
    comb_sems,
    part_sems,
):
    tokens, width = h_ref.shape
    half = length // 2
    rows = tokens // 2
    shard = width // 4
    blocks = length // BLK
    number = xs_ref.shape[0]
    ff = wg_ref.shape[2]
    ctx, fsdp = lax.axis_index("ctx"), lax.axis_index("fsdp")
    side = lax.rem(ctx, 2)
    first = (fsdp * 2 + side) * number
    core, group = neighbours()
    sub = own_ref.shape[1]
    cuts = PIECE // sub
    early = number * 6 * cuts
    line = LineSum(early + 2 * cuts, own_ref, other_ref, inbox, across, mine, (line_send, line_recv, mid_send, mid_recv, side_send, side_recv, line_store, line_load))

    def source(t):
        return pieces_ref.at[t // cuts, pl.ds(pl.multiple_of(lax.rem(t, cuts) * sub, sub), sub)]

    def tick(t):
        line.tick(jnp.int32(t) if isinstance(t, int) else t, source)

    sems = lambda k: [group_sems.at[k, j] for j in range(6)]
    lands = (land, land_x, land_y)
    ext = tokens + EXPERTS
    gx = GroupSum(gx_ref, 2 * ext, lands, None, sems(0), None, free, True, core, group)
    ys = GroupSum(yp_ref, 2 * tokens, (y_land, y_land_x, y_land_y), own_buf, sems(1), group_load, free, True, core, group)

    def strip(r):
        f = fsdp
        if r & ORDER_X:
            f = flip(f, 2)
        if r & ORDER_CORE:
            f = flip(f, 1)
        return 2 * f + (1 - side if r & ORDER_Y else side)

    def experts(wg, wu, wd, xb, gb, gateb, stage, out_acc, back_acc, outb, backb, go, dgate, comb_o, comb_b, gst, yst, slots):
        def loads(e):
            s = lax.rem(e, 2)
            at = side * number + e
            pairs = ((wg_ref.at[at], wg), (wu_ref.at[at], wu), (wd_ref.at[at], wd), (xs_ref.at[e], xb), (gs_ref.at[e], gb), (gates_ref.at[e], gateb))
            return [pltpu.make_async_copy(src, dst.at[s], load_sems.at[s, k]) for k, (src, dst) in enumerate(pairs)]

        def slot_copy(b):
            src = cxs_ref.at[b] if b < 2 else rest_ref.at[b - 2]
            return pltpu.make_async_copy(src.at[pl.ds(tokens, EXPERTS), pl.ds(0, tokens)], slots.at[b], part_sems.at[0, b])

        def stores(e):
            pairs = (
                (stage.at[pl.ds(0, 3)], pieces_ref.at[pl.ds(6 * e, 3)]),
                (stage.at[pl.ds(3, 3)], pieces_ref.at[pl.ds(6 * e + 3, 3)]),
                (outb, outs_ref.at[e]),
                (backb, backs_ref.at[e]),
            )
            return [pltpu.make_async_copy(src, dst, store_sems.at[k]) for k, (src, dst) in enumerate(pairs)]

        for copy in loads(jnp.int32(0)):
            copy.start()
        for b in range(8):
            slot_copy(b).start()
        greet([core, group[0]] + [{"ctx": c} for c in others(n)])

        def one(e, carry):
            s = lax.rem(e, 2)

            @pl.when(e + 1 < number)
            def _():
                for copy in loads(e + 1):
                    copy.start()

            for copy in loads(e):
                copy.wait()

            @pl.when(e > 0)
            def _():
                for copy in stores(e - 1)[2:]:
                    copy.wait()

            x = xb[s]
            gate = gateb[s][:, :1]
            go[...] = (gate * (RESIDUAL * gb[s].astype(F32))).astype(BF16)
            part = ff // 2
            for chunk in range(2):
                at = slice(chunk * part, (chunk + 1) * part)
                wgc, wuc, wdc = wg[s, :, at], wu[s, :, at], wd[s, at, :]
                pre_gate = dot(x, wgc)
                pre_up = dot(x, wuc)
                sig = jax.nn.sigmoid(pre_gate)
                hidden = (pre_gate * sig * pre_up).astype(BF16)
                out_part = dot(hidden, wdc)
                grad_hidden = dot(go[...], wdc, NT)
                grad_gate = (grad_hidden * pre_up * sig * (1.0 + pre_gate * (1.0 - sig))).astype(BF16)
                grad_up = (grad_hidden * pre_gate * sig).astype(BF16)
                row_part = dot(grad_gate, wgc, NT) + dot(grad_up, wuc, NT)
                dwg = dot(x, grad_gate, TN).astype(BF16)
                dwu = dot(x, grad_up, TN).astype(BF16)
                dwd = dot(hidden, go[...], TN).astype(BF16)
                for k in range(2):
                    cut = slice(k * PIECE, (k + 1) * PIECE)
                    stage[3 * chunk + k, :, :part] = dwg[cut]
                    stage[3 * chunk + k, :, part:] = dwu[cut]
                    stage[3 * chunk + 2, k * part : (k + 1) * part, :] = dwd[:, cut]
                stores(e)[chunk].start()
                if chunk == 0:
                    out_acc[...] = out_part
                    back_acc[...] = row_part
                    stores(e)[0].wait()
                    tick(2 * e)
                else:
                    out = (out_acc[...] + out_part).astype(BF16).astype(F32)
                    outb[...] = (gate * out).astype(BF16)
                    backb[...] = (back_acc[...] + row_part).astype(BF16)
                    grad = jnp.sum(RESIDUAL * gb[s].astype(F32) * out, 1, keepdims=True)
                    dgate[e] = jnp.broadcast_to(grad, dgate.shape[1:])
            for copy in stores(e)[2:]:
                copy.start()
            stores(e)[1].wait()
            tick(2 * e + 1)
            return carry

        lax.fori_loop(0, number, one, 0)
        for copy in stores(jnp.int32(number - 1))[2:]:
            copy.wait()
        for b in range(8):
            slot_copy(b).wait()

        def which(s):
            k = lax.rem(s, 4)
            i = jnp.where(k == 0, 1, jnp.where(k == 1, 3, jnp.where(k == 2, 2, 0)))
            return jnp.where(s < 4, 4 + i, i), i

        def comb(s):
            k = lax.rem(s, 2)
            at = pl.ds(pl.multiple_of(which(s)[0] * capp, 16), capp)
            return [
                pltpu.make_async_copy(outs_ref.at[:, at], comb_o.at[k], comb_sems.at[0, k]),
                pltpu.make_async_copy(backs_ref.at[:, at], comb_b.at[k], comb_sems.at[1, k]),
            ]

        def put(s):
            k = lax.rem(s, 2)
            r, _ = which(s)
            return [
                pltpu.make_async_copy(gst.at[k], gx_ref.at[r], part_sems.at[1, k]),
                pltpu.make_async_copy(yst.at[k], yp_ref.at[r], part_sems.at[1, 2 + k]),
            ]

        for copy in comb(jnp.int32(0)):
            copy.start()

        def join(s, carry):
            k = lax.rem(s, 2)
            r, i = which(s)

            @pl.when(s + 1 < 8)
            def _():
                for copy in comb(s + 1):
                    copy.start()

            for copy in comb(s):
                copy.wait()

            @pl.when(s >= 2)
            def _():
                put(s - 2)[1].wait()

            hots = one_hot(slots[r].astype(F32), first, number, capp)
            places = jnp.concatenate(hots, 0).astype(BF16)
            y = dot(places, comb_o[k].reshape(number * capp, width), TN).astype(BF16)
            back = dot(places, comb_b[k].reshape(number * capp, width), TN).astype(BF16)
            extra = jnp.zeros((EXPERTS, 2 * tokens), F32)
            for j in range(number):
                grads = dgate[j, pl.ds(pl.multiple_of(r * capp, 16), capp), :][:, :1]
                grad = jnp.sum(hots[j] * grads, 0, keepdims=True)
                high = grad.astype(BF16).astype(F32)
                extra = jnp.where(row_iota(extra.shape) == first + j, jnp.concatenate([high, grad - high], 1), extra)
            for q in range(2):
                yst[k, q * tokens : (q + 1) * tokens, :] = y[:, q * PIECE : (q + 1) * PIECE]
                gst[k, q * ext : q * ext + tokens, :] = back[:, q * PIECE : (q + 1) * PIECE]
            gst[k, tokens:ext, :] = extra.astype(BF16)
            gst[k, ext + tokens :, :] = jnp.zeros((EXPERTS, PIECE), BF16)
            put(s)[1].start()

            @pl.when(s < 4)
            def _():
                put(s)[0].start()
                put(s)[0].wait()
                gx.to_core(i).start()

            @pl.when(s >= 4)
            def _():
                gx.to_core(i).wait_recv()
                land[i, : gx.rows] = (land[i, : gx.rows].astype(F32) + gst[k].astype(F32)).astype(BF16)

            @pl.when((s == 4) | (s == 5))
            def _():
                gx.to_far(s - 4).start()

            @pl.when(lax.rem(s, 2) == 1)
            def _():
                tick(2 * number + s // 2)

            return carry

        lax.fori_loop(0, 8, join, 0)
        for s in range(6, 8):
            put(jnp.int32(s))[1].wait()

    slots_rows = xs_ref.shape[1]
    pl.run_scoped(
        experts,
        pltpu.VMEM((2, width, ff), BF16),
        pltpu.VMEM((2, width, ff), BF16),
        pltpu.VMEM((2, ff, width), BF16),
        pltpu.VMEM((2, slots_rows, width), BF16),
        pltpu.VMEM((2, slots_rows, width), BF16),
        pltpu.VMEM((2, slots_rows, 128), F32),
        pltpu.VMEM((6, PIECE, PIECE), BF16),
        pltpu.VMEM((slots_rows, width), F32),
        pltpu.VMEM((slots_rows, width), F32),
        pltpu.VMEM((slots_rows, width), BF16),
        pltpu.VMEM((slots_rows, width), BF16),
        pltpu.VMEM((slots_rows, width), BF16),
        pltpu.VMEM((number, slots_rows, 128), F32),
        pltpu.VMEM((2, number, capp, width), BF16),
        pltpu.VMEM((2, number, capp, width), BF16),
        pltpu.VMEM((2, 2 * ext, PIECE), BF16),
        pltpu.VMEM((2, 2 * tokens, PIECE), BF16),
        pltpu.VMEM((8, EXPERTS, tokens), BF16),
    )
    at_tick = [2 * number + 4]

    def go_on(k=1):
        for _ in range(k):
            tick(at_tick[0])
            at_tick[0] += 1

    def backward(packs, table, keys, values, keys_t, grad_q, grad_k, grad_v, acc, full_buf, ga, pack_out, wbuf, total, grad_middle, dgain, col, small, columns, cot, wo, attn, x_in, h_attn):
        ws = GroupSum(small, PIECE, lands, None, sems(2), None, free, False, core, group)
        cs = GroupSum(columns, PIECE + 16, lands, None, sems(3), None, free, False, core, group)
        copies = [
            pltpu.make_async_copy(src, dst, local_sems.at[4 + k])
            for k, (src, dst) in enumerate(
                ((cot_hbm, cot), (wo_hbm, wo), (attn_hbm, attn), (packs_hbm, packs), (table_hbm, table), (x_hbm, x_in), (h_attn_hbm, h_attn))
            )
        ]
        for copy in copies:
            copy.start()
        small[:, PIECE // 2 : PIECE, :] = jnp.zeros((8, PIECE // 2, PIECE), BF16)
        columns[:, PIECE:, :] = jnp.zeros((8, 16, PIECE), BF16)
        go_on(2)
        gx.over_x(go_on)
        go_on(2)
        arrived = gx.finish()
        arrived = jnp.concatenate([arrived[:ext], arrived[ext:]], 1)
        gx.release()

        h = h_ref[...]
        gain = gains_ref[1:2]
        extra = arrived[tokens:, :]
        grad_router = extra[:, :tokens] + extra[:, tokens : 2 * tokens]
        grad_router = jnp.transpose(jnp.concatenate([grad_router, jnp.zeros((128 - EXPERTS, tokens), F32)], 0))
        logits = dot(h, wr_ref[...])
        logits = jnp.where(lane_iota(logits.shape) < EXPERTS, logits, MASKED)
        raw = jnp.exp(logits - jnp.max(logits, -1, keepdims=True))
        router = raw / jnp.sum(raw, -1, keepdims=True)
        grad_logits = (router * (grad_router - jnp.sum(router * grad_router, -1, keepdims=True))).astype(BF16)
        go_on()
        grad_h = arrived[:tokens, :] + dot(grad_logits, wr_ref[...], NT)
        normed, scale = norm_parts(middle_ref[...])
        dgain[1:2, :] = jnp.sum(grad_h * normed, 0, keepdims=True)
        for copy in copies[:3]:
            copy.wait()
        grad_mid = cot[...] + norm_back(grad_h * gain, normed, scale)
        grad_middle[...] = grad_mid
        grad_branch = (RESIDUAL * grad_mid).astype(BF16)
        for c in range(n):
            ga[c] = dot(grad_branch, wo[c], NT).astype(BF16)
        ga_exchange = (ga, ga_in, ga_send, ga_recv, local_sems.at[2], n)
        exchange_start(*ga_exchange)
        go_on()
        col[:, :128] = dot(h, grad_logits, TN).astype(BF16)
        for r in range(8):
            at = strip(r)
            dwo = dot(attn[at], grad_branch, TN).astype(BF16)
            small[r, 0:128, :] = dwo[:, :PIECE]
            small[r, 128:256, :] = dwo[:, PIECE:]
            small[r, 256:384, 0:128] = col[pl.ds(pl.multiple_of(at * 128, 128), 128), 0:128]
        ws.start()
        ys.start()
        go_on()
        copies[3].wait()
        for hh in range(2):
            for c in range(n):
                kk, vv = pair_keys(packs[c, hh, :, 128:256].astype(F32))
                at = hh * half + c * rows
                keys[at : at + rows, :] = kk.astype(BF16)
                values[at : at + rows, :] = vv.astype(BF16)
                keys_t[:, at : at + rows] = jnp.transpose(kk).astype(BF16)
        grad_k[...] = jnp.zeros_like(grad_k)
        grad_v[...] = jnp.zeros_like(grad_v)
        go_on()
        ws.over_cores()
        ys.over_cores()
        go_on()
        exchange_wait(*ga_exchange)

        per = BLK // rows
        per_half = blocks // 2

        def fetch_full(b):
            return pltpu.make_async_copy(full_ref.at[b], full_buf.at[lax.rem(b, 2)], full_sems.at[lax.rem(b, 2)])

        fetch_full(jnp.int32(0)).start()
        attend_tick = at_tick[0]

        def attend(block, carry):
            late = block // per_half
            c0 = lax.rem(block, per_half) * per
            q2 = stack_heads(jnp.concatenate([packs[c0 + k, late, :, :128] for k in range(per)], 0))
            g2 = stack_heads(jnp.concatenate([ga_in[c0 + k, pl.ds(pl.multiple_of(late * rows, rows), rows), :] for k in range(per)], 0))
            position, start = query_rows(ends_ref, block, length)
            lse = lse_ref[block]

            @pl.when(block + 1 < blocks)
            def _():
                fetch_full(block + 1).start()

            fetch_full(block).wait()
            delta = jnp.sum(jnp.transpose(g2.astype(F32)) * full_buf[lax.rem(block, 2)], 0, keepdims=True)
            acc[...] = jnp.zeros_like(acc)

            def body(kb, carry):
                at = pl.multiple_of(kb * BLK, BLK)
                scores = dot(keys[pl.ds(at, BLK), :], q2, NT) * ATTN_SCALE
                where = key_position(kb, length)
                probs = jnp.where((where <= position) & (where >= start), jnp.exp(scores - lse), 0.0)
                grad_probs = dot(values[pl.ds(at, BLK), :], g2, NT)
                grad_scores = (probs * (grad_probs - delta)).astype(BF16)
                acc[...] += dot(keys_t[:, pl.ds(at, BLK)], grad_scores)
                grad_k[pl.ds(at, BLK), :] += dot(grad_scores, q2)
                grad_v[pl.ds(at, BLK), :] += dot(probs.astype(BF16), g2)

                @pl.when((kb == block) & ((block == per_half) | (block == per_half + 1)))
                def _():
                    tick(attend_tick + 2 + 2 * (block - per_half))

                return carry

            block_loop(block, per_half, body, 0)
            grad_q[pl.ds(pl.multiple_of(block * BLK, BLK), BLK), :] = fold_heads(jnp.transpose(acc[...]))

            @pl.when((block == 1) | (block >= 3))
            def _():
                past = block - per_half
                late_tick = jnp.where(past < 2, 3 + 2 * past, 4 + past)
                tick(attend_tick + jnp.where(block < per_half, block // 2, late_tick))

            return carry

        lax.fori_loop(0, blocks, attend, 0)
        at_tick[0] += blocks
        copies[4].wait()
        for c in range(n):
            for hh in range(2):
                at = slice(hh * half + c * rows, hh * half + (c + 1) * rows)
                kk = grad_k[at, :]
                vv = grad_v[at, :]
                kk = (kk + pltpu.roll(kk, 64, 1)) * ATTN_SCALE
                vv = vv + pltpu.roll(vv, 64, 1)
                both = jnp.where(lane_iota(kk.shape) < 64, kk, vv)
                package = jnp.concatenate([grad_q[at, :] * ATTN_SCALE, both], -1)
                pack_out[c, hh * rows : (hh + 1) * rows, :] = turn(package, table[at, :], -1.0).astype(BF16)
        gr_exchange = (pack_out, grads_in, gr_send, gr_recv, local_sems.at[3], n)
        exchange_start(*gr_exchange)

        def fetch_w(c):
            slot = lax.rem(c, 2)
            at = pl.ds(pl.multiple_of(c * 128, 128), 128)
            return [
                pltpu.make_async_copy(weights_ref.at[1 - k, :, :, at], wbuf.at[slot, :, :, pl.ds(128 * k, 128)], w_sems.at[slot, k])
                for k in range(2)
            ]

        for copy in fetch_w(jnp.int32(0)):
            copy.start()
        go_on()
        ws.over_x()
        ys.over_x()
        go_on(2)
        total[...] = jnp.zeros_like(total)
        late_pieces[:PIECE] = ws.finish().astype(BF16)
        ws.release()
        ffn = ys.finish()
        mixed_ref[...] = middle_ref[...] + RESIDUAL * jnp.concatenate([ffn[:tokens], ffn[tokens:]], 1)
        go_on(3)
        exchange_wait(*gr_exchange)
        copies[5].wait()
        copies[6].wait()

        columns_tick = at_tick[0]

        def finish_columns(c, carry):
            @pl.when(c + 1 < n)
            def _():
                for copy in fetch_w(c + 1):
                    copy.start()

            for copy in fetch_w(c):
                copy.wait()
            slot = lax.rem(c, 2)
            g = grads_in[c]
            col[...] = dot(h_attn[...], g, TN).astype(BF16)
            for r in range(8):
                at = pl.ds(pl.multiple_of(strip(r) * 128, 128), 128)
                columns[r, pl.ds(pl.multiple_of(c // 2 * 128, 128), 128), pl.ds(pl.multiple_of(lax.rem(c, 2) * PACK, PACK), PACK)] = col[at, :]
            for f in range(4):
                total[:, f * shard : (f + 1) * shard] += dot(g, wbuf[slot, f, :shard, :], NT)

            @pl.when(lax.rem(c, 4) == 3)
            def _():
                tick(columns_tick + c // 4)

            return carry

        lax.fori_loop(0, n, finish_columns, 0)
        at_tick[0] += n // 4
        normed, scale = norm_parts(x_in[...])
        grad_h = total[...]
        dgain[0:1, :] = jnp.sum(grad_h * normed, 0, keepdims=True)
        grad_x_ref[...] = grad_middle[...] + norm_back(grad_h * gains_ref[0:1], normed, scale)
        for r in range(8):
            at = pl.ds(pl.multiple_of(strip(r) * 128, 128), 128)
            row = row_iota((16, 128))
            both = jnp.where(row == 0, dgain[0:1, at], jnp.where(row == 1, dgain[1:2, at], 0.0))
            columns[r, PIECE:, 0:128] = both.astype(BF16)
        cs.start()
        go_on()
        cs.over_cores()
        go_on(3)
        cs.over_x(go_on)
        go_on(3)
        summed = cs.finish().astype(BF16)
        late_pieces[PIECE:] = summed[:PIECE]
        late_pieces[384:400] = summed[PIECE:]

    f32, bf = (lambda *shape: pltpu.VMEM(shape, F32)), (lambda *shape: pltpu.VMEM(shape, BF16))
    pl.run_scoped(
        backward,
        bf(*packs_hbm.shape),
        f32(*table_hbm.shape),
        bf(length, 128),
        bf(length, 128),
        bf(128, length),
        f32(length, 128),
        f32(length, 128),
        f32(length, 128),
        f32(128, 2 * BLK),
        f32(2, 128, 2 * BLK),
        bf(n, tokens, 128),
        bf(n, tokens, PACK),
        bf(2, 4, weights_ref.shape[2], PACK),
        f32(tokens, width),
        f32(tokens, width),
        f32(8, width),
        bf(width, PACK),
        bf(8, PIECE, PIECE),
        bf(8, PIECE + 16, PIECE),
        f32(tokens, width),
        bf(*wo_hbm.shape),
        bf(*attn_hbm.shape),
        f32(tokens, width),
        bf(tokens, width),
    )

    def rest(t, carry):
        tick(t)
        return carry

    lax.fori_loop(at_tick[0], early, rest, 0)

    def late_source(t):
        return late_pieces.at[pl.ds(pl.multiple_of((t - early) * sub, sub), sub)]

    def late(t, carry):
        line.tick(t, late_source)
        return carry

    lax.fori_loop(early, line.count + LAG_END, late, 0)
    line.finish()


def backward_step(ends, xs, gs, gates, w_gate, w_up, w_down, cxs, rest, full, weights, packs, table, cot, wo, attn, x, h_attn, h, middle, wr, gains, lse, n, length, capp):
    tokens, width = x.shape
    number, slots_rows, _ = xs.shape
    hbm, vmem = pl.BlockSpec(memory_space=pl.ANY), pl.BlockSpec(memory_space=pltpu.VMEM)
    smem = pl.BlockSpec(memory_space=pltpu.SMEM)
    dma = lambda *k: pltpu.SemaphoreType.DMA(k)
    shaped = lambda shape, dtype=BF16: jax.ShapeDtypeStruct(shape, dtype)
    sub = PIECE // 2
    piece = (sub, PIECE)
    count = (number * 6 + 2) * 2
    land_rows = max(2 * (tokens + EXPERTS), PIECE + 16)
    return pl.pallas_call(
        functools.partial(backward_kernel, n, length, capp),
        in_specs=[smem] + [hbm] * 17 + [vmem] * 5,
        out_specs=[hbm] * 7 + [vmem, vmem],
        out_shape=[
            shaped((count,) + piece),
            shaped((count,) + piece),
            shaped((number * 6, PIECE, PIECE)),
            shaped(xs.shape),
            shaped(xs.shape),
            shaped((8, 2 * (tokens + EXPERTS), PIECE)),
            shaped((8, 2 * tokens, PIECE)),
            shaped((tokens, width), F32),
            shaped((tokens, width), F32),
        ],
        scratch_shapes=[
            pltpu.VMEM((RING,) + piece, BF16),
            pltpu.VMEM((RING,) + piece, BF16),
            pltpu.VMEM((4,) + piece, BF16),
            pltpu.VMEM((4, land_rows, PIECE), BF16),
            pltpu.VMEM((2, land_rows, PIECE), BF16),
            pltpu.VMEM((land_rows, PIECE), BF16),
            pltpu.VMEM((4, 2 * tokens, PIECE), BF16),
            pltpu.VMEM((2, 2 * tokens, PIECE), BF16),
            pltpu.VMEM((2 * tokens, PIECE), BF16),
            pltpu.VMEM((2, 2 * tokens, PIECE), BF16),
            pltpu.VMEM((2 * PIECE, PIECE), BF16),
            pltpu.VMEM((n, tokens, 128), BF16),
            pltpu.VMEM((n, tokens, PACK), BF16),
            dma(RING),
            dma(RING),
            dma(RING),
            dma(RING),
            dma(RING),
            dma(count),
            dma(RING),
            dma(4),
            dma(n - 1),
            dma(n - 1),
            dma(n - 1),
            dma(n - 1),
            dma(4, 6, 4),
            dma(2),
            pltpu.SemaphoreType.REGULAR((3,)),
            dma(11),
            dma(2),
            dma(2, 2),
            dma(2, 6),
            dma(4),
            dma(2, 2),
            dma(2, 8),
        ],
        compiler_params=params(63, collective_id=0, has_side_effects=True),
        cost_estimate=cost(6e10, 1e9),
        name="backward_step",
    )(ends, xs, gs, gates, w_gate, w_up, w_down, cxs, rest, full, weights, packs, table, cot, wo, attn, x, h_attn, h, middle, wr, gains, lse)


def local(
    inputs,
    cotangent,
    doc_lengths,
    routes,
    attn_gain,
    ffn_gain,
    w_query,
    key_weight,
    value_weight,
    w_out,
    w_router,
    w_gate,
    w_up,
    w_down,
):
    rows = inputs.shape[2]
    width = inputs.shape[3]
    n = lax.axis_size("ctx")
    fsdp = lax.axis_size("fsdp")
    me, mine = lax.axis_index("ctx"), lax.axis_index("fsdp")
    tokens = 2 * rows
    length = tokens * n
    experts_here = w_gate.shape[0]
    number = experts_here // 2
    capacity = 5 * tokens * TOP // (4 * EXPERTS)
    capp = -(-capacity // 16) * 16
    shard = width // fsdp
    heads = QUERY_HEADS // n
    head_lanes = heads * HEAD_DIMENSION
    copies = n // KEY_VALUE_HEADS
    bits = group_bits(fsdp)

    x = inputs.reshape(tokens, width)
    cot = cotangent.reshape(tokens, width)
    side = me % 2
    base = (side * number).astype(jnp.int32).reshape(1)
    first = (mine * experts_here + side * number).astype(jnp.int32).reshape(1)
    index = jnp.stack([side * number, (1 - side) * number]).astype(jnp.int32)
    ends = doc_lengths
    table = jnp.asarray(rotary_table(length))

    out_part = w_out.reshape(shard // head_lanes, head_lanes, width)
    if head_lanes < 128:
        out_part = jnp.pad(out_part, ((0, 0), (0, 128 - head_lanes), (0, 0)))
    merge = lambda a: a.reshape(number, -1, a.shape[-1])

    if n == 8 and fsdp == 4:
        packs, h_attn, weights, wo, wr, cxs, gains = front(
            w_query,
            key_weight,
            value_weight,
            out_part,
            jnp.transpose(w_router),
            jnp.stack([attn_gain, ffn_gain]),
            x,
            table.reshape(2, n, rows, 256),
            jnp.transpose(routes[0], (0, 2, 1)),
            cot,
            capacity,
            n,
        )
        wo, wr = wo.reshape(n, 128, width), wr.reshape(width, 128)
        packs = packs.reshape(n, 2, rows, PACK)
        attn, lse, full, cx_rest = attend(ends, packs, cxs, length)
        middle, h_ffn, attn, xs, gs, gates = mid_step(attn.reshape(n, tokens, 128), cxs, cx_rest, wo, wr, x, gains, number, capp, n)
        own, other, _, _, _, _, _, grad_x, mixed = backward_step(
            ends,
            merge(xs),
            merge(gs),
            merge(gates),
            w_gate,
            w_up,
            w_down,
            cxs,
            cx_rest,
            full,
            weights,
            packs,
            table,
            cot,
            wo,
            attn,
            x,
            h_attn,
            h_ffn,
            middle,
            wr,
            gains,
            lse,
            n,
            length,
            capp,
        )
        own, other = own.reshape(-1, PIECE, PIECE), other.reshape(-1, PIECE, PIECE)
        shapes = [w.shape for w in (w_gate, w_up, w_down)]
        outs = tail(index, own, other, mixed, grad_x, shapes, shard)
        return (
            outs[3].reshape(inputs.shape),
            outs[4].reshape(inputs.shape),
            outs[10].reshape(shard),
            outs[11].reshape(shard),
            outs[5],
            outs[6],
            outs[7],
            outs[8],
            jnp.transpose(outs[9]),
            outs[0],
            outs[1],
            outs[2],
        )

    else:
        own_table = lax.dynamic_slice_in_dim(table.reshape(2, n, rows, 256), me, 1, 1).reshape(tokens, 256)
        query_part = w_query.reshape(shard, n, head_lanes)
        if head_lanes < 128:
            query_part = jnp.pad(query_part, ((0, 0), (0, 0), (0, 128 - head_lanes)))
        key_part = jnp.repeat(key_weight.reshape(shard, KEY_VALUE_HEADS, HEAD_DIMENSION), copies, 1)
        value_part = jnp.repeat(value_weight.reshape(shard, KEY_VALUE_HEADS, HEAD_DIMENSION), copies, 1)
        packed = jnp.concatenate([query_part, key_part, value_part], -1).reshape(shard, n * PACK)
        padding = 2 * 16 * (shard // 32 + 1) - shard
        gains = jnp.pad(jnp.stack([attn_gain, ffn_gain]), ((0, padding - 2), (0, n * PACK - shard)))
        packed = jnp.concatenate([packed, gains], 0)
        router_part = jnp.pad(w_router, ((0, 0), (0, 128 - EXPERTS)))
        weights = lax.all_gather(packed, "fsdp", axis=0)
        gain_one = weights[:, shard, :shard].reshape(1, width).astype(F32)
        gain_two = weights[:, shard + 1, :shard].reshape(1, width).astype(F32)
        wo = lax.all_gather(out_part, "fsdp", axis=0, tiled=True)
        wr = lax.all_gather(router_part, "fsdp", axis=0, tiled=True)
        cxs = group_gather(prep(jnp.transpose(routes[0], (0, 2, 1)), cot, capacity), bits)
        packs, h_attn = qkv(x, gain_one, weights, own_table, shard, n)
        packs = lax.all_to_all(packs, "ctx", split_axis=0, concat_axis=0, tiled=True).reshape(n, 2, rows, PACK)
        attn, lse, full = attn_forward(ends, packs, length)
        attn = lax.all_to_all(attn.reshape(n, tokens, 128), "ctx", split_axis=0, concat_axis=0, tiled=True)
        middle, h_ffn = middle_step(attn, wo, x, gain_two)
        xs, gs, gates = gather_rows(first, group_gather(h_ffn, bits), cxs, jnp.transpose(wr), number, capp)
        slots = cxs[:, tokens:]
    xs, gs, gates = merge(xs), merge(gs), merge(gates)
    pieces, outs, back, dgates = expert_step(base, xs, gs, gates, w_gate, w_up, w_down)
    y_part, gx_part = combine(first, slots, outs, back, dgates, tokens, capp)
    pieces = pieces.reshape(number * 6, PIECE, PIECE)
    gx = group_reduce(gx_part, bits)
    grad_middle, dwo, grad_attn, dwr, dgain_two = home_step(gx, h_ffn, middle, cot, wr, wo, gain_two, attn)
    grad_attn = lax.all_to_all(grad_attn, "ctx", split_axis=0, concat_axis=0, tiled=True).reshape(n, 2, rows, 128)
    grads = attn_backward(ends, packs, grad_attn, lse, full, table, length)
    grads = lax.all_to_all(grads.reshape(n, tokens, PACK), "ctx", split_axis=0, concat_axis=0, tiled=True)
    dw, grad_x, dgain_one = final_step(grads, weights, h_attn, x, gain_one, grad_middle, shard)
    mixed = middle + RESIDUAL * group_reduce(y_part, bits).astype(F32)
    own = line_sum(pieces, n)
    other = swap(own, "ctx", 1)
    scatter = lambda a: lax.psum(lax.psum_scatter(a, "fsdp", scatter_dimension=0, tiled=True), "ctx").astype(F32)
    dwo = scatter(dwo)[:, :head_lanes, :].reshape(shard, width)
    small = jnp.concatenate([dwr[:, :EXPERTS], dgain_two.reshape(width, 1).astype(BF16)], 1)
    small = scatter(jnp.pad(small, ((0, 0), (0, 127 - EXPERTS))))
    dwr, dgain_two = small[:, :EXPERTS], small[:, EXPERTS]
    dw = scatter(dw).reshape(shard, n, PACK)
    dgain_one = scatter(dgain_one.reshape(width).astype(BF16))

    outs = widen(index, own, other, [w.shape for w in (w_gate, w_up, w_down)])
    fold = lambda a: a.reshape(shard, KEY_VALUE_HEADS, copies, HEAD_DIMENSION).sum(2).reshape(shard, -1)
    return (
        mixed.reshape(inputs.shape),
        grad_x.reshape(inputs.shape),
        dgain_one,
        dgain_two,
        dw[:, :, :head_lanes].reshape(shard, -1),
        fold(dw[:, :, 128:192]),
        fold(dw[:, :, 192:256]),
        dwo,
        dwr,
        outs[0],
        outs[1],
        outs[2],
    )


def solution(mesh):
    tokens = P("fsdp", None, "ctx", None)
    one, two, three = P("fsdp"), P("fsdp", None), P("fsdp", None, None)
    return jax.shard_map(
        local,
        mesh=mesh,
        in_specs=(tokens, tokens, two, tokens, one, one, two, two, two, two, two, three, three, three),
        out_specs=(tokens, tokens, one, one, two, two, two, two, two, three, three, three),
        check_vma=False,
    )
```

```python
import functools

import jax
import jax.numpy as jnp
import numpy as np
from jax import lax
from jax.experimental import pallas as pl
from jax.experimental.pallas import tpu as pltpu
from jax.sharding import PartitionSpec as P

QUERY_HEADS = 16
KEY_VALUE_HEADS = 8
HEAD_DIMENSION = 64
EXPERTS = 32
TOP = 8

ATTN_SCALE = 0.015625
RESIDUAL = 0.22
NORM_EPS = 1e-06
ROPE_BASE = 10000.0
MASKED = -1e30

F32 = jnp.float32
BF16 = jnp.bfloat16
MIB = 1 << 20
NT = (((1,), (1,)), ((), ()))
TN = (((0,), (0,)), ((), ()))
BLK = 256
PACK = 256


def dot(a, b, dims=None):
    if dims is None:
        return jnp.dot(a, b, preferred_element_type=F32)
    return lax.dot_general(a, b, dims, preferred_element_type=F32)


def params(limit=56, **kw):
    return pltpu.CompilerParams(vmem_limit_bytes=limit * MIB, **kw)


def cost(flops, bytes_accessed):
    return pl.CostEstimate(flops=int(flops), bytes_accessed=int(bytes_accessed), transcendentals=0)


def lane_iota(shape):
    return lax.broadcasted_iota(jnp.int32, shape, len(shape) - 1)


def row_iota(shape):
    return lax.broadcasted_iota(jnp.int32, shape, len(shape) - 2)


def rotary_table(length):
    half = length // 2
    order = np.arange(half, dtype=np.float32)
    positions = np.concatenate([order, length - 1 - order]).astype(np.float32)
    m = np.arange(HEAD_DIMENSION // 2, dtype=np.float64)
    frequency = (ROPE_BASE ** (-2.0 * m / HEAD_DIMENSION)).astype(np.float32)
    angles = (positions[:, None] * frequency[None, :]).astype(np.float64)
    cosine, sine = np.cos(angles), np.sin(angles)
    cos_head = np.concatenate([cosine, cosine], -1)
    sin_head = np.concatenate([-sine, sine], -1)
    return np.concatenate([cos_head, cos_head, sin_head, sin_head], -1).astype(np.float32)


def turn(v, table, direction):
    lanes = lane_iota(v.shape)
    cosine = jnp.concatenate([table[:, :128], table[:, :128]], -1)
    sine = jnp.concatenate([table[:, 128:], table[:, 128:]], -1)
    turned = lanes < 3 * HEAD_DIMENSION
    swapped = jnp.where(lanes % HEAD_DIMENSION < HEAD_DIMENSION // 2, pltpu.roll(v, PACK - 32, 1), pltpu.roll(v, 32, 1))
    return jnp.where(turned, v * cosine + direction * (swapped * sine), v)


def norm_parts(values):
    inv_rms = lax.rsqrt(jnp.mean(values * values, -1, keepdims=True) + NORM_EPS)
    return values * inv_rms, inv_rms


def norm_back(grad_normed, normed, inv_rms):
    return inv_rms * (grad_normed - normed * jnp.mean(grad_normed * normed, -1, keepdims=True))


def prep_kernel(cap, routes_ref, cot_ref, out_ref):
    tokens, width = cot_ref.shape
    earlier = (row_iota((tokens, tokens)) < lane_iota((tokens, tokens))).astype(BF16)
    experts = row_iota((EXPERTS, tokens))
    base = jnp.zeros((EXPERTS, 1), F32)
    plus = jnp.zeros((EXPERTS, tokens), F32)
    for k in range(TOP):
        row = jnp.concatenate([routes_ref[0, k : k + 1, :], routes_ref[1, k : k + 1, :]], 1)
        chosen = experts == row
        ones = chosen.astype(F32)
        slot = dot(ones.astype(BF16), earlier) + base
        plus = plus + jnp.where(chosen & (slot < cap), slot + 1.0, 0.0)
        base = base + jnp.sum(ones, 1, keepdims=True)
    out_ref[:tokens, :] = cot_ref[...].astype(BF16)
    out_ref[tokens:, :] = jnp.concatenate([plus - 1.0, jnp.zeros((EXPERTS, width - tokens), F32)], -1).astype(BF16)


def prep(routes, cot, cap):
    tokens, width = cot.shape
    return pl.pallas_call(
        functools.partial(prep_kernel, cap),
        out_shape=jax.ShapeDtypeStruct((tokens + EXPERTS, width), BF16),
        compiler_params=params(),
        cost_estimate=cost(1e9, 2e6),
        name="prep",
    )(routes, cot)


def qkv_kernel(shard, x_ref, gain_ref, w_ref, table_ref, out_ref, h_ref):
    @pl.when(pl.program_id(0) == 0)
    def _():
        normed, _ = norm_parts(x_ref[...])
        h_ref[...] = (normed * gain_ref[...]).astype(BF16)

    total = None
    for f in range(w_ref.shape[0]):
        part = dot(h_ref[:, f * shard : (f + 1) * shard], w_ref[f, :shard, :])
        total = part if total is None else total + part
    for d in range(out_ref.shape[0]):
        out_ref[d] = turn(total[:, d * PACK : (d + 1) * PACK], table_ref[...], 1.0).astype(BF16)


def qkv(x, gain, weights, table, shard, n):
    tokens, width = x.shape
    fsdp, padded, _ = weights.shape
    return pl.pallas_call(
        functools.partial(qkv_kernel, shard),
        grid=(n // 2,),
        in_specs=[
            pl.BlockSpec((tokens, width), lambda i: (0, 0)),
            pl.BlockSpec((1, width), lambda i: (0, 0)),
            pl.BlockSpec((fsdp, padded, 2 * PACK), lambda i: (0, 0, i)),
            pl.BlockSpec((tokens, 256), lambda i: (0, 0)),
        ],
        out_specs=[
            pl.BlockSpec((2, tokens, PACK), lambda i: (i, 0, 0)),
            pl.BlockSpec((tokens, width), lambda i: (0, 0)),
        ],
        out_shape=[
            jax.ShapeDtypeStruct((n, tokens, PACK), BF16),
            jax.ShapeDtypeStruct((tokens, width), BF16),
        ],
        compiler_params=params(),
        cost_estimate=cost(2 * tokens * width * n * PACK, 8e6),
        name="qkv",
    )(x, gain, weights, table)


def pair_keys(kv):
    other = pltpu.roll(kv, 64, 1)
    low = lane_iota(kv.shape) < 64
    return jnp.where(low, kv, other), jnp.where(low, other, kv)


def stack_heads(q):
    low = lane_iota(q.shape) < 64
    zero = jnp.zeros_like(q)
    return jnp.concatenate([jnp.where(low, q, zero), jnp.where(low, zero, q)], 0)


def fold_heads(stacked):
    rows = stacked.shape[0] // 2
    return jnp.where(lane_iota((rows, 128)) < 64, stacked[:rows], stacked[rows:])


def query_rows(ends_ref, block, length):
    half = length // 2
    lanes = lane_iota((1, 2 * BLK))
    index = block * BLK + jnp.where(lanes < BLK, lanes, lanes - BLK)
    position = jnp.where(index < half, index, length + half - 1 - index)
    start = jnp.zeros_like(position)
    end = 0
    for j in range(3):
        end = end + ends_ref[0, j]
        start = jnp.where(position >= end, jnp.maximum(start, end), start)
    return position, start


def key_position(kb, length):
    half = length // 2
    index = kb * BLK + row_iota((BLK, 1))
    return jnp.where(index < half, index, length + half - 1 - index)


def block_loop(block, per_half, body, init):
    late = block >= per_half
    inner = jnp.where(late, block - per_half, block)
    count = jnp.where(late, 2 * per_half - inner, inner + 1)

    def step(j, carry):
        kb = jnp.where(late & (j >= per_half), inner + j, j)
        return body(kb, carry)

    return lax.fori_loop(0, count, step, init)


def load_package(pack_ref, c, h):
    return pack_ref[c, h].astype(F32)


def attn_forward_kernel(length, ends_ref, q_ref, pack_ref, out_ref, lse_ref, full_ref, keys, values_t, acc):
    block = pl.program_id(0)
    half = length // 2
    n, _, rows, _ = pack_ref.shape

    @pl.when(block == 0)
    def _():
        for h in range(2):
            for c in range(n):
                kk, vv = pair_keys(pack_ref[c, h, :, 128:256].astype(F32))
                at = h * half + c * rows
                keys[at : at + rows, :] = kk.astype(BF16)
                if rows % 128 == 0:
                    values_t[:, at : at + rows] = jnp.transpose(vv).astype(BF16)
        if rows % 128 != 0:
            for h in range(2):
                for c in range(0, n, 2):
                    pair = jnp.concatenate([pack_ref[c, h, :, 128:256], pack_ref[c + 1, h, :, 128:256]], 0)
                    _, vv = pair_keys(pair.astype(F32))
                    at = h * half + c * rows
                    values_t[:, at : at + 2 * rows] = jnp.transpose(vv).astype(BF16)

    q = q_ref[...].reshape(BLK, PACK)[:, :128]
    q2 = stack_heads(q)
    position, start = query_rows(ends_ref, block, length)
    acc[...] = jnp.zeros_like(acc)

    def body(kb, carry):
        peak, total = carry
        at = pl.multiple_of(kb * BLK, BLK)
        scores = dot(keys[pl.ds(at, BLK), :], q2, NT) * ATTN_SCALE
        where = key_position(kb, length)
        scores = jnp.where((where <= position) & (where >= start), scores, MASKED)
        new_peak = jnp.maximum(peak, jnp.max(scores, 0, keepdims=True))
        weights = jnp.exp(scores - new_peak)
        fade = jnp.exp(peak - new_peak)
        total = total * fade + jnp.sum(weights, 0, keepdims=True)
        acc[...] = acc[...] * fade + dot(values_t[:, pl.ds(at, BLK)], weights.astype(BF16))
        return new_peak, total

    init = (jnp.full((1, 2 * BLK), MASKED, F32), jnp.zeros((1, 2 * BLK), F32))
    peak, total = block_loop(block, half // BLK, body, init)
    result = acc[...] / total
    full_ref[0] = result
    lse_ref[0] = peak + jnp.log(total)
    folded = fold_heads(jnp.transpose(result)).astype(BF16)
    out_ref[...] = folded.reshape(out_ref.shape)


def attn_forward(ends, packs, length):
    n, _, rows, _ = packs.shape
    blocks, per = length // BLK, BLK // rows
    per_half = blocks // 2
    tiles = lambda i, ends: (lax.rem(i, per_half), i // per_half, 0, 0)
    return pl.pallas_call(
        functools.partial(attn_forward_kernel, length),
        grid_spec=pltpu.PrefetchScalarGridSpec(
            num_scalar_prefetch=1,
            grid=(blocks,),
            in_specs=[
                pl.BlockSpec((per, 1, rows, PACK), tiles),
                pl.BlockSpec(packs.shape, lambda i, ends: (0, 0, 0, 0)),
            ],
            out_specs=[
                pl.BlockSpec((per, 1, rows, 128), tiles),
                pl.BlockSpec((1, 1, 2 * BLK), lambda i, ends: (i, 0, 0)),
                pl.BlockSpec((1, 128, 2 * BLK), lambda i, ends: (i, 0, 0)),
            ],
            scratch_shapes=[
                pltpu.VMEM((length, 128), BF16),
                pltpu.VMEM((128, length), BF16),
                pltpu.VMEM((128, 2 * BLK), F32),
            ],
        ),
        out_shape=[
            jax.ShapeDtypeStruct((n, 2, rows, 128), BF16),
            jax.ShapeDtypeStruct((blocks, 1, 2 * BLK), F32),
            jax.ShapeDtypeStruct((blocks, 128, 2 * BLK), F32),
        ],
        compiler_params=params(),
        cost_estimate=cost(1.5e10, 6e6),
        name="attn_forward",
    )(ends, packs, packs)


def attn_backward_kernel(length, ends_ref, q_ref, g_ref, pack_ref, lse_ref, full_ref, table_ref, out_ref, keys, values, keys_t, grad_q, grad_k, grad_v, acc):
    block = pl.program_id(0)
    half = length // 2
    n, _, rows, _ = pack_ref.shape

    @pl.when(block == 0)
    def _():
        for h in range(2):
            for c in range(n):
                kk, vv = pair_keys(pack_ref[c, h, :, 128:256].astype(F32))
                at = h * half + c * rows
                keys[at : at + rows, :] = kk.astype(BF16)
                values[at : at + rows, :] = vv.astype(BF16)
        for b in range(length // BLK):
            keys_t[:, b * BLK : (b + 1) * BLK] = jnp.transpose(keys[b * BLK : (b + 1) * BLK, :].astype(F32)).astype(BF16)
        grad_k[...] = jnp.zeros_like(grad_k)
        grad_v[...] = jnp.zeros_like(grad_v)

    q2 = stack_heads(q_ref[...].reshape(BLK, PACK)[:, :128])
    g2 = stack_heads(g_ref[...].reshape(BLK, 128))
    position, start = query_rows(ends_ref, block, length)
    lse = lse_ref[0]
    delta = jnp.sum(jnp.transpose(g2.astype(F32)) * full_ref[0], 0, keepdims=True)
    acc[...] = jnp.zeros_like(acc)

    def body(kb, carry):
        at = pl.multiple_of(kb * BLK, BLK)
        scores = dot(keys[pl.ds(at, BLK), :], q2, NT) * ATTN_SCALE
        where = key_position(kb, length)
        probs = jnp.where((where <= position) & (where >= start), jnp.exp(scores - lse), 0.0)
        grad_probs = dot(values[pl.ds(at, BLK), :], g2, NT)
        grad_scores = (probs * (grad_probs - delta)).astype(BF16)
        acc[...] += dot(keys_t[:, pl.ds(at, BLK)], grad_scores)
        grad_k[pl.ds(at, BLK), :] += dot(grad_scores, q2)
        grad_v[pl.ds(at, BLK), :] += dot(probs.astype(BF16), g2)
        return carry

    block_loop(block, half // BLK, body, 0)
    grad_q[pl.ds(pl.multiple_of(block * BLK, BLK), BLK), :] = fold_heads(jnp.transpose(acc[...]))

    @pl.when(block == length // BLK - 1)
    def _():
        for h in range(2):
            for c in range(n):
                at = slice(h * half + c * rows, h * half + (c + 1) * rows)
                kk = grad_k[at, :]
                vv = grad_v[at, :]
                kk = (kk + pltpu.roll(kk, 64, 1)) * ATTN_SCALE
                vv = vv + pltpu.roll(vv, 64, 1)
                both = jnp.where(lane_iota(kk.shape) < 64, kk, vv)
                package = jnp.concatenate([grad_q[at, :] * ATTN_SCALE, both], -1)
                out_ref[c, h] = turn(package, table_ref[at, :], -1.0).astype(BF16)


def attn_backward(ends, packs, grads, lse, full, table, length):
    n, _, rows, _ = packs.shape
    blocks, per = length // BLK, BLK // rows
    per_half = blocks // 2
    tiles = lambda i, ends: (lax.rem(i, per_half), i // per_half, 0, 0)
    return pl.pallas_call(
        functools.partial(attn_backward_kernel, length),
        grid_spec=pltpu.PrefetchScalarGridSpec(
            num_scalar_prefetch=1,
            grid=(blocks,),
            in_specs=[
                pl.BlockSpec((per, 1, rows, PACK), tiles),
                pl.BlockSpec((per, 1, rows, 128), tiles),
                pl.BlockSpec(packs.shape, lambda i, ends: (0, 0, 0, 0)),
                pl.BlockSpec((1, 1, 2 * BLK), lambda i, ends: (i, 0, 0)),
                pl.BlockSpec((1, 128, 2 * BLK), lambda i, ends: (i, 0, 0)),
                pl.BlockSpec(table.shape, lambda i, ends: (0, 0)),
            ],
            out_specs=pl.BlockSpec(packs.shape, lambda i, ends: (0, 0, 0, 0)),
            scratch_shapes=[
                pltpu.VMEM((length, 128), BF16),
                pltpu.VMEM((length, 128), BF16),
                pltpu.VMEM((128, length), BF16),
                pltpu.VMEM((length, 128), F32),
                pltpu.VMEM((length, 128), F32),
                pltpu.VMEM((length, 128), F32),
                pltpu.VMEM((128, 2 * BLK), F32),
            ],
        ),
        out_shape=jax.ShapeDtypeStruct(packs.shape, BF16),
        compiler_params=params(),
        cost_estimate=cost(3e10, 8e6),
        name="attn_backward",
    )(ends, packs, grads, packs, lse, full, table)


def middle_kernel(attn_ref, wo_ref, x_ref, gain_ref, middle_ref, h_ref):
    total = None
    for c in range(attn_ref.shape[0]):
        part = dot(attn_ref[c], wo_ref[c])
        total = part if total is None else total + part
    middle = x_ref[...] + RESIDUAL * total
    middle_ref[...] = middle
    normed, _ = norm_parts(middle)
    h_ref[...] = (normed * gain_ref[...]).astype(BF16)


def middle_step(attn, wo, x, gain):
    tokens, width = x.shape
    return pl.pallas_call(
        middle_kernel,
        out_shape=[jax.ShapeDtypeStruct((tokens, width), F32), jax.ShapeDtypeStruct((tokens, width), BF16)],
        compiler_params=params(),
        cost_estimate=cost(2 * tokens * width * width, 5e6),
        name="middle",
    )(attn, wo, x, gain)


def own_row(table, row):
    return jnp.sum(jnp.where(row_iota(table.shape) == row, table, 0.0), 0, keepdims=True)


def one_hot(slots, first, number, capp):
    tokens = slots.shape[1]
    order = row_iota((capp, tokens)).astype(F32)
    return [(order == own_row(slots, first + j)).astype(F32) for j in range(number)]


def gather_kernel(number, capp, first_ref, h_ref, cx_ref, wrt_ref, x_ref, g_ref, gate_ref):
    tokens = h_ref.shape[1]
    first = first_ref[0]
    h = h_ref[0]
    slots = cx_ref[0, tokens:, :tokens].astype(F32)
    logits = dot(wrt_ref[...], h, NT)[:EXPERTS, :]
    raw = jnp.exp(logits - jnp.max(logits, 0, keepdims=True))
    router = raw / jnp.sum(raw, 0, keepdims=True)
    hots = one_hot(slots, first, number, capp)
    places = jnp.concatenate(hots, 0).astype(BF16)
    rows = dot(places, h).astype(BF16)
    grads = dot(places, cx_ref[0, :tokens, :]).astype(BF16)
    for j in range(number):
        at = slice(j * capp, (j + 1) * capp)
        x_ref[j, 0] = rows[at]
        g_ref[j, 0] = grads[at]
        gate = jnp.sum(hots[j] * own_row(router, first + j), 1, keepdims=True)
        gate_ref[j, 0] = jnp.broadcast_to(gate, (capp, 128))


def gather_rows(first, hs, cxs, wrt, number, capp):
    nb, tokens, width = hs.shape
    return pl.pallas_call(
        functools.partial(gather_kernel, number, capp),
        grid_spec=pltpu.PrefetchScalarGridSpec(
            num_scalar_prefetch=1,
            grid=(nb,),
            in_specs=[
                pl.BlockSpec((1, tokens, width), lambda b, f: (b, 0, 0)),
                pl.BlockSpec((1, tokens + EXPERTS, width), lambda b, f: (b, 0, 0)),
                pl.BlockSpec(wrt.shape, lambda b, f: (0, 0)),
            ],
            out_specs=[
                pl.BlockSpec((number, 1, capp, width), lambda b, f: (0, b, 0, 0)),
                pl.BlockSpec((number, 1, capp, width), lambda b, f: (0, b, 0, 0)),
                pl.BlockSpec((number, 1, capp, 128), lambda b, f: (0, b, 0, 0)),
            ],
        ),
        out_shape=[
            jax.ShapeDtypeStruct((number, nb, capp, width), BF16),
            jax.ShapeDtypeStruct((number, nb, capp, width), BF16),
            jax.ShapeDtypeStruct((number, nb, capp, 128), F32),
        ],
        compiler_params=params(),
        cost_estimate=cost(4 * nb * number * capp * tokens * width, 2e7),
        name="gather_rows",
    )(first, hs, cxs, wrt)


PIECE = 512


def expert_kernel(base_ref, x_ref, g_ref, gate_ref, wg_ref, wu_ref, wd_ref, piece_ref, out_ref, rows_ref, dg_ref):
    x = x_ref[0]
    gate = gate_ref[0][:, :1]
    grad_ffn = RESIDUAL * g_ref[0].astype(F32)
    go = (gate * grad_ffn).astype(BF16)
    part = wg_ref.shape[2] // 2
    out = rows = None
    for chunk in range(2):
        at = slice(chunk * part, (chunk + 1) * part)
        wg, wu, wd = wg_ref[0, :, at], wu_ref[0, :, at], wd_ref[0, at, :]
        pre_gate = dot(x, wg)
        pre_up = dot(x, wu)
        sig = jax.nn.sigmoid(pre_gate)
        hidden = (pre_gate * sig * pre_up).astype(BF16)
        out_part = dot(hidden, wd)
        grad_hidden = dot(go, wd, NT)
        grad_gate = (grad_hidden * pre_up * sig * (1.0 + pre_gate * (1.0 - sig))).astype(BF16)
        grad_up = (grad_hidden * pre_gate * sig).astype(BF16)
        row_part = dot(grad_gate, wg, NT) + dot(grad_up, wu, NT)
        dwg = dot(x, grad_gate, TN).astype(BF16)
        dwu = dot(x, grad_up, TN).astype(BF16)
        dwd = dot(hidden, go, TN).astype(BF16)
        for half in range(2):
            side = slice(half * PIECE, (half + 1) * PIECE)
            piece_ref[0, 3 * chunk + half, :, :part] = dwg[side]
            piece_ref[0, 3 * chunk + half, :, part:] = dwu[side]
            piece_ref[0, 3 * chunk + 2, half * part : (half + 1) * part, :] = dwd[:, side]
        out = out_part if out is None else out + out_part
        rows = row_part if rows is None else rows + row_part
    out = out.astype(BF16).astype(F32)
    out_ref[0] = (gate * out).astype(BF16)
    rows_ref[0] = rows.astype(BF16)
    grad = jnp.sum(grad_ffn * out, 1, keepdims=True)
    dg_ref[0] = jnp.broadcast_to(grad, dg_ref.shape[1:])


def expert_step(base, xs, gs, gates, w_gate, w_up, w_down):
    number, rows, width = xs.shape
    ff = w_gate.shape[2]
    row = lambda e, b: (e, 0, 0)
    weight = lambda e, b: (b[0] + e, 0, 0)
    return pl.pallas_call(
        expert_kernel,
        grid_spec=pltpu.PrefetchScalarGridSpec(
            num_scalar_prefetch=1,
            grid=(number,),
            in_specs=[
                pl.BlockSpec((1, rows, width), row),
                pl.BlockSpec((1, rows, width), row),
                pl.BlockSpec((1, rows, 128), row),
                pl.BlockSpec((1, width, ff), weight),
                pl.BlockSpec((1, width, ff), weight),
                pl.BlockSpec((1, ff, width), weight),
            ],
            out_specs=[
                pl.BlockSpec((1, 6, PIECE, PIECE), lambda e, b: (e, 0, 0, 0)),
                pl.BlockSpec((1, rows, width), row),
                pl.BlockSpec((1, rows, width), row),
                pl.BlockSpec((1, rows, 128), row),
            ],
        ),
        out_shape=[
            jax.ShapeDtypeStruct((number, 6, PIECE, PIECE), BF16),
            jax.ShapeDtypeStruct((number, rows, width), BF16),
            jax.ShapeDtypeStruct((number, rows, width), BF16),
            jax.ShapeDtypeStruct((number, rows, 128), F32),
        ],
        compiler_params=params(60),
        cost_estimate=cost(18 * number * rows * width * ff, 5e7),
        name="expert_step",
    )(base, xs, gs, gates, w_gate, w_up, w_down)


def combine_kernel(number, capp, first_ref, slot_ref, outs, rows, grads, y_ref, gx_ref):
    tokens = y_ref.shape[1]
    width = y_ref.shape[2]
    first = first_ref[0]
    slots = slot_ref[0][:, :tokens].astype(F32)
    hots = one_hot(slots, first, number, capp)
    places = jnp.concatenate(hots, 0).astype(BF16)
    y_ref[0] = dot(places, outs[:, 0].reshape(number * capp, width), TN).astype(BF16)
    gx_ref[0, :tokens] = dot(places, rows[:, 0].reshape(number * capp, width), TN).astype(BF16)
    extra = jnp.zeros((EXPERTS, 2 * tokens), F32)
    for j in range(number):
        grad = jnp.sum(hots[j] * grads[j, 0][:, :1], 0, keepdims=True)
        high = grad.astype(BF16).astype(F32)
        both = jnp.concatenate([high, grad - high], 1)
        extra = jnp.where(row_iota(extra.shape) == first + j, both, extra)
    rest = jnp.zeros((EXPERTS, width - 2 * tokens), F32)
    gx_ref[0, tokens:] = jnp.concatenate([extra, rest], 1).astype(BF16)


def combine(first, slots, outs, rows, grads, tokens, capp):
    number = outs.shape[0]
    nb, _, width = slots.shape
    split = lambda a: a.reshape(number, nb, capp, a.shape[-1])
    wide = pl.BlockSpec((number, 1, capp, width), lambda b, f: (0, b, 0, 0))
    thin = pl.BlockSpec((number, 1, capp, 128), lambda b, f: (0, b, 0, 0))
    return pl.pallas_call(
        functools.partial(combine_kernel, number, capp),
        grid_spec=pltpu.PrefetchScalarGridSpec(
            num_scalar_prefetch=1,
            grid=(nb,),
            in_specs=[pl.BlockSpec((1, EXPERTS, width), lambda b, f: (b, 0, 0))] + [wide, wide, thin],
            out_specs=[
                pl.BlockSpec((1, tokens, width), lambda b, f: (b, 0, 0)),
                pl.BlockSpec((1, tokens + EXPERTS, width), lambda b, f: (b, 0, 0)),
            ],
        ),
        out_shape=[
            jax.ShapeDtypeStruct((nb, tokens, width), BF16),
            jax.ShapeDtypeStruct((nb, tokens + EXPERTS, width), BF16),
        ],
        compiler_params=params(),
        cost_estimate=cost(4 * nb * number * capp * tokens * width, 2e7),
        name="combine",
    )(first, slots, split(outs), split(rows), split(grads))


def home_kernel(gx_ref, h_ref, middle_ref, cot_ref, wr_ref, wo_ref, gain_ref, attn_ref, grad_middle_ref, dwo_ref, ga_ref, dwr_ref, dgain_ref):
    tokens, width = h_ref.shape
    h = h_ref[...]
    gain = gain_ref[...]
    extra = gx_ref[tokens:, :].astype(F32)
    grad_router = extra[:, :tokens] + extra[:, tokens : 2 * tokens]
    grad_router = jnp.transpose(jnp.concatenate([grad_router, jnp.zeros((128 - EXPERTS, tokens), F32)], 0))
    logits = dot(h, wr_ref[...])
    logits = jnp.where(lane_iota(logits.shape) < EXPERTS, logits, MASKED)
    raw = jnp.exp(logits - jnp.max(logits, -1, keepdims=True))
    router = raw / jnp.sum(raw, -1, keepdims=True)
    grad_logits = (router * (grad_router - jnp.sum(router * grad_router, -1, keepdims=True))).astype(BF16)
    dwr_ref[...] = dot(h, grad_logits, TN).astype(BF16)
    grad_h = gx_ref[:tokens, :].astype(F32) + dot(grad_logits, wr_ref[...], NT)
    normed, scale = norm_parts(middle_ref[...])
    dgain_ref[...] = jnp.sum(grad_h * normed, 0, keepdims=True)
    grad_middle = cot_ref[...] + norm_back(grad_h * gain, normed, scale)
    grad_middle_ref[...] = grad_middle
    grad_branch = (RESIDUAL * grad_middle).astype(BF16)
    for c in range(attn_ref.shape[0]):
        dwo_ref[c] = dot(attn_ref[c], grad_branch, TN).astype(BF16)
        ga_ref[c] = dot(grad_branch, wo_ref[c], NT).astype(BF16)


def home_step(gx, h, middle, cot, wr, wo, gain, attn):
    tokens, width = h.shape
    n = attn.shape[0]
    return pl.pallas_call(
        home_kernel,
        out_shape=[
            jax.ShapeDtypeStruct((tokens, width), F32),
            jax.ShapeDtypeStruct((n, 128, width), BF16),
            jax.ShapeDtypeStruct((n, tokens, 128), BF16),
            jax.ShapeDtypeStruct((width, 128), BF16),
            jax.ShapeDtypeStruct((1, width), F32),
        ],
        compiler_params=params(),
        cost_estimate=cost(4 * tokens * width * width, 1e7),
        name="home_step",
    )(gx, h, middle, cot, wr, wo, gain, attn)


def final_kernel(shard, grads_ref, w_ref, h_ref, x_ref, gain_ref, grad_middle_ref, dw_ref, grad_x_ref, dgain_ref, total):
    c = pl.program_id(0)
    g = grads_ref[0]
    dw_ref[...] = dot(h_ref[...], g, TN).astype(BF16)

    @pl.when(c == 0)
    def _():
        total[...] = jnp.zeros_like(total)

    for f in range(w_ref.shape[0]):
        total[:, f * shard : (f + 1) * shard] += dot(g, w_ref[f, :shard, :], NT)

    @pl.when(c == pl.num_programs(0) - 1)
    def _():
        normed, scale = norm_parts(x_ref[...])
        grad_h = total[...]
        dgain_ref[...] = jnp.sum(grad_h * normed, 0, keepdims=True)
        grad_x_ref[...] = grad_middle_ref[...] + norm_back(grad_h * gain_ref[...], normed, scale)


def final_step(grads, weights, h, x, gain, grad_middle, shard):
    n, tokens, _ = grads.shape
    width = x.shape[1]
    fsdp, padded, _ = weights.shape
    same = lambda c: (0, 0)
    return pl.pallas_call(
        functools.partial(final_kernel, shard),
        grid=(n,),
        in_specs=[
            pl.BlockSpec((1, tokens, PACK), lambda c: (c, 0, 0)),
            pl.BlockSpec((fsdp, padded, PACK), lambda c: (0, 0, c)),
            pl.BlockSpec((tokens, width), same),
            pl.BlockSpec((tokens, width), same),
            pl.BlockSpec((1, width), same),
            pl.BlockSpec((tokens, width), same),
        ],
        out_specs=[
            pl.BlockSpec((width, PACK), lambda c: (0, c)),
            pl.BlockSpec((tokens, width), same),
            pl.BlockSpec((1, width), same),
        ],
        out_shape=[
            jax.ShapeDtypeStruct((width, n * PACK), BF16),
            jax.ShapeDtypeStruct((tokens, width), F32),
            jax.ShapeDtypeStruct((1, width), F32),
        ],
        scratch_shapes=[pltpu.VMEM((tokens, width), F32)],
        compiler_params=params(),
        cost_estimate=cost(4 * tokens * width * n * PACK, 1.2e7),
        name="final_step",
    )(grads, weights, h, x, gain, grad_middle)


def widen_kernel(number, index_ref, own_ref, other_ref, gate_ref, up_ref, down_ref):
    part = gate_ref.shape[2] // 2

    def write(ref):
        for chunk in range(2):
            columns = slice(chunk * part, (chunk + 1) * part)
            for half in range(2):
                at = slice(half * PIECE, (half + 1) * PIECE)
                gate_ref[0, at, columns] = ref[3 * chunk + half, :, :part].astype(F32)
                up_ref[0, at, columns] = ref[3 * chunk + half, :, part:].astype(F32)
                down_ref[0, columns, at] = ref[3 * chunk + 2, half * part : (half + 1) * part, :].astype(F32)

    @pl.when(pl.program_id(0) == 0)
    def _():
        write(own_ref)

    @pl.when(pl.program_id(0) == 1)
    def _():
        write(other_ref)


def tail_kernel(number, index_ref, own_ref, other_ref, own_small_ref, other_small_ref, mixed_in, grad_in, gate_ref, up_ref, down_ref, mixed_ref, grad_ref, dwq_ref, dwk_ref, dwv_ref, dwo_ref, dwr_ref, g1_ref, g2_ref):
    widen_kernel(number, index_ref, own_ref, other_ref, gate_ref, up_ref, down_ref)
    mixed_ref[...] = mixed_in[...]
    grad_ref[...] = grad_in[...]

    @pl.when((pl.program_id(0) == 0) & (pl.program_id(1) == 0))
    def _():
        for which, ref in enumerate((own_small_ref, other_small_ref)):
            part = index_ref[which] // number
            at = pl.ds(pl.multiple_of(part * 128, 128), 128)
            for q in range(4):
                block = ref[1, q * 128 : (q + 1) * 128, :].astype(F32)
                dwq_ref[at, q * 256 : q * 256 + 128] = block[:, :128]
                dwq_ref[at, q * 256 + 128 : (q + 1) * 256] = block[:, 256:384]
                one, two = block[:, 128:256], block[:, 384:]
                low = lane_iota(one.shape) < HEAD_DIMENSION
                dwk_ref[at, q * 128 : (q + 1) * 128] = jnp.where(low, one, pltpu.roll(two, 64, 1))
                dwv_ref[at, q * 128 : (q + 1) * 128] = jnp.where(low, pltpu.roll(one, 64, 1), two)
            dwo_ref[at, :PIECE] = ref[0, 0:128, :].astype(F32)
            dwo_ref[at, PIECE:] = ref[0, 128:256, :].astype(F32)
            dwr_ref[:, at] = jnp.transpose(ref[0, 256:384, :128].astype(F32))[:EXPERTS]
            gains = ref[0, 384:400, :128].astype(F32)
            g1_ref[pl.ds(part, 1), :] = gains[0:1]
            g2_ref[pl.ds(part, 1), :] = gains[1:2]


def expert_specs(number, shapes):
    last = number - 1
    ins = [
        pl.BlockSpec((6, PIECE, PIECE), lambda s, e, at: (jnp.where(s == 0, e, last), 0, 0)),
        pl.BlockSpec((6, PIECE, PIECE), lambda s, e, at: (jnp.where(s == 0, 0, e), 0, 0)),
    ]
    outs = [pl.BlockSpec((1,) + tuple(shape[1:]), lambda s, e, at: (at[s] + e, 0, 0)) for shape in shapes]
    return ins, outs, [jax.ShapeDtypeStruct(shape, F32) for shape in shapes]


def widen(index, own, other, shapes):
    number = shapes[0][0] // 2
    ins, outs, out_shapes = expert_specs(number, shapes)
    return pl.pallas_call(
        functools.partial(widen_kernel, number),
        grid_spec=pltpu.PrefetchScalarGridSpec(num_scalar_prefetch=1, grid=(2, number), in_specs=ins, out_specs=outs),
        out_shape=out_shapes,
        compiler_params=params(),
        cost_estimate=cost(0, 1e8),
        name="widen",
    )(index, own, other)


def tail(index, own, other, mixed, grad_x, shapes, shard):
    number = shapes[0][0] // 2
    tokens, width = mixed.shape
    ins, outs, out_shapes = expert_specs(number, shapes)
    small = pl.BlockSpec((2, PIECE, PIECE), lambda s, e, at: (3 * number, 0, 0))
    rows = pl.BlockSpec((tokens // (2 * number), width), lambda s, e, at: (s * number + e, 0))
    small_shapes = [(shard, width), (shard, width // 2), (shard, width // 2), (shard, width), (EXPERTS, shard), (2, 128), (2, 128)]
    whole = [pl.BlockSpec(shape, lambda s, e, at: (0, 0)) for shape in small_shapes]
    return pl.pallas_call(
        functools.partial(tail_kernel, number),
        grid_spec=pltpu.PrefetchScalarGridSpec(
            num_scalar_prefetch=1,
            grid=(2, number),
            in_specs=ins + [small, small, rows, rows],
            out_specs=outs + [rows, rows] + whole,
        ),
        out_shape=out_shapes
        + [jax.ShapeDtypeStruct((tokens, width), F32)] * 2
        + [jax.ShapeDtypeStruct(shape, F32) for shape in small_shapes],
        compiler_params=params(),
        cost_estimate=cost(0, 1e8),
        name="tail",
    )(index, own, other, own, other, mixed, grad_x)


def swap(value, axis, bit):
    size = lax.axis_size(axis)
    return lax.ppermute(value, axis, [(i, i ^ bit) for i in range(size)])


def group_bits(fsdp):
    bits = [("fsdp", 1 << b) for b in range(1, fsdp.bit_length() - 1)]
    return bits + [("ctx", 1), ("fsdp", 1)]


def group_gather(value, bits):
    stacked = value[None]
    for axis, bit in bits:
        stacked = jnp.concatenate([stacked, swap(stacked, axis, bit)], 0)
    return stacked


def group_reduce(stacked, bits):
    for axis, bit in reversed(bits):
        half = stacked.shape[0] // 2
        arrived = swap(stacked[half:], axis, bit)
        stacked = (stacked[:half].astype(F32) + arrived.astype(F32)).astype(stacked.dtype)
    return stacked[0]


def line_sum(value, ctx):
    pairs = ctx // 2
    if pairs != 4:
        bit = 2
        while bit < ctx:
            value = value + swap(value, "ctx", bit)
            bit *= 2
        return value
    at = lambda z, y: 2 * z + y
    inward = [(at(0, y), at(1, y)) for y in range(2)] + [(at(3, y), at(2, y)) for y in range(2)]
    across = [(at(1, y), at(2, y)) for y in range(2)] + [(at(2, y), at(1, y)) for y in range(2)]
    outward = [(b, a) for a, b in inward]
    value = value + lax.ppermute(value, "ctx", inward)
    value = value + lax.ppermute(value, "ctx", across)
    arrived = lax.ppermute(value, "ctx", outward)
    z = lax.axis_index("ctx") // 2
    return jnp.where((z == 0) | (z == 3), arrived, value)


MESH = pl.DeviceIdType.MESH


def flip(index, bit):
    return jnp.where((index // bit) % 2 == 0, index + bit, index - bit)


def send(src, dst, send_sem, recv_sem, device):
    return pltpu.make_async_remote_copy(src_ref=src, dst_ref=dst, send_sem=send_sem, recv_sem=recv_sem, device_id=device, device_id_type=MESH)


def neighbours():
    ctx, fsdp = lax.axis_index("ctx"), lax.axis_index("fsdp")
    side, across = flip(ctx, 1), flip(fsdp, 2)
    core = {"fsdp": flip(fsdp, 1)}
    return core, [{"fsdp": across}, {"ctx": side}, {"ctx": side, "fsdp": across}]


def greet(devices):
    barrier = pltpu.get_barrier_semaphore()
    for device in devices:
        pl.semaphore_signal(barrier, inc=1, device_id=device, device_id_type=MESH)
    pl.semaphore_wait(barrier, len(devices))


def others(n):
    ctx = lax.axis_index("ctx")
    return [lax.rem(ctx + d, n) for d in range(1, n)]


def exchange_start(src, dst, send_sems, recv_sems, local_sem, n):
    ctx = lax.axis_index("ctx")
    for d, c in enumerate(others(n)):
        send(src.at[c], dst.at[ctx], send_sems.at[d], recv_sems.at[d], {"ctx": c}).start()
    pltpu.make_async_copy(src.at[ctx], dst.at[ctx], local_sem).start()


def exchange_wait(src, dst, send_sems, recv_sems, local_sem, n, arrived=None):
    ctx = lax.axis_index("ctx")
    pltpu.make_async_copy(src.at[ctx], dst.at[ctx], local_sem).wait()
    if arrived is not None:
        arrived(ctx)
    for d in range(n - 1):
        source = lax.rem(ctx + n - 1 - d, n)
        send(src.at[source], dst.at[source], send_sems.at[d], recv_sems.at[d], {"ctx": source}).wait_recv()
        if arrived is not None:
            arrived(source)
    for d, c in enumerate(others(n)):
        send(src.at[c], dst.at[ctx], send_sems.at[d], recv_sems.at[d], {"ctx": c}).wait_send()


def turn_half(v, table, direction, lanes_turned):
    lanes = lane_iota(v.shape)
    swapped = jnp.where(lanes % HEAD_DIMENSION < HEAD_DIMENSION // 2, pltpu.roll(v, 96, 1), pltpu.roll(v, 32, 1))
    return jnp.where(lanes < lanes_turned, v * table[:, :128] + direction * (swapped * table[:, 128:]), v)


def front_kernel(n, cap, wq_ref, wk_ref, wv_ref, wo_part_ref, wr_raw_ref, gain_ref, x_ref, table_ref, routes_ref, cot_ref, packs_ref, h_ref, weights_ref, wo_ref, wr_ref, cxs_ref, gains_ref, wall, packed_ref, wr_part_ref, cx, table, normed_ref, total, out, exch_send, exch_recv, full_send, full_recv, x_send, x_recv, y_send, y_recv, xs_send, xs_recv, ys_send, ys_recv, cx_send, cx_recv, local_sems):
    tokens, width = x_ref.shape
    shard = width // 4
    ctx, fsdp = lax.axis_index("ctx"), lax.axis_index("fsdp")
    parity = lax.rem(ctx, 2)
    core, group = neighbours()
    far, near = group[0], group[1]
    sibling, distant = flip(fsdp, 1), flip(fsdp, 2)
    other = flip(distant, 1)
    for k in range(2):
        pltpu.make_async_copy(table_ref.at[k, ctx], table.at[k], local_sems.at[6 + k]).start()

    pair = HEAD_DIMENSION * 2
    for c in range(0, n, 2):
        keys, values = wk_ref[:, c // 2 * pair : (c // 2 + 1) * pair].astype(F32), wv_ref[:, c // 2 * pair : (c // 2 + 1) * pair].astype(F32)
        low = lane_iota(keys.shape) < HEAD_DIMENSION
        packed_ref[0, :shard, c * 128 : (c + 1) * 128] = jnp.where(low, keys, pltpu.roll(values, 64, 1)).astype(BF16)
        packed_ref[0, :shard, (c + 1) * 128 : (c + 2) * 128] = jnp.where(low, pltpu.roll(keys, 64, 1), values).astype(BF16)
    below = packed_ref.shape[1] - shard
    packed_ref[0, shard:, :] = jnp.zeros((below, width), BF16)
    row = row_iota((16, shard))
    gains = gain_ref[...].astype(F32)
    gain_rows = jnp.where(row == 0, gains[0:1], jnp.where(row == 1, gains[1:2], 0.0))
    packed_ref[0, shard : shard + 16, :shard] = gain_rows.astype(BF16)
    packed_ref[1, :shard, :] = wq_ref[...]
    packed_ref[1, shard:, :] = jnp.zeros((below, width), BF16)
    router = jnp.concatenate([wr_raw_ref[...].astype(F32), jnp.zeros((128 - EXPERTS, shard), F32)], 0)
    wr_part_ref[...] = jnp.transpose(router).astype(BF16)
    greet([core, far] + [{"ctx": c} for c in others(n)])

    half_rows = packed_ref.shape[1] // 2

    def cut(k, part):
        if k < 2:
            return pl.ds(pl.multiple_of(part * half_rows, 16), half_rows)
        if k == 2:
            return pl.ds(part, 1)
        return pl.ds(pl.multiple_of(part * (shard // 2), 16), shard // 2)

    sources = [packed_ref.at[0], packed_ref.at[1], wo_part_ref, wr_part_ref]
    targets = [wall.at[0], wall.at[1], wo_ref, wr_ref]

    def whole(k):
        return send(sources[k], targets[k].at[fsdp], full_send.at[k], full_recv.at[k], core)

    def own(k):
        return pltpu.make_async_copy(sources[k], targets[k].at[fsdp], local_sems.at[k])

    def to_far(k):
        return send(sources[k].at[cut(k, parity)], targets[k].at[fsdp, cut(k, parity)], x_send.at[k], x_recv.at[k], far)

    def pass_on(k, part, sems, device):
        ref = targets[k].at[distant, cut(k, part)]
        return send(ref, ref, sems[0].at[k], sems[1].at[k], device)

    def sibling_arrived(k):
        ref = targets[k].at[sibling]
        send(ref, ref, full_send.at[k], full_recv.at[k], core).wait_recv()

    def far_arrived(k):
        ref = targets[k].at[distant, cut(k, parity)]
        send(ref, ref, x_send.at[k], x_recv.at[k], far).wait_recv()
        pass_on(k, parity, (y_send, y_recv), near).start()
        pass_on(k, parity, (xs_send, xs_recv), core).start()

    def near_arrived(k):
        pass_on(k, 1 - parity, (y_send, y_recv), near).wait_recv()
        pass_on(k, 1 - parity, (ys_send, ys_recv), core).start()

    def core_arrived(k):
        for part, sems in ((parity, (xs_send, xs_recv)), (1 - parity, (ys_send, ys_recv))):
            ref = targets[k].at[other, cut(k, part)]
            send(ref, ref, sems[0].at[k], sems[1].at[k], core).wait_recv()

    for k in range(2):
        to_far(k).start()
    for k in range(2):
        whole(k).start()
        own(k).start()

    prep_kernel(cap, routes_ref, cot_ref, cx)
    pltpu.make_async_copy(cx, cxs_ref.at[0], local_sems.at[4]).start()
    normed, _ = norm_parts(x_ref[...])
    normed_ref[...] = normed

    def project(k, block, begin):
        at = pl.ds(pl.multiple_of(block * shard, shard), shard)
        if k == 0:
            gain = wall[0, block, shard : shard + 16, :shard].astype(F32)
            gains_ref[:, at] = gain
            h_ref[:, at] = (normed_ref[:, at] * gain[:1]).astype(BF16)
        part = dot(h_ref[:, at], wall[k, block, :shard, :])
        total[k] = part if begin else total[k] + part

    for k in range(2):
        own(k).wait()
        project(k, fsdp, True)
        sibling_arrived(k)
        project(k, sibling, False)
        if k == 0:
            far_arrived(0)

    exchanges = []

    def emit(k):
        lanes = slice(128, 256) if k == 0 else slice(0, 128)
        for c in range(n):
            out[c, :, lanes] = turn_half(total[k, :, c * 128 : (c + 1) * 128], angles, 1.0, 64 if k == 0 else 128).astype(BF16)
        cut_lanes = pl.ds(128 if k == 0 else 0, 128)
        source, target = out.at[:, :, cut_lanes], packs_ref.at[:, :, cut_lanes]
        exchanges.append((source, target, exch_send.at[k], exch_recv.at[k], local_sems.at[8 + k], n))
        exchange_start(*exchanges[-1])

    near_arrived(0)
    project(0, distant, False)
    core_arrived(0)
    project(0, other, False)
    for k in range(2):
        pltpu.make_async_copy(table_ref.at[k, ctx], table.at[k], local_sems.at[6 + k]).wait()
    angles = table[...].reshape(tokens, 256)
    emit(0)
    far_arrived(1)
    for k in (2, 3):
        own(k).start()
        whole(k).start()
        to_far(k).start()
    send(cx, cxs_ref.at[1], cx_send.at[0], cx_recv.at[0], far).start()
    near_arrived(1)
    project(1, distant, False)
    core_arrived(1)
    project(1, other, False)
    emit(1)
    keep = pltpu.make_async_copy(wall, weights_ref, local_sems.at[5])
    keep.start()
    for k in (2, 3):
        far_arrived(k)
    for k in (2, 3):
        near_arrived(k)
    for k in (2, 3):
        core_arrived(k)
        sibling_arrived(k)
        own(k).wait()
    for exchange in exchanges:
        exchange_wait(*exchange)
    for k in range(4):
        whole(k).wait_send()
        to_far(k).wait_send()
        pass_on(k, parity, (y_send, y_recv), near).wait_send()
        pass_on(k, parity, (xs_send, xs_recv), core).wait_send()
        pass_on(k, 1 - parity, (ys_send, ys_recv), core).wait_send()
    send(cx, cxs_ref.at[1], cx_send.at[0], cx_recv.at[0], far).wait()
    pltpu.make_async_copy(cx, cxs_ref.at[0], local_sems.at[4]).wait()
    keep.wait()


def front(wq, wk, wv, wo_part, wr, gains, x, table, routes, cot, cap, n):
    tokens, width = x.shape
    shard = wq.shape[0]
    hbm, vmem = pl.BlockSpec(memory_space=pl.ANY), pl.BlockSpec(memory_space=pltpu.VMEM)
    dma = lambda *k: pltpu.SemaphoreType.DMA(k)
    shaped = lambda shape, dtype=BF16: jax.ShapeDtypeStruct(shape, dtype)
    cx_shape = (tokens + EXPERTS, width)
    padded = 2 * 16 * (shard // 32 + 1)
    return pl.pallas_call(
        functools.partial(front_kernel, n, cap),
        in_specs=[vmem, vmem, vmem, hbm, vmem, vmem, vmem, hbm, vmem, vmem],
        out_specs=[hbm, vmem, hbm, hbm, hbm, hbm, vmem],
        out_shape=[
            shaped((n, tokens, PACK)),
            shaped((tokens, width)),
            shaped((2, 4, padded, width)),
            shaped((4,) + wo_part.shape),
            shaped((4, shard, 128)),
            shaped((2,) + cx_shape),
            shaped((16, width), F32),
        ],
        scratch_shapes=[
            pltpu.VMEM((2, 4, padded, width), BF16),
            pltpu.VMEM((2, padded, width), BF16),
            pltpu.VMEM((shard, 128), BF16),
            pltpu.VMEM(cx_shape, BF16),
            pltpu.VMEM((2, tokens // 2, 256), F32),
            pltpu.VMEM((tokens, width), F32),
            pltpu.VMEM((2, tokens, width), F32),
            pltpu.VMEM((n, tokens, PACK), BF16),
            dma(2, n - 1),
            dma(2, n - 1),
        ]
        + [dma(4)] * 10
        + [dma(1), dma(1), dma(10)],
        compiler_params=params(collective_id=1, has_side_effects=True),
        cost_estimate=cost(2e9, 5e7),
        name="front",
    )(wq, wk, wv, wo_part, wr, gains, x, table, routes, cot)


def attend_kernel(length, n, ends_ref, q_ref, pack_ref, cxs_ref, out_ref, lse_ref, full_ref, rest_ref, keys, values_t, acc, near_send, near_recv, far_send, far_recv, core_send, core_recv):
    block = pl.program_id(0)
    core, group = neighbours()
    far, near = group[0], group[1]
    split = cxs_ref.shape[1] // 2

    def to_near(i):
        at = pl.ds(0, cxs_ref.shape[1] if i == 0 else split)
        return send(cxs_ref.at[i, at], rest_ref.at[i, at], near_send.at[i], near_recv.at[i], near)

    def to_far():
        at = pl.ds(split, split)
        return send(rest_ref.at[0, at], rest_ref.at[1, at], far_send.at[0], far_recv.at[0], far)

    def to_core(i):
        src = cxs_ref.at[i] if i < 2 else rest_ref.at[i - 2]
        return send(src, rest_ref.at[2 + i], core_send.at[i], core_recv.at[i], core)

    @pl.when(block == 0)
    def _():
        greet([core, far, near])
        for i in range(2):
            to_near(i).start()
        for i in range(2):
            to_core(i).start()

    attn_forward_kernel(length, ends_ref, q_ref, pack_ref, out_ref, lse_ref, full_ref, keys, values_t, acc)

    @pl.when(block == pl.num_programs(0) - 4)
    def _():
        to_near(0).wait_recv()
        to_far().start()
        to_core(2).start()

    @pl.when(block == pl.num_programs(0) - 1)
    def _():
        to_near(1).wait_recv()
        to_far().wait_recv()
        to_core(3).start()
        for i in range(4):
            to_core(i).wait()
        for i in range(2):
            to_near(i).wait_send()
        to_far().wait_send()


def attend(ends, packs, cxs, length):
    n, _, rows, _ = packs.shape
    blocks, per = length // BLK, BLK // rows
    per_half = blocks // 2
    tiles = lambda i: (lax.rem(i, per_half), i // per_half, 0, 0)
    hbm = pl.BlockSpec(memory_space=pl.ANY)
    dma = lambda k: pltpu.SemaphoreType.DMA((k,))
    return pl.pallas_call(
        functools.partial(attend_kernel, length, n),
        grid=(blocks,),
        in_specs=[
            pl.BlockSpec(memory_space=pltpu.SMEM),
            pl.BlockSpec((per, 1, rows, PACK), tiles),
            pl.BlockSpec(packs.shape, lambda i: (0, 0, 0, 0)),
            hbm,
        ],
        out_specs=[
            pl.BlockSpec((per, 1, rows, 128), tiles),
            pl.BlockSpec((1, 1, 2 * BLK), lambda i: (i, 0, 0)),
            pl.BlockSpec((1, 128, 2 * BLK), lambda i: (i, 0, 0)),
            hbm,
        ],
        scratch_shapes=[
            pltpu.VMEM((length, 128), BF16),
            pltpu.VMEM((128, length), BF16),
            pltpu.VMEM((128, 2 * BLK), F32),
            dma(2),
            dma(2),
            dma(1),
            dma(1),
            dma(4),
            dma(4),
        ],
        out_shape=[
            jax.ShapeDtypeStruct((n, 2, rows, 128), BF16),
            jax.ShapeDtypeStruct((blocks, 1, 2 * BLK), F32),
            jax.ShapeDtypeStruct((blocks, 128, 2 * BLK), F32),
            jax.ShapeDtypeStruct((6,) + cxs.shape[1:], BF16),
        ],
        compiler_params=params(collective_id=3, has_side_effects=True),
        cost_estimate=cost(1.5e10, 2e7),
        name="attend",
    )(ends, packs, packs, cxs)


def mid_kernel(n, number, capp, attn_ref, cxs_ref, rest_ref, wo_hbm, wr_ref, x_hbm, gain_ref, middle_ref, h_ref, kept_ref, xs_ref, gs_ref, gates_ref, arrived, hs, wo_ref, x_ref, cx, rows_out, grads_out, gates_out, exch_send, exch_recv, hop_send, hop_recv, cross_send, cross_recv, fwd_send, fwd_recv, local_sems, load_sems, store_sems):
    tokens, width = x_ref.shape
    split = tokens // 2
    ctx, fsdp = lax.axis_index("ctx"), lax.axis_index("fsdp")
    first = (fsdp * 2 + lax.rem(ctx, 2)) * number
    core, group = neighbours()
    copies = [pltpu.make_async_copy(wo_hbm, wo_ref, local_sems.at[2]), pltpu.make_async_copy(x_hbm, x_ref, local_sems.at[3])]
    for copy in copies:
        copy.start()
    order = (0, 4, 1, 2, 3, 5, 6, 7)

    def load(step):
        b = order[step]
        src = cxs_ref.at[b] if b < 2 else rest_ref.at[b - 2]
        return pltpu.make_async_copy(src, cx.at[step % 2], load_sems.at[step % 2])

    load(0).start()
    greet([core, group[0]] + [{"ctx": c} for c in others(n)])
    halves = [pl.ds(k * split, split) for k in range(2)]
    exchanges = [(attn_ref.at[:, halves[k]], arrived.at[:, halves[k]], exch_send.at[k], exch_recv.at[k], local_sems.at[4 + k], n) for k in range(2)]
    for exchange in exchanges:
        exchange_start(*exchange)
    for copy in copies:
        copy.wait()

    def hop(i, k):
        return send(hs.at[0, halves[k]], hs.at[(1, 2, 4)[i], halves[k]], hop_send.at[i, k], hop_recv.at[i, k], (group[0], group[1], core)[i])

    def cross(i):
        return send(hs.at[1 + i, halves[i]], hs.at[3, halves[i]], cross_send.at[i], cross_recv.at[i], group[1 - i])

    def forward(i):
        return send(hs.at[1 + i], hs.at[5 + i], fwd_send.at[i], fwd_recv.at[i], core)

    for k in range(2):
        exchange_wait(*exchanges[k])
        at = slice(k * split, (k + 1) * split)
        total = None
        for c in range(n):
            part = dot(arrived[c, at, :], wo_ref[c])
            total = part if total is None else total + part
        middle = x_ref[at, :] + RESIDUAL * total
        middle_ref[at, :] = middle
        normed, _ = norm_parts(middle)
        h = (normed * gain_ref[1:2]).astype(BF16)
        h_ref[at, :] = h
        hs[0, at, :] = h
        for i in range(3):
            hop(i, k).start()
    keep = pltpu.make_async_copy(arrived, kept_ref, local_sems.at[1])
    keep.start()

    def stores(step):
        b = order[step]
        pairs = ((rows_out, xs_ref), (grads_out, gs_ref), (gates_out, gates_ref))
        return [pltpu.make_async_copy(src.at[step % 2], dst.at[:, b], store_sems.at[step % 2, k]) for k, (src, dst) in enumerate(pairs)]

    def place(step):
        b, slot = order[step], step % 2
        load(step).wait()
        if step >= 2:
            for copy in stores(step - 2):
                copy.wait()
        h = hs[b]
        logits = jnp.transpose(dot(h, wr_ref[...]))[:EXPERTS, :]
        raw = jnp.exp(logits - jnp.max(logits, 0, keepdims=True))
        router = raw / jnp.sum(raw, 0, keepdims=True)
        slots = cx[slot, tokens:, :tokens].astype(F32)
        hots = one_hot(slots, first, number, capp)
        places = jnp.concatenate(hots, 0).astype(BF16)
        rows = dot(places, h).astype(BF16)
        grads = dot(places, cx[slot, :tokens, :]).astype(BF16)
        for j in range(number):
            at = slice(j * capp, (j + 1) * capp)
            rows_out[slot, j] = rows[at]
            grads_out[slot, j] = grads[at]
            gate = jnp.sum(hots[j] * own_row(router, first + j), 1, keepdims=True)
            gates_out[slot, j] = jnp.broadcast_to(gate, (capp, 128))
        for copy in stores(step):
            copy.start()
        if step + 2 < 8:
            load(step + 2).start()

    load(1).start()
    place(0)
    for k in range(2):
        hop(2, k).wait_recv()
    place(1)
    hop(0, 0).wait_recv()
    cross(0).start()
    hop(1, 0).wait_recv()
    hop(1, 1).wait_recv()
    cross(1).start()
    forward(1).start()
    hop(0, 1).wait_recv()
    forward(0).start()
    place(2)
    place(3)
    for i in range(2):
        cross(i).wait_recv()
    forward(2).start()
    place(4)
    for i in range(3):
        forward(i).wait_recv()
        place(5 + i)
    for step in (6, 7):
        for copy in stores(step):
            copy.wait()
    for i in range(2):
        cross(i).wait_send()
    for i in range(3):
        for k in range(2):
            hop(i, k).wait_send()
        forward(i).wait_send()
    keep.wait()


def mid_step(attn, cxs, rest, wo, wr, x, gains, number, capp, n):
    tokens, width = x.shape
    hbm, vmem = pl.BlockSpec(memory_space=pl.ANY), pl.BlockSpec(memory_space=pltpu.VMEM)
    dma = lambda *k: pltpu.SemaphoreType.DMA(k)
    shaped = lambda shape, dtype=BF16: jax.ShapeDtypeStruct(shape, dtype)
    return pl.pallas_call(
        functools.partial(mid_kernel, n, number, capp),
        in_specs=[hbm, hbm, hbm, hbm, vmem, hbm, vmem],
        out_specs=[vmem, vmem, hbm, hbm, hbm, hbm],
        out_shape=[
            shaped((tokens, width), F32),
            shaped((tokens, width)),
            shaped(attn.shape),
            shaped((number, 8, capp, width)),
            shaped((number, 8, capp, width)),
            shaped((number, 8, capp, 128), F32),
        ],
        scratch_shapes=[
            pltpu.VMEM(attn.shape, BF16),
            pltpu.VMEM((8, tokens, width), BF16),
            pltpu.VMEM(wo.shape, BF16),
            pltpu.VMEM((tokens, width), F32),
            pltpu.VMEM((2,) + cxs.shape[1:], BF16),
            pltpu.VMEM((2, number, capp, width), BF16),
            pltpu.VMEM((2, number, capp, width), BF16),
            pltpu.VMEM((2, number, capp, 128), F32),
            dma(2, n - 1),
            dma(2, n - 1),
            dma(3, 2),
            dma(3, 2),
            dma(2),
            dma(2),
            dma(3),
            dma(3),
            dma(6),
            dma(2),
            dma(2, 3),
        ],
        compiler_params=params(collective_id=2, has_side_effects=True),
        cost_estimate=cost(4e9, 5e7),
        name="mid_step",
    )(attn, cxs, rest, wo, wr, x, gains)


RING = 12
BY_LINE = (20, 22)
LAG_BY_LINE = 6
LAG_MIDDLE, LAG_ACROSS, LAG_END = 1, 2, 4
ORDER_X, ORDER_Y, ORDER_CORE = 1, 2, 4


class GroupSum:
    def __init__(self, part, rows, lands, own, sems, load, free, first, core, group):
        self.part, self.rows, self.own, self.load, self.free, self.first = part, rows, own, load, free, first
        self.land, self.land_x, self.land_y = lands
        self.core_send, self.core_recv, self.x_send, self.x_recv, self.y_send, self.y_recv = sems
        self.core, self.far, self.near = core, group[0], group[1]

    def place(self, i):
        return self.land.at[i, pl.ds(0, self.rows)]

    def ready(self, which):
        if not self.first:
            pl.semaphore_wait(self.free.at[which], 1)

    def to_core(self, i):
        return send(self.part.at[4 + i], self.place(i), self.core_send.at[i], self.core_recv.at[i], self.core)

    def to_far(self, k):
        return send(self.place(1 + 2 * k), self.land_x.at[k, pl.ds(0, self.rows)], self.x_send.at[k], self.x_recv.at[k], self.far)

    def to_near(self):
        return send(self.place(2), self.land_y.at[pl.ds(0, self.rows)], self.y_send.at[0], self.y_recv.at[0], self.near)

    def fetch(self, i):
        return pltpu.make_async_copy(self.part.at[i], self.own.at[i % 2, pl.ds(0, self.rows)], self.load.at[i % 2])

    def start(self):
        self.ready(0)
        for i in (1, 3, 2, 0):
            self.to_core(i).start()

    def over_cores(self):
        order = (1, 3, 2, 0)
        if self.own is not None:
            self.fetch(1).start()
        for step, i in enumerate(order):
            if self.own is None:
                mine = self.part[i]
            else:
                self.fetch(i).wait()
                mine = self.own[i % 2, : self.rows]
            self.to_core(i).wait_recv()
            self.land[i, : self.rows] = (self.land[i, : self.rows].astype(F32) + mine.astype(F32)).astype(BF16)
            if self.own is not None and step < 3:
                self.fetch(order[step + 1]).start()
            if i % 2 == 1:
                if step == 0:
                    self.ready(1)
                self.to_far(i // 2).start()

    def over_x(self, between=None):
        for k in (1, 0):
            if k == 0 and between is not None:
                between()
            self.to_far(k).wait_recv()
            both = self.land[2 * k, : self.rows].astype(F32) + self.land_x[k, : self.rows].astype(F32)
            self.land[2 * k, : self.rows] = both.astype(BF16)
            if k == 1:
                self.ready(2)
                self.to_near().start()

    def finish(self):
        self.to_near().wait_recv()
        for i in range(4):
            self.to_core(i).wait_send()
        for k in range(2):
            self.to_far(k).wait_send()
        self.to_near().wait_send()
        return self.land[0, : self.rows].astype(F32) + self.land_y[: self.rows].astype(F32)

    def release(self):
        for which, device in enumerate((self.core, self.far, self.near)):
            pl.semaphore_signal(self.free.at[which], inc=1, device_id=device, device_id_type=MESH)


class LineSum:
    def __init__(self, count, own_ref, other_ref, inbox, across, mine, sems):
        self.count, self.own_ref, self.other_ref = count, own_ref, other_ref
        self.inbox, self.across, self.mine = inbox, across, mine
        self.line_send, self.line_recv, self.mid_send, self.mid_recv, self.side_send, self.side_recv, self.relay_send, self.store, self.load = sems
        ctx = lax.axis_index("ctx")
        z = ctx // 2
        self.middle = (z == 1) | (z == 2)
        self.line = {"ctx": jnp.where(z % 2 == 0, ctx + 2, ctx - 2)}
        self.peer = {"ctx": jnp.where(z == 1, ctx + 2, ctx - 2)}
        self.side = {"ctx": flip(ctx, 1)}

    def send_line(self, src, i):
        s = lax.rem(i, RING)
        return send(src, self.inbox.at[s], self.line_send.at[s], self.line_recv.at[s], self.line)

    def send_mid(self, i):
        s = lax.rem(i, RING)
        return send(self.inbox.at[s], self.across.at[s], self.mid_send.at[s], self.mid_recv.at[s], self.peer)

    def send_side(self, src, i):
        return send(src, self.other_ref.at[i], self.side_send.at[lax.rem(i, RING)], self.side_recv.at[i], self.side)

    def keep(self, src, i):
        return pltpu.make_async_copy(src, self.own_ref.at[i], self.store.at[lax.rem(i, RING)])

    def relay(self, i):
        ref = self.other_ref.at[i]
        return send(ref, ref, self.relay_send.at[i - BY_LINE[0]], self.side_recv.at[i], self.line)

    def by_side(self, i):
        return (i < BY_LINE[0]) | (i >= BY_LINE[1])

    def fetch(self, src, i):
        s = lax.rem(i, 4)
        return pltpu.make_async_copy(src, self.mine.at[s], self.load.at[s])

    def drain_middle(self, i):
        src = self.across.at[lax.rem(i, RING)]
        self.send_line(src, i).wait_send()
        self.send_side(src, i).wait_send()
        self.keep(src, i).wait()

    def drain_end(self, i):
        src = self.inbox.at[lax.rem(i, RING)]

        @pl.when(self.by_side(i))
        def _():
            self.send_side(src, i).wait_send()

        self.keep(src, i).wait()

    def tick(self, t, source):
        count = self.count
        fixed = isinstance(t, int)

        def when(condition):
            if fixed:
                return (lambda f: f()) if condition else (lambda f: None)
            return pl.when(condition)

        i32 = (lambda v: jnp.int32(v)) if fixed else (lambda v: v)

        @pl.when(self.middle)
        def _():
            @when((t >= LAG_MIDDLE) & (t < count + LAG_MIDDLE))
            def _():
                i = i32(t - LAG_MIDDLE)

                @when(t >= LAG_ACROSS + 4)
                def _():
                    self.drain_middle(i32(t - LAG_ACROSS - 4))

                s = lax.rem(i, RING)
                self.fetch(self.own_ref.at[i], i).wait()
                self.send_line(self.inbox.at[s], i).wait_recv()
                self.inbox[s] = self.inbox[s] + self.mine[lax.rem(i, 4)]
                self.send_mid(i).start()

            @when(t < count)
            def _():
                self.fetch(source(t), i32(t)).start()

            @when((t >= LAG_ACROSS) & (t < count + LAG_ACROSS))
            def _():
                i = i32(t - LAG_ACROSS)
                s = lax.rem(i, RING)
                self.send_mid(i).wait()
                self.across[s] = self.across[s] + self.inbox[s]
                self.send_line(self.across.at[s], i).start()
                self.send_side(self.across.at[s], i).start()
                self.keep(self.across.at[s], i).start()

            @when((t >= BY_LINE[0] + LAG_BY_LINE) & (t < BY_LINE[1] + LAG_BY_LINE))
            def _():
                i = i32(t - LAG_BY_LINE)
                self.send_side(self.mine.at[0], i).wait_recv()
                self.relay(i).start()

        @pl.when(jnp.logical_not(self.middle))
        def _():
            @when(t < count)
            def _():
                @when(t >= LAG_END + 2)
                def _():
                    self.drain_end(i32(t - LAG_END - 2))

                @when(t >= 3)
                def _():
                    self.send_line(self.mine.at[0], i32(t - 3)).wait_send()

                self.send_line(source(t), i32(t)).start()

            @when(t >= LAG_END)
            def _():
                i = i32(t - LAG_END)
                s = lax.rem(i, RING)
                self.send_line(self.inbox.at[s], i).wait_recv()

                @pl.when(self.by_side(i))
                def _():
                    self.send_side(self.inbox.at[s], i).start()

                self.keep(self.inbox.at[s], i).start()

    def finish(self):
        count = self.count

        @pl.when(self.middle)
        def _():
            for i in range(count + LAG_MIDDLE - LAG_ACROSS - 4, count):
                self.drain_middle(jnp.int32(i))
            for i in range(*BY_LINE):
                self.relay(jnp.int32(i)).wait_send()

        @pl.when(jnp.logical_not(self.middle))
        def _():
            for i in range(count - 3, count):
                self.send_line(self.mine.at[0], jnp.int32(i)).wait_send()
            for i in range(count - LAG_END - 2, count):
                self.drain_end(jnp.int32(i))

        def arrived(i, carry):
            @pl.when(jnp.logical_not(self.middle) | self.by_side(i))
            def _():
                self.send_side(self.mine.at[0], i).wait_recv()

            return carry

        lax.fori_loop(0, count, arrived, 0)


def backward_kernel(
    n,
    length,
    capp,
    ends_ref,
    xs_ref,
    gs_ref,
    gates_ref,
    wg_ref,
    wu_ref,
    wd_ref,
    cxs_ref,
    rest_ref,
    full_ref,
    weights_ref,
    packs_hbm,
    table_hbm,
    cot_hbm,
    wo_hbm,
    attn_hbm,
    x_hbm,
    h_attn_hbm,
    h_ref,
    middle_ref,
    wr_ref,
    gains_ref,
    lse_ref,
    own_ref,
    other_ref,
    pieces_ref,
    outs_ref,
    backs_ref,
    gx_ref,
    yp_ref,
    grad_x_ref,
    mixed_ref,
    inbox,
    across,
    mine,
    land,
    land_x,
    land_y,
    y_land,
    y_land_x,
    y_land_y,
    own_buf,
    late_pieces,
    ga_in,
    grads_in,
    line_send,
    line_recv,
    mid_send,
    mid_recv,
    side_send,
    side_recv,
    relay_send,
    line_store,
    line_load,
    ga_send,
    ga_recv,
    gr_send,
    gr_recv,
    group_sems,
    group_load,
    free,
    local_sems,
    full_sems,
    w_sems,
    load_sems,
    store_sems,
    comb_sems,
    part_sems,
):
    tokens, width = h_ref.shape
    half = length // 2
    rows = tokens // 2
    shard = width // 4
    blocks = length // BLK
    number = xs_ref.shape[0]
    ff = wg_ref.shape[2]
    ctx, fsdp = lax.axis_index("ctx"), lax.axis_index("fsdp")
    side = lax.rem(ctx, 2)
    first = (fsdp * 2 + side) * number
    core, group = neighbours()
    sub = own_ref.shape[1]
    cuts = PIECE // sub
    early = number * 6 * cuts
    line = LineSum(early + 2 * cuts, own_ref, other_ref, inbox, across, mine, (line_send, line_recv, mid_send, mid_recv, side_send, side_recv, relay_send, line_store, line_load))

    def source(t):
        return pieces_ref.at[t // cuts, pl.ds(pl.multiple_of(lax.rem(t, cuts) * sub, sub), sub)]

    def tick(t):
        line.tick(jnp.int32(t) if isinstance(t, int) else t, source)

    sems = lambda k: [group_sems.at[k, j] for j in range(6)]
    lands = (land, land_x, land_y)
    ext = tokens + EXPERTS
    gx = GroupSum(gx_ref, 2 * ext, lands, None, sems(0), None, free, True, core, group)
    ys = GroupSum(yp_ref, 2 * tokens, (y_land, y_land_x, y_land_y), own_buf, sems(1), group_load, free, True, core, group)

    def strip(r):
        f = fsdp
        if r & ORDER_X:
            f = flip(f, 2)
        if r & ORDER_CORE:
            f = flip(f, 1)
        return 2 * f + (1 - side if r & ORDER_Y else side)

    def experts(wg, wu, wd, xb, gb, gateb, stage, out_acc, back_acc, outb, backb, go, dgate, comb_o, comb_b, gst, yst, slots):
        def loads(e):
            s = lax.rem(e, 2)
            at = side * number + e
            pairs = ((wg_ref.at[at], wg), (wu_ref.at[at], wu), (wd_ref.at[at], wd), (xs_ref.at[e], xb), (gs_ref.at[e], gb), (gates_ref.at[e], gateb))
            return [pltpu.make_async_copy(src, dst.at[s], load_sems.at[s, k]) for k, (src, dst) in enumerate(pairs)]

        def slot_copy(b):
            src = cxs_ref.at[b] if b < 2 else rest_ref.at[b - 2]
            return pltpu.make_async_copy(src.at[pl.ds(tokens, EXPERTS), pl.ds(0, tokens)], slots.at[b], part_sems.at[0, b])

        def stores(e):
            pairs = (
                (stage.at[pl.ds(0, 3)], pieces_ref.at[pl.ds(6 * e, 3)]),
                (stage.at[pl.ds(3, 3)], pieces_ref.at[pl.ds(6 * e + 3, 3)]),
                (outb, outs_ref.at[e]),
                (backb, backs_ref.at[e]),
            )
            return [pltpu.make_async_copy(src, dst, store_sems.at[k]) for k, (src, dst) in enumerate(pairs)]

        for copy in loads(jnp.int32(0)):
            copy.start()
        for b in range(8):
            slot_copy(b).start()
        greet([core, group[0]] + [{"ctx": c} for c in others(n)])

        def one(e, carry):
            s = lax.rem(e, 2)

            @pl.when(e + 1 < number)
            def _():
                for copy in loads(e + 1):
                    copy.start()

            for copy in loads(e):
                copy.wait()

            @pl.when(e > 0)
            def _():
                for copy in stores(e - 1)[2:]:
                    copy.wait()

            x = xb[s]
            gate = gateb[s][:, :1]
            go[...] = (gate * (RESIDUAL * gb[s].astype(F32))).astype(BF16)
            part = ff // 2
            for chunk in range(2):
                at = slice(chunk * part, (chunk + 1) * part)
                wgc, wuc, wdc = wg[s, :, at], wu[s, :, at], wd[s, at, :]
                pre_gate = dot(x, wgc)
                pre_up = dot(x, wuc)
                sig = jax.nn.sigmoid(pre_gate)
                hidden = (pre_gate * sig * pre_up).astype(BF16)
                out_part = dot(hidden, wdc)
                grad_hidden = dot(go[...], wdc, NT)
                grad_gate = (grad_hidden * pre_up * sig * (1.0 + pre_gate * (1.0 - sig))).astype(BF16)
                grad_up = (grad_hidden * pre_gate * sig).astype(BF16)
                row_part = dot(grad_gate, wgc, NT) + dot(grad_up, wuc, NT)
                dwg = dot(x, grad_gate, TN).astype(BF16)
                dwu = dot(x, grad_up, TN).astype(BF16)
                dwd = dot(hidden, go[...], TN).astype(BF16)
                for k in range(2):
                    cut = slice(k * PIECE, (k + 1) * PIECE)
                    stage[3 * chunk + k, :, :part] = dwg[cut]
                    stage[3 * chunk + k, :, part:] = dwu[cut]
                    stage[3 * chunk + 2, k * part : (k + 1) * part, :] = dwd[:, cut]
                stores(e)[chunk].start()
                if chunk == 0:
                    out_acc[...] = out_part
                    back_acc[...] = row_part
                    stores(e)[0].wait()
                    tick(2 * e)
                else:
                    out = (out_acc[...] + out_part).astype(BF16).astype(F32)
                    outb[...] = (gate * out).astype(BF16)
                    backb[...] = (back_acc[...] + row_part).astype(BF16)
                    grad = jnp.sum(RESIDUAL * gb[s].astype(F32) * out, 1, keepdims=True)
                    dgate[e] = jnp.broadcast_to(grad, dgate.shape[1:])
            for copy in stores(e)[2:]:
                copy.start()
            stores(e)[1].wait()
            tick(2 * e + 1)
            return carry

        lax.fori_loop(0, number, one, 0)
        for copy in stores(jnp.int32(number - 1))[2:]:
            copy.wait()
        for b in range(8):
            slot_copy(b).wait()

        def which(s):
            k = lax.rem(s, 4)
            i = jnp.where(k == 0, 1, jnp.where(k == 1, 3, jnp.where(k == 2, 2, 0)))
            return jnp.where(s < 4, 4 + i, i), i

        def comb(s):
            k = lax.rem(s, 2)
            at = pl.ds(pl.multiple_of(which(s)[0] * capp, 16), capp)
            return [
                pltpu.make_async_copy(outs_ref.at[:, at], comb_o.at[k], comb_sems.at[0, k]),
                pltpu.make_async_copy(backs_ref.at[:, at], comb_b.at[k], comb_sems.at[1, k]),
            ]

        def put(s):
            k = lax.rem(s, 2)
            r, _ = which(s)
            return [
                pltpu.make_async_copy(gst.at[k], gx_ref.at[r], part_sems.at[1, k]),
                pltpu.make_async_copy(yst.at[k], yp_ref.at[r], part_sems.at[1, 2 + k]),
            ]

        for copy in comb(jnp.int32(0)):
            copy.start()

        def join(s, carry):
            k = lax.rem(s, 2)
            r, i = which(s)

            @pl.when(s + 1 < 8)
            def _():
                for copy in comb(s + 1):
                    copy.start()

            for copy in comb(s):
                copy.wait()

            @pl.when(s >= 2)
            def _():
                put(s - 2)[1].wait()

            hots = one_hot(slots[r].astype(F32), first, number, capp)
            places = jnp.concatenate(hots, 0).astype(BF16)
            y = dot(places, comb_o[k].reshape(number * capp, width), TN).astype(BF16)
            back = dot(places, comb_b[k].reshape(number * capp, width), TN).astype(BF16)
            extra = jnp.zeros((EXPERTS, 2 * tokens), F32)
            for j in range(number):
                grads = dgate[j, pl.ds(pl.multiple_of(r * capp, 16), capp), :][:, :1]
                grad = jnp.sum(hots[j] * grads, 0, keepdims=True)
                high = grad.astype(BF16).astype(F32)
                extra = jnp.where(row_iota(extra.shape) == first + j, jnp.concatenate([high, grad - high], 1), extra)
            for q in range(2):
                yst[k, q * tokens : (q + 1) * tokens, :] = y[:, q * PIECE : (q + 1) * PIECE]
                gst[k, q * ext : q * ext + tokens, :] = back[:, q * PIECE : (q + 1) * PIECE]
            gst[k, tokens:ext, :] = extra.astype(BF16)
            gst[k, ext + tokens :, :] = jnp.zeros((EXPERTS, PIECE), BF16)
            put(s)[1].start()

            @pl.when(s < 4)
            def _():
                put(s)[0].start()
                put(s)[0].wait()
                gx.to_core(i).start()

            @pl.when(s >= 4)
            def _():
                gx.to_core(i).wait_recv()
                land[i, : gx.rows] = (land[i, : gx.rows].astype(F32) + gst[k].astype(F32)).astype(BF16)

            @pl.when((s == 4) | (s == 5))
            def _():
                gx.to_far(s - 4).start()

            @pl.when(lax.rem(s, 2) == 1)
            def _():
                tick(2 * number + s // 2)

            return carry

        lax.fori_loop(0, 8, join, 0)
        for s in range(6, 8):
            put(jnp.int32(s))[1].wait()

    slots_rows = xs_ref.shape[1]
    pl.run_scoped(
        experts,
        pltpu.VMEM((2, width, ff), BF16),
        pltpu.VMEM((2, width, ff), BF16),
        pltpu.VMEM((2, ff, width), BF16),
        pltpu.VMEM((2, slots_rows, width), BF16),
        pltpu.VMEM((2, slots_rows, width), BF16),
        pltpu.VMEM((2, slots_rows, 128), F32),
        pltpu.VMEM((6, PIECE, PIECE), BF16),
        pltpu.VMEM((slots_rows, width), F32),
        pltpu.VMEM((slots_rows, width), F32),
        pltpu.VMEM((slots_rows, width), BF16),
        pltpu.VMEM((slots_rows, width), BF16),
        pltpu.VMEM((slots_rows, width), BF16),
        pltpu.VMEM((number, slots_rows, 128), F32),
        pltpu.VMEM((2, number, capp, width), BF16),
        pltpu.VMEM((2, number, capp, width), BF16),
        pltpu.VMEM((2, 2 * ext, PIECE), BF16),
        pltpu.VMEM((2, 2 * tokens, PIECE), BF16),
        pltpu.VMEM((8, EXPERTS, tokens), BF16),
    )
    at_tick = [2 * number + 4]

    def go_on(k=1):
        for _ in range(k):
            tick(at_tick[0])
            at_tick[0] += 1

    def backward(packs, table, keys, values, keys_t, grad_q, grad_k, grad_v, acc, full_buf, ga, pack_out, wbuf, total, grad_middle, dgain, col, small, columns, cot, wo, attn, x_in, h_attn):
        ws = GroupSum(small, PIECE, lands, None, sems(2), None, free, False, core, group)
        cs = GroupSum(columns, PIECE + 16, lands, None, sems(3), None, free, False, core, group)
        copies = [
            pltpu.make_async_copy(src, dst, local_sems.at[4 + k])
            for k, (src, dst) in enumerate(
                ((cot_hbm, cot), (wo_hbm, wo), (attn_hbm, attn), (packs_hbm, packs), (table_hbm, table), (x_hbm, x_in), (h_attn_hbm, h_attn))
            )
        ]
        for copy in copies:
            copy.start()
        small[:, PIECE // 2 : PIECE, :] = jnp.zeros((8, PIECE // 2, PIECE), BF16)
        columns[:, PIECE:, :] = jnp.zeros((8, 16, PIECE), BF16)
        go_on(2)
        gx.over_x(go_on)
        go_on(2)
        arrived = gx.finish()
        arrived = jnp.concatenate([arrived[:ext], arrived[ext:]], 1)
        gx.release()

        h = h_ref[...]
        gain = gains_ref[1:2]
        extra = arrived[tokens:, :]
        grad_router = extra[:, :tokens] + extra[:, tokens : 2 * tokens]
        grad_router = jnp.transpose(jnp.concatenate([grad_router, jnp.zeros((128 - EXPERTS, tokens), F32)], 0))
        logits = dot(h, wr_ref[...])
        logits = jnp.where(lane_iota(logits.shape) < EXPERTS, logits, MASKED)
        raw = jnp.exp(logits - jnp.max(logits, -1, keepdims=True))
        router = raw / jnp.sum(raw, -1, keepdims=True)
        grad_logits = (router * (grad_router - jnp.sum(router * grad_router, -1, keepdims=True))).astype(BF16)
        go_on()
        grad_h = arrived[:tokens, :] + dot(grad_logits, wr_ref[...], NT)
        normed, scale = norm_parts(middle_ref[...])
        dgain[1:2, :] = jnp.sum(grad_h * normed, 0, keepdims=True)
        for copy in copies[:3]:
            copy.wait()
        grad_mid = cot[...] + norm_back(grad_h * gain, normed, scale)
        grad_middle[...] = grad_mid
        grad_branch = (RESIDUAL * grad_mid).astype(BF16)
        for c in range(n):
            ga[c] = dot(grad_branch, wo[c], NT).astype(BF16)
        ga_exchange = (ga, ga_in, ga_send, ga_recv, local_sems.at[2], n)
        exchange_start(*ga_exchange)
        go_on()
        col[:, :128] = dot(h, grad_logits, TN).astype(BF16)
        for r in range(8):
            at = strip(r)
            dwo = dot(attn[at], grad_branch, TN).astype(BF16)
            small[r, 0:128, :] = dwo[:, :PIECE]
            small[r, 128:256, :] = dwo[:, PIECE:]
            small[r, 256:384, 0:128] = col[pl.ds(pl.multiple_of(at * 128, 128), 128), 0:128]
        ws.start()
        ys.start()
        go_on()
        copies[3].wait()
        for hh in range(2):
            for c in range(n):
                kk, vv = pair_keys(packs[c, hh, :, 128:256].astype(F32))
                at = hh * half + c * rows
                keys[at : at + rows, :] = kk.astype(BF16)
                values[at : at + rows, :] = vv.astype(BF16)
                keys_t[:, at : at + rows] = jnp.transpose(kk).astype(BF16)
        grad_k[...] = jnp.zeros_like(grad_k)
        grad_v[...] = jnp.zeros_like(grad_v)
        go_on()
        ws.over_cores()
        ys.over_cores()
        go_on()
        exchange_wait(*ga_exchange)

        per = BLK // rows
        per_half = blocks // 2

        def fetch_full(b):
            return pltpu.make_async_copy(full_ref.at[b], full_buf.at[lax.rem(b, 2)], full_sems.at[lax.rem(b, 2)])

        fetch_full(jnp.int32(0)).start()
        attend_tick = at_tick[0]

        def attend(block, carry):
            late = block // per_half
            c0 = lax.rem(block, per_half) * per
            q2 = stack_heads(jnp.concatenate([packs[c0 + k, late, :, :128] for k in range(per)], 0))
            g2 = stack_heads(jnp.concatenate([ga_in[c0 + k, pl.ds(pl.multiple_of(late * rows, rows), rows), :] for k in range(per)], 0))
            position, start = query_rows(ends_ref, block, length)
            lse = lse_ref[block]

            @pl.when(block + 1 < blocks)
            def _():
                fetch_full(block + 1).start()

            fetch_full(block).wait()
            delta = jnp.sum(jnp.transpose(g2.astype(F32)) * full_buf[lax.rem(block, 2)], 0, keepdims=True)
            acc[...] = jnp.zeros_like(acc)

            def body(kb, carry):
                at = pl.multiple_of(kb * BLK, BLK)
                scores = dot(keys[pl.ds(at, BLK), :], q2, NT) * ATTN_SCALE
                where = key_position(kb, length)
                probs = jnp.where((where <= position) & (where >= start), jnp.exp(scores - lse), 0.0)
                grad_probs = dot(values[pl.ds(at, BLK), :], g2, NT)
                grad_scores = (probs * (grad_probs - delta)).astype(BF16)
                acc[...] += dot(keys_t[:, pl.ds(at, BLK)], grad_scores)
                grad_k[pl.ds(at, BLK), :] += dot(grad_scores, q2)
                grad_v[pl.ds(at, BLK), :] += dot(probs.astype(BF16), g2)

                @pl.when((kb == block) & ((block == per_half) | (block == per_half + 1)))
                def _():
                    tick(attend_tick + 2 + 2 * (block - per_half))

                return carry

            block_loop(block, per_half, body, 0)
            grad_q[pl.ds(pl.multiple_of(block * BLK, BLK), BLK), :] = fold_heads(jnp.transpose(acc[...]))

            @pl.when((block == 1) | (block >= 3))
            def _():
                past = block - per_half
                late_tick = jnp.where(past < 2, 3 + 2 * past, 4 + past)
                tick(attend_tick + jnp.where(block < per_half, block // 2, late_tick))

            return carry

        lax.fori_loop(0, blocks, attend, 0)
        at_tick[0] += blocks
        copies[4].wait()
        for c in range(n):
            for hh in range(2):
                at = slice(hh * half + c * rows, hh * half + (c + 1) * rows)
                kk = grad_k[at, :]
                vv = grad_v[at, :]
                kk = (kk + pltpu.roll(kk, 64, 1)) * ATTN_SCALE
                vv = vv + pltpu.roll(vv, 64, 1)
                both = jnp.where(lane_iota(kk.shape) < 64, kk, vv)
                package = jnp.concatenate([grad_q[at, :] * ATTN_SCALE, both], -1)
                pack_out[c, hh * rows : (hh + 1) * rows, :] = turn(package, table[at, :], -1.0).astype(BF16)
        gr_exchange = (pack_out, grads_in, gr_send, gr_recv, local_sems.at[3], n)
        exchange_start(*gr_exchange)

        def fetch_w(c):
            slot = lax.rem(c, 2)
            at = pl.ds(pl.multiple_of(c * 128, 128), 128)
            return [
                pltpu.make_async_copy(weights_ref.at[1 - k, :, :, at], wbuf.at[slot, :, :, pl.ds(128 * k, 128)], w_sems.at[slot, k])
                for k in range(2)
            ]

        for copy in fetch_w(jnp.int32(0)):
            copy.start()
        go_on()
        ws.over_x()
        ys.over_x()
        go_on(2)
        total[...] = jnp.zeros_like(total)
        late_pieces[:PIECE] = ws.finish().astype(BF16)
        ws.release()
        ffn = ys.finish()
        mixed_ref[...] = middle_ref[...] + RESIDUAL * jnp.concatenate([ffn[:tokens], ffn[tokens:]], 1)
        go_on(3)
        exchange_wait(*gr_exchange)
        copies[5].wait()
        copies[6].wait()

        columns_tick = at_tick[0]

        def finish_columns(c, carry):
            @pl.when(c + 1 < n)
            def _():
                for copy in fetch_w(c + 1):
                    copy.start()

            for copy in fetch_w(c):
                copy.wait()
            slot = lax.rem(c, 2)
            g = grads_in[c]
            col[...] = dot(h_attn[...], g, TN).astype(BF16)
            for r in range(8):
                at = pl.ds(pl.multiple_of(strip(r) * 128, 128), 128)
                columns[r, pl.ds(pl.multiple_of(c // 2 * 128, 128), 128), pl.ds(pl.multiple_of(lax.rem(c, 2) * PACK, PACK), PACK)] = col[at, :]
            for f in range(4):
                total[:, f * shard : (f + 1) * shard] += dot(g, wbuf[slot, f, :shard, :], NT)

            @pl.when(lax.rem(c, 4) == 3)
            def _():
                tick(columns_tick + c // 4)

            return carry

        lax.fori_loop(0, n, finish_columns, 0)
        at_tick[0] += n // 4
        normed, scale = norm_parts(x_in[...])
        grad_h = total[...]
        dgain[0:1, :] = jnp.sum(grad_h * normed, 0, keepdims=True)
        grad_x_ref[...] = grad_middle[...] + norm_back(grad_h * gains_ref[0:1], normed, scale)
        for r in range(8):
            at = pl.ds(pl.multiple_of(strip(r) * 128, 128), 128)
            row = row_iota((16, 128))
            both = jnp.where(row == 0, dgain[0:1, at], jnp.where(row == 1, dgain[1:2, at], 0.0))
            columns[r, PIECE:, 0:128] = both.astype(BF16)
        cs.start()
        go_on()
        cs.over_cores()
        go_on(3)
        cs.over_x(go_on)
        go_on(3)
        summed = cs.finish().astype(BF16)
        late_pieces[PIECE:] = summed[:PIECE]
        late_pieces[384:400] = summed[PIECE:]

    f32, bf = (lambda *shape: pltpu.VMEM(shape, F32)), (lambda *shape: pltpu.VMEM(shape, BF16))
    pl.run_scoped(
        backward,
        bf(*packs_hbm.shape),
        f32(*table_hbm.shape),
        bf(length, 128),
        bf(length, 128),
        bf(128, length),
        f32(length, 128),
        f32(length, 128),
        f32(length, 128),
        f32(128, 2 * BLK),
        f32(2, 128, 2 * BLK),
        bf(n, tokens, 128),
        bf(n, tokens, PACK),
        bf(2, 4, weights_ref.shape[2], PACK),
        f32(tokens, width),
        f32(tokens, width),
        f32(8, width),
        bf(width, PACK),
        bf(8, PIECE, PIECE),
        bf(8, PIECE + 16, PIECE),
        f32(tokens, width),
        bf(*wo_hbm.shape),
        bf(*attn_hbm.shape),
        f32(tokens, width),
        bf(tokens, width),
    )

    def rest(t, carry):
        tick(t)
        return carry

    lax.fori_loop(at_tick[0], early, rest, 0)

    def late_source(t):
        return late_pieces.at[pl.ds(pl.multiple_of((t - early) * sub, sub), sub)]

    def late(t, carry):
        line.tick(t, late_source)
        return carry

    lax.fori_loop(early, line.count + LAG_END, late, 0)
    line.finish()


def backward_step(ends, xs, gs, gates, w_gate, w_up, w_down, cxs, rest, full, weights, packs, table, cot, wo, attn, x, h_attn, h, middle, wr, gains, lse, n, length, capp):
    tokens, width = x.shape
    number, slots_rows, _ = xs.shape
    hbm, vmem = pl.BlockSpec(memory_space=pl.ANY), pl.BlockSpec(memory_space=pltpu.VMEM)
    smem = pl.BlockSpec(memory_space=pltpu.SMEM)
    dma = lambda *k: pltpu.SemaphoreType.DMA(k)
    shaped = lambda shape, dtype=BF16: jax.ShapeDtypeStruct(shape, dtype)
    sub = PIECE // 2
    piece = (sub, PIECE)
    count = (number * 6 + 2) * 2
    land_rows = max(2 * (tokens + EXPERTS), PIECE + 16)
    return pl.pallas_call(
        functools.partial(backward_kernel, n, length, capp),
        in_specs=[smem] + [hbm] * 17 + [vmem] * 5,
        out_specs=[hbm] * 7 + [vmem, vmem],
        out_shape=[
            shaped((count,) + piece),
            shaped((count,) + piece),
            shaped((number * 6, PIECE, PIECE)),
            shaped(xs.shape),
            shaped(xs.shape),
            shaped((8, 2 * (tokens + EXPERTS), PIECE)),
            shaped((8, 2 * tokens, PIECE)),
            shaped((tokens, width), F32),
            shaped((tokens, width), F32),
        ],
        scratch_shapes=[
            pltpu.VMEM((RING,) + piece, BF16),
            pltpu.VMEM((RING,) + piece, BF16),
            pltpu.VMEM((4,) + piece, BF16),
            pltpu.VMEM((4, land_rows, PIECE), BF16),
            pltpu.VMEM((2, land_rows, PIECE), BF16),
            pltpu.VMEM((land_rows, PIECE), BF16),
            pltpu.VMEM((4, 2 * tokens, PIECE), BF16),
            pltpu.VMEM((2, 2 * tokens, PIECE), BF16),
            pltpu.VMEM((2 * tokens, PIECE), BF16),
            pltpu.VMEM((2, 2 * tokens, PIECE), BF16),
            pltpu.VMEM((2 * PIECE, PIECE), BF16),
            pltpu.VMEM((n, tokens, 128), BF16),
            pltpu.VMEM((n, tokens, PACK), BF16),
            dma(RING),
            dma(RING),
            dma(RING),
            dma(RING),
            dma(RING),
            dma(count),
            dma(BY_LINE[1] - BY_LINE[0]),
            dma(RING),
            dma(4),
            dma(n - 1),
            dma(n - 1),
            dma(n - 1),
            dma(n - 1),
            dma(4, 6, 4),
            dma(2),
            pltpu.SemaphoreType.REGULAR((3,)),
            dma(11),
            dma(2),
            dma(2, 2),
            dma(2, 6),
            dma(4),
            dma(2, 2),
            dma(2, 8),
        ],
        compiler_params=params(63, collective_id=0, has_side_effects=True),
        cost_estimate=cost(6e10, 1e9),
        name="backward_step",
    )(ends, xs, gs, gates, w_gate, w_up, w_down, cxs, rest, full, weights, packs, table, cot, wo, attn, x, h_attn, h, middle, wr, gains, lse)


def local(
    inputs,
    cotangent,
    doc_lengths,
    routes,
    attn_gain,
    ffn_gain,
    w_query,
    key_weight,
    value_weight,
    w_out,
    w_router,
    w_gate,
    w_up,
    w_down,
):
    rows = inputs.shape[2]
    width = inputs.shape[3]
    n = lax.axis_size("ctx")
    fsdp = lax.axis_size("fsdp")
    me, mine = lax.axis_index("ctx"), lax.axis_index("fsdp")
    tokens = 2 * rows
    length = tokens * n
    experts_here = w_gate.shape[0]
    number = experts_here // 2
    capacity = 5 * tokens * TOP // (4 * EXPERTS)
    capp = -(-capacity // 16) * 16
    shard = width // fsdp
    heads = QUERY_HEADS // n
    head_lanes = heads * HEAD_DIMENSION
    copies = n // KEY_VALUE_HEADS
    bits = group_bits(fsdp)

    x = inputs.reshape(tokens, width)
    cot = cotangent.reshape(tokens, width)
    side = me % 2
    base = (side * number).astype(jnp.int32).reshape(1)
    first = (mine * experts_here + side * number).astype(jnp.int32).reshape(1)
    index = jnp.stack([side * number, (1 - side) * number]).astype(jnp.int32)
    ends = doc_lengths
    table = jnp.asarray(rotary_table(length))

    out_part = w_out.reshape(shard // head_lanes, head_lanes, width)
    if head_lanes < 128:
        out_part = jnp.pad(out_part, ((0, 0), (0, 128 - head_lanes), (0, 0)))
    merge = lambda a: a.reshape(number, -1, a.shape[-1])

    if n == 8 and fsdp == 4:
        packs, h_attn, weights, wo, wr, cxs, gains = front(
            w_query,
            key_weight,
            value_weight,
            out_part,
            jnp.transpose(w_router),
            jnp.stack([attn_gain, ffn_gain]),
            x,
            table.reshape(2, n, rows, 256),
            jnp.transpose(routes[0], (0, 2, 1)),
            cot,
            capacity,
            n,
        )
        wo, wr = wo.reshape(n, 128, width), wr.reshape(width, 128)
        packs = packs.reshape(n, 2, rows, PACK)
        attn, lse, full, cx_rest = attend(ends, packs, cxs, length)
        middle, h_ffn, attn, xs, gs, gates = mid_step(attn.reshape(n, tokens, 128), cxs, cx_rest, wo, wr, x, gains, number, capp, n)
        own, other, _, _, _, _, _, grad_x, mixed = backward_step(
            ends,
            merge(xs),
            merge(gs),
            merge(gates),
            w_gate,
            w_up,
            w_down,
            cxs,
            cx_rest,
            full,
            weights,
            packs,
            table,
            cot,
            wo,
            attn,
            x,
            h_attn,
            h_ffn,
            middle,
            wr,
            gains,
            lse,
            n,
            length,
            capp,
        )
        own, other = own.reshape(-1, PIECE, PIECE), other.reshape(-1, PIECE, PIECE)
        shapes = [w.shape for w in (w_gate, w_up, w_down)]
        outs = tail(index, own, other, mixed, grad_x, shapes, shard)
        return (
            outs[3].reshape(inputs.shape),
            outs[4].reshape(inputs.shape),
            outs[10].reshape(shard),
            outs[11].reshape(shard),
            outs[5],
            outs[6],
            outs[7],
            outs[8],
            jnp.transpose(outs[9]),
            outs[0],
            outs[1],
            outs[2],
        )

    else:
        own_table = lax.dynamic_slice_in_dim(table.reshape(2, n, rows, 256), me, 1, 1).reshape(tokens, 256)
        query_part = w_query.reshape(shard, n, head_lanes)
        if head_lanes < 128:
            query_part = jnp.pad(query_part, ((0, 0), (0, 0), (0, 128 - head_lanes)))
        key_part = jnp.repeat(key_weight.reshape(shard, KEY_VALUE_HEADS, HEAD_DIMENSION), copies, 1)
        value_part = jnp.repeat(value_weight.reshape(shard, KEY_VALUE_HEADS, HEAD_DIMENSION), copies, 1)
        packed = jnp.concatenate([query_part, key_part, value_part], -1).reshape(shard, n * PACK)
        padding = 2 * 16 * (shard // 32 + 1) - shard
        gains = jnp.pad(jnp.stack([attn_gain, ffn_gain]), ((0, padding - 2), (0, n * PACK - shard)))
        packed = jnp.concatenate([packed, gains], 0)
        router_part = jnp.pad(w_router, ((0, 0), (0, 128 - EXPERTS)))
        weights = lax.all_gather(packed, "fsdp", axis=0)
        gain_one = weights[:, shard, :shard].reshape(1, width).astype(F32)
        gain_two = weights[:, shard + 1, :shard].reshape(1, width).astype(F32)
        wo = lax.all_gather(out_part, "fsdp", axis=0, tiled=True)
        wr = lax.all_gather(router_part, "fsdp", axis=0, tiled=True)
        cxs = group_gather(prep(jnp.transpose(routes[0], (0, 2, 1)), cot, capacity), bits)
        packs, h_attn = qkv(x, gain_one, weights, own_table, shard, n)
        packs = lax.all_to_all(packs, "ctx", split_axis=0, concat_axis=0, tiled=True).reshape(n, 2, rows, PACK)
        attn, lse, full = attn_forward(ends, packs, length)
        attn = lax.all_to_all(attn.reshape(n, tokens, 128), "ctx", split_axis=0, concat_axis=0, tiled=True)
        middle, h_ffn = middle_step(attn, wo, x, gain_two)
        xs, gs, gates = gather_rows(first, group_gather(h_ffn, bits), cxs, jnp.transpose(wr), number, capp)
        slots = cxs[:, tokens:]
    xs, gs, gates = merge(xs), merge(gs), merge(gates)
    pieces, outs, back, dgates = expert_step(base, xs, gs, gates, w_gate, w_up, w_down)
    y_part, gx_part = combine(first, slots, outs, back, dgates, tokens, capp)
    pieces = pieces.reshape(number * 6, PIECE, PIECE)
    gx = group_reduce(gx_part, bits)
    grad_middle, dwo, grad_attn, dwr, dgain_two = home_step(gx, h_ffn, middle, cot, wr, wo, gain_two, attn)
    grad_attn = lax.all_to_all(grad_attn, "ctx", split_axis=0, concat_axis=0, tiled=True).reshape(n, 2, rows, 128)
    grads = attn_backward(ends, packs, grad_attn, lse, full, table, length)
    grads = lax.all_to_all(grads.reshape(n, tokens, PACK), "ctx", split_axis=0, concat_axis=0, tiled=True)
    dw, grad_x, dgain_one = final_step(grads, weights, h_attn, x, gain_one, grad_middle, shard)
    mixed = middle + RESIDUAL * group_reduce(y_part, bits).astype(F32)
    own = line_sum(pieces, n)
    other = swap(own, "ctx", 1)
    scatter = lambda a: lax.psum(lax.psum_scatter(a, "fsdp", scatter_dimension=0, tiled=True), "ctx").astype(F32)
    dwo = scatter(dwo)[:, :head_lanes, :].reshape(shard, width)
    small = jnp.concatenate([dwr[:, :EXPERTS], dgain_two.reshape(width, 1).astype(BF16)], 1)
    small = scatter(jnp.pad(small, ((0, 0), (0, 127 - EXPERTS))))
    dwr, dgain_two = small[:, :EXPERTS], small[:, EXPERTS]
    dw = scatter(dw).reshape(shard, n, PACK)
    dgain_one = scatter(dgain_one.reshape(width).astype(BF16))

    outs = widen(index, own, other, [w.shape for w in (w_gate, w_up, w_down)])
    fold = lambda a: a.reshape(shard, KEY_VALUE_HEADS, copies, HEAD_DIMENSION).sum(2).reshape(shard, -1)
    return (
        mixed.reshape(inputs.shape),
        grad_x.reshape(inputs.shape),
        dgain_one,
        dgain_two,
        dw[:, :, :head_lanes].reshape(shard, -1),
        fold(dw[:, :, 128:192]),
        fold(dw[:, :, 192:256]),
        dwo,
        dwr,
        outs[0],
        outs[1],
        outs[2],
    )


def solution(mesh):
    tokens = P("fsdp", None, "ctx", None)
    one, two, three = P("fsdp"), P("fsdp", None), P("fsdp", None, None)
    return jax.shard_map(
        local,
        mesh=mesh,
        in_specs=(tokens, tokens, two, tokens, one, one, two, two, two, two, two, three, three, three),
        out_specs=(tokens, tokens, one, one, two, two, two, two, two, three, three, three),
        check_vma=False,
    )
```

```python
import functools

import jax
import jax.numpy as jnp
import numpy as np
from jax import lax
from jax.experimental import pallas as pl
from jax.experimental.pallas import tpu as pltpu
from jax.sharding import PartitionSpec as P

QUERY_HEADS = 16
KEY_VALUE_HEADS = 8
HEAD_DIMENSION = 64
EXPERTS = 32
TOP = 8

ATTN_SCALE = 0.015625
RESIDUAL = 0.22
NORM_EPS = 1e-06
ROPE_BASE = 10000.0
MASKED = -1e30

F32 = jnp.float32
BF16 = jnp.bfloat16
MIB = 1 << 20
NT = (((1,), (1,)), ((), ()))
TN = (((0,), (0,)), ((), ()))
BLK = 256
PACK = 256


def dot(a, b, dims=None):
    if dims is None:
        return jnp.dot(a, b, preferred_element_type=F32)
    return lax.dot_general(a, b, dims, preferred_element_type=F32)


def params(limit=56, **kw):
    return pltpu.CompilerParams(vmem_limit_bytes=limit * MIB, **kw)


def cost(flops, bytes_accessed):
    return pl.CostEstimate(flops=int(flops), bytes_accessed=int(bytes_accessed), transcendentals=0)


def lane_iota(shape):
    return lax.broadcasted_iota(jnp.int32, shape, len(shape) - 1)


def row_iota(shape):
    return lax.broadcasted_iota(jnp.int32, shape, len(shape) - 2)


def rotary_table(length):
    half = length // 2
    order = np.arange(half, dtype=np.float32)
    positions = np.concatenate([order, length - 1 - order]).astype(np.float32)
    m = np.arange(HEAD_DIMENSION // 2, dtype=np.float64)
    frequency = (ROPE_BASE ** (-2.0 * m / HEAD_DIMENSION)).astype(np.float32)
    angles = (positions[:, None] * frequency[None, :]).astype(np.float64)
    cosine, sine = np.cos(angles), np.sin(angles)
    cos_head = np.concatenate([cosine, cosine], -1)
    sin_head = np.concatenate([-sine, sine], -1)
    return np.concatenate([cos_head, cos_head, sin_head, sin_head], -1).astype(np.float32)


def turn(v, table, direction):
    lanes = lane_iota(v.shape)
    cosine = jnp.concatenate([table[:, :128], table[:, :128]], -1)
    sine = jnp.concatenate([table[:, 128:], table[:, 128:]], -1)
    turned = lanes < 3 * HEAD_DIMENSION
    swapped = jnp.where(lanes % HEAD_DIMENSION < HEAD_DIMENSION // 2, pltpu.roll(v, PACK - 32, 1), pltpu.roll(v, 32, 1))
    return jnp.where(turned, v * cosine + direction * (swapped * sine), v)


def norm_parts(values):
    inv_rms = lax.rsqrt(jnp.mean(values * values, -1, keepdims=True) + NORM_EPS)
    return values * inv_rms, inv_rms


def norm_back(grad_normed, normed, inv_rms):
    return inv_rms * (grad_normed - normed * jnp.mean(grad_normed * normed, -1, keepdims=True))


def prep_kernel(cap, routes_ref, cot_ref, out_ref):
    tokens, width = cot_ref.shape
    earlier = (row_iota((tokens, tokens)) < lane_iota((tokens, tokens))).astype(BF16)
    experts = row_iota((EXPERTS, tokens))
    base = jnp.zeros((EXPERTS, 1), F32)
    plus = jnp.zeros((EXPERTS, tokens), F32)
    for k in range(TOP):
        row = jnp.concatenate([routes_ref[0, k : k + 1, :], routes_ref[1, k : k + 1, :]], 1)
        chosen = experts == row
        ones = chosen.astype(F32)
        slot = dot(ones.astype(BF16), earlier) + base
        plus = plus + jnp.where(chosen & (slot < cap), slot + 1.0, 0.0)
        base = base + jnp.sum(ones, 1, keepdims=True)
    out_ref[:tokens, :] = cot_ref[...].astype(BF16)
    out_ref[tokens:, :] = jnp.concatenate([plus - 1.0, jnp.zeros((EXPERTS, width - tokens), F32)], -1).astype(BF16)


def prep(routes, cot, cap):
    tokens, width = cot.shape
    return pl.pallas_call(
        functools.partial(prep_kernel, cap),
        out_shape=jax.ShapeDtypeStruct((tokens + EXPERTS, width), BF16),
        compiler_params=params(),
        cost_estimate=cost(1e9, 2e6),
        name="prep",
    )(routes, cot)


def qkv_kernel(shard, x_ref, gain_ref, w_ref, table_ref, out_ref, h_ref):
    @pl.when(pl.program_id(0) == 0)
    def _():
        normed, _ = norm_parts(x_ref[...])
        h_ref[...] = (normed * gain_ref[...]).astype(BF16)

    total = None
    for f in range(w_ref.shape[0]):
        part = dot(h_ref[:, f * shard : (f + 1) * shard], w_ref[f, :shard, :])
        total = part if total is None else total + part
    for d in range(out_ref.shape[0]):
        out_ref[d] = turn(total[:, d * PACK : (d + 1) * PACK], table_ref[...], 1.0).astype(BF16)


def qkv(x, gain, weights, table, shard, n):
    tokens, width = x.shape
    fsdp, padded, _ = weights.shape
    return pl.pallas_call(
        functools.partial(qkv_kernel, shard),
        grid=(n // 2,),
        in_specs=[
            pl.BlockSpec((tokens, width), lambda i: (0, 0)),
            pl.BlockSpec((1, width), lambda i: (0, 0)),
            pl.BlockSpec((fsdp, padded, 2 * PACK), lambda i: (0, 0, i)),
            pl.BlockSpec((tokens, 256), lambda i: (0, 0)),
        ],
        out_specs=[
            pl.BlockSpec((2, tokens, PACK), lambda i: (i, 0, 0)),
            pl.BlockSpec((tokens, width), lambda i: (0, 0)),
        ],
        out_shape=[
            jax.ShapeDtypeStruct((n, tokens, PACK), BF16),
            jax.ShapeDtypeStruct((tokens, width), BF16),
        ],
        compiler_params=params(),
        cost_estimate=cost(2 * tokens * width * n * PACK, 8e6),
        name="qkv",
    )(x, gain, weights, table)


def pair_keys(kv):
    other = pltpu.roll(kv, 64, 1)
    low = lane_iota(kv.shape) < 64
    return jnp.where(low, kv, other), jnp.where(low, other, kv)


def stack_heads(q):
    low = lane_iota(q.shape) < 64
    zero = jnp.zeros_like(q)
    return jnp.concatenate([jnp.where(low, q, zero), jnp.where(low, zero, q)], 0)


def fold_heads(stacked):
    rows = stacked.shape[0] // 2
    return jnp.where(lane_iota((rows, 128)) < 64, stacked[:rows], stacked[rows:])


def query_rows(ends_ref, block, length):
    half = length // 2
    lanes = lane_iota((1, 2 * BLK))
    index = block * BLK + jnp.where(lanes < BLK, lanes, lanes - BLK)
    position = jnp.where(index < half, index, length + half - 1 - index)
    start = jnp.zeros_like(position)
    end = 0
    for j in range(3):
        end = end + ends_ref[0, j]
        start = jnp.where(position >= end, jnp.maximum(start, end), start)
    return position, start


def key_position(kb, length):
    half = length // 2
    index = kb * BLK + row_iota((BLK, 1))
    return jnp.where(index < half, index, length + half - 1 - index)


def block_loop(block, per_half, body, init):
    late = block >= per_half
    inner = jnp.where(late, block - per_half, block)

    def plain(kb, carry):
        return body(kb, True, carry)

    def masked(kb, carry):
        return body(kb, False, carry)

    carry = lax.fori_loop(0, jnp.where(late, per_half, inner), plain, init)
    return lax.fori_loop(block, jnp.where(late, 2 * per_half, block + 1), masked, carry)


def attn_forward_kernel(length, ends_ref, q_ref, pack_ref, out_ref, lse_ref, full_ref, keys, values_t, acc):
    block = pl.program_id(0)
    half = length // 2
    n, _, rows, _ = pack_ref.shape

    @pl.when(block == 0)
    def _():
        for h in range(2):
            for c in range(n):
                kk, vv = pair_keys(pack_ref[c, h, :, 128:256].astype(F32))
                at = h * half + c * rows
                keys[at : at + rows, :] = kk.astype(BF16)
                if rows % 128 == 0:
                    values_t[:, at : at + rows] = jnp.transpose(vv).astype(BF16)
        if rows % 128 != 0:
            for h in range(2):
                for c in range(0, n, 2):
                    pair = jnp.concatenate([pack_ref[c, h, :, 128:256], pack_ref[c + 1, h, :, 128:256]], 0)
                    _, vv = pair_keys(pair.astype(F32))
                    at = h * half + c * rows
                    values_t[:, at : at + 2 * rows] = jnp.transpose(vv).astype(BF16)

    q = q_ref[...].reshape(BLK, PACK)[:, :128]
    q2 = stack_heads((q.astype(F32) * ATTN_SCALE).astype(BF16))
    position, start = query_rows(ends_ref, block, length)
    bias = jnp.where(start > 0, MASKED, 0.0)
    acc[...] = jnp.zeros_like(acc)

    def body(kb, whole, carry):
        peak, total = carry
        at = pl.multiple_of(kb * BLK, BLK)
        scores = dot(keys[pl.ds(at, BLK), :], q2, NT)
        if whole:
            scores = scores + bias
        else:
            where = key_position(kb, length)
            scores = jnp.where((where <= position) & (where >= start), scores, MASKED)
        new_peak = jnp.maximum(peak, jnp.max(scores, 0, keepdims=True))
        weights = jnp.exp(scores - new_peak)
        fade = jnp.exp(peak - new_peak)
        total = total * fade + jnp.sum(weights, 0, keepdims=True)
        acc[...] = acc[...] * fade + dot(values_t[:, pl.ds(at, BLK)], weights.astype(BF16))
        return new_peak, total

    init = (jnp.full((1, 2 * BLK), MASKED, F32), jnp.zeros((1, 2 * BLK), F32))
    peak, total = block_loop(block, half // BLK, body, init)
    result = acc[...] / total
    full_ref[0] = result
    lse_ref[0] = peak + jnp.log(total)
    folded = fold_heads(jnp.transpose(result)).astype(BF16)
    out_ref[...] = folded.reshape(out_ref.shape)


def attn_forward(ends, packs, length):
    n, _, rows, _ = packs.shape
    blocks, per = length // BLK, BLK // rows
    per_half = blocks // 2
    tiles = lambda i, ends: (lax.rem(i, per_half), i // per_half, 0, 0)
    return pl.pallas_call(
        functools.partial(attn_forward_kernel, length),
        grid_spec=pltpu.PrefetchScalarGridSpec(
            num_scalar_prefetch=1,
            grid=(blocks,),
            in_specs=[
                pl.BlockSpec((per, 1, rows, PACK), tiles),
                pl.BlockSpec(packs.shape, lambda i, ends: (0, 0, 0, 0)),
            ],
            out_specs=[
                pl.BlockSpec((per, 1, rows, 128), tiles),
                pl.BlockSpec((1, 1, 2 * BLK), lambda i, ends: (i, 0, 0)),
                pl.BlockSpec((1, 128, 2 * BLK), lambda i, ends: (i, 0, 0)),
            ],
            scratch_shapes=[
                pltpu.VMEM((length, 128), BF16),
                pltpu.VMEM((128, length), BF16),
                pltpu.VMEM((128, 2 * BLK), F32),
            ],
        ),
        out_shape=[
            jax.ShapeDtypeStruct((n, 2, rows, 128), BF16),
            jax.ShapeDtypeStruct((blocks, 1, 2 * BLK), F32),
            jax.ShapeDtypeStruct((blocks, 128, 2 * BLK), F32),
        ],
        compiler_params=params(),
        cost_estimate=cost(1.5e10, 6e6),
        name="attn_forward",
    )(ends, packs, packs)


def attn_backward_kernel(length, ends_ref, q_ref, g_ref, pack_ref, lse_ref, full_ref, table_ref, out_ref, keys, values, keys_t, grad_q, grad_k, grad_v, acc):
    block = pl.program_id(0)
    half = length // 2
    n, _, rows, _ = pack_ref.shape

    @pl.when(block == 0)
    def _():
        for h in range(2):
            for c in range(n):
                kk, vv = pair_keys(pack_ref[c, h, :, 128:256].astype(F32))
                at = h * half + c * rows
                keys[at : at + rows, :] = kk.astype(BF16)
                values[at : at + rows, :] = vv.astype(BF16)
        for b in range(length // BLK):
            keys_t[:, b * BLK : (b + 1) * BLK] = jnp.transpose(keys[b * BLK : (b + 1) * BLK, :].astype(F32)).astype(BF16)
        grad_k[...] = jnp.zeros_like(grad_k)
        grad_v[...] = jnp.zeros_like(grad_v)

    q2 = stack_heads((q_ref[...].reshape(BLK, PACK)[:, :128].astype(F32) * ATTN_SCALE).astype(BF16))
    g2 = stack_heads(g_ref[...].reshape(BLK, 128))
    position, start = query_rows(ends_ref, block, length)
    lse = lse_ref[0]
    shift = jnp.where(start > 0, MASKED, 0.0) - lse
    delta = jnp.sum(jnp.transpose(g2.astype(F32)) * full_ref[0], 0, keepdims=True)
    acc[...] = jnp.zeros_like(acc)

    def body(kb, whole, carry):
        at = pl.multiple_of(kb * BLK, BLK)
        scores = dot(keys[pl.ds(at, BLK), :], q2, NT)
        if whole:
            probs = jnp.exp(scores + shift)
        else:
            where = key_position(kb, length)
            probs = jnp.where((where <= position) & (where >= start), jnp.exp(scores - lse), 0.0)
        grad_probs = dot(values[pl.ds(at, BLK), :], g2, NT)
        grad_scores = (probs * (grad_probs - delta)).astype(BF16)
        acc[...] += dot(keys_t[:, pl.ds(at, BLK)], grad_scores)
        grad_k[pl.ds(at, BLK), :] += dot(grad_scores, q2)
        grad_v[pl.ds(at, BLK), :] += dot(probs.astype(BF16), g2)
        return carry

    block_loop(block, half // BLK, body, 0)
    grad_q[pl.ds(pl.multiple_of(block * BLK, BLK), BLK), :] = fold_heads(jnp.transpose(acc[...]))

    @pl.when(block == length // BLK - 1)
    def _():
        for h in range(2):
            for c in range(n):
                at = slice(h * half + c * rows, h * half + (c + 1) * rows)
                kk = grad_k[at, :]
                vv = grad_v[at, :]
                kk = kk + pltpu.roll(kk, 64, 1)
                vv = vv + pltpu.roll(vv, 64, 1)
                both = jnp.where(lane_iota(kk.shape) < 64, kk, vv)
                package = jnp.concatenate([grad_q[at, :] * ATTN_SCALE, both], -1)
                out_ref[c, h] = turn(package, table_ref[at, :], -1.0).astype(BF16)


def attn_backward(ends, packs, grads, lse, full, table, length):
    n, _, rows, _ = packs.shape
    blocks, per = length // BLK, BLK // rows
    per_half = blocks // 2
    tiles = lambda i, ends: (lax.rem(i, per_half), i // per_half, 0, 0)
    return pl.pallas_call(
        functools.partial(attn_backward_kernel, length),
        grid_spec=pltpu.PrefetchScalarGridSpec(
            num_scalar_prefetch=1,
            grid=(blocks,),
            in_specs=[
                pl.BlockSpec((per, 1, rows, PACK), tiles),
                pl.BlockSpec((per, 1, rows, 128), tiles),
                pl.BlockSpec(packs.shape, lambda i, ends: (0, 0, 0, 0)),
                pl.BlockSpec((1, 1, 2 * BLK), lambda i, ends: (i, 0, 0)),
                pl.BlockSpec((1, 128, 2 * BLK), lambda i, ends: (i, 0, 0)),
                pl.BlockSpec(table.shape, lambda i, ends: (0, 0)),
            ],
            out_specs=pl.BlockSpec(packs.shape, lambda i, ends: (0, 0, 0, 0)),
            scratch_shapes=[
                pltpu.VMEM((length, 128), BF16),
                pltpu.VMEM((length, 128), BF16),
                pltpu.VMEM((128, length), BF16),
                pltpu.VMEM((length, 128), F32),
                pltpu.VMEM((length, 128), F32),
                pltpu.VMEM((length, 128), F32),
                pltpu.VMEM((128, 2 * BLK), F32),
            ],
        ),
        out_shape=jax.ShapeDtypeStruct(packs.shape, BF16),
        compiler_params=params(),
        cost_estimate=cost(3e10, 8e6),
        name="attn_backward",
    )(ends, packs, grads, packs, lse, full, table)


def middle_kernel(attn_ref, wo_ref, x_ref, gain_ref, middle_ref, h_ref):
    total = None
    for c in range(attn_ref.shape[0]):
        part = dot(attn_ref[c], wo_ref[c])
        total = part if total is None else total + part
    middle = x_ref[...] + RESIDUAL * total
    middle_ref[...] = middle
    normed, _ = norm_parts(middle)
    h_ref[...] = (normed * gain_ref[...]).astype(BF16)


def middle_step(attn, wo, x, gain):
    tokens, width = x.shape
    return pl.pallas_call(
        middle_kernel,
        out_shape=[jax.ShapeDtypeStruct((tokens, width), F32), jax.ShapeDtypeStruct((tokens, width), BF16)],
        compiler_params=params(),
        cost_estimate=cost(2 * tokens * width * width, 5e6),
        name="middle",
    )(attn, wo, x, gain)


def own_row(table, row):
    return jnp.sum(jnp.where(row_iota(table.shape) == row, table, 0.0), 0, keepdims=True)


def one_hot(slots, first, number, capp):
    tokens = slots.shape[1]
    order = row_iota((capp, tokens)).astype(F32)
    return [(order == own_row(slots, first + j)).astype(F32) for j in range(number)]


def gather_kernel(number, capp, first_ref, h_ref, cx_ref, wrt_ref, x_ref, g_ref, gate_ref):
    tokens = h_ref.shape[1]
    first = first_ref[0]
    h = h_ref[0]
    slots = cx_ref[0, tokens:, :tokens].astype(F32)
    logits = dot(wrt_ref[...], h, NT)[:EXPERTS, :]
    raw = jnp.exp(logits - jnp.max(logits, 0, keepdims=True))
    router = raw / jnp.sum(raw, 0, keepdims=True)
    hots = one_hot(slots, first, number, capp)
    places = jnp.concatenate(hots, 0).astype(BF16)
    rows = dot(places, h).astype(BF16)
    grads = dot(places, cx_ref[0, :tokens, :]).astype(BF16)
    for j in range(number):
        at = slice(j * capp, (j + 1) * capp)
        x_ref[j, 0] = rows[at]
        g_ref[j, 0] = grads[at]
        gate = jnp.sum(hots[j] * own_row(router, first + j), 1, keepdims=True)
        gate_ref[j, 0] = jnp.broadcast_to(gate, (capp, 128))


def gather_rows(first, hs, cxs, wrt, number, capp):
    nb, tokens, width = hs.shape
    return pl.pallas_call(
        functools.partial(gather_kernel, number, capp),
        grid_spec=pltpu.PrefetchScalarGridSpec(
            num_scalar_prefetch=1,
            grid=(nb,),
            in_specs=[
                pl.BlockSpec((1, tokens, width), lambda b, f: (b, 0, 0)),
                pl.BlockSpec((1, tokens + EXPERTS, width), lambda b, f: (b, 0, 0)),
                pl.BlockSpec(wrt.shape, lambda b, f: (0, 0)),
            ],
            out_specs=[
                pl.BlockSpec((number, 1, capp, width), lambda b, f: (0, b, 0, 0)),
                pl.BlockSpec((number, 1, capp, width), lambda b, f: (0, b, 0, 0)),
                pl.BlockSpec((number, 1, capp, 128), lambda b, f: (0, b, 0, 0)),
            ],
        ),
        out_shape=[
            jax.ShapeDtypeStruct((number, nb, capp, width), BF16),
            jax.ShapeDtypeStruct((number, nb, capp, width), BF16),
            jax.ShapeDtypeStruct((number, nb, capp, 128), F32),
        ],
        compiler_params=params(),
        cost_estimate=cost(4 * nb * number * capp * tokens * width, 2e7),
        name="gather_rows",
    )(first, hs, cxs, wrt)


PIECE = 512


def expert_kernel(base_ref, x_ref, g_ref, gate_ref, wg_ref, wu_ref, wd_ref, piece_ref, out_ref, rows_ref, dg_ref):
    x = x_ref[0]
    gate = gate_ref[0][:, :1]
    grad_ffn = RESIDUAL * g_ref[0].astype(F32)
    go = (gate * grad_ffn).astype(BF16)
    part = wg_ref.shape[2] // 2
    out = rows = None
    for chunk in range(2):
        at = slice(chunk * part, (chunk + 1) * part)
        wg, wu, wd = wg_ref[0, :, at], wu_ref[0, :, at], wd_ref[0, at, :]
        pre_gate = dot(x, wg)
        pre_up = dot(x, wu)
        sig = jax.nn.sigmoid(pre_gate)
        hidden = (pre_gate * sig * pre_up).astype(BF16)
        out_part = dot(hidden, wd)
        grad_hidden = dot(go, wd, NT)
        grad_gate = (grad_hidden * pre_up * sig * (1.0 + pre_gate * (1.0 - sig))).astype(BF16)
        grad_up = (grad_hidden * pre_gate * sig).astype(BF16)
        row_part = dot(grad_gate, wg, NT) + dot(grad_up, wu, NT)
        dwg = dot(x, grad_gate, TN).astype(BF16)
        dwu = dot(x, grad_up, TN).astype(BF16)
        dwd = dot(hidden, go, TN).astype(BF16)
        for half in range(2):
            side = slice(half * PIECE, (half + 1) * PIECE)
            piece_ref[0, 3 * chunk + half, :, :part] = dwg[side]
            piece_ref[0, 3 * chunk + half, :, part:] = dwu[side]
            piece_ref[0, 3 * chunk + 2, half * part : (half + 1) * part, :] = dwd[:, side]
        out = out_part if out is None else out + out_part
        rows = row_part if rows is None else rows + row_part
    out = out.astype(BF16).astype(F32)
    out_ref[0] = (gate * out).astype(BF16)
    rows_ref[0] = rows.astype(BF16)
    grad = jnp.sum(grad_ffn * out, 1, keepdims=True)
    dg_ref[0] = jnp.broadcast_to(grad, dg_ref.shape[1:])


def expert_step(base, xs, gs, gates, w_gate, w_up, w_down):
    number, rows, width = xs.shape
    ff = w_gate.shape[2]
    row = lambda e, b: (e, 0, 0)
    weight = lambda e, b: (b[0] + e, 0, 0)
    return pl.pallas_call(
        expert_kernel,
        grid_spec=pltpu.PrefetchScalarGridSpec(
            num_scalar_prefetch=1,
            grid=(number,),
            in_specs=[
                pl.BlockSpec((1, rows, width), row),
                pl.BlockSpec((1, rows, width), row),
                pl.BlockSpec((1, rows, 128), row),
                pl.BlockSpec((1, width, ff), weight),
                pl.BlockSpec((1, width, ff), weight),
                pl.BlockSpec((1, ff, width), weight),
            ],
            out_specs=[
                pl.BlockSpec((1, 6, PIECE, PIECE), lambda e, b: (e, 0, 0, 0)),
                pl.BlockSpec((1, rows, width), row),
                pl.BlockSpec((1, rows, width), row),
                pl.BlockSpec((1, rows, 128), row),
            ],
        ),
        out_shape=[
            jax.ShapeDtypeStruct((number, 6, PIECE, PIECE), BF16),
            jax.ShapeDtypeStruct((number, rows, width), BF16),
            jax.ShapeDtypeStruct((number, rows, width), BF16),
            jax.ShapeDtypeStruct((number, rows, 128), F32),
        ],
        compiler_params=params(60),
        cost_estimate=cost(18 * number * rows * width * ff, 5e7),
        name="expert_step",
    )(base, xs, gs, gates, w_gate, w_up, w_down)


def combine_kernel(number, capp, first_ref, slot_ref, outs, rows, grads, y_ref, gx_ref):
    tokens = y_ref.shape[1]
    width = y_ref.shape[2]
    first = first_ref[0]
    slots = slot_ref[0][:, :tokens].astype(F32)
    hots = one_hot(slots, first, number, capp)
    places = jnp.concatenate(hots, 0).astype(BF16)
    y_ref[0] = dot(places, outs[:, 0].reshape(number * capp, width), TN).astype(BF16)
    gx_ref[0, :tokens] = dot(places, rows[:, 0].reshape(number * capp, width), TN).astype(BF16)
    extra = jnp.zeros((EXPERTS, 2 * tokens), F32)
    for j in range(number):
        grad = jnp.sum(hots[j] * grads[j, 0][:, :1], 0, keepdims=True)
        high = grad.astype(BF16).astype(F32)
        both = jnp.concatenate([high, grad - high], 1)
        extra = jnp.where(row_iota(extra.shape) == first + j, both, extra)
    rest = jnp.zeros((EXPERTS, width - 2 * tokens), F32)
    gx_ref[0, tokens:] = jnp.concatenate([extra, rest], 1).astype(BF16)


def combine(first, slots, outs, rows, grads, tokens, capp):
    number = outs.shape[0]
    nb, _, width = slots.shape
    split = lambda a: a.reshape(number, nb, capp, a.shape[-1])
    wide = pl.BlockSpec((number, 1, capp, width), lambda b, f: (0, b, 0, 0))
    thin = pl.BlockSpec((number, 1, capp, 128), lambda b, f: (0, b, 0, 0))
    return pl.pallas_call(
        functools.partial(combine_kernel, number, capp),
        grid_spec=pltpu.PrefetchScalarGridSpec(
            num_scalar_prefetch=1,
            grid=(nb,),
            in_specs=[pl.BlockSpec((1, EXPERTS, width), lambda b, f: (b, 0, 0))] + [wide, wide, thin],
            out_specs=[
                pl.BlockSpec((1, tokens, width), lambda b, f: (b, 0, 0)),
                pl.BlockSpec((1, tokens + EXPERTS, width), lambda b, f: (b, 0, 0)),
            ],
        ),
        out_shape=[
            jax.ShapeDtypeStruct((nb, tokens, width), BF16),
            jax.ShapeDtypeStruct((nb, tokens + EXPERTS, width), BF16),
        ],
        compiler_params=params(),
        cost_estimate=cost(4 * nb * number * capp * tokens * width, 2e7),
        name="combine",
    )(first, slots, split(outs), split(rows), split(grads))


def home_kernel(gx_ref, h_ref, middle_ref, cot_ref, wr_ref, wo_ref, gain_ref, attn_ref, grad_middle_ref, dwo_ref, ga_ref, dwr_ref, dgain_ref):
    tokens, width = h_ref.shape
    h = h_ref[...]
    gain = gain_ref[...]
    extra = gx_ref[tokens:, :].astype(F32)
    grad_router = extra[:, :tokens] + extra[:, tokens : 2 * tokens]
    grad_router = jnp.transpose(jnp.concatenate([grad_router, jnp.zeros((128 - EXPERTS, tokens), F32)], 0))
    logits = dot(h, wr_ref[...])
    logits = jnp.where(lane_iota(logits.shape) < EXPERTS, logits, MASKED)
    raw = jnp.exp(logits - jnp.max(logits, -1, keepdims=True))
    router = raw / jnp.sum(raw, -1, keepdims=True)
    grad_logits = (router * (grad_router - jnp.sum(router * grad_router, -1, keepdims=True))).astype(BF16)
    dwr_ref[...] = dot(h, grad_logits, TN).astype(BF16)
    grad_h = gx_ref[:tokens, :].astype(F32) + dot(grad_logits, wr_ref[...], NT)
    normed, scale = norm_parts(middle_ref[...])
    dgain_ref[...] = jnp.sum(grad_h * normed, 0, keepdims=True)
    grad_middle = cot_ref[...] + norm_back(grad_h * gain, normed, scale)
    grad_middle_ref[...] = grad_middle
    grad_branch = (RESIDUAL * grad_middle).astype(BF16)
    for c in range(attn_ref.shape[0]):
        dwo_ref[c] = dot(attn_ref[c], grad_branch, TN).astype(BF16)
        ga_ref[c] = dot(grad_branch, wo_ref[c], NT).astype(BF16)


def home_step(gx, h, middle, cot, wr, wo, gain, attn):
    tokens, width = h.shape
    n = attn.shape[0]
    return pl.pallas_call(
        home_kernel,
        out_shape=[
            jax.ShapeDtypeStruct((tokens, width), F32),
            jax.ShapeDtypeStruct((n, 128, width), BF16),
            jax.ShapeDtypeStruct((n, tokens, 128), BF16),
            jax.ShapeDtypeStruct((width, 128), BF16),
            jax.ShapeDtypeStruct((1, width), F32),
        ],
        compiler_params=params(),
        cost_estimate=cost(4 * tokens * width * width, 1e7),
        name="home_step",
    )(gx, h, middle, cot, wr, wo, gain, attn)


def final_kernel(shard, grads_ref, w_ref, h_ref, x_ref, gain_ref, grad_middle_ref, dw_ref, grad_x_ref, dgain_ref, total):
    c = pl.program_id(0)
    g = grads_ref[0]
    dw_ref[...] = dot(h_ref[...], g, TN).astype(BF16)

    @pl.when(c == 0)
    def _():
        total[...] = jnp.zeros_like(total)

    for f in range(w_ref.shape[0]):
        total[:, f * shard : (f + 1) * shard] += dot(g, w_ref[f, :shard, :], NT)

    @pl.when(c == pl.num_programs(0) - 1)
    def _():
        normed, scale = norm_parts(x_ref[...])
        grad_h = total[...]
        dgain_ref[...] = jnp.sum(grad_h * normed, 0, keepdims=True)
        grad_x_ref[...] = grad_middle_ref[...] + norm_back(grad_h * gain_ref[...], normed, scale)


def final_step(grads, weights, h, x, gain, grad_middle, shard):
    n, tokens, _ = grads.shape
    width = x.shape[1]
    fsdp, padded, _ = weights.shape
    same = lambda c: (0, 0)
    return pl.pallas_call(
        functools.partial(final_kernel, shard),
        grid=(n,),
        in_specs=[
            pl.BlockSpec((1, tokens, PACK), lambda c: (c, 0, 0)),
            pl.BlockSpec((fsdp, padded, PACK), lambda c: (0, 0, c)),
            pl.BlockSpec((tokens, width), same),
            pl.BlockSpec((tokens, width), same),
            pl.BlockSpec((1, width), same),
            pl.BlockSpec((tokens, width), same),
        ],
        out_specs=[
            pl.BlockSpec((width, PACK), lambda c: (0, c)),
            pl.BlockSpec((tokens, width), same),
            pl.BlockSpec((1, width), same),
        ],
        out_shape=[
            jax.ShapeDtypeStruct((width, n * PACK), BF16),
            jax.ShapeDtypeStruct((tokens, width), F32),
            jax.ShapeDtypeStruct((1, width), F32),
        ],
        scratch_shapes=[pltpu.VMEM((tokens, width), F32)],
        compiler_params=params(),
        cost_estimate=cost(4 * tokens * width * n * PACK, 1.2e7),
        name="final_step",
    )(grads, weights, h, x, gain, grad_middle)


def widen_kernel(number, index_ref, own_ref, other_ref, gate_ref, up_ref, down_ref):
    part = gate_ref.shape[2] // 2

    def write(ref):
        for chunk in range(2):
            columns = slice(chunk * part, (chunk + 1) * part)
            for half in range(2):
                at = slice(half * PIECE, (half + 1) * PIECE)
                gate_ref[0, at, columns] = ref[3 * chunk + half, :, :part].astype(F32)
                up_ref[0, at, columns] = ref[3 * chunk + half, :, part:].astype(F32)
                down_ref[0, columns, at] = ref[3 * chunk + 2, half * part : (half + 1) * part, :].astype(F32)

    @pl.when(pl.program_id(0) == 0)
    def _():
        write(own_ref)

    @pl.when(pl.program_id(0) == 1)
    def _():
        write(other_ref)


def tail_kernel(number, index_ref, own_ref, other_ref, own_small_ref, other_small_ref, mixed_in, grad_in, gate_ref, up_ref, down_ref, mixed_ref, grad_ref, dwq_ref, dwk_ref, dwv_ref, dwo_ref, dwr_ref, g1_ref, g2_ref):
    widen_kernel(number, index_ref, own_ref, other_ref, gate_ref, up_ref, down_ref)
    mixed_ref[...] = mixed_in[...]
    grad_ref[...] = grad_in[...]

    @pl.when((pl.program_id(0) == 0) & (pl.program_id(1) == 0))
    def _():
        for which, ref in enumerate((own_small_ref, other_small_ref)):
            part = index_ref[which] // number
            at = pl.ds(pl.multiple_of(part * 128, 128), 128)
            for q in range(4):
                block = ref[1, q * 128 : (q + 1) * 128, :].astype(F32)
                dwq_ref[at, q * 256 : q * 256 + 128] = block[:, :128]
                dwq_ref[at, q * 256 + 128 : (q + 1) * 256] = block[:, 256:384]
                one, two = block[:, 128:256], block[:, 384:]
                low = lane_iota(one.shape) < HEAD_DIMENSION
                dwk_ref[at, q * 128 : (q + 1) * 128] = jnp.where(low, one, pltpu.roll(two, 64, 1))
                dwv_ref[at, q * 128 : (q + 1) * 128] = jnp.where(low, pltpu.roll(one, 64, 1), two)
            dwo_ref[at, :PIECE] = ref[0, 0:128, :].astype(F32)
            dwo_ref[at, PIECE:] = ref[0, 128:256, :].astype(F32)
            dwr_ref[:, at] = jnp.transpose(ref[0, 256:384, :128].astype(F32))[:EXPERTS]
            gains = ref[0, 384:400, :128].astype(F32)
            g1_ref[pl.ds(part, 1), :] = gains[0:1]
            g2_ref[pl.ds(part, 1), :] = gains[1:2]


def expert_specs(number, shapes):
    last = number - 1
    ins = [
        pl.BlockSpec((6, PIECE, PIECE), lambda s, e, at: (jnp.where(s == 0, e, last), 0, 0)),
        pl.BlockSpec((6, PIECE, PIECE), lambda s, e, at: (jnp.where(s == 0, 0, e), 0, 0)),
    ]
    outs = [pl.BlockSpec((1,) + tuple(shape[1:]), lambda s, e, at: (at[s] + e, 0, 0)) for shape in shapes]
    return ins, outs, [jax.ShapeDtypeStruct(shape, F32) for shape in shapes]


def widen(index, own, other, shapes):
    number = shapes[0][0] // 2
    ins, outs, out_shapes = expert_specs(number, shapes)
    return pl.pallas_call(
        functools.partial(widen_kernel, number),
        grid_spec=pltpu.PrefetchScalarGridSpec(num_scalar_prefetch=1, grid=(2, number), in_specs=ins, out_specs=outs),
        out_shape=out_shapes,
        compiler_params=params(),
        cost_estimate=cost(0, 1e8),
        name="widen",
    )(index, own, other)


def tail(index, own, other, mixed, grad_x, shapes, shard):
    number = shapes[0][0] // 2
    tokens, width = mixed.shape
    ins, outs, out_shapes = expert_specs(number, shapes)
    small = pl.BlockSpec((2, PIECE, PIECE), lambda s, e, at: (3 * number, 0, 0))
    rows = pl.BlockSpec((tokens // (2 * number), width), lambda s, e, at: (s * number + e, 0))
    small_shapes = [(shard, width), (shard, width // 2), (shard, width // 2), (shard, width), (EXPERTS, shard), (2, 128), (2, 128)]
    whole = [pl.BlockSpec(shape, lambda s, e, at: (0, 0)) for shape in small_shapes]
    return pl.pallas_call(
        functools.partial(tail_kernel, number),
        grid_spec=pltpu.PrefetchScalarGridSpec(
            num_scalar_prefetch=1,
            grid=(2, number),
            in_specs=ins + [small, small, rows, rows],
            out_specs=outs + [rows, rows] + whole,
        ),
        out_shape=out_shapes
        + [jax.ShapeDtypeStruct((tokens, width), F32)] * 2
        + [jax.ShapeDtypeStruct(shape, F32) for shape in small_shapes],
        compiler_params=params(),
        cost_estimate=cost(0, 1e8),
        name="tail",
    )(index, own, other, own, other, mixed, grad_x)


def swap(value, axis, bit):
    size = lax.axis_size(axis)
    return lax.ppermute(value, axis, [(i, i ^ bit) for i in range(size)])


def group_bits(fsdp):
    bits = [("fsdp", 1 << b) for b in range(1, fsdp.bit_length() - 1)]
    return bits + [("ctx", 1), ("fsdp", 1)]


def group_gather(value, bits):
    stacked = value[None]
    for axis, bit in bits:
        stacked = jnp.concatenate([stacked, swap(stacked, axis, bit)], 0)
    return stacked


def group_reduce(stacked, bits):
    for axis, bit in reversed(bits):
        half = stacked.shape[0] // 2
        arrived = swap(stacked[half:], axis, bit)
        stacked = (stacked[:half].astype(F32) + arrived.astype(F32)).astype(stacked.dtype)
    return stacked[0]


def line_sum(value, ctx):
    pairs = ctx // 2
    if pairs != 4:
        bit = 2
        while bit < ctx:
            value = value + swap(value, "ctx", bit)
            bit *= 2
        return value
    at = lambda z, y: 2 * z + y
    inward = [(at(0, y), at(1, y)) for y in range(2)] + [(at(3, y), at(2, y)) for y in range(2)]
    across = [(at(1, y), at(2, y)) for y in range(2)] + [(at(2, y), at(1, y)) for y in range(2)]
    outward = [(b, a) for a, b in inward]
    value = value + lax.ppermute(value, "ctx", inward)
    value = value + lax.ppermute(value, "ctx", across)
    arrived = lax.ppermute(value, "ctx", outward)
    z = lax.axis_index("ctx") // 2
    return jnp.where((z == 0) | (z == 3), arrived, value)


MESH = pl.DeviceIdType.MESH


def flip(index, bit):
    return jnp.where((index // bit) % 2 == 0, index + bit, index - bit)


def send(src, dst, send_sem, recv_sem, device):
    return pltpu.make_async_remote_copy(src_ref=src, dst_ref=dst, send_sem=send_sem, recv_sem=recv_sem, device_id=device, device_id_type=MESH)


def neighbours():
    ctx, fsdp = lax.axis_index("ctx"), lax.axis_index("fsdp")
    side, across = flip(ctx, 1), flip(fsdp, 2)
    core = {"fsdp": flip(fsdp, 1)}
    return core, [{"fsdp": across}, {"ctx": side}, {"ctx": side, "fsdp": across}]


def greet(devices):
    barrier = pltpu.get_barrier_semaphore()
    for device in devices:
        pl.semaphore_signal(barrier, inc=1, device_id=device, device_id_type=MESH)
    pl.semaphore_wait(barrier, len(devices))


def others(n):
    ctx = lax.axis_index("ctx")
    return [lax.rem(ctx + d, n) for d in range(1, n)]


def exchange_start(src, dst, send_sems, recv_sems, local_sem, n):
    ctx = lax.axis_index("ctx")
    for d, c in enumerate(others(n)):
        send(src.at[c], dst.at[ctx], send_sems.at[d], recv_sems.at[d], {"ctx": c}).start()
    pltpu.make_async_copy(src.at[ctx], dst.at[ctx], local_sem).start()


def exchange_wait(src, dst, send_sems, recv_sems, local_sem, n, arrived=None):
    ctx = lax.axis_index("ctx")
    pltpu.make_async_copy(src.at[ctx], dst.at[ctx], local_sem).wait()
    if arrived is not None:
        arrived(ctx)
    for d in range(n - 1):
        source = lax.rem(ctx + n - 1 - d, n)
        send(src.at[source], dst.at[source], send_sems.at[d], recv_sems.at[d], {"ctx": source}).wait_recv()
        if arrived is not None:
            arrived(source)
    for d, c in enumerate(others(n)):
        send(src.at[c], dst.at[ctx], send_sems.at[d], recv_sems.at[d], {"ctx": c}).wait_send()


def turn_half(v, table, direction, lanes_turned):
    lanes = lane_iota(v.shape)
    swapped = jnp.where(lanes % HEAD_DIMENSION < HEAD_DIMENSION // 2, pltpu.roll(v, 96, 1), pltpu.roll(v, 32, 1))
    return jnp.where(lanes < lanes_turned, v * table[:, :128] + direction * (swapped * table[:, 128:]), v)


def front_kernel(n, cap, wq_ref, wk_ref, wv_ref, wo_part_ref, wr_raw_ref, gain_ref, x_ref, table_ref, routes_ref, cot_ref, packs_ref, h_ref, weights_ref, wo_ref, wr_ref, cxs_ref, gains_ref, wall, packed_ref, wr_part_ref, cx, table, normed_ref, total, out, exch_send, exch_recv, full_send, full_recv, x_send, x_recv, y_send, y_recv, xs_send, xs_recv, ys_send, ys_recv, cx_send, cx_recv, local_sems):
    tokens, width = x_ref.shape
    shard = width // 4
    ctx, fsdp = lax.axis_index("ctx"), lax.axis_index("fsdp")
    parity = lax.rem(ctx, 2)
    core, group = neighbours()
    far, near = group[0], group[1]
    sibling, distant = flip(fsdp, 1), flip(fsdp, 2)
    other = flip(distant, 1)
    for k in range(2):
        pltpu.make_async_copy(table_ref.at[k, ctx], table.at[k], local_sems.at[6 + k]).start()

    pair = HEAD_DIMENSION * 2
    for c in range(0, n, 2):
        keys, values = wk_ref[:, c // 2 * pair : (c // 2 + 1) * pair].astype(F32), wv_ref[:, c // 2 * pair : (c // 2 + 1) * pair].astype(F32)
        low = lane_iota(keys.shape) < HEAD_DIMENSION
        packed_ref[0, :shard, c * 128 : (c + 1) * 128] = jnp.where(low, keys, pltpu.roll(values, 64, 1)).astype(BF16)
        packed_ref[0, :shard, (c + 1) * 128 : (c + 2) * 128] = jnp.where(low, pltpu.roll(keys, 64, 1), values).astype(BF16)
    below = packed_ref.shape[1] - shard
    packed_ref[0, shard:, :] = jnp.zeros((below, width), BF16)
    row = row_iota((16, shard))
    gains = gain_ref[...].astype(F32)
    gain_rows = jnp.where(row == 0, gains[0:1], jnp.where(row == 1, gains[1:2], 0.0))
    packed_ref[0, shard : shard + 16, :shard] = gain_rows.astype(BF16)
    packed_ref[1, :shard, :] = wq_ref[...]
    packed_ref[1, shard:, :] = jnp.zeros((below, width), BF16)
    router = jnp.concatenate([wr_raw_ref[...].astype(F32), jnp.zeros((128 - EXPERTS, shard), F32)], 0)
    wr_part_ref[...] = jnp.transpose(router).astype(BF16)
    greet([core, far] + [{"ctx": c} for c in others(n)])

    half_rows = packed_ref.shape[1] // 2

    def cut(k, part):
        if k < 2:
            return pl.ds(pl.multiple_of(part * half_rows, 16), half_rows)
        if k == 2:
            return pl.ds(part, 1)
        return pl.ds(pl.multiple_of(part * (shard // 2), 16), shard // 2)

    sources = [packed_ref.at[0], packed_ref.at[1], wo_part_ref, wr_part_ref]
    targets = [wall.at[0], wall.at[1], wo_ref, wr_ref]

    def whole(k):
        return send(sources[k], targets[k].at[fsdp], full_send.at[k], full_recv.at[k], core)

    def own(k):
        return pltpu.make_async_copy(sources[k], targets[k].at[fsdp], local_sems.at[k])

    def to_far(k):
        return send(sources[k].at[cut(k, parity)], targets[k].at[fsdp, cut(k, parity)], x_send.at[k], x_recv.at[k], far)

    def pass_on(k, part, sems, device):
        ref = targets[k].at[distant, cut(k, part)]
        return send(ref, ref, sems[0].at[k], sems[1].at[k], device)

    def sibling_arrived(k):
        ref = targets[k].at[sibling]
        send(ref, ref, full_send.at[k], full_recv.at[k], core).wait_recv()

    def far_arrived(k):
        ref = targets[k].at[distant, cut(k, parity)]
        send(ref, ref, x_send.at[k], x_recv.at[k], far).wait_recv()
        pass_on(k, parity, (y_send, y_recv), near).start()
        pass_on(k, parity, (xs_send, xs_recv), core).start()

    def near_arrived(k):
        pass_on(k, 1 - parity, (y_send, y_recv), near).wait_recv()
        pass_on(k, 1 - parity, (ys_send, ys_recv), core).start()

    def core_arrived(k):
        for part, sems in ((parity, (xs_send, xs_recv)), (1 - parity, (ys_send, ys_recv))):
            ref = targets[k].at[other, cut(k, part)]
            send(ref, ref, sems[0].at[k], sems[1].at[k], core).wait_recv()

    for k in range(2):
        to_far(k).start()
    for k in range(2):
        whole(k).start()
        own(k).start()

    prep_kernel(cap, routes_ref, cot_ref, cx)
    pltpu.make_async_copy(cx, cxs_ref.at[0], local_sems.at[4]).start()
    normed, _ = norm_parts(x_ref[...])
    normed_ref[...] = normed

    def project(k, block, begin):
        at = pl.ds(pl.multiple_of(block * shard, shard), shard)
        if k == 0:
            gain = wall[0, block, shard : shard + 16, :shard].astype(F32)
            gains_ref[:, at] = gain
            h_ref[:, at] = (normed_ref[:, at] * gain[:1]).astype(BF16)
        part = dot(h_ref[:, at], wall[k, block, :shard, :])
        total[k] = part if begin else total[k] + part

    for k in range(2):
        own(k).wait()
        project(k, fsdp, True)
        sibling_arrived(k)
        project(k, sibling, False)
        if k == 0:
            far_arrived(0)

    exchanges = []

    def emit(k):
        lanes = slice(128, 256) if k == 0 else slice(0, 128)
        for c in range(n):
            out[c, :, lanes] = turn_half(total[k, :, c * 128 : (c + 1) * 128], angles, 1.0, 64 if k == 0 else 128).astype(BF16)
        cut_lanes = pl.ds(128 if k == 0 else 0, 128)
        source, target = out.at[:, :, cut_lanes], packs_ref.at[:, :, cut_lanes]
        exchanges.append((source, target, exch_send.at[k], exch_recv.at[k], local_sems.at[8 + k], n))
        exchange_start(*exchanges[-1])

    near_arrived(0)
    project(0, distant, False)
    core_arrived(0)
    project(0, other, False)
    for k in range(2):
        pltpu.make_async_copy(table_ref.at[k, ctx], table.at[k], local_sems.at[6 + k]).wait()
    angles = table[...].reshape(tokens, 256)
    emit(0)
    far_arrived(1)
    for k in (2, 3):
        own(k).start()
        whole(k).start()
        to_far(k).start()
    send(cx, cxs_ref.at[1], cx_send.at[0], cx_recv.at[0], far).start()
    near_arrived(1)
    project(1, distant, False)
    core_arrived(1)
    project(1, other, False)
    emit(1)
    keep = pltpu.make_async_copy(wall, weights_ref, local_sems.at[5])
    keep.start()
    for k in (2, 3):
        far_arrived(k)
    for k in (2, 3):
        near_arrived(k)
    for k in (2, 3):
        core_arrived(k)
        sibling_arrived(k)
        own(k).wait()
    for exchange in exchanges:
        exchange_wait(*exchange)
    for k in range(4):
        whole(k).wait_send()
        to_far(k).wait_send()
        pass_on(k, parity, (y_send, y_recv), near).wait_send()
        pass_on(k, parity, (xs_send, xs_recv), core).wait_send()
        pass_on(k, 1 - parity, (ys_send, ys_recv), core).wait_send()
    send(cx, cxs_ref.at[1], cx_send.at[0], cx_recv.at[0], far).wait()
    pltpu.make_async_copy(cx, cxs_ref.at[0], local_sems.at[4]).wait()
    keep.wait()


def front(wq, wk, wv, wo_part, wr, gains, x, table, routes, cot, cap, n):
    tokens, width = x.shape
    shard = wq.shape[0]
    hbm, vmem = pl.BlockSpec(memory_space=pl.ANY), pl.BlockSpec(memory_space=pltpu.VMEM)
    dma = lambda *k: pltpu.SemaphoreType.DMA(k)
    shaped = lambda shape, dtype=BF16: jax.ShapeDtypeStruct(shape, dtype)
    cx_shape = (tokens + EXPERTS, width)
    padded = 2 * 16 * (shard // 32 + 1)
    return pl.pallas_call(
        functools.partial(front_kernel, n, cap),
        in_specs=[vmem, vmem, vmem, hbm, vmem, vmem, vmem, hbm, vmem, vmem],
        out_specs=[hbm, vmem, hbm, hbm, hbm, hbm, vmem],
        out_shape=[
            shaped((n, tokens, PACK)),
            shaped((tokens, width)),
            shaped((2, 4, padded, width)),
            shaped((4,) + wo_part.shape),
            shaped((4, shard, 128)),
            shaped((2,) + cx_shape),
            shaped((16, width), F32),
        ],
        scratch_shapes=[
            pltpu.VMEM((2, 4, padded, width), BF16),
            pltpu.VMEM((2, padded, width), BF16),
            pltpu.VMEM((shard, 128), BF16),
            pltpu.VMEM(cx_shape, BF16),
            pltpu.VMEM((2, tokens // 2, 256), F32),
            pltpu.VMEM((tokens, width), F32),
            pltpu.VMEM((2, tokens, width), F32),
            pltpu.VMEM((n, tokens, PACK), BF16),
            dma(2, n - 1),
            dma(2, n - 1),
        ]
        + [dma(4)] * 10
        + [dma(1), dma(1), dma(10)],
        compiler_params=params(collective_id=1, has_side_effects=True),
        cost_estimate=cost(2e9, 5e7),
        name="front",
    )(wq, wk, wv, wo_part, wr, gains, x, table, routes, cot)


def attend_kernel(length, n, ends_ref, q_ref, pack_ref, cxs_ref, out_ref, lse_ref, full_ref, rest_ref, keys, values_t, acc, near_send, near_recv, core_send, core_recv):
    block = pl.program_id(0)
    core, group = neighbours()
    near = group[1]

    def to_near():
        return send(cxs_ref.at[0], rest_ref.at[0], near_send.at[0], near_recv.at[0], near)

    def to_core(i):
        src = cxs_ref.at[i] if i < 2 else rest_ref.at[0]
        return send(src, rest_ref.at[1 + i], core_send.at[i], core_recv.at[i], core)

    @pl.when(block == 0)
    def _():
        greet([core, near])
        to_near().start()
        for i in range(2):
            to_core(i).start()

    attn_forward_kernel(length, ends_ref, q_ref, pack_ref, out_ref, lse_ref, full_ref, keys, values_t, acc)

    @pl.when(block == pl.num_programs(0) - 2)
    def _():
        to_near().wait_recv()
        to_core(2).start()

    @pl.when(block == pl.num_programs(0) - 1)
    def _():
        for i in range(3):
            to_core(i).wait()
        to_near().wait_send()


def attend(ends, packs, cxs, length):
    n, _, rows, _ = packs.shape
    blocks, per = length // BLK, BLK // rows
    per_half = blocks // 2
    tiles = lambda i: (lax.rem(i, per_half), i // per_half, 0, 0)
    hbm = pl.BlockSpec(memory_space=pl.ANY)
    dma = lambda k: pltpu.SemaphoreType.DMA((k,))
    return pl.pallas_call(
        functools.partial(attend_kernel, length, n),
        grid=(blocks,),
        in_specs=[
            pl.BlockSpec(memory_space=pltpu.SMEM),
            pl.BlockSpec((per, 1, rows, PACK), tiles),
            pl.BlockSpec(packs.shape, lambda i: (0, 0, 0, 0)),
            hbm,
        ],
        out_specs=[
            pl.BlockSpec((per, 1, rows, 128), tiles),
            pl.BlockSpec((1, 1, 2 * BLK), lambda i: (i, 0, 0)),
            pl.BlockSpec((1, 128, 2 * BLK), lambda i: (i, 0, 0)),
            hbm,
        ],
        scratch_shapes=[
            pltpu.VMEM((length, 128), BF16),
            pltpu.VMEM((128, length), BF16),
            pltpu.VMEM((128, 2 * BLK), F32),
            dma(1),
            dma(1),
            dma(3),
            dma(3),
        ],
        out_shape=[
            jax.ShapeDtypeStruct((n, 2, rows, 128), BF16),
            jax.ShapeDtypeStruct((blocks, 1, 2 * BLK), F32),
            jax.ShapeDtypeStruct((blocks, 128, 2 * BLK), F32),
            jax.ShapeDtypeStruct((4,) + cxs.shape[1:], BF16),
        ],
        compiler_params=params(collective_id=3, has_side_effects=True),
        cost_estimate=cost(1.5e10, 2e7),
        name="attend",
    )(ends, packs, packs, cxs)


def mid_kernel(n, number, capp, attn_ref, cxs_ref, rest_ref, wo_hbm, wr_ref, x_hbm, gain_ref, middle_ref, h_ref, kept_ref, xs_ref, gs_ref, gates_ref, diag_ref, arrived, hs, wo_ref, x_ref, cx, rows_out, grads_out, gates_out, exch_send, exch_recv, hop_send, hop_recv, cross_send, cross_recv, cx_send, cx_recv, fwd_send, fwd_recv, local_sems, load_sems, store_sems):
    tokens, width = x_ref.shape
    split = tokens // 2
    ctx, fsdp = lax.axis_index("ctx"), lax.axis_index("fsdp")
    first = (fsdp * 2 + lax.rem(ctx, 2)) * number
    core, group = neighbours()
    copies = [pltpu.make_async_copy(wo_hbm, wo_ref, local_sems.at[2]), pltpu.make_async_copy(x_hbm, x_ref, local_sems.at[3])]
    for copy in copies:
        copy.start()
    order = (0, 4, 1, 2, 3, 5, 6, 7)

    def load(step):
        refs = (cxs_ref.at[0], cxs_ref.at[1], rest_ref.at[0], diag_ref.at[0], rest_ref.at[1], rest_ref.at[2], rest_ref.at[3], diag_ref.at[1])
        return pltpu.make_async_copy(refs[order[step]], cx.at[step % 2], load_sems.at[step % 2])

    cx_half = cxs_ref.shape[1] // 2

    def cx_cross(i):
        at = pl.ds(i * cx_half, cx_half)
        src = cxs_ref.at[1, at] if i == 0 else rest_ref.at[0, at]
        return send(src, diag_ref.at[0, at], cx_send.at[i], cx_recv.at[i], group[1 - i])

    def cx_core():
        return send(diag_ref.at[0], diag_ref.at[1], cx_send.at[2], cx_recv.at[2], core)

    load(0).start()
    greet([core, group[0]] + [{"ctx": c} for c in others(n)])
    for i in range(2):
        cx_cross(i).start()
    halves = [pl.ds(k * split, split) for k in range(2)]
    exchanges = [(attn_ref.at[:, halves[k]], arrived.at[:, halves[k]], exch_send.at[k], exch_recv.at[k], local_sems.at[4 + k], n) for k in range(2)]
    for exchange in exchanges:
        exchange_start(*exchange)
    for copy in copies:
        copy.wait()

    def hop(i, k):
        return send(hs.at[0, halves[k]], hs.at[(1, 2, 4)[i], halves[k]], hop_send.at[i, k], hop_recv.at[i, k], (group[0], group[1], core)[i])

    def cross(i):
        return send(hs.at[1 + i, halves[i]], hs.at[3, halves[i]], cross_send.at[i], cross_recv.at[i], group[1 - i])

    def forward(i):
        return send(hs.at[1 + i], hs.at[5 + i], fwd_send.at[i], fwd_recv.at[i], core)

    for k in range(2):
        exchange_wait(*exchanges[k])
        at = slice(k * split, (k + 1) * split)
        total = None
        for c in range(n):
            part = dot(arrived[c, at, :], wo_ref[c])
            total = part if total is None else total + part
        middle = x_ref[at, :] + RESIDUAL * total
        middle_ref[at, :] = middle
        normed, _ = norm_parts(middle)
        h = (normed * gain_ref[1:2]).astype(BF16)
        h_ref[at, :] = h
        hs[0, at, :] = h
        for i in range(3):
            hop(i, k).start()
        if k == 0:
            for i in range(2):
                cx_cross(i).wait_recv()
            cx_core().start()
    keep = pltpu.make_async_copy(arrived, kept_ref, local_sems.at[1])
    keep.start()

    def stores(step):
        b = order[step]
        pairs = ((rows_out, xs_ref), (grads_out, gs_ref), (gates_out, gates_ref))
        return [pltpu.make_async_copy(src.at[step % 2], dst.at[:, b], store_sems.at[step % 2, k]) for k, (src, dst) in enumerate(pairs)]

    def place(step):
        b, slot = order[step], step % 2
        load(step).wait()
        if step >= 2:
            for copy in stores(step - 2):
                copy.wait()
        h = hs[b]
        logits = jnp.transpose(dot(h, wr_ref[...]))[:EXPERTS, :]
        raw = jnp.exp(logits - jnp.max(logits, 0, keepdims=True))
        router = raw / jnp.sum(raw, 0, keepdims=True)
        slots = cx[slot, tokens:, :tokens].astype(F32)
        hots = one_hot(slots, first, number, capp)
        places = jnp.concatenate(hots, 0).astype(BF16)
        rows = dot(places, h).astype(BF16)
        grads = dot(places, cx[slot, :tokens, :]).astype(BF16)
        for j in range(number):
            at = slice(j * capp, (j + 1) * capp)
            rows_out[slot, j] = rows[at]
            grads_out[slot, j] = grads[at]
            gate = jnp.sum(hots[j] * own_row(router, first + j), 1, keepdims=True)
            gates_out[slot, j] = jnp.broadcast_to(gate, (capp, 128))
        for copy in stores(step):
            copy.start()
        if step + 2 < 8:
            if step + 2 == 7:
                cx_core().wait_recv()
            load(step + 2).start()

    load(1).start()
    place(0)
    for k in range(2):
        hop(2, k).wait_recv()
    place(1)
    hop(0, 0).wait_recv()
    cross(0).start()
    hop(1, 0).wait_recv()
    hop(1, 1).wait_recv()
    cross(1).start()
    forward(1).start()
    hop(0, 1).wait_recv()
    forward(0).start()
    place(2)
    place(3)
    for i in range(2):
        cross(i).wait_recv()
    forward(2).start()
    place(4)
    for i in range(3):
        forward(i).wait_recv()
        place(5 + i)
    for step in (6, 7):
        for copy in stores(step):
            copy.wait()
    for i in range(2):
        cross(i).wait_send()
        cx_cross(i).wait_send()
    cx_core().wait_send()
    for i in range(3):
        for k in range(2):
            hop(i, k).wait_send()
        forward(i).wait_send()
    keep.wait()


def mid_step(attn, cxs, rest, wo, wr, x, gains, number, capp, n):
    tokens, width = x.shape
    hbm, vmem = pl.BlockSpec(memory_space=pl.ANY), pl.BlockSpec(memory_space=pltpu.VMEM)
    dma = lambda *k: pltpu.SemaphoreType.DMA(k)
    shaped = lambda shape, dtype=BF16: jax.ShapeDtypeStruct(shape, dtype)
    return pl.pallas_call(
        functools.partial(mid_kernel, n, number, capp),
        in_specs=[hbm, hbm, hbm, hbm, vmem, hbm, vmem],
        out_specs=[vmem, vmem, hbm, hbm, hbm, hbm, hbm],
        out_shape=[
            shaped((tokens, width), F32),
            shaped((tokens, width)),
            shaped(attn.shape),
            shaped((number, 8, capp, width)),
            shaped((number, 8, capp, width)),
            shaped((number, 8, capp, 128), F32),
            shaped((2,) + cxs.shape[1:]),
        ],
        scratch_shapes=[
            pltpu.VMEM(attn.shape, BF16),
            pltpu.VMEM((8, tokens, width), BF16),
            pltpu.VMEM(wo.shape, BF16),
            pltpu.VMEM((tokens, width), F32),
            pltpu.VMEM((2,) + cxs.shape[1:], BF16),
            pltpu.VMEM((2, number, capp, width), BF16),
            pltpu.VMEM((2, number, capp, width), BF16),
            pltpu.VMEM((2, number, capp, 128), F32),
            dma(2, n - 1),
            dma(2, n - 1),
            dma(3, 2),
            dma(3, 2),
            dma(2),
            dma(2),
            dma(3),
            dma(3),
            dma(3),
            dma(3),
            dma(6),
            dma(2),
            dma(2, 3),
        ],
        compiler_params=params(collective_id=2, has_side_effects=True),
        cost_estimate=cost(4e9, 5e7),
        name="mid_step",
    )(attn, cxs, rest, wo, wr, x, gains)


RING = 12
LAG_MIDDLE, LAG_ACROSS, LAG_END = 1, 2, 4
ORDER_X, ORDER_Y, ORDER_CORE = 1, 2, 4


class GroupSum:
    def __init__(self, part, rows, lands, own, sems, load, free, first, core, group):
        self.part, self.rows, self.own, self.load, self.free, self.first = part, rows, own, load, free, first
        self.land, self.land_x, self.land_y = lands
        self.core_send, self.core_recv, self.x_send, self.x_recv, self.y_send, self.y_recv = sems
        self.core, self.far, self.near = core, group[0], group[1]

    def place(self, i):
        return self.land.at[i, pl.ds(0, self.rows)]

    def ready(self, which):
        if not self.first:
            pl.semaphore_wait(self.free.at[which], 1)

    def to_core(self, i):
        return send(self.part.at[4 + i], self.place(i), self.core_send.at[i], self.core_recv.at[i], self.core)

    def to_far(self, k):
        return send(self.place(1 + 2 * k), self.land_x.at[k, pl.ds(0, self.rows)], self.x_send.at[k], self.x_recv.at[k], self.far)

    def to_near(self):
        return send(self.place(2), self.land_y.at[pl.ds(0, self.rows)], self.y_send.at[0], self.y_recv.at[0], self.near)

    def fetch(self, i):
        return pltpu.make_async_copy(self.part.at[i], self.own.at[i % 2, pl.ds(0, self.rows)], self.load.at[i % 2])

    def start(self):
        self.ready(0)
        for i in (1, 3, 2, 0):
            self.to_core(i).start()

    def over_cores(self):
        order = (1, 3, 2, 0)
        if self.own is not None:
            self.fetch(1).start()
        for step, i in enumerate(order):
            if self.own is None:
                mine = self.part[i]
            else:
                self.fetch(i).wait()
                mine = self.own[i % 2, : self.rows]
            self.to_core(i).wait_recv()
            self.land[i, : self.rows] = (self.land[i, : self.rows].astype(F32) + mine.astype(F32)).astype(BF16)
            if self.own is not None and step < 3:
                self.fetch(order[step + 1]).start()
            if i % 2 == 1:
                if step == 0:
                    self.ready(1)
                self.to_far(i // 2).start()

    def over_x(self, between=None):
        for k in (1, 0):
            if k == 0 and between is not None:
                between()
            self.to_far(k).wait_recv()
            both = self.land[2 * k, : self.rows].astype(F32) + self.land_x[k, : self.rows].astype(F32)
            self.land[2 * k, : self.rows] = both.astype(BF16)
            if k == 1:
                self.ready(2)
                self.to_near().start()

    def finish(self):
        self.to_near().wait_recv()
        for i in range(4):
            self.to_core(i).wait_send()
        for k in range(2):
            self.to_far(k).wait_send()
        self.to_near().wait_send()
        return self.land[0, : self.rows].astype(F32) + self.land_y[: self.rows].astype(F32)

    def release(self):
        for which, device in enumerate((self.core, self.far, self.near)):
            pl.semaphore_signal(self.free.at[which], inc=1, device_id=device, device_id_type=MESH)


class LineSum:
    def __init__(self, count, own_ref, other_ref, inbox, across, mine, sems):
        self.count, self.own_ref, self.other_ref = count, own_ref, other_ref
        self.inbox, self.across, self.mine = inbox, across, mine
        self.line_send, self.line_recv, self.mid_send, self.mid_recv, self.side_send, self.side_recv, self.store, self.load = sems
        ctx = lax.axis_index("ctx")
        z = ctx // 2
        self.middle = (z == 1) | (z == 2)
        self.line = {"ctx": jnp.where(z % 2 == 0, ctx + 2, ctx - 2)}
        self.peer = {"ctx": jnp.where(z == 1, ctx + 2, ctx - 2)}
        self.side = {"ctx": flip(ctx, 1)}

    def send_line(self, src, i):
        s = lax.rem(i, RING)
        return send(src, self.inbox.at[s], self.line_send.at[s], self.line_recv.at[s], self.line)

    def send_mid(self, i):
        s = lax.rem(i, RING)
        return send(self.inbox.at[s], self.across.at[s], self.mid_send.at[s], self.mid_recv.at[s], self.peer)

    def send_side(self, src, i):
        return send(src, self.other_ref.at[i], self.side_send.at[lax.rem(i, RING)], self.side_recv.at[i], self.side)

    def keep(self, src, i):
        return pltpu.make_async_copy(src, self.own_ref.at[i], self.store.at[lax.rem(i, RING)])

    def fetch(self, src, i):
        s = lax.rem(i, 4)
        return pltpu.make_async_copy(src, self.mine.at[s], self.load.at[s])

    def drain_middle(self, i):
        src = self.across.at[lax.rem(i, RING)]
        self.send_line(src, i).wait_send()
        self.send_side(src, i).wait_send()
        self.keep(src, i).wait()

    def drain_end(self, i):
        src = self.inbox.at[lax.rem(i, RING)]
        self.send_side(src, i).wait_send()
        self.keep(src, i).wait()

    def tick(self, t, source):
        count = self.count
        fixed = isinstance(t, int)

        def when(condition):
            if fixed:
                return (lambda f: f()) if condition else (lambda f: None)
            return pl.when(condition)

        i32 = (lambda v: jnp.int32(v)) if fixed else (lambda v: v)

        @pl.when(self.middle)
        def _():
            @when((t >= LAG_MIDDLE) & (t < count + LAG_MIDDLE))
            def _():
                i = i32(t - LAG_MIDDLE)

                @when(t >= LAG_ACROSS + 4)
                def _():
                    self.drain_middle(i32(t - LAG_ACROSS - 4))

                s = lax.rem(i, RING)
                self.fetch(self.own_ref.at[i], i).wait()
                self.send_line(self.inbox.at[s], i).wait_recv()
                self.inbox[s] = self.inbox[s] + self.mine[lax.rem(i, 4)]
                self.send_mid(i).start()

            @when(t < count)
            def _():
                self.fetch(source(t), i32(t)).start()

            @when((t >= LAG_ACROSS) & (t < count + LAG_ACROSS))
            def _():
                i = i32(t - LAG_ACROSS)
                s = lax.rem(i, RING)
                self.send_mid(i).wait()
                self.across[s] = self.across[s] + self.inbox[s]
                self.send_line(self.across.at[s], i).start()
                self.send_side(self.across.at[s], i).start()
                self.keep(self.across.at[s], i).start()

        @pl.when(jnp.logical_not(self.middle))
        def _():
            @when(t < count)
            def _():
                @when(t >= LAG_END + 2)
                def _():
                    self.drain_end(i32(t - LAG_END - 2))

                @when(t >= 3)
                def _():
                    self.send_line(self.mine.at[0], i32(t - 3)).wait_send()

                self.send_line(source(t), i32(t)).start()

            @when(t >= LAG_END)
            def _():
                i = i32(t - LAG_END)
                s = lax.rem(i, RING)
                self.send_line(self.inbox.at[s], i).wait_recv()
                self.send_side(self.inbox.at[s], i).start()
                self.keep(self.inbox.at[s], i).start()

    def finish(self):
        count = self.count

        @pl.when(self.middle)
        def _():
            for i in range(count + LAG_MIDDLE - LAG_ACROSS - 4, count):
                self.drain_middle(jnp.int32(i))

        @pl.when(jnp.logical_not(self.middle))
        def _():
            for i in range(count - 3, count):
                self.send_line(self.mine.at[0], jnp.int32(i)).wait_send()
            for i in range(count - LAG_END - 2, count):
                self.drain_end(jnp.int32(i))

        def arrived(i, carry):
            self.send_side(self.mine.at[0], i).wait_recv()
            return carry

        lax.fori_loop(0, count, arrived, 0)


def backward_kernel(
    n,
    length,
    capp,
    ends_ref,
    xs_ref,
    gs_ref,
    gates_ref,
    wg_ref,
    wu_ref,
    wd_ref,
    cxs_ref,
    rest_ref,
    diag_ref,
    full_ref,
    weights_ref,
    packs_hbm,
    table_hbm,
    cot_hbm,
    wo_hbm,
    attn_hbm,
    x_hbm,
    h_attn_hbm,
    h_ref,
    middle_ref,
    wr_ref,
    gains_ref,
    lse_ref,
    own_ref,
    other_ref,
    pieces_ref,
    outs_ref,
    backs_ref,
    gx_ref,
    yp_ref,
    grad_x_ref,
    mixed_ref,
    inbox,
    across,
    mine,
    land,
    land_x,
    land_y,
    y_land,
    y_land_x,
    y_land_y,
    own_buf,
    late_pieces,
    ga_in,
    grads_in,
    line_send,
    line_recv,
    mid_send,
    mid_recv,
    side_send,
    side_recv,
    line_store,
    line_load,
    ga_send,
    ga_recv,
    gr_send,
    gr_recv,
    group_sems,
    group_load,
    free,
    local_sems,
    full_sems,
    w_sems,
    load_sems,
    store_sems,
    comb_sems,
    part_sems,
):
    tokens, width = h_ref.shape
    half = length // 2
    rows = tokens // 2
    shard = width // 4
    blocks = length // BLK
    number = xs_ref.shape[0]
    ff = wg_ref.shape[2]
    ctx, fsdp = lax.axis_index("ctx"), lax.axis_index("fsdp")
    side = lax.rem(ctx, 2)
    first = (fsdp * 2 + side) * number
    core, group = neighbours()
    sub = own_ref.shape[1]
    cuts = PIECE // sub
    early = number * 6 * cuts
    line = LineSum(early + 2 * cuts, own_ref, other_ref, inbox, across, mine, (line_send, line_recv, mid_send, mid_recv, side_send, side_recv, line_store, line_load))

    def source(t):
        return pieces_ref.at[t // cuts, pl.ds(pl.multiple_of(lax.rem(t, cuts) * sub, sub), sub)]

    def tick(t):
        line.tick(jnp.int32(t) if isinstance(t, int) else t, source)

    sems = lambda k: [group_sems.at[k, j] for j in range(6)]
    lands = (land, land_x, land_y)
    ext = tokens + EXPERTS
    gx = GroupSum(gx_ref, 2 * ext, lands, None, sems(0), None, free, True, core, group)
    ys = GroupSum(yp_ref, 2 * tokens, (y_land, y_land_x, y_land_y), own_buf, sems(1), group_load, free, True, core, group)

    def strip(r):
        f = fsdp
        if r & ORDER_X:
            f = flip(f, 2)
        if r & ORDER_CORE:
            f = flip(f, 1)
        return 2 * f + (1 - side if r & ORDER_Y else side)

    def experts(wg, wu, wd, xb, gb, gateb, stage, out_acc, back_acc, outb, backb, go, dgate, comb_o, comb_b, gst, yst, slots):
        def loads(e):
            s = lax.rem(e, 2)
            at = side * number + e
            pairs = ((wg_ref.at[at], wg), (wu_ref.at[at], wu), (wd_ref.at[at], wd), (xs_ref.at[e], xb), (gs_ref.at[e], gb), (gates_ref.at[e], gateb))
            return [pltpu.make_async_copy(src, dst.at[s], load_sems.at[s, k]) for k, (src, dst) in enumerate(pairs)]

        def slot_copy(b):
            refs = (cxs_ref.at[0], cxs_ref.at[1], rest_ref.at[0], diag_ref.at[0], rest_ref.at[1], rest_ref.at[2], rest_ref.at[3], diag_ref.at[1])
            return pltpu.make_async_copy(refs[b].at[pl.ds(tokens, EXPERTS), pl.ds(0, tokens)], slots.at[b], part_sems.at[0, b])

        def stores(e):
            pairs = (
                (stage.at[pl.ds(0, 3)], pieces_ref.at[pl.ds(6 * e, 3)]),
                (stage.at[pl.ds(3, 3)], pieces_ref.at[pl.ds(6 * e + 3, 3)]),
                (outb, outs_ref.at[e]),
                (backb, backs_ref.at[e]),
            )
            return [pltpu.make_async_copy(src, dst, store_sems.at[k]) for k, (src, dst) in enumerate(pairs)]

        for copy in loads(jnp.int32(0)):
            copy.start()
        for b in range(8):
            slot_copy(b).start()
        greet([core, group[0]] + [{"ctx": c} for c in others(n)])

        def one(e, carry):
            s = lax.rem(e, 2)

            @pl.when(e + 1 < number)
            def _():
                for copy in loads(e + 1):
                    copy.start()

            for copy in loads(e):
                copy.wait()

            @pl.when(e > 0)
            def _():
                for copy in stores(e - 1)[2:]:
                    copy.wait()

            x = xb[s]
            gate = gateb[s][:, :1]
            go[...] = (gate * (RESIDUAL * gb[s].astype(F32))).astype(BF16)
            part = ff // 2
            for chunk in range(2):
                at = slice(chunk * part, (chunk + 1) * part)
                wgc, wuc, wdc = wg[s, :, at], wu[s, :, at], wd[s, at, :]
                pre_gate = dot(x, wgc)
                pre_up = dot(x, wuc)
                sig = jax.nn.sigmoid(pre_gate)
                hidden = (pre_gate * sig * pre_up).astype(BF16)
                out_part = dot(hidden, wdc)
                grad_hidden = dot(go[...], wdc, NT)
                grad_gate = (grad_hidden * pre_up * sig * (1.0 + pre_gate * (1.0 - sig))).astype(BF16)
                grad_up = (grad_hidden * pre_gate * sig).astype(BF16)
                row_part = dot(grad_gate, wgc, NT) + dot(grad_up, wuc, NT)
                dwg = dot(x, grad_gate, TN).astype(BF16)
                dwu = dot(x, grad_up, TN).astype(BF16)
                dwd = dot(hidden, go[...], TN).astype(BF16)
                for k in range(2):
                    cut = slice(k * PIECE, (k + 1) * PIECE)
                    stage[3 * chunk + k, :, :part] = dwg[cut]
                    stage[3 * chunk + k, :, part:] = dwu[cut]
                    stage[3 * chunk + 2, k * part : (k + 1) * part, :] = dwd[:, cut]
                stores(e)[chunk].start()
                if chunk == 0:
                    out_acc[...] = out_part
                    back_acc[...] = row_part
                    stores(e)[0].wait()
                    tick(2 * e)
                else:
                    out = (out_acc[...] + out_part).astype(BF16).astype(F32)
                    outb[...] = (gate * out).astype(BF16)
                    backb[...] = (back_acc[...] + row_part).astype(BF16)
                    grad = jnp.sum(RESIDUAL * gb[s].astype(F32) * out, 1, keepdims=True)
                    dgate[e] = jnp.broadcast_to(grad, dgate.shape[1:])
            for copy in stores(e)[2:]:
                copy.start()
            stores(e)[1].wait()
            tick(2 * e + 1)
            return carry

        lax.fori_loop(0, number, one, 0)
        for copy in stores(jnp.int32(number - 1))[2:]:
            copy.wait()
        for b in range(8):
            slot_copy(b).wait()

        def which(s):
            k = lax.rem(s, 4)
            i = jnp.where(k == 0, 1, jnp.where(k == 1, 3, jnp.where(k == 2, 2, 0)))
            return jnp.where(s < 4, 4 + i, i), i

        def comb(s):
            k = lax.rem(s, 2)
            at = pl.ds(pl.multiple_of(which(s)[0] * capp, 16), capp)
            return [
                pltpu.make_async_copy(outs_ref.at[:, at], comb_o.at[k], comb_sems.at[0, k]),
                pltpu.make_async_copy(backs_ref.at[:, at], comb_b.at[k], comb_sems.at[1, k]),
            ]

        def put(s):
            k = lax.rem(s, 2)
            r, _ = which(s)
            return [
                pltpu.make_async_copy(gst.at[k], gx_ref.at[r], part_sems.at[1, k]),
                pltpu.make_async_copy(yst.at[k], yp_ref.at[r], part_sems.at[1, 2 + k]),
            ]

        for copy in comb(jnp.int32(0)):
            copy.start()

        def join(s, carry):
            k = lax.rem(s, 2)
            r, i = which(s)

            @pl.when(s + 1 < 8)
            def _():
                for copy in comb(s + 1):
                    copy.start()

            for copy in comb(s):
                copy.wait()

            @pl.when(s >= 2)
            def _():
                put(s - 2)[1].wait()

            hots = one_hot(slots[r].astype(F32), first, number, capp)
            places = jnp.concatenate(hots, 0).astype(BF16)
            y = dot(places, comb_o[k].reshape(number * capp, width), TN).astype(BF16)
            back = dot(places, comb_b[k].reshape(number * capp, width), TN).astype(BF16)
            extra = jnp.zeros((EXPERTS, 2 * tokens), F32)
            for j in range(number):
                grads = dgate[j, pl.ds(pl.multiple_of(r * capp, 16), capp), :][:, :1]
                grad = jnp.sum(hots[j] * grads, 0, keepdims=True)
                high = grad.astype(BF16).astype(F32)
                extra = jnp.where(row_iota(extra.shape) == first + j, jnp.concatenate([high, grad - high], 1), extra)
            for q in range(2):
                yst[k, q * tokens : (q + 1) * tokens, :] = y[:, q * PIECE : (q + 1) * PIECE]
                gst[k, q * ext : q * ext + tokens, :] = back[:, q * PIECE : (q + 1) * PIECE]
            gst[k, tokens:ext, :] = extra.astype(BF16)
            gst[k, ext + tokens :, :] = jnp.zeros((EXPERTS, PIECE), BF16)
            put(s)[1].start()

            @pl.when(s < 4)
            def _():
                put(s)[0].start()
                put(s)[0].wait()
                gx.to_core(i).start()

            @pl.when(s >= 4)
            def _():
                gx.to_core(i).wait_recv()
                land[i, : gx.rows] = (land[i, : gx.rows].astype(F32) + gst[k].astype(F32)).astype(BF16)

            @pl.when((s == 4) | (s == 5))
            def _():
                gx.to_far(s - 4).start()

            @pl.when(lax.rem(s, 2) == 1)
            def _():
                tick(2 * number + s // 2)

            return carry

        lax.fori_loop(0, 8, join, 0)
        for s in range(6, 8):
            put(jnp.int32(s))[1].wait()

    slots_rows = xs_ref.shape[1]
    pl.run_scoped(
        experts,
        pltpu.VMEM((2, width, ff), BF16),
        pltpu.VMEM((2, width, ff), BF16),
        pltpu.VMEM((2, ff, width), BF16),
        pltpu.VMEM((2, slots_rows, width), BF16),
        pltpu.VMEM((2, slots_rows, width), BF16),
        pltpu.VMEM((2, slots_rows, 128), F32),
        pltpu.VMEM((6, PIECE, PIECE), BF16),
        pltpu.VMEM((slots_rows, width), F32),
        pltpu.VMEM((slots_rows, width), F32),
        pltpu.VMEM((slots_rows, width), BF16),
        pltpu.VMEM((slots_rows, width), BF16),
        pltpu.VMEM((slots_rows, width), BF16),
        pltpu.VMEM((number, slots_rows, 128), F32),
        pltpu.VMEM((2, number, capp, width), BF16),
        pltpu.VMEM((2, number, capp, width), BF16),
        pltpu.VMEM((2, 2 * ext, PIECE), BF16),
        pltpu.VMEM((2, 2 * tokens, PIECE), BF16),
        pltpu.VMEM((8, EXPERTS, tokens), BF16),
    )
    at_tick = [2 * number + 4]

    def go_on(k=1):
        for _ in range(k):
            tick(at_tick[0])
            at_tick[0] += 1

    def backward(packs, table, keys, values, keys_t, grad_q, grad_k, grad_v, acc, full_buf, ga, pack_out, wbuf, total, grad_middle, dgain, col, small, columns, cot, wo, attn, x_in, h_attn):
        ws = GroupSum(small, PIECE, lands, None, sems(2), None, free, False, core, group)
        cs = GroupSum(columns, PIECE + 16, lands, None, sems(3), None, free, False, core, group)
        copies = [
            pltpu.make_async_copy(src, dst, local_sems.at[4 + k])
            for k, (src, dst) in enumerate(
                ((cot_hbm, cot), (wo_hbm, wo), (attn_hbm, attn), (packs_hbm, packs), (table_hbm, table), (x_hbm, x_in), (h_attn_hbm, h_attn))
            )
        ]
        for copy in copies:
            copy.start()
        small[:, PIECE // 2 : PIECE, :] = jnp.zeros((8, PIECE // 2, PIECE), BF16)
        columns[:, PIECE:, :] = jnp.zeros((8, 16, PIECE), BF16)
        go_on(2)
        gx.over_x(go_on)
        go_on(2)
        arrived = gx.finish()
        arrived = jnp.concatenate([arrived[:ext], arrived[ext:]], 1)
        gx.release()

        h = h_ref[...]
        gain = gains_ref[1:2]
        extra = arrived[tokens:, :]
        grad_router = extra[:, :tokens] + extra[:, tokens : 2 * tokens]
        grad_router = jnp.transpose(jnp.concatenate([grad_router, jnp.zeros((128 - EXPERTS, tokens), F32)], 0))
        logits = dot(h, wr_ref[...])
        logits = jnp.where(lane_iota(logits.shape) < EXPERTS, logits, MASKED)
        raw = jnp.exp(logits - jnp.max(logits, -1, keepdims=True))
        router = raw / jnp.sum(raw, -1, keepdims=True)
        grad_logits = (router * (grad_router - jnp.sum(router * grad_router, -1, keepdims=True))).astype(BF16)
        go_on()
        grad_h = arrived[:tokens, :] + dot(grad_logits, wr_ref[...], NT)
        normed, scale = norm_parts(middle_ref[...])
        dgain[1:2, :] = jnp.sum(grad_h * normed, 0, keepdims=True)
        for copy in copies[:3]:
            copy.wait()
        grad_mid = cot[...] + norm_back(grad_h * gain, normed, scale)
        grad_middle[...] = grad_mid
        grad_branch = (RESIDUAL * grad_mid).astype(BF16)
        for c in range(n):
            ga[c] = dot(grad_branch, wo[c], NT).astype(BF16)
        ga_exchange = (ga, ga_in, ga_send, ga_recv, local_sems.at[2], n)
        exchange_start(*ga_exchange)
        go_on()
        col[:, :128] = dot(h, grad_logits, TN).astype(BF16)
        for r in range(8):
            at = strip(r)
            dwo = dot(attn[at], grad_branch, TN).astype(BF16)
            small[r, 0:128, :] = dwo[:, :PIECE]
            small[r, 128:256, :] = dwo[:, PIECE:]
            small[r, 256:384, 0:128] = col[pl.ds(pl.multiple_of(at * 128, 128), 128), 0:128]
        ws.start()
        ys.start()
        go_on()
        copies[3].wait()
        for hh in range(2):
            for c in range(n):
                kk, vv = pair_keys(packs[c, hh, :, 128:256].astype(F32))
                at = hh * half + c * rows
                keys[at : at + rows, :] = kk.astype(BF16)
                values[at : at + rows, :] = vv.astype(BF16)
                keys_t[:, at : at + rows] = jnp.transpose(kk).astype(BF16)
        grad_k[...] = jnp.zeros_like(grad_k)
        grad_v[...] = jnp.zeros_like(grad_v)
        go_on()
        ws.over_cores()
        ys.over_cores()
        go_on()
        exchange_wait(*ga_exchange)

        per = BLK // rows
        per_half = blocks // 2

        def fetch_full(b):
            return pltpu.make_async_copy(full_ref.at[b], full_buf.at[lax.rem(b, 2)], full_sems.at[lax.rem(b, 2)])

        fetch_full(jnp.int32(0)).start()
        attend_tick = at_tick[0]

        def attend(block, carry):
            late = block // per_half
            c0 = lax.rem(block, per_half) * per
            q2 = jnp.concatenate([packs[c0 + k, late, :, :128] for k in range(per)], 0)
            q2 = stack_heads((q2.astype(F32) * ATTN_SCALE).astype(BF16))
            g2 = stack_heads(jnp.concatenate([ga_in[c0 + k, pl.ds(pl.multiple_of(late * rows, rows), rows), :] for k in range(per)], 0))
            position, start = query_rows(ends_ref, block, length)
            lse = lse_ref[block]
            shift = jnp.where(start > 0, MASKED, 0.0) - lse

            @pl.when(block + 1 < blocks)
            def _():
                fetch_full(block + 1).start()

            fetch_full(block).wait()
            delta = jnp.sum(jnp.transpose(g2.astype(F32)) * full_buf[lax.rem(block, 2)], 0, keepdims=True)
            acc[...] = jnp.zeros_like(acc)

            def body(kb, whole, carry):
                at = pl.multiple_of(kb * BLK, BLK)
                scores = dot(keys[pl.ds(at, BLK), :], q2, NT)
                if whole:
                    probs = jnp.exp(scores + shift)
                else:
                    where = key_position(kb, length)
                    probs = jnp.where((where <= position) & (where >= start), jnp.exp(scores - lse), 0.0)
                grad_probs = dot(values[pl.ds(at, BLK), :], g2, NT)
                grad_scores = (probs * (grad_probs - delta)).astype(BF16)
                acc[...] += dot(keys_t[:, pl.ds(at, BLK)], grad_scores)
                grad_k[pl.ds(at, BLK), :] += dot(grad_scores, q2)
                grad_v[pl.ds(at, BLK), :] += dot(probs.astype(BF16), g2)

                if not whole:

                    @pl.when((kb == block) & ((block == per_half) | (block == per_half + 1)))
                    def _():
                        tick(attend_tick + 2 + 2 * (block - per_half))

                return carry

            block_loop(block, per_half, body, 0)
            grad_q[pl.ds(pl.multiple_of(block * BLK, BLK), BLK), :] = fold_heads(jnp.transpose(acc[...]))

            @pl.when((block == 1) | (block >= 3))
            def _():
                past = block - per_half
                late_tick = jnp.where(past < 2, 3 + 2 * past, 4 + past)
                tick(attend_tick + jnp.where(block < per_half, block // 2, late_tick))

            return carry

        lax.fori_loop(0, blocks, attend, 0)
        at_tick[0] += blocks
        copies[4].wait()
        for c in range(n):
            for hh in range(2):
                at = slice(hh * half + c * rows, hh * half + (c + 1) * rows)
                kk = grad_k[at, :]
                vv = grad_v[at, :]
                kk = kk + pltpu.roll(kk, 64, 1)
                vv = vv + pltpu.roll(vv, 64, 1)
                both = jnp.where(lane_iota(kk.shape) < 64, kk, vv)
                package = jnp.concatenate([grad_q[at, :] * ATTN_SCALE, both], -1)
                pack_out[c, hh * rows : (hh + 1) * rows, :] = turn(package, table[at, :], -1.0).astype(BF16)
        gr_exchange = (pack_out, grads_in, gr_send, gr_recv, local_sems.at[3], n)
        exchange_start(*gr_exchange)

        def fetch_w(c):
            slot = lax.rem(c, 2)
            at = pl.ds(pl.multiple_of(c * 128, 128), 128)
            return [
                pltpu.make_async_copy(weights_ref.at[1 - k, :, :, at], wbuf.at[slot, :, :, pl.ds(128 * k, 128)], w_sems.at[slot, k])
                for k in range(2)
            ]

        for copy in fetch_w(jnp.int32(0)):
            copy.start()
        go_on()
        ws.over_x()
        ys.over_x()
        go_on(2)
        total[...] = jnp.zeros_like(total)
        late_pieces[:PIECE] = ws.finish().astype(BF16)
        ws.release()
        ffn = ys.finish()
        mixed_ref[...] = middle_ref[...] + RESIDUAL * jnp.concatenate([ffn[:tokens], ffn[tokens:]], 1)
        go_on(3)
        exchange_wait(*gr_exchange)
        copies[5].wait()
        copies[6].wait()

        columns_tick = at_tick[0]

        def finish_columns(c, carry):
            @pl.when(c + 1 < n)
            def _():
                for copy in fetch_w(c + 1):
                    copy.start()

            for copy in fetch_w(c):
                copy.wait()
            slot = lax.rem(c, 2)
            g = grads_in[c]
            col[...] = dot(h_attn[...], g, TN).astype(BF16)
            for r in range(8):
                at = pl.ds(pl.multiple_of(strip(r) * 128, 128), 128)
                columns[r, pl.ds(pl.multiple_of(c // 2 * 128, 128), 128), pl.ds(pl.multiple_of(lax.rem(c, 2) * PACK, PACK), PACK)] = col[at, :]
            for f in range(4):
                total[:, f * shard : (f + 1) * shard] += dot(g, wbuf[slot, f, :shard, :], NT)

            @pl.when(lax.rem(c, 4) == 3)
            def _():
                tick(columns_tick + c // 4)

            return carry

        lax.fori_loop(0, n, finish_columns, 0)
        at_tick[0] += n // 4
        normed, scale = norm_parts(x_in[...])
        grad_h = total[...]
        dgain[0:1, :] = jnp.sum(grad_h * normed, 0, keepdims=True)
        grad_x_ref[...] = grad_middle[...] + norm_back(grad_h * gains_ref[0:1], normed, scale)
        for r in range(8):
            at = pl.ds(pl.multiple_of(strip(r) * 128, 128), 128)
            row = row_iota((16, 128))
            both = jnp.where(row == 0, dgain[0:1, at], jnp.where(row == 1, dgain[1:2, at], 0.0))
            columns[r, PIECE:, 0:128] = both.astype(BF16)
        cs.start()
        go_on()
        cs.over_cores()
        go_on(3)
        cs.over_x(go_on)
        go_on(3)
        summed = cs.finish().astype(BF16)
        late_pieces[PIECE:] = summed[:PIECE]
        late_pieces[384:400] = summed[PIECE:]

    f32, bf = (lambda *shape: pltpu.VMEM(shape, F32)), (lambda *shape: pltpu.VMEM(shape, BF16))
    pl.run_scoped(
        backward,
        bf(*packs_hbm.shape),
        f32(*table_hbm.shape),
        bf(length, 128),
        bf(length, 128),
        bf(128, length),
        f32(length, 128),
        f32(length, 128),
        f32(length, 128),
        f32(128, 2 * BLK),
        f32(2, 128, 2 * BLK),
        bf(n, tokens, 128),
        bf(n, tokens, PACK),
        bf(2, 4, weights_ref.shape[2], PACK),
        f32(tokens, width),
        f32(tokens, width),
        f32(8, width),
        bf(width, PACK),
        bf(8, PIECE, PIECE),
        bf(8, PIECE + 16, PIECE),
        f32(tokens, width),
        bf(*wo_hbm.shape),
        bf(*attn_hbm.shape),
        f32(tokens, width),
        bf(tokens, width),
    )

    def rest(t, carry):
        tick(t)
        return carry

    lax.fori_loop(at_tick[0], early, rest, 0)

    def late_source(t):
        return late_pieces.at[pl.ds(pl.multiple_of((t - early) * sub, sub), sub)]

    def late(t, carry):
        line.tick(t, late_source)
        return carry

    lax.fori_loop(early, line.count + LAG_END, late, 0)
    line.finish()


def backward_step(ends, xs, gs, gates, w_gate, w_up, w_down, cxs, rest, diag, full, weights, packs, table, cot, wo, attn, x, h_attn, h, middle, wr, gains, lse, n, length, capp):
    tokens, width = x.shape
    number, slots_rows, _ = xs.shape
    hbm, vmem = pl.BlockSpec(memory_space=pl.ANY), pl.BlockSpec(memory_space=pltpu.VMEM)
    smem = pl.BlockSpec(memory_space=pltpu.SMEM)
    dma = lambda *k: pltpu.SemaphoreType.DMA(k)
    shaped = lambda shape, dtype=BF16: jax.ShapeDtypeStruct(shape, dtype)
    sub = PIECE // 2
    piece = (sub, PIECE)
    count = (number * 6 + 2) * 2
    land_rows = max(2 * (tokens + EXPERTS), PIECE + 16)
    return pl.pallas_call(
        functools.partial(backward_kernel, n, length, capp),
        in_specs=[smem] + [hbm] * 18 + [vmem] * 5,
        out_specs=[hbm] * 7 + [vmem, vmem],
        out_shape=[
            shaped((count,) + piece),
            shaped((count,) + piece),
            shaped((number * 6, PIECE, PIECE)),
            shaped(xs.shape),
            shaped(xs.shape),
            shaped((8, 2 * (tokens + EXPERTS), PIECE)),
            shaped((8, 2 * tokens, PIECE)),
            shaped((tokens, width), F32),
            shaped((tokens, width), F32),
        ],
        scratch_shapes=[
            pltpu.VMEM((RING,) + piece, BF16),
            pltpu.VMEM((RING,) + piece, BF16),
            pltpu.VMEM((4,) + piece, BF16),
            pltpu.VMEM((4, land_rows, PIECE), BF16),
            pltpu.VMEM((2, land_rows, PIECE), BF16),
            pltpu.VMEM((land_rows, PIECE), BF16),
            pltpu.VMEM((4, 2 * tokens, PIECE), BF16),
            pltpu.VMEM((2, 2 * tokens, PIECE), BF16),
            pltpu.VMEM((2 * tokens, PIECE), BF16),
            pltpu.VMEM((2, 2 * tokens, PIECE), BF16),
            pltpu.VMEM((2 * PIECE, PIECE), BF16),
            pltpu.VMEM((n, tokens, 128), BF16),
            pltpu.VMEM((n, tokens, PACK), BF16),
            dma(RING),
            dma(RING),
            dma(RING),
            dma(RING),
            dma(RING),
            dma(count),
            dma(RING),
            dma(4),
            dma(n - 1),
            dma(n - 1),
            dma(n - 1),
            dma(n - 1),
            dma(4, 6, 4),
            dma(2),
            pltpu.SemaphoreType.REGULAR((3,)),
            dma(11),
            dma(2),
            dma(2, 2),
            dma(2, 6),
            dma(4),
            dma(2, 2),
            dma(2, 8),
        ],
        compiler_params=params(63, collective_id=0, has_side_effects=True),
        cost_estimate=cost(6e10, 1e9),
        name="backward_step",
    )(ends, xs, gs, gates, w_gate, w_up, w_down, cxs, rest, diag, full, weights, packs, table, cot, wo, attn, x, h_attn, h, middle, wr, gains, lse)


def local(
    inputs,
    cotangent,
    doc_lengths,
    routes,
    attn_gain,
    ffn_gain,
    w_query,
    key_weight,
    value_weight,
    w_out,
    w_router,
    w_gate,
    w_up,
    w_down,
):
    rows = inputs.shape[2]
    width = inputs.shape[3]
    n = lax.axis_size("ctx")
    fsdp = lax.axis_size("fsdp")
    me, mine = lax.axis_index("ctx"), lax.axis_index("fsdp")
    tokens = 2 * rows
    length = tokens * n
    experts_here = w_gate.shape[0]
    number = experts_here // 2
    capacity = 5 * tokens * TOP // (4 * EXPERTS)
    capp = -(-capacity // 16) * 16
    shard = width // fsdp
    heads = QUERY_HEADS // n
    head_lanes = heads * HEAD_DIMENSION
    copies = n // KEY_VALUE_HEADS
    bits = group_bits(fsdp)

    x = inputs.reshape(tokens, width)
    cot = cotangent.reshape(tokens, width)
    side = me % 2
    base = (side * number).astype(jnp.int32).reshape(1)
    first = (mine * experts_here + side * number).astype(jnp.int32).reshape(1)
    index = jnp.stack([side * number, (1 - side) * number]).astype(jnp.int32)
    ends = doc_lengths
    table = jnp.asarray(rotary_table(length))

    out_part = w_out.reshape(shard // head_lanes, head_lanes, width)
    if head_lanes < 128:
        out_part = jnp.pad(out_part, ((0, 0), (0, 128 - head_lanes), (0, 0)))
    merge = lambda a: a.reshape(number, -1, a.shape[-1])

    if n == 8 and fsdp == 4:
        packs, h_attn, weights, wo, wr, cxs, gains = front(
            w_query,
            key_weight,
            value_weight,
            out_part,
            jnp.transpose(w_router),
            jnp.stack([attn_gain, ffn_gain]),
            x,
            table.reshape(2, n, rows, 256),
            jnp.transpose(routes[0], (0, 2, 1)),
            cot,
            capacity,
            n,
        )
        wo, wr = wo.reshape(n, 128, width), wr.reshape(width, 128)
        packs = packs.reshape(n, 2, rows, PACK)
        attn, lse, full, cx_rest = attend(ends, packs, cxs, length)
        middle, h_ffn, attn, xs, gs, gates, diag = mid_step(attn.reshape(n, tokens, 128), cxs, cx_rest, wo, wr, x, gains, number, capp, n)
        own, other, _, _, _, _, _, grad_x, mixed = backward_step(
            ends,
            merge(xs),
            merge(gs),
            merge(gates),
            w_gate,
            w_up,
            w_down,
            cxs,
            cx_rest,
            diag,
            full,
            weights,
            packs,
            table,
            cot,
            wo,
            attn,
            x,
            h_attn,
            h_ffn,
            middle,
            wr,
            gains,
            lse,
            n,
            length,
            capp,
        )
        own, other = own.reshape(-1, PIECE, PIECE), other.reshape(-1, PIECE, PIECE)
        shapes = [w.shape for w in (w_gate, w_up, w_down)]
        outs = tail(index, own, other, mixed, grad_x, shapes, shard)
        return (
            outs[3].reshape(inputs.shape),
            outs[4].reshape(inputs.shape),
            outs[10].reshape(shard),
            outs[11].reshape(shard),
            outs[5],
            outs[6],
            outs[7],
            outs[8],
            jnp.transpose(outs[9]),
            outs[0],
            outs[1],
            outs[2],
        )

    else:
        own_table = lax.dynamic_slice_in_dim(table.reshape(2, n, rows, 256), me, 1, 1).reshape(tokens, 256)
        query_part = w_query.reshape(shard, n, head_lanes)
        if head_lanes < 128:
            query_part = jnp.pad(query_part, ((0, 0), (0, 0), (0, 128 - head_lanes)))
        key_part = jnp.repeat(key_weight.reshape(shard, KEY_VALUE_HEADS, HEAD_DIMENSION), copies, 1)
        value_part = jnp.repeat(value_weight.reshape(shard, KEY_VALUE_HEADS, HEAD_DIMENSION), copies, 1)
        packed = jnp.concatenate([query_part, key_part, value_part], -1).reshape(shard, n * PACK)
        padding = 2 * 16 * (shard // 32 + 1) - shard
        gains = jnp.pad(jnp.stack([attn_gain, ffn_gain]), ((0, padding - 2), (0, n * PACK - shard)))
        packed = jnp.concatenate([packed, gains], 0)
        router_part = jnp.pad(w_router, ((0, 0), (0, 128 - EXPERTS)))
        weights = lax.all_gather(packed, "fsdp", axis=0)
        gain_one = weights[:, shard, :shard].reshape(1, width).astype(F32)
        gain_two = weights[:, shard + 1, :shard].reshape(1, width).astype(F32)
        wo = lax.all_gather(out_part, "fsdp", axis=0, tiled=True)
        wr = lax.all_gather(router_part, "fsdp", axis=0, tiled=True)
        cxs = group_gather(prep(jnp.transpose(routes[0], (0, 2, 1)), cot, capacity), bits)
        packs, h_attn = qkv(x, gain_one, weights, own_table, shard, n)
        packs = lax.all_to_all(packs, "ctx", split_axis=0, concat_axis=0, tiled=True).reshape(n, 2, rows, PACK)
        attn, lse, full = attn_forward(ends, packs, length)
        attn = lax.all_to_all(attn.reshape(n, tokens, 128), "ctx", split_axis=0, concat_axis=0, tiled=True)
        middle, h_ffn = middle_step(attn, wo, x, gain_two)
        xs, gs, gates = gather_rows(first, group_gather(h_ffn, bits), cxs, jnp.transpose(wr), number, capp)
        slots = cxs[:, tokens:]
    xs, gs, gates = merge(xs), merge(gs), merge(gates)
    pieces, outs, back, dgates = expert_step(base, xs, gs, gates, w_gate, w_up, w_down)
    y_part, gx_part = combine(first, slots, outs, back, dgates, tokens, capp)
    pieces = pieces.reshape(number * 6, PIECE, PIECE)
    gx = group_reduce(gx_part, bits)
    grad_middle, dwo, grad_attn, dwr, dgain_two = home_step(gx, h_ffn, middle, cot, wr, wo, gain_two, attn)
    grad_attn = lax.all_to_all(grad_attn, "ctx", split_axis=0, concat_axis=0, tiled=True).reshape(n, 2, rows, 128)
    grads = attn_backward(ends, packs, grad_attn, lse, full, table, length)
    grads = lax.all_to_all(grads.reshape(n, tokens, PACK), "ctx", split_axis=0, concat_axis=0, tiled=True)
    dw, grad_x, dgain_one = final_step(grads, weights, h_attn, x, gain_one, grad_middle, shard)
    mixed = middle + RESIDUAL * group_reduce(y_part, bits).astype(F32)
    own = line_sum(pieces, n)
    other = swap(own, "ctx", 1)
    scatter = lambda a: lax.psum(lax.psum_scatter(a, "fsdp", scatter_dimension=0, tiled=True), "ctx").astype(F32)
    dwo = scatter(dwo)[:, :head_lanes, :].reshape(shard, width)
    small = jnp.concatenate([dwr[:, :EXPERTS], dgain_two.reshape(width, 1).astype(BF16)], 1)
    small = scatter(jnp.pad(small, ((0, 0), (0, 127 - EXPERTS))))
    dwr, dgain_two = small[:, :EXPERTS], small[:, EXPERTS]
    dw = scatter(dw).reshape(shard, n, PACK)
    dgain_one = scatter(dgain_one.reshape(width).astype(BF16))

    outs = widen(index, own, other, [w.shape for w in (w_gate, w_up, w_down)])
    fold = lambda a: a.reshape(shard, KEY_VALUE_HEADS, copies, HEAD_DIMENSION).sum(2).reshape(shard, -1)
    return (
        mixed.reshape(inputs.shape),
        grad_x.reshape(inputs.shape),
        dgain_one,
        dgain_two,
        dw[:, :, :head_lanes].reshape(shard, -1),
        fold(dw[:, :, 128:192]),
        fold(dw[:, :, 192:256]),
        dwo,
        dwr,
        outs[0],
        outs[1],
        outs[2],
    )


def solution(mesh):
    tokens = P("fsdp", None, "ctx", None)
    one, two, three = P("fsdp"), P("fsdp", None), P("fsdp", None, None)
    return jax.shard_map(
        local,
        mesh=mesh,
        in_specs=(tokens, tokens, two, tokens, one, one, two, two, two, two, two, three, three, three),
        out_specs=(tokens, tokens, one, one, two, two, two, two, two, three, three, three),
        check_vma=False,
    )
```

```python
import functools

import jax
import jax.numpy as jnp
import numpy as np
from jax import lax
from jax.experimental import pallas as pl
from jax.experimental.pallas import tpu as pltpu
from jax.sharding import PartitionSpec as P

QUERY_HEADS = 16
KEY_VALUE_HEADS = 8
HEAD_DIMENSION = 64
EXPERTS = 32
TOP = 8

ATTN_SCALE = 0.015625
RESIDUAL = 0.22
NORM_EPS = 1e-06
ROPE_BASE = 10000.0
MASKED = -1e30

F32 = jnp.float32
BF16 = jnp.bfloat16
MIB = 1 << 20
NT = (((1,), (1,)), ((), ()))
TN = (((0,), (0,)), ((), ()))
BLK = 256
PACK = 256


def dot(a, b, dims=None):
    if dims is None:
        return jnp.dot(a, b, preferred_element_type=F32)
    return lax.dot_general(a, b, dims, preferred_element_type=F32)


def params(limit=56, **kw):
    return pltpu.CompilerParams(vmem_limit_bytes=limit * MIB, **kw)


def cost(flops, bytes_accessed):
    return pl.CostEstimate(flops=int(flops), bytes_accessed=int(bytes_accessed), transcendentals=0)


def lane_iota(shape):
    return lax.broadcasted_iota(jnp.int32, shape, len(shape) - 1)


def row_iota(shape):
    return lax.broadcasted_iota(jnp.int32, shape, len(shape) - 2)


def rotary_table(length):
    half = length // 2
    order = np.arange(half, dtype=np.float32)
    positions = np.concatenate([order, length - 1 - order]).astype(np.float32)
    m = np.arange(HEAD_DIMENSION // 2, dtype=np.float64)
    frequency = (ROPE_BASE ** (-2.0 * m / HEAD_DIMENSION)).astype(np.float32)
    angles = (positions[:, None] * frequency[None, :]).astype(np.float64)
    cosine, sine = np.cos(angles), np.sin(angles)
    cos_head = np.concatenate([cosine, cosine], -1)
    sin_head = np.concatenate([-sine, sine], -1)
    return np.concatenate([cos_head, cos_head, sin_head, sin_head], -1).astype(np.float32)


def turn(v, table, direction):
    lanes = lane_iota(v.shape)
    cosine = jnp.concatenate([table[:, :128], table[:, :128]], -1)
    sine = jnp.concatenate([table[:, 128:], table[:, 128:]], -1)
    turned = lanes < 3 * HEAD_DIMENSION
    swapped = jnp.where(lanes % HEAD_DIMENSION < HEAD_DIMENSION // 2, pltpu.roll(v, PACK - 32, 1), pltpu.roll(v, 32, 1))
    return jnp.where(turned, v * cosine + direction * (swapped * sine), v)


def norm_parts(values):
    inv_rms = lax.rsqrt(jnp.mean(values * values, -1, keepdims=True) + NORM_EPS)
    return values * inv_rms, inv_rms


def norm_back(grad_normed, normed, inv_rms):
    return inv_rms * (grad_normed - normed * jnp.mean(grad_normed * normed, -1, keepdims=True))


def prep_kernel(cap, routes_ref, cot_ref, out_ref):
    tokens, width = cot_ref.shape
    earlier = (row_iota((tokens, tokens)) < lane_iota((tokens, tokens))).astype(BF16)
    experts = row_iota((EXPERTS, tokens))
    base = jnp.zeros((EXPERTS, 1), F32)
    plus = jnp.zeros((EXPERTS, tokens), F32)
    for k in range(TOP):
        row = jnp.concatenate([routes_ref[0, k : k + 1, :], routes_ref[1, k : k + 1, :]], 1)
        chosen = experts == row
        ones = chosen.astype(F32)
        slot = dot(ones.astype(BF16), earlier) + base
        plus = plus + jnp.where(chosen & (slot < cap), slot + 1.0, 0.0)
        base = base + jnp.sum(ones, 1, keepdims=True)
    out_ref[:tokens, :] = cot_ref[...].astype(BF16)
    out_ref[tokens:, :] = jnp.concatenate([plus - 1.0, jnp.zeros((EXPERTS, width - tokens), F32)], -1).astype(BF16)


def prep(routes, cot, cap):
    tokens, width = cot.shape
    return pl.pallas_call(
        functools.partial(prep_kernel, cap),
        out_shape=jax.ShapeDtypeStruct((tokens + EXPERTS, width), BF16),
        compiler_params=params(),
        cost_estimate=cost(1e9, 2e6),
        name="prep",
    )(routes, cot)


def qkv_kernel(shard, x_ref, gain_ref, w_ref, table_ref, out_ref, h_ref):
    @pl.when(pl.program_id(0) == 0)
    def _():
        normed, _ = norm_parts(x_ref[...])
        h_ref[...] = (normed * gain_ref[...]).astype(BF16)

    total = None
    for f in range(w_ref.shape[0]):
        part = dot(h_ref[:, f * shard : (f + 1) * shard], w_ref[f, :shard, :])
        total = part if total is None else total + part
    for d in range(out_ref.shape[0]):
        out_ref[d] = turn(total[:, d * PACK : (d + 1) * PACK], table_ref[...], 1.0).astype(BF16)


def qkv(x, gain, weights, table, shard, n):
    tokens, width = x.shape
    fsdp, padded, _ = weights.shape
    return pl.pallas_call(
        functools.partial(qkv_kernel, shard),
        grid=(n // 2,),
        in_specs=[
            pl.BlockSpec((tokens, width), lambda i: (0, 0)),
            pl.BlockSpec((1, width), lambda i: (0, 0)),
            pl.BlockSpec((fsdp, padded, 2 * PACK), lambda i: (0, 0, i)),
            pl.BlockSpec((tokens, 256), lambda i: (0, 0)),
        ],
        out_specs=[
            pl.BlockSpec((2, tokens, PACK), lambda i: (i, 0, 0)),
            pl.BlockSpec((tokens, width), lambda i: (0, 0)),
        ],
        out_shape=[
            jax.ShapeDtypeStruct((n, tokens, PACK), BF16),
            jax.ShapeDtypeStruct((tokens, width), BF16),
        ],
        compiler_params=params(),
        cost_estimate=cost(2 * tokens * width * n * PACK, 8e6),
        name="qkv",
    )(x, gain, weights, table)


def pair_keys(kv):
    other = pltpu.roll(kv, 64, 1)
    low = lane_iota(kv.shape) < 64
    return jnp.where(low, kv, other), jnp.where(low, other, kv)


def stack_heads(q):
    low = lane_iota(q.shape) < 64
    zero = jnp.zeros_like(q)
    return jnp.concatenate([jnp.where(low, q, zero), jnp.where(low, zero, q)], 0)


def fold_heads(stacked):
    rows = stacked.shape[0] // 2
    return jnp.where(lane_iota((rows, 128)) < 64, stacked[:rows], stacked[rows:])


def query_rows(ends_ref, block, length):
    half = length // 2
    lanes = lane_iota((1, 2 * BLK))
    index = block * BLK + jnp.where(lanes < BLK, lanes, lanes - BLK)
    position = jnp.where(index < half, index, length + half - 1 - index)
    start = jnp.zeros_like(position)
    end = 0
    for j in range(3):
        end = end + ends_ref[0, j]
        start = jnp.where(position >= end, jnp.maximum(start, end), start)
    return position, start


def key_position(kb, length):
    half = length // 2
    index = kb * BLK + row_iota((BLK, 1))
    return jnp.where(index < half, index, length + half - 1 - index)


def block_loop(block, per_half, body, init):
    late = block >= per_half
    inner = jnp.where(late, block - per_half, block)

    def plain(kb, carry):
        return body(kb, True, carry)

    def masked(kb, carry):
        return body(kb, False, carry)

    carry = lax.fori_loop(0, jnp.where(late, per_half, inner), plain, init)
    return lax.fori_loop(block, jnp.where(late, 2 * per_half, block + 1), masked, carry)


def attn_forward_kernel(length, ends_ref, q_ref, pack_ref, out_ref, lse_ref, full_ref, keys, values_t, acc):
    block = pl.program_id(0)
    half = length // 2
    n, _, rows, _ = pack_ref.shape

    @pl.when(block == 0)
    def _():
        for h in range(2):
            for c in range(n):
                kk, vv = pair_keys(pack_ref[c, h, :, 128:256].astype(F32))
                at = h * half + c * rows
                keys[at : at + rows, :] = kk.astype(BF16)
                if rows % 128 == 0:
                    values_t[:, at : at + rows] = jnp.transpose(vv).astype(BF16)
        if rows % 128 != 0:
            for h in range(2):
                for c in range(0, n, 2):
                    pair = jnp.concatenate([pack_ref[c, h, :, 128:256], pack_ref[c + 1, h, :, 128:256]], 0)
                    _, vv = pair_keys(pair.astype(F32))
                    at = h * half + c * rows
                    values_t[:, at : at + 2 * rows] = jnp.transpose(vv).astype(BF16)

    q = q_ref[...].reshape(BLK, PACK)[:, :128]
    q2 = stack_heads((q.astype(F32) * ATTN_SCALE).astype(BF16))
    position, start = query_rows(ends_ref, block, length)
    bias = jnp.where(start > 0, MASKED, 0.0)
    acc[...] = jnp.zeros_like(acc)

    def body(kb, whole, carry):
        peak, total = carry
        at = pl.multiple_of(kb * BLK, BLK)
        scores = dot(keys[pl.ds(at, BLK), :], q2, NT)
        if whole:
            scores = scores + bias
        else:
            where = key_position(kb, length)
            scores = jnp.where((where <= position) & (where >= start), scores, MASKED)
        new_peak = jnp.maximum(peak, jnp.max(scores, 0, keepdims=True))
        weights = jnp.exp(scores - new_peak)
        fade = jnp.exp(peak - new_peak)
        total = total * fade + jnp.sum(weights, 0, keepdims=True)
        acc[...] = acc[...] * fade + dot(values_t[:, pl.ds(at, BLK)], weights.astype(BF16))
        return new_peak, total

    init = (jnp.full((1, 2 * BLK), MASKED, F32), jnp.zeros((1, 2 * BLK), F32))
    peak, total = block_loop(block, half // BLK, body, init)
    result = acc[...] / total
    full_ref[0] = result
    lse_ref[0] = peak + jnp.log(total)
    folded = fold_heads(jnp.transpose(result)).astype(BF16)
    out_ref[...] = folded.reshape(out_ref.shape)


def attn_forward(ends, packs, length):
    n, _, rows, _ = packs.shape
    blocks, per = length // BLK, BLK // rows
    per_half = blocks // 2
    tiles = lambda i, ends: (lax.rem(i, per_half), i // per_half, 0, 0)
    return pl.pallas_call(
        functools.partial(attn_forward_kernel, length),
        grid_spec=pltpu.PrefetchScalarGridSpec(
            num_scalar_prefetch=1,
            grid=(blocks,),
            in_specs=[
                pl.BlockSpec((per, 1, rows, PACK), tiles),
                pl.BlockSpec(packs.shape, lambda i, ends: (0, 0, 0, 0)),
            ],
            out_specs=[
                pl.BlockSpec((per, 1, rows, 128), tiles),
                pl.BlockSpec((1, 1, 2 * BLK), lambda i, ends: (i, 0, 0)),
                pl.BlockSpec((1, 128, 2 * BLK), lambda i, ends: (i, 0, 0)),
            ],
            scratch_shapes=[
                pltpu.VMEM((length, 128), BF16),
                pltpu.VMEM((128, length), BF16),
                pltpu.VMEM((128, 2 * BLK), F32),
            ],
        ),
        out_shape=[
            jax.ShapeDtypeStruct((n, 2, rows, 128), BF16),
            jax.ShapeDtypeStruct((blocks, 1, 2 * BLK), F32),
            jax.ShapeDtypeStruct((blocks, 128, 2 * BLK), F32),
        ],
        compiler_params=params(),
        cost_estimate=cost(1.5e10, 6e6),
        name="attn_forward",
    )(ends, packs, packs)


def attn_backward_kernel(length, ends_ref, q_ref, g_ref, pack_ref, lse_ref, full_ref, table_ref, out_ref, keys, values, keys_t, grad_q, grad_k, grad_v, acc):
    block = pl.program_id(0)
    half = length // 2
    n, _, rows, _ = pack_ref.shape

    @pl.when(block == 0)
    def _():
        for h in range(2):
            for c in range(n):
                kk, vv = pair_keys(pack_ref[c, h, :, 128:256].astype(F32))
                at = h * half + c * rows
                keys[at : at + rows, :] = kk.astype(BF16)
                values[at : at + rows, :] = vv.astype(BF16)
        for b in range(length // BLK):
            keys_t[:, b * BLK : (b + 1) * BLK] = jnp.transpose(keys[b * BLK : (b + 1) * BLK, :].astype(F32)).astype(BF16)
        grad_k[...] = jnp.zeros_like(grad_k)
        grad_v[...] = jnp.zeros_like(grad_v)

    q2 = stack_heads((q_ref[...].reshape(BLK, PACK)[:, :128].astype(F32) * ATTN_SCALE).astype(BF16))
    g2 = stack_heads(g_ref[...].reshape(BLK, 128))
    position, start = query_rows(ends_ref, block, length)
    lse = lse_ref[0]
    shift = jnp.where(start > 0, MASKED, 0.0) - lse
    delta = jnp.sum(jnp.transpose(g2.astype(F32)) * full_ref[0], 0, keepdims=True)
    acc[...] = jnp.zeros_like(acc)

    def body(kb, whole, carry):
        at = pl.multiple_of(kb * BLK, BLK)
        scores = dot(keys[pl.ds(at, BLK), :], q2, NT)
        if whole:
            probs = jnp.exp(scores + shift)
        else:
            where = key_position(kb, length)
            probs = jnp.where((where <= position) & (where >= start), jnp.exp(scores - lse), 0.0)
        grad_probs = dot(values[pl.ds(at, BLK), :], g2, NT)
        grad_scores = (probs * (grad_probs - delta)).astype(BF16)
        acc[...] += dot(keys_t[:, pl.ds(at, BLK)], grad_scores)
        grad_k[pl.ds(at, BLK), :] += dot(grad_scores, q2)
        grad_v[pl.ds(at, BLK), :] += dot(probs.astype(BF16), g2)
        return carry

    block_loop(block, half // BLK, body, 0)
    grad_q[pl.ds(pl.multiple_of(block * BLK, BLK), BLK), :] = fold_heads(jnp.transpose(acc[...]))

    @pl.when(block == length // BLK - 1)
    def _():
        for h in range(2):
            for c in range(n):
                at = slice(h * half + c * rows, h * half + (c + 1) * rows)
                kk = grad_k[at, :]
                vv = grad_v[at, :]
                kk = kk + pltpu.roll(kk, 64, 1)
                vv = vv + pltpu.roll(vv, 64, 1)
                both = jnp.where(lane_iota(kk.shape) < 64, kk, vv)
                package = jnp.concatenate([grad_q[at, :] * ATTN_SCALE, both], -1)
                out_ref[c, h] = turn(package, table_ref[at, :], -1.0).astype(BF16)


def attn_backward(ends, packs, grads, lse, full, table, length):
    n, _, rows, _ = packs.shape
    blocks, per = length // BLK, BLK // rows
    per_half = blocks // 2
    tiles = lambda i, ends: (lax.rem(i, per_half), i // per_half, 0, 0)
    return pl.pallas_call(
        functools.partial(attn_backward_kernel, length),
        grid_spec=pltpu.PrefetchScalarGridSpec(
            num_scalar_prefetch=1,
            grid=(blocks,),
            in_specs=[
                pl.BlockSpec((per, 1, rows, PACK), tiles),
                pl.BlockSpec((per, 1, rows, 128), tiles),
                pl.BlockSpec(packs.shape, lambda i, ends: (0, 0, 0, 0)),
                pl.BlockSpec((1, 1, 2 * BLK), lambda i, ends: (i, 0, 0)),
                pl.BlockSpec((1, 128, 2 * BLK), lambda i, ends: (i, 0, 0)),
                pl.BlockSpec(table.shape, lambda i, ends: (0, 0)),
            ],
            out_specs=pl.BlockSpec(packs.shape, lambda i, ends: (0, 0, 0, 0)),
            scratch_shapes=[
                pltpu.VMEM((length, 128), BF16),
                pltpu.VMEM((length, 128), BF16),
                pltpu.VMEM((128, length), BF16),
                pltpu.VMEM((length, 128), F32),
                pltpu.VMEM((length, 128), F32),
                pltpu.VMEM((length, 128), F32),
                pltpu.VMEM((128, 2 * BLK), F32),
            ],
        ),
        out_shape=jax.ShapeDtypeStruct(packs.shape, BF16),
        compiler_params=params(),
        cost_estimate=cost(3e10, 8e6),
        name="attn_backward",
    )(ends, packs, grads, packs, lse, full, table)


def middle_kernel(attn_ref, wo_ref, x_ref, gain_ref, middle_ref, h_ref):
    total = None
    for c in range(attn_ref.shape[0]):
        part = dot(attn_ref[c], wo_ref[c])
        total = part if total is None else total + part
    middle = x_ref[...] + RESIDUAL * total
    middle_ref[...] = middle
    normed, _ = norm_parts(middle)
    h_ref[...] = (normed * gain_ref[...]).astype(BF16)


def middle_step(attn, wo, x, gain):
    tokens, width = x.shape
    return pl.pallas_call(
        middle_kernel,
        out_shape=[jax.ShapeDtypeStruct((tokens, width), F32), jax.ShapeDtypeStruct((tokens, width), BF16)],
        compiler_params=params(),
        cost_estimate=cost(2 * tokens * width * width, 5e6),
        name="middle",
    )(attn, wo, x, gain)


def own_row(table, row):
    return jnp.sum(jnp.where(row_iota(table.shape) == row, table, 0.0), 0, keepdims=True)


def one_hot(slots, first, number, capp):
    tokens = slots.shape[1]
    order = row_iota((capp, tokens)).astype(F32)
    return [(order == own_row(slots, first + j)).astype(F32) for j in range(number)]


def gather_kernel(number, capp, first_ref, h_ref, cx_ref, wrt_ref, x_ref, g_ref, gate_ref):
    tokens = h_ref.shape[1]
    first = first_ref[0]
    h = h_ref[0]
    slots = cx_ref[0, tokens:, :tokens].astype(F32)
    logits = dot(wrt_ref[...], h, NT)[:EXPERTS, :]
    raw = jnp.exp(logits - jnp.max(logits, 0, keepdims=True))
    router = raw / jnp.sum(raw, 0, keepdims=True)
    hots = one_hot(slots, first, number, capp)
    places = jnp.concatenate(hots, 0).astype(BF16)
    rows = dot(places, h).astype(BF16)
    grads = dot(places, cx_ref[0, :tokens, :]).astype(BF16)
    for j in range(number):
        at = slice(j * capp, (j + 1) * capp)
        x_ref[j, 0] = rows[at]
        g_ref[j, 0] = grads[at]
        gate = jnp.sum(hots[j] * own_row(router, first + j), 1, keepdims=True)
        gate_ref[j, 0] = jnp.broadcast_to(gate, (capp, 128))


def gather_rows(first, hs, cxs, wrt, number, capp):
    nb, tokens, width = hs.shape
    return pl.pallas_call(
        functools.partial(gather_kernel, number, capp),
        grid_spec=pltpu.PrefetchScalarGridSpec(
            num_scalar_prefetch=1,
            grid=(nb,),
            in_specs=[
                pl.BlockSpec((1, tokens, width), lambda b, f: (b, 0, 0)),
                pl.BlockSpec((1, tokens + EXPERTS, width), lambda b, f: (b, 0, 0)),
                pl.BlockSpec(wrt.shape, lambda b, f: (0, 0)),
            ],
            out_specs=[
                pl.BlockSpec((number, 1, capp, width), lambda b, f: (0, b, 0, 0)),
                pl.BlockSpec((number, 1, capp, width), lambda b, f: (0, b, 0, 0)),
                pl.BlockSpec((number, 1, capp, 128), lambda b, f: (0, b, 0, 0)),
            ],
        ),
        out_shape=[
            jax.ShapeDtypeStruct((number, nb, capp, width), BF16),
            jax.ShapeDtypeStruct((number, nb, capp, width), BF16),
            jax.ShapeDtypeStruct((number, nb, capp, 128), F32),
        ],
        compiler_params=params(),
        cost_estimate=cost(4 * nb * number * capp * tokens * width, 2e7),
        name="gather_rows",
    )(first, hs, cxs, wrt)


PIECE = 512


def expert_kernel(base_ref, x_ref, g_ref, gate_ref, wg_ref, wu_ref, wd_ref, piece_ref, out_ref, rows_ref, dg_ref):
    x = x_ref[0]
    gate = gate_ref[0][:, :1]
    grad_ffn = RESIDUAL * g_ref[0].astype(F32)
    go = (gate * grad_ffn).astype(BF16)
    part = wg_ref.shape[2] // 2
    out = rows = None
    for chunk in range(2):
        at = slice(chunk * part, (chunk + 1) * part)
        wg, wu, wd = wg_ref[0, :, at], wu_ref[0, :, at], wd_ref[0, at, :]
        pre_gate = dot(x, wg)
        pre_up = dot(x, wu)
        sig = jax.nn.sigmoid(pre_gate)
        hidden = (pre_gate * sig * pre_up).astype(BF16)
        out_part = dot(hidden, wd)
        grad_hidden = dot(go, wd, NT)
        grad_gate = (grad_hidden * pre_up * sig * (1.0 + pre_gate * (1.0 - sig))).astype(BF16)
        grad_up = (grad_hidden * pre_gate * sig).astype(BF16)
        row_part = dot(grad_gate, wg, NT) + dot(grad_up, wu, NT)
        dwg = dot(x, grad_gate, TN).astype(BF16)
        dwu = dot(x, grad_up, TN).astype(BF16)
        dwd = dot(hidden, go, TN).astype(BF16)
        for half in range(2):
            side = slice(half * PIECE, (half + 1) * PIECE)
            piece_ref[0, 3 * chunk + half, :, :part] = dwg[side]
            piece_ref[0, 3 * chunk + half, :, part:] = dwu[side]
            piece_ref[0, 3 * chunk + 2, half * part : (half + 1) * part, :] = dwd[:, side]
        out = out_part if out is None else out + out_part
        rows = row_part if rows is None else rows + row_part
    out = out.astype(BF16).astype(F32)
    out_ref[0] = (gate * out).astype(BF16)
    rows_ref[0] = rows.astype(BF16)
    grad = jnp.sum(grad_ffn * out, 1, keepdims=True)
    dg_ref[0] = jnp.broadcast_to(grad, dg_ref.shape[1:])


def expert_step(base, xs, gs, gates, w_gate, w_up, w_down):
    number, rows, width = xs.shape
    ff = w_gate.shape[2]
    row = lambda e, b: (e, 0, 0)
    weight = lambda e, b: (b[0] + e, 0, 0)
    return pl.pallas_call(
        expert_kernel,
        grid_spec=pltpu.PrefetchScalarGridSpec(
            num_scalar_prefetch=1,
            grid=(number,),
            in_specs=[
                pl.BlockSpec((1, rows, width), row),
                pl.BlockSpec((1, rows, width), row),
                pl.BlockSpec((1, rows, 128), row),
                pl.BlockSpec((1, width, ff), weight),
                pl.BlockSpec((1, width, ff), weight),
                pl.BlockSpec((1, ff, width), weight),
            ],
            out_specs=[
                pl.BlockSpec((1, 6, PIECE, PIECE), lambda e, b: (e, 0, 0, 0)),
                pl.BlockSpec((1, rows, width), row),
                pl.BlockSpec((1, rows, width), row),
                pl.BlockSpec((1, rows, 128), row),
            ],
        ),
        out_shape=[
            jax.ShapeDtypeStruct((number, 6, PIECE, PIECE), BF16),
            jax.ShapeDtypeStruct((number, rows, width), BF16),
            jax.ShapeDtypeStruct((number, rows, width), BF16),
            jax.ShapeDtypeStruct((number, rows, 128), F32),
        ],
        compiler_params=params(60),
        cost_estimate=cost(18 * number * rows * width * ff, 5e7),
        name="expert_step",
    )(base, xs, gs, gates, w_gate, w_up, w_down)


def combine_kernel(number, capp, first_ref, slot_ref, outs, rows, grads, y_ref, gx_ref):
    tokens = y_ref.shape[1]
    width = y_ref.shape[2]
    first = first_ref[0]
    slots = slot_ref[0][:, :tokens].astype(F32)
    hots = one_hot(slots, first, number, capp)
    places = jnp.concatenate(hots, 0).astype(BF16)
    y_ref[0] = dot(places, outs[:, 0].reshape(number * capp, width), TN).astype(BF16)
    gx_ref[0, :tokens] = dot(places, rows[:, 0].reshape(number * capp, width), TN).astype(BF16)
    extra = jnp.zeros((EXPERTS, 2 * tokens), F32)
    for j in range(number):
        grad = jnp.sum(hots[j] * grads[j, 0][:, :1], 0, keepdims=True)
        high = grad.astype(BF16).astype(F32)
        both = jnp.concatenate([high, grad - high], 1)
        extra = jnp.where(row_iota(extra.shape) == first + j, both, extra)
    rest = jnp.zeros((EXPERTS, width - 2 * tokens), F32)
    gx_ref[0, tokens:] = jnp.concatenate([extra, rest], 1).astype(BF16)


def combine(first, slots, outs, rows, grads, tokens, capp):
    number = outs.shape[0]
    nb, _, width = slots.shape
    split = lambda a: a.reshape(number, nb, capp, a.shape[-1])
    wide = pl.BlockSpec((number, 1, capp, width), lambda b, f: (0, b, 0, 0))
    thin = pl.BlockSpec((number, 1, capp, 128), lambda b, f: (0, b, 0, 0))
    return pl.pallas_call(
        functools.partial(combine_kernel, number, capp),
        grid_spec=pltpu.PrefetchScalarGridSpec(
            num_scalar_prefetch=1,
            grid=(nb,),
            in_specs=[pl.BlockSpec((1, EXPERTS, width), lambda b, f: (b, 0, 0))] + [wide, wide, thin],
            out_specs=[
                pl.BlockSpec((1, tokens, width), lambda b, f: (b, 0, 0)),
                pl.BlockSpec((1, tokens + EXPERTS, width), lambda b, f: (b, 0, 0)),
            ],
        ),
        out_shape=[
            jax.ShapeDtypeStruct((nb, tokens, width), BF16),
            jax.ShapeDtypeStruct((nb, tokens + EXPERTS, width), BF16),
        ],
        compiler_params=params(),
        cost_estimate=cost(4 * nb * number * capp * tokens * width, 2e7),
        name="combine",
    )(first, slots, split(outs), split(rows), split(grads))


def home_kernel(gx_ref, h_ref, middle_ref, cot_ref, wr_ref, wo_ref, gain_ref, attn_ref, grad_middle_ref, dwo_ref, ga_ref, dwr_ref, dgain_ref):
    tokens, width = h_ref.shape
    h = h_ref[...]
    gain = gain_ref[...]
    extra = gx_ref[tokens:, :].astype(F32)
    grad_router = extra[:, :tokens] + extra[:, tokens : 2 * tokens]
    grad_router = jnp.transpose(jnp.concatenate([grad_router, jnp.zeros((128 - EXPERTS, tokens), F32)], 0))
    logits = dot(h, wr_ref[...])
    logits = jnp.where(lane_iota(logits.shape) < EXPERTS, logits, MASKED)
    raw = jnp.exp(logits - jnp.max(logits, -1, keepdims=True))
    router = raw / jnp.sum(raw, -1, keepdims=True)
    grad_logits = (router * (grad_router - jnp.sum(router * grad_router, -1, keepdims=True))).astype(BF16)
    dwr_ref[...] = dot(h, grad_logits, TN).astype(BF16)
    grad_h = gx_ref[:tokens, :].astype(F32) + dot(grad_logits, wr_ref[...], NT)
    normed, scale = norm_parts(middle_ref[...])
    dgain_ref[...] = jnp.sum(grad_h * normed, 0, keepdims=True)
    grad_middle = cot_ref[...] + norm_back(grad_h * gain, normed, scale)
    grad_middle_ref[...] = grad_middle
    grad_branch = (RESIDUAL * grad_middle).astype(BF16)
    for c in range(attn_ref.shape[0]):
        dwo_ref[c] = dot(attn_ref[c], grad_branch, TN).astype(BF16)
        ga_ref[c] = dot(grad_branch, wo_ref[c], NT).astype(BF16)


def home_step(gx, h, middle, cot, wr, wo, gain, attn):
    tokens, width = h.shape
    n = attn.shape[0]
    return pl.pallas_call(
        home_kernel,
        out_shape=[
            jax.ShapeDtypeStruct((tokens, width), F32),
            jax.ShapeDtypeStruct((n, 128, width), BF16),
            jax.ShapeDtypeStruct((n, tokens, 128), BF16),
            jax.ShapeDtypeStruct((width, 128), BF16),
            jax.ShapeDtypeStruct((1, width), F32),
        ],
        compiler_params=params(),
        cost_estimate=cost(4 * tokens * width * width, 1e7),
        name="home_step",
    )(gx, h, middle, cot, wr, wo, gain, attn)


def final_kernel(shard, grads_ref, w_ref, h_ref, x_ref, gain_ref, grad_middle_ref, dw_ref, grad_x_ref, dgain_ref, total):
    c = pl.program_id(0)
    g = grads_ref[0]
    dw_ref[...] = dot(h_ref[...], g, TN).astype(BF16)

    @pl.when(c == 0)
    def _():
        total[...] = jnp.zeros_like(total)

    for f in range(w_ref.shape[0]):
        total[:, f * shard : (f + 1) * shard] += dot(g, w_ref[f, :shard, :], NT)

    @pl.when(c == pl.num_programs(0) - 1)
    def _():
        normed, scale = norm_parts(x_ref[...])
        grad_h = total[...]
        dgain_ref[...] = jnp.sum(grad_h * normed, 0, keepdims=True)
        grad_x_ref[...] = grad_middle_ref[...] + norm_back(grad_h * gain_ref[...], normed, scale)


def final_step(grads, weights, h, x, gain, grad_middle, shard):
    n, tokens, _ = grads.shape
    width = x.shape[1]
    fsdp, padded, _ = weights.shape
    same = lambda c: (0, 0)
    return pl.pallas_call(
        functools.partial(final_kernel, shard),
        grid=(n,),
        in_specs=[
            pl.BlockSpec((1, tokens, PACK), lambda c: (c, 0, 0)),
            pl.BlockSpec((fsdp, padded, PACK), lambda c: (0, 0, c)),
            pl.BlockSpec((tokens, width), same),
            pl.BlockSpec((tokens, width), same),
            pl.BlockSpec((1, width), same),
            pl.BlockSpec((tokens, width), same),
        ],
        out_specs=[
            pl.BlockSpec((width, PACK), lambda c: (0, c)),
            pl.BlockSpec((tokens, width), same),
            pl.BlockSpec((1, width), same),
        ],
        out_shape=[
            jax.ShapeDtypeStruct((width, n * PACK), BF16),
            jax.ShapeDtypeStruct((tokens, width), F32),
            jax.ShapeDtypeStruct((1, width), F32),
        ],
        scratch_shapes=[pltpu.VMEM((tokens, width), F32)],
        compiler_params=params(),
        cost_estimate=cost(4 * tokens * width * n * PACK, 1.2e7),
        name="final_step",
    )(grads, weights, h, x, gain, grad_middle)


def widen_kernel(number, index_ref, own_ref, other_ref, gate_ref, up_ref, down_ref):
    part = gate_ref.shape[2] // 2

    def write(ref):
        for chunk in range(2):
            columns = slice(chunk * part, (chunk + 1) * part)
            for half in range(2):
                at = slice(half * PIECE, (half + 1) * PIECE)
                gate_ref[0, at, columns] = ref[3 * chunk + half, :, :part].astype(F32)
                up_ref[0, at, columns] = ref[3 * chunk + half, :, part:].astype(F32)
                down_ref[0, columns, at] = ref[3 * chunk + 2, half * part : (half + 1) * part, :].astype(F32)

    @pl.when(pl.program_id(0) == 0)
    def _():
        write(own_ref)

    @pl.when(pl.program_id(0) == 1)
    def _():
        write(other_ref)


def tail_kernel(number, index_ref, own_ref, other_ref, own_small_ref, other_small_ref, mixed_in, grad_in, gate_ref, up_ref, down_ref, mixed_ref, grad_ref, dwq_ref, dwk_ref, dwv_ref, dwo_ref, dwr_ref, g1_ref, g2_ref):
    widen_kernel(number, index_ref, own_ref, other_ref, gate_ref, up_ref, down_ref)
    mixed_ref[...] = mixed_in[...]
    grad_ref[...] = grad_in[...]

    @pl.when((pl.program_id(0) == 0) & (pl.program_id(1) == 0))
    def _():
        for which, ref in enumerate((own_small_ref, other_small_ref)):
            part = index_ref[which] // number
            at = pl.ds(pl.multiple_of(part * 128, 128), 128)
            for q in range(4):
                block = ref[1, q * 128 : (q + 1) * 128, :].astype(F32)
                dwq_ref[at, q * 256 : q * 256 + 128] = block[:, :128]
                dwq_ref[at, q * 256 + 128 : (q + 1) * 256] = block[:, 256:384]
                one, two = block[:, 128:256], block[:, 384:]
                low = lane_iota(one.shape) < HEAD_DIMENSION
                dwk_ref[at, q * 128 : (q + 1) * 128] = jnp.where(low, one, pltpu.roll(two, 64, 1))
                dwv_ref[at, q * 128 : (q + 1) * 128] = jnp.where(low, pltpu.roll(one, 64, 1), two)
            dwo_ref[at, :PIECE] = ref[0, 0:128, :].astype(F32)
            dwo_ref[at, PIECE:] = ref[0, 128:256, :].astype(F32)
            dwr_ref[:, at] = jnp.transpose(ref[0, 256:384, :128].astype(F32))[:EXPERTS]
            gains = ref[0, 384:400, :128].astype(F32)
            g1_ref[pl.ds(part, 1), :] = gains[0:1]
            g2_ref[pl.ds(part, 1), :] = gains[1:2]


def expert_specs(number, shapes):
    last = number - 1
    ins = [
        pl.BlockSpec((6, PIECE, PIECE), lambda s, e, at: (jnp.where(s == 0, e, last), 0, 0)),
        pl.BlockSpec((6, PIECE, PIECE), lambda s, e, at: (jnp.where(s == 0, 0, e), 0, 0)),
    ]
    outs = [pl.BlockSpec((1,) + tuple(shape[1:]), lambda s, e, at: (at[s] + e, 0, 0)) for shape in shapes]
    return ins, outs, [jax.ShapeDtypeStruct(shape, F32) for shape in shapes]


def widen(index, own, other, shapes):
    number = shapes[0][0] // 2
    ins, outs, out_shapes = expert_specs(number, shapes)
    return pl.pallas_call(
        functools.partial(widen_kernel, number),
        grid_spec=pltpu.PrefetchScalarGridSpec(num_scalar_prefetch=1, grid=(2, number), in_specs=ins, out_specs=outs),
        out_shape=out_shapes,
        compiler_params=params(),
        cost_estimate=cost(0, 1e8),
        name="widen",
    )(index, own, other)


def tail(index, own, other, mixed, grad_x, shapes, shard):
    number = shapes[0][0] // 2
    tokens, width = mixed.shape
    ins, outs, out_shapes = expert_specs(number, shapes)
    small = pl.BlockSpec((2, PIECE, PIECE), lambda s, e, at: (3 * number, 0, 0))
    rows = pl.BlockSpec((tokens // (2 * number), width), lambda s, e, at: (s * number + e, 0))
    small_shapes = [(shard, width), (shard, width // 2), (shard, width // 2), (shard, width), (EXPERTS, shard), (2, 128), (2, 128)]
    whole = [pl.BlockSpec(shape, lambda s, e, at: (0, 0)) for shape in small_shapes]
    return pl.pallas_call(
        functools.partial(tail_kernel, number),
        grid_spec=pltpu.PrefetchScalarGridSpec(
            num_scalar_prefetch=1,
            grid=(2, number),
            in_specs=ins + [small, small, rows, rows],
            out_specs=outs + [rows, rows] + whole,
        ),
        out_shape=out_shapes
        + [jax.ShapeDtypeStruct((tokens, width), F32)] * 2
        + [jax.ShapeDtypeStruct(shape, F32) for shape in small_shapes],
        compiler_params=params(),
        cost_estimate=cost(0, 1e8),
        name="tail",
    )(index, own, other, own, other, mixed, grad_x)


def swap(value, axis, bit):
    size = lax.axis_size(axis)
    return lax.ppermute(value, axis, [(i, i ^ bit) for i in range(size)])


def group_bits(fsdp):
    bits = [("fsdp", 1 << b) for b in range(1, fsdp.bit_length() - 1)]
    return bits + [("ctx", 1), ("fsdp", 1)]


def group_gather(value, bits):
    stacked = value[None]
    for axis, bit in bits:
        stacked = jnp.concatenate([stacked, swap(stacked, axis, bit)], 0)
    return stacked


def group_reduce(stacked, bits):
    for axis, bit in reversed(bits):
        half = stacked.shape[0] // 2
        arrived = swap(stacked[half:], axis, bit)
        stacked = (stacked[:half].astype(F32) + arrived.astype(F32)).astype(stacked.dtype)
    return stacked[0]


def line_sum(value, ctx):
    pairs = ctx // 2
    if pairs != 4:
        bit = 2
        while bit < ctx:
            value = value + swap(value, "ctx", bit)
            bit *= 2
        return value
    at = lambda z, y: 2 * z + y
    inward = [(at(0, y), at(1, y)) for y in range(2)] + [(at(3, y), at(2, y)) for y in range(2)]
    across = [(at(1, y), at(2, y)) for y in range(2)] + [(at(2, y), at(1, y)) for y in range(2)]
    outward = [(b, a) for a, b in inward]
    value = value + lax.ppermute(value, "ctx", inward)
    value = value + lax.ppermute(value, "ctx", across)
    arrived = lax.ppermute(value, "ctx", outward)
    z = lax.axis_index("ctx") // 2
    return jnp.where((z == 0) | (z == 3), arrived, value)


MESH = pl.DeviceIdType.MESH


def flip(index, bit):
    return jnp.where((index // bit) % 2 == 0, index + bit, index - bit)


def send(src, dst, send_sem, recv_sem, device):
    return pltpu.make_async_remote_copy(src_ref=src, dst_ref=dst, send_sem=send_sem, recv_sem=recv_sem, device_id=device, device_id_type=MESH)


def neighbours():
    ctx, fsdp = lax.axis_index("ctx"), lax.axis_index("fsdp")
    side, across = flip(ctx, 1), flip(fsdp, 2)
    core = {"fsdp": flip(fsdp, 1)}
    return core, [{"fsdp": across}, {"ctx": side}, {"ctx": side, "fsdp": across}]


def greet(devices):
    barrier = pltpu.get_barrier_semaphore()
    for device in devices:
        pl.semaphore_signal(barrier, inc=1, device_id=device, device_id_type=MESH)
    pl.semaphore_wait(barrier, len(devices))


def others(n):
    ctx = lax.axis_index("ctx")
    return [lax.rem(ctx + d, n) for d in range(1, n)]


def exchange_start(src, dst, send_sems, recv_sems, local_sem, n):
    ctx = lax.axis_index("ctx")
    for d, c in enumerate(others(n)):
        send(src.at[c], dst.at[ctx], send_sems.at[d], recv_sems.at[d], {"ctx": c}).start()
    pltpu.make_async_copy(src.at[ctx], dst.at[ctx], local_sem).start()


def exchange_wait(src, dst, send_sems, recv_sems, local_sem, n, arrived=None):
    ctx = lax.axis_index("ctx")
    pltpu.make_async_copy(src.at[ctx], dst.at[ctx], local_sem).wait()
    if arrived is not None:
        arrived(ctx)
    for d in range(n - 1):
        source = lax.rem(ctx + n - 1 - d, n)
        send(src.at[source], dst.at[source], send_sems.at[d], recv_sems.at[d], {"ctx": source}).wait_recv()
        if arrived is not None:
            arrived(source)
    for d, c in enumerate(others(n)):
        send(src.at[c], dst.at[ctx], send_sems.at[d], recv_sems.at[d], {"ctx": c}).wait_send()


def turn_half(v, table, direction, lanes_turned):
    lanes = lane_iota(v.shape)
    swapped = jnp.where(lanes % HEAD_DIMENSION < HEAD_DIMENSION // 2, pltpu.roll(v, 96, 1), pltpu.roll(v, 32, 1))
    return jnp.where(lanes < lanes_turned, v * table[:, :128] + direction * (swapped * table[:, 128:]), v)


def front_kernel(n, cap, wq_ref, wk_ref, wv_ref, wo_part_ref, wr_raw_ref, gain_ref, x_ref, table_ref, routes_ref, cot_ref, packs_ref, h_ref, weights_ref, wo_ref, wr_ref, cxs_ref, gains_ref, wall, packed_ref, wr_part_ref, cx, table, normed_ref, total, out, exch_send, exch_recv, full_send, full_recv, x_send, x_recv, y_send, y_recv, xs_send, xs_recv, ys_send, ys_recv, cx_send, cx_recv, local_sems):
    tokens, width = x_ref.shape
    shard = width // 4
    ctx, fsdp = lax.axis_index("ctx"), lax.axis_index("fsdp")
    parity = lax.rem(ctx, 2)
    core, group = neighbours()
    far, near = group[0], group[1]
    sibling, distant = flip(fsdp, 1), flip(fsdp, 2)
    other = flip(distant, 1)
    for k in range(2):
        pltpu.make_async_copy(table_ref.at[k, ctx], table.at[k], local_sems.at[6 + k]).start()

    pair = HEAD_DIMENSION * 2
    for c in range(0, n, 2):
        keys, values = wk_ref[:, c // 2 * pair : (c // 2 + 1) * pair].astype(F32), wv_ref[:, c // 2 * pair : (c // 2 + 1) * pair].astype(F32)
        low = lane_iota(keys.shape) < HEAD_DIMENSION
        packed_ref[0, :shard, c * 128 : (c + 1) * 128] = jnp.where(low, keys, pltpu.roll(values, 64, 1)).astype(BF16)
        packed_ref[0, :shard, (c + 1) * 128 : (c + 2) * 128] = jnp.where(low, pltpu.roll(keys, 64, 1), values).astype(BF16)
    below = packed_ref.shape[1] - shard
    packed_ref[0, shard:, :] = jnp.zeros((below, width), BF16)
    row = row_iota((16, shard))
    gains = gain_ref[...].astype(F32)
    gain_rows = jnp.where(row == 0, gains[0:1], jnp.where(row == 1, gains[1:2], 0.0))
    packed_ref[0, shard : shard + 16, :shard] = gain_rows.astype(BF16)
    packed_ref[1, :shard, :] = wq_ref[...]
    packed_ref[1, shard:, :] = jnp.zeros((below, width), BF16)
    router = jnp.concatenate([wr_raw_ref[...].astype(F32), jnp.zeros((128 - EXPERTS, shard), F32)], 0)
    wr_part_ref[...] = jnp.transpose(router).astype(BF16)
    greet([core, far] + [{"ctx": c} for c in others(n)])

    half_rows = packed_ref.shape[1] // 2

    def cut(k, part):
        if k < 2:
            return pl.ds(pl.multiple_of(part * half_rows, 16), half_rows)
        if k == 2:
            return pl.ds(part, 1)
        return pl.ds(pl.multiple_of(part * (shard // 2), 16), shard // 2)

    sources = [packed_ref.at[0], packed_ref.at[1], wo_part_ref, wr_part_ref]
    targets = [wall.at[0], wall.at[1], wo_ref, wr_ref]

    def whole(k):
        return send(sources[k], targets[k].at[fsdp], full_send.at[k], full_recv.at[k], core)

    def own(k):
        return pltpu.make_async_copy(sources[k], targets[k].at[fsdp], local_sems.at[k])

    def to_far(k):
        return send(sources[k].at[cut(k, parity)], targets[k].at[fsdp, cut(k, parity)], x_send.at[k], x_recv.at[k], far)

    def pass_on(k, part, sems, device):
        ref = targets[k].at[distant, cut(k, part)]
        return send(ref, ref, sems[0].at[k], sems[1].at[k], device)

    def sibling_arrived(k):
        ref = targets[k].at[sibling]
        send(ref, ref, full_send.at[k], full_recv.at[k], core).wait_recv()

    def far_arrived(k):
        ref = targets[k].at[distant, cut(k, parity)]
        send(ref, ref, x_send.at[k], x_recv.at[k], far).wait_recv()
        pass_on(k, parity, (y_send, y_recv), near).start()
        pass_on(k, parity, (xs_send, xs_recv), core).start()

    def near_arrived(k):
        pass_on(k, 1 - parity, (y_send, y_recv), near).wait_recv()
        pass_on(k, 1 - parity, (ys_send, ys_recv), core).start()

    def core_arrived(k):
        for part, sems in ((parity, (xs_send, xs_recv)), (1 - parity, (ys_send, ys_recv))):
            ref = targets[k].at[other, cut(k, part)]
            send(ref, ref, sems[0].at[k], sems[1].at[k], core).wait_recv()

    for k in range(2):
        to_far(k).start()
    for k in range(2):
        whole(k).start()
        own(k).start()

    prep_kernel(cap, routes_ref, cot_ref, cx)
    pltpu.make_async_copy(cx, cxs_ref.at[0], local_sems.at[4]).start()
    normed, _ = norm_parts(x_ref[...])
    normed_ref[...] = normed

    def project(k, block, begin):
        at = pl.ds(pl.multiple_of(block * shard, shard), shard)
        if k == 0:
            gain = wall[0, block, shard : shard + 16, :shard].astype(F32)
            gains_ref[:, at] = gain
            h_ref[:, at] = (normed_ref[:, at] * gain[:1]).astype(BF16)
        part = dot(h_ref[:, at], wall[k, block, :shard, :])
        total[k] = part if begin else total[k] + part

    for k in range(2):
        own(k).wait()
        project(k, fsdp, True)
        sibling_arrived(k)
        project(k, sibling, False)
        if k == 0:
            far_arrived(0)

    exchanges = []

    def emit(k):
        lanes = slice(128, 256) if k == 0 else slice(0, 128)
        for c in range(n):
            out[c, :, lanes] = turn_half(total[k, :, c * 128 : (c + 1) * 128], angles, 1.0, 64 if k == 0 else 128).astype(BF16)
        cut_lanes = pl.ds(128 if k == 0 else 0, 128)
        source, target = out.at[:, :, cut_lanes], packs_ref.at[:, :, cut_lanes]
        exchanges.append((source, target, exch_send.at[k], exch_recv.at[k], local_sems.at[8 + k], n))
        exchange_start(*exchanges[-1])

    near_arrived(0)
    project(0, distant, False)
    core_arrived(0)
    project(0, other, False)
    for k in range(2):
        pltpu.make_async_copy(table_ref.at[k, ctx], table.at[k], local_sems.at[6 + k]).wait()
    angles = table[...].reshape(tokens, 256)
    emit(0)
    far_arrived(1)
    for k in (2, 3):
        own(k).start()
        whole(k).start()
        to_far(k).start()
    send(cx, cxs_ref.at[1], cx_send.at[0], cx_recv.at[0], far).start()
    near_arrived(1)
    project(1, distant, False)
    core_arrived(1)
    project(1, other, False)
    emit(1)
    keep = pltpu.make_async_copy(wall, weights_ref, local_sems.at[5])
    keep.start()
    for k in (2, 3):
        far_arrived(k)
    for k in (2, 3):
        near_arrived(k)
    for k in (2, 3):
        core_arrived(k)
        sibling_arrived(k)
        own(k).wait()
    for exchange in exchanges:
        exchange_wait(*exchange)
    for k in range(4):
        whole(k).wait_send()
        to_far(k).wait_send()
        pass_on(k, parity, (y_send, y_recv), near).wait_send()
        pass_on(k, parity, (xs_send, xs_recv), core).wait_send()
        pass_on(k, 1 - parity, (ys_send, ys_recv), core).wait_send()
    send(cx, cxs_ref.at[1], cx_send.at[0], cx_recv.at[0], far).wait()
    pltpu.make_async_copy(cx, cxs_ref.at[0], local_sems.at[4]).wait()
    keep.wait()


def front(wq, wk, wv, wo_part, wr, gains, x, table, routes, cot, cap, n):
    tokens, width = x.shape
    shard = wq.shape[0]
    hbm, vmem = pl.BlockSpec(memory_space=pl.ANY), pl.BlockSpec(memory_space=pltpu.VMEM)
    dma = lambda *k: pltpu.SemaphoreType.DMA(k)
    shaped = lambda shape, dtype=BF16: jax.ShapeDtypeStruct(shape, dtype)
    cx_shape = (tokens + EXPERTS, width)
    padded = 2 * 16 * (shard // 32 + 1)
    return pl.pallas_call(
        functools.partial(front_kernel, n, cap),
        in_specs=[vmem, vmem, vmem, hbm, vmem, vmem, vmem, hbm, vmem, vmem],
        out_specs=[hbm, vmem, hbm, hbm, hbm, hbm, vmem],
        out_shape=[
            shaped((n, tokens, PACK)),
            shaped((tokens, width)),
            shaped((2, 4, padded, width)),
            shaped((4,) + wo_part.shape),
            shaped((4, shard, 128)),
            shaped((2,) + cx_shape),
            shaped((16, width), F32),
        ],
        scratch_shapes=[
            pltpu.VMEM((2, 4, padded, width), BF16),
            pltpu.VMEM((2, padded, width), BF16),
            pltpu.VMEM((shard, 128), BF16),
            pltpu.VMEM(cx_shape, BF16),
            pltpu.VMEM((2, tokens // 2, 256), F32),
            pltpu.VMEM((tokens, width), F32),
            pltpu.VMEM((2, tokens, width), F32),
            pltpu.VMEM((n, tokens, PACK), BF16),
            dma(2, n - 1),
            dma(2, n - 1),
        ]
        + [dma(4)] * 10
        + [dma(1), dma(1), dma(10)],
        compiler_params=params(collective_id=1, has_side_effects=True),
        cost_estimate=cost(2e9, 5e7),
        name="front",
    )(wq, wk, wv, wo_part, wr, gains, x, table, routes, cot)


def attend_kernel(length, n, ends_ref, q_ref, pack_ref, cxs_ref, out_ref, lse_ref, full_ref, rest_ref, keys, values_t, acc, near_send, near_recv, core_send, core_recv):
    block = pl.program_id(0)
    core, group = neighbours()
    near = group[1]

    def to_near():
        return send(cxs_ref.at[0], rest_ref.at[0], near_send.at[0], near_recv.at[0], near)

    def to_core(i):
        src = cxs_ref.at[i] if i < 2 else rest_ref.at[0]
        return send(src, rest_ref.at[1 + i], core_send.at[i], core_recv.at[i], core)

    @pl.when(block == 0)
    def _():
        greet([core, near])
        to_near().start()
        for i in range(2):
            to_core(i).start()

    attn_forward_kernel(length, ends_ref, q_ref, pack_ref, out_ref, lse_ref, full_ref, keys, values_t, acc)

    @pl.when(block == pl.num_programs(0) - 2)
    def _():
        to_near().wait_recv()
        to_core(2).start()

    @pl.when(block == pl.num_programs(0) - 1)
    def _():
        for i in range(3):
            to_core(i).wait()
        to_near().wait_send()


def attend(ends, packs, cxs, length):
    n, _, rows, _ = packs.shape
    blocks, per = length // BLK, BLK // rows
    per_half = blocks // 2
    tiles = lambda i: (lax.rem(i, per_half), i // per_half, 0, 0)
    hbm = pl.BlockSpec(memory_space=pl.ANY)
    dma = lambda k: pltpu.SemaphoreType.DMA((k,))
    return pl.pallas_call(
        functools.partial(attend_kernel, length, n),
        grid=(blocks,),
        in_specs=[
            pl.BlockSpec(memory_space=pltpu.SMEM),
            pl.BlockSpec((per, 1, rows, PACK), tiles),
            pl.BlockSpec(packs.shape, lambda i: (0, 0, 0, 0)),
            hbm,
        ],
        out_specs=[
            pl.BlockSpec((per, 1, rows, 128), tiles),
            pl.BlockSpec((1, 1, 2 * BLK), lambda i: (i, 0, 0)),
            pl.BlockSpec((1, 128, 2 * BLK), lambda i: (i, 0, 0)),
            hbm,
        ],
        scratch_shapes=[
            pltpu.VMEM((length, 128), BF16),
            pltpu.VMEM((128, length), BF16),
            pltpu.VMEM((128, 2 * BLK), F32),
            dma(1),
            dma(1),
            dma(3),
            dma(3),
        ],
        out_shape=[
            jax.ShapeDtypeStruct((n, 2, rows, 128), BF16),
            jax.ShapeDtypeStruct((blocks, 1, 2 * BLK), F32),
            jax.ShapeDtypeStruct((blocks, 128, 2 * BLK), F32),
            jax.ShapeDtypeStruct((4,) + cxs.shape[1:], BF16),
        ],
        compiler_params=params(collective_id=3, has_side_effects=True),
        cost_estimate=cost(1.5e10, 2e7),
        name="attend",
    )(ends, packs, packs, cxs)


def mid_kernel(n, number, capp, attn_ref, cxs_ref, rest_ref, wo_hbm, wr_ref, x_hbm, gain_ref, middle_ref, h_ref, kept_ref, xs_ref, gs_ref, gates_ref, diag_ref, arrived, hs, wo_ref, x_ref, cx, rows_out, grads_out, gates_out, exch_send, exch_recv, hop_send, hop_recv, cross_send, cross_recv, cx_send, cx_recv, fwd_send, fwd_recv, local_sems, load_sems, store_sems):
    tokens, width = x_ref.shape
    split = tokens // 2
    ctx, fsdp = lax.axis_index("ctx"), lax.axis_index("fsdp")
    first = (fsdp * 2 + lax.rem(ctx, 2)) * number
    core, group = neighbours()
    copies = [pltpu.make_async_copy(wo_hbm, wo_ref, local_sems.at[2]), pltpu.make_async_copy(x_hbm, x_ref, local_sems.at[3])]
    for copy in copies:
        copy.start()
    order = (0, 4, 1, 2, 3, 5, 6, 7)

    def load(step):
        refs = (cxs_ref.at[0], cxs_ref.at[1], rest_ref.at[0], diag_ref.at[0], rest_ref.at[1], rest_ref.at[2], rest_ref.at[3], diag_ref.at[1])
        return pltpu.make_async_copy(refs[order[step]], cx.at[step % 2], load_sems.at[step % 2])

    def cx_cross():
        return send(rest_ref.at[0], diag_ref.at[0], cx_send.at[0], cx_recv.at[0], group[0])

    def cx_core():
        return send(diag_ref.at[0], diag_ref.at[1], cx_send.at[1], cx_recv.at[1], core)

    load(0).start()
    greet([core, group[0]] + [{"ctx": c} for c in others(n)])
    cx_cross().start()
    halves = [pl.ds(k * split, split) for k in range(2)]
    exchanges = [(attn_ref.at[:, halves[k]], arrived.at[:, halves[k]], exch_send.at[k], exch_recv.at[k], local_sems.at[4 + k], n) for k in range(2)]
    for exchange in exchanges:
        exchange_start(*exchange)
    for copy in copies:
        copy.wait()

    def hop(i, k):
        return send(hs.at[0, halves[k]], hs.at[(1, 2, 4)[i], halves[k]], hop_send.at[i, k], hop_recv.at[i, k], (group[0], group[1], core)[i])

    def cross(i):
        return send(hs.at[1 + i, halves[i]], hs.at[3, halves[i]], cross_send.at[i], cross_recv.at[i], group[1 - i])

    def forward(i):
        return send(hs.at[1 + i], hs.at[5 + i], fwd_send.at[i], fwd_recv.at[i], core)

    for k in range(2):
        exchange_wait(*exchanges[k])
        at = slice(k * split, (k + 1) * split)
        total = None
        for c in range(n):
            part = dot(arrived[c, at, :], wo_ref[c])
            total = part if total is None else total + part
        middle = x_ref[at, :] + RESIDUAL * total
        middle_ref[at, :] = middle
        normed, _ = norm_parts(middle)
        h = (normed * gain_ref[1:2]).astype(BF16)
        h_ref[at, :] = h
        hs[0, at, :] = h
        for i in range(3):
            hop(i, k).start()
    cx_cross().wait_recv()
    cx_core().start()
    keep = pltpu.make_async_copy(arrived, kept_ref, local_sems.at[1])
    keep.start()

    def stores(step):
        b = order[step]
        pairs = ((rows_out, xs_ref), (grads_out, gs_ref), (gates_out, gates_ref))
        return [pltpu.make_async_copy(src.at[step % 2], dst.at[:, b], store_sems.at[step % 2, k]) for k, (src, dst) in enumerate(pairs)]

    def place(step):
        b, slot = order[step], step % 2
        load(step).wait()
        if step >= 2:
            for copy in stores(step - 2):
                copy.wait()
        h = hs[b]
        logits = jnp.transpose(dot(h, wr_ref[...]))[:EXPERTS, :]
        raw = jnp.exp(logits - jnp.max(logits, 0, keepdims=True))
        router = raw / jnp.sum(raw, 0, keepdims=True)
        slots = cx[slot, tokens:, :tokens].astype(F32)
        hots = one_hot(slots, first, number, capp)
        places = jnp.concatenate(hots, 0).astype(BF16)
        rows = dot(places, h).astype(BF16)
        grads = dot(places, cx[slot, :tokens, :]).astype(BF16)
        for j in range(number):
            at = slice(j * capp, (j + 1) * capp)
            rows_out[slot, j] = rows[at]
            grads_out[slot, j] = grads[at]
            gate = jnp.sum(hots[j] * own_row(router, first + j), 1, keepdims=True)
            gates_out[slot, j] = jnp.broadcast_to(gate, (capp, 128))
        for copy in stores(step):
            copy.start()
        if step + 2 < 8:
            if step + 2 == 7:
                cx_core().wait_recv()
            load(step + 2).start()

    load(1).start()
    place(0)
    for k in range(2):
        hop(2, k).wait_recv()
    place(1)
    hop(0, 0).wait_recv()
    cross(0).start()
    hop(1, 0).wait_recv()
    hop(1, 1).wait_recv()
    cross(1).start()
    forward(1).start()
    hop(0, 1).wait_recv()
    forward(0).start()
    place(2)
    place(3)
    for i in range(2):
        cross(i).wait_recv()
    forward(2).start()
    place(4)
    for i in range(3):
        forward(i).wait_recv()
        place(5 + i)
    for step in (6, 7):
        for copy in stores(step):
            copy.wait()
    for i in range(2):
        cross(i).wait_send()
    cx_cross().wait_send()
    cx_core().wait_send()
    for i in range(3):
        for k in range(2):
            hop(i, k).wait_send()
        forward(i).wait_send()
    keep.wait()


def mid_step(attn, cxs, rest, wo, wr, x, gains, number, capp, n):
    tokens, width = x.shape
    hbm, vmem = pl.BlockSpec(memory_space=pl.ANY), pl.BlockSpec(memory_space=pltpu.VMEM)
    dma = lambda *k: pltpu.SemaphoreType.DMA(k)
    shaped = lambda shape, dtype=BF16: jax.ShapeDtypeStruct(shape, dtype)
    return pl.pallas_call(
        functools.partial(mid_kernel, n, number, capp),
        in_specs=[hbm, hbm, hbm, hbm, vmem, hbm, vmem],
        out_specs=[vmem, vmem, hbm, hbm, hbm, hbm, hbm],
        out_shape=[
            shaped((tokens, width), F32),
            shaped((tokens, width)),
            shaped(attn.shape),
            shaped((number, 8, capp, width)),
            shaped((number, 8, capp, width)),
            shaped((number, 8, capp, 128), F32),
            shaped((2,) + cxs.shape[1:]),
        ],
        scratch_shapes=[
            pltpu.VMEM(attn.shape, BF16),
            pltpu.VMEM((8, tokens, width), BF16),
            pltpu.VMEM(wo.shape, BF16),
            pltpu.VMEM((tokens, width), F32),
            pltpu.VMEM((2,) + cxs.shape[1:], BF16),
            pltpu.VMEM((2, number, capp, width), BF16),
            pltpu.VMEM((2, number, capp, width), BF16),
            pltpu.VMEM((2, number, capp, 128), F32),
            dma(2, n - 1),
            dma(2, n - 1),
            dma(3, 2),
            dma(3, 2),
            dma(2),
            dma(2),
            dma(2),
            dma(2),
            dma(3),
            dma(3),
            dma(6),
            dma(2),
            dma(2, 3),
        ],
        compiler_params=params(collective_id=2, has_side_effects=True),
        cost_estimate=cost(4e9, 5e7),
        name="mid_step",
    )(attn, cxs, rest, wo, wr, x, gains)


RING = 12
LAG_MIDDLE, LAG_ACROSS, LAG_END = 1, 2, 3
ORDER_X, ORDER_Y, ORDER_CORE = 1, 2, 4


class GroupSum:
    def __init__(self, part, rows, lands, own, sems, load, free, first, core, group):
        self.part, self.rows, self.own, self.load, self.free, self.first = part, rows, own, load, free, first
        self.land, self.land_x, self.land_y = lands
        self.core_send, self.core_recv, self.x_send, self.x_recv, self.y_send, self.y_recv = sems
        self.core, self.far, self.near = core, group[0], group[1]

    def place(self, i):
        return self.land.at[i, pl.ds(0, self.rows)]

    def ready(self, which):
        if not self.first:
            pl.semaphore_wait(self.free.at[which], 1)

    def to_core(self, i):
        return send(self.part.at[4 + i], self.place(i), self.core_send.at[i], self.core_recv.at[i], self.core)

    def to_far(self, k):
        return send(self.place(1 + 2 * k), self.land_x.at[k, pl.ds(0, self.rows)], self.x_send.at[k], self.x_recv.at[k], self.far)

    def to_near(self):
        return send(self.place(2), self.land_y.at[pl.ds(0, self.rows)], self.y_send.at[0], self.y_recv.at[0], self.near)

    def fetch(self, i):
        return pltpu.make_async_copy(self.part.at[i], self.own.at[i % 2, pl.ds(0, self.rows)], self.load.at[i % 2])

    def start(self):
        self.ready(0)
        for i in (1, 3, 2, 0):
            self.to_core(i).start()

    def over_cores(self):
        order = (1, 3, 2, 0)
        if self.own is not None:
            self.fetch(1).start()
        for step, i in enumerate(order):
            if self.own is None:
                mine = self.part[i]
            else:
                self.fetch(i).wait()
                mine = self.own[i % 2, : self.rows]
            self.to_core(i).wait_recv()
            self.land[i, : self.rows] = (self.land[i, : self.rows].astype(F32) + mine.astype(F32)).astype(BF16)
            if self.own is not None and step < 3:
                self.fetch(order[step + 1]).start()
            if i % 2 == 1:
                if step == 0:
                    self.ready(1)
                self.to_far(i // 2).start()

    def over_x(self, between=None):
        for k in (1, 0):
            if k == 0 and between is not None:
                between()
            self.to_far(k).wait_recv()
            both = self.land[2 * k, : self.rows].astype(F32) + self.land_x[k, : self.rows].astype(F32)
            self.land[2 * k, : self.rows] = both.astype(BF16)
            if k == 1:
                self.ready(2)
                self.to_near().start()

    def finish(self):
        self.to_near().wait_recv()
        for i in range(4):
            self.to_core(i).wait_send()
        for k in range(2):
            self.to_far(k).wait_send()
        self.to_near().wait_send()
        return self.land[0, : self.rows].astype(F32) + self.land_y[: self.rows].astype(F32)

    def release(self):
        for which, device in enumerate((self.core, self.far, self.near)):
            pl.semaphore_signal(self.free.at[which], inc=1, device_id=device, device_id_type=MESH)


class LineSum:
    def __init__(self, count, own_ref, other_ref, inbox, across, mine, sems):
        self.count, self.own_ref, self.other_ref = count, own_ref, other_ref
        self.inbox, self.across, self.mine = inbox, across, mine
        self.line_send, self.line_recv, self.mid_send, self.mid_recv, self.side_send, self.side_recv, self.store, self.load = sems
        ctx = lax.axis_index("ctx")
        z = ctx // 2
        self.middle = (z == 1) | (z == 2)
        self.line = {"ctx": jnp.where(z % 2 == 0, ctx + 2, ctx - 2)}
        self.peer = {"ctx": jnp.where(z == 1, ctx + 2, ctx - 2)}
        self.side = {"ctx": flip(ctx, 1)}

    def send_line(self, src, i):
        s = lax.rem(i, RING)
        return send(src, self.inbox.at[s], self.line_send.at[s], self.line_recv.at[s], self.line)

    def send_mid(self, i):
        s = lax.rem(i, RING)
        return send(self.inbox.at[s], self.across.at[s], self.mid_send.at[s], self.mid_recv.at[s], self.peer)

    def send_side(self, src, i):
        return send(src, self.other_ref.at[i], self.side_send.at[lax.rem(i, RING)], self.side_recv.at[i], self.side)

    def keep(self, src, i):
        return pltpu.make_async_copy(src, self.own_ref.at[i], self.store.at[lax.rem(i, RING)])

    def fetch(self, src, i):
        s = lax.rem(i, 4)
        return pltpu.make_async_copy(src, self.mine.at[s], self.load.at[s])

    def drain_middle(self, i):
        src = self.across.at[lax.rem(i, RING)]
        self.send_line(src, i).wait_send()
        self.send_side(src, i).wait_send()
        self.keep(src, i).wait()

    def drain_end(self, i):
        src = self.inbox.at[lax.rem(i, RING)]
        self.send_side(src, i).wait_send()
        self.keep(src, i).wait()

    def tick(self, t, source):
        count = self.count
        fixed = isinstance(t, int)

        def when(condition):
            if fixed:
                return (lambda f: f()) if condition else (lambda f: None)
            return pl.when(condition)

        i32 = (lambda v: jnp.int32(v)) if fixed else (lambda v: v)

        @pl.when(self.middle)
        def _():
            @when((t >= LAG_MIDDLE) & (t < count + LAG_MIDDLE))
            def _():
                i = i32(t - LAG_MIDDLE)

                @when(t >= LAG_ACROSS + 4)
                def _():
                    self.drain_middle(i32(t - LAG_ACROSS - 4))

                s = lax.rem(i, RING)
                self.fetch(self.own_ref.at[i], i).wait()
                self.send_line(self.inbox.at[s], i).wait_recv()
                self.inbox[s] = self.inbox[s] + self.mine[lax.rem(i, 4)]
                self.send_mid(i).start()

            @when(t < count)
            def _():
                self.fetch(source(t), i32(t)).start()

            @when((t >= LAG_ACROSS) & (t < count + LAG_ACROSS))
            def _():
                i = i32(t - LAG_ACROSS)
                s = lax.rem(i, RING)
                self.send_mid(i).wait()
                self.across[s] = self.across[s] + self.inbox[s]
                self.send_line(self.across.at[s], i).start()
                self.send_side(self.across.at[s], i).start()
                self.keep(self.across.at[s], i).start()

        @pl.when(jnp.logical_not(self.middle))
        def _():
            @when(t < count)
            def _():
                @when(t >= LAG_END + 2)
                def _():
                    self.drain_end(i32(t - LAG_END - 2))

                @when(t >= 3)
                def _():
                    self.send_line(self.mine.at[0], i32(t - 3)).wait_send()

                self.send_line(source(t), i32(t)).start()

            @when(t >= LAG_END)
            def _():
                i = i32(t - LAG_END)
                s = lax.rem(i, RING)
                self.send_line(self.inbox.at[s], i).wait_recv()
                self.send_side(self.inbox.at[s], i).start()
                self.keep(self.inbox.at[s], i).start()

    def finish(self):
        count = self.count

        @pl.when(self.middle)
        def _():
            for i in range(count + LAG_MIDDLE - LAG_ACROSS - 4, count):
                self.drain_middle(jnp.int32(i))

        @pl.when(jnp.logical_not(self.middle))
        def _():
            for i in range(count - 3, count):
                self.send_line(self.mine.at[0], jnp.int32(i)).wait_send()
            for i in range(count - LAG_END - 2, count):
                self.drain_end(jnp.int32(i))

        def arrived(i, carry):
            self.send_side(self.mine.at[0], i).wait_recv()
            return carry

        lax.fori_loop(0, count, arrived, 0)


def backward_kernel(
    n,
    length,
    capp,
    ends_ref,
    xs_ref,
    gs_ref,
    gates_ref,
    wg_ref,
    wu_ref,
    wd_ref,
    cxs_ref,
    rest_ref,
    diag_ref,
    full_ref,
    weights_ref,
    packs_hbm,
    table_hbm,
    cot_hbm,
    wo_hbm,
    attn_hbm,
    x_hbm,
    h_attn_hbm,
    h_hbm,
    middle_hbm,
    wr_hbm,
    gains_hbm,
    lse_hbm,
    own_ref,
    other_ref,
    pieces_ref,
    outs_ref,
    backs_ref,
    gx_ref,
    yp_ref,
    grad_x_ref,
    mixed_ref,
    inbox,
    across,
    mine,
    land,
    land_x,
    land_y,
    y_land,
    y_land_x,
    y_land_y,
    own_buf,
    late_pieces,
    ga_in,
    grads_in,
    line_send,
    line_recv,
    mid_send,
    mid_recv,
    side_send,
    side_recv,
    line_store,
    line_load,
    ga_send,
    ga_recv,
    gr_send,
    gr_recv,
    group_sems,
    group_load,
    free,
    local_sems,
    full_sems,
    w_sems,
    load_sems,
    store_sems,
    comb_sems,
    part_sems,
):
    tokens, width = h_hbm.shape
    half = length // 2
    rows = tokens // 2
    shard = width // 4
    blocks = length // BLK
    number = xs_ref.shape[0]
    ff = wg_ref.shape[2]
    ctx, fsdp = lax.axis_index("ctx"), lax.axis_index("fsdp")
    side = lax.rem(ctx, 2)
    first = (fsdp * 2 + side) * number
    core, group = neighbours()
    sub = own_ref.shape[1]
    cuts = PIECE // sub
    early = number * 6 * cuts
    line = LineSum(early + 2 * cuts, own_ref, other_ref, inbox, across, mine, (line_send, line_recv, mid_send, mid_recv, side_send, side_recv, line_store, line_load))

    def source(t):
        return pieces_ref.at[t // cuts, pl.ds(pl.multiple_of(lax.rem(t, cuts) * sub, sub), sub)]

    def tick(t):
        line.tick(jnp.int32(t) if isinstance(t, int) else t, source)

    sems = lambda k: [group_sems.at[k, j] for j in range(6)]
    lands = (land, land_x, land_y)
    ext = tokens + EXPERTS
    gx = GroupSum(gx_ref, 2 * ext, lands, None, sems(0), None, free, True, core, group)
    ys = GroupSum(yp_ref, 2 * tokens, (y_land, y_land_x, y_land_y), own_buf, sems(1), group_load, free, True, core, group)

    def strip(r):
        f = fsdp
        if r & ORDER_X:
            f = flip(f, 2)
        if r & ORDER_CORE:
            f = flip(f, 1)
        return 2 * f + (1 - side if r & ORDER_Y else side)

    def experts(wg, wu, wd, xb, gb, gateb, stage, out_acc, back_acc, outb, backb, go, dgate, comb_o, comb_b, gst, yst, slots):
        def loads(e):
            s = lax.rem(e, 2)
            at = side * number + e
            pairs = ((wg_ref.at[at], wg), (wu_ref.at[at], wu), (wd_ref.at[at], wd), (xs_ref.at[e], xb), (gs_ref.at[e], gb), (gates_ref.at[e], gateb))
            return [pltpu.make_async_copy(src, dst.at[s], load_sems.at[s, k]) for k, (src, dst) in enumerate(pairs)]

        def slot_copy(b):
            refs = (cxs_ref.at[0], cxs_ref.at[1], rest_ref.at[0], diag_ref.at[0], rest_ref.at[1], rest_ref.at[2], rest_ref.at[3], diag_ref.at[1])
            return pltpu.make_async_copy(refs[b].at[pl.ds(tokens, EXPERTS), pl.ds(0, tokens)], slots.at[b], part_sems.at[0, b])

        def stores(e):
            pairs = (
                (stage.at[pl.ds(0, 3)], pieces_ref.at[pl.ds(6 * e, 3)]),
                (stage.at[pl.ds(3, 3)], pieces_ref.at[pl.ds(6 * e + 3, 3)]),
                (outb, outs_ref.at[e]),
                (backb, backs_ref.at[e]),
            )
            return [pltpu.make_async_copy(src, dst, store_sems.at[k]) for k, (src, dst) in enumerate(pairs)]

        for copy in loads(jnp.int32(0)):
            copy.start()
        for b in range(8):
            slot_copy(b).start()
        greet([core, group[0]] + [{"ctx": c} for c in others(n)])

        def one(e, carry):
            s = lax.rem(e, 2)

            @pl.when(e + 1 < number)
            def _():
                for copy in loads(e + 1):
                    copy.start()

            for copy in loads(e):
                copy.wait()

            @pl.when(e > 0)
            def _():
                for copy in stores(e - 1)[2:]:
                    copy.wait()

            x = xb[s]
            gate = gateb[s][:, :1]
            go[...] = (gate * (RESIDUAL * gb[s].astype(F32))).astype(BF16)
            part = ff // 2
            for chunk in range(2):
                at = slice(chunk * part, (chunk + 1) * part)
                wgc, wuc, wdc = wg[s, :, at], wu[s, :, at], wd[s, at, :]
                pre_gate = dot(x, wgc)
                pre_up = dot(x, wuc)
                sig = jax.nn.sigmoid(pre_gate)
                hidden = (pre_gate * sig * pre_up).astype(BF16)
                out_part = dot(hidden, wdc)
                grad_hidden = dot(go[...], wdc, NT)
                grad_gate = (grad_hidden * pre_up * sig * (1.0 + pre_gate * (1.0 - sig))).astype(BF16)
                grad_up = (grad_hidden * pre_gate * sig).astype(BF16)
                row_part = dot(grad_gate, wgc, NT) + dot(grad_up, wuc, NT)
                dwg = dot(x, grad_gate, TN).astype(BF16)
                dwu = dot(x, grad_up, TN).astype(BF16)
                dwd = dot(hidden, go[...], TN).astype(BF16)
                for k in range(2):
                    cut = slice(k * PIECE, (k + 1) * PIECE)
                    stage[3 * chunk + k, :, :part] = dwg[cut]
                    stage[3 * chunk + k, :, part:] = dwu[cut]
                    stage[3 * chunk + 2, k * part : (k + 1) * part, :] = dwd[:, cut]
                stores(e)[chunk].start()
                if chunk == 0:
                    out_acc[...] = out_part
                    back_acc[...] = row_part
                    stores(e)[0].wait()
                    tick(2 * e)
                else:
                    out = (out_acc[...] + out_part).astype(BF16).astype(F32)
                    outb[...] = (gate * out).astype(BF16)
                    backb[...] = (back_acc[...] + row_part).astype(BF16)
                    grad = jnp.sum(RESIDUAL * gb[s].astype(F32) * out, 1, keepdims=True)
                    dgate[e] = jnp.broadcast_to(grad, dgate.shape[1:])
            for copy in stores(e)[2:]:
                copy.start()
            stores(e)[1].wait()
            tick(2 * e + 1)
            return carry

        lax.fori_loop(0, number, one, 0)
        for copy in stores(jnp.int32(number - 1))[2:]:
            copy.wait()
        for b in range(8):
            slot_copy(b).wait()

        def which(s):
            k = lax.rem(s, 4)
            i = jnp.where(k == 0, 1, jnp.where(k == 1, 3, jnp.where(k == 2, 2, 0)))
            return jnp.where(s < 4, 4 + i, i), i

        def comb(s):
            k = lax.rem(s, 2)
            at = pl.ds(pl.multiple_of(which(s)[0] * capp, 16), capp)
            return [
                pltpu.make_async_copy(outs_ref.at[:, at], comb_o.at[k], comb_sems.at[0, k]),
                pltpu.make_async_copy(backs_ref.at[:, at], comb_b.at[k], comb_sems.at[1, k]),
            ]

        def put(s):
            k = lax.rem(s, 2)
            r, _ = which(s)
            return [
                pltpu.make_async_copy(gst.at[k], gx_ref.at[r], part_sems.at[1, k]),
                pltpu.make_async_copy(yst.at[k], yp_ref.at[r], part_sems.at[1, 2 + k]),
            ]

        for copy in comb(jnp.int32(0)):
            copy.start()

        def join(s, carry):
            k = lax.rem(s, 2)
            r, i = which(s)

            @pl.when(s + 1 < 8)
            def _():
                for copy in comb(s + 1):
                    copy.start()

            for copy in comb(s):
                copy.wait()

            @pl.when(s >= 2)
            def _():
                put(s - 2)[1].wait()

            hots = one_hot(slots[r].astype(F32), first, number, capp)
            places = jnp.concatenate(hots, 0).astype(BF16)
            y = dot(places, comb_o[k].reshape(number * capp, width), TN).astype(BF16)
            back = dot(places, comb_b[k].reshape(number * capp, width), TN).astype(BF16)
            extra = jnp.zeros((EXPERTS, 2 * tokens), F32)
            for j in range(number):
                grads = dgate[j, pl.ds(pl.multiple_of(r * capp, 16), capp), :][:, :1]
                grad = jnp.sum(hots[j] * grads, 0, keepdims=True)
                high = grad.astype(BF16).astype(F32)
                extra = jnp.where(row_iota(extra.shape) == first + j, jnp.concatenate([high, grad - high], 1), extra)
            for q in range(2):
                yst[k, q * tokens : (q + 1) * tokens, :] = y[:, q * PIECE : (q + 1) * PIECE]
                gst[k, q * ext : q * ext + tokens, :] = back[:, q * PIECE : (q + 1) * PIECE]
            gst[k, tokens:ext, :] = extra.astype(BF16)
            gst[k, ext + tokens :, :] = jnp.zeros((EXPERTS, PIECE), BF16)
            put(s)[1].start()

            @pl.when(s < 4)
            def _():
                put(s)[0].start()
                put(s)[0].wait()
                gx.to_core(i).start()

            @pl.when(s >= 4)
            def _():
                gx.to_core(i).wait_recv()
                land[i, : gx.rows] = (land[i, : gx.rows].astype(F32) + gst[k].astype(F32)).astype(BF16)

            @pl.when((s == 4) | (s == 5))
            def _():
                gx.to_far(s - 4).start()

            @pl.when(lax.rem(s, 2) == 1)
            def _():
                tick(2 * number + s // 2)

            return carry

        lax.fori_loop(0, 8, join, 0)
        for s in range(6, 8):
            put(jnp.int32(s))[1].wait()

    slots_rows = xs_ref.shape[1]
    pl.run_scoped(
        experts,
        pltpu.VMEM((2, width, ff), BF16),
        pltpu.VMEM((2, width, ff), BF16),
        pltpu.VMEM((2, ff, width), BF16),
        pltpu.VMEM((2, slots_rows, width), BF16),
        pltpu.VMEM((2, slots_rows, width), BF16),
        pltpu.VMEM((2, slots_rows, 128), F32),
        pltpu.VMEM((6, PIECE, PIECE), BF16),
        pltpu.VMEM((slots_rows, width), F32),
        pltpu.VMEM((slots_rows, width), F32),
        pltpu.VMEM((slots_rows, width), BF16),
        pltpu.VMEM((slots_rows, width), BF16),
        pltpu.VMEM((slots_rows, width), BF16),
        pltpu.VMEM((number, slots_rows, 128), F32),
        pltpu.VMEM((2, number, capp, width), BF16),
        pltpu.VMEM((2, number, capp, width), BF16),
        pltpu.VMEM((2, 2 * ext, PIECE), BF16),
        pltpu.VMEM((2, 2 * tokens, PIECE), BF16),
        pltpu.VMEM((8, EXPERTS, tokens), BF16),
    )
    at_tick = [2 * number + 4]

    def go_on(k=1):
        for _ in range(k):
            tick(at_tick[0])
            at_tick[0] += 1

    def backward(packs, table, keys, values, keys_t, grad_q, grad_k, grad_v, acc, full_buf, ga, pack_out, wbuf, total, grad_middle, dgain, col, small, columns, cot, wo, attn, x_in, h_attn, h_ref, middle_ref, wr_ref, gains_ref, lse_ref):
        ws = GroupSum(small, small.shape[1], lands, None, sems(2), None, free, False, core, group)
        cs = GroupSum(columns, PIECE + 16, lands, None, sems(3), None, free, False, core, group)
        copies = [
            pltpu.make_async_copy(src, dst, local_sems.at[4 + k])
            for k, (src, dst) in enumerate(
                (
                    (cot_hbm, cot),
                    (wo_hbm, wo),
                    (attn_hbm, attn),
                    (packs_hbm, packs),
                    (table_hbm, table),
                    (x_hbm, x_in),
                    (h_attn_hbm, h_attn),
                    (h_hbm, h_ref),
                    (middle_hbm, middle_ref),
                    (wr_hbm, wr_ref),
                    (gains_hbm, gains_ref),
                    (lse_hbm, lse_ref),
                )
            )
        ]
        for copy in copies:
            copy.start()
        small[:, 256:384, :] = jnp.zeros((8, 128, PIECE), BF16)
        late_pieces[384:PIECE, :] = jnp.zeros((PIECE - 384, PIECE), BF16)
        columns[:, PIECE:, :] = jnp.zeros((8, 16, PIECE), BF16)
        go_on(2)
        gx.over_x(go_on)
        go_on(2)
        arrived = gx.finish()
        arrived = jnp.concatenate([arrived[:ext], arrived[ext:]], 1)
        gx.release()

        for copy in copies[7:]:
            copy.wait()
        h = h_ref[...]
        gain = gains_ref[1:2]
        extra = arrived[tokens:, :]
        grad_router = extra[:, :tokens] + extra[:, tokens : 2 * tokens]
        grad_router = jnp.transpose(jnp.concatenate([grad_router, jnp.zeros((128 - EXPERTS, tokens), F32)], 0))
        logits = dot(h, wr_ref[...])
        logits = jnp.where(lane_iota(logits.shape) < EXPERTS, logits, MASKED)
        raw = jnp.exp(logits - jnp.max(logits, -1, keepdims=True))
        router = raw / jnp.sum(raw, -1, keepdims=True)
        grad_logits = (router * (grad_router - jnp.sum(router * grad_router, -1, keepdims=True))).astype(BF16)
        go_on()
        grad_h = arrived[:tokens, :] + dot(grad_logits, wr_ref[...], NT)
        normed, scale = norm_parts(middle_ref[...])
        dgain[1:2, :] = jnp.sum(grad_h * normed, 0, keepdims=True)
        for copy in copies[:3]:
            copy.wait()
        grad_mid = cot[...] + norm_back(grad_h * gain, normed, scale)
        grad_middle[...] = grad_mid
        grad_branch = (RESIDUAL * grad_mid).astype(BF16)
        for c in range(n):
            ga[c] = dot(grad_branch, wo[c], NT).astype(BF16)
        ga_exchange = (ga, ga_in, ga_send, ga_recv, local_sems.at[2], n)
        exchange_start(*ga_exchange)
        go_on()
        col[:, :128] = dot(h, grad_logits, TN).astype(BF16)
        for r in range(8):
            at = strip(r)
            dwo = dot(attn[at], grad_branch, TN).astype(BF16)
            small[r, 0:128, :] = dwo[:, :PIECE]
            small[r, 128:256, :] = dwo[:, PIECE:]
            small[r, 256:384, 0:128] = col[pl.ds(pl.multiple_of(at * 128, 128), 128), 0:128]
        ws.start()
        ys.start()
        go_on()
        copies[3].wait()
        for hh in range(2):
            for c in range(n):
                kk, vv = pair_keys(packs[c, hh, :, 128:256].astype(F32))
                at = hh * half + c * rows
                keys[at : at + rows, :] = kk.astype(BF16)
                values[at : at + rows, :] = vv.astype(BF16)
                keys_t[:, at : at + rows] = jnp.transpose(kk).astype(BF16)
        grad_k[...] = jnp.zeros_like(grad_k)
        grad_v[...] = jnp.zeros_like(grad_v)
        go_on()
        ws.over_cores()
        ys.over_cores()
        go_on()
        exchange_wait(*ga_exchange)

        per = BLK // rows
        per_half = blocks // 2

        def fetch_full(b):
            return pltpu.make_async_copy(full_ref.at[b], full_buf.at[lax.rem(b, 2)], full_sems.at[lax.rem(b, 2)])

        fetch_full(jnp.int32(0)).start()
        attend_tick = at_tick[0]

        def attend(block, carry):
            late = block // per_half
            c0 = lax.rem(block, per_half) * per
            q2 = jnp.concatenate([packs[c0 + k, late, :, :128] for k in range(per)], 0)
            q2 = stack_heads((q2.astype(F32) * ATTN_SCALE).astype(BF16))
            g2 = stack_heads(jnp.concatenate([ga_in[c0 + k, pl.ds(pl.multiple_of(late * rows, rows), rows), :] for k in range(per)], 0))
            position, start = query_rows(ends_ref, block, length)
            lse = lse_ref[block]
            shift = jnp.where(start > 0, MASKED, 0.0) - lse

            @pl.when(block + 1 < blocks)
            def _():
                fetch_full(block + 1).start()

            fetch_full(block).wait()
            delta = jnp.sum(jnp.transpose(g2.astype(F32)) * full_buf[lax.rem(block, 2)], 0, keepdims=True)
            acc[...] = jnp.zeros_like(acc)

            def body(kb, whole, carry):
                at = pl.multiple_of(kb * BLK, BLK)
                scores = dot(keys[pl.ds(at, BLK), :], q2, NT)
                if whole:
                    probs = jnp.exp(scores + shift)
                else:
                    where = key_position(kb, length)
                    probs = jnp.where((where <= position) & (where >= start), jnp.exp(scores - lse), 0.0)
                grad_probs = dot(values[pl.ds(at, BLK), :], g2, NT)
                grad_scores = (probs * (grad_probs - delta)).astype(BF16)
                acc[...] += dot(keys_t[:, pl.ds(at, BLK)], grad_scores)
                grad_k[pl.ds(at, BLK), :] += dot(grad_scores, q2)
                grad_v[pl.ds(at, BLK), :] += dot(probs.astype(BF16), g2)

                if not whole:

                    @pl.when((kb == block) & ((block == per_half) | (block == per_half + 1)))
                    def _():
                        tick(attend_tick + 2 + 2 * (block - per_half))

                return carry

            block_loop(block, per_half, body, 0)
            grad_q[pl.ds(pl.multiple_of(block * BLK, BLK), BLK), :] = fold_heads(jnp.transpose(acc[...]))

            @pl.when((block == 1) | (block >= 3))
            def _():
                past = block - per_half
                late_tick = jnp.where(past < 2, 3 + 2 * past, 4 + past)
                tick(attend_tick + jnp.where(block < per_half, block // 2, late_tick))

            return carry

        lax.fori_loop(0, blocks, attend, 0)
        at_tick[0] += blocks
        copies[4].wait()
        for c in range(n):
            for hh in range(2):
                at = slice(hh * half + c * rows, hh * half + (c + 1) * rows)
                kk = grad_k[at, :]
                vv = grad_v[at, :]
                kk = kk + pltpu.roll(kk, 64, 1)
                vv = vv + pltpu.roll(vv, 64, 1)
                both = jnp.where(lane_iota(kk.shape) < 64, kk, vv)
                package = jnp.concatenate([grad_q[at, :] * ATTN_SCALE, both], -1)
                pack_out[c, hh * rows : (hh + 1) * rows, :] = turn(package, table[at, :], -1.0).astype(BF16)
        gr_exchange = (pack_out, grads_in, gr_send, gr_recv, local_sems.at[3], n)
        exchange_start(*gr_exchange)

        def fetch_w(c):
            slot = lax.rem(c, 2)
            at = pl.ds(pl.multiple_of(c * 128, 128), 128)
            return [
                pltpu.make_async_copy(weights_ref.at[1 - k, :, :, at], wbuf.at[slot, :, :, pl.ds(128 * k, 128)], w_sems.at[slot, k])
                for k in range(2)
            ]

        for copy in fetch_w(jnp.int32(0)):
            copy.start()
        go_on()
        ws.over_x()
        ys.over_x()
        go_on(2)
        total[...] = jnp.zeros_like(total)
        late_pieces[:384] = ws.finish().astype(BF16)
        ws.release()
        ffn = ys.finish()
        mixed_ref[...] = middle_ref[...] + RESIDUAL * jnp.concatenate([ffn[:tokens], ffn[tokens:]], 1)
        go_on(3)
        exchange_wait(*gr_exchange)
        copies[5].wait()
        copies[6].wait()

        columns_tick = at_tick[0]

        def finish_columns(c, carry):
            @pl.when(c + 1 < n)
            def _():
                for copy in fetch_w(c + 1):
                    copy.start()

            for copy in fetch_w(c):
                copy.wait()
            slot = lax.rem(c, 2)
            g = grads_in[c]
            col[...] = dot(h_attn[...], g, TN).astype(BF16)
            for r in range(8):
                at = pl.ds(pl.multiple_of(strip(r) * 128, 128), 128)
                columns[r, pl.ds(pl.multiple_of(c // 2 * 128, 128), 128), pl.ds(pl.multiple_of(lax.rem(c, 2) * PACK, PACK), PACK)] = col[at, :]
            for f in range(4):
                total[:, f * shard : (f + 1) * shard] += dot(g, wbuf[slot, f, :shard, :], NT)

            @pl.when(lax.rem(c, 4) == 3)
            def _():
                tick(columns_tick + c // 4)

            return carry

        lax.fori_loop(0, n, finish_columns, 0)
        at_tick[0] += n // 4
        normed, scale = norm_parts(x_in[...])
        grad_h = total[...]
        dgain[0:1, :] = jnp.sum(grad_h * normed, 0, keepdims=True)
        grad_x_ref[...] = grad_middle[...] + norm_back(grad_h * gains_ref[0:1], normed, scale)
        for r in range(8):
            at = pl.ds(pl.multiple_of(strip(r) * 128, 128), 128)
            row = row_iota((16, 128))
            both = jnp.where(row == 0, dgain[0:1, at], jnp.where(row == 1, dgain[1:2, at], 0.0))
            columns[r, PIECE:, 0:128] = both.astype(BF16)
        cs.start()
        go_on()
        cs.over_cores()
        go_on(3)
        cs.over_x(go_on)
        go_on(3)
        summed = cs.finish().astype(BF16)
        late_pieces[PIECE:] = summed[:PIECE]
        late_pieces[384:400] = summed[PIECE:]

    f32, bf = (lambda *shape: pltpu.VMEM(shape, F32)), (lambda *shape: pltpu.VMEM(shape, BF16))
    pl.run_scoped(
        backward,
        bf(*packs_hbm.shape),
        f32(*table_hbm.shape),
        bf(length, 128),
        bf(length, 128),
        bf(128, length),
        f32(length, 128),
        f32(length, 128),
        f32(length, 128),
        f32(128, 2 * BLK),
        f32(2, 128, 2 * BLK),
        bf(n, tokens, 128),
        bf(n, tokens, PACK),
        bf(2, 4, weights_ref.shape[2], PACK),
        f32(tokens, width),
        f32(tokens, width),
        f32(8, width),
        bf(width, PACK),
        bf(8, 384, PIECE),
        bf(8, PIECE + 16, PIECE),
        f32(tokens, width),
        bf(*wo_hbm.shape),
        bf(*attn_hbm.shape),
        f32(tokens, width),
        bf(tokens, width),
        bf(tokens, width),
        f32(tokens, width),
        bf(*wr_hbm.shape),
        f32(*gains_hbm.shape),
        f32(*lse_hbm.shape),
    )

    def rest(t, carry):
        tick(t)
        return carry

    lax.fori_loop(at_tick[0], early, rest, 0)

    def late_source(t):
        return late_pieces.at[pl.ds(pl.multiple_of((t - early) * sub, sub), sub)]

    def late(t, carry):
        line.tick(t, late_source)
        return carry

    lax.fori_loop(early, line.count + LAG_END, late, 0)
    line.finish()


def backward_step(ends, xs, gs, gates, w_gate, w_up, w_down, cxs, rest, diag, full, weights, packs, table, cot, wo, attn, x, h_attn, h, middle, wr, gains, lse, n, length, capp):
    tokens, width = x.shape
    number, slots_rows, _ = xs.shape
    hbm, vmem = pl.BlockSpec(memory_space=pl.ANY), pl.BlockSpec(memory_space=pltpu.VMEM)
    smem = pl.BlockSpec(memory_space=pltpu.SMEM)
    dma = lambda *k: pltpu.SemaphoreType.DMA(k)
    shaped = lambda shape, dtype=BF16: jax.ShapeDtypeStruct(shape, dtype)
    sub = PIECE // 2
    piece = (sub, PIECE)
    count = (number * 6 + 2) * 2
    land_rows = max(2 * (tokens + EXPERTS), PIECE + 16)
    return pl.pallas_call(
        functools.partial(backward_kernel, n, length, capp),
        in_specs=[smem] + [hbm] * 23,
        out_specs=[hbm] * 7 + [vmem, vmem],
        out_shape=[
            shaped((count,) + piece),
            shaped((count,) + piece),
            shaped((number * 6, PIECE, PIECE)),
            shaped(xs.shape),
            shaped(xs.shape),
            shaped((8, 2 * (tokens + EXPERTS), PIECE)),
            shaped((8, 2 * tokens, PIECE)),
            shaped((tokens, width), F32),
            shaped((tokens, width), F32),
        ],
        scratch_shapes=[
            pltpu.VMEM((RING,) + piece, BF16),
            pltpu.VMEM((RING,) + piece, BF16),
            pltpu.VMEM((4,) + piece, BF16),
            pltpu.VMEM((4, land_rows, PIECE), BF16),
            pltpu.VMEM((2, land_rows, PIECE), BF16),
            pltpu.VMEM((land_rows, PIECE), BF16),
            pltpu.VMEM((4, 2 * tokens, PIECE), BF16),
            pltpu.VMEM((2, 2 * tokens, PIECE), BF16),
            pltpu.VMEM((2 * tokens, PIECE), BF16),
            pltpu.VMEM((2, 2 * tokens, PIECE), BF16),
            pltpu.VMEM((2 * PIECE, PIECE), BF16),
            pltpu.VMEM((n, tokens, 128), BF16),
            pltpu.VMEM((n, tokens, PACK), BF16),
            dma(RING),
            dma(RING),
            dma(RING),
            dma(RING),
            dma(RING),
            dma(count),
            dma(RING),
            dma(4),
            dma(n - 1),
            dma(n - 1),
            dma(n - 1),
            dma(n - 1),
            dma(4, 6, 4),
            dma(2),
            pltpu.SemaphoreType.REGULAR((3,)),
            dma(16),
            dma(2),
            dma(2, 2),
            dma(2, 6),
            dma(4),
            dma(2, 2),
            dma(2, 8),
        ],
        compiler_params=params(63, collective_id=0, has_side_effects=True),
        cost_estimate=cost(6e10, 1e9),
        name="backward_step",
    )(ends, xs, gs, gates, w_gate, w_up, w_down, cxs, rest, diag, full, weights, packs, table, cot, wo, attn, x, h_attn, h, middle, wr, gains, lse)


def local(
    inputs,
    cotangent,
    doc_lengths,
    routes,
    attn_gain,
    ffn_gain,
    w_query,
    key_weight,
    value_weight,
    w_out,
    w_router,
    w_gate,
    w_up,
    w_down,
):
    rows = inputs.shape[2]
    width = inputs.shape[3]
    n = lax.axis_size("ctx")
    fsdp = lax.axis_size("fsdp")
    me, mine = lax.axis_index("ctx"), lax.axis_index("fsdp")
    tokens = 2 * rows
    length = tokens * n
    experts_here = w_gate.shape[0]
    number = experts_here // 2
    capacity = 5 * tokens * TOP // (4 * EXPERTS)
    capp = -(-capacity // 16) * 16
    shard = width // fsdp
    heads = QUERY_HEADS // n
    head_lanes = heads * HEAD_DIMENSION
    copies = n // KEY_VALUE_HEADS
    bits = group_bits(fsdp)

    x = inputs.reshape(tokens, width)
    cot = cotangent.reshape(tokens, width)
    side = me % 2
    base = (side * number).astype(jnp.int32).reshape(1)
    first = (mine * experts_here + side * number).astype(jnp.int32).reshape(1)
    index = jnp.stack([side * number, (1 - side) * number]).astype(jnp.int32)
    ends = doc_lengths
    table = jnp.asarray(rotary_table(length))

    out_part = w_out.reshape(shard // head_lanes, head_lanes, width)
    if head_lanes < 128:
        out_part = jnp.pad(out_part, ((0, 0), (0, 128 - head_lanes), (0, 0)))
    merge = lambda a: a.reshape(number, -1, a.shape[-1])

    if n == 8 and fsdp == 4:
        packs, h_attn, weights, wo, wr, cxs, gains = front(
            w_query,
            key_weight,
            value_weight,
            out_part,
            jnp.transpose(w_router),
            jnp.stack([attn_gain, ffn_gain]),
            x,
            table.reshape(2, n, rows, 256),
            jnp.transpose(routes[0], (0, 2, 1)),
            cot,
            capacity,
            n,
        )
        wo, wr = wo.reshape(n, 128, width), wr.reshape(width, 128)
        packs = packs.reshape(n, 2, rows, PACK)
        attn, lse, full, cx_rest = attend(ends, packs, cxs, length)
        middle, h_ffn, attn, xs, gs, gates, diag = mid_step(attn.reshape(n, tokens, 128), cxs, cx_rest, wo, wr, x, gains, number, capp, n)
        own, other, _, _, _, _, _, grad_x, mixed = backward_step(
            ends,
            merge(xs),
            merge(gs),
            merge(gates),
            w_gate,
            w_up,
            w_down,
            cxs,
            cx_rest,
            diag,
            full,
            weights,
            packs,
            table,
            cot,
            wo,
            attn,
            x,
            h_attn,
            h_ffn,
            middle,
            wr,
            gains,
            lse,
            n,
            length,
            capp,
        )
        own, other = own.reshape(-1, PIECE, PIECE), other.reshape(-1, PIECE, PIECE)
        shapes = [w.shape for w in (w_gate, w_up, w_down)]
        outs = tail(index, own, other, mixed, grad_x, shapes, shard)
        return (
            outs[3].reshape(inputs.shape),
            outs[4].reshape(inputs.shape),
            outs[10].reshape(shard),
            outs[11].reshape(shard),
            outs[5],
            outs[6],
            outs[7],
            outs[8],
            jnp.transpose(outs[9]),
            outs[0],
            outs[1],
            outs[2],
        )

    else:
        own_table = lax.dynamic_slice_in_dim(table.reshape(2, n, rows, 256), me, 1, 1).reshape(tokens, 256)
        query_part = w_query.reshape(shard, n, head_lanes)
        if head_lanes < 128:
            query_part = jnp.pad(query_part, ((0, 0), (0, 0), (0, 128 - head_lanes)))
        key_part = jnp.repeat(key_weight.reshape(shard, KEY_VALUE_HEADS, HEAD_DIMENSION), copies, 1)
        value_part = jnp.repeat(value_weight.reshape(shard, KEY_VALUE_HEADS, HEAD_DIMENSION), copies, 1)
        packed = jnp.concatenate([query_part, key_part, value_part], -1).reshape(shard, n * PACK)
        padding = 2 * 16 * (shard // 32 + 1) - shard
        gains = jnp.pad(jnp.stack([attn_gain, ffn_gain]), ((0, padding - 2), (0, n * PACK - shard)))
        packed = jnp.concatenate([packed, gains], 0)
        router_part = jnp.pad(w_router, ((0, 0), (0, 128 - EXPERTS)))
        weights = lax.all_gather(packed, "fsdp", axis=0)
        gain_one = weights[:, shard, :shard].reshape(1, width).astype(F32)
        gain_two = weights[:, shard + 1, :shard].reshape(1, width).astype(F32)
        wo = lax.all_gather(out_part, "fsdp", axis=0, tiled=True)
        wr = lax.all_gather(router_part, "fsdp", axis=0, tiled=True)
        cxs = group_gather(prep(jnp.transpose(routes[0], (0, 2, 1)), cot, capacity), bits)
        packs, h_attn = qkv(x, gain_one, weights, own_table, shard, n)
        packs = lax.all_to_all(packs, "ctx", split_axis=0, concat_axis=0, tiled=True).reshape(n, 2, rows, PACK)
        attn, lse, full = attn_forward(ends, packs, length)
        attn = lax.all_to_all(attn.reshape(n, tokens, 128), "ctx", split_axis=0, concat_axis=0, tiled=True)
        middle, h_ffn = middle_step(attn, wo, x, gain_two)
        xs, gs, gates = gather_rows(first, group_gather(h_ffn, bits), cxs, jnp.transpose(wr), number, capp)
        slots = cxs[:, tokens:]
    xs, gs, gates = merge(xs), merge(gs), merge(gates)
    pieces, outs, back, dgates = expert_step(base, xs, gs, gates, w_gate, w_up, w_down)
    y_part, gx_part = combine(first, slots, outs, back, dgates, tokens, capp)
    pieces = pieces.reshape(number * 6, PIECE, PIECE)
    gx = group_reduce(gx_part, bits)
    grad_middle, dwo, grad_attn, dwr, dgain_two = home_step(gx, h_ffn, middle, cot, wr, wo, gain_two, attn)
    grad_attn = lax.all_to_all(grad_attn, "ctx", split_axis=0, concat_axis=0, tiled=True).reshape(n, 2, rows, 128)
    grads = attn_backward(ends, packs, grad_attn, lse, full, table, length)
    grads = lax.all_to_all(grads.reshape(n, tokens, PACK), "ctx", split_axis=0, concat_axis=0, tiled=True)
    dw, grad_x, dgain_one = final_step(grads, weights, h_attn, x, gain_one, grad_middle, shard)
    mixed = middle + RESIDUAL * group_reduce(y_part, bits).astype(F32)
    own = line_sum(pieces, n)
    other = swap(own, "ctx", 1)
    scatter = lambda a: lax.psum(lax.psum_scatter(a, "fsdp", scatter_dimension=0, tiled=True), "ctx").astype(F32)
    dwo = scatter(dwo)[:, :head_lanes, :].reshape(shard, width)
    small = jnp.concatenate([dwr[:, :EXPERTS], dgain_two.reshape(width, 1).astype(BF16)], 1)
    small = scatter(jnp.pad(small, ((0, 0), (0, 127 - EXPERTS))))
    dwr, dgain_two = small[:, :EXPERTS], small[:, EXPERTS]
    dw = scatter(dw).reshape(shard, n, PACK)
    dgain_one = scatter(dgain_one.reshape(width).astype(BF16))

    outs = widen(index, own, other, [w.shape for w in (w_gate, w_up, w_down)])
    fold = lambda a: a.reshape(shard, KEY_VALUE_HEADS, copies, HEAD_DIMENSION).sum(2).reshape(shard, -1)
    return (
        mixed.reshape(inputs.shape),
        grad_x.reshape(inputs.shape),
        dgain_one,
        dgain_two,
        dw[:, :, :head_lanes].reshape(shard, -1),
        fold(dw[:, :, 128:192]),
        fold(dw[:, :, 192:256]),
        dwo,
        dwr,
        outs[0],
        outs[1],
        outs[2],
    )


def solution(mesh):
    tokens = P("fsdp", None, "ctx", None)
    one, two, three = P("fsdp"), P("fsdp", None), P("fsdp", None, None)
    return jax.shard_map(
        local,
        mesh=mesh,
        in_specs=(tokens, tokens, two, tokens, one, one, two, two, two, two, two, three, three, three),
        out_specs=(tokens, tokens, one, one, two, two, two, two, two, three, three, three),
        check_vma=False,
    )
```

```python
import functools

import jax
import jax.numpy as jnp
import numpy as np
from jax import lax
from jax.experimental import pallas as pl
from jax.experimental.pallas import tpu as pltpu
from jax.sharding import PartitionSpec as P

QUERY_HEADS = 16
KEY_VALUE_HEADS = 8
HEAD_DIMENSION = 64
EXPERTS = 32
TOP = 8

ATTN_SCALE = 0.015625
RESIDUAL = 0.22
NORM_EPS = 1e-06
ROPE_BASE = 10000.0
MASKED = -1e30

F32 = jnp.float32
BF16 = jnp.bfloat16
MIB = 1 << 20
NT = (((1,), (1,)), ((), ()))
TN = (((0,), (0,)), ((), ()))
BLK = 256
PACK = 256


def dot(a, b, dims=None):
    if dims is None:
        return jnp.dot(a, b, preferred_element_type=F32)
    return lax.dot_general(a, b, dims, preferred_element_type=F32)


def params(limit=56, **kw):
    return pltpu.CompilerParams(vmem_limit_bytes=limit * MIB, **kw)


def cost(flops, bytes_accessed):
    return pl.CostEstimate(flops=int(flops), bytes_accessed=int(bytes_accessed), transcendentals=0)


def lane_iota(shape):
    return lax.broadcasted_iota(jnp.int32, shape, len(shape) - 1)


def row_iota(shape):
    return lax.broadcasted_iota(jnp.int32, shape, len(shape) - 2)


def rotary_table(length):
    half = length // 2
    order = np.arange(half, dtype=np.float32)
    positions = np.concatenate([order, length - 1 - order]).astype(np.float32)
    m = np.arange(HEAD_DIMENSION // 2, dtype=np.float64)
    frequency = (ROPE_BASE ** (-2.0 * m / HEAD_DIMENSION)).astype(np.float32)
    angles = (positions[:, None] * frequency[None, :]).astype(np.float64)
    cosine, sine = np.cos(angles), np.sin(angles)
    cos_head = np.concatenate([cosine, cosine], -1)
    sin_head = np.concatenate([-sine, sine], -1)
    return np.concatenate([cos_head, cos_head, sin_head, sin_head], -1).astype(np.float32)


def turn(v, table, direction):
    lanes = lane_iota(v.shape)
    cosine = jnp.concatenate([table[:, :128], table[:, :128]], -1)
    sine = jnp.concatenate([table[:, 128:], table[:, 128:]], -1)
    turned = lanes < 3 * HEAD_DIMENSION
    swapped = jnp.where(lanes % HEAD_DIMENSION < HEAD_DIMENSION // 2, pltpu.roll(v, PACK - 32, 1), pltpu.roll(v, 32, 1))
    return jnp.where(turned, v * cosine + direction * (swapped * sine), v)


def norm_parts(values):
    inv_rms = lax.rsqrt(jnp.mean(values * values, -1, keepdims=True) + NORM_EPS)
    return values * inv_rms, inv_rms


def norm_back(grad_normed, normed, inv_rms):
    return inv_rms * (grad_normed - normed * jnp.mean(grad_normed * normed, -1, keepdims=True))


def prep_kernel(cap, routes_ref, cot_ref, out_ref):
    tokens, width = cot_ref.shape
    earlier = (row_iota((tokens, tokens)) < lane_iota((tokens, tokens))).astype(BF16)
    experts = row_iota((EXPERTS, tokens))
    base = jnp.zeros((EXPERTS, 1), F32)
    plus = jnp.zeros((EXPERTS, tokens), F32)
    for k in range(TOP):
        row = jnp.concatenate([routes_ref[0, k : k + 1, :], routes_ref[1, k : k + 1, :]], 1)
        chosen = experts == row
        ones = chosen.astype(F32)
        slot = dot(ones.astype(BF16), earlier) + base
        plus = plus + jnp.where(chosen & (slot < cap), slot + 1.0, 0.0)
        base = base + jnp.sum(ones, 1, keepdims=True)
    out_ref[:tokens, :] = cot_ref[...].astype(BF16)
    out_ref[tokens:, :] = jnp.concatenate([plus - 1.0, jnp.zeros((EXPERTS, width - tokens), F32)], -1).astype(BF16)


def prep(routes, cot, cap):
    tokens, width = cot.shape
    return pl.pallas_call(
        functools.partial(prep_kernel, cap),
        out_shape=jax.ShapeDtypeStruct((tokens + EXPERTS, width), BF16),
        compiler_params=params(),
        cost_estimate=cost(1e9, 2e6),
        name="prep",
    )(routes, cot)


def qkv_kernel(shard, x_ref, gain_ref, w_ref, table_ref, out_ref, h_ref):
    @pl.when(pl.program_id(0) == 0)
    def _():
        normed, _ = norm_parts(x_ref[...])
        h_ref[...] = (normed * gain_ref[...]).astype(BF16)

    total = None
    for f in range(w_ref.shape[0]):
        part = dot(h_ref[:, f * shard : (f + 1) * shard], w_ref[f, :shard, :])
        total = part if total is None else total + part
    for d in range(out_ref.shape[0]):
        out_ref[d] = turn(total[:, d * PACK : (d + 1) * PACK], table_ref[...], 1.0).astype(BF16)


def qkv(x, gain, weights, table, shard, n):
    tokens, width = x.shape
    fsdp, padded, _ = weights.shape
    return pl.pallas_call(
        functools.partial(qkv_kernel, shard),
        grid=(n // 2,),
        in_specs=[
            pl.BlockSpec((tokens, width), lambda i: (0, 0)),
            pl.BlockSpec((1, width), lambda i: (0, 0)),
            pl.BlockSpec((fsdp, padded, 2 * PACK), lambda i: (0, 0, i)),
            pl.BlockSpec((tokens, 256), lambda i: (0, 0)),
        ],
        out_specs=[
            pl.BlockSpec((2, tokens, PACK), lambda i: (i, 0, 0)),
            pl.BlockSpec((tokens, width), lambda i: (0, 0)),
        ],
        out_shape=[
            jax.ShapeDtypeStruct((n, tokens, PACK), BF16),
            jax.ShapeDtypeStruct((tokens, width), BF16),
        ],
        compiler_params=params(),
        cost_estimate=cost(2 * tokens * width * n * PACK, 8e6),
        name="qkv",
    )(x, gain, weights, table)


def pair_keys(kv):
    other = pltpu.roll(kv, 64, 1)
    low = lane_iota(kv.shape) < 64
    return jnp.where(low, kv, other), jnp.where(low, other, kv)


def stack_heads(q):
    low = lane_iota(q.shape) < 64
    zero = jnp.zeros_like(q)
    return jnp.concatenate([jnp.where(low, q, zero), jnp.where(low, zero, q)], 0)


def fold_heads(stacked):
    rows = stacked.shape[0] // 2
    return jnp.where(lane_iota((rows, 128)) < 64, stacked[:rows], stacked[rows:])


def query_rows(ends_ref, block, length):
    half = length // 2
    lanes = lane_iota((1, 2 * BLK))
    index = block * BLK + jnp.where(lanes < BLK, lanes, lanes - BLK)
    position = jnp.where(index < half, index, length + half - 1 - index)
    start = jnp.zeros_like(position)
    end = 0
    for j in range(3):
        end = end + ends_ref[0, j]
        start = jnp.where(position >= end, jnp.maximum(start, end), start)
    return position, start


def key_position(kb, length):
    half = length // 2
    index = kb * BLK + row_iota((BLK, 1))
    return jnp.where(index < half, index, length + half - 1 - index)


def block_loop(block, per_half, body, init):
    late = block >= per_half
    inner = jnp.where(late, block - per_half, block)

    def plain(kb, carry):
        return body(kb, True, carry)

    def masked(kb, carry):
        return body(kb, False, carry)

    carry = lax.fori_loop(0, jnp.where(late, per_half, inner), plain, init)
    return lax.fori_loop(block, jnp.where(late, 2 * per_half, block + 1), masked, carry)


def attn_forward_kernel(length, ends_ref, q_ref, pack_ref, out_ref, lse_ref, full_ref, keys, values_t, acc):
    block = pl.program_id(0)
    half = length // 2
    n, _, rows, _ = pack_ref.shape

    @pl.when(block == 0)
    def _():
        for h in range(2):
            for c in range(n):
                kk, vv = pair_keys(pack_ref[c, h, :, 128:256].astype(F32))
                at = h * half + c * rows
                keys[at : at + rows, :] = kk.astype(BF16)
                if rows % 128 == 0:
                    values_t[:, at : at + rows] = jnp.transpose(vv).astype(BF16)
        if rows % 128 != 0:
            for h in range(2):
                for c in range(0, n, 2):
                    pair = jnp.concatenate([pack_ref[c, h, :, 128:256], pack_ref[c + 1, h, :, 128:256]], 0)
                    _, vv = pair_keys(pair.astype(F32))
                    at = h * half + c * rows
                    values_t[:, at : at + 2 * rows] = jnp.transpose(vv).astype(BF16)

    q = q_ref[...].reshape(BLK, PACK)[:, :128]
    q2 = stack_heads((q.astype(F32) * ATTN_SCALE).astype(BF16))
    position, start = query_rows(ends_ref, block, length)
    bias = jnp.where(start > 0, MASKED, 0.0)
    acc[...] = jnp.zeros_like(acc)

    def body(kb, whole, carry):
        peak, total = carry
        at = pl.multiple_of(kb * BLK, BLK)
        scores = dot(keys[pl.ds(at, BLK), :], q2, NT)
        if whole:
            scores = scores + bias
        else:
            where = key_position(kb, length)
            scores = jnp.where((where <= position) & (where >= start), scores, MASKED)
        new_peak = jnp.maximum(peak, jnp.max(scores, 0, keepdims=True))
        weights = jnp.exp(scores - new_peak)
        fade = jnp.exp(peak - new_peak)
        total = total * fade + jnp.sum(weights, 0, keepdims=True)
        acc[...] = acc[...] * fade + dot(values_t[:, pl.ds(at, BLK)], weights.astype(BF16))
        return new_peak, total

    init = (jnp.full((1, 2 * BLK), MASKED, F32), jnp.zeros((1, 2 * BLK), F32))
    peak, total = block_loop(block, half // BLK, body, init)
    result = acc[...] / total
    full_ref[0] = result
    lse_ref[0] = peak + jnp.log(total)
    if out_ref is not None:
        folded = fold_heads(jnp.transpose(result)).astype(BF16)
        out_ref[...] = folded.reshape(out_ref.shape)


def attn_forward(ends, packs, length):
    n, _, rows, _ = packs.shape
    blocks, per = length // BLK, BLK // rows
    per_half = blocks // 2
    tiles = lambda i, ends: (lax.rem(i, per_half), i // per_half, 0, 0)
    return pl.pallas_call(
        functools.partial(attn_forward_kernel, length),
        grid_spec=pltpu.PrefetchScalarGridSpec(
            num_scalar_prefetch=1,
            grid=(blocks,),
            in_specs=[
                pl.BlockSpec((per, 1, rows, PACK), tiles),
                pl.BlockSpec(packs.shape, lambda i, ends: (0, 0, 0, 0)),
            ],
            out_specs=[
                pl.BlockSpec((per, 1, rows, 128), tiles),
                pl.BlockSpec((1, 1, 2 * BLK), lambda i, ends: (i, 0, 0)),
                pl.BlockSpec((1, 128, 2 * BLK), lambda i, ends: (i, 0, 0)),
            ],
            scratch_shapes=[
                pltpu.VMEM((length, 128), BF16),
                pltpu.VMEM((128, length), BF16),
                pltpu.VMEM((128, 2 * BLK), F32),
            ],
        ),
        out_shape=[
            jax.ShapeDtypeStruct((n, 2, rows, 128), BF16),
            jax.ShapeDtypeStruct((blocks, 1, 2 * BLK), F32),
            jax.ShapeDtypeStruct((blocks, 128, 2 * BLK), F32),
        ],
        compiler_params=params(),
        cost_estimate=cost(1.5e10, 6e6),
        name="attn_forward",
    )(ends, packs, packs)


def attn_backward_kernel(length, ends_ref, q_ref, g_ref, pack_ref, lse_ref, full_ref, table_ref, out_ref, keys, values, keys_t, grad_q, grad_k, grad_v, acc):
    block = pl.program_id(0)
    half = length // 2
    n, _, rows, _ = pack_ref.shape

    @pl.when(block == 0)
    def _():
        for h in range(2):
            for c in range(n):
                kk, vv = pair_keys(pack_ref[c, h, :, 128:256].astype(F32))
                at = h * half + c * rows
                keys[at : at + rows, :] = kk.astype(BF16)
                values[at : at + rows, :] = vv.astype(BF16)
        for b in range(length // BLK):
            keys_t[:, b * BLK : (b + 1) * BLK] = jnp.transpose(keys[b * BLK : (b + 1) * BLK, :].astype(F32)).astype(BF16)
        grad_k[...] = jnp.zeros_like(grad_k)
        grad_v[...] = jnp.zeros_like(grad_v)

    q2 = stack_heads((q_ref[...].reshape(BLK, PACK)[:, :128].astype(F32) * ATTN_SCALE).astype(BF16))
    g2 = stack_heads(g_ref[...].reshape(BLK, 128))
    position, start = query_rows(ends_ref, block, length)
    lse = lse_ref[0]
    shift = jnp.where(start > 0, MASKED, 0.0) - lse
    delta = jnp.sum(jnp.transpose(g2.astype(F32)) * full_ref[0], 0, keepdims=True)
    acc[...] = jnp.zeros_like(acc)

    def body(kb, whole, carry):
        at = pl.multiple_of(kb * BLK, BLK)
        scores = dot(keys[pl.ds(at, BLK), :], q2, NT)
        if whole:
            probs = jnp.exp(scores + shift)
        else:
            where = key_position(kb, length)
            probs = jnp.where((where <= position) & (where >= start), jnp.exp(scores - lse), 0.0)
        grad_probs = dot(values[pl.ds(at, BLK), :], g2, NT)
        grad_scores = (probs * (grad_probs - delta)).astype(BF16)
        acc[...] += dot(keys_t[:, pl.ds(at, BLK)], grad_scores)
        grad_k[pl.ds(at, BLK), :] += dot(grad_scores, q2)
        grad_v[pl.ds(at, BLK), :] += dot(probs.astype(BF16), g2)
        return carry

    block_loop(block, half // BLK, body, 0)
    grad_q[pl.ds(pl.multiple_of(block * BLK, BLK), BLK), :] = fold_heads(jnp.transpose(acc[...]))

    @pl.when(block == length // BLK - 1)
    def _():
        for h in range(2):
            for c in range(n):
                at = slice(h * half + c * rows, h * half + (c + 1) * rows)
                kk = grad_k[at, :]
                vv = grad_v[at, :]
                kk = kk + pltpu.roll(kk, 64, 1)
                vv = vv + pltpu.roll(vv, 64, 1)
                both = jnp.where(lane_iota(kk.shape) < 64, kk, vv)
                package = jnp.concatenate([grad_q[at, :] * ATTN_SCALE, both], -1)
                out_ref[c, h] = turn(package, table_ref[at, :], -1.0).astype(BF16)


def attn_backward(ends, packs, grads, lse, full, table, length):
    n, _, rows, _ = packs.shape
    blocks, per = length // BLK, BLK // rows
    per_half = blocks // 2
    tiles = lambda i, ends: (lax.rem(i, per_half), i // per_half, 0, 0)
    return pl.pallas_call(
        functools.partial(attn_backward_kernel, length),
        grid_spec=pltpu.PrefetchScalarGridSpec(
            num_scalar_prefetch=1,
            grid=(blocks,),
            in_specs=[
                pl.BlockSpec((per, 1, rows, PACK), tiles),
                pl.BlockSpec((per, 1, rows, 128), tiles),
                pl.BlockSpec(packs.shape, lambda i, ends: (0, 0, 0, 0)),
                pl.BlockSpec((1, 1, 2 * BLK), lambda i, ends: (i, 0, 0)),
                pl.BlockSpec((1, 128, 2 * BLK), lambda i, ends: (i, 0, 0)),
                pl.BlockSpec(table.shape, lambda i, ends: (0, 0)),
            ],
            out_specs=pl.BlockSpec(packs.shape, lambda i, ends: (0, 0, 0, 0)),
            scratch_shapes=[
                pltpu.VMEM((length, 128), BF16),
                pltpu.VMEM((length, 128), BF16),
                pltpu.VMEM((128, length), BF16),
                pltpu.VMEM((length, 128), F32),
                pltpu.VMEM((length, 128), F32),
                pltpu.VMEM((length, 128), F32),
                pltpu.VMEM((128, 2 * BLK), F32),
            ],
        ),
        out_shape=jax.ShapeDtypeStruct(packs.shape, BF16),
        compiler_params=params(),
        cost_estimate=cost(3e10, 8e6),
        name="attn_backward",
    )(ends, packs, grads, packs, lse, full, table)


def middle_kernel(attn_ref, wo_ref, x_ref, gain_ref, middle_ref, h_ref):
    total = None
    for c in range(attn_ref.shape[0]):
        part = dot(attn_ref[c], wo_ref[c])
        total = part if total is None else total + part
    middle = x_ref[...] + RESIDUAL * total
    middle_ref[...] = middle
    normed, _ = norm_parts(middle)
    h_ref[...] = (normed * gain_ref[...]).astype(BF16)


def middle_step(attn, wo, x, gain):
    tokens, width = x.shape
    return pl.pallas_call(
        middle_kernel,
        out_shape=[jax.ShapeDtypeStruct((tokens, width), F32), jax.ShapeDtypeStruct((tokens, width), BF16)],
        compiler_params=params(),
        cost_estimate=cost(2 * tokens * width * width, 5e6),
        name="middle",
    )(attn, wo, x, gain)


def own_row(table, row):
    return jnp.sum(jnp.where(row_iota(table.shape) == row, table, 0.0), 0, keepdims=True)


def one_hot(slots, first, number, capp):
    tokens = slots.shape[1]
    order = row_iota((capp, tokens)).astype(F32)
    return [(order == own_row(slots, first + j)).astype(F32) for j in range(number)]


def gather_kernel(number, capp, first_ref, h_ref, cx_ref, wrt_ref, x_ref, g_ref, gate_ref):
    tokens = h_ref.shape[1]
    first = first_ref[0]
    h = h_ref[0]
    slots = cx_ref[0, tokens:, :tokens].astype(F32)
    logits = dot(wrt_ref[...], h, NT)[:EXPERTS, :]
    raw = jnp.exp(logits - jnp.max(logits, 0, keepdims=True))
    router = raw / jnp.sum(raw, 0, keepdims=True)
    hots = one_hot(slots, first, number, capp)
    places = jnp.concatenate(hots, 0).astype(BF16)
    rows = dot(places, h).astype(BF16)
    grads = dot(places, cx_ref[0, :tokens, :]).astype(BF16)
    for j in range(number):
        at = slice(j * capp, (j + 1) * capp)
        x_ref[j, 0] = rows[at]
        g_ref[j, 0] = grads[at]
        gate = jnp.sum(hots[j] * own_row(router, first + j), 1, keepdims=True)
        gate_ref[j, 0] = jnp.broadcast_to(gate, (capp, 128))


def gather_rows(first, hs, cxs, wrt, number, capp):
    nb, tokens, width = hs.shape
    return pl.pallas_call(
        functools.partial(gather_kernel, number, capp),
        grid_spec=pltpu.PrefetchScalarGridSpec(
            num_scalar_prefetch=1,
            grid=(nb,),
            in_specs=[
                pl.BlockSpec((1, tokens, width), lambda b, f: (b, 0, 0)),
                pl.BlockSpec((1, tokens + EXPERTS, width), lambda b, f: (b, 0, 0)),
                pl.BlockSpec(wrt.shape, lambda b, f: (0, 0)),
            ],
            out_specs=[
                pl.BlockSpec((number, 1, capp, width), lambda b, f: (0, b, 0, 0)),
                pl.BlockSpec((number, 1, capp, width), lambda b, f: (0, b, 0, 0)),
                pl.BlockSpec((number, 1, capp, 128), lambda b, f: (0, b, 0, 0)),
            ],
        ),
        out_shape=[
            jax.ShapeDtypeStruct((number, nb, capp, width), BF16),
            jax.ShapeDtypeStruct((number, nb, capp, width), BF16),
            jax.ShapeDtypeStruct((number, nb, capp, 128), F32),
        ],
        compiler_params=params(),
        cost_estimate=cost(4 * nb * number * capp * tokens * width, 2e7),
        name="gather_rows",
    )(first, hs, cxs, wrt)


PIECE = 512


def expert_kernel(base_ref, x_ref, g_ref, gate_ref, wg_ref, wu_ref, wd_ref, piece_ref, out_ref, rows_ref, dg_ref):
    x = x_ref[0]
    gate = gate_ref[0][:, :1]
    grad_ffn = RESIDUAL * g_ref[0].astype(F32)
    go = (gate * grad_ffn).astype(BF16)
    part = wg_ref.shape[2] // 2
    out = rows = None
    for chunk in range(2):
        at = slice(chunk * part, (chunk + 1) * part)
        wg, wu, wd = wg_ref[0, :, at], wu_ref[0, :, at], wd_ref[0, at, :]
        pre_gate = dot(x, wg)
        pre_up = dot(x, wu)
        sig = jax.nn.sigmoid(pre_gate)
        hidden = (pre_gate * sig * pre_up).astype(BF16)
        out_part = dot(hidden, wd)
        grad_hidden = dot(go, wd, NT)
        grad_gate = (grad_hidden * pre_up * sig * (1.0 + pre_gate * (1.0 - sig))).astype(BF16)
        grad_up = (grad_hidden * pre_gate * sig).astype(BF16)
        row_part = dot(grad_gate, wg, NT) + dot(grad_up, wu, NT)
        dwg = dot(x, grad_gate, TN).astype(BF16)
        dwu = dot(x, grad_up, TN).astype(BF16)
        dwd = dot(hidden, go, TN).astype(BF16)
        for half in range(2):
            side = slice(half * PIECE, (half + 1) * PIECE)
            piece_ref[0, 3 * chunk + half, :, :part] = dwg[side]
            piece_ref[0, 3 * chunk + half, :, part:] = dwu[side]
            piece_ref[0, 3 * chunk + 2, half * part : (half + 1) * part, :] = dwd[:, side]
        out = out_part if out is None else out + out_part
        rows = row_part if rows is None else rows + row_part
    out = out.astype(BF16).astype(F32)
    out_ref[0] = (gate * out).astype(BF16)
    rows_ref[0] = rows.astype(BF16)
    grad = jnp.sum(grad_ffn * out, 1, keepdims=True)
    dg_ref[0] = jnp.broadcast_to(grad, dg_ref.shape[1:])


def expert_step(base, xs, gs, gates, w_gate, w_up, w_down):
    number, rows, width = xs.shape
    ff = w_gate.shape[2]
    row = lambda e, b: (e, 0, 0)
    weight = lambda e, b: (b[0] + e, 0, 0)
    return pl.pallas_call(
        expert_kernel,
        grid_spec=pltpu.PrefetchScalarGridSpec(
            num_scalar_prefetch=1,
            grid=(number,),
            in_specs=[
                pl.BlockSpec((1, rows, width), row),
                pl.BlockSpec((1, rows, width), row),
                pl.BlockSpec((1, rows, 128), row),
                pl.BlockSpec((1, width, ff), weight),
                pl.BlockSpec((1, width, ff), weight),
                pl.BlockSpec((1, ff, width), weight),
            ],
            out_specs=[
                pl.BlockSpec((1, 6, PIECE, PIECE), lambda e, b: (e, 0, 0, 0)),
                pl.BlockSpec((1, rows, width), row),
                pl.BlockSpec((1, rows, width), row),
                pl.BlockSpec((1, rows, 128), row),
            ],
        ),
        out_shape=[
            jax.ShapeDtypeStruct((number, 6, PIECE, PIECE), BF16),
            jax.ShapeDtypeStruct((number, rows, width), BF16),
            jax.ShapeDtypeStruct((number, rows, width), BF16),
            jax.ShapeDtypeStruct((number, rows, 128), F32),
        ],
        compiler_params=params(60),
        cost_estimate=cost(18 * number * rows * width * ff, 5e7),
        name="expert_step",
    )(base, xs, gs, gates, w_gate, w_up, w_down)


def combine_kernel(number, capp, first_ref, slot_ref, outs, rows, grads, y_ref, gx_ref):
    tokens = y_ref.shape[1]
    width = y_ref.shape[2]
    first = first_ref[0]
    slots = slot_ref[0][:, :tokens].astype(F32)
    hots = one_hot(slots, first, number, capp)
    places = jnp.concatenate(hots, 0).astype(BF16)
    y_ref[0] = dot(places, outs[:, 0].reshape(number * capp, width), TN).astype(BF16)
    gx_ref[0, :tokens] = dot(places, rows[:, 0].reshape(number * capp, width), TN).astype(BF16)
    extra = jnp.zeros((EXPERTS, 2 * tokens), F32)
    for j in range(number):
        grad = jnp.sum(hots[j] * grads[j, 0][:, :1], 0, keepdims=True)
        high = grad.astype(BF16).astype(F32)
        both = jnp.concatenate([high, grad - high], 1)
        extra = jnp.where(row_iota(extra.shape) == first + j, both, extra)
    rest = jnp.zeros((EXPERTS, width - 2 * tokens), F32)
    gx_ref[0, tokens:] = jnp.concatenate([extra, rest], 1).astype(BF16)


def combine(first, slots, outs, rows, grads, tokens, capp):
    number = outs.shape[0]
    nb, _, width = slots.shape
    split = lambda a: a.reshape(number, nb, capp, a.shape[-1])
    wide = pl.BlockSpec((number, 1, capp, width), lambda b, f: (0, b, 0, 0))
    thin = pl.BlockSpec((number, 1, capp, 128), lambda b, f: (0, b, 0, 0))
    return pl.pallas_call(
        functools.partial(combine_kernel, number, capp),
        grid_spec=pltpu.PrefetchScalarGridSpec(
            num_scalar_prefetch=1,
            grid=(nb,),
            in_specs=[pl.BlockSpec((1, EXPERTS, width), lambda b, f: (b, 0, 0))] + [wide, wide, thin],
            out_specs=[
                pl.BlockSpec((1, tokens, width), lambda b, f: (b, 0, 0)),
                pl.BlockSpec((1, tokens + EXPERTS, width), lambda b, f: (b, 0, 0)),
            ],
        ),
        out_shape=[
            jax.ShapeDtypeStruct((nb, tokens, width), BF16),
            jax.ShapeDtypeStruct((nb, tokens + EXPERTS, width), BF16),
        ],
        compiler_params=params(),
        cost_estimate=cost(4 * nb * number * capp * tokens * width, 2e7),
        name="combine",
    )(first, slots, split(outs), split(rows), split(grads))


def home_kernel(gx_ref, h_ref, middle_ref, cot_ref, wr_ref, wo_ref, gain_ref, attn_ref, grad_middle_ref, dwo_ref, ga_ref, dwr_ref, dgain_ref):
    tokens, width = h_ref.shape
    h = h_ref[...]
    gain = gain_ref[...]
    extra = gx_ref[tokens:, :].astype(F32)
    grad_router = extra[:, :tokens] + extra[:, tokens : 2 * tokens]
    grad_router = jnp.transpose(jnp.concatenate([grad_router, jnp.zeros((128 - EXPERTS, tokens), F32)], 0))
    logits = dot(h, wr_ref[...])
    logits = jnp.where(lane_iota(logits.shape) < EXPERTS, logits, MASKED)
    raw = jnp.exp(logits - jnp.max(logits, -1, keepdims=True))
    router = raw / jnp.sum(raw, -1, keepdims=True)
    grad_logits = (router * (grad_router - jnp.sum(router * grad_router, -1, keepdims=True))).astype(BF16)
    dwr_ref[...] = dot(h, grad_logits, TN).astype(BF16)
    grad_h = gx_ref[:tokens, :].astype(F32) + dot(grad_logits, wr_ref[...], NT)
    normed, scale = norm_parts(middle_ref[...])
    dgain_ref[...] = jnp.sum(grad_h * normed, 0, keepdims=True)
    grad_middle = cot_ref[...] + norm_back(grad_h * gain, normed, scale)
    grad_middle_ref[...] = grad_middle
    grad_branch = (RESIDUAL * grad_middle).astype(BF16)
    for c in range(attn_ref.shape[0]):
        dwo_ref[c] = dot(attn_ref[c], grad_branch, TN).astype(BF16)
        ga_ref[c] = dot(grad_branch, wo_ref[c], NT).astype(BF16)


def home_step(gx, h, middle, cot, wr, wo, gain, attn):
    tokens, width = h.shape
    n = attn.shape[0]
    return pl.pallas_call(
        home_kernel,
        out_shape=[
            jax.ShapeDtypeStruct((tokens, width), F32),
            jax.ShapeDtypeStruct((n, 128, width), BF16),
            jax.ShapeDtypeStruct((n, tokens, 128), BF16),
            jax.ShapeDtypeStruct((width, 128), BF16),
            jax.ShapeDtypeStruct((1, width), F32),
        ],
        compiler_params=params(),
        cost_estimate=cost(4 * tokens * width * width, 1e7),
        name="home_step",
    )(gx, h, middle, cot, wr, wo, gain, attn)


def final_kernel(shard, grads_ref, w_ref, h_ref, x_ref, gain_ref, grad_middle_ref, dw_ref, grad_x_ref, dgain_ref, total):
    c = pl.program_id(0)
    g = grads_ref[0]
    dw_ref[...] = dot(h_ref[...], g, TN).astype(BF16)

    @pl.when(c == 0)
    def _():
        total[...] = jnp.zeros_like(total)

    for f in range(w_ref.shape[0]):
        total[:, f * shard : (f + 1) * shard] += dot(g, w_ref[f, :shard, :], NT)

    @pl.when(c == pl.num_programs(0) - 1)
    def _():
        normed, scale = norm_parts(x_ref[...])
        grad_h = total[...]
        dgain_ref[...] = jnp.sum(grad_h * normed, 0, keepdims=True)
        grad_x_ref[...] = grad_middle_ref[...] + norm_back(grad_h * gain_ref[...], normed, scale)


def final_step(grads, weights, h, x, gain, grad_middle, shard):
    n, tokens, _ = grads.shape
    width = x.shape[1]
    fsdp, padded, _ = weights.shape
    same = lambda c: (0, 0)
    return pl.pallas_call(
        functools.partial(final_kernel, shard),
        grid=(n,),
        in_specs=[
            pl.BlockSpec((1, tokens, PACK), lambda c: (c, 0, 0)),
            pl.BlockSpec((fsdp, padded, PACK), lambda c: (0, 0, c)),
            pl.BlockSpec((tokens, width), same),
            pl.BlockSpec((tokens, width), same),
            pl.BlockSpec((1, width), same),
            pl.BlockSpec((tokens, width), same),
        ],
        out_specs=[
            pl.BlockSpec((width, PACK), lambda c: (0, c)),
            pl.BlockSpec((tokens, width), same),
            pl.BlockSpec((1, width), same),
        ],
        out_shape=[
            jax.ShapeDtypeStruct((width, n * PACK), BF16),
            jax.ShapeDtypeStruct((tokens, width), F32),
            jax.ShapeDtypeStruct((1, width), F32),
        ],
        scratch_shapes=[pltpu.VMEM((tokens, width), F32)],
        compiler_params=params(),
        cost_estimate=cost(4 * tokens * width * n * PACK, 1.2e7),
        name="final_step",
    )(grads, weights, h, x, gain, grad_middle)


def widen_kernel(number, index_ref, own_ref, other_ref, gate_ref, up_ref, down_ref):
    part = gate_ref.shape[2] // 2

    def write(ref):
        for chunk in range(2):
            columns = slice(chunk * part, (chunk + 1) * part)
            for half in range(2):
                at = slice(half * PIECE, (half + 1) * PIECE)
                gate_ref[0, at, columns] = ref[3 * chunk + half, :, :part].astype(F32)
                up_ref[0, at, columns] = ref[3 * chunk + half, :, part:].astype(F32)
                down_ref[0, columns, at] = ref[3 * chunk + 2, half * part : (half + 1) * part, :].astype(F32)

    @pl.when(pl.program_id(0) == 0)
    def _():
        write(own_ref)

    @pl.when(pl.program_id(0) == 1)
    def _():
        write(other_ref)


def tail_kernel(number, index_ref, own_ref, other_ref, own_small_ref, other_small_ref, mixed_in, grad_in, gate_ref, up_ref, down_ref, mixed_ref, grad_ref, dwq_ref, dwk_ref, dwv_ref, dwo_ref, dwr_ref, g1_ref, g2_ref):
    widen_kernel(number, index_ref, own_ref, other_ref, gate_ref, up_ref, down_ref)
    mixed_ref[...] = mixed_in[...]
    grad_ref[...] = grad_in[...]

    @pl.when((pl.program_id(0) == 0) & (pl.program_id(1) == 0))
    def _():
        for which, ref in enumerate((own_small_ref, other_small_ref)):
            part = index_ref[which] // number
            at = pl.ds(pl.multiple_of(part * 128, 128), 128)
            for q in range(4):
                block = ref[1, q * 128 : (q + 1) * 128, :].astype(F32)
                dwq_ref[at, q * 256 : q * 256 + 128] = block[:, :128]
                dwq_ref[at, q * 256 + 128 : (q + 1) * 256] = block[:, 256:384]
                one, two = block[:, 128:256], block[:, 384:]
                low = lane_iota(one.shape) < HEAD_DIMENSION
                dwk_ref[at, q * 128 : (q + 1) * 128] = jnp.where(low, one, pltpu.roll(two, 64, 1))
                dwv_ref[at, q * 128 : (q + 1) * 128] = jnp.where(low, pltpu.roll(one, 64, 1), two)
            dwo_ref[at, :PIECE] = ref[0, 0:128, :].astype(F32)
            dwo_ref[at, PIECE:] = ref[0, 128:256, :].astype(F32)
            dwr_ref[:, at] = jnp.transpose(ref[0, 256:384, :128].astype(F32))[:EXPERTS]
            gains = ref[0, 384:400, :128].astype(F32)
            g1_ref[pl.ds(part, 1), :] = gains[0:1]
            g2_ref[pl.ds(part, 1), :] = gains[1:2]


def expert_specs(number, shapes):
    last = number - 1
    ins = [
        pl.BlockSpec((6, PIECE, PIECE), lambda s, e, at: (jnp.where(s == 0, e, last), 0, 0)),
        pl.BlockSpec((6, PIECE, PIECE), lambda s, e, at: (jnp.where(s == 0, 0, e), 0, 0)),
    ]
    outs = [pl.BlockSpec((1,) + tuple(shape[1:]), lambda s, e, at: (at[s] + e, 0, 0)) for shape in shapes]
    return ins, outs, [jax.ShapeDtypeStruct(shape, F32) for shape in shapes]


def widen(index, own, other, shapes):
    number = shapes[0][0] // 2
    ins, outs, out_shapes = expert_specs(number, shapes)
    return pl.pallas_call(
        functools.partial(widen_kernel, number),
        grid_spec=pltpu.PrefetchScalarGridSpec(num_scalar_prefetch=1, grid=(2, number), in_specs=ins, out_specs=outs),
        out_shape=out_shapes,
        compiler_params=params(),
        cost_estimate=cost(0, 1e8),
        name="widen",
    )(index, own, other)


def tail(index, own, other, mixed, grad_x, shapes, shard):
    number = shapes[0][0] // 2
    tokens, width = mixed.shape
    ins, outs, out_shapes = expert_specs(number, shapes)
    small = pl.BlockSpec((2, PIECE, PIECE), lambda s, e, at: (3 * number, 0, 0))
    rows = pl.BlockSpec((tokens // (2 * number), width), lambda s, e, at: (s * number + e, 0))
    small_shapes = [(shard, width), (shard, width // 2), (shard, width // 2), (shard, width), (EXPERTS, shard), (2, 128), (2, 128)]
    whole = [pl.BlockSpec(shape, lambda s, e, at: (0, 0)) for shape in small_shapes]
    return pl.pallas_call(
        functools.partial(tail_kernel, number),
        grid_spec=pltpu.PrefetchScalarGridSpec(
            num_scalar_prefetch=1,
            grid=(2, number),
            in_specs=ins + [small, small, rows, rows],
            out_specs=outs + [rows, rows] + whole,
        ),
        out_shape=out_shapes
        + [jax.ShapeDtypeStruct((tokens, width), F32)] * 2
        + [jax.ShapeDtypeStruct(shape, F32) for shape in small_shapes],
        compiler_params=params(),
        cost_estimate=cost(0, 1e8),
        name="tail",
    )(index, own, other, own, other, mixed, grad_x)


def swap(value, axis, bit):
    size = lax.axis_size(axis)
    return lax.ppermute(value, axis, [(i, i ^ bit) for i in range(size)])


def group_bits(fsdp):
    bits = [("fsdp", 1 << b) for b in range(1, fsdp.bit_length() - 1)]
    return bits + [("ctx", 1), ("fsdp", 1)]


def group_gather(value, bits):
    stacked = value[None]
    for axis, bit in bits:
        stacked = jnp.concatenate([stacked, swap(stacked, axis, bit)], 0)
    return stacked


def group_reduce(stacked, bits):
    for axis, bit in reversed(bits):
        half = stacked.shape[0] // 2
        arrived = swap(stacked[half:], axis, bit)
        stacked = (stacked[:half].astype(F32) + arrived.astype(F32)).astype(stacked.dtype)
    return stacked[0]


def line_sum(value, ctx):
    pairs = ctx // 2
    if pairs != 4:
        bit = 2
        while bit < ctx:
            value = value + swap(value, "ctx", bit)
            bit *= 2
        return value
    at = lambda z, y: 2 * z + y
    inward = [(at(0, y), at(1, y)) for y in range(2)] + [(at(3, y), at(2, y)) for y in range(2)]
    across = [(at(1, y), at(2, y)) for y in range(2)] + [(at(2, y), at(1, y)) for y in range(2)]
    outward = [(b, a) for a, b in inward]
    value = value + lax.ppermute(value, "ctx", inward)
    value = value + lax.ppermute(value, "ctx", across)
    arrived = lax.ppermute(value, "ctx", outward)
    z = lax.axis_index("ctx") // 2
    return jnp.where((z == 0) | (z == 3), arrived, value)


MESH = pl.DeviceIdType.MESH


def flip(index, bit):
    return jnp.where((index // bit) % 2 == 0, index + bit, index - bit)


def send(src, dst, send_sem, recv_sem, device):
    return pltpu.make_async_remote_copy(src_ref=src, dst_ref=dst, send_sem=send_sem, recv_sem=recv_sem, device_id=device, device_id_type=MESH)


def neighbours():
    ctx, fsdp = lax.axis_index("ctx"), lax.axis_index("fsdp")
    side, across = flip(ctx, 1), flip(fsdp, 2)
    core = {"fsdp": flip(fsdp, 1)}
    return core, [{"fsdp": across}, {"ctx": side}, {"ctx": side, "fsdp": across}]


def greet(devices):
    barrier = pltpu.get_barrier_semaphore()
    for device in devices:
        pl.semaphore_signal(barrier, inc=1, device_id=device, device_id_type=MESH)
    pl.semaphore_wait(barrier, len(devices))


def others(n):
    ctx = lax.axis_index("ctx")
    return [lax.rem(ctx + d, n) for d in range(1, n)]


def exchange_start(src, dst, send_sems, recv_sems, local_sem, n):
    ctx = lax.axis_index("ctx")
    for d, c in enumerate(others(n)):
        send(src.at[c], dst.at[ctx], send_sems.at[d], recv_sems.at[d], {"ctx": c}).start()
    pltpu.make_async_copy(src.at[ctx], dst.at[ctx], local_sem).start()


def exchange_wait(src, dst, send_sems, recv_sems, local_sem, n, arrived=None):
    ctx = lax.axis_index("ctx")
    pltpu.make_async_copy(src.at[ctx], dst.at[ctx], local_sem).wait()
    if arrived is not None:
        arrived(ctx)
    for d in range(n - 1):
        source = lax.rem(ctx + n - 1 - d, n)
        send(src.at[source], dst.at[source], send_sems.at[d], recv_sems.at[d], {"ctx": source}).wait_recv()
        if arrived is not None:
            arrived(source)
    for d, c in enumerate(others(n)):
        send(src.at[c], dst.at[ctx], send_sems.at[d], recv_sems.at[d], {"ctx": c}).wait_send()


def turn_half(v, table, direction, lanes_turned):
    lanes = lane_iota(v.shape)
    swapped = jnp.where(lanes % HEAD_DIMENSION < HEAD_DIMENSION // 2, pltpu.roll(v, 96, 1), pltpu.roll(v, 32, 1))
    return jnp.where(lanes < lanes_turned, v * table[:, :128] + direction * (swapped * table[:, 128:]), v)


def front_kernel(n, cap, wq_ref, wk_ref, wv_ref, wo_part_ref, wr_raw_ref, gain_ref, x_ref, table_ref, routes_ref, cot_ref, packs_ref, h_ref, weights_ref, wo_ref, wr_ref, cxs_ref, gains_ref, wall, packed_ref, wr_part_ref, cx, table, normed_ref, total, out, exch_send, exch_recv, full_send, full_recv, x_send, x_recv, y_send, y_recv, xs_send, xs_recv, ys_send, ys_recv, cx_send, cx_recv, local_sems):
    tokens, width = x_ref.shape
    shard = width // 4
    ctx, fsdp = lax.axis_index("ctx"), lax.axis_index("fsdp")
    parity = lax.rem(ctx, 2)
    core, group = neighbours()
    far, near = group[0], group[1]
    sibling, distant = flip(fsdp, 1), flip(fsdp, 2)
    other = flip(distant, 1)
    for k in range(2):
        pltpu.make_async_copy(table_ref.at[k, ctx], table.at[k], local_sems.at[6 + k]).start()

    pair = HEAD_DIMENSION * 2
    for c in range(0, n, 2):
        keys, values = wk_ref[:, c // 2 * pair : (c // 2 + 1) * pair].astype(F32), wv_ref[:, c // 2 * pair : (c // 2 + 1) * pair].astype(F32)
        low = lane_iota(keys.shape) < HEAD_DIMENSION
        packed_ref[0, :shard, c * 128 : (c + 1) * 128] = jnp.where(low, keys, pltpu.roll(values, 64, 1)).astype(BF16)
        packed_ref[0, :shard, (c + 1) * 128 : (c + 2) * 128] = jnp.where(low, pltpu.roll(keys, 64, 1), values).astype(BF16)
    below = packed_ref.shape[1] - shard
    packed_ref[0, shard:, :] = jnp.zeros((below, width), BF16)
    row = row_iota((16, shard))
    gains = gain_ref[...].astype(F32)
    gain_rows = jnp.where(row == 0, gains[0:1], jnp.where(row == 1, gains[1:2], 0.0))
    packed_ref[0, shard : shard + 16, :shard] = gain_rows.astype(BF16)
    packed_ref[1, :shard, :] = wq_ref[...]
    packed_ref[1, shard:, :] = jnp.zeros((below, width), BF16)
    router = jnp.concatenate([wr_raw_ref[...].astype(F32), jnp.zeros((128 - EXPERTS, shard), F32)], 0)
    wr_part_ref[...] = jnp.transpose(router).astype(BF16)
    greet([core, far] + [{"ctx": c} for c in others(n)])

    half_rows = packed_ref.shape[1] // 2

    def cut(k, part):
        if k < 2:
            return pl.ds(pl.multiple_of(part * half_rows, 16), half_rows)
        if k == 2:
            return pl.ds(part, 1)
        return pl.ds(pl.multiple_of(part * (shard // 2), 16), shard // 2)

    sources = [packed_ref.at[0], packed_ref.at[1], wo_part_ref, wr_part_ref]
    targets = [wall.at[0], wall.at[1], wo_ref, wr_ref]

    def whole(k):
        return send(sources[k], targets[k].at[fsdp], full_send.at[k], full_recv.at[k], core)

    def own(k):
        return pltpu.make_async_copy(sources[k], targets[k].at[fsdp], local_sems.at[k])

    def to_far(k):
        return send(sources[k].at[cut(k, parity)], targets[k].at[fsdp, cut(k, parity)], x_send.at[k], x_recv.at[k], far)

    def pass_on(k, part, sems, device):
        ref = targets[k].at[distant, cut(k, part)]
        return send(ref, ref, sems[0].at[k], sems[1].at[k], device)

    def sibling_arrived(k):
        ref = targets[k].at[sibling]
        send(ref, ref, full_send.at[k], full_recv.at[k], core).wait_recv()

    def far_arrived(k):
        ref = targets[k].at[distant, cut(k, parity)]
        send(ref, ref, x_send.at[k], x_recv.at[k], far).wait_recv()
        pass_on(k, parity, (y_send, y_recv), near).start()
        pass_on(k, parity, (xs_send, xs_recv), core).start()

    def near_arrived(k):
        pass_on(k, 1 - parity, (y_send, y_recv), near).wait_recv()
        pass_on(k, 1 - parity, (ys_send, ys_recv), core).start()

    def core_arrived(k):
        for part, sems in ((parity, (xs_send, xs_recv)), (1 - parity, (ys_send, ys_recv))):
            ref = targets[k].at[other, cut(k, part)]
            send(ref, ref, sems[0].at[k], sems[1].at[k], core).wait_recv()

    for k in range(2):
        to_far(k).start()
    for k in range(2):
        whole(k).start()
        own(k).start()

    prep_kernel(cap, routes_ref, cot_ref, cx)
    pltpu.make_async_copy(cx, cxs_ref.at[0], local_sems.at[4]).start()
    normed, _ = norm_parts(x_ref[...])
    normed_ref[...] = normed

    def project(k, block, begin):
        at = pl.ds(pl.multiple_of(block * shard, shard), shard)
        if k == 0:
            gain = wall[0, block, shard : shard + 16, :shard].astype(F32)
            gains_ref[:, at] = gain
            h_ref[:, at] = (normed_ref[:, at] * gain[:1]).astype(BF16)
        part = dot(h_ref[:, at], wall[k, block, :shard, :])
        total[k] = part if begin else total[k] + part

    for k in range(2):
        own(k).wait()
        project(k, fsdp, True)
        sibling_arrived(k)
        project(k, sibling, False)
        if k == 0:
            far_arrived(0)

    exchanges = []

    def emit(k):
        lanes = slice(128, 256) if k == 0 else slice(0, 128)
        for c in range(n):
            out[c, :, lanes] = turn_half(total[k, :, c * 128 : (c + 1) * 128], angles, 1.0, 64 if k == 0 else 128).astype(BF16)
        cut_lanes = pl.ds(128 if k == 0 else 0, 128)
        source, target = out.at[:, :, cut_lanes], packs_ref.at[:, :, cut_lanes]
        exchanges.append((source, target, exch_send.at[k], exch_recv.at[k], local_sems.at[8 + k], n))
        exchange_start(*exchanges[-1])

    near_arrived(0)
    project(0, distant, False)
    core_arrived(0)
    project(0, other, False)
    for k in range(2):
        pltpu.make_async_copy(table_ref.at[k, ctx], table.at[k], local_sems.at[6 + k]).wait()
    angles = table[...].reshape(tokens, 256)
    emit(0)
    far_arrived(1)
    for k in (2, 3):
        own(k).start()
        whole(k).start()
        to_far(k).start()
    send(cx, cxs_ref.at[1], cx_send.at[0], cx_recv.at[0], far).start()
    near_arrived(1)
    project(1, distant, False)
    core_arrived(1)
    project(1, other, False)
    emit(1)
    keep = pltpu.make_async_copy(wall, weights_ref, local_sems.at[5])
    keep.start()
    for k in (2, 3):
        far_arrived(k)
    for k in (2, 3):
        near_arrived(k)
    for k in (2, 3):
        core_arrived(k)
        sibling_arrived(k)
        own(k).wait()
    for exchange in exchanges:
        exchange_wait(*exchange)
    for k in range(4):
        whole(k).wait_send()
        to_far(k).wait_send()
        pass_on(k, parity, (y_send, y_recv), near).wait_send()
        pass_on(k, parity, (xs_send, xs_recv), core).wait_send()
        pass_on(k, 1 - parity, (ys_send, ys_recv), core).wait_send()
    send(cx, cxs_ref.at[1], cx_send.at[0], cx_recv.at[0], far).wait()
    pltpu.make_async_copy(cx, cxs_ref.at[0], local_sems.at[4]).wait()
    keep.wait()


def front(wq, wk, wv, wo_part, wr, gains, x, table, routes, cot, cap, n):
    tokens, width = x.shape
    shard = wq.shape[0]
    hbm, vmem = pl.BlockSpec(memory_space=pl.ANY), pl.BlockSpec(memory_space=pltpu.VMEM)
    dma = lambda *k: pltpu.SemaphoreType.DMA(k)
    shaped = lambda shape, dtype=BF16: jax.ShapeDtypeStruct(shape, dtype)
    cx_shape = (tokens + EXPERTS, width)
    padded = 2 * 16 * (shard // 32 + 1)
    return pl.pallas_call(
        functools.partial(front_kernel, n, cap),
        in_specs=[vmem, vmem, vmem, hbm, vmem, vmem, vmem, hbm, vmem, vmem],
        out_specs=[hbm, vmem, hbm, hbm, hbm, hbm, vmem],
        out_shape=[
            shaped((n, tokens, PACK)),
            shaped((tokens, width)),
            shaped((2, 4, padded, width)),
            shaped((4,) + wo_part.shape),
            shaped((4, shard, 128)),
            shaped((2,) + cx_shape),
            shaped((16, width), F32),
        ],
        scratch_shapes=[
            pltpu.VMEM((2, 4, padded, width), BF16),
            pltpu.VMEM((2, padded, width), BF16),
            pltpu.VMEM((shard, 128), BF16),
            pltpu.VMEM(cx_shape, BF16),
            pltpu.VMEM((2, tokens // 2, 256), F32),
            pltpu.VMEM((tokens, width), F32),
            pltpu.VMEM((2, tokens, width), F32),
            pltpu.VMEM((n, tokens, PACK), BF16),
            dma(2, n - 1),
            dma(2, n - 1),
        ]
        + [dma(4)] * 10
        + [dma(1), dma(1), dma(10)],
        compiler_params=params(collective_id=1, has_side_effects=True),
        cost_estimate=cost(2e9, 5e7),
        name="front",
    )(wq, wk, wv, wo_part, wr, gains, x, table, routes, cot)


def attend_kernel(
    length,
    n,
    number,
    capp,
    ends_ref,
    q_ref,
    pack_ref,
    cxs_ref,
    wo_hbm,
    wr_ref,
    x_hbm,
    gain_ref,
    lse_ref,
    full_ref,
    middle_ref,
    h_ref,
    kept_ref,
    xs_ref,
    gs_ref,
    gates_ref,
    rest_ref,
    diag_ref,
    keys,
    values_t,
    acc,
    result,
    arrived,
    hs,
    wo_ref,
    x_ref,
    cx,
    rows_out,
    grads_out,
    gates_out,
    near_send,
    near_recv,
    core_send,
    core_recv,
    exch_send,
    exch_recv,
    hop_send,
    hop_recv,
    cross_send,
    cross_recv,
    cx_send,
    cx_recv,
    fwd_send,
    fwd_recv,
    local_sems,
    own_sems,
    load_sems,
    store_sems,
):
    block = pl.program_id(0)
    last = pl.num_programs(0) - 1
    tokens, width = x_ref.shape
    split = tokens // 2
    per = BLK // split
    per_half = length // BLK // 2
    ctx, fsdp = lax.axis_index("ctx"), lax.axis_index("fsdp")
    first = (fsdp * 2 + lax.rem(ctx, 2)) * number
    core, group = neighbours()
    near = group[1]
    copies = [pltpu.make_async_copy(wo_hbm, wo_ref, local_sems.at[0]), pltpu.make_async_copy(x_hbm, x_ref, local_sems.at[1])]

    def to_near():
        return send(cxs_ref.at[0], rest_ref.at[0], near_send.at[0], near_recv.at[0], near)

    def to_core(i):
        src = cxs_ref.at[i] if i < 2 else rest_ref.at[0]
        return send(src, rest_ref.at[1 + i], core_send.at[i], core_recv.at[i], core)

    def cx_cross():
        return send(rest_ref.at[0], diag_ref.at[0], cx_send.at[0], cx_recv.at[0], group[0])

    def cx_core():
        return send(diag_ref.at[0], diag_ref.at[1], cx_send.at[1], cx_recv.at[1], core)

    def to_home(c, late):
        at = pl.ds(pl.multiple_of(late * split, split), split)
        d = lax.rem(c - ctx + n - 1, n)
        return send(result.at[c, at], arrived.at[ctx, at], exch_send.at[late, d], exch_recv.at[late, d], {"ctx": c})

    def from_device(c, late):
        at = pl.ds(late * split, split)
        d = lax.rem(ctx - c + n - 1, n)
        return send(result.at[c, at], arrived.at[c, at], exch_send.at[late, d], exch_recv.at[late, d], {"ctx": c})

    def own_rows(late):
        at = pl.ds(pl.multiple_of(late * split, split), split)
        return pltpu.make_async_copy(result.at[ctx, at], arrived.at[ctx, at], own_sems.at[late])

    @pl.when(block == 0)
    def _():
        for copy in copies:
            copy.start()
        greet([core, group[0]] + [{"ctx": c} for c in others(n)])
        to_near().start()
        for i in range(2):
            to_core(i).start()

    attn_forward_kernel(length, ends_ref, q_ref, pack_ref, None, lse_ref, full_ref, keys, values_t, acc)
    late = block // per_half
    folded = fold_heads(jnp.transpose(full_ref[0])).astype(BF16)
    for k in range(per):
        c = lax.rem(block, per_half) * per + k
        result[c, pl.ds(pl.multiple_of(late * split, split), split), :] = folded[k * split : (k + 1) * split]

        @pl.when(c == ctx)
        def _():
            own_rows(late).start()

        @pl.when(c != ctx)
        def _():
            to_home(c, late).start()

    @pl.when(block == last - 1)
    def _():
        to_near().wait_recv()
        to_core(2).start()
        cx_cross().start()

    @pl.when(block == last)
    def _():
        order = (0, 4, 1, 2, 3, 5, 6, 7)
        halves = [pl.ds(k * split, split) for k in range(2)]

        def load(step):
            refs = (cxs_ref.at[0], cxs_ref.at[1], rest_ref.at[0], diag_ref.at[0], rest_ref.at[1], rest_ref.at[2], rest_ref.at[3], diag_ref.at[1])
            return pltpu.make_async_copy(refs[order[step]], cx.at[step % 2], load_sems.at[step % 2])

        def hop(i, k):
            return send(hs.at[0, halves[k]], hs.at[(1, 2, 4)[i], halves[k]], hop_send.at[i, k], hop_recv.at[i, k], (group[0], group[1], core)[i])

        def cross(i):
            return send(hs.at[1 + i, halves[i]], hs.at[3, halves[i]], cross_send.at[i], cross_recv.at[i], group[1 - i])

        def forward(i):
            return send(hs.at[1 + i], hs.at[5 + i], fwd_send.at[i], fwd_recv.at[i], core)

        load(0).start()
        for i in range(3):
            to_core(i).wait_recv()
        load(1).start()
        for copy in copies:
            copy.wait()
        for k in range(2):
            own_rows(k).wait()
            for d in range(1, n):
                from_device(lax.rem(ctx + d, n), k).wait_recv()
            at = slice(k * split, (k + 1) * split)
            total = None
            for c in range(n):
                part = dot(arrived[c, at, :], wo_ref[c])
                total = part if total is None else total + part
            middle = x_ref[at, :] + RESIDUAL * total
            middle_ref[at, :] = middle
            normed, _ = norm_parts(middle)
            h = (normed * gain_ref[1:2]).astype(BF16)
            h_ref[at, :] = h
            hs[0, at, :] = h
            for i in range(3):
                hop(i, k).start()
        keep = pltpu.make_async_copy(arrived, kept_ref, local_sems.at[2])
        keep.start()

        def stores(step):
            b = order[step]
            pairs = ((rows_out, xs_ref), (grads_out, gs_ref), (gates_out, gates_ref))
            return [pltpu.make_async_copy(src.at[step % 2], dst.at[:, b], store_sems.at[step % 2, k]) for k, (src, dst) in enumerate(pairs)]

        def place(step):
            b, slot = order[step], step % 2
            load(step).wait()
            if step >= 2:
                for copy in stores(step - 2):
                    copy.wait()
            h = hs[b]
            logits = jnp.transpose(dot(h, wr_ref[...]))[:EXPERTS, :]
            raw = jnp.exp(logits - jnp.max(logits, 0, keepdims=True))
            router = raw / jnp.sum(raw, 0, keepdims=True)
            slots = cx[slot, tokens:, :tokens].astype(F32)
            hots = one_hot(slots, first, number, capp)
            places = jnp.concatenate(hots, 0).astype(BF16)
            rows = dot(places, h).astype(BF16)
            grads = dot(places, cx[slot, :tokens, :]).astype(BF16)
            for j in range(number):
                at = slice(j * capp, (j + 1) * capp)
                rows_out[slot, j] = rows[at]
                grads_out[slot, j] = grads[at]
                gate = jnp.sum(hots[j] * own_row(router, first + j), 1, keepdims=True)
                gates_out[slot, j] = jnp.broadcast_to(gate, (capp, 128))
            for copy in stores(step):
                copy.start()
            if step + 2 < 8:
                if step + 2 == 4:
                    cx_cross().wait_recv()
                    cx_core().start()
                if step + 2 == 7:
                    cx_core().wait_recv()
                load(step + 2).start()

        place(0)
        for k in range(2):
            hop(2, k).wait_recv()
        place(1)
        hop(0, 0).wait_recv()
        cross(0).start()
        hop(1, 0).wait_recv()
        hop(1, 1).wait_recv()
        cross(1).start()
        forward(1).start()
        hop(0, 1).wait_recv()
        forward(0).start()
        place(2)
        place(3)
        for i in range(2):
            cross(i).wait_recv()
        forward(2).start()
        place(4)
        for i in range(3):
            forward(i).wait_recv()
            place(5 + i)
        for step in (6, 7):
            for copy in stores(step):
                copy.wait()
        for k in range(2):
            for d in range(1, n):
                to_home(lax.rem(ctx + d, n), k).wait_send()
        for i in range(2):
            cross(i).wait_send()
        cx_cross().wait_send()
        cx_core().wait_send()
        for i in range(3):
            for k in range(2):
                hop(i, k).wait_send()
            forward(i).wait_send()
            to_core(i).wait_send()
        to_near().wait_send()
        keep.wait()


def attend(ends, packs, cxs, wo, wr, x, gains, length, number, capp):
    n, _, rows, _ = packs.shape
    tokens, width = x.shape
    blocks, per = length // BLK, BLK // rows
    per_half = blocks // 2
    tiles = lambda i: (lax.rem(i, per_half), i // per_half, 0, 0)
    hbm = pl.BlockSpec(memory_space=pl.ANY)
    dma = lambda *k: pltpu.SemaphoreType.DMA(k)
    same = lambda shape: pl.BlockSpec(shape, lambda i: (0,) * len(shape))
    shaped = lambda shape, dtype=BF16: jax.ShapeDtypeStruct(shape, dtype)
    return pl.pallas_call(
        functools.partial(attend_kernel, length, n, number, capp),
        grid=(blocks,),
        in_specs=[
            pl.BlockSpec(memory_space=pltpu.SMEM),
            pl.BlockSpec((per, 1, rows, PACK), tiles),
            same(packs.shape),
            hbm,
            hbm,
            same(wr.shape),
            hbm,
            same(gains.shape),
        ],
        out_specs=[
            pl.BlockSpec((1, 1, 2 * BLK), lambda i: (i, 0, 0)),
            pl.BlockSpec((1, 128, 2 * BLK), lambda i: (i, 0, 0)),
            same((tokens, width)),
            same((tokens, width)),
            hbm,
            hbm,
            hbm,
            hbm,
            hbm,
            hbm,
        ],
        out_shape=[
            shaped((blocks, 1, 2 * BLK), F32),
            shaped((blocks, 128, 2 * BLK), F32),
            shaped((tokens, width), F32),
            shaped((tokens, width)),
            shaped((n, tokens, 128)),
            shaped((number, 8, capp, width)),
            shaped((number, 8, capp, width)),
            shaped((number, 8, capp, 128), F32),
            shaped((4,) + cxs.shape[1:]),
            shaped((2,) + cxs.shape[1:]),
        ],
        scratch_shapes=[
            pltpu.VMEM((length, 128), BF16),
            pltpu.VMEM((128, length), BF16),
            pltpu.VMEM((128, 2 * BLK), F32),
            pltpu.VMEM((n, tokens, 128), BF16),
            pltpu.VMEM((n, tokens, 128), BF16),
            pltpu.VMEM((8, tokens, width), BF16),
            pltpu.VMEM(wo.shape, BF16),
            pltpu.VMEM((tokens, width), F32),
            pltpu.VMEM((2,) + cxs.shape[1:], BF16),
            pltpu.VMEM((2, number, capp, width), BF16),
            pltpu.VMEM((2, number, capp, width), BF16),
            pltpu.VMEM((2, number, capp, 128), F32),
            dma(1),
            dma(1),
            dma(3),
            dma(3),
            dma(2, n - 1),
            dma(2, n - 1),
            dma(3, 2),
            dma(3, 2),
            dma(2),
            dma(2),
            dma(2),
            dma(2),
            dma(3),
            dma(3),
            dma(3),
            dma(2),
            dma(2),
            dma(2, 3),
        ],
        compiler_params=params(collective_id=3, has_side_effects=True),
        cost_estimate=cost(2e10, 7e7),
        name="attend",
    )(ends, packs, packs, cxs, wo, wr, x, gains)


RING = 12
LAG_MIDDLE, LAG_ACROSS, LAG_END = 1, 2, 4
ORDER_X, ORDER_Y, ORDER_CORE = 1, 2, 4


class GroupSum:
    def __init__(self, part, rows, lands, own, sems, load, free, first, core, group):
        self.part, self.rows, self.own, self.load, self.free, self.first = part, rows, own, load, free, first
        self.land, self.land_x, self.land_y = lands
        self.core_send, self.core_recv, self.x_send, self.x_recv, self.y_send, self.y_recv = sems
        self.core, self.far, self.near = core, group[0], group[1]

    def place(self, i):
        return self.land.at[i, pl.ds(0, self.rows)]

    def ready(self, which):
        if not self.first:
            pl.semaphore_wait(self.free.at[which], 1)

    def to_core(self, i):
        return send(self.part.at[4 + i], self.place(i), self.core_send.at[i], self.core_recv.at[i], self.core)

    def to_far(self, k):
        return send(self.place(1 + 2 * k), self.land_x.at[k, pl.ds(0, self.rows)], self.x_send.at[k], self.x_recv.at[k], self.far)

    def to_near(self):
        return send(self.place(2), self.land_y.at[pl.ds(0, self.rows)], self.y_send.at[0], self.y_recv.at[0], self.near)

    def fetch(self, i):
        return pltpu.make_async_copy(self.part.at[i], self.own.at[i % 2, pl.ds(0, self.rows)], self.load.at[i % 2])

    def start(self):
        self.ready(0)
        for i in (1, 3, 2, 0):
            self.to_core(i).start()

    def over_cores(self):
        order = (1, 3, 2, 0)
        if self.own is not None:
            self.fetch(1).start()
        for step, i in enumerate(order):
            if self.own is None:
                mine = self.part[i]
            else:
                self.fetch(i).wait()
                mine = self.own[i % 2, : self.rows]
            self.to_core(i).wait_recv()
            self.land[i, : self.rows] = (self.land[i, : self.rows].astype(F32) + mine.astype(F32)).astype(BF16)
            if self.own is not None and step < 3:
                self.fetch(order[step + 1]).start()
            if i % 2 == 1:
                if step == 0:
                    self.ready(1)
                self.to_far(i // 2).start()

    def over_x(self, between=None):
        for k in (1, 0):
            if k == 0 and between is not None:
                between()
            self.to_far(k).wait_recv()
            both = self.land[2 * k, : self.rows].astype(F32) + self.land_x[k, : self.rows].astype(F32)
            self.land[2 * k, : self.rows] = both.astype(BF16)
            if k == 1:
                self.ready(2)
                self.to_near().start()

    def finish(self):
        self.to_near().wait_recv()
        for i in range(4):
            self.to_core(i).wait_send()
        for k in range(2):
            self.to_far(k).wait_send()
        self.to_near().wait_send()
        return self.land[0, : self.rows].astype(F32) + self.land_y[: self.rows].astype(F32)

    def release(self):
        for which, device in enumerate((self.core, self.far, self.near)):
            pl.semaphore_signal(self.free.at[which], inc=1, device_id=device, device_id_type=MESH)


class LineSum:
    def __init__(self, count, own_ref, other_ref, inbox, across, mine, sems):
        self.count, self.own_ref, self.other_ref = count, own_ref, other_ref
        self.inbox, self.across, self.mine = inbox, across, mine
        self.line_send, self.line_recv, self.mid_send, self.mid_recv, self.side_send, self.side_recv, self.store, self.load = sems
        ctx = lax.axis_index("ctx")
        z = ctx // 2
        self.middle = (z == 1) | (z == 2)
        self.line = {"ctx": jnp.where(z % 2 == 0, ctx + 2, ctx - 2)}
        self.peer = {"ctx": jnp.where(z == 1, ctx + 2, ctx - 2)}
        self.side = {"ctx": flip(ctx, 1)}

    def send_line(self, src, i):
        s = lax.rem(i, RING)
        return send(src, self.inbox.at[s], self.line_send.at[s], self.line_recv.at[s], self.line)

    def send_mid(self, i):
        s = lax.rem(i, RING)
        return send(self.inbox.at[s], self.across.at[s], self.mid_send.at[s], self.mid_recv.at[s], self.peer)

    def send_side(self, src, i):
        return send(src, self.other_ref.at[i], self.side_send.at[lax.rem(i, RING)], self.side_recv.at[i], self.side)

    def keep(self, src, i):
        return pltpu.make_async_copy(src, self.own_ref.at[i], self.store.at[lax.rem(i, RING)])

    def fetch(self, src, i):
        s = lax.rem(i, 4)
        return pltpu.make_async_copy(src, self.mine.at[s], self.load.at[s])

    def drain_middle(self, i):
        src = self.across.at[lax.rem(i, RING)]
        self.send_line(src, i).wait_send()
        self.send_side(src, i).wait_send()
        self.keep(src, i).wait()

    def drain_end(self, i):
        src = self.inbox.at[lax.rem(i, RING)]
        self.send_side(src, i).wait_send()
        self.keep(src, i).wait()

    def tick(self, t, source):
        count = self.count
        fixed = isinstance(t, int)

        def when(condition):
            if fixed:
                return (lambda f: f()) if condition else (lambda f: None)
            return pl.when(condition)

        i32 = (lambda v: jnp.int32(v)) if fixed else (lambda v: v)

        @pl.when(self.middle)
        def _():
            @when((t >= LAG_MIDDLE) & (t < count + LAG_MIDDLE))
            def _():
                i = i32(t - LAG_MIDDLE)

                @when(t >= LAG_ACROSS + 4)
                def _():
                    self.drain_middle(i32(t - LAG_ACROSS - 4))

                s = lax.rem(i, RING)
                self.fetch(self.own_ref.at[i], i).wait()
                self.send_line(self.inbox.at[s], i).wait_recv()
                self.inbox[s] = self.inbox[s] + self.mine[lax.rem(i, 4)]
                self.send_mid(i).start()

            @when(t < count)
            def _():
                self.fetch(source(t), i32(t)).start()

            @when((t >= LAG_ACROSS) & (t < count + LAG_ACROSS))
            def _():
                i = i32(t - LAG_ACROSS)
                s = lax.rem(i, RING)
                self.send_mid(i).wait()
                self.across[s] = self.across[s] + self.inbox[s]
                self.send_line(self.across.at[s], i).start()
                self.send_side(self.across.at[s], i).start()
                self.keep(self.across.at[s], i).start()

        @pl.when(jnp.logical_not(self.middle))
        def _():
            @when(t < count)
            def _():
                @when(t >= LAG_END + 2)
                def _():
                    self.drain_end(i32(t - LAG_END - 2))

                @when(t >= 3)
                def _():
                    self.send_line(self.mine.at[0], i32(t - 3)).wait_send()

                self.send_line(source(t), i32(t)).start()

            @when(t >= LAG_END)
            def _():
                i = i32(t - LAG_END)
                s = lax.rem(i, RING)
                self.send_line(self.inbox.at[s], i).wait_recv()
                self.send_side(self.inbox.at[s], i).start()
                self.keep(self.inbox.at[s], i).start()

    def finish(self):
        count = self.count

        @pl.when(self.middle)
        def _():
            for i in range(count + LAG_MIDDLE - LAG_ACROSS - 4, count):
                self.drain_middle(jnp.int32(i))

        @pl.when(jnp.logical_not(self.middle))
        def _():
            for i in range(count - 3, count):
                self.send_line(self.mine.at[0], jnp.int32(i)).wait_send()
            for i in range(count - LAG_END - 2, count):
                self.drain_end(jnp.int32(i))

        def arrived(i, carry):
            self.send_side(self.mine.at[0], i).wait_recv()
            return carry

        lax.fori_loop(0, count, arrived, 0)


def backward_kernel(
    n,
    length,
    capp,
    ends_ref,
    xs_ref,
    gs_ref,
    gates_ref,
    wg_ref,
    wu_ref,
    wd_ref,
    cxs_ref,
    rest_ref,
    diag_ref,
    full_ref,
    weights_ref,
    packs_hbm,
    table_hbm,
    cot_hbm,
    wo_hbm,
    attn_hbm,
    x_hbm,
    h_attn_hbm,
    h_hbm,
    middle_hbm,
    wr_hbm,
    gains_hbm,
    lse_hbm,
    own_ref,
    other_ref,
    pieces_ref,
    outs_ref,
    backs_ref,
    gx_ref,
    yp_ref,
    grad_x_ref,
    mixed_ref,
    inbox,
    across,
    mine,
    land,
    land_x,
    land_y,
    y_land,
    y_land_x,
    y_land_y,
    own_buf,
    late_pieces,
    ga_in,
    grads_in,
    line_send,
    line_recv,
    mid_send,
    mid_recv,
    side_send,
    side_recv,
    line_store,
    line_load,
    ga_send,
    ga_recv,
    gr_send,
    gr_recv,
    group_sems,
    group_load,
    free,
    local_sems,
    full_sems,
    w_sems,
    load_sems,
    store_sems,
    comb_sems,
    part_sems,
):
    tokens, width = h_hbm.shape
    half = length // 2
    rows = tokens // 2
    shard = width // 4
    blocks = length // BLK
    number = xs_ref.shape[0]
    ff = wg_ref.shape[2]
    ctx, fsdp = lax.axis_index("ctx"), lax.axis_index("fsdp")
    side = lax.rem(ctx, 2)
    first = (fsdp * 2 + side) * number
    core, group = neighbours()
    sub = own_ref.shape[1]
    cuts = PIECE // sub
    early = number * 6 * cuts
    line = LineSum(early + 2 * cuts, own_ref, other_ref, inbox, across, mine, (line_send, line_recv, mid_send, mid_recv, side_send, side_recv, line_store, line_load))

    def source(t):
        return pieces_ref.at[t // cuts, pl.ds(pl.multiple_of(lax.rem(t, cuts) * sub, sub), sub)]

    def tick(t):
        line.tick(jnp.int32(t) if isinstance(t, int) else t, source)

    sems = lambda k: [group_sems.at[k, j] for j in range(6)]
    lands = (land, land_x, land_y)
    ext = tokens + EXPERTS
    gx = GroupSum(gx_ref, 2 * ext, lands, None, sems(0), None, free, True, core, group)
    ys = GroupSum(yp_ref, 2 * tokens, (y_land, y_land_x, y_land_y), own_buf, sems(1), group_load, free, True, core, group)

    def strip(r):
        f = fsdp
        if r & ORDER_X:
            f = flip(f, 2)
        if r & ORDER_CORE:
            f = flip(f, 1)
        return 2 * f + (1 - side if r & ORDER_Y else side)

    def experts(wg, wu, wd, xb, gb, gateb, stage, out_acc, back_acc, outb, backb, go, dgate, comb_o, comb_b, gst, yst, slots):
        def loads(e):
            s = lax.rem(e, 2)
            at = side * number + e
            pairs = ((wg_ref.at[at], wg), (wu_ref.at[at], wu), (wd_ref.at[at], wd), (xs_ref.at[e], xb), (gs_ref.at[e], gb), (gates_ref.at[e], gateb))
            return [pltpu.make_async_copy(src, dst.at[s], load_sems.at[s, k]) for k, (src, dst) in enumerate(pairs)]

        def slot_copy(b):
            refs = (cxs_ref.at[0], cxs_ref.at[1], rest_ref.at[0], diag_ref.at[0], rest_ref.at[1], rest_ref.at[2], rest_ref.at[3], diag_ref.at[1])
            return pltpu.make_async_copy(refs[b].at[pl.ds(tokens, EXPERTS), pl.ds(0, tokens)], slots.at[b], part_sems.at[0, b])

        def stores(e):
            pairs = (
                (stage.at[pl.ds(0, 3)], pieces_ref.at[pl.ds(6 * e, 3)]),
                (stage.at[pl.ds(3, 3)], pieces_ref.at[pl.ds(6 * e + 3, 3)]),
                (outb, outs_ref.at[e]),
                (backb, backs_ref.at[e]),
            )
            return [pltpu.make_async_copy(src, dst, store_sems.at[k]) for k, (src, dst) in enumerate(pairs)]

        for copy in loads(jnp.int32(0)):
            copy.start()
        for b in range(8):
            slot_copy(b).start()
        greet([core, group[0]] + [{"ctx": c} for c in others(n)])

        def one(e, carry):
            s = lax.rem(e, 2)

            @pl.when(e + 1 < number)
            def _():
                for copy in loads(e + 1):
                    copy.start()

            for copy in loads(e):
                copy.wait()

            @pl.when(e > 0)
            def _():
                for copy in stores(e - 1)[2:]:
                    copy.wait()

            x = xb[s]
            gate = gateb[s][:, :1]
            go[...] = (gate * (RESIDUAL * gb[s].astype(F32))).astype(BF16)
            part = ff // 2
            for chunk in range(2):
                at = slice(chunk * part, (chunk + 1) * part)
                wgc, wuc, wdc = wg[s, :, at], wu[s, :, at], wd[s, at, :]
                pre_gate = dot(x, wgc)
                pre_up = dot(x, wuc)
                sig = jax.nn.sigmoid(pre_gate)
                hidden = (pre_gate * sig * pre_up).astype(BF16)
                out_part = dot(hidden, wdc)
                grad_hidden = dot(go[...], wdc, NT)
                grad_gate = (grad_hidden * pre_up * sig * (1.0 + pre_gate * (1.0 - sig))).astype(BF16)
                grad_up = (grad_hidden * pre_gate * sig).astype(BF16)
                row_part = dot(grad_gate, wgc, NT) + dot(grad_up, wuc, NT)
                dwg = dot(x, grad_gate, TN).astype(BF16)
                dwu = dot(x, grad_up, TN).astype(BF16)
                dwd = dot(hidden, go[...], TN).astype(BF16)
                for k in range(2):
                    cut = slice(k * PIECE, (k + 1) * PIECE)
                    stage[3 * chunk + k, :, :part] = dwg[cut]
                    stage[3 * chunk + k, :, part:] = dwu[cut]
                    stage[3 * chunk + 2, k * part : (k + 1) * part, :] = dwd[:, cut]
                stores(e)[chunk].start()
                if chunk == 0:
                    out_acc[...] = out_part
                    back_acc[...] = row_part
                    stores(e)[0].wait()
                    tick(2 * e)
                else:
                    out = (out_acc[...] + out_part).astype(BF16).astype(F32)
                    outb[...] = (gate * out).astype(BF16)
                    backb[...] = (back_acc[...] + row_part).astype(BF16)
                    grad = jnp.sum(RESIDUAL * gb[s].astype(F32) * out, 1, keepdims=True)
                    dgate[e] = jnp.broadcast_to(grad, dgate.shape[1:])
            for copy in stores(e)[2:]:
                copy.start()
            stores(e)[1].wait()
            tick(2 * e + 1)
            return carry

        lax.fori_loop(0, number, one, 0)
        for copy in stores(jnp.int32(number - 1))[2:]:
            copy.wait()
        for b in range(8):
            slot_copy(b).wait()

        def which(s):
            k = lax.rem(s, 4)
            i = jnp.where(k == 0, 1, jnp.where(k == 1, 3, jnp.where(k == 2, 2, 0)))
            return jnp.where(s < 4, 4 + i, i), i

        def comb(s):
            k = lax.rem(s, 2)
            at = pl.ds(pl.multiple_of(which(s)[0] * capp, 16), capp)
            return [
                pltpu.make_async_copy(outs_ref.at[:, at], comb_o.at[k], comb_sems.at[0, k]),
                pltpu.make_async_copy(backs_ref.at[:, at], comb_b.at[k], comb_sems.at[1, k]),
            ]

        def put(s):
            k = lax.rem(s, 2)
            r, _ = which(s)
            return [
                pltpu.make_async_copy(gst.at[k], gx_ref.at[r], part_sems.at[1, k]),
                pltpu.make_async_copy(yst.at[k], yp_ref.at[r], part_sems.at[1, 2 + k]),
            ]

        for copy in comb(jnp.int32(0)):
            copy.start()

        def join(s, carry):
            k = lax.rem(s, 2)
            r, i = which(s)

            @pl.when(s + 1 < 8)
            def _():
                for copy in comb(s + 1):
                    copy.start()

            for copy in comb(s):
                copy.wait()

            @pl.when(s >= 2)
            def _():
                put(s - 2)[1].wait()

            hots = one_hot(slots[r].astype(F32), first, number, capp)
            places = jnp.concatenate(hots, 0).astype(BF16)
            y = dot(places, comb_o[k].reshape(number * capp, width), TN).astype(BF16)
            back = dot(places, comb_b[k].reshape(number * capp, width), TN).astype(BF16)
            extra = jnp.zeros((EXPERTS, 2 * tokens), F32)
            for j in range(number):
                grads = dgate[j, pl.ds(pl.multiple_of(r * capp, 16), capp), :][:, :1]
                grad = jnp.sum(hots[j] * grads, 0, keepdims=True)
                high = grad.astype(BF16).astype(F32)
                extra = jnp.where(row_iota(extra.shape) == first + j, jnp.concatenate([high, grad - high], 1), extra)
            for q in range(2):
                yst[k, q * tokens : (q + 1) * tokens, :] = y[:, q * PIECE : (q + 1) * PIECE]
                gst[k, q * ext : q * ext + tokens, :] = back[:, q * PIECE : (q + 1) * PIECE]
            gst[k, tokens:ext, :] = extra.astype(BF16)
            gst[k, ext + tokens :, :] = jnp.zeros((EXPERTS, PIECE), BF16)
            put(s)[1].start()

            @pl.when(s < 4)
            def _():
                put(s)[0].start()
                put(s)[0].wait()
                gx.to_core(i).start()

            @pl.when(s >= 4)
            def _():
                gx.to_core(i).wait_recv()
                land[i, : gx.rows] = (land[i, : gx.rows].astype(F32) + gst[k].astype(F32)).astype(BF16)

            @pl.when((s == 4) | (s == 5))
            def _():
                gx.to_far(s - 4).start()

            @pl.when(lax.rem(s, 2) == 1)
            def _():
                tick(2 * number + s // 2)

            return carry

        lax.fori_loop(0, 8, join, 0)
        for s in range(6, 8):
            put(jnp.int32(s))[1].wait()

    slots_rows = xs_ref.shape[1]
    pl.run_scoped(
        experts,
        pltpu.VMEM((2, width, ff), BF16),
        pltpu.VMEM((2, width, ff), BF16),
        pltpu.VMEM((2, ff, width), BF16),
        pltpu.VMEM((2, slots_rows, width), BF16),
        pltpu.VMEM((2, slots_rows, width), BF16),
        pltpu.VMEM((2, slots_rows, 128), F32),
        pltpu.VMEM((6, PIECE, PIECE), BF16),
        pltpu.VMEM((slots_rows, width), F32),
        pltpu.VMEM((slots_rows, width), F32),
        pltpu.VMEM((slots_rows, width), BF16),
        pltpu.VMEM((slots_rows, width), BF16),
        pltpu.VMEM((slots_rows, width), BF16),
        pltpu.VMEM((number, slots_rows, 128), F32),
        pltpu.VMEM((2, number, capp, width), BF16),
        pltpu.VMEM((2, number, capp, width), BF16),
        pltpu.VMEM((2, 2 * ext, PIECE), BF16),
        pltpu.VMEM((2, 2 * tokens, PIECE), BF16),
        pltpu.VMEM((8, EXPERTS, tokens), BF16),
    )
    at_tick = [2 * number + 4]

    def go_on(k=1):
        for _ in range(k):
            tick(at_tick[0])
            at_tick[0] += 1

    def backward(packs, table, keys, values, keys_t, grad_q, grad_k, grad_v, acc, full_buf, ga, pack_out, wbuf, total, grad_middle, dgain, col, small, columns, cot, wo, attn, x_in, h_attn, h_ref, middle_ref, wr_ref, gains_ref, lse_ref):
        ws = GroupSum(small, small.shape[1], lands, None, sems(2), None, free, False, core, group)
        cs = GroupSum(columns, PIECE + 16, lands, None, sems(3), None, free, False, core, group)
        copies = [
            pltpu.make_async_copy(src, dst, local_sems.at[4 + k])
            for k, (src, dst) in enumerate(
                (
                    (cot_hbm, cot),
                    (wo_hbm, wo),
                    (attn_hbm, attn),
                    (packs_hbm, packs),
                    (table_hbm, table),
                    (x_hbm, x_in),
                    (h_attn_hbm, h_attn),
                    (h_hbm, h_ref),
                    (middle_hbm, middle_ref),
                    (wr_hbm, wr_ref),
                    (gains_hbm, gains_ref),
                    (lse_hbm, lse_ref),
                )
            )
        ]
        for copy in copies:
            copy.start()
        small[:, 256:384, :] = jnp.zeros((8, 128, PIECE), BF16)
        late_pieces[384:PIECE, :] = jnp.zeros((PIECE - 384, PIECE), BF16)
        columns[:, PIECE:, :] = jnp.zeros((8, 16, PIECE), BF16)
        go_on(2)
        gx.over_x(go_on)
        go_on(2)
        arrived = gx.finish()
        arrived = jnp.concatenate([arrived[:ext], arrived[ext:]], 1)
        gx.release()

        for copy in copies[7:]:
            copy.wait()
        h = h_ref[...]
        gain = gains_ref[1:2]
        extra = arrived[tokens:, :]
        grad_router = extra[:, :tokens] + extra[:, tokens : 2 * tokens]
        grad_router = jnp.transpose(jnp.concatenate([grad_router, jnp.zeros((128 - EXPERTS, tokens), F32)], 0))
        logits = dot(h, wr_ref[...])
        logits = jnp.where(lane_iota(logits.shape) < EXPERTS, logits, MASKED)
        raw = jnp.exp(logits - jnp.max(logits, -1, keepdims=True))
        router = raw / jnp.sum(raw, -1, keepdims=True)
        grad_logits = (router * (grad_router - jnp.sum(router * grad_router, -1, keepdims=True))).astype(BF16)
        go_on()
        grad_h = arrived[:tokens, :] + dot(grad_logits, wr_ref[...], NT)
        normed, scale = norm_parts(middle_ref[...])
        dgain[1:2, :] = jnp.sum(grad_h * normed, 0, keepdims=True)
        for copy in copies[:3]:
            copy.wait()
        grad_mid = cot[...] + norm_back(grad_h * gain, normed, scale)
        grad_middle[...] = grad_mid
        grad_branch = (RESIDUAL * grad_mid).astype(BF16)
        for c in range(n):
            ga[c] = dot(grad_branch, wo[c], NT).astype(BF16)
        ga_exchange = (ga, ga_in, ga_send, ga_recv, local_sems.at[2], n)
        exchange_start(*ga_exchange)
        go_on()
        col[:, :128] = dot(h, grad_logits, TN).astype(BF16)
        for r in range(8):
            at = strip(r)
            dwo = dot(attn[at], grad_branch, TN).astype(BF16)
            small[r, 0:128, :] = dwo[:, :PIECE]
            small[r, 128:256, :] = dwo[:, PIECE:]
            small[r, 256:384, 0:128] = col[pl.ds(pl.multiple_of(at * 128, 128), 128), 0:128]
        ws.start()
        ys.start()
        go_on()
        copies[3].wait()
        for hh in range(2):
            for c in range(n):
                kk, vv = pair_keys(packs[c, hh, :, 128:256].astype(F32))
                at = hh * half + c * rows
                keys[at : at + rows, :] = kk.astype(BF16)
                values[at : at + rows, :] = vv.astype(BF16)
                keys_t[:, at : at + rows] = jnp.transpose(kk).astype(BF16)
        grad_k[...] = jnp.zeros_like(grad_k)
        grad_v[...] = jnp.zeros_like(grad_v)
        go_on()
        ws.over_cores()
        ys.over_cores()
        go_on()
        exchange_wait(*ga_exchange)

        per = BLK // rows
        per_half = blocks // 2

        def fetch_full(b):
            return pltpu.make_async_copy(full_ref.at[b], full_buf.at[lax.rem(b, 2)], full_sems.at[lax.rem(b, 2)])

        fetch_full(jnp.int32(0)).start()
        attend_tick = at_tick[0]

        def attend(block, carry):
            late = block // per_half
            c0 = lax.rem(block, per_half) * per
            q2 = jnp.concatenate([packs[c0 + k, late, :, :128] for k in range(per)], 0)
            q2 = stack_heads((q2.astype(F32) * ATTN_SCALE).astype(BF16))
            g2 = stack_heads(jnp.concatenate([ga_in[c0 + k, pl.ds(pl.multiple_of(late * rows, rows), rows), :] for k in range(per)], 0))
            position, start = query_rows(ends_ref, block, length)
            lse = lse_ref[block]
            shift = jnp.where(start > 0, MASKED, 0.0) - lse

            @pl.when(block + 1 < blocks)
            def _():
                fetch_full(block + 1).start()

            fetch_full(block).wait()
            delta = jnp.sum(jnp.transpose(g2.astype(F32)) * full_buf[lax.rem(block, 2)], 0, keepdims=True)
            acc[...] = jnp.zeros_like(acc)

            def body(kb, whole, carry):
                at = pl.multiple_of(kb * BLK, BLK)
                scores = dot(keys[pl.ds(at, BLK), :], q2, NT)
                if whole:
                    probs = jnp.exp(scores + shift)
                else:
                    where = key_position(kb, length)
                    probs = jnp.where((where <= position) & (where >= start), jnp.exp(scores - lse), 0.0)
                grad_probs = dot(values[pl.ds(at, BLK), :], g2, NT)
                grad_scores = (probs * (grad_probs - delta)).astype(BF16)
                acc[...] += dot(keys_t[:, pl.ds(at, BLK)], grad_scores)
                grad_k[pl.ds(at, BLK), :] += dot(grad_scores, q2)
                grad_v[pl.ds(at, BLK), :] += dot(probs.astype(BF16), g2)

                if not whole:

                    @pl.when((kb == block) & ((block == per_half) | (block == per_half + 1)))
                    def _():
                        tick(attend_tick + 2 + 2 * (block - per_half))

                return carry

            block_loop(block, per_half, body, 0)
            grad_q[pl.ds(pl.multiple_of(block * BLK, BLK), BLK), :] = fold_heads(jnp.transpose(acc[...]))

            @pl.when((block == 1) | (block >= 3))
            def _():
                past = block - per_half
                late_tick = jnp.where(past < 2, 3 + 2 * past, 4 + past)
                tick(attend_tick + jnp.where(block < per_half, block // 2, late_tick))

            return carry

        lax.fori_loop(0, blocks, attend, 0)
        at_tick[0] += blocks
        copies[4].wait()
        for c in range(n):
            for hh in range(2):
                at = slice(hh * half + c * rows, hh * half + (c + 1) * rows)
                kk = grad_k[at, :]
                vv = grad_v[at, :]
                kk = kk + pltpu.roll(kk, 64, 1)
                vv = vv + pltpu.roll(vv, 64, 1)
                both = jnp.where(lane_iota(kk.shape) < 64, kk, vv)
                package = jnp.concatenate([grad_q[at, :] * ATTN_SCALE, both], -1)
                pack_out[c, hh * rows : (hh + 1) * rows, :] = turn(package, table[at, :], -1.0).astype(BF16)
        gr_exchange = (pack_out, grads_in, gr_send, gr_recv, local_sems.at[3], n)
        exchange_start(*gr_exchange)

        def fetch_w(c):
            slot = lax.rem(c, 2)
            at = pl.ds(pl.multiple_of(c * 128, 128), 128)
            return [
                pltpu.make_async_copy(weights_ref.at[1 - k, :, :, at], wbuf.at[slot, :, :, pl.ds(128 * k, 128)], w_sems.at[slot, k])
                for k in range(2)
            ]

        for copy in fetch_w(jnp.int32(0)):
            copy.start()
        go_on()
        ws.over_x()
        ys.over_x()
        go_on(2)
        total[...] = jnp.zeros_like(total)
        late_pieces[:384] = ws.finish().astype(BF16)
        ws.release()
        ffn = ys.finish()
        mixed_ref[...] = middle_ref[...] + RESIDUAL * jnp.concatenate([ffn[:tokens], ffn[tokens:]], 1)
        go_on(3)
        exchange_wait(*gr_exchange)
        copies[5].wait()
        copies[6].wait()

        columns_tick = at_tick[0]

        def finish_columns(c, carry):
            @pl.when(c + 1 < n)
            def _():
                for copy in fetch_w(c + 1):
                    copy.start()

            for copy in fetch_w(c):
                copy.wait()
            slot = lax.rem(c, 2)
            g = grads_in[c]
            col[...] = dot(h_attn[...], g, TN).astype(BF16)
            for r in range(8):
                at = pl.ds(pl.multiple_of(strip(r) * 128, 128), 128)
                columns[r, pl.ds(pl.multiple_of(c // 2 * 128, 128), 128), pl.ds(pl.multiple_of(lax.rem(c, 2) * PACK, PACK), PACK)] = col[at, :]
            for f in range(4):
                total[:, f * shard : (f + 1) * shard] += dot(g, wbuf[slot, f, :shard, :], NT)

            @pl.when(lax.rem(c, 4) == 3)
            def _():
                tick(columns_tick + c // 4)

            return carry

        lax.fori_loop(0, n, finish_columns, 0)
        at_tick[0] += n // 4
        normed, scale = norm_parts(x_in[...])
        grad_h = total[...]
        dgain[0:1, :] = jnp.sum(grad_h * normed, 0, keepdims=True)
        grad_x_ref[...] = grad_middle[...] + norm_back(grad_h * gains_ref[0:1], normed, scale)
        for r in range(8):
            at = pl.ds(pl.multiple_of(strip(r) * 128, 128), 128)
            row = row_iota((16, 128))
            both = jnp.where(row == 0, dgain[0:1, at], jnp.where(row == 1, dgain[1:2, at], 0.0))
            columns[r, PIECE:, 0:128] = both.astype(BF16)
        cs.start()
        go_on()
        cs.over_cores()
        go_on(3)
        cs.over_x(go_on)
        go_on(3)
        summed = cs.finish().astype(BF16)
        late_pieces[PIECE:] = summed[:PIECE]
        late_pieces[384:400] = summed[PIECE:]

    f32, bf = (lambda *shape: pltpu.VMEM(shape, F32)), (lambda *shape: pltpu.VMEM(shape, BF16))
    pl.run_scoped(
        backward,
        bf(*packs_hbm.shape),
        f32(*table_hbm.shape),
        bf(length, 128),
        bf(length, 128),
        bf(128, length),
        f32(length, 128),
        f32(length, 128),
        f32(length, 128),
        f32(128, 2 * BLK),
        f32(2, 128, 2 * BLK),
        bf(n, tokens, 128),
        bf(n, tokens, PACK),
        bf(2, 4, weights_ref.shape[2], PACK),
        f32(tokens, width),
        f32(tokens, width),
        f32(8, width),
        bf(width, PACK),
        bf(8, 384, PIECE),
        bf(8, PIECE + 16, PIECE),
        f32(tokens, width),
        bf(*wo_hbm.shape),
        bf(*attn_hbm.shape),
        f32(tokens, width),
        bf(tokens, width),
        bf(tokens, width),
        f32(tokens, width),
        bf(*wr_hbm.shape),
        f32(*gains_hbm.shape),
        f32(*lse_hbm.shape),
    )

    def rest(t, carry):
        tick(t)
        return carry

    lax.fori_loop(at_tick[0], early, rest, 0)

    def late_source(t):
        return late_pieces.at[pl.ds(pl.multiple_of((t - early) * sub, sub), sub)]

    def late(t, carry):
        line.tick(t, late_source)
        return carry

    lax.fori_loop(early, line.count + LAG_END, late, 0)
    line.finish()


def backward_step(ends, xs, gs, gates, w_gate, w_up, w_down, cxs, rest, diag, full, weights, packs, table, cot, wo, attn, x, h_attn, h, middle, wr, gains, lse, n, length, capp):
    tokens, width = x.shape
    number, slots_rows, _ = xs.shape
    hbm, vmem = pl.BlockSpec(memory_space=pl.ANY), pl.BlockSpec(memory_space=pltpu.VMEM)
    smem = pl.BlockSpec(memory_space=pltpu.SMEM)
    dma = lambda *k: pltpu.SemaphoreType.DMA(k)
    shaped = lambda shape, dtype=BF16: jax.ShapeDtypeStruct(shape, dtype)
    sub = PIECE // 2
    piece = (sub, PIECE)
    count = (number * 6 + 2) * 2
    land_rows = max(2 * (tokens + EXPERTS), PIECE + 16)
    return pl.pallas_call(
        functools.partial(backward_kernel, n, length, capp),
        in_specs=[smem] + [hbm] * 23,
        out_specs=[hbm] * 7 + [vmem, vmem],
        out_shape=[
            shaped((count,) + piece),
            shaped((count,) + piece),
            shaped((number * 6, PIECE, PIECE)),
            shaped(xs.shape),
            shaped(xs.shape),
            shaped((8, 2 * (tokens + EXPERTS), PIECE)),
            shaped((8, 2 * tokens, PIECE)),
            shaped((tokens, width), F32),
            shaped((tokens, width), F32),
        ],
        scratch_shapes=[
            pltpu.VMEM((RING,) + piece, BF16),
            pltpu.VMEM((RING,) + piece, BF16),
            pltpu.VMEM((4,) + piece, BF16),
            pltpu.VMEM((4, land_rows, PIECE), BF16),
            pltpu.VMEM((2, land_rows, PIECE), BF16),
            pltpu.VMEM((land_rows, PIECE), BF16),
            pltpu.VMEM((4, 2 * tokens, PIECE), BF16),
            pltpu.VMEM((2, 2 * tokens, PIECE), BF16),
            pltpu.VMEM((2 * tokens, PIECE), BF16),
            pltpu.VMEM((2, 2 * tokens, PIECE), BF16),
            pltpu.VMEM((2 * PIECE, PIECE), BF16),
            pltpu.VMEM((n, tokens, 128), BF16),
            pltpu.VMEM((n, tokens, PACK), BF16),
            dma(RING),
            dma(RING),
            dma(RING),
            dma(RING),
            dma(RING),
            dma(count),
            dma(RING),
            dma(4),
            dma(n - 1),
            dma(n - 1),
            dma(n - 1),
            dma(n - 1),
            dma(4, 6, 4),
            dma(2),
            pltpu.SemaphoreType.REGULAR((3,)),
            dma(16),
            dma(2),
            dma(2, 2),
            dma(2, 6),
            dma(4),
            dma(2, 2),
            dma(2, 8),
        ],
        compiler_params=params(63, collective_id=0, has_side_effects=True),
        cost_estimate=cost(6e10, 1e9),
        name="backward_step",
    )(ends, xs, gs, gates, w_gate, w_up, w_down, cxs, rest, diag, full, weights, packs, table, cot, wo, attn, x, h_attn, h, middle, wr, gains, lse)


def local(
    inputs,
    cotangent,
    doc_lengths,
    routes,
    attn_gain,
    ffn_gain,
    w_query,
    key_weight,
    value_weight,
    w_out,
    w_router,
    w_gate,
    w_up,
    w_down,
):
    rows = inputs.shape[2]
    width = inputs.shape[3]
    n = lax.axis_size("ctx")
    fsdp = lax.axis_size("fsdp")
    me, mine = lax.axis_index("ctx"), lax.axis_index("fsdp")
    tokens = 2 * rows
    length = tokens * n
    experts_here = w_gate.shape[0]
    number = experts_here // 2
    capacity = 5 * tokens * TOP // (4 * EXPERTS)
    capp = -(-capacity // 16) * 16
    shard = width // fsdp
    heads = QUERY_HEADS // n
    head_lanes = heads * HEAD_DIMENSION
    copies = n // KEY_VALUE_HEADS
    bits = group_bits(fsdp)

    x = inputs.reshape(tokens, width)
    cot = cotangent.reshape(tokens, width)
    side = me % 2
    base = (side * number).astype(jnp.int32).reshape(1)
    first = (mine * experts_here + side * number).astype(jnp.int32).reshape(1)
    index = jnp.stack([side * number, (1 - side) * number]).astype(jnp.int32)
    ends = doc_lengths
    table = jnp.asarray(rotary_table(length))

    out_part = w_out.reshape(shard // head_lanes, head_lanes, width)
    if head_lanes < 128:
        out_part = jnp.pad(out_part, ((0, 0), (0, 128 - head_lanes), (0, 0)))
    merge = lambda a: a.reshape(number, -1, a.shape[-1])

    if n == 8 and fsdp == 4:
        packs, h_attn, weights, wo, wr, cxs, gains = front(
            w_query,
            key_weight,
            value_weight,
            out_part,
            jnp.transpose(w_router),
            jnp.stack([attn_gain, ffn_gain]),
            x,
            table.reshape(2, n, rows, 256),
            jnp.transpose(routes[0], (0, 2, 1)),
            cot,
            capacity,
            n,
        )
        wo, wr = wo.reshape(n, 128, width), wr.reshape(width, 128)
        packs = packs.reshape(n, 2, rows, PACK)
        lse, full, middle, h_ffn, attn, xs, gs, gates, cx_rest, diag = attend(ends, packs, cxs, wo, wr, x, gains, length, number, capp)
        own, other, _, _, _, _, _, grad_x, mixed = backward_step(
            ends,
            merge(xs),
            merge(gs),
            merge(gates),
            w_gate,
            w_up,
            w_down,
            cxs,
            cx_rest,
            diag,
            full,
            weights,
            packs,
            table,
            cot,
            wo,
            attn,
            x,
            h_attn,
            h_ffn,
            middle,
            wr,
            gains,
            lse,
            n,
            length,
            capp,
        )
        own, other = own.reshape(-1, PIECE, PIECE), other.reshape(-1, PIECE, PIECE)
        shapes = [w.shape for w in (w_gate, w_up, w_down)]
        outs = tail(index, own, other, mixed, grad_x, shapes, shard)
        return (
            outs[3].reshape(inputs.shape),
            outs[4].reshape(inputs.shape),
            outs[10].reshape(shard),
            outs[11].reshape(shard),
            outs[5],
            outs[6],
            outs[7],
            outs[8],
            jnp.transpose(outs[9]),
            outs[0],
            outs[1],
            outs[2],
        )

    else:
        own_table = lax.dynamic_slice_in_dim(table.reshape(2, n, rows, 256), me, 1, 1).reshape(tokens, 256)
        query_part = w_query.reshape(shard, n, head_lanes)
        if head_lanes < 128:
            query_part = jnp.pad(query_part, ((0, 0), (0, 0), (0, 128 - head_lanes)))
        key_part = jnp.repeat(key_weight.reshape(shard, KEY_VALUE_HEADS, HEAD_DIMENSION), copies, 1)
        value_part = jnp.repeat(value_weight.reshape(shard, KEY_VALUE_HEADS, HEAD_DIMENSION), copies, 1)
        packed = jnp.concatenate([query_part, key_part, value_part], -1).reshape(shard, n * PACK)
        padding = 2 * 16 * (shard // 32 + 1) - shard
        gains = jnp.pad(jnp.stack([attn_gain, ffn_gain]), ((0, padding - 2), (0, n * PACK - shard)))
        packed = jnp.concatenate([packed, gains], 0)
        router_part = jnp.pad(w_router, ((0, 0), (0, 128 - EXPERTS)))
        weights = lax.all_gather(packed, "fsdp", axis=0)
        gain_one = weights[:, shard, :shard].reshape(1, width).astype(F32)
        gain_two = weights[:, shard + 1, :shard].reshape(1, width).astype(F32)
        wo = lax.all_gather(out_part, "fsdp", axis=0, tiled=True)
        wr = lax.all_gather(router_part, "fsdp", axis=0, tiled=True)
        cxs = group_gather(prep(jnp.transpose(routes[0], (0, 2, 1)), cot, capacity), bits)
        packs, h_attn = qkv(x, gain_one, weights, own_table, shard, n)
        packs = lax.all_to_all(packs, "ctx", split_axis=0, concat_axis=0, tiled=True).reshape(n, 2, rows, PACK)
        attn, lse, full = attn_forward(ends, packs, length)
        attn = lax.all_to_all(attn.reshape(n, tokens, 128), "ctx", split_axis=0, concat_axis=0, tiled=True)
        middle, h_ffn = middle_step(attn, wo, x, gain_two)
        xs, gs, gates = gather_rows(first, group_gather(h_ffn, bits), cxs, jnp.transpose(wr), number, capp)
        slots = cxs[:, tokens:]
    xs, gs, gates = merge(xs), merge(gs), merge(gates)
    pieces, outs, back, dgates = expert_step(base, xs, gs, gates, w_gate, w_up, w_down)
    y_part, gx_part = combine(first, slots, outs, back, dgates, tokens, capp)
    pieces = pieces.reshape(number * 6, PIECE, PIECE)
    gx = group_reduce(gx_part, bits)
    grad_middle, dwo, grad_attn, dwr, dgain_two = home_step(gx, h_ffn, middle, cot, wr, wo, gain_two, attn)
    grad_attn = lax.all_to_all(grad_attn, "ctx", split_axis=0, concat_axis=0, tiled=True).reshape(n, 2, rows, 128)
    grads = attn_backward(ends, packs, grad_attn, lse, full, table, length)
    grads = lax.all_to_all(grads.reshape(n, tokens, PACK), "ctx", split_axis=0, concat_axis=0, tiled=True)
    dw, grad_x, dgain_one = final_step(grads, weights, h_attn, x, gain_one, grad_middle, shard)
    mixed = middle + RESIDUAL * group_reduce(y_part, bits).astype(F32)
    own = line_sum(pieces, n)
    other = swap(own, "ctx", 1)
    scatter = lambda a: lax.psum(lax.psum_scatter(a, "fsdp", scatter_dimension=0, tiled=True), "ctx").astype(F32)
    dwo = scatter(dwo)[:, :head_lanes, :].reshape(shard, width)
    small = jnp.concatenate([dwr[:, :EXPERTS], dgain_two.reshape(width, 1).astype(BF16)], 1)
    small = scatter(jnp.pad(small, ((0, 0), (0, 127 - EXPERTS))))
    dwr, dgain_two = small[:, :EXPERTS], small[:, EXPERTS]
    dw = scatter(dw).reshape(shard, n, PACK)
    dgain_one = scatter(dgain_one.reshape(width).astype(BF16))

    outs = widen(index, own, other, [w.shape for w in (w_gate, w_up, w_down)])
    fold = lambda a: a.reshape(shard, KEY_VALUE_HEADS, copies, HEAD_DIMENSION).sum(2).reshape(shard, -1)
    return (
        mixed.reshape(inputs.shape),
        grad_x.reshape(inputs.shape),
        dgain_one,
        dgain_two,
        dw[:, :, :head_lanes].reshape(shard, -1),
        fold(dw[:, :, 128:192]),
        fold(dw[:, :, 192:256]),
        dwo,
        dwr,
        outs[0],
        outs[1],
        outs[2],
    )


def solution(mesh):
    tokens = P("fsdp", None, "ctx", None)
    one, two, three = P("fsdp"), P("fsdp", None), P("fsdp", None, None)
    return jax.shard_map(
        local,
        mesh=mesh,
        in_specs=(tokens, tokens, two, tokens, one, one, two, two, two, two, two, three, three, three),
        out_specs=(tokens, tokens, one, one, two, two, two, two, two, three, three, three),
        check_vma=False,
    )
```

```python
import functools

import jax
import jax.numpy as jnp
import numpy as np
from jax import lax
from jax.experimental import pallas as pl
from jax.experimental.pallas import tpu as pltpu
from jax.sharding import PartitionSpec as P

QUERY_HEADS = 16
KEY_VALUE_HEADS = 8
HEAD_DIMENSION = 64
EXPERTS = 32
TOP = 8

ATTN_SCALE = 0.015625
RESIDUAL = 0.22
NORM_EPS = 1e-06
ROPE_BASE = 10000.0
MASKED = -1e30

F32 = jnp.float32
BF16 = jnp.bfloat16
MIB = 1 << 20
NT = (((1,), (1,)), ((), ()))
TN = (((0,), (0,)), ((), ()))
BLK = 256
PACK = 256


def dot(a, b, dims=None):
    if dims is None:
        return jnp.dot(a, b, preferred_element_type=F32)
    return lax.dot_general(a, b, dims, preferred_element_type=F32)


def params(limit=56, **kw):
    return pltpu.CompilerParams(vmem_limit_bytes=limit * MIB, **kw)


def cost(flops, bytes_accessed):
    return pl.CostEstimate(flops=int(flops), bytes_accessed=int(bytes_accessed), transcendentals=0)


def lane_iota(shape):
    return lax.broadcasted_iota(jnp.int32, shape, len(shape) - 1)


def row_iota(shape):
    return lax.broadcasted_iota(jnp.int32, shape, len(shape) - 2)


def rotary_table(length):
    half = length // 2
    order = np.arange(half, dtype=np.float32)
    positions = np.concatenate([order, length - 1 - order]).astype(np.float32)
    m = np.arange(HEAD_DIMENSION // 2, dtype=np.float64)
    frequency = (ROPE_BASE ** (-2.0 * m / HEAD_DIMENSION)).astype(np.float32)
    angles = (positions[:, None] * frequency[None, :]).astype(np.float64)
    cosine, sine = np.cos(angles), np.sin(angles)
    cos_head = np.concatenate([cosine, cosine], -1)
    sin_head = np.concatenate([-sine, sine], -1)
    return np.concatenate([cos_head, cos_head, sin_head, sin_head], -1).astype(np.float32)


def turn(v, table, direction):
    lanes = lane_iota(v.shape)
    cosine = jnp.concatenate([table[:, :128], table[:, :128]], -1)
    sine = jnp.concatenate([table[:, 128:], table[:, 128:]], -1)
    turned = lanes < 3 * HEAD_DIMENSION
    swapped = jnp.where(lanes % HEAD_DIMENSION < HEAD_DIMENSION // 2, pltpu.roll(v, PACK - 32, 1), pltpu.roll(v, 32, 1))
    return jnp.where(turned, v * cosine + direction * (swapped * sine), v)


def norm_parts(values):
    inv_rms = lax.rsqrt(jnp.mean(values * values, -1, keepdims=True) + NORM_EPS)
    return values * inv_rms, inv_rms


def norm_back(grad_normed, normed, inv_rms):
    return inv_rms * (grad_normed - normed * jnp.mean(grad_normed * normed, -1, keepdims=True))


def prep_kernel(cap, routes_ref, cot_ref, out_ref):
    tokens, width = cot_ref.shape
    earlier = (row_iota((tokens, tokens)) < lane_iota((tokens, tokens))).astype(BF16)
    experts = row_iota((EXPERTS, tokens))
    base = jnp.zeros((EXPERTS, 1), F32)
    plus = jnp.zeros((EXPERTS, tokens), F32)
    for k in range(TOP):
        row = jnp.concatenate([routes_ref[0, k : k + 1, :], routes_ref[1, k : k + 1, :]], 1)
        chosen = experts == row
        ones = chosen.astype(F32)
        slot = dot(ones.astype(BF16), earlier) + base
        plus = plus + jnp.where(chosen & (slot < cap), slot + 1.0, 0.0)
        base = base + jnp.sum(ones, 1, keepdims=True)
    out_ref[:tokens, :] = cot_ref[...].astype(BF16)
    out_ref[tokens:, :] = jnp.concatenate([plus - 1.0, jnp.zeros((EXPERTS, width - tokens), F32)], -1).astype(BF16)


def prep(routes, cot, cap):
    tokens, width = cot.shape
    return pl.pallas_call(
        functools.partial(prep_kernel, cap),
        out_shape=jax.ShapeDtypeStruct((tokens + EXPERTS, width), BF16),
        compiler_params=params(),
        cost_estimate=cost(1e9, 2e6),
        name="prep",
    )(routes, cot)


def qkv_kernel(shard, x_ref, gain_ref, w_ref, table_ref, out_ref, h_ref):
    @pl.when(pl.program_id(0) == 0)
    def _():
        normed, _ = norm_parts(x_ref[...])
        h_ref[...] = (normed * gain_ref[...]).astype(BF16)

    total = None
    for f in range(w_ref.shape[0]):
        part = dot(h_ref[:, f * shard : (f + 1) * shard], w_ref[f, :shard, :])
        total = part if total is None else total + part
    for d in range(out_ref.shape[0]):
        out_ref[d] = turn(total[:, d * PACK : (d + 1) * PACK], table_ref[...], 1.0).astype(BF16)


def qkv(x, gain, weights, table, shard, n):
    tokens, width = x.shape
    fsdp, padded, _ = weights.shape
    return pl.pallas_call(
        functools.partial(qkv_kernel, shard),
        grid=(n // 2,),
        in_specs=[
            pl.BlockSpec((tokens, width), lambda i: (0, 0)),
            pl.BlockSpec((1, width), lambda i: (0, 0)),
            pl.BlockSpec((fsdp, padded, 2 * PACK), lambda i: (0, 0, i)),
            pl.BlockSpec((tokens, 256), lambda i: (0, 0)),
        ],
        out_specs=[
            pl.BlockSpec((2, tokens, PACK), lambda i: (i, 0, 0)),
            pl.BlockSpec((tokens, width), lambda i: (0, 0)),
        ],
        out_shape=[
            jax.ShapeDtypeStruct((n, tokens, PACK), BF16),
            jax.ShapeDtypeStruct((tokens, width), BF16),
        ],
        compiler_params=params(),
        cost_estimate=cost(2 * tokens * width * n * PACK, 8e6),
        name="qkv",
    )(x, gain, weights, table)


def pair_keys(kv):
    other = pltpu.roll(kv, 64, 1)
    low = lane_iota(kv.shape) < 64
    return jnp.where(low, kv, other), jnp.where(low, other, kv)


def stack_heads(q):
    low = lane_iota(q.shape) < 64
    zero = jnp.zeros_like(q)
    return jnp.concatenate([jnp.where(low, q, zero), jnp.where(low, zero, q)], 0)


def fold_heads(stacked):
    rows = stacked.shape[0] // 2
    return jnp.where(lane_iota((rows, 128)) < 64, stacked[:rows], stacked[rows:])


def query_rows(ends_ref, block, length):
    half = length // 2
    lanes = lane_iota((1, 2 * BLK))
    index = block * BLK + jnp.where(lanes < BLK, lanes, lanes - BLK)
    position = jnp.where(index < half, index, length + half - 1 - index)
    start = jnp.zeros_like(position)
    end = 0
    for j in range(3):
        end = end + ends_ref[0, j]
        start = jnp.where(position >= end, jnp.maximum(start, end), start)
    return position, start


def key_position(kb, length):
    half = length // 2
    index = kb * BLK + row_iota((BLK, 1))
    return jnp.where(index < half, index, length + half - 1 - index)


def block_loop(block, per_half, body, init):
    late = block >= per_half
    inner = jnp.where(late, block - per_half, block)

    def plain(kb, carry):
        return body(kb, True, carry)

    def masked(kb, carry):
        return body(kb, False, carry)

    carry = lax.fori_loop(0, jnp.where(late, per_half, inner), plain, init)
    return lax.fori_loop(block, jnp.where(late, 2 * per_half, block + 1), masked, carry)


def attn_forward_kernel(length, ends_ref, q_ref, pack_ref, out_ref, lse_ref, full_ref, keys, values_t, acc):
    block = pl.program_id(0)
    half = length // 2
    n, _, rows, _ = pack_ref.shape

    @pl.when(block == 0)
    def _():
        for h in range(2):
            for c in range(n):
                kk, vv = pair_keys(pack_ref[c, h, :, 128:256].astype(F32))
                at = h * half + c * rows
                keys[at : at + rows, :] = kk.astype(BF16)
                if rows % 128 == 0:
                    values_t[:, at : at + rows] = jnp.transpose(vv).astype(BF16)
        if rows % 128 != 0:
            for h in range(2):
                for c in range(0, n, 2):
                    pair = jnp.concatenate([pack_ref[c, h, :, 128:256], pack_ref[c + 1, h, :, 128:256]], 0)
                    _, vv = pair_keys(pair.astype(F32))
                    at = h * half + c * rows
                    values_t[:, at : at + 2 * rows] = jnp.transpose(vv).astype(BF16)

    q = q_ref[...].reshape(BLK, PACK)[:, :128]
    q2 = stack_heads((q.astype(F32) * ATTN_SCALE).astype(BF16))
    position, start = query_rows(ends_ref, block, length)
    bias = jnp.where(start > 0, MASKED, 0.0)
    acc[...] = jnp.zeros_like(acc)

    def body(kb, whole, carry):
        peak, total = carry
        at = pl.multiple_of(kb * BLK, BLK)
        scores = dot(keys[pl.ds(at, BLK), :], q2, NT)
        if whole:
            scores = scores + bias
        else:
            where = key_position(kb, length)
            scores = jnp.where((where <= position) & (where >= start), scores, MASKED)
        new_peak = jnp.maximum(peak, jnp.max(scores, 0, keepdims=True))
        weights = jnp.exp(scores - new_peak)
        fade = jnp.exp(peak - new_peak)
        total = total * fade + jnp.sum(weights, 0, keepdims=True)
        acc[...] = acc[...] * fade + dot(values_t[:, pl.ds(at, BLK)], weights.astype(BF16))
        return new_peak, total

    init = (jnp.full((1, 2 * BLK), MASKED, F32), jnp.zeros((1, 2 * BLK), F32))
    peak, total = block_loop(block, half // BLK, body, init)
    result = acc[...] / total
    full_ref[0] = result
    lse_ref[0] = peak + jnp.log(total)
    if out_ref is not None:
        folded = fold_heads(jnp.transpose(result)).astype(BF16)
        out_ref[...] = folded.reshape(out_ref.shape)


def attn_forward(ends, packs, length):
    n, _, rows, _ = packs.shape
    blocks, per = length // BLK, BLK // rows
    per_half = blocks // 2
    tiles = lambda i, ends: (lax.rem(i, per_half), i // per_half, 0, 0)
    return pl.pallas_call(
        functools.partial(attn_forward_kernel, length),
        grid_spec=pltpu.PrefetchScalarGridSpec(
            num_scalar_prefetch=1,
            grid=(blocks,),
            in_specs=[
                pl.BlockSpec((per, 1, rows, PACK), tiles),
                pl.BlockSpec(packs.shape, lambda i, ends: (0, 0, 0, 0)),
            ],
            out_specs=[
                pl.BlockSpec((per, 1, rows, 128), tiles),
                pl.BlockSpec((1, 1, 2 * BLK), lambda i, ends: (i, 0, 0)),
                pl.BlockSpec((1, 128, 2 * BLK), lambda i, ends: (i, 0, 0)),
            ],
            scratch_shapes=[
                pltpu.VMEM((length, 128), BF16),
                pltpu.VMEM((128, length), BF16),
                pltpu.VMEM((128, 2 * BLK), F32),
            ],
        ),
        out_shape=[
            jax.ShapeDtypeStruct((n, 2, rows, 128), BF16),
            jax.ShapeDtypeStruct((blocks, 1, 2 * BLK), F32),
            jax.ShapeDtypeStruct((blocks, 128, 2 * BLK), F32),
        ],
        compiler_params=params(),
        cost_estimate=cost(1.5e10, 6e6),
        name="attn_forward",
    )(ends, packs, packs)


def attn_backward_kernel(length, ends_ref, q_ref, g_ref, pack_ref, lse_ref, full_ref, table_ref, out_ref, keys, values, keys_t, grad_q, grad_k, grad_v, acc):
    block = pl.program_id(0)
    half = length // 2
    n, _, rows, _ = pack_ref.shape

    @pl.when(block == 0)
    def _():
        for h in range(2):
            for c in range(n):
                kk, vv = pair_keys(pack_ref[c, h, :, 128:256].astype(F32))
                at = h * half + c * rows
                keys[at : at + rows, :] = kk.astype(BF16)
                values[at : at + rows, :] = vv.astype(BF16)
        for b in range(length // BLK):
            keys_t[:, b * BLK : (b + 1) * BLK] = jnp.transpose(keys[b * BLK : (b + 1) * BLK, :].astype(F32)).astype(BF16)
        grad_k[...] = jnp.zeros_like(grad_k)
        grad_v[...] = jnp.zeros_like(grad_v)

    q2 = stack_heads((q_ref[...].reshape(BLK, PACK)[:, :128].astype(F32) * ATTN_SCALE).astype(BF16))
    g2 = stack_heads(g_ref[...].reshape(BLK, 128))
    position, start = query_rows(ends_ref, block, length)
    lse = lse_ref[0]
    shift = jnp.where(start > 0, MASKED, 0.0) - lse
    delta = jnp.sum(jnp.transpose(g2.astype(F32)) * full_ref[0], 0, keepdims=True)
    acc[...] = jnp.zeros_like(acc)

    def body(kb, whole, carry):
        at = pl.multiple_of(kb * BLK, BLK)
        scores = dot(keys[pl.ds(at, BLK), :], q2, NT)
        if whole:
            probs = jnp.exp(scores + shift)
        else:
            where = key_position(kb, length)
            probs = jnp.where((where <= position) & (where >= start), jnp.exp(scores - lse), 0.0)
        grad_probs = dot(values[pl.ds(at, BLK), :], g2, NT)
        grad_scores = (probs * (grad_probs - delta)).astype(BF16)
        acc[...] += dot(keys_t[:, pl.ds(at, BLK)], grad_scores)
        grad_k[pl.ds(at, BLK), :] += dot(grad_scores, q2)
        grad_v[pl.ds(at, BLK), :] += dot(probs.astype(BF16), g2)
        return carry

    block_loop(block, half // BLK, body, 0)
    grad_q[pl.ds(pl.multiple_of(block * BLK, BLK), BLK), :] = fold_heads(jnp.transpose(acc[...]))

    @pl.when(block == length // BLK - 1)
    def _():
        for h in range(2):
            for c in range(n):
                at = slice(h * half + c * rows, h * half + (c + 1) * rows)
                kk = grad_k[at, :]
                vv = grad_v[at, :]
                kk = kk + pltpu.roll(kk, 64, 1)
                vv = vv + pltpu.roll(vv, 64, 1)
                both = jnp.where(lane_iota(kk.shape) < 64, kk, vv)
                package = jnp.concatenate([grad_q[at, :] * ATTN_SCALE, both], -1)
                out_ref[c, h] = turn(package, table_ref[at, :], -1.0).astype(BF16)


def attn_backward(ends, packs, grads, lse, full, table, length):
    n, _, rows, _ = packs.shape
    blocks, per = length // BLK, BLK // rows
    per_half = blocks // 2
    tiles = lambda i, ends: (lax.rem(i, per_half), i // per_half, 0, 0)
    return pl.pallas_call(
        functools.partial(attn_backward_kernel, length),
        grid_spec=pltpu.PrefetchScalarGridSpec(
            num_scalar_prefetch=1,
            grid=(blocks,),
            in_specs=[
                pl.BlockSpec((per, 1, rows, PACK), tiles),
                pl.BlockSpec((per, 1, rows, 128), tiles),
                pl.BlockSpec(packs.shape, lambda i, ends: (0, 0, 0, 0)),
                pl.BlockSpec((1, 1, 2 * BLK), lambda i, ends: (i, 0, 0)),
                pl.BlockSpec((1, 128, 2 * BLK), lambda i, ends: (i, 0, 0)),
                pl.BlockSpec(table.shape, lambda i, ends: (0, 0)),
            ],
            out_specs=pl.BlockSpec(packs.shape, lambda i, ends: (0, 0, 0, 0)),
            scratch_shapes=[
                pltpu.VMEM((length, 128), BF16),
                pltpu.VMEM((length, 128), BF16),
                pltpu.VMEM((128, length), BF16),
                pltpu.VMEM((length, 128), F32),
                pltpu.VMEM((length, 128), F32),
                pltpu.VMEM((length, 128), F32),
                pltpu.VMEM((128, 2 * BLK), F32),
            ],
        ),
        out_shape=jax.ShapeDtypeStruct(packs.shape, BF16),
        compiler_params=params(),
        cost_estimate=cost(3e10, 8e6),
        name="attn_backward",
    )(ends, packs, grads, packs, lse, full, table)


def middle_kernel(attn_ref, wo_ref, x_ref, gain_ref, middle_ref, h_ref):
    total = None
    for c in range(attn_ref.shape[0]):
        part = dot(attn_ref[c], wo_ref[c])
        total = part if total is None else total + part
    middle = x_ref[...] + RESIDUAL * total
    middle_ref[...] = middle
    normed, _ = norm_parts(middle)
    h_ref[...] = (normed * gain_ref[...]).astype(BF16)


def middle_step(attn, wo, x, gain):
    tokens, width = x.shape
    return pl.pallas_call(
        middle_kernel,
        out_shape=[jax.ShapeDtypeStruct((tokens, width), F32), jax.ShapeDtypeStruct((tokens, width), BF16)],
        compiler_params=params(),
        cost_estimate=cost(2 * tokens * width * width, 5e6),
        name="middle",
    )(attn, wo, x, gain)


def own_row(table, row):
    return jnp.sum(jnp.where(row_iota(table.shape) == row, table, 0.0), 0, keepdims=True)


def one_hot(slots, first, number, capp):
    tokens = slots.shape[1]
    order = row_iota((capp, tokens)).astype(F32)
    return [(order == own_row(slots, first + j)).astype(F32) for j in range(number)]


def gather_kernel(number, capp, first_ref, h_ref, cx_ref, wrt_ref, x_ref, g_ref, gate_ref):
    tokens = h_ref.shape[1]
    first = first_ref[0]
    h = h_ref[0]
    slots = cx_ref[0, tokens:, :tokens].astype(F32)
    logits = dot(wrt_ref[...], h, NT)[:EXPERTS, :]
    raw = jnp.exp(logits - jnp.max(logits, 0, keepdims=True))
    router = raw / jnp.sum(raw, 0, keepdims=True)
    hots = one_hot(slots, first, number, capp)
    places = jnp.concatenate(hots, 0).astype(BF16)
    rows = dot(places, h).astype(BF16)
    grads = dot(places, cx_ref[0, :tokens, :]).astype(BF16)
    for j in range(number):
        at = slice(j * capp, (j + 1) * capp)
        x_ref[j, 0] = rows[at]
        g_ref[j, 0] = grads[at]
        gate = jnp.sum(hots[j] * own_row(router, first + j), 1, keepdims=True)
        gate_ref[j, 0] = jnp.broadcast_to(gate, (capp, 128))


def gather_rows(first, hs, cxs, wrt, number, capp):
    nb, tokens, width = hs.shape
    return pl.pallas_call(
        functools.partial(gather_kernel, number, capp),
        grid_spec=pltpu.PrefetchScalarGridSpec(
            num_scalar_prefetch=1,
            grid=(nb,),
            in_specs=[
                pl.BlockSpec((1, tokens, width), lambda b, f: (b, 0, 0)),
                pl.BlockSpec((1, tokens + EXPERTS, width), lambda b, f: (b, 0, 0)),
                pl.BlockSpec(wrt.shape, lambda b, f: (0, 0)),
            ],
            out_specs=[
                pl.BlockSpec((number, 1, capp, width), lambda b, f: (0, b, 0, 0)),
                pl.BlockSpec((number, 1, capp, width), lambda b, f: (0, b, 0, 0)),
                pl.BlockSpec((number, 1, capp, 128), lambda b, f: (0, b, 0, 0)),
            ],
        ),
        out_shape=[
            jax.ShapeDtypeStruct((number, nb, capp, width), BF16),
            jax.ShapeDtypeStruct((number, nb, capp, width), BF16),
            jax.ShapeDtypeStruct((number, nb, capp, 128), F32),
        ],
        compiler_params=params(),
        cost_estimate=cost(4 * nb * number * capp * tokens * width, 2e7),
        name="gather_rows",
    )(first, hs, cxs, wrt)


PIECE = 512


def expert_kernel(base_ref, x_ref, g_ref, gate_ref, wg_ref, wu_ref, wd_ref, piece_ref, out_ref, rows_ref, dg_ref):
    x = x_ref[0]
    gate = gate_ref[0][:, :1]
    grad_ffn = RESIDUAL * g_ref[0].astype(F32)
    go = (gate * grad_ffn).astype(BF16)
    part = wg_ref.shape[2] // 2
    out = rows = None
    for chunk in range(2):
        at = slice(chunk * part, (chunk + 1) * part)
        wg, wu, wd = wg_ref[0, :, at], wu_ref[0, :, at], wd_ref[0, at, :]
        pre_gate = dot(x, wg)
        pre_up = dot(x, wu)
        sig = jax.nn.sigmoid(pre_gate)
        hidden = (pre_gate * sig * pre_up).astype(BF16)
        out_part = dot(hidden, wd)
        grad_hidden = dot(go, wd, NT)
        grad_gate = (grad_hidden * pre_up * sig * (1.0 + pre_gate * (1.0 - sig))).astype(BF16)
        grad_up = (grad_hidden * pre_gate * sig).astype(BF16)
        row_part = dot(grad_gate, wg, NT) + dot(grad_up, wu, NT)
        dwg = dot(x, grad_gate, TN).astype(BF16)
        dwu = dot(x, grad_up, TN).astype(BF16)
        dwd = dot(hidden, go, TN).astype(BF16)
        for half in range(2):
            side = slice(half * PIECE, (half + 1) * PIECE)
            piece_ref[0, 3 * chunk + half, :, :part] = dwg[side]
            piece_ref[0, 3 * chunk + half, :, part:] = dwu[side]
            piece_ref[0, 3 * chunk + 2, half * part : (half + 1) * part, :] = dwd[:, side]
        out = out_part if out is None else out + out_part
        rows = row_part if rows is None else rows + row_part
    out = out.astype(BF16).astype(F32)
    out_ref[0] = (gate * out).astype(BF16)
    rows_ref[0] = rows.astype(BF16)
    grad = jnp.sum(grad_ffn * out, 1, keepdims=True)
    dg_ref[0] = jnp.broadcast_to(grad, dg_ref.shape[1:])


def expert_step(base, xs, gs, gates, w_gate, w_up, w_down):
    number, rows, width = xs.shape
    ff = w_gate.shape[2]
    row = lambda e, b: (e, 0, 0)
    weight = lambda e, b: (b[0] + e, 0, 0)
    return pl.pallas_call(
        expert_kernel,
        grid_spec=pltpu.PrefetchScalarGridSpec(
            num_scalar_prefetch=1,
            grid=(number,),
            in_specs=[
                pl.BlockSpec((1, rows, width), row),
                pl.BlockSpec((1, rows, width), row),
                pl.BlockSpec((1, rows, 128), row),
                pl.BlockSpec((1, width, ff), weight),
                pl.BlockSpec((1, width, ff), weight),
                pl.BlockSpec((1, ff, width), weight),
            ],
            out_specs=[
                pl.BlockSpec((1, 6, PIECE, PIECE), lambda e, b: (e, 0, 0, 0)),
                pl.BlockSpec((1, rows, width), row),
                pl.BlockSpec((1, rows, width), row),
                pl.BlockSpec((1, rows, 128), row),
            ],
        ),
        out_shape=[
            jax.ShapeDtypeStruct((number, 6, PIECE, PIECE), BF16),
            jax.ShapeDtypeStruct((number, rows, width), BF16),
            jax.ShapeDtypeStruct((number, rows, width), BF16),
            jax.ShapeDtypeStruct((number, rows, 128), F32),
        ],
        compiler_params=params(60),
        cost_estimate=cost(18 * number * rows * width * ff, 5e7),
        name="expert_step",
    )(base, xs, gs, gates, w_gate, w_up, w_down)


def combine_kernel(number, capp, first_ref, slot_ref, outs, rows, grads, y_ref, gx_ref):
    tokens = y_ref.shape[1]
    width = y_ref.shape[2]
    first = first_ref[0]
    slots = slot_ref[0][:, :tokens].astype(F32)
    hots = one_hot(slots, first, number, capp)
    places = jnp.concatenate(hots, 0).astype(BF16)
    y_ref[0] = dot(places, outs[:, 0].reshape(number * capp, width), TN).astype(BF16)
    gx_ref[0, :tokens] = dot(places, rows[:, 0].reshape(number * capp, width), TN).astype(BF16)
    extra = jnp.zeros((EXPERTS, 2 * tokens), F32)
    for j in range(number):
        grad = jnp.sum(hots[j] * grads[j, 0][:, :1], 0, keepdims=True)
        high = grad.astype(BF16).astype(F32)
        both = jnp.concatenate([high, grad - high], 1)
        extra = jnp.where(row_iota(extra.shape) == first + j, both, extra)
    rest = jnp.zeros((EXPERTS, width - 2 * tokens), F32)
    gx_ref[0, tokens:] = jnp.concatenate([extra, rest], 1).astype(BF16)


def combine(first, slots, outs, rows, grads, tokens, capp):
    number = outs.shape[0]
    nb, _, width = slots.shape
    split = lambda a: a.reshape(number, nb, capp, a.shape[-1])
    wide = pl.BlockSpec((number, 1, capp, width), lambda b, f: (0, b, 0, 0))
    thin = pl.BlockSpec((number, 1, capp, 128), lambda b, f: (0, b, 0, 0))
    return pl.pallas_call(
        functools.partial(combine_kernel, number, capp),
        grid_spec=pltpu.PrefetchScalarGridSpec(
            num_scalar_prefetch=1,
            grid=(nb,),
            in_specs=[pl.BlockSpec((1, EXPERTS, width), lambda b, f: (b, 0, 0))] + [wide, wide, thin],
            out_specs=[
                pl.BlockSpec((1, tokens, width), lambda b, f: (b, 0, 0)),
                pl.BlockSpec((1, tokens + EXPERTS, width), lambda b, f: (b, 0, 0)),
            ],
        ),
        out_shape=[
            jax.ShapeDtypeStruct((nb, tokens, width), BF16),
            jax.ShapeDtypeStruct((nb, tokens + EXPERTS, width), BF16),
        ],
        compiler_params=params(),
        cost_estimate=cost(4 * nb * number * capp * tokens * width, 2e7),
        name="combine",
    )(first, slots, split(outs), split(rows), split(grads))


def home_kernel(gx_ref, h_ref, middle_ref, cot_ref, wr_ref, wo_ref, gain_ref, attn_ref, grad_middle_ref, dwo_ref, ga_ref, dwr_ref, dgain_ref):
    tokens, width = h_ref.shape
    h = h_ref[...]
    gain = gain_ref[...]
    extra = gx_ref[tokens:, :].astype(F32)
    grad_router = extra[:, :tokens] + extra[:, tokens : 2 * tokens]
    grad_router = jnp.transpose(jnp.concatenate([grad_router, jnp.zeros((128 - EXPERTS, tokens), F32)], 0))
    logits = dot(h, wr_ref[...])
    logits = jnp.where(lane_iota(logits.shape) < EXPERTS, logits, MASKED)
    raw = jnp.exp(logits - jnp.max(logits, -1, keepdims=True))
    router = raw / jnp.sum(raw, -1, keepdims=True)
    grad_logits = (router * (grad_router - jnp.sum(router * grad_router, -1, keepdims=True))).astype(BF16)
    dwr_ref[...] = dot(h, grad_logits, TN).astype(BF16)
    grad_h = gx_ref[:tokens, :].astype(F32) + dot(grad_logits, wr_ref[...], NT)
    normed, scale = norm_parts(middle_ref[...])
    dgain_ref[...] = jnp.sum(grad_h * normed, 0, keepdims=True)
    grad_middle = cot_ref[...] + norm_back(grad_h * gain, normed, scale)
    grad_middle_ref[...] = grad_middle
    grad_branch = (RESIDUAL * grad_middle).astype(BF16)
    for c in range(attn_ref.shape[0]):
        dwo_ref[c] = dot(attn_ref[c], grad_branch, TN).astype(BF16)
        ga_ref[c] = dot(grad_branch, wo_ref[c], NT).astype(BF16)


def home_step(gx, h, middle, cot, wr, wo, gain, attn):
    tokens, width = h.shape
    n = attn.shape[0]
    return pl.pallas_call(
        home_kernel,
        out_shape=[
            jax.ShapeDtypeStruct((tokens, width), F32),
            jax.ShapeDtypeStruct((n, 128, width), BF16),
            jax.ShapeDtypeStruct((n, tokens, 128), BF16),
            jax.ShapeDtypeStruct((width, 128), BF16),
            jax.ShapeDtypeStruct((1, width), F32),
        ],
        compiler_params=params(),
        cost_estimate=cost(4 * tokens * width * width, 1e7),
        name="home_step",
    )(gx, h, middle, cot, wr, wo, gain, attn)


def final_kernel(shard, grads_ref, w_ref, h_ref, x_ref, gain_ref, grad_middle_ref, dw_ref, grad_x_ref, dgain_ref, total):
    c = pl.program_id(0)
    g = grads_ref[0]
    dw_ref[...] = dot(h_ref[...], g, TN).astype(BF16)

    @pl.when(c == 0)
    def _():
        total[...] = jnp.zeros_like(total)

    for f in range(w_ref.shape[0]):
        total[:, f * shard : (f + 1) * shard] += dot(g, w_ref[f, :shard, :], NT)

    @pl.when(c == pl.num_programs(0) - 1)
    def _():
        normed, scale = norm_parts(x_ref[...])
        grad_h = total[...]
        dgain_ref[...] = jnp.sum(grad_h * normed, 0, keepdims=True)
        grad_x_ref[...] = grad_middle_ref[...] + norm_back(grad_h * gain_ref[...], normed, scale)


def final_step(grads, weights, h, x, gain, grad_middle, shard):
    n, tokens, _ = grads.shape
    width = x.shape[1]
    fsdp, padded, _ = weights.shape
    same = lambda c: (0, 0)
    return pl.pallas_call(
        functools.partial(final_kernel, shard),
        grid=(n,),
        in_specs=[
            pl.BlockSpec((1, tokens, PACK), lambda c: (c, 0, 0)),
            pl.BlockSpec((fsdp, padded, PACK), lambda c: (0, 0, c)),
            pl.BlockSpec((tokens, width), same),
            pl.BlockSpec((tokens, width), same),
            pl.BlockSpec((1, width), same),
            pl.BlockSpec((tokens, width), same),
        ],
        out_specs=[
            pl.BlockSpec((width, PACK), lambda c: (0, c)),
            pl.BlockSpec((tokens, width), same),
            pl.BlockSpec((1, width), same),
        ],
        out_shape=[
            jax.ShapeDtypeStruct((width, n * PACK), BF16),
            jax.ShapeDtypeStruct((tokens, width), F32),
            jax.ShapeDtypeStruct((1, width), F32),
        ],
        scratch_shapes=[pltpu.VMEM((tokens, width), F32)],
        compiler_params=params(),
        cost_estimate=cost(4 * tokens * width * n * PACK, 1.2e7),
        name="final_step",
    )(grads, weights, h, x, gain, grad_middle)


def widen_kernel(number, index_ref, own_ref, other_ref, gate_ref, up_ref, down_ref):
    part = gate_ref.shape[2] // 2

    def write(ref):
        for chunk in range(2):
            columns = slice(chunk * part, (chunk + 1) * part)
            for half in range(2):
                for q in range(2):
                    at = slice(half * PIECE + q * 256, half * PIECE + (q + 1) * 256)
                    gate_ref[0, at, columns] = ref[6 * chunk + 2 * half + q, :, :part].astype(F32)
                    up_ref[0, at, columns] = ref[6 * chunk + 2 * half + q, :, part:].astype(F32)
                down_ref[0, columns, half * PIECE : (half + 1) * PIECE] = ref[6 * chunk + 4 + half].astype(F32)

    @pl.when(pl.program_id(0) == 0)
    def _():
        write(own_ref)

    @pl.when(pl.program_id(0) == 1)
    def _():
        write(other_ref)


def tail_kernel(number, index_ref, own_ref, other_ref, own_small_ref, other_small_ref, own_rest_ref, other_rest_ref, mixed_in, grad_in, gate_ref, up_ref, down_ref, mixed_ref, grad_ref, dwq_ref, dwk_ref, dwv_ref, dwo_ref, dwr_ref, g1_ref, g2_ref):
    widen_kernel(number, index_ref, own_ref, other_ref, gate_ref, up_ref, down_ref)
    mixed_ref[...] = mixed_in[...]
    grad_ref[...] = grad_in[...]

    @pl.when((pl.program_id(0) == 0) & (pl.program_id(1) == 0))
    def _():
        for which, (ref, rest) in enumerate(((own_small_ref, own_rest_ref), (other_small_ref, other_rest_ref))):
            part = index_ref[which] // number
            at = pl.ds(pl.multiple_of(part * 128, 128), 128)
            for q in range(4):
                block = ref[1 + q // 2, q % 2 * 128 : (q % 2 + 1) * 128, :].astype(F32)
                dwq_ref[at, q * 256 : q * 256 + 128] = block[:, :128]
                dwq_ref[at, q * 256 + 128 : (q + 1) * 256] = block[:, 256:384]
                one, two = block[:, 128:256], block[:, 384:]
                low = lane_iota(one.shape) < HEAD_DIMENSION
                dwk_ref[at, q * 128 : (q + 1) * 128] = jnp.where(low, one, pltpu.roll(two, 64, 1))
                dwv_ref[at, q * 128 : (q + 1) * 128] = jnp.where(low, pltpu.roll(one, 64, 1), two)
            dwo_ref[at, :PIECE] = ref[0, 0:128, :].astype(F32)
            dwo_ref[at, PIECE:] = ref[0, 128:256, :].astype(F32)
            low_rows = rest[0].astype(F32)
            for q in range(EXPERTS // 8):
                dwr_ref[q * 8 : (q + 1) * 8, at] = low_rows[:8, q * 128 : (q + 1) * 128]
            g1_ref[pl.ds(part, 1), :] = low_rows[8:9, :128]
            g2_ref[pl.ds(part, 1), :] = low_rows[9:10, :128]


def expert_specs(number, shapes):
    last = number - 1
    ins = [
        pl.BlockSpec((12, PIECE // 2, PIECE), lambda s, e, at: (jnp.where(s == 0, e, last), 0, 0)),
        pl.BlockSpec((12, PIECE // 2, PIECE), lambda s, e, at: (jnp.where(s == 0, 0, e), 0, 0)),
    ]
    outs = [pl.BlockSpec((1,) + tuple(shape[1:]), lambda s, e, at: (at[s] + e, 0, 0)) for shape in shapes]
    return ins, outs, [jax.ShapeDtypeStruct(shape, F32) for shape in shapes]


def widen(index, own, other, shapes):
    number = shapes[0][0] // 2
    ins, outs, out_shapes = expert_specs(number, shapes)
    return pl.pallas_call(
        functools.partial(widen_kernel, number),
        grid_spec=pltpu.PrefetchScalarGridSpec(num_scalar_prefetch=1, grid=(2, number), in_specs=ins, out_specs=outs),
        out_shape=out_shapes,
        compiler_params=params(),
        cost_estimate=cost(0, 1e8),
        name="widen",
    )(index, own, other)


def tail(index, own, other, own_rest, other_rest, mixed, grad_x, shapes, shard):
    number = shapes[0][0] // 2
    tokens, width = mixed.shape
    ins, outs, out_shapes = expert_specs(number, shapes)
    small = pl.BlockSpec((3, PIECE // 2, PIECE), lambda s, e, at: (4 * number, 0, 0))
    rest = pl.BlockSpec(own_rest.shape, lambda s, e, at: (0, 0, 0))
    rows = pl.BlockSpec((tokens // (2 * number), width), lambda s, e, at: (s * number + e, 0))
    small_shapes = [(shard, width), (shard, width // 2), (shard, width // 2), (shard, width), (EXPERTS, shard), (2, 128), (2, 128)]
    whole = [pl.BlockSpec(shape, lambda s, e, at: (0, 0)) for shape in small_shapes]
    return pl.pallas_call(
        functools.partial(tail_kernel, number),
        grid_spec=pltpu.PrefetchScalarGridSpec(
            num_scalar_prefetch=1,
            grid=(2, number),
            in_specs=ins + [small, small, rest, rest, rows, rows],
            out_specs=outs + [rows, rows] + whole,
        ),
        out_shape=out_shapes
        + [jax.ShapeDtypeStruct((tokens, width), F32)] * 2
        + [jax.ShapeDtypeStruct(shape, F32) for shape in small_shapes],
        compiler_params=params(),
        cost_estimate=cost(0, 1e8),
        name="tail",
    )(index, own, other, own, other, own_rest, other_rest, mixed, grad_x)


def swap(value, axis, bit):
    size = lax.axis_size(axis)
    return lax.ppermute(value, axis, [(i, i ^ bit) for i in range(size)])


def group_bits(fsdp):
    bits = [("fsdp", 1 << b) for b in range(1, fsdp.bit_length() - 1)]
    return bits + [("ctx", 1), ("fsdp", 1)]


def group_gather(value, bits):
    stacked = value[None]
    for axis, bit in bits:
        stacked = jnp.concatenate([stacked, swap(stacked, axis, bit)], 0)
    return stacked


def group_reduce(stacked, bits):
    for axis, bit in reversed(bits):
        half = stacked.shape[0] // 2
        arrived = swap(stacked[half:], axis, bit)
        stacked = (stacked[:half].astype(F32) + arrived.astype(F32)).astype(stacked.dtype)
    return stacked[0]


def line_sum(value, ctx):
    pairs = ctx // 2
    if pairs != 4:
        bit = 2
        while bit < ctx:
            value = value + swap(value, "ctx", bit)
            bit *= 2
        return value
    at = lambda z, y: 2 * z + y
    inward = [(at(0, y), at(1, y)) for y in range(2)] + [(at(3, y), at(2, y)) for y in range(2)]
    across = [(at(1, y), at(2, y)) for y in range(2)] + [(at(2, y), at(1, y)) for y in range(2)]
    outward = [(b, a) for a, b in inward]
    value = value + lax.ppermute(value, "ctx", inward)
    value = value + lax.ppermute(value, "ctx", across)
    arrived = lax.ppermute(value, "ctx", outward)
    z = lax.axis_index("ctx") // 2
    return jnp.where((z == 0) | (z == 3), arrived, value)


MESH = pl.DeviceIdType.MESH


def flip(index, bit):
    return jnp.where((index // bit) % 2 == 0, index + bit, index - bit)


def send(src, dst, send_sem, recv_sem, device):
    return pltpu.make_async_remote_copy(src_ref=src, dst_ref=dst, send_sem=send_sem, recv_sem=recv_sem, device_id=device, device_id_type=MESH)


def neighbours():
    ctx, fsdp = lax.axis_index("ctx"), lax.axis_index("fsdp")
    side, across = flip(ctx, 1), flip(fsdp, 2)
    core = {"fsdp": flip(fsdp, 1)}
    return core, [{"fsdp": across}, {"ctx": side}, {"ctx": side, "fsdp": across}]


def greet(devices):
    barrier = pltpu.get_barrier_semaphore()
    for device in devices:
        pl.semaphore_signal(barrier, inc=1, device_id=device, device_id_type=MESH)
    pl.semaphore_wait(barrier, len(devices))


def others(n):
    ctx = lax.axis_index("ctx")
    return [lax.rem(ctx + d, n) for d in range(1, n)]


def exchange_start(src, dst, send_sems, recv_sems, local_sem, n):
    ctx = lax.axis_index("ctx")
    for d, c in enumerate(others(n)):
        send(src.at[c], dst.at[ctx], send_sems.at[d], recv_sems.at[d], {"ctx": c}).start()
    pltpu.make_async_copy(src.at[ctx], dst.at[ctx], local_sem).start()


def exchange_wait(src, dst, send_sems, recv_sems, local_sem, n, arrived=None):
    ctx = lax.axis_index("ctx")
    pltpu.make_async_copy(src.at[ctx], dst.at[ctx], local_sem).wait()
    if arrived is not None:
        arrived(ctx)
    for d in range(n - 1):
        source = lax.rem(ctx + n - 1 - d, n)
        send(src.at[source], dst.at[source], send_sems.at[d], recv_sems.at[d], {"ctx": source}).wait_recv()
        if arrived is not None:
            arrived(source)
    for d, c in enumerate(others(n)):
        send(src.at[c], dst.at[ctx], send_sems.at[d], recv_sems.at[d], {"ctx": c}).wait_send()


def turn_half(v, table, direction, lanes_turned):
    lanes = lane_iota(v.shape)
    swapped = jnp.where(lanes % HEAD_DIMENSION < HEAD_DIMENSION // 2, pltpu.roll(v, 96, 1), pltpu.roll(v, 32, 1))
    return jnp.where(lanes < lanes_turned, v * table[:, :128] + direction * (swapped * table[:, 128:]), v)


def front_kernel(n, cap, wq_ref, wk_ref, wv_ref, wo_part_ref, wr_raw_ref, gain_ref, x_ref, table_ref, routes_ref, cot_ref, packs_ref, h_ref, weights_ref, wo_ref, wr_ref, cxs_ref, gains_ref, wall, packed_ref, wr_part_ref, cx, table, normed_ref, total, out, exch_send, exch_recv, full_send, full_recv, x_send, x_recv, y_send, y_recv, xs_send, xs_recv, ys_send, ys_recv, cx_send, cx_recv, local_sems):
    tokens, width = x_ref.shape
    shard = width // 4
    ctx, fsdp = lax.axis_index("ctx"), lax.axis_index("fsdp")
    parity = lax.rem(ctx, 2)
    core, group = neighbours()
    far, near = group[0], group[1]
    sibling, distant = flip(fsdp, 1), flip(fsdp, 2)
    other = flip(distant, 1)
    for k in range(2):
        pltpu.make_async_copy(table_ref.at[k, ctx], table.at[k], local_sems.at[6 + k]).start()

    pair = HEAD_DIMENSION * 2
    for c in range(0, n, 2):
        keys, values = wk_ref[:, c // 2 * pair : (c // 2 + 1) * pair].astype(F32), wv_ref[:, c // 2 * pair : (c // 2 + 1) * pair].astype(F32)
        low = lane_iota(keys.shape) < HEAD_DIMENSION
        packed_ref[0, :shard, c * 128 : (c + 1) * 128] = jnp.where(low, keys, pltpu.roll(values, 64, 1)).astype(BF16)
        packed_ref[0, :shard, (c + 1) * 128 : (c + 2) * 128] = jnp.where(low, pltpu.roll(keys, 64, 1), values).astype(BF16)
    below = packed_ref.shape[1] - shard
    packed_ref[0, shard:, :] = jnp.zeros((below, width), BF16)
    row = row_iota((16, shard))
    gains = gain_ref[...].astype(F32)
    gain_rows = jnp.where(row == 0, gains[0:1], jnp.where(row == 1, gains[1:2], 0.0))
    packed_ref[0, shard : shard + 16, :shard] = gain_rows.astype(BF16)
    packed_ref[1, :shard, :] = wq_ref[...]
    packed_ref[1, shard:, :] = jnp.zeros((below, width), BF16)
    router = jnp.concatenate([wr_raw_ref[...].astype(F32), jnp.zeros((128 - EXPERTS, shard), F32)], 0)
    wr_part_ref[...] = jnp.transpose(router).astype(BF16)
    greet([core, far] + [{"ctx": c} for c in others(n)])

    half_rows = packed_ref.shape[1] // 2

    def cut(k, part):
        if k < 2:
            return pl.ds(pl.multiple_of(part * half_rows, 16), half_rows)
        if k == 2:
            return pl.ds(part, 1)
        return pl.ds(pl.multiple_of(part * (shard // 2), 16), shard // 2)

    sources = [packed_ref.at[0], packed_ref.at[1], wo_part_ref, wr_part_ref]
    targets = [wall.at[0], wall.at[1], wo_ref, wr_ref]

    def whole(k):
        return send(sources[k], targets[k].at[fsdp], full_send.at[k], full_recv.at[k], core)

    def own(k):
        return pltpu.make_async_copy(sources[k], targets[k].at[fsdp], local_sems.at[k])

    def to_far(k):
        return send(sources[k].at[cut(k, parity)], targets[k].at[fsdp, cut(k, parity)], x_send.at[k], x_recv.at[k], far)

    def pass_on(k, part, sems, device):
        ref = targets[k].at[distant, cut(k, part)]
        return send(ref, ref, sems[0].at[k], sems[1].at[k], device)

    def sibling_arrived(k):
        ref = targets[k].at[sibling]
        send(ref, ref, full_send.at[k], full_recv.at[k], core).wait_recv()

    def far_arrived(k):
        ref = targets[k].at[distant, cut(k, parity)]
        send(ref, ref, x_send.at[k], x_recv.at[k], far).wait_recv()
        pass_on(k, parity, (y_send, y_recv), near).start()
        pass_on(k, parity, (xs_send, xs_recv), core).start()

    def near_arrived(k):
        pass_on(k, 1 - parity, (y_send, y_recv), near).wait_recv()
        pass_on(k, 1 - parity, (ys_send, ys_recv), core).start()

    def core_arrived(k):
        for part, sems in ((parity, (xs_send, xs_recv)), (1 - parity, (ys_send, ys_recv))):
            ref = targets[k].at[other, cut(k, part)]
            send(ref, ref, sems[0].at[k], sems[1].at[k], core).wait_recv()

    for k in range(2):
        to_far(k).start()
    for k in range(2):
        whole(k).start()
        own(k).start()

    prep_kernel(cap, routes_ref, cot_ref, cx)
    pltpu.make_async_copy(cx, cxs_ref.at[0], local_sems.at[4]).start()
    normed, _ = norm_parts(x_ref[...])
    normed_ref[...] = normed

    def project(k, block, begin):
        at = pl.ds(pl.multiple_of(block * shard, shard), shard)
        if k == 0:
            gain = wall[0, block, shard : shard + 16, :shard].astype(F32)
            gains_ref[:, at] = gain
            h_ref[:, at] = (normed_ref[:, at] * gain[:1]).astype(BF16)
        part = dot(h_ref[:, at], wall[k, block, :shard, :])
        total[k] = part if begin else total[k] + part

    for k in range(2):
        own(k).wait()
        project(k, fsdp, True)
        sibling_arrived(k)
        project(k, sibling, False)
        if k == 0:
            far_arrived(0)

    exchanges = []

    def emit(k):
        lanes = slice(128, 256) if k == 0 else slice(0, 128)
        for c in range(n):
            out[c, :, lanes] = turn_half(total[k, :, c * 128 : (c + 1) * 128], angles, 1.0, 64 if k == 0 else 128).astype(BF16)
        cut_lanes = pl.ds(128 if k == 0 else 0, 128)
        source, target = out.at[:, :, cut_lanes], packs_ref.at[:, :, cut_lanes]
        exchanges.append((source, target, exch_send.at[k], exch_recv.at[k], local_sems.at[8 + k], n))
        exchange_start(*exchanges[-1])

    near_arrived(0)
    project(0, distant, False)
    core_arrived(0)
    project(0, other, False)
    for k in range(2):
        pltpu.make_async_copy(table_ref.at[k, ctx], table.at[k], local_sems.at[6 + k]).wait()
    angles = table[...].reshape(tokens, 256)
    emit(0)
    far_arrived(1)
    for k in (2, 3):
        own(k).start()
        whole(k).start()
        to_far(k).start()
    send(cx, cxs_ref.at[1], cx_send.at[0], cx_recv.at[0], far).start()
    near_arrived(1)
    project(1, distant, False)
    core_arrived(1)
    project(1, other, False)
    emit(1)
    keep = pltpu.make_async_copy(wall, weights_ref, local_sems.at[5])
    keep.start()
    for k in (2, 3):
        far_arrived(k)
    for k in (2, 3):
        near_arrived(k)
    for k in (2, 3):
        core_arrived(k)
        sibling_arrived(k)
        own(k).wait()
    for exchange in exchanges:
        exchange_wait(*exchange)
    for k in range(4):
        whole(k).wait_send()
        to_far(k).wait_send()
        pass_on(k, parity, (y_send, y_recv), near).wait_send()
        pass_on(k, parity, (xs_send, xs_recv), core).wait_send()
        pass_on(k, 1 - parity, (ys_send, ys_recv), core).wait_send()
    send(cx, cxs_ref.at[1], cx_send.at[0], cx_recv.at[0], far).wait()
    pltpu.make_async_copy(cx, cxs_ref.at[0], local_sems.at[4]).wait()
    keep.wait()


def front(wq, wk, wv, wo_part, wr, gains, x, table, routes, cot, cap, n):
    tokens, width = x.shape
    shard = wq.shape[0]
    hbm, vmem = pl.BlockSpec(memory_space=pl.ANY), pl.BlockSpec(memory_space=pltpu.VMEM)
    dma = lambda *k: pltpu.SemaphoreType.DMA(k)
    shaped = lambda shape, dtype=BF16: jax.ShapeDtypeStruct(shape, dtype)
    cx_shape = (tokens + EXPERTS, width)
    padded = 2 * 16 * (shard // 32 + 1)
    return pl.pallas_call(
        functools.partial(front_kernel, n, cap),
        in_specs=[vmem, vmem, vmem, hbm, vmem, vmem, vmem, hbm, vmem, vmem],
        out_specs=[hbm, vmem, hbm, hbm, hbm, hbm, vmem],
        out_shape=[
            shaped((n, tokens, PACK)),
            shaped((tokens, width)),
            shaped((2, 4, padded, width)),
            shaped((4,) + wo_part.shape),
            shaped((4, shard, 128)),
            shaped((2,) + cx_shape),
            shaped((16, width), F32),
        ],
        scratch_shapes=[
            pltpu.VMEM((2, 4, padded, width), BF16),
            pltpu.VMEM((2, padded, width), BF16),
            pltpu.VMEM((shard, 128), BF16),
            pltpu.VMEM(cx_shape, BF16),
            pltpu.VMEM((2, tokens // 2, 256), F32),
            pltpu.VMEM((tokens, width), F32),
            pltpu.VMEM((2, tokens, width), F32),
            pltpu.VMEM((n, tokens, PACK), BF16),
            dma(2, n - 1),
            dma(2, n - 1),
        ]
        + [dma(4)] * 10
        + [dma(1), dma(1), dma(10)],
        compiler_params=params(collective_id=1, has_side_effects=True),
        cost_estimate=cost(2e9, 5e7),
        name="front",
    )(wq, wk, wv, wo_part, wr, gains, x, table, routes, cot)


def attend_kernel(
    length,
    n,
    number,
    capp,
    ends_ref,
    q_ref,
    pack_ref,
    cxs_ref,
    wo_hbm,
    wr_ref,
    x_hbm,
    gain_ref,
    lse_ref,
    full_ref,
    middle_ref,
    h_ref,
    kept_ref,
    xs_ref,
    gs_ref,
    gates_ref,
    rest_ref,
    diag_ref,
    keys,
    values_t,
    acc,
    result,
    arrived,
    hs,
    wo_ref,
    x_ref,
    cx,
    rows_out,
    grads_out,
    gates_out,
    near_send,
    near_recv,
    core_send,
    core_recv,
    exch_send,
    exch_recv,
    hop_send,
    hop_recv,
    cross_send,
    cross_recv,
    cx_send,
    cx_recv,
    fwd_send,
    fwd_recv,
    local_sems,
    own_sems,
    load_sems,
    store_sems,
):
    block = pl.program_id(0)
    last = pl.num_programs(0) - 1
    tokens, width = x_ref.shape
    split = tokens // 2
    per = BLK // split
    per_half = length // BLK // 2
    ctx, fsdp = lax.axis_index("ctx"), lax.axis_index("fsdp")
    first = (fsdp * 2 + lax.rem(ctx, 2)) * number
    core, group = neighbours()
    near = group[1]
    copies = [pltpu.make_async_copy(wo_hbm, wo_ref, local_sems.at[0]), pltpu.make_async_copy(x_hbm, x_ref, local_sems.at[1])]

    def to_near():
        return send(cxs_ref.at[0], rest_ref.at[0], near_send.at[0], near_recv.at[0], near)

    def to_core(i):
        src = cxs_ref.at[i] if i < 2 else rest_ref.at[0]
        return send(src, rest_ref.at[1 + i], core_send.at[i], core_recv.at[i], core)

    def cx_cross():
        return send(rest_ref.at[0], diag_ref.at[0], cx_send.at[0], cx_recv.at[0], group[0])

    def cx_core():
        return send(diag_ref.at[0], diag_ref.at[1], cx_send.at[1], cx_recv.at[1], core)

    def to_home(c, late):
        at = pl.ds(pl.multiple_of(late * split, split), split)
        d = lax.rem(c - ctx + n - 1, n)
        return send(result.at[c, at], arrived.at[ctx, at], exch_send.at[late, d], exch_recv.at[late, d], {"ctx": c})

    def from_device(c, late):
        at = pl.ds(late * split, split)
        d = lax.rem(ctx - c + n - 1, n)
        return send(result.at[c, at], arrived.at[c, at], exch_send.at[late, d], exch_recv.at[late, d], {"ctx": c})

    def own_rows(late):
        at = pl.ds(pl.multiple_of(late * split, split), split)
        return pltpu.make_async_copy(result.at[ctx, at], arrived.at[ctx, at], own_sems.at[late])

    @pl.when(block == 0)
    def _():
        for copy in copies:
            copy.start()
        greet([core, group[0]] + [{"ctx": c} for c in others(n)])
        to_near().start()
        for i in range(2):
            to_core(i).start()

    attn_forward_kernel(length, ends_ref, q_ref, pack_ref, None, lse_ref, full_ref, keys, values_t, acc)
    late = block // per_half
    folded = fold_heads(jnp.transpose(full_ref[0])).astype(BF16)
    for k in range(per):
        c = lax.rem(block, per_half) * per + k
        result[c, pl.ds(pl.multiple_of(late * split, split), split), :] = folded[k * split : (k + 1) * split]

        @pl.when(c == ctx)
        def _():
            own_rows(late).start()

        @pl.when(c != ctx)
        def _():
            to_home(c, late).start()

    @pl.when(block == last - 1)
    def _():
        to_near().wait_recv()
        to_core(2).start()
        cx_cross().start()

    @pl.when(block == last)
    def _():
        order = (0, 4, 1, 2, 3, 5, 6, 7)
        halves = [pl.ds(k * split, split) for k in range(2)]

        def load(step):
            refs = (cxs_ref.at[0], cxs_ref.at[1], rest_ref.at[0], diag_ref.at[0], rest_ref.at[1], rest_ref.at[2], rest_ref.at[3], diag_ref.at[1])
            return pltpu.make_async_copy(refs[order[step]], cx.at[step % 2], load_sems.at[step % 2])

        def hop(i, k):
            return send(hs.at[0, halves[k]], hs.at[(1, 2, 4)[i], halves[k]], hop_send.at[i, k], hop_recv.at[i, k], (group[0], group[1], core)[i])

        def cross(i):
            return send(hs.at[1 + i, halves[i]], hs.at[3, halves[i]], cross_send.at[i], cross_recv.at[i], group[1 - i])

        def forward(i):
            return send(hs.at[1 + i], hs.at[5 + i], fwd_send.at[i], fwd_recv.at[i], core)

        load(0).start()
        for i in range(3):
            to_core(i).wait_recv()
        load(1).start()
        for copy in copies:
            copy.wait()
        for k in range(2):
            own_rows(k).wait()
            for d in range(1, n):
                from_device(lax.rem(ctx + d, n), k).wait_recv()
            at = slice(k * split, (k + 1) * split)
            total = None
            for c in range(n):
                part = dot(arrived[c, at, :], wo_ref[c])
                total = part if total is None else total + part
            middle = x_ref[at, :] + RESIDUAL * total
            middle_ref[at, :] = middle
            normed, _ = norm_parts(middle)
            h = (normed * gain_ref[1:2]).astype(BF16)
            h_ref[at, :] = h
            hs[0, at, :] = h
            for i in range(3):
                hop(i, k).start()
        keep = pltpu.make_async_copy(arrived, kept_ref, local_sems.at[2])
        keep.start()

        def stores(step):
            b = order[step]
            pairs = ((rows_out, xs_ref), (grads_out, gs_ref), (gates_out, gates_ref))
            return [pltpu.make_async_copy(src.at[step % 2], dst.at[:, b], store_sems.at[step % 2, k]) for k, (src, dst) in enumerate(pairs)]

        def place(step):
            b, slot = order[step], step % 2
            load(step).wait()
            if step >= 2:
                for copy in stores(step - 2):
                    copy.wait()
            h = hs[b]
            logits = jnp.transpose(dot(h, wr_ref[...]))[:EXPERTS, :]
            raw = jnp.exp(logits - jnp.max(logits, 0, keepdims=True))
            router = raw / jnp.sum(raw, 0, keepdims=True)
            slots = cx[slot, tokens:, :tokens].astype(F32)
            hots = one_hot(slots, first, number, capp)
            places = jnp.concatenate(hots, 0).astype(BF16)
            rows = dot(places, h).astype(BF16)
            grads = dot(places, cx[slot, :tokens, :]).astype(BF16)
            for j in range(number):
                at = slice(j * capp, (j + 1) * capp)
                rows_out[slot, j] = rows[at]
                grads_out[slot, j] = grads[at]
                gate = jnp.sum(hots[j] * own_row(router, first + j), 1, keepdims=True)
                gates_out[slot, j] = jnp.broadcast_to(gate, (capp, 128))
            for copy in stores(step):
                copy.start()
            if step + 2 < 8:
                if step + 2 == 4:
                    cx_cross().wait_recv()
                    cx_core().start()
                if step + 2 == 7:
                    cx_core().wait_recv()
                load(step + 2).start()

        place(0)
        for k in range(2):
            hop(2, k).wait_recv()
        place(1)
        hop(0, 0).wait_recv()
        cross(0).start()
        hop(1, 0).wait_recv()
        hop(1, 1).wait_recv()
        cross(1).start()
        forward(1).start()
        hop(0, 1).wait_recv()
        forward(0).start()
        place(2)
        place(3)
        for i in range(2):
            cross(i).wait_recv()
        forward(2).start()
        place(4)
        for i in range(3):
            forward(i).wait_recv()
            place(5 + i)
        for step in (6, 7):
            for copy in stores(step):
                copy.wait()
        for k in range(2):
            for d in range(1, n):
                to_home(lax.rem(ctx + d, n), k).wait_send()
        for i in range(2):
            cross(i).wait_send()
        cx_cross().wait_send()
        cx_core().wait_send()
        for i in range(3):
            for k in range(2):
                hop(i, k).wait_send()
            forward(i).wait_send()
            to_core(i).wait_send()
        to_near().wait_send()
        keep.wait()


def attend(ends, packs, cxs, wo, wr, x, gains, length, number, capp):
    n, _, rows, _ = packs.shape
    tokens, width = x.shape
    blocks, per = length // BLK, BLK // rows
    per_half = blocks // 2
    tiles = lambda i: (lax.rem(i, per_half), i // per_half, 0, 0)
    hbm = pl.BlockSpec(memory_space=pl.ANY)
    dma = lambda *k: pltpu.SemaphoreType.DMA(k)
    same = lambda shape: pl.BlockSpec(shape, lambda i: (0,) * len(shape))
    shaped = lambda shape, dtype=BF16: jax.ShapeDtypeStruct(shape, dtype)
    return pl.pallas_call(
        functools.partial(attend_kernel, length, n, number, capp),
        grid=(blocks,),
        in_specs=[
            pl.BlockSpec(memory_space=pltpu.SMEM),
            pl.BlockSpec((per, 1, rows, PACK), tiles),
            same(packs.shape),
            hbm,
            hbm,
            same(wr.shape),
            hbm,
            same(gains.shape),
        ],
        out_specs=[
            pl.BlockSpec((1, 1, 2 * BLK), lambda i: (i, 0, 0)),
            pl.BlockSpec((1, 128, 2 * BLK), lambda i: (i, 0, 0)),
            same((tokens, width)),
            same((tokens, width)),
            hbm,
            hbm,
            hbm,
            hbm,
            hbm,
            hbm,
        ],
        out_shape=[
            shaped((blocks, 1, 2 * BLK), F32),
            shaped((blocks, 128, 2 * BLK), F32),
            shaped((tokens, width), F32),
            shaped((tokens, width)),
            shaped((n, tokens, 128)),
            shaped((number, 8, capp, width)),
            shaped((number, 8, capp, width)),
            shaped((number, 8, capp, 128), F32),
            shaped((4,) + cxs.shape[1:]),
            shaped((2,) + cxs.shape[1:]),
        ],
        scratch_shapes=[
            pltpu.VMEM((length, 128), BF16),
            pltpu.VMEM((128, length), BF16),
            pltpu.VMEM((128, 2 * BLK), F32),
            pltpu.VMEM((n, tokens, 128), BF16),
            pltpu.VMEM((n, tokens, 128), BF16),
            pltpu.VMEM((8, tokens, width), BF16),
            pltpu.VMEM(wo.shape, BF16),
            pltpu.VMEM((tokens, width), F32),
            pltpu.VMEM((2,) + cxs.shape[1:], BF16),
            pltpu.VMEM((2, number, capp, width), BF16),
            pltpu.VMEM((2, number, capp, width), BF16),
            pltpu.VMEM((2, number, capp, 128), F32),
            dma(1),
            dma(1),
            dma(3),
            dma(3),
            dma(2, n - 1),
            dma(2, n - 1),
            dma(3, 2),
            dma(3, 2),
            dma(2),
            dma(2),
            dma(2),
            dma(2),
            dma(3),
            dma(3),
            dma(3),
            dma(2),
            dma(2),
            dma(2, 3),
        ],
        compiler_params=params(collective_id=3, has_side_effects=True),
        cost_estimate=cost(2e10, 7e7),
        name="attend",
    )(ends, packs, packs, cxs, wo, wr, x, gains)


RING = 12
LAG_MIDDLE, LAG_ACROSS, LAG_END = 1, 2, 4
ORDER_X, ORDER_Y, ORDER_CORE = 1, 2, 4


class GroupSum:
    def __init__(self, part, rows, lands, own, sems, load, free, first, core, group):
        self.part, self.rows, self.own, self.load, self.free, self.first = part, rows, own, load, free, first
        self.land, self.land_x, self.land_y = lands
        self.core_send, self.core_recv, self.x_send, self.x_recv, self.y_send, self.y_recv = sems
        self.core, self.far, self.near = core, group[0], group[1]

    def place(self, i):
        return self.land.at[i, pl.ds(0, self.rows)]

    def ready(self, which):
        if not self.first:
            pl.semaphore_wait(self.free.at[which], 1)

    def to_core(self, i):
        return send(self.part.at[4 + i], self.place(i), self.core_send.at[i], self.core_recv.at[i], self.core)

    def to_far(self, k):
        return send(self.place(1 + 2 * k), self.land_x.at[k, pl.ds(0, self.rows)], self.x_send.at[k], self.x_recv.at[k], self.far)

    def to_near(self):
        return send(self.place(2), self.land_y.at[pl.ds(0, self.rows)], self.y_send.at[0], self.y_recv.at[0], self.near)

    def fetch(self, i):
        return pltpu.make_async_copy(self.part.at[i], self.own.at[i % 2, pl.ds(0, self.rows)], self.load.at[i % 2])

    def start(self):
        self.ready(0)
        for i in (1, 3, 2, 0):
            self.to_core(i).start()

    def over_cores(self):
        order = (1, 3, 2, 0)
        if self.own is not None:
            self.fetch(1).start()
        for step, i in enumerate(order):
            if self.own is None:
                mine = self.part[i]
            else:
                self.fetch(i).wait()
                mine = self.own[i % 2, : self.rows]
            self.to_core(i).wait_recv()
            self.land[i, : self.rows] = (self.land[i, : self.rows].astype(F32) + mine.astype(F32)).astype(BF16)
            if self.own is not None and step < 3:
                self.fetch(order[step + 1]).start()
            if i % 2 == 1:
                if step == 0:
                    self.ready(1)
                self.to_far(i // 2).start()

    def over_x(self, between=None):
        for k in (1, 0):
            if k == 0 and between is not None:
                between()
            self.to_far(k).wait_recv()
            both = self.land[2 * k, : self.rows].astype(F32) + self.land_x[k, : self.rows].astype(F32)
            self.land[2 * k, : self.rows] = both.astype(BF16)
            if k == 1:
                self.ready(2)
                self.to_near().start()

    def finish(self):
        self.to_near().wait_recv()
        for i in range(4):
            self.to_core(i).wait_send()
        for k in range(2):
            self.to_far(k).wait_send()
        self.to_near().wait_send()
        return self.land[0, : self.rows].astype(F32) + self.land_y[: self.rows].astype(F32)

    def release(self):
        for which, device in enumerate((self.core, self.far, self.near)):
            pl.semaphore_signal(self.free.at[which], inc=1, device_id=device, device_id_type=MESH)


class LineSum:
    def __init__(self, count, own_ref, other_ref, inbox, across, mine, sems):
        self.count, self.own_ref, self.other_ref = count, own_ref, other_ref
        self.inbox, self.across, self.mine = inbox, across, mine
        self.line_send, self.line_recv, self.mid_send, self.mid_recv, self.side_send, self.side_recv, self.store, self.load = sems
        ctx = lax.axis_index("ctx")
        z = ctx // 2
        self.middle = (z == 1) | (z == 2)
        self.line = {"ctx": jnp.where(z % 2 == 0, ctx + 2, ctx - 2)}
        self.peer = {"ctx": jnp.where(z == 1, ctx + 2, ctx - 2)}
        self.side = {"ctx": flip(ctx, 1)}

    def send_line(self, src, i):
        s = lax.rem(i, RING)
        return send(src, self.inbox.at[s], self.line_send.at[s], self.line_recv.at[s], self.line)

    def send_mid(self, i):
        s = lax.rem(i, RING)
        return send(self.inbox.at[s], self.across.at[s], self.mid_send.at[s], self.mid_recv.at[s], self.peer)

    def send_side(self, src, i):
        return send(src, self.other_ref.at[i], self.side_send.at[lax.rem(i, RING)], self.side_recv.at[i], self.side)

    def keep(self, src, i):
        return pltpu.make_async_copy(src, self.own_ref.at[i], self.store.at[lax.rem(i, RING)])

    def fetch(self, src, i):
        s = lax.rem(i, 4)
        return pltpu.make_async_copy(src, self.mine.at[s], self.load.at[s])

    def drain_middle(self, i):
        src = self.across.at[lax.rem(i, RING)]
        self.send_line(src, i).wait_send()
        self.send_side(src, i).wait_send()
        self.keep(src, i).wait()

    def drain_end(self, i):
        src = self.inbox.at[lax.rem(i, RING)]
        self.send_side(src, i).wait_send()
        self.keep(src, i).wait()

    def tick(self, t, source):
        count = self.count
        fixed = isinstance(t, int)

        def when(condition):
            if fixed:
                return (lambda f: f()) if condition else (lambda f: None)
            return pl.when(condition)

        i32 = (lambda v: jnp.int32(v)) if fixed else (lambda v: v)

        @pl.when(self.middle)
        def _():
            @when((t >= LAG_MIDDLE) & (t < count + LAG_MIDDLE))
            def _():
                i = i32(t - LAG_MIDDLE)

                @when(t >= LAG_ACROSS + 4)
                def _():
                    self.drain_middle(i32(t - LAG_ACROSS - 4))

                s = lax.rem(i, RING)
                self.fetch(self.own_ref.at[i], i).wait()
                self.send_line(self.inbox.at[s], i).wait_recv()
                self.inbox[s] = self.inbox[s] + self.mine[lax.rem(i, 4)]
                self.send_mid(i).start()

            @when(t < count)
            def _():
                self.fetch(source(t), i32(t)).start()

            @when((t >= LAG_ACROSS) & (t < count + LAG_ACROSS))
            def _():
                i = i32(t - LAG_ACROSS)
                s = lax.rem(i, RING)
                self.send_mid(i).wait()
                self.across[s] = self.across[s] + self.inbox[s]
                self.send_line(self.across.at[s], i).start()
                self.send_side(self.across.at[s], i).start()
                self.keep(self.across.at[s], i).start()

        @pl.when(jnp.logical_not(self.middle))
        def _():
            @when(t < count)
            def _():
                @when(t >= LAG_END + 2)
                def _():
                    self.drain_end(i32(t - LAG_END - 2))

                @when(t >= 3)
                def _():
                    self.send_line(self.mine.at[0], i32(t - 3)).wait_send()

                self.send_line(source(t), i32(t)).start()

            @when(t >= LAG_END)
            def _():
                i = i32(t - LAG_END)
                s = lax.rem(i, RING)
                self.send_line(self.inbox.at[s], i).wait_recv()
                self.send_side(self.inbox.at[s], i).start()
                self.keep(self.inbox.at[s], i).start()

    def finish(self):
        count = self.count

        @pl.when(self.middle)
        def _():
            for i in range(max(0, count + LAG_MIDDLE - LAG_ACROSS - 4), count):
                self.drain_middle(jnp.int32(i))

        @pl.when(jnp.logical_not(self.middle))
        def _():
            for i in range(max(0, count - 3), count):
                self.send_line(self.mine.at[0], jnp.int32(i)).wait_send()
            for i in range(max(0, count - LAG_END - 2), count):
                self.drain_end(jnp.int32(i))

        def arrived(i, carry):
            self.send_side(self.mine.at[0], i).wait_recv()
            return carry

        lax.fori_loop(0, count, arrived, 0)


def backward_kernel(
    n,
    length,
    capp,
    ends_ref,
    xs_ref,
    gs_ref,
    gates_ref,
    wg_ref,
    wu_ref,
    wd_ref,
    cxs_ref,
    rest_ref,
    diag_ref,
    full_ref,
    weights_ref,
    packs_hbm,
    table_hbm,
    cot_hbm,
    wo_hbm,
    attn_hbm,
    x_hbm,
    h_attn_hbm,
    h_hbm,
    middle_hbm,
    wr_hbm,
    gains_hbm,
    lse_hbm,
    own_ref,
    other_ref,
    own_rest_ref,
    other_rest_ref,
    pieces_ref,
    outs_ref,
    backs_ref,
    gx_ref,
    yp_ref,
    grad_x_ref,
    mixed_ref,
    inbox,
    across,
    mine,
    land,
    land_x,
    land_y,
    y_land,
    y_land_x,
    y_land_y,
    own_buf,
    late_pieces,
    late_rest,
    rest_inbox,
    rest_across,
    rest_mine,
    ga_in,
    grads_in,
    line_send,
    line_recv,
    mid_send,
    mid_recv,
    side_send,
    side_recv,
    line_store,
    line_load,
    ga_send,
    ga_recv,
    gr_send,
    gr_recv,
    group_sems,
    group_load,
    free,
    local_sems,
    full_sems,
    w_sems,
    load_sems,
    store_sems,
    comb_sems,
    part_sems,
    rest_sems,
):
    tokens, width = h_hbm.shape
    half = length // 2
    rows = tokens // 2
    shard = width // 4
    blocks = length // BLK
    number = xs_ref.shape[0]
    ff = wg_ref.shape[2]
    ctx, fsdp = lax.axis_index("ctx"), lax.axis_index("fsdp")
    side = lax.rem(ctx, 2)
    first = (fsdp * 2 + side) * number
    core, group = neighbours()
    sub = own_ref.shape[1]
    cuts = PIECE // sub
    early = number * 6 * cuts
    line = LineSum(own_ref.shape[0], own_ref, other_ref, inbox, across, mine, (line_send, line_recv, mid_send, mid_recv, side_send, side_recv, line_store, line_load))

    small_line = LineSum(1, own_rest_ref, other_rest_ref, rest_inbox, rest_across, rest_mine, [rest_sems.at[k] for k in range(8)])

    def source(t):
        return pieces_ref.at[t // cuts, pl.ds(pl.multiple_of(lax.rem(t, cuts) * sub, sub), sub)]

    def tick(t):
        line.tick(jnp.int32(t) if isinstance(t, int) else t, source)

    sems = lambda k: [group_sems.at[k, j] for j in range(6)]
    lands = (land, land_x, land_y)
    ext = tokens + EXPERTS
    gx = GroupSum(gx_ref, 2 * ext, lands, None, sems(0), None, free, True, core, group)
    ys = GroupSum(yp_ref, 2 * tokens, (y_land, y_land_x, y_land_y), own_buf, sems(1), group_load, free, True, core, group)

    def strip(r):
        f = fsdp
        if r & ORDER_X:
            f = flip(f, 2)
        if r & ORDER_CORE:
            f = flip(f, 1)
        return 2 * f + (1 - side if r & ORDER_Y else side)

    def experts(wg, wu, wd, xb, gb, gateb, stage, out_acc, back_acc, outb, backb, go, dgate, comb_o, comb_b, gst, yst, slots):
        def loads(e):
            s = lax.rem(e, 2)
            at = side * number + e
            pairs = ((wg_ref.at[at], wg), (wu_ref.at[at], wu), (wd_ref.at[at], wd), (xs_ref.at[e], xb), (gs_ref.at[e], gb), (gates_ref.at[e], gateb))
            return [pltpu.make_async_copy(src, dst.at[s], load_sems.at[s, k]) for k, (src, dst) in enumerate(pairs)]

        def slot_copy(b):
            refs = (cxs_ref.at[0], cxs_ref.at[1], rest_ref.at[0], diag_ref.at[0], rest_ref.at[1], rest_ref.at[2], rest_ref.at[3], diag_ref.at[1])
            return pltpu.make_async_copy(refs[b].at[pl.ds(tokens, EXPERTS), pl.ds(0, tokens)], slots.at[b], part_sems.at[0, b])

        def stores(e):
            pairs = (
                (stage.at[pl.ds(0, 3)], pieces_ref.at[pl.ds(6 * e, 3)]),
                (stage.at[pl.ds(3, 3)], pieces_ref.at[pl.ds(6 * e + 3, 3)]),
                (outb, outs_ref.at[e]),
                (backb, backs_ref.at[e]),
            )
            return [pltpu.make_async_copy(src, dst, store_sems.at[k]) for k, (src, dst) in enumerate(pairs)]

        for copy in loads(jnp.int32(0)):
            copy.start()
        for b in range(8):
            slot_copy(b).start()
        greet([core, group[0]] + [{"ctx": c} for c in others(n)])

        def one(e, carry):
            s = lax.rem(e, 2)

            @pl.when(e + 1 < number)
            def _():
                for copy in loads(e + 1):
                    copy.start()

            for copy in loads(e):
                copy.wait()

            @pl.when(e > 0)
            def _():
                for copy in stores(e - 1)[2:]:
                    copy.wait()

            x = xb[s]
            gate = gateb[s][:, :1]
            go[...] = (gate * (RESIDUAL * gb[s].astype(F32))).astype(BF16)
            part = ff // 2
            for chunk in range(2):
                at = slice(chunk * part, (chunk + 1) * part)
                wgc, wuc, wdc = wg[s, :, at], wu[s, :, at], wd[s, at, :]
                pre_gate = dot(x, wgc)
                pre_up = dot(x, wuc)
                sig = jax.nn.sigmoid(pre_gate)
                hidden = (pre_gate * sig * pre_up).astype(BF16)
                out_part = dot(hidden, wdc)
                grad_hidden = dot(go[...], wdc, NT)
                grad_gate = (grad_hidden * pre_up * sig * (1.0 + pre_gate * (1.0 - sig))).astype(BF16)
                grad_up = (grad_hidden * pre_gate * sig).astype(BF16)
                row_part = dot(grad_gate, wgc, NT) + dot(grad_up, wuc, NT)
                dwg = dot(x, grad_gate, TN).astype(BF16)
                dwu = dot(x, grad_up, TN).astype(BF16)
                dwd = dot(hidden, go[...], TN).astype(BF16)
                for k in range(2):
                    cut = slice(k * PIECE, (k + 1) * PIECE)
                    stage[3 * chunk + k, :, :part] = dwg[cut]
                    stage[3 * chunk + k, :, part:] = dwu[cut]
                    stage[3 * chunk + 2, k * part : (k + 1) * part, :] = dwd[:, cut]
                stores(e)[chunk].start()
                if chunk == 0:
                    out_acc[...] = out_part
                    back_acc[...] = row_part
                    stores(e)[0].wait()
                    tick(2 * e)
                else:
                    out = (out_acc[...] + out_part).astype(BF16).astype(F32)
                    outb[...] = (gate * out).astype(BF16)
                    backb[...] = (back_acc[...] + row_part).astype(BF16)
                    grad = jnp.sum(RESIDUAL * gb[s].astype(F32) * out, 1, keepdims=True)
                    dgate[e] = jnp.broadcast_to(grad, dgate.shape[1:])
            for copy in stores(e)[2:]:
                copy.start()
            stores(e)[1].wait()
            tick(2 * e + 1)
            return carry

        lax.fori_loop(0, number, one, 0)
        for copy in stores(jnp.int32(number - 1))[2:]:
            copy.wait()
        for b in range(8):
            slot_copy(b).wait()

        def which(s):
            k = lax.rem(s, 4)
            i = jnp.where(k == 0, 1, jnp.where(k == 1, 3, jnp.where(k == 2, 2, 0)))
            return jnp.where(s < 4, 4 + i, i), i

        def comb(s):
            k = lax.rem(s, 2)
            at = pl.ds(pl.multiple_of(which(s)[0] * capp, 16), capp)
            return [
                pltpu.make_async_copy(outs_ref.at[:, at], comb_o.at[k], comb_sems.at[0, k]),
                pltpu.make_async_copy(backs_ref.at[:, at], comb_b.at[k], comb_sems.at[1, k]),
            ]

        def put(s):
            k = lax.rem(s, 2)
            r, _ = which(s)
            return [
                pltpu.make_async_copy(gst.at[k], gx_ref.at[r], part_sems.at[1, k]),
                pltpu.make_async_copy(yst.at[k], yp_ref.at[r], part_sems.at[1, 2 + k]),
            ]

        for copy in comb(jnp.int32(0)):
            copy.start()

        def join(s, carry):
            k = lax.rem(s, 2)
            r, i = which(s)

            @pl.when(s + 1 < 8)
            def _():
                for copy in comb(s + 1):
                    copy.start()

            for copy in comb(s):
                copy.wait()

            @pl.when(s >= 2)
            def _():
                put(s - 2)[1].wait()

            hots = one_hot(slots[r].astype(F32), first, number, capp)
            places = jnp.concatenate(hots, 0).astype(BF16)
            y = dot(places, comb_o[k].reshape(number * capp, width), TN).astype(BF16)
            back = dot(places, comb_b[k].reshape(number * capp, width), TN).astype(BF16)
            extra = jnp.zeros((EXPERTS, 2 * tokens), F32)
            for j in range(number):
                grads = dgate[j, pl.ds(pl.multiple_of(r * capp, 16), capp), :][:, :1]
                grad = jnp.sum(hots[j] * grads, 0, keepdims=True)
                high = grad.astype(BF16).astype(F32)
                extra = jnp.where(row_iota(extra.shape) == first + j, jnp.concatenate([high, grad - high], 1), extra)
            for q in range(2):
                yst[k, q * tokens : (q + 1) * tokens, :] = y[:, q * PIECE : (q + 1) * PIECE]
                gst[k, q * ext : q * ext + tokens, :] = back[:, q * PIECE : (q + 1) * PIECE]
            gst[k, tokens:ext, :] = extra.astype(BF16)
            gst[k, ext + tokens :, :] = jnp.zeros((EXPERTS, PIECE), BF16)
            put(s)[1].start()

            @pl.when(s < 4)
            def _():
                put(s)[0].start()
                put(s)[0].wait()
                gx.to_core(i).start()

            @pl.when(s >= 4)
            def _():
                gx.to_core(i).wait_recv()
                land[i, : gx.rows] = (land[i, : gx.rows].astype(F32) + gst[k].astype(F32)).astype(BF16)

            @pl.when((s == 4) | (s == 5))
            def _():
                gx.to_far(s - 4).start()

            @pl.when(lax.rem(s, 2) == 1)
            def _():
                tick(2 * number + s // 2)

            return carry

        lax.fori_loop(0, 8, join, 0)
        for s in range(6, 8):
            put(jnp.int32(s))[1].wait()

    slots_rows = xs_ref.shape[1]
    pl.run_scoped(
        experts,
        pltpu.VMEM((2, width, ff), BF16),
        pltpu.VMEM((2, width, ff), BF16),
        pltpu.VMEM((2, ff, width), BF16),
        pltpu.VMEM((2, slots_rows, width), BF16),
        pltpu.VMEM((2, slots_rows, width), BF16),
        pltpu.VMEM((2, slots_rows, 128), F32),
        pltpu.VMEM((6, PIECE, PIECE), BF16),
        pltpu.VMEM((slots_rows, width), F32),
        pltpu.VMEM((slots_rows, width), F32),
        pltpu.VMEM((slots_rows, width), BF16),
        pltpu.VMEM((slots_rows, width), BF16),
        pltpu.VMEM((slots_rows, width), BF16),
        pltpu.VMEM((number, slots_rows, 128), F32),
        pltpu.VMEM((2, number, capp, width), BF16),
        pltpu.VMEM((2, number, capp, width), BF16),
        pltpu.VMEM((2, 2 * ext, PIECE), BF16),
        pltpu.VMEM((2, 2 * tokens, PIECE), BF16),
        pltpu.VMEM((8, EXPERTS, tokens), BF16),
    )
    at_tick = [2 * number + 4]

    def go_on(k=1):
        for _ in range(k):
            tick(at_tick[0])
            at_tick[0] += 1

    def backward(packs, table, keys, values, keys_t, grad_q, grad_k, grad_v, acc, full_buf, ga, pack_out, wbuf, total, grad_middle, dgain, dwr, col, small, columns, cot, wo, attn, x_in, h_attn, h_ref, middle_ref, wr_ref, gains_ref, lse_ref):
        ws = GroupSum(small, small.shape[1], lands, None, sems(2), None, free, False, core, group)
        cs = GroupSum(columns, PIECE + 16, lands, None, sems(3), None, free, False, core, group)
        copies = [
            pltpu.make_async_copy(src, dst, local_sems.at[4 + k])
            for k, (src, dst) in enumerate(
                (
                    (cot_hbm, cot),
                    (wo_hbm, wo),
                    (attn_hbm, attn),
                    (packs_hbm, packs),
                    (table_hbm, table),
                    (x_hbm, x_in),
                    (h_attn_hbm, h_attn),
                    (h_hbm, h_ref),
                    (middle_hbm, middle_ref),
                    (wr_hbm, wr_ref),
                    (gains_hbm, gains_ref),
                    (lse_hbm, lse_ref),
                )
            )
        ]
        for copy in copies:
            copy.start()
        go_on(2)
        gx.over_x(go_on)
        go_on(2)
        arrived = gx.finish()
        arrived = jnp.concatenate([arrived[:ext], arrived[ext:]], 1)
        gx.release()

        for copy in copies[7:]:
            copy.wait()
        h = h_ref[...]
        gain = gains_ref[1:2]
        extra = arrived[tokens:, :]
        grad_router = extra[:, :tokens] + extra[:, tokens : 2 * tokens]
        grad_router = jnp.transpose(jnp.concatenate([grad_router, jnp.zeros((128 - EXPERTS, tokens), F32)], 0))
        logits = dot(h, wr_ref[...])
        logits = jnp.where(lane_iota(logits.shape) < EXPERTS, logits, MASKED)
        raw = jnp.exp(logits - jnp.max(logits, -1, keepdims=True))
        router = raw / jnp.sum(raw, -1, keepdims=True)
        grad_logits = (router * (grad_router - jnp.sum(router * grad_router, -1, keepdims=True))).astype(BF16)
        go_on()
        grad_h = arrived[:tokens, :] + dot(grad_logits, wr_ref[...], NT)
        normed, scale = norm_parts(middle_ref[...])
        dgain[1:2, :] = jnp.sum(grad_h * normed, 0, keepdims=True)
        for copy in copies[:3]:
            copy.wait()
        grad_mid = cot[...] + norm_back(grad_h * gain, normed, scale)
        grad_middle[...] = grad_mid
        grad_branch = (RESIDUAL * grad_mid).astype(BF16)
        for c in range(n):
            ga[c] = dot(grad_branch, wo[c], NT).astype(BF16)
        ga_exchange = (ga, ga_in, ga_send, ga_recv, local_sems.at[2], n)
        exchange_start(*ga_exchange)
        go_on()
        dwr[...] = dot(grad_logits, h, TN)[:EXPERTS]
        for r in range(8):
            at = strip(r)
            dwo = dot(attn[at], grad_branch, TN).astype(BF16)
            small[r, 0:128, :] = dwo[:, :PIECE]
            small[r, 128:256, :] = dwo[:, PIECE:]
        ws.start()
        ys.start()
        go_on()
        copies[3].wait()
        for hh in range(2):
            for c in range(n):
                kk, vv = pair_keys(packs[c, hh, :, 128:256].astype(F32))
                at = hh * half + c * rows
                keys[at : at + rows, :] = kk.astype(BF16)
                values[at : at + rows, :] = vv.astype(BF16)
                keys_t[:, at : at + rows] = jnp.transpose(kk).astype(BF16)
        grad_k[...] = jnp.zeros_like(grad_k)
        grad_v[...] = jnp.zeros_like(grad_v)
        go_on()
        ws.over_cores()
        ys.over_cores()
        go_on()
        exchange_wait(*ga_exchange)

        per = BLK // rows
        per_half = blocks // 2

        def fetch_full(b):
            return pltpu.make_async_copy(full_ref.at[b], full_buf.at[lax.rem(b, 2)], full_sems.at[lax.rem(b, 2)])

        fetch_full(jnp.int32(0)).start()
        attend_tick = at_tick[0]

        def attend(block, carry):
            late = block // per_half
            c0 = lax.rem(block, per_half) * per
            q2 = jnp.concatenate([packs[c0 + k, late, :, :128] for k in range(per)], 0)
            q2 = stack_heads((q2.astype(F32) * ATTN_SCALE).astype(BF16))
            g2 = stack_heads(jnp.concatenate([ga_in[c0 + k, pl.ds(pl.multiple_of(late * rows, rows), rows), :] for k in range(per)], 0))
            position, start = query_rows(ends_ref, block, length)
            lse = lse_ref[block]
            shift = jnp.where(start > 0, MASKED, 0.0) - lse

            @pl.when(block + 1 < blocks)
            def _():
                fetch_full(block + 1).start()

            fetch_full(block).wait()
            delta = jnp.sum(jnp.transpose(g2.astype(F32)) * full_buf[lax.rem(block, 2)], 0, keepdims=True)
            acc[...] = jnp.zeros_like(acc)

            def body(kb, whole, carry):
                at = pl.multiple_of(kb * BLK, BLK)
                scores = dot(keys[pl.ds(at, BLK), :], q2, NT)
                if whole:
                    probs = jnp.exp(scores + shift)
                else:
                    where = key_position(kb, length)
                    probs = jnp.where((where <= position) & (where >= start), jnp.exp(scores - lse), 0.0)
                grad_probs = dot(values[pl.ds(at, BLK), :], g2, NT)
                grad_scores = (probs * (grad_probs - delta)).astype(BF16)
                acc[...] += dot(keys_t[:, pl.ds(at, BLK)], grad_scores)
                grad_k[pl.ds(at, BLK), :] += dot(grad_scores, q2)
                grad_v[pl.ds(at, BLK), :] += dot(probs.astype(BF16), g2)

                if not whole:

                    @pl.when((kb == block) & ((block == per_half) | (block == per_half + 1)))
                    def _():
                        tick(attend_tick + 2 + 2 * (block - per_half))

                return carry

            block_loop(block, per_half, body, 0)
            grad_q[pl.ds(pl.multiple_of(block * BLK, BLK), BLK), :] = fold_heads(jnp.transpose(acc[...]))

            @pl.when((block == 1) | (block >= 3))
            def _():
                past = block - per_half
                late_tick = jnp.where(past < 2, 3 + 2 * past, 4 + past)
                tick(attend_tick + jnp.where(block < per_half, block // 2, late_tick))

            return carry

        lax.fori_loop(0, blocks, attend, 0)
        at_tick[0] += blocks
        copies[4].wait()
        for c in range(n):
            for hh in range(2):
                at = slice(hh * half + c * rows, hh * half + (c + 1) * rows)
                kk = grad_k[at, :]
                vv = grad_v[at, :]
                kk = kk + pltpu.roll(kk, 64, 1)
                vv = vv + pltpu.roll(vv, 64, 1)
                both = jnp.where(lane_iota(kk.shape) < 64, kk, vv)
                package = jnp.concatenate([grad_q[at, :] * ATTN_SCALE, both], -1)
                pack_out[c, hh * rows : (hh + 1) * rows, :] = turn(package, table[at, :], -1.0).astype(BF16)
        gr_exchange = (pack_out, grads_in, gr_send, gr_recv, local_sems.at[3], n)
        exchange_start(*gr_exchange)

        def fetch_w(c):
            slot = lax.rem(c, 2)
            at = pl.ds(pl.multiple_of(c * 128, 128), 128)
            return [
                pltpu.make_async_copy(weights_ref.at[1 - k, :, :, at], wbuf.at[slot, :, :, pl.ds(128 * k, 128)], w_sems.at[slot, k])
                for k in range(2)
            ]

        for copy in fetch_w(jnp.int32(0)):
            copy.start()
        go_on()
        ws.over_x()
        ys.over_x()
        go_on(2)
        total[...] = jnp.zeros_like(total)
        late_pieces[:256] = ws.finish().astype(BF16)
        ws.release()
        ffn = ys.finish()
        mixed_ref[...] = middle_ref[...] + RESIDUAL * jnp.concatenate([ffn[:tokens], ffn[tokens:]], 1)
        go_on(3)
        exchange_wait(*gr_exchange)
        copies[5].wait()
        copies[6].wait()

        columns_tick = at_tick[0]

        def finish_columns(c, carry):
            @pl.when(c + 1 < n)
            def _():
                for copy in fetch_w(c + 1):
                    copy.start()

            for copy in fetch_w(c):
                copy.wait()
            slot = lax.rem(c, 2)
            g = grads_in[c]
            col[...] = dot(h_attn[...], g, TN).astype(BF16)
            for r in range(8):
                at = pl.ds(pl.multiple_of(strip(r) * 128, 128), 128)
                columns[r, pl.ds(pl.multiple_of(c // 2 * 128, 128), 128), pl.ds(pl.multiple_of(lax.rem(c, 2) * PACK, PACK), PACK)] = col[at, :]
            for f in range(4):
                total[:, f * shard : (f + 1) * shard] += dot(g, wbuf[slot, f, :shard, :], NT)

            @pl.when(lax.rem(c, 4) == 3)
            def _():
                tick(columns_tick + c // 4)

            return carry

        lax.fori_loop(0, n, finish_columns, 0)
        at_tick[0] += n // 4
        normed, scale = norm_parts(x_in[...])
        grad_h = total[...]
        dgain[0:1, :] = jnp.sum(grad_h * normed, 0, keepdims=True)
        grad_x_ref[...] = grad_middle[...] + norm_back(grad_h * gains_ref[0:1], normed, scale)
        for r in range(8):
            at = pl.ds(pl.multiple_of(strip(r) * 128, 128), 128)
            router_rows = jnp.concatenate([dwr[q * 8 : (q + 1) * 8, at] for q in range(EXPERTS // 8)], 1)
            row = row_iota((8, 128))
            gain_rows = jnp.where(row == 0, dgain[0:1, at], jnp.where(row == 1, dgain[1:2, at], 0.0))
            gain_rows = jnp.concatenate([gain_rows, jnp.zeros((8, PIECE - 128), F32)], 1)
            columns[r, PIECE:, :] = jnp.concatenate([router_rows, gain_rows], 0).astype(BF16)
        cs.start()
        go_on()
        cs.over_cores()
        go_on(3)
        cs.over_x(go_on)
        go_on(3)
        summed = cs.finish().astype(BF16)
        late_pieces[256:] = summed[:PIECE]
        late_rest[...] = summed[PIECE:]

    f32, bf = (lambda *shape: pltpu.VMEM(shape, F32)), (lambda *shape: pltpu.VMEM(shape, BF16))
    pl.run_scoped(
        backward,
        bf(*packs_hbm.shape),
        f32(*table_hbm.shape),
        bf(length, 128),
        bf(length, 128),
        bf(128, length),
        f32(length, 128),
        f32(length, 128),
        f32(length, 128),
        f32(128, 2 * BLK),
        f32(2, 128, 2 * BLK),
        bf(n, tokens, 128),
        bf(n, tokens, PACK),
        bf(2, 4, weights_ref.shape[2], PACK),
        f32(tokens, width),
        f32(tokens, width),
        f32(8, width),
        f32(EXPERTS, width),
        bf(width, PACK),
        bf(8, 256, PIECE),
        bf(8, PIECE + 16, PIECE),
        f32(tokens, width),
        bf(*wo_hbm.shape),
        bf(*attn_hbm.shape),
        f32(tokens, width),
        bf(tokens, width),
        bf(tokens, width),
        f32(tokens, width),
        bf(*wr_hbm.shape),
        f32(*gains_hbm.shape),
        f32(*lse_hbm.shape),
    )

    def rest(t, carry):
        tick(t)
        return carry

    lax.fori_loop(at_tick[0], early, rest, 0)

    def late_source(t):
        return late_pieces.at[pl.ds(pl.multiple_of((t - early) * sub, sub), sub)]

    def late(t, carry):
        line.tick(t, late_source)
        return carry

    for t in range(1 + LAG_END):
        small_line.tick(jnp.int32(t), lambda t: late_rest)
        late(jnp.int32(early + t), 0)
    lax.fori_loop(early + 1 + LAG_END, line.count + LAG_END, late, 0)
    line.finish()
    small_line.finish()


def backward_step(ends, xs, gs, gates, w_gate, w_up, w_down, cxs, rest, diag, full, weights, packs, table, cot, wo, attn, x, h_attn, h, middle, wr, gains, lse, n, length, capp):
    tokens, width = x.shape
    number, slots_rows, _ = xs.shape
    hbm, vmem = pl.BlockSpec(memory_space=pl.ANY), pl.BlockSpec(memory_space=pltpu.VMEM)
    smem = pl.BlockSpec(memory_space=pltpu.SMEM)
    dma = lambda *k: pltpu.SemaphoreType.DMA(k)
    shaped = lambda shape, dtype=BF16: jax.ShapeDtypeStruct(shape, dtype)
    sub = PIECE // 2
    piece = (sub, PIECE)
    count = number * 12 + 3
    rest_shape = (16, PIECE)
    land_rows = max(2 * (tokens + EXPERTS), PIECE + 16)
    return pl.pallas_call(
        functools.partial(backward_kernel, n, length, capp),
        in_specs=[smem] + [hbm] * 23,
        out_specs=[hbm] * 9 + [vmem, vmem],
        out_shape=[
            shaped((count,) + piece),
            shaped((count,) + piece),
            shaped((1,) + rest_shape),
            shaped((1,) + rest_shape),
            shaped((number * 6, PIECE, PIECE)),
            shaped(xs.shape),
            shaped(xs.shape),
            shaped((8, 2 * (tokens + EXPERTS), PIECE)),
            shaped((8, 2 * tokens, PIECE)),
            shaped((tokens, width), F32),
            shaped((tokens, width), F32),
        ],
        scratch_shapes=[
            pltpu.VMEM((RING,) + piece, BF16),
            pltpu.VMEM((RING,) + piece, BF16),
            pltpu.VMEM((4,) + piece, BF16),
            pltpu.VMEM((4, land_rows, PIECE), BF16),
            pltpu.VMEM((2, land_rows, PIECE), BF16),
            pltpu.VMEM((land_rows, PIECE), BF16),
            pltpu.VMEM((4, 2 * tokens, PIECE), BF16),
            pltpu.VMEM((2, 2 * tokens, PIECE), BF16),
            pltpu.VMEM((2 * tokens, PIECE), BF16),
            pltpu.VMEM((2, 2 * tokens, PIECE), BF16),
            pltpu.VMEM((768, PIECE), BF16),
            pltpu.VMEM(rest_shape, BF16),
            pltpu.VMEM((RING,) + rest_shape, BF16),
            pltpu.VMEM((RING,) + rest_shape, BF16),
            pltpu.VMEM((4,) + rest_shape, BF16),
            pltpu.VMEM((n, tokens, 128), BF16),
            pltpu.VMEM((n, tokens, PACK), BF16),
            dma(RING),
            dma(RING),
            dma(RING),
            dma(RING),
            dma(RING),
            dma(count),
            dma(RING),
            dma(4),
            dma(n - 1),
            dma(n - 1),
            dma(n - 1),
            dma(n - 1),
            dma(4, 6, 4),
            dma(2),
            pltpu.SemaphoreType.REGULAR((3,)),
            dma(16),
            dma(2),
            dma(2, 2),
            dma(2, 6),
            dma(4),
            dma(2, 2),
            dma(2, 8),
            dma(8, RING),
        ],
        compiler_params=params(63, collective_id=0, has_side_effects=True),
        cost_estimate=cost(6e10, 1e9),
        name="backward_step",
    )(ends, xs, gs, gates, w_gate, w_up, w_down, cxs, rest, diag, full, weights, packs, table, cot, wo, attn, x, h_attn, h, middle, wr, gains, lse)


def local(
    inputs,
    cotangent,
    doc_lengths,
    routes,
    attn_gain,
    ffn_gain,
    w_query,
    key_weight,
    value_weight,
    w_out,
    w_router,
    w_gate,
    w_up,
    w_down,
):
    rows = inputs.shape[2]
    width = inputs.shape[3]
    n = lax.axis_size("ctx")
    fsdp = lax.axis_size("fsdp")
    me, mine = lax.axis_index("ctx"), lax.axis_index("fsdp")
    tokens = 2 * rows
    length = tokens * n
    experts_here = w_gate.shape[0]
    number = experts_here // 2
    capacity = 5 * tokens * TOP // (4 * EXPERTS)
    capp = -(-capacity // 16) * 16
    shard = width // fsdp
    heads = QUERY_HEADS // n
    head_lanes = heads * HEAD_DIMENSION
    copies = n // KEY_VALUE_HEADS
    bits = group_bits(fsdp)

    x = inputs.reshape(tokens, width)
    cot = cotangent.reshape(tokens, width)
    side = me % 2
    base = (side * number).astype(jnp.int32).reshape(1)
    first = (mine * experts_here + side * number).astype(jnp.int32).reshape(1)
    index = jnp.stack([side * number, (1 - side) * number]).astype(jnp.int32)
    ends = doc_lengths
    table = jnp.asarray(rotary_table(length))

    out_part = w_out.reshape(shard // head_lanes, head_lanes, width)
    if head_lanes < 128:
        out_part = jnp.pad(out_part, ((0, 0), (0, 128 - head_lanes), (0, 0)))
    merge = lambda a: a.reshape(number, -1, a.shape[-1])

    if n == 8 and fsdp == 4:
        packs, h_attn, weights, wo, wr, cxs, gains = front(
            w_query,
            key_weight,
            value_weight,
            out_part,
            jnp.transpose(w_router),
            jnp.stack([attn_gain, ffn_gain]),
            x,
            table.reshape(2, n, rows, 256),
            jnp.transpose(routes[0], (0, 2, 1)),
            cot,
            capacity,
            n,
        )
        wo, wr = wo.reshape(n, 128, width), wr.reshape(width, 128)
        packs = packs.reshape(n, 2, rows, PACK)
        lse, full, middle, h_ffn, attn, xs, gs, gates, cx_rest, diag = attend(ends, packs, cxs, wo, wr, x, gains, length, number, capp)
        own, other, own_rest, other_rest, _, _, _, _, _, grad_x, mixed = backward_step(
            ends,
            merge(xs),
            merge(gs),
            merge(gates),
            w_gate,
            w_up,
            w_down,
            cxs,
            cx_rest,
            diag,
            full,
            weights,
            packs,
            table,
            cot,
            wo,
            attn,
            x,
            h_attn,
            h_ffn,
            middle,
            wr,
            gains,
            lse,
            n,
            length,
            capp,
        )
        shapes = [w.shape for w in (w_gate, w_up, w_down)]
        outs = tail(index, own, other, own_rest, other_rest, mixed, grad_x, shapes, shard)
        return (
            outs[3].reshape(inputs.shape),
            outs[4].reshape(inputs.shape),
            outs[10].reshape(shard),
            outs[11].reshape(shard),
            outs[5],
            outs[6],
            outs[7],
            outs[8],
            jnp.transpose(outs[9]),
            outs[0],
            outs[1],
            outs[2],
        )

    else:
        own_table = lax.dynamic_slice_in_dim(table.reshape(2, n, rows, 256), me, 1, 1).reshape(tokens, 256)
        query_part = w_query.reshape(shard, n, head_lanes)
        if head_lanes < 128:
            query_part = jnp.pad(query_part, ((0, 0), (0, 0), (0, 128 - head_lanes)))
        key_part = jnp.repeat(key_weight.reshape(shard, KEY_VALUE_HEADS, HEAD_DIMENSION), copies, 1)
        value_part = jnp.repeat(value_weight.reshape(shard, KEY_VALUE_HEADS, HEAD_DIMENSION), copies, 1)
        packed = jnp.concatenate([query_part, key_part, value_part], -1).reshape(shard, n * PACK)
        padding = 2 * 16 * (shard // 32 + 1) - shard
        gains = jnp.pad(jnp.stack([attn_gain, ffn_gain]), ((0, padding - 2), (0, n * PACK - shard)))
        packed = jnp.concatenate([packed, gains], 0)
        router_part = jnp.pad(w_router, ((0, 0), (0, 128 - EXPERTS)))
        weights = lax.all_gather(packed, "fsdp", axis=0)
        gain_one = weights[:, shard, :shard].reshape(1, width).astype(F32)
        gain_two = weights[:, shard + 1, :shard].reshape(1, width).astype(F32)
        wo = lax.all_gather(out_part, "fsdp", axis=0, tiled=True)
        wr = lax.all_gather(router_part, "fsdp", axis=0, tiled=True)
        cxs = group_gather(prep(jnp.transpose(routes[0], (0, 2, 1)), cot, capacity), bits)
        packs, h_attn = qkv(x, gain_one, weights, own_table, shard, n)
        packs = lax.all_to_all(packs, "ctx", split_axis=0, concat_axis=0, tiled=True).reshape(n, 2, rows, PACK)
        attn, lse, full = attn_forward(ends, packs, length)
        attn = lax.all_to_all(attn.reshape(n, tokens, 128), "ctx", split_axis=0, concat_axis=0, tiled=True)
        middle, h_ffn = middle_step(attn, wo, x, gain_two)
        xs, gs, gates = gather_rows(first, group_gather(h_ffn, bits), cxs, jnp.transpose(wr), number, capp)
        slots = cxs[:, tokens:]
    xs, gs, gates = merge(xs), merge(gs), merge(gates)
    pieces, outs, back, dgates = expert_step(base, xs, gs, gates, w_gate, w_up, w_down)
    y_part, gx_part = combine(first, slots, outs, back, dgates, tokens, capp)
    pieces = pieces.reshape(number * 6, PIECE, PIECE)
    gx = group_reduce(gx_part, bits)
    grad_middle, dwo, grad_attn, dwr, dgain_two = home_step(gx, h_ffn, middle, cot, wr, wo, gain_two, attn)
    grad_attn = lax.all_to_all(grad_attn, "ctx", split_axis=0, concat_axis=0, tiled=True).reshape(n, 2, rows, 128)
    grads = attn_backward(ends, packs, grad_attn, lse, full, table, length)
    grads = lax.all_to_all(grads.reshape(n, tokens, PACK), "ctx", split_axis=0, concat_axis=0, tiled=True)
    dw, grad_x, dgain_one = final_step(grads, weights, h_attn, x, gain_one, grad_middle, shard)
    mixed = middle + RESIDUAL * group_reduce(y_part, bits).astype(F32)
    own = line_sum(pieces.reshape(-1, PIECE // 2, PIECE), n)
    other = swap(own, "ctx", 1)
    scatter = lambda a: lax.psum(lax.psum_scatter(a, "fsdp", scatter_dimension=0, tiled=True), "ctx").astype(F32)
    dwo = scatter(dwo)[:, :head_lanes, :].reshape(shard, width)
    small = jnp.concatenate([dwr[:, :EXPERTS], dgain_two.reshape(width, 1).astype(BF16)], 1)
    small = scatter(jnp.pad(small, ((0, 0), (0, 127 - EXPERTS))))
    dwr, dgain_two = small[:, :EXPERTS], small[:, EXPERTS]
    dw = scatter(dw).reshape(shard, n, PACK)
    dgain_one = scatter(dgain_one.reshape(width).astype(BF16))

    outs = widen(index, own, other, [w.shape for w in (w_gate, w_up, w_down)])
    fold = lambda a: a.reshape(shard, KEY_VALUE_HEADS, copies, HEAD_DIMENSION).sum(2).reshape(shard, -1)
    return (
        mixed.reshape(inputs.shape),
        grad_x.reshape(inputs.shape),
        dgain_one,
        dgain_two,
        dw[:, :, :head_lanes].reshape(shard, -1),
        fold(dw[:, :, 128:192]),
        fold(dw[:, :, 192:256]),
        dwo,
        dwr,
        outs[0],
        outs[1],
        outs[2],
    )


def solution(mesh):
    tokens = P("fsdp", None, "ctx", None)
    one, two, three = P("fsdp"), P("fsdp", None), P("fsdp", None, None)
    return jax.shard_map(
        local,
        mesh=mesh,
        in_specs=(tokens, tokens, two, tokens, one, one, two, two, two, two, two, three, three, three),
        out_specs=(tokens, tokens, one, one, two, two, two, two, two, three, three, three),
        check_vma=False,
    )
```

```python
import functools

import jax
import jax.numpy as jnp
import numpy as np
from jax import lax
from jax.experimental import pallas as pl
from jax.experimental.pallas import tpu as pltpu
from jax.sharding import PartitionSpec as P

QUERY_HEADS = 16
KEY_VALUE_HEADS = 8
HEAD_DIMENSION = 64
EXPERTS = 32
TOP = 8

ATTN_SCALE = 0.015625
RESIDUAL = 0.22
NORM_EPS = 1e-06
ROPE_BASE = 10000.0
MASKED = -1e30

F32 = jnp.float32
BF16 = jnp.bfloat16
MIB = 1 << 20
NT = (((1,), (1,)), ((), ()))
TN = (((0,), (0,)), ((), ()))
BLK = 256
PACK = 256


def dot(a, b, dims=None):
    if dims is None:
        return jnp.dot(a, b, preferred_element_type=F32)
    return lax.dot_general(a, b, dims, preferred_element_type=F32)


def params(limit=56, **kw):
    return pltpu.CompilerParams(vmem_limit_bytes=limit * MIB, **kw)


def cost(flops, bytes_accessed):
    return pl.CostEstimate(flops=int(flops), bytes_accessed=int(bytes_accessed), transcendentals=0)


def lane_iota(shape):
    return lax.broadcasted_iota(jnp.int32, shape, len(shape) - 1)


def row_iota(shape):
    return lax.broadcasted_iota(jnp.int32, shape, len(shape) - 2)


def rotary_table(length):
    half = length // 2
    order = np.arange(half, dtype=np.float32)
    positions = np.concatenate([order, length - 1 - order]).astype(np.float32)
    m = np.arange(HEAD_DIMENSION // 2, dtype=np.float64)
    frequency = (ROPE_BASE ** (-2.0 * m / HEAD_DIMENSION)).astype(np.float32)
    angles = (positions[:, None] * frequency[None, :]).astype(np.float64)
    cosine, sine = np.cos(angles), np.sin(angles)
    cos_head = np.concatenate([cosine, cosine], -1)
    sin_head = np.concatenate([-sine, sine], -1)
    return np.concatenate([cos_head, cos_head, sin_head, sin_head], -1).astype(np.float32)


def turn(v, table, direction):
    lanes = lane_iota(v.shape)
    cosine = jnp.concatenate([table[:, :128], table[:, :128]], -1)
    sine = jnp.concatenate([table[:, 128:], table[:, 128:]], -1)
    turned = lanes < 3 * HEAD_DIMENSION
    swapped = jnp.where(lanes % HEAD_DIMENSION < HEAD_DIMENSION // 2, pltpu.roll(v, PACK - 32, 1), pltpu.roll(v, 32, 1))
    return jnp.where(turned, v * cosine + direction * (swapped * sine), v)


def norm_parts(values):
    inv_rms = lax.rsqrt(jnp.mean(values * values, -1, keepdims=True) + NORM_EPS)
    return values * inv_rms, inv_rms


def norm_back(grad_normed, normed, inv_rms):
    return inv_rms * (grad_normed - normed * jnp.mean(grad_normed * normed, -1, keepdims=True))


def prep_kernel(cap, routes_ref, cot_ref, out_ref):
    tokens, width = cot_ref.shape
    earlier = (row_iota((tokens, tokens)) < lane_iota((tokens, tokens))).astype(BF16)
    experts = row_iota((EXPERTS, tokens))
    base = jnp.zeros((EXPERTS, 1), F32)
    plus = jnp.zeros((EXPERTS, tokens), F32)
    for k in range(TOP):
        row = jnp.concatenate([routes_ref[0, k : k + 1, :], routes_ref[1, k : k + 1, :]], 1)
        chosen = experts == row
        ones = chosen.astype(F32)
        slot = dot(ones.astype(BF16), earlier) + base
        plus = plus + jnp.where(chosen & (slot < cap), slot + 1.0, 0.0)
        base = base + jnp.sum(ones, 1, keepdims=True)
    out_ref[:tokens, :] = cot_ref[...].astype(BF16)
    out_ref[tokens:, :] = jnp.concatenate([plus - 1.0, jnp.zeros((EXPERTS, width - tokens), F32)], -1).astype(BF16)


def prep(routes, cot, cap):
    tokens, width = cot.shape
    return pl.pallas_call(
        functools.partial(prep_kernel, cap),
        out_shape=jax.ShapeDtypeStruct((tokens + EXPERTS, width), BF16),
        compiler_params=params(),
        cost_estimate=cost(1e9, 2e6),
        name="prep",
    )(routes, cot)


def qkv_kernel(shard, x_ref, gain_ref, w_ref, table_ref, out_ref, h_ref):
    @pl.when(pl.program_id(0) == 0)
    def _():
        normed, _ = norm_parts(x_ref[...])
        h_ref[...] = (normed * gain_ref[...]).astype(BF16)

    total = None
    for f in range(w_ref.shape[0]):
        part = dot(h_ref[:, f * shard : (f + 1) * shard], w_ref[f, :shard, :])
        total = part if total is None else total + part
    for d in range(out_ref.shape[0]):
        out_ref[d] = turn(total[:, d * PACK : (d + 1) * PACK], table_ref[...], 1.0).astype(BF16)


def qkv(x, gain, weights, table, shard, n):
    tokens, width = x.shape
    fsdp, padded, _ = weights.shape
    return pl.pallas_call(
        functools.partial(qkv_kernel, shard),
        grid=(n // 2,),
        in_specs=[
            pl.BlockSpec((tokens, width), lambda i: (0, 0)),
            pl.BlockSpec((1, width), lambda i: (0, 0)),
            pl.BlockSpec((fsdp, padded, 2 * PACK), lambda i: (0, 0, i)),
            pl.BlockSpec((tokens, 256), lambda i: (0, 0)),
        ],
        out_specs=[
            pl.BlockSpec((2, tokens, PACK), lambda i: (i, 0, 0)),
            pl.BlockSpec((tokens, width), lambda i: (0, 0)),
        ],
        out_shape=[
            jax.ShapeDtypeStruct((n, tokens, PACK), BF16),
            jax.ShapeDtypeStruct((tokens, width), BF16),
        ],
        compiler_params=params(),
        cost_estimate=cost(2 * tokens * width * n * PACK, 8e6),
        name="qkv",
    )(x, gain, weights, table)


def pair_keys(kv):
    other = pltpu.roll(kv, 64, 1)
    low = lane_iota(kv.shape) < 64
    return jnp.where(low, kv, other), jnp.where(low, other, kv)


def stack_heads(q):
    low = lane_iota(q.shape) < 64
    zero = jnp.zeros_like(q)
    return jnp.concatenate([jnp.where(low, q, zero), jnp.where(low, zero, q)], 0)


def fold_heads(stacked):
    rows = stacked.shape[0] // 2
    return jnp.where(lane_iota((rows, 128)) < 64, stacked[:rows], stacked[rows:])


def query_rows(ends_ref, block, length):
    half = length // 2
    lanes = lane_iota((1, 2 * BLK))
    index = block * BLK + jnp.where(lanes < BLK, lanes, lanes - BLK)
    position = jnp.where(index < half, index, length + half - 1 - index)
    start = jnp.zeros_like(position)
    end = 0
    for j in range(3):
        end = end + ends_ref[0, j]
        start = jnp.where(position >= end, jnp.maximum(start, end), start)
    return position, start


def key_position(kb, length):
    half = length // 2
    index = kb * BLK + row_iota((BLK, 1))
    return jnp.where(index < half, index, length + half - 1 - index)


def block_loop(block, per_half, body, init):
    late = block >= per_half
    inner = jnp.where(late, block - per_half, block)

    def plain(kb, carry):
        return body(kb, True, carry)

    def masked(kb, carry):
        return body(kb, False, carry)

    carry = lax.fori_loop(0, jnp.where(late, per_half, inner), plain, init)
    return lax.fori_loop(block, jnp.where(late, 2 * per_half, block + 1), masked, carry)


def attn_forward_kernel(length, ends_ref, q_ref, pack_ref, out_ref, lse_ref, full_ref, keys, values_t, acc):
    block = pl.program_id(0)
    half = length // 2
    n, _, rows, _ = pack_ref.shape

    @pl.when(block == 0)
    def _():
        for h in range(2):
            for c in range(n):
                kk, vv = pair_keys(pack_ref[c, h, :, 128:256].astype(F32))
                at = h * half + c * rows
                keys[at : at + rows, :] = kk.astype(BF16)
                if rows % 128 == 0:
                    values_t[:, at : at + rows] = jnp.transpose(vv).astype(BF16)
        if rows % 128 != 0:
            for h in range(2):
                for c in range(0, n, 2):
                    pair = jnp.concatenate([pack_ref[c, h, :, 128:256], pack_ref[c + 1, h, :, 128:256]], 0)
                    _, vv = pair_keys(pair.astype(F32))
                    at = h * half + c * rows
                    values_t[:, at : at + 2 * rows] = jnp.transpose(vv).astype(BF16)

    q = q_ref[...].reshape(BLK, PACK)[:, :128]
    q2 = stack_heads((q.astype(F32) * ATTN_SCALE).astype(BF16))
    position, start = query_rows(ends_ref, block, length)
    bias = jnp.where(start > 0, MASKED, 0.0)
    acc[...] = jnp.zeros_like(acc)

    def body(kb, whole, carry):
        peak, total = carry
        at = pl.multiple_of(kb * BLK, BLK)
        scores = dot(keys[pl.ds(at, BLK), :], q2, NT)
        if whole:
            scores = scores + bias
        else:
            where = key_position(kb, length)
            scores = jnp.where((where <= position) & (where >= start), scores, MASKED)
        new_peak = jnp.maximum(peak, jnp.max(scores, 0, keepdims=True))
        weights = jnp.exp(scores - new_peak)
        fade = jnp.exp(peak - new_peak)
        total = total * fade + jnp.sum(weights, 0, keepdims=True)
        acc[...] = acc[...] * fade + dot(values_t[:, pl.ds(at, BLK)], weights.astype(BF16))
        return new_peak, total

    init = (jnp.full((1, 2 * BLK), MASKED, F32), jnp.zeros((1, 2 * BLK), F32))
    peak, total = block_loop(block, half // BLK, body, init)
    result = acc[...] / total
    full_ref[0] = result
    lse_ref[0] = peak + jnp.log(total)
    if out_ref is not None:
        folded = fold_heads(jnp.transpose(result)).astype(BF16)
        out_ref[...] = folded.reshape(out_ref.shape)


def attn_forward(ends, packs, length):
    n, _, rows, _ = packs.shape
    blocks, per = length // BLK, BLK // rows
    per_half = blocks // 2
    tiles = lambda i, ends: (lax.rem(i, per_half), i // per_half, 0, 0)
    return pl.pallas_call(
        functools.partial(attn_forward_kernel, length),
        grid_spec=pltpu.PrefetchScalarGridSpec(
            num_scalar_prefetch=1,
            grid=(blocks,),
            in_specs=[
                pl.BlockSpec((per, 1, rows, PACK), tiles),
                pl.BlockSpec(packs.shape, lambda i, ends: (0, 0, 0, 0)),
            ],
            out_specs=[
                pl.BlockSpec((per, 1, rows, 128), tiles),
                pl.BlockSpec((1, 1, 2 * BLK), lambda i, ends: (i, 0, 0)),
                pl.BlockSpec((1, 128, 2 * BLK), lambda i, ends: (i, 0, 0)),
            ],
            scratch_shapes=[
                pltpu.VMEM((length, 128), BF16),
                pltpu.VMEM((128, length), BF16),
                pltpu.VMEM((128, 2 * BLK), F32),
            ],
        ),
        out_shape=[
            jax.ShapeDtypeStruct((n, 2, rows, 128), BF16),
            jax.ShapeDtypeStruct((blocks, 1, 2 * BLK), F32),
            jax.ShapeDtypeStruct((blocks, 128, 2 * BLK), F32),
        ],
        compiler_params=params(),
        cost_estimate=cost(1.5e10, 6e6),
        name="attn_forward",
    )(ends, packs, packs)


def attn_backward_kernel(length, ends_ref, q_ref, g_ref, pack_ref, lse_ref, full_ref, table_ref, out_ref, keys, values, keys_t, grad_q, grad_k, grad_v, acc):
    block = pl.program_id(0)
    half = length // 2
    n, _, rows, _ = pack_ref.shape

    @pl.when(block == 0)
    def _():
        for h in range(2):
            for c in range(n):
                kk, vv = pair_keys(pack_ref[c, h, :, 128:256].astype(F32))
                at = h * half + c * rows
                keys[at : at + rows, :] = kk.astype(BF16)
                values[at : at + rows, :] = vv.astype(BF16)
        for b in range(length // BLK):
            keys_t[:, b * BLK : (b + 1) * BLK] = jnp.transpose(keys[b * BLK : (b + 1) * BLK, :].astype(F32)).astype(BF16)
        grad_k[...] = jnp.zeros_like(grad_k)
        grad_v[...] = jnp.zeros_like(grad_v)

    q2 = stack_heads((q_ref[...].reshape(BLK, PACK)[:, :128].astype(F32) * ATTN_SCALE).astype(BF16))
    g2 = stack_heads(g_ref[...].reshape(BLK, 128))
    position, start = query_rows(ends_ref, block, length)
    lse = lse_ref[0]
    shift = jnp.where(start > 0, MASKED, 0.0) - lse
    delta = jnp.sum(jnp.transpose(g2.astype(F32)) * full_ref[0], 0, keepdims=True)
    acc[...] = jnp.zeros_like(acc)

    def body(kb, whole, carry):
        at = pl.multiple_of(kb * BLK, BLK)
        scores = dot(keys[pl.ds(at, BLK), :], q2, NT)
        if whole:
            probs = jnp.exp(scores + shift)
        else:
            where = key_position(kb, length)
            probs = jnp.where((where <= position) & (where >= start), jnp.exp(scores - lse), 0.0)
        grad_probs = dot(values[pl.ds(at, BLK), :], g2, NT)
        grad_scores = (probs * (grad_probs - delta)).astype(BF16)
        acc[...] += dot(keys_t[:, pl.ds(at, BLK)], grad_scores)
        grad_k[pl.ds(at, BLK), :] += dot(grad_scores, q2)
        grad_v[pl.ds(at, BLK), :] += dot(probs.astype(BF16), g2)
        return carry

    block_loop(block, half // BLK, body, 0)
    grad_q[pl.ds(pl.multiple_of(block * BLK, BLK), BLK), :] = fold_heads(jnp.transpose(acc[...]))

    @pl.when(block == length // BLK - 1)
    def _():
        for h in range(2):
            for c in range(n):
                at = slice(h * half + c * rows, h * half + (c + 1) * rows)
                kk = grad_k[at, :]
                vv = grad_v[at, :]
                kk = kk + pltpu.roll(kk, 64, 1)
                vv = vv + pltpu.roll(vv, 64, 1)
                both = jnp.where(lane_iota(kk.shape) < 64, kk, vv)
                package = jnp.concatenate([grad_q[at, :] * ATTN_SCALE, both], -1)
                out_ref[c, h] = turn(package, table_ref[at, :], -1.0).astype(BF16)


def attn_backward(ends, packs, grads, lse, full, table, length):
    n, _, rows, _ = packs.shape
    blocks, per = length // BLK, BLK // rows
    per_half = blocks // 2
    tiles = lambda i, ends: (lax.rem(i, per_half), i // per_half, 0, 0)
    return pl.pallas_call(
        functools.partial(attn_backward_kernel, length),
        grid_spec=pltpu.PrefetchScalarGridSpec(
            num_scalar_prefetch=1,
            grid=(blocks,),
            in_specs=[
                pl.BlockSpec((per, 1, rows, PACK), tiles),
                pl.BlockSpec((per, 1, rows, 128), tiles),
                pl.BlockSpec(packs.shape, lambda i, ends: (0, 0, 0, 0)),
                pl.BlockSpec((1, 1, 2 * BLK), lambda i, ends: (i, 0, 0)),
                pl.BlockSpec((1, 128, 2 * BLK), lambda i, ends: (i, 0, 0)),
                pl.BlockSpec(table.shape, lambda i, ends: (0, 0)),
            ],
            out_specs=pl.BlockSpec(packs.shape, lambda i, ends: (0, 0, 0, 0)),
            scratch_shapes=[
                pltpu.VMEM((length, 128), BF16),
                pltpu.VMEM((length, 128), BF16),
                pltpu.VMEM((128, length), BF16),
                pltpu.VMEM((length, 128), F32),
                pltpu.VMEM((length, 128), F32),
                pltpu.VMEM((length, 128), F32),
                pltpu.VMEM((128, 2 * BLK), F32),
            ],
        ),
        out_shape=jax.ShapeDtypeStruct(packs.shape, BF16),
        compiler_params=params(),
        cost_estimate=cost(3e10, 8e6),
        name="attn_backward",
    )(ends, packs, grads, packs, lse, full, table)


def middle_kernel(attn_ref, wo_ref, x_ref, gain_ref, middle_ref, h_ref):
    total = None
    for c in range(attn_ref.shape[0]):
        part = dot(attn_ref[c], wo_ref[c])
        total = part if total is None else total + part
    middle = x_ref[...] + RESIDUAL * total
    middle_ref[...] = middle
    normed, _ = norm_parts(middle)
    h_ref[...] = (normed * gain_ref[...]).astype(BF16)


def middle_step(attn, wo, x, gain):
    tokens, width = x.shape
    return pl.pallas_call(
        middle_kernel,
        out_shape=[jax.ShapeDtypeStruct((tokens, width), F32), jax.ShapeDtypeStruct((tokens, width), BF16)],
        compiler_params=params(),
        cost_estimate=cost(2 * tokens * width * width, 5e6),
        name="middle",
    )(attn, wo, x, gain)


def own_row(table, row):
    return jnp.sum(jnp.where(row_iota(table.shape) == row, table, 0.0), 0, keepdims=True)


def one_hot(slots, first, number, capp):
    tokens = slots.shape[1]
    order = row_iota((capp, tokens)).astype(F32)
    return [(order == own_row(slots, first + j)).astype(F32) for j in range(number)]


def gather_kernel(number, capp, first_ref, h_ref, cx_ref, wrt_ref, x_ref, g_ref, gate_ref):
    tokens = h_ref.shape[1]
    first = first_ref[0]
    h = h_ref[0]
    slots = cx_ref[0, tokens:, :tokens].astype(F32)
    logits = dot(wrt_ref[...], h, NT)[:EXPERTS, :]
    raw = jnp.exp(logits - jnp.max(logits, 0, keepdims=True))
    router = raw / jnp.sum(raw, 0, keepdims=True)
    hots = one_hot(slots, first, number, capp)
    places = jnp.concatenate(hots, 0).astype(BF16)
    rows = dot(places, h).astype(BF16)
    grads = dot(places, cx_ref[0, :tokens, :]).astype(BF16)
    for j in range(number):
        at = slice(j * capp, (j + 1) * capp)
        x_ref[j, 0] = rows[at]
        g_ref[j, 0] = grads[at]
        gate = jnp.sum(hots[j] * own_row(router, first + j), 1, keepdims=True)
        gate_ref[j, 0] = jnp.broadcast_to(gate, (capp, 128))


def gather_rows(first, hs, cxs, wrt, number, capp):
    nb, tokens, width = hs.shape
    return pl.pallas_call(
        functools.partial(gather_kernel, number, capp),
        grid_spec=pltpu.PrefetchScalarGridSpec(
            num_scalar_prefetch=1,
            grid=(nb,),
            in_specs=[
                pl.BlockSpec((1, tokens, width), lambda b, f: (b, 0, 0)),
                pl.BlockSpec((1, tokens + EXPERTS, width), lambda b, f: (b, 0, 0)),
                pl.BlockSpec(wrt.shape, lambda b, f: (0, 0)),
            ],
            out_specs=[
                pl.BlockSpec((number, 1, capp, width), lambda b, f: (0, b, 0, 0)),
                pl.BlockSpec((number, 1, capp, width), lambda b, f: (0, b, 0, 0)),
                pl.BlockSpec((number, 1, capp, 128), lambda b, f: (0, b, 0, 0)),
            ],
        ),
        out_shape=[
            jax.ShapeDtypeStruct((number, nb, capp, width), BF16),
            jax.ShapeDtypeStruct((number, nb, capp, width), BF16),
            jax.ShapeDtypeStruct((number, nb, capp, 128), F32),
        ],
        compiler_params=params(),
        cost_estimate=cost(4 * nb * number * capp * tokens * width, 2e7),
        name="gather_rows",
    )(first, hs, cxs, wrt)


PIECE = 512


def expert_kernel(base_ref, x_ref, g_ref, gate_ref, wg_ref, wu_ref, wd_ref, piece_ref, out_ref, rows_ref, dg_ref):
    x = x_ref[0]
    gate = gate_ref[0][:, :1]
    grad_ffn = RESIDUAL * g_ref[0].astype(F32)
    go = (gate * grad_ffn).astype(BF16)
    part = wg_ref.shape[2] // 2
    out = rows = None
    for chunk in range(2):
        at = slice(chunk * part, (chunk + 1) * part)
        wg, wu, wd = wg_ref[0, :, at], wu_ref[0, :, at], wd_ref[0, at, :]
        pre_gate = dot(x, wg)
        pre_up = dot(x, wu)
        sig = jax.nn.sigmoid(pre_gate)
        hidden = (pre_gate * sig * pre_up).astype(BF16)
        out_part = dot(hidden, wd)
        grad_hidden = dot(go, wd, NT)
        grad_gate = (grad_hidden * pre_up * sig * (1.0 + pre_gate * (1.0 - sig))).astype(BF16)
        grad_up = (grad_hidden * pre_gate * sig).astype(BF16)
        row_part = dot(grad_gate, wg, NT) + dot(grad_up, wu, NT)
        dwg = dot(x, grad_gate, TN).astype(BF16)
        dwu = dot(x, grad_up, TN).astype(BF16)
        dwd = dot(hidden, go, TN).astype(BF16)
        for half in range(2):
            side = slice(half * PIECE, (half + 1) * PIECE)
            piece_ref[0, 3 * chunk + half, :, :part] = dwg[side]
            piece_ref[0, 3 * chunk + half, :, part:] = dwu[side]
            piece_ref[0, 3 * chunk + 2, half * part : (half + 1) * part, :] = dwd[:, side]
        out = out_part if out is None else out + out_part
        rows = row_part if rows is None else rows + row_part
    out = out.astype(BF16).astype(F32)
    out_ref[0] = (gate * out).astype(BF16)
    rows_ref[0] = rows.astype(BF16)
    grad = jnp.sum(grad_ffn * out, 1, keepdims=True)
    dg_ref[0] = jnp.broadcast_to(grad, dg_ref.shape[1:])


def expert_step(base, xs, gs, gates, w_gate, w_up, w_down):
    number, rows, width = xs.shape
    ff = w_gate.shape[2]
    row = lambda e, b: (e, 0, 0)
    weight = lambda e, b: (b[0] + e, 0, 0)
    return pl.pallas_call(
        expert_kernel,
        grid_spec=pltpu.PrefetchScalarGridSpec(
            num_scalar_prefetch=1,
            grid=(number,),
            in_specs=[
                pl.BlockSpec((1, rows, width), row),
                pl.BlockSpec((1, rows, width), row),
                pl.BlockSpec((1, rows, 128), row),
                pl.BlockSpec((1, width, ff), weight),
                pl.BlockSpec((1, width, ff), weight),
                pl.BlockSpec((1, ff, width), weight),
            ],
            out_specs=[
                pl.BlockSpec((1, 6, PIECE, PIECE), lambda e, b: (e, 0, 0, 0)),
                pl.BlockSpec((1, rows, width), row),
                pl.BlockSpec((1, rows, width), row),
                pl.BlockSpec((1, rows, 128), row),
            ],
        ),
        out_shape=[
            jax.ShapeDtypeStruct((number, 6, PIECE, PIECE), BF16),
            jax.ShapeDtypeStruct((number, rows, width), BF16),
            jax.ShapeDtypeStruct((number, rows, width), BF16),
            jax.ShapeDtypeStruct((number, rows, 128), F32),
        ],
        compiler_params=params(60),
        cost_estimate=cost(18 * number * rows * width * ff, 5e7),
        name="expert_step",
    )(base, xs, gs, gates, w_gate, w_up, w_down)


def combine_kernel(number, capp, first_ref, slot_ref, outs, rows, grads, y_ref, gx_ref):
    tokens = y_ref.shape[1]
    width = y_ref.shape[2]
    first = first_ref[0]
    slots = slot_ref[0][:, :tokens].astype(F32)
    hots = one_hot(slots, first, number, capp)
    places = jnp.concatenate(hots, 0).astype(BF16)
    y_ref[0] = dot(places, outs[:, 0].reshape(number * capp, width), TN).astype(BF16)
    gx_ref[0, :tokens] = dot(places, rows[:, 0].reshape(number * capp, width), TN).astype(BF16)
    extra = jnp.zeros((EXPERTS, 2 * tokens), F32)
    for j in range(number):
        grad = jnp.sum(hots[j] * grads[j, 0][:, :1], 0, keepdims=True)
        high = grad.astype(BF16).astype(F32)
        both = jnp.concatenate([high, grad - high], 1)
        extra = jnp.where(row_iota(extra.shape) == first + j, both, extra)
    rest = jnp.zeros((EXPERTS, width - 2 * tokens), F32)
    gx_ref[0, tokens:] = jnp.concatenate([extra, rest], 1).astype(BF16)


def combine(first, slots, outs, rows, grads, tokens, capp):
    number = outs.shape[0]
    nb, _, width = slots.shape
    split = lambda a: a.reshape(number, nb, capp, a.shape[-1])
    wide = pl.BlockSpec((number, 1, capp, width), lambda b, f: (0, b, 0, 0))
    thin = pl.BlockSpec((number, 1, capp, 128), lambda b, f: (0, b, 0, 0))
    return pl.pallas_call(
        functools.partial(combine_kernel, number, capp),
        grid_spec=pltpu.PrefetchScalarGridSpec(
            num_scalar_prefetch=1,
            grid=(nb,),
            in_specs=[pl.BlockSpec((1, EXPERTS, width), lambda b, f: (b, 0, 0))] + [wide, wide, thin],
            out_specs=[
                pl.BlockSpec((1, tokens, width), lambda b, f: (b, 0, 0)),
                pl.BlockSpec((1, tokens + EXPERTS, width), lambda b, f: (b, 0, 0)),
            ],
        ),
        out_shape=[
            jax.ShapeDtypeStruct((nb, tokens, width), BF16),
            jax.ShapeDtypeStruct((nb, tokens + EXPERTS, width), BF16),
        ],
        compiler_params=params(),
        cost_estimate=cost(4 * nb * number * capp * tokens * width, 2e7),
        name="combine",
    )(first, slots, split(outs), split(rows), split(grads))


def home_kernel(gx_ref, h_ref, middle_ref, cot_ref, wr_ref, wo_ref, gain_ref, attn_ref, grad_middle_ref, dwo_ref, ga_ref, dwr_ref, dgain_ref):
    tokens, width = h_ref.shape
    h = h_ref[...]
    gain = gain_ref[...]
    extra = gx_ref[tokens:, :].astype(F32)
    grad_router = extra[:, :tokens] + extra[:, tokens : 2 * tokens]
    grad_router = jnp.transpose(jnp.concatenate([grad_router, jnp.zeros((128 - EXPERTS, tokens), F32)], 0))
    logits = dot(h, wr_ref[...])
    logits = jnp.where(lane_iota(logits.shape) < EXPERTS, logits, MASKED)
    raw = jnp.exp(logits - jnp.max(logits, -1, keepdims=True))
    router = raw / jnp.sum(raw, -1, keepdims=True)
    grad_logits = (router * (grad_router - jnp.sum(router * grad_router, -1, keepdims=True))).astype(BF16)
    dwr_ref[...] = dot(h, grad_logits, TN).astype(BF16)
    grad_h = gx_ref[:tokens, :].astype(F32) + dot(grad_logits, wr_ref[...], NT)
    normed, scale = norm_parts(middle_ref[...])
    dgain_ref[...] = jnp.sum(grad_h * normed, 0, keepdims=True)
    grad_middle = cot_ref[...] + norm_back(grad_h * gain, normed, scale)
    grad_middle_ref[...] = grad_middle
    grad_branch = (RESIDUAL * grad_middle).astype(BF16)
    for c in range(attn_ref.shape[0]):
        dwo_ref[c] = dot(attn_ref[c], grad_branch, TN).astype(BF16)
        ga_ref[c] = dot(grad_branch, wo_ref[c], NT).astype(BF16)


def home_step(gx, h, middle, cot, wr, wo, gain, attn):
    tokens, width = h.shape
    n = attn.shape[0]
    return pl.pallas_call(
        home_kernel,
        out_shape=[
            jax.ShapeDtypeStruct((tokens, width), F32),
            jax.ShapeDtypeStruct((n, 128, width), BF16),
            jax.ShapeDtypeStruct((n, tokens, 128), BF16),
            jax.ShapeDtypeStruct((width, 128), BF16),
            jax.ShapeDtypeStruct((1, width), F32),
        ],
        compiler_params=params(),
        cost_estimate=cost(4 * tokens * width * width, 1e7),
        name="home_step",
    )(gx, h, middle, cot, wr, wo, gain, attn)


def final_kernel(shard, grads_ref, w_ref, h_ref, x_ref, gain_ref, grad_middle_ref, dw_ref, grad_x_ref, dgain_ref, total):
    c = pl.program_id(0)
    g = grads_ref[0]
    dw_ref[...] = dot(h_ref[...], g, TN).astype(BF16)

    @pl.when(c == 0)
    def _():
        total[...] = jnp.zeros_like(total)

    for f in range(w_ref.shape[0]):
        total[:, f * shard : (f + 1) * shard] += dot(g, w_ref[f, :shard, :], NT)

    @pl.when(c == pl.num_programs(0) - 1)
    def _():
        normed, scale = norm_parts(x_ref[...])
        grad_h = total[...]
        dgain_ref[...] = jnp.sum(grad_h * normed, 0, keepdims=True)
        grad_x_ref[...] = grad_middle_ref[...] + norm_back(grad_h * gain_ref[...], normed, scale)


def final_step(grads, weights, h, x, gain, grad_middle, shard):
    n, tokens, _ = grads.shape
    width = x.shape[1]
    fsdp, padded, _ = weights.shape
    same = lambda c: (0, 0)
    return pl.pallas_call(
        functools.partial(final_kernel, shard),
        grid=(n,),
        in_specs=[
            pl.BlockSpec((1, tokens, PACK), lambda c: (c, 0, 0)),
            pl.BlockSpec((fsdp, padded, PACK), lambda c: (0, 0, c)),
            pl.BlockSpec((tokens, width), same),
            pl.BlockSpec((tokens, width), same),
            pl.BlockSpec((1, width), same),
            pl.BlockSpec((tokens, width), same),
        ],
        out_specs=[
            pl.BlockSpec((width, PACK), lambda c: (0, c)),
            pl.BlockSpec((tokens, width), same),
            pl.BlockSpec((1, width), same),
        ],
        out_shape=[
            jax.ShapeDtypeStruct((width, n * PACK), BF16),
            jax.ShapeDtypeStruct((tokens, width), F32),
            jax.ShapeDtypeStruct((1, width), F32),
        ],
        scratch_shapes=[pltpu.VMEM((tokens, width), F32)],
        compiler_params=params(),
        cost_estimate=cost(4 * tokens * width * n * PACK, 1.2e7),
        name="final_step",
    )(grads, weights, h, x, gain, grad_middle)


def widen_kernel(number, index_ref, own_ref, other_ref, gate_ref, up_ref, down_ref):
    part = gate_ref.shape[2] // 2

    def write(ref):
        for chunk in range(2):
            columns = slice(chunk * part, (chunk + 1) * part)
            for half in range(2):
                for q in range(2):
                    at = slice(half * PIECE + q * 256, half * PIECE + (q + 1) * 256)
                    gate_ref[0, at, columns] = ref[6 * chunk + 2 * half + q, :, :part].astype(F32)
                    up_ref[0, at, columns] = ref[6 * chunk + 2 * half + q, :, part:].astype(F32)
                down_ref[0, columns, half * PIECE : (half + 1) * PIECE] = ref[6 * chunk + 4 + half].astype(F32)

    @pl.when(pl.program_id(0) == 0)
    def _():
        write(own_ref)

    @pl.when(pl.program_id(0) == 1)
    def _():
        write(other_ref)


def tail_kernel(number, index_ref, own_ref, other_ref, own_small_ref, other_small_ref, own_rest_ref, other_rest_ref, mixed_in, grad_in, gate_ref, up_ref, down_ref, mixed_ref, grad_ref, dwq_ref, dwk_ref, dwv_ref, dwo_ref, dwr_ref, g1_ref, g2_ref):
    widen_kernel(number, index_ref, own_ref, other_ref, gate_ref, up_ref, down_ref)
    mixed_ref[...] = mixed_in[...]
    grad_ref[...] = grad_in[...]

    @pl.when((pl.program_id(0) == 0) & (pl.program_id(1) == 0))
    def _():
        for which, (ref, rest) in enumerate(((own_small_ref, own_rest_ref), (other_small_ref, other_rest_ref))):
            part = index_ref[which] // number
            at = pl.ds(pl.multiple_of(part * 128, 128), 128)
            for q in range(4):
                block = ref[1 + q // 2, q % 2 * 128 : (q % 2 + 1) * 128, :].astype(F32)
                dwq_ref[at, q * 256 : q * 256 + 128] = block[:, :128]
                dwq_ref[at, q * 256 + 128 : (q + 1) * 256] = block[:, 256:384]
                one, two = block[:, 128:256], block[:, 384:]
                low = lane_iota(one.shape) < HEAD_DIMENSION
                dwk_ref[at, q * 128 : (q + 1) * 128] = jnp.where(low, one, pltpu.roll(two, 64, 1))
                dwv_ref[at, q * 128 : (q + 1) * 128] = jnp.where(low, pltpu.roll(one, 64, 1), two)
            dwo_ref[at, :PIECE] = ref[0, 0:128, :].astype(F32)
            dwo_ref[at, PIECE:] = ref[0, 128:256, :].astype(F32)
            low_rows = rest[0].astype(F32)
            for q in range(EXPERTS // 8):
                dwr_ref[q * 8 : (q + 1) * 8, at] = low_rows[:8, q * 128 : (q + 1) * 128]
            g1_ref[pl.ds(part, 1), :] = low_rows[8:9, :128]
            g2_ref[pl.ds(part, 1), :] = low_rows[9:10, :128]


def expert_specs(number, shapes):
    last = number - 1
    ins = [
        pl.BlockSpec((12, PIECE // 2, PIECE), lambda s, e, at: (jnp.where(s == 0, e, last), 0, 0)),
        pl.BlockSpec((12, PIECE // 2, PIECE), lambda s, e, at: (jnp.where(s == 0, 0, e), 0, 0)),
    ]
    outs = [pl.BlockSpec((1,) + tuple(shape[1:]), lambda s, e, at: (at[s] + e, 0, 0)) for shape in shapes]
    return ins, outs, [jax.ShapeDtypeStruct(shape, F32) for shape in shapes]


def widen(index, own, other, shapes):
    number = shapes[0][0] // 2
    ins, outs, out_shapes = expert_specs(number, shapes)
    return pl.pallas_call(
        functools.partial(widen_kernel, number),
        grid_spec=pltpu.PrefetchScalarGridSpec(num_scalar_prefetch=1, grid=(2, number), in_specs=ins, out_specs=outs),
        out_shape=out_shapes,
        compiler_params=params(),
        cost_estimate=cost(0, 1e8),
        name="widen",
    )(index, own, other)


def tail(index, own, other, own_rest, other_rest, mixed, grad_x, shapes, shard):
    number = shapes[0][0] // 2
    tokens, width = mixed.shape
    ins, outs, out_shapes = expert_specs(number, shapes)
    small = pl.BlockSpec((3, PIECE // 2, PIECE), lambda s, e, at: (4 * number, 0, 0))
    rest = pl.BlockSpec(own_rest.shape, lambda s, e, at: (0, 0, 0))
    rows = pl.BlockSpec((tokens // (2 * number), width), lambda s, e, at: (s * number + e, 0))
    small_shapes = [(shard, width), (shard, width // 2), (shard, width // 2), (shard, width), (EXPERTS, shard), (2, 128), (2, 128)]
    whole = [pl.BlockSpec(shape, lambda s, e, at: (0, 0)) for shape in small_shapes]
    return pl.pallas_call(
        functools.partial(tail_kernel, number),
        grid_spec=pltpu.PrefetchScalarGridSpec(
            num_scalar_prefetch=1,
            grid=(2, number),
            in_specs=ins + [small, small, rest, rest, rows, rows],
            out_specs=outs + [rows, rows] + whole,
        ),
        out_shape=out_shapes
        + [jax.ShapeDtypeStruct((tokens, width), F32)] * 2
        + [jax.ShapeDtypeStruct(shape, F32) for shape in small_shapes],
        compiler_params=params(),
        cost_estimate=cost(0, 1e8),
        name="tail",
    )(index, own, other, own, other, own_rest, other_rest, mixed, grad_x)


def swap(value, axis, bit):
    size = lax.axis_size(axis)
    return lax.ppermute(value, axis, [(i, i ^ bit) for i in range(size)])


def group_bits(fsdp):
    bits = [("fsdp", 1 << b) for b in range(1, fsdp.bit_length() - 1)]
    return bits + [("ctx", 1), ("fsdp", 1)]


def group_gather(value, bits):
    stacked = value[None]
    for axis, bit in bits:
        stacked = jnp.concatenate([stacked, swap(stacked, axis, bit)], 0)
    return stacked


def group_reduce(stacked, bits):
    for axis, bit in reversed(bits):
        half = stacked.shape[0] // 2
        arrived = swap(stacked[half:], axis, bit)
        stacked = (stacked[:half].astype(F32) + arrived.astype(F32)).astype(stacked.dtype)
    return stacked[0]


def line_sum(value, ctx):
    pairs = ctx // 2
    if pairs != 4:
        bit = 2
        while bit < ctx:
            value = value + swap(value, "ctx", bit)
            bit *= 2
        return value
    at = lambda z, y: 2 * z + y
    inward = [(at(0, y), at(1, y)) for y in range(2)] + [(at(3, y), at(2, y)) for y in range(2)]
    across = [(at(1, y), at(2, y)) for y in range(2)] + [(at(2, y), at(1, y)) for y in range(2)]
    outward = [(b, a) for a, b in inward]
    value = value + lax.ppermute(value, "ctx", inward)
    value = value + lax.ppermute(value, "ctx", across)
    arrived = lax.ppermute(value, "ctx", outward)
    z = lax.axis_index("ctx") // 2
    return jnp.where((z == 0) | (z == 3), arrived, value)


MESH = pl.DeviceIdType.MESH


def flip(index, bit):
    return jnp.where((index // bit) % 2 == 0, index + bit, index - bit)


def send(src, dst, send_sem, recv_sem, device):
    return pltpu.make_async_remote_copy(src_ref=src, dst_ref=dst, send_sem=send_sem, recv_sem=recv_sem, device_id=device, device_id_type=MESH)


def neighbours():
    ctx, fsdp = lax.axis_index("ctx"), lax.axis_index("fsdp")
    side, across = flip(ctx, 1), flip(fsdp, 2)
    core = {"fsdp": flip(fsdp, 1)}
    return core, [{"fsdp": across}, {"ctx": side}, {"ctx": side, "fsdp": across}]


def greet(devices):
    barrier = pltpu.get_barrier_semaphore()
    for device in devices:
        pl.semaphore_signal(barrier, inc=1, device_id=device, device_id_type=MESH)
    pl.semaphore_wait(barrier, len(devices))


def others(n):
    ctx = lax.axis_index("ctx")
    return [lax.rem(ctx + d, n) for d in range(1, n)]


def exchange_start(src, dst, send_sems, recv_sems, local_sem, n):
    ctx = lax.axis_index("ctx")
    for d, c in enumerate(others(n)):
        send(src.at[c], dst.at[ctx], send_sems.at[d], recv_sems.at[d], {"ctx": c}).start()
    pltpu.make_async_copy(src.at[ctx], dst.at[ctx], local_sem).start()


def exchange_wait(src, dst, send_sems, recv_sems, local_sem, n, arrived=None):
    ctx = lax.axis_index("ctx")
    pltpu.make_async_copy(src.at[ctx], dst.at[ctx], local_sem).wait()
    if arrived is not None:
        arrived(ctx)
    for d in range(n - 1):
        source = lax.rem(ctx + n - 1 - d, n)
        send(src.at[source], dst.at[source], send_sems.at[d], recv_sems.at[d], {"ctx": source}).wait_recv()
        if arrived is not None:
            arrived(source)
    for d, c in enumerate(others(n)):
        send(src.at[c], dst.at[ctx], send_sems.at[d], recv_sems.at[d], {"ctx": c}).wait_send()


def turn_half(v, table, direction, lanes_turned):
    lanes = lane_iota(v.shape)
    swapped = jnp.where(lanes % HEAD_DIMENSION < HEAD_DIMENSION // 2, pltpu.roll(v, 96, 1), pltpu.roll(v, 32, 1))
    return jnp.where(lanes < lanes_turned, v * table[:, :128] + direction * (swapped * table[:, 128:]), v)


def front_kernel(n, cap, wq_ref, wk_ref, wv_ref, wo_part_ref, wr_raw_ref, gain_ref, x_ref, table_ref, routes_ref, cot_ref, packs_ref, h_ref, weights_ref, wo_ref, wr_ref, cxs_ref, gains_ref, wall, packed_ref, wr_part_ref, cx, table, normed_ref, total, out, exch_send, exch_recv, full_send, full_recv, x_send, x_recv, y_send, y_recv, xs_send, xs_recv, ys_send, ys_recv, cx_send, cx_recv, local_sems):
    tokens, width = x_ref.shape
    shard = width // 4
    ctx, fsdp = lax.axis_index("ctx"), lax.axis_index("fsdp")
    parity = lax.rem(ctx, 2)
    core, group = neighbours()
    far, near = group[0], group[1]
    sibling, distant = flip(fsdp, 1), flip(fsdp, 2)
    other = flip(distant, 1)
    for k in range(2):
        pltpu.make_async_copy(table_ref.at[k, ctx], table.at[k], local_sems.at[6 + k]).start()

    pair = HEAD_DIMENSION * 2
    for c in range(0, n, 2):
        keys, values = wk_ref[:, c // 2 * pair : (c // 2 + 1) * pair].astype(F32), wv_ref[:, c // 2 * pair : (c // 2 + 1) * pair].astype(F32)
        low = lane_iota(keys.shape) < HEAD_DIMENSION
        packed_ref[0, :shard, c * 128 : (c + 1) * 128] = jnp.where(low, keys, pltpu.roll(values, 64, 1)).astype(BF16)
        packed_ref[0, :shard, (c + 1) * 128 : (c + 2) * 128] = jnp.where(low, pltpu.roll(keys, 64, 1), values).astype(BF16)
    below = packed_ref.shape[1] - shard
    packed_ref[0, shard:, :] = jnp.zeros((below, width), BF16)
    row = row_iota((16, shard))
    gains = gain_ref[...].astype(F32)
    gain_rows = jnp.where(row == 0, gains[0:1], jnp.where(row == 1, gains[1:2], 0.0))
    packed_ref[0, shard : shard + 16, :shard] = gain_rows.astype(BF16)
    packed_ref[1, :shard, :] = wq_ref[...]
    packed_ref[1, shard:, :] = jnp.zeros((below, width), BF16)
    router = jnp.concatenate([wr_raw_ref[...].astype(F32), jnp.zeros((128 - EXPERTS, shard), F32)], 0)
    wr_part_ref[...] = jnp.transpose(router).astype(BF16)
    greet([core, far] + [{"ctx": c} for c in others(n)])

    half_rows = packed_ref.shape[1] // 2

    def cut(k, part):
        if k < 2:
            return pl.ds(pl.multiple_of(part * half_rows, 16), half_rows)
        if k == 2:
            return pl.ds(part, 1)
        return pl.ds(pl.multiple_of(part * (shard // 2), 16), shard // 2)

    sources = [packed_ref.at[0], packed_ref.at[1], wo_part_ref, wr_part_ref]
    targets = [wall.at[0], wall.at[1], wo_ref, wr_ref]

    def whole(k):
        return send(sources[k], targets[k].at[fsdp], full_send.at[k], full_recv.at[k], core)

    def own(k):
        return pltpu.make_async_copy(sources[k], targets[k].at[fsdp], local_sems.at[k])

    def to_far(k):
        return send(sources[k].at[cut(k, parity)], targets[k].at[fsdp, cut(k, parity)], x_send.at[k], x_recv.at[k], far)

    def pass_on(k, part, sems, device):
        ref = targets[k].at[distant, cut(k, part)]
        return send(ref, ref, sems[0].at[k], sems[1].at[k], device)

    def sibling_arrived(k):
        ref = targets[k].at[sibling]
        send(ref, ref, full_send.at[k], full_recv.at[k], core).wait_recv()

    def far_arrived(k):
        ref = targets[k].at[distant, cut(k, parity)]
        send(ref, ref, x_send.at[k], x_recv.at[k], far).wait_recv()
        pass_on(k, parity, (y_send, y_recv), near).start()
        pass_on(k, parity, (xs_send, xs_recv), core).start()

    def near_arrived(k):
        pass_on(k, 1 - parity, (y_send, y_recv), near).wait_recv()
        pass_on(k, 1 - parity, (ys_send, ys_recv), core).start()

    def core_arrived(k):
        for part, sems in ((parity, (xs_send, xs_recv)), (1 - parity, (ys_send, ys_recv))):
            ref = targets[k].at[other, cut(k, part)]
            send(ref, ref, sems[0].at[k], sems[1].at[k], core).wait_recv()

    for k in range(2):
        to_far(k).start()
    for k in range(2):
        whole(k).start()
        own(k).start()

    prep_kernel(cap, routes_ref, cot_ref, cx)
    pltpu.make_async_copy(cx, cxs_ref.at[0], local_sems.at[4]).start()
    normed, _ = norm_parts(x_ref[...])
    normed_ref[...] = normed

    def project(k, block, begin):
        at = pl.ds(pl.multiple_of(block * shard, shard), shard)
        if k == 0:
            gain = wall[0, block, shard : shard + 16, :shard].astype(F32)
            gains_ref[:, at] = gain
            h_ref[:, at] = (normed_ref[:, at] * gain[:1]).astype(BF16)
        part = dot(h_ref[:, at], wall[k, block, :shard, :])
        total[k] = part if begin else total[k] + part

    for k in range(2):
        own(k).wait()
        project(k, fsdp, True)
        sibling_arrived(k)
        project(k, sibling, False)
        if k == 0:
            far_arrived(0)

    exchanges = []

    def emit(k):
        lanes = slice(128, 256) if k == 0 else slice(0, 128)
        for c in range(n):
            out[c, :, lanes] = turn_half(total[k, :, c * 128 : (c + 1) * 128], angles, 1.0, 64 if k == 0 else 128).astype(BF16)
        cut_lanes = pl.ds(128 if k == 0 else 0, 128)
        source, target = out.at[:, :, cut_lanes], packs_ref.at[:, :, cut_lanes]
        exchanges.append((source, target, exch_send.at[k], exch_recv.at[k], local_sems.at[8 + k], n))
        exchange_start(*exchanges[-1])

    near_arrived(0)
    project(0, distant, False)
    core_arrived(0)
    project(0, other, False)
    for k in range(2):
        pltpu.make_async_copy(table_ref.at[k, ctx], table.at[k], local_sems.at[6 + k]).wait()
    angles = table[...].reshape(tokens, 256)
    emit(0)
    far_arrived(1)
    for k in (2, 3):
        own(k).start()
        whole(k).start()
        to_far(k).start()
    send(cx, cxs_ref.at[1], cx_send.at[0], cx_recv.at[0], far).start()
    near_arrived(1)
    project(1, distant, False)
    core_arrived(1)
    project(1, other, False)
    emit(1)
    keep = pltpu.make_async_copy(wall, weights_ref, local_sems.at[5])
    keep.start()
    for k in (2, 3):
        far_arrived(k)
    for k in (2, 3):
        near_arrived(k)
    for k in (2, 3):
        core_arrived(k)
        sibling_arrived(k)
        own(k).wait()
    for exchange in exchanges:
        exchange_wait(*exchange)
    for k in range(4):
        whole(k).wait_send()
        to_far(k).wait_send()
        pass_on(k, parity, (y_send, y_recv), near).wait_send()
        pass_on(k, parity, (xs_send, xs_recv), core).wait_send()
        pass_on(k, 1 - parity, (ys_send, ys_recv), core).wait_send()
    send(cx, cxs_ref.at[1], cx_send.at[0], cx_recv.at[0], far).wait()
    pltpu.make_async_copy(cx, cxs_ref.at[0], local_sems.at[4]).wait()
    keep.wait()


def front(wq, wk, wv, wo_part, wr, gains, x, table, routes, cot, cap, n):
    tokens, width = x.shape
    shard = wq.shape[0]
    hbm, vmem = pl.BlockSpec(memory_space=pl.ANY), pl.BlockSpec(memory_space=pltpu.VMEM)
    dma = lambda *k: pltpu.SemaphoreType.DMA(k)
    shaped = lambda shape, dtype=BF16: jax.ShapeDtypeStruct(shape, dtype)
    cx_shape = (tokens + EXPERTS, width)
    padded = 2 * 16 * (shard // 32 + 1)
    return pl.pallas_call(
        functools.partial(front_kernel, n, cap),
        in_specs=[vmem, vmem, vmem, hbm, vmem, vmem, vmem, hbm, vmem, vmem],
        out_specs=[hbm, vmem, hbm, hbm, hbm, hbm, vmem],
        out_shape=[
            shaped((n, tokens, PACK)),
            shaped((tokens, width)),
            shaped((2, 4, padded, width)),
            shaped((4,) + wo_part.shape),
            shaped((4, shard, 128)),
            shaped((2,) + cx_shape),
            shaped((16, width), F32),
        ],
        scratch_shapes=[
            pltpu.VMEM((2, 4, padded, width), BF16),
            pltpu.VMEM((2, padded, width), BF16),
            pltpu.VMEM((shard, 128), BF16),
            pltpu.VMEM(cx_shape, BF16),
            pltpu.VMEM((2, tokens // 2, 256), F32),
            pltpu.VMEM((tokens, width), F32),
            pltpu.VMEM((2, tokens, width), F32),
            pltpu.VMEM((n, tokens, PACK), BF16),
            dma(2, n - 1),
            dma(2, n - 1),
        ]
        + [dma(4)] * 10
        + [dma(1), dma(1), dma(10)],
        compiler_params=params(collective_id=1, has_side_effects=True),
        cost_estimate=cost(2e9, 5e7),
        name="front",
    )(wq, wk, wv, wo_part, wr, gains, x, table, routes, cot)


def attend_kernel(
    length,
    n,
    number,
    capp,
    ends_ref,
    q_ref,
    pack_ref,
    cxs_ref,
    wo_hbm,
    wr_ref,
    x_hbm,
    gain_ref,
    lse_ref,
    full_ref,
    middle_ref,
    h_ref,
    kept_ref,
    xs_ref,
    gs_ref,
    gates_ref,
    rest_ref,
    diag_ref,
    keys,
    values_t,
    acc,
    result,
    arrived,
    hs,
    wo_ref,
    x_ref,
    cx,
    rows_out,
    grads_out,
    gates_out,
    near_send,
    near_recv,
    core_send,
    core_recv,
    exch_send,
    exch_recv,
    hop_send,
    hop_recv,
    cross_send,
    cross_recv,
    cx_send,
    cx_recv,
    fwd_send,
    fwd_recv,
    local_sems,
    own_sems,
    load_sems,
    store_sems,
):
    block = pl.program_id(0)
    last = pl.num_programs(0) - 1
    tokens, width = x_ref.shape
    split = tokens // 2
    per = BLK // split
    per_half = length // BLK // 2
    ctx, fsdp = lax.axis_index("ctx"), lax.axis_index("fsdp")
    first = (fsdp * 2 + lax.rem(ctx, 2)) * number
    core, group = neighbours()
    near = group[1]
    copies = [pltpu.make_async_copy(wo_hbm, wo_ref, local_sems.at[0]), pltpu.make_async_copy(x_hbm, x_ref, local_sems.at[1])]

    def to_near():
        return send(cxs_ref.at[0], rest_ref.at[0], near_send.at[0], near_recv.at[0], near)

    def to_core(i):
        src = cxs_ref.at[i] if i < 2 else rest_ref.at[0]
        return send(src, rest_ref.at[1 + i], core_send.at[i], core_recv.at[i], core)

    def cx_cross():
        return send(rest_ref.at[0], diag_ref.at[0], cx_send.at[0], cx_recv.at[0], group[0])

    def cx_core():
        return send(diag_ref.at[0], diag_ref.at[1], cx_send.at[1], cx_recv.at[1], core)

    def to_home(c, late):
        at = pl.ds(pl.multiple_of(late * split, split), split)
        d = lax.rem(c - ctx + n - 1, n)
        return send(result.at[c, at], arrived.at[ctx, at], exch_send.at[late, d], exch_recv.at[late, d], {"ctx": c})

    def from_device(c, late):
        at = pl.ds(late * split, split)
        d = lax.rem(ctx - c + n - 1, n)
        return send(result.at[c, at], arrived.at[c, at], exch_send.at[late, d], exch_recv.at[late, d], {"ctx": c})

    def own_rows(late):
        at = pl.ds(pl.multiple_of(late * split, split), split)
        return pltpu.make_async_copy(result.at[ctx, at], arrived.at[ctx, at], own_sems.at[late])

    @pl.when(block == 0)
    def _():
        for copy in copies:
            copy.start()
        greet([core, group[0]] + [{"ctx": c} for c in others(n)])
        to_near().start()
        for i in range(2):
            to_core(i).start()

    attn_forward_kernel(length, ends_ref, q_ref, pack_ref, None, lse_ref, full_ref, keys, values_t, acc)
    late = block // per_half
    folded = fold_heads(jnp.transpose(full_ref[0])).astype(BF16)
    for k in range(per):
        c = lax.rem(block, per_half) * per + k
        result[c, pl.ds(pl.multiple_of(late * split, split), split), :] = folded[k * split : (k + 1) * split]

        @pl.when(c == ctx)
        def _():
            own_rows(late).start()

        @pl.when(c != ctx)
        def _():
            to_home(c, late).start()

    @pl.when(block == last - 1)
    def _():
        to_near().wait_recv()
        to_core(2).start()
        cx_cross().start()

    halves = [pl.ds(k * split, split) for k in range(2)]

    def hop(i, k):
        return send(hs.at[0, halves[k]], hs.at[(1, 2, 4)[i], halves[k]], hop_send.at[i, k], hop_recv.at[i, k], (group[0], group[1], core)[i])

    def form(k):
        own_rows(k).wait()
        for d in range(1, n):
            from_device(lax.rem(ctx + d, n), k).wait_recv()
        at = slice(k * split, (k + 1) * split)
        total = None
        for c in range(n):
            part = dot(arrived[c, at, :], wo_ref[c])
            total = part if total is None else total + part
        middle = x_ref[at, :] + RESIDUAL * total
        middle_ref[at, :] = middle
        normed, _ = norm_parts(middle)
        h = (normed * gain_ref[1:2]).astype(BF16)
        h_ref[at, :] = h
        hs[0, at, :] = h
        for i in range(3):
            hop(i, k).start()

    @pl.when(block == per_half + 1)
    def _():
        for copy in copies:
            copy.wait()
        form(0)

    @pl.when(block == last)
    def _():
        order = (0, 4, 1, 2, 3, 5, 6, 7)

        def load(step):
            refs = (cxs_ref.at[0], cxs_ref.at[1], rest_ref.at[0], diag_ref.at[0], rest_ref.at[1], rest_ref.at[2], rest_ref.at[3], diag_ref.at[1])
            return pltpu.make_async_copy(refs[order[step]], cx.at[step % 2], load_sems.at[step % 2])

        def cross(i):
            return send(hs.at[1 + i, halves[i]], hs.at[3, halves[i]], cross_send.at[i], cross_recv.at[i], group[1 - i])

        def forward(i):
            return send(hs.at[1 + i], hs.at[5 + i], fwd_send.at[i], fwd_recv.at[i], core)

        load(0).start()
        for i in range(3):
            to_core(i).wait_recv()
        load(1).start()
        hop(0, 0).wait_recv()
        cross(0).start()
        form(1)
        keep = pltpu.make_async_copy(arrived, kept_ref, local_sems.at[2])
        keep.start()

        def stores(step):
            b = order[step]
            pairs = ((rows_out, xs_ref), (grads_out, gs_ref), (gates_out, gates_ref))
            return [pltpu.make_async_copy(src.at[step % 2], dst.at[:, b], store_sems.at[step % 2, k]) for k, (src, dst) in enumerate(pairs)]

        def place(step):
            b, slot = order[step], step % 2
            load(step).wait()
            if step >= 2:
                for copy in stores(step - 2):
                    copy.wait()
            h = hs[b]
            logits = jnp.transpose(dot(h, wr_ref[...]))[:EXPERTS, :]
            raw = jnp.exp(logits - jnp.max(logits, 0, keepdims=True))
            router = raw / jnp.sum(raw, 0, keepdims=True)
            slots = cx[slot, tokens:, :tokens].astype(F32)
            hots = one_hot(slots, first, number, capp)
            places = jnp.concatenate(hots, 0).astype(BF16)
            rows = dot(places, h).astype(BF16)
            grads = dot(places, cx[slot, :tokens, :]).astype(BF16)
            for j in range(number):
                at = slice(j * capp, (j + 1) * capp)
                rows_out[slot, j] = rows[at]
                grads_out[slot, j] = grads[at]
                gate = jnp.sum(hots[j] * own_row(router, first + j), 1, keepdims=True)
                gates_out[slot, j] = jnp.broadcast_to(gate, (capp, 128))
            for copy in stores(step):
                copy.start()
            if step + 2 < 8:
                if step + 2 == 4:
                    cx_cross().wait_recv()
                    cx_core().start()
                if step + 2 == 7:
                    cx_core().wait_recv()
                load(step + 2).start()

        place(0)
        for k in range(2):
            hop(2, k).wait_recv()
        place(1)
        hop(1, 0).wait_recv()
        hop(1, 1).wait_recv()
        cross(1).start()
        forward(1).start()
        hop(0, 1).wait_recv()
        forward(0).start()
        place(2)
        place(3)
        for i in range(2):
            cross(i).wait_recv()
        forward(2).start()
        place(4)
        for i in range(3):
            forward(i).wait_recv()
            place(5 + i)
        for step in (6, 7):
            for copy in stores(step):
                copy.wait()
        for k in range(2):
            for d in range(1, n):
                to_home(lax.rem(ctx + d, n), k).wait_send()
        for i in range(2):
            cross(i).wait_send()
        cx_cross().wait_send()
        cx_core().wait_send()
        for i in range(3):
            for k in range(2):
                hop(i, k).wait_send()
            forward(i).wait_send()
            to_core(i).wait_send()
        to_near().wait_send()
        keep.wait()


def attend(ends, packs, cxs, wo, wr, x, gains, length, number, capp):
    n, _, rows, _ = packs.shape
    tokens, width = x.shape
    blocks, per = length // BLK, BLK // rows
    per_half = blocks // 2
    tiles = lambda i: (lax.rem(i, per_half), i // per_half, 0, 0)
    hbm = pl.BlockSpec(memory_space=pl.ANY)
    dma = lambda *k: pltpu.SemaphoreType.DMA(k)
    same = lambda shape: pl.BlockSpec(shape, lambda i: (0,) * len(shape))
    shaped = lambda shape, dtype=BF16: jax.ShapeDtypeStruct(shape, dtype)
    return pl.pallas_call(
        functools.partial(attend_kernel, length, n, number, capp),
        grid=(blocks,),
        in_specs=[
            pl.BlockSpec(memory_space=pltpu.SMEM),
            pl.BlockSpec((per, 1, rows, PACK), tiles),
            same(packs.shape),
            hbm,
            hbm,
            same(wr.shape),
            hbm,
            same(gains.shape),
        ],
        out_specs=[
            pl.BlockSpec((1, 1, 2 * BLK), lambda i: (i, 0, 0)),
            pl.BlockSpec((1, 128, 2 * BLK), lambda i: (i, 0, 0)),
            same((tokens, width)),
            same((tokens, width)),
            hbm,
            hbm,
            hbm,
            hbm,
            hbm,
            hbm,
        ],
        out_shape=[
            shaped((blocks, 1, 2 * BLK), F32),
            shaped((blocks, 128, 2 * BLK), F32),
            shaped((tokens, width), F32),
            shaped((tokens, width)),
            shaped((n, tokens, 128)),
            shaped((number, 8, capp, width)),
            shaped((number, 8, capp, width)),
            shaped((number, 8, capp, 128), F32),
            shaped((4,) + cxs.shape[1:]),
            shaped((2,) + cxs.shape[1:]),
        ],
        scratch_shapes=[
            pltpu.VMEM((length, 128), BF16),
            pltpu.VMEM((128, length), BF16),
            pltpu.VMEM((128, 2 * BLK), F32),
            pltpu.VMEM((n, tokens, 128), BF16),
            pltpu.VMEM((n, tokens, 128), BF16),
            pltpu.VMEM((8, tokens, width), BF16),
            pltpu.VMEM(wo.shape, BF16),
            pltpu.VMEM((tokens, width), F32),
            pltpu.VMEM((2,) + cxs.shape[1:], BF16),
            pltpu.VMEM((2, number, capp, width), BF16),
            pltpu.VMEM((2, number, capp, width), BF16),
            pltpu.VMEM((2, number, capp, 128), F32),
            dma(1),
            dma(1),
            dma(3),
            dma(3),
            dma(2, n - 1),
            dma(2, n - 1),
            dma(3, 2),
            dma(3, 2),
            dma(2),
            dma(2),
            dma(2),
            dma(2),
            dma(3),
            dma(3),
            dma(3),
            dma(2),
            dma(2),
            dma(2, 3),
        ],
        compiler_params=params(collective_id=3, has_side_effects=True),
        cost_estimate=cost(2e10, 7e7),
        name="attend",
    )(ends, packs, packs, cxs, wo, wr, x, gains)


RING = 12
LAG_MIDDLE, LAG_ACROSS, LAG_END = 1, 2, 4
ORDER_X, ORDER_Y, ORDER_CORE = 1, 2, 4


class GroupSum:
    def __init__(self, part, rows, lands, own, sems, load, free, first, core, group):
        self.part, self.rows, self.own, self.load, self.free, self.first = part, rows, own, load, free, first
        self.land, self.land_x, self.land_y = lands
        self.core_send, self.core_recv, self.x_send, self.x_recv, self.y_send, self.y_recv = sems
        self.core, self.far, self.near = core, group[0], group[1]

    def place(self, i):
        return self.land.at[i, pl.ds(0, self.rows)]

    def ready(self, which):
        if not self.first:
            pl.semaphore_wait(self.free.at[which], 1)

    def to_core(self, i):
        return send(self.part.at[4 + i], self.place(i), self.core_send.at[i], self.core_recv.at[i], self.core)

    def to_far(self, k):
        return send(self.place(1 + 2 * k), self.land_x.at[k, pl.ds(0, self.rows)], self.x_send.at[k], self.x_recv.at[k], self.far)

    def to_near(self):
        return send(self.place(2), self.land_y.at[pl.ds(0, self.rows)], self.y_send.at[0], self.y_recv.at[0], self.near)

    def fetch(self, i):
        return pltpu.make_async_copy(self.part.at[i], self.own.at[i % 2, pl.ds(0, self.rows)], self.load.at[i % 2])

    def start(self):
        self.ready(0)
        for i in (1, 3, 2, 0):
            self.to_core(i).start()

    def over_cores(self):
        order = (1, 3, 2, 0)
        if self.own is not None:
            self.fetch(1).start()
        for step, i in enumerate(order):
            if self.own is None:
                mine = self.part[i]
            else:
                self.fetch(i).wait()
                mine = self.own[i % 2, : self.rows]
            self.to_core(i).wait_recv()
            self.land[i, : self.rows] = (self.land[i, : self.rows].astype(F32) + mine.astype(F32)).astype(BF16)
            if self.own is not None and step < 3:
                self.fetch(order[step + 1]).start()
            if i % 2 == 1:
                if step == 0:
                    self.ready(1)
                self.to_far(i // 2).start()

    def over_x(self, between=None):
        for k in (1, 0):
            if k == 0 and between is not None:
                between()
            self.to_far(k).wait_recv()
            both = self.land[2 * k, : self.rows].astype(F32) + self.land_x[k, : self.rows].astype(F32)
            self.land[2 * k, : self.rows] = both.astype(BF16)
            if k == 1:
                self.ready(2)
                self.to_near().start()

    def finish(self):
        self.to_near().wait_recv()
        for i in range(4):
            self.to_core(i).wait_send()
        for k in range(2):
            self.to_far(k).wait_send()
        self.to_near().wait_send()
        return self.land[0, : self.rows].astype(F32) + self.land_y[: self.rows].astype(F32)

    def release(self):
        for which, device in enumerate((self.core, self.far, self.near)):
            pl.semaphore_signal(self.free.at[which], inc=1, device_id=device, device_id_type=MESH)


class LineSum:
    def __init__(self, count, own_ref, other_ref, inbox, across, mine, sems):
        self.count, self.own_ref, self.other_ref = count, own_ref, other_ref
        self.inbox, self.across, self.mine = inbox, across, mine
        self.line_send, self.line_recv, self.mid_send, self.mid_recv, self.side_send, self.side_recv, self.store, self.load = sems
        ctx = lax.axis_index("ctx")
        z = ctx // 2
        self.middle = (z == 1) | (z == 2)
        self.line = {"ctx": jnp.where(z % 2 == 0, ctx + 2, ctx - 2)}
        self.peer = {"ctx": jnp.where(z == 1, ctx + 2, ctx - 2)}
        self.side = {"ctx": flip(ctx, 1)}

    def send_line(self, src, i):
        s = lax.rem(i, RING)
        return send(src, self.inbox.at[s], self.line_send.at[s], self.line_recv.at[s], self.line)

    def send_mid(self, i):
        s = lax.rem(i, RING)
        return send(self.inbox.at[s], self.across.at[s], self.mid_send.at[s], self.mid_recv.at[s], self.peer)

    def send_side(self, src, i):
        return send(src, self.other_ref.at[i], self.side_send.at[lax.rem(i, RING)], self.side_recv.at[i], self.side)

    def keep(self, src, i):
        return pltpu.make_async_copy(src, self.own_ref.at[i], self.store.at[lax.rem(i, RING)])

    def fetch(self, src, i):
        s = lax.rem(i, 4)
        return pltpu.make_async_copy(src, self.mine.at[s], self.load.at[s])

    def drain_middle(self, i):
        src = self.across.at[lax.rem(i, RING)]
        self.send_line(src, i).wait_send()
        self.send_side(src, i).wait_send()
        self.keep(src, i).wait()

    def drain_end(self, i):
        src = self.inbox.at[lax.rem(i, RING)]
        self.send_side(src, i).wait_send()
        self.keep(src, i).wait()

    def tick(self, t, source):
        count = self.count
        fixed = isinstance(t, int)

        def when(condition):
            if fixed:
                return (lambda f: f()) if condition else (lambda f: None)
            return pl.when(condition)

        i32 = (lambda v: jnp.int32(v)) if fixed else (lambda v: v)

        @pl.when(self.middle)
        def _():
            @when((t >= LAG_MIDDLE) & (t < count + LAG_MIDDLE))
            def _():
                i = i32(t - LAG_MIDDLE)

                @when(t >= LAG_ACROSS + 4)
                def _():
                    self.drain_middle(i32(t - LAG_ACROSS - 4))

                s = lax.rem(i, RING)
                self.fetch(self.own_ref.at[i], i).wait()
                self.send_line(self.inbox.at[s], i).wait_recv()
                self.inbox[s] = self.inbox[s] + self.mine[lax.rem(i, 4)]
                self.send_mid(i).start()

            @when(t < count)
            def _():
                self.fetch(source(t), i32(t)).start()

            @when((t >= LAG_ACROSS) & (t < count + LAG_ACROSS))
            def _():
                i = i32(t - LAG_ACROSS)
                s = lax.rem(i, RING)
                self.send_mid(i).wait()
                self.across[s] = self.across[s] + self.inbox[s]
                self.send_line(self.across.at[s], i).start()
                self.send_side(self.across.at[s], i).start()
                self.keep(self.across.at[s], i).start()

        @pl.when(jnp.logical_not(self.middle))
        def _():
            @when(t < count)
            def _():
                @when(t >= LAG_END + 2)
                def _():
                    self.drain_end(i32(t - LAG_END - 2))

                @when(t >= 3)
                def _():
                    self.send_line(self.mine.at[0], i32(t - 3)).wait_send()

                self.send_line(source(t), i32(t)).start()

            @when(t >= LAG_END)
            def _():
                i = i32(t - LAG_END)
                s = lax.rem(i, RING)
                self.send_line(self.inbox.at[s], i).wait_recv()
                self.send_side(self.inbox.at[s], i).start()
                self.keep(self.inbox.at[s], i).start()

    def finish(self):
        count = self.count

        @pl.when(self.middle)
        def _():
            for i in range(max(0, count + LAG_MIDDLE - LAG_ACROSS - 4), count):
                self.drain_middle(jnp.int32(i))

        @pl.when(jnp.logical_not(self.middle))
        def _():
            for i in range(max(0, count - 3), count):
                self.send_line(self.mine.at[0], jnp.int32(i)).wait_send()
            for i in range(max(0, count - LAG_END - 2), count):
                self.drain_end(jnp.int32(i))

        def arrived(i, carry):
            self.send_side(self.mine.at[0], i).wait_recv()
            return carry

        lax.fori_loop(0, count, arrived, 0)


def backward_kernel(
    n,
    length,
    capp,
    ends_ref,
    xs_ref,
    gs_ref,
    gates_ref,
    wg_ref,
    wu_ref,
    wd_ref,
    cxs_ref,
    rest_ref,
    diag_ref,
    full_ref,
    weights_ref,
    packs_hbm,
    table_hbm,
    cot_hbm,
    wo_hbm,
    attn_hbm,
    x_hbm,
    h_attn_hbm,
    h_hbm,
    middle_hbm,
    wr_hbm,
    gains_hbm,
    lse_hbm,
    own_ref,
    other_ref,
    own_rest_ref,
    other_rest_ref,
    pieces_ref,
    outs_ref,
    backs_ref,
    gx_ref,
    yp_ref,
    grad_x_ref,
    mixed_ref,
    inbox,
    across,
    mine,
    land,
    land_x,
    land_y,
    y_land,
    y_land_x,
    y_land_y,
    own_buf,
    late_pieces,
    late_rest,
    rest_inbox,
    rest_across,
    rest_mine,
    ga_in,
    grads_in,
    line_send,
    line_recv,
    mid_send,
    mid_recv,
    side_send,
    side_recv,
    line_store,
    line_load,
    ga_send,
    ga_recv,
    gr_send,
    gr_recv,
    group_sems,
    group_load,
    free,
    local_sems,
    full_sems,
    w_sems,
    load_sems,
    store_sems,
    comb_sems,
    part_sems,
    rest_sems,
):
    tokens, width = h_hbm.shape
    half = length // 2
    rows = tokens // 2
    shard = width // 4
    blocks = length // BLK
    number = xs_ref.shape[0]
    ff = wg_ref.shape[2]
    ctx, fsdp = lax.axis_index("ctx"), lax.axis_index("fsdp")
    side = lax.rem(ctx, 2)
    first = (fsdp * 2 + side) * number
    core, group = neighbours()
    sub = own_ref.shape[1]
    cuts = PIECE // sub
    early = number * 6 * cuts
    line = LineSum(own_ref.shape[0], own_ref, other_ref, inbox, across, mine, (line_send, line_recv, mid_send, mid_recv, side_send, side_recv, line_store, line_load))

    small_line = LineSum(1, own_rest_ref, other_rest_ref, rest_inbox, rest_across, rest_mine, [rest_sems.at[k] for k in range(8)])

    def source(t):
        return pieces_ref.at[t // cuts, pl.ds(pl.multiple_of(lax.rem(t, cuts) * sub, sub), sub)]

    def tick(t):
        line.tick(jnp.int32(t) if isinstance(t, int) else t, source)

    sems = lambda k: [group_sems.at[k, j] for j in range(6)]
    lands = (land, land_x, land_y)
    ext = tokens + EXPERTS
    gx = GroupSum(gx_ref, 2 * ext, lands, None, sems(0), None, free, True, core, group)
    ys = GroupSum(yp_ref, 2 * tokens, (y_land, y_land_x, y_land_y), own_buf, sems(1), group_load, free, True, core, group)

    def strip(r):
        f = fsdp
        if r & ORDER_X:
            f = flip(f, 2)
        if r & ORDER_CORE:
            f = flip(f, 1)
        return 2 * f + (1 - side if r & ORDER_Y else side)

    def experts(wg, wu, wd, xb, gb, gateb, stage, out_acc, back_acc, outb, backb, go, dgate, comb_o, comb_b, gst, yst, slots):
        def loads(e):
            s = lax.rem(e, 2)
            at = side * number + e
            pairs = ((wg_ref.at[at], wg), (wu_ref.at[at], wu), (wd_ref.at[at], wd), (xs_ref.at[e], xb), (gs_ref.at[e], gb), (gates_ref.at[e], gateb))
            return [pltpu.make_async_copy(src, dst.at[s], load_sems.at[s, k]) for k, (src, dst) in enumerate(pairs)]

        def slot_copy(b):
            refs = (cxs_ref.at[0], cxs_ref.at[1], rest_ref.at[0], diag_ref.at[0], rest_ref.at[1], rest_ref.at[2], rest_ref.at[3], diag_ref.at[1])
            return pltpu.make_async_copy(refs[b].at[pl.ds(tokens, EXPERTS), pl.ds(0, tokens)], slots.at[b], part_sems.at[0, b])

        def stores(e):
            pairs = (
                (stage.at[pl.ds(0, 3)], pieces_ref.at[pl.ds(6 * e, 3)]),
                (stage.at[pl.ds(3, 3)], pieces_ref.at[pl.ds(6 * e + 3, 3)]),
                (outb, outs_ref.at[e]),
                (backb, backs_ref.at[e]),
            )
            return [pltpu.make_async_copy(src, dst, store_sems.at[k]) for k, (src, dst) in enumerate(pairs)]

        for copy in loads(jnp.int32(0)):
            copy.start()
        for b in range(8):
            slot_copy(b).start()
        greet([core, group[0]] + [{"ctx": c} for c in others(n)])

        def one(e, carry):
            s = lax.rem(e, 2)

            @pl.when(e + 1 < number)
            def _():
                for copy in loads(e + 1):
                    copy.start()

            for copy in loads(e):
                copy.wait()

            @pl.when(e > 0)
            def _():
                for copy in stores(e - 1)[2:]:
                    copy.wait()

            x = xb[s]
            gate = gateb[s][:, :1]
            go[...] = (gate * (RESIDUAL * gb[s].astype(F32))).astype(BF16)
            part = ff // 2
            for chunk in range(2):
                at = slice(chunk * part, (chunk + 1) * part)
                wgc, wuc, wdc = wg[s, :, at], wu[s, :, at], wd[s, at, :]
                pre_gate = dot(x, wgc)
                pre_up = dot(x, wuc)
                sig = jax.nn.sigmoid(pre_gate)
                hidden = (pre_gate * sig * pre_up).astype(BF16)
                out_part = dot(hidden, wdc)
                grad_hidden = dot(go[...], wdc, NT)
                grad_gate = (grad_hidden * pre_up * sig * (1.0 + pre_gate * (1.0 - sig))).astype(BF16)
                grad_up = (grad_hidden * pre_gate * sig).astype(BF16)
                row_part = dot(grad_gate, wgc, NT) + dot(grad_up, wuc, NT)
                dwg = dot(x, grad_gate, TN).astype(BF16)
                dwu = dot(x, grad_up, TN).astype(BF16)
                dwd = dot(hidden, go[...], TN).astype(BF16)
                for k in range(2):
                    cut = slice(k * PIECE, (k + 1) * PIECE)
                    stage[3 * chunk + k, :, :part] = dwg[cut]
                    stage[3 * chunk + k, :, part:] = dwu[cut]
                    stage[3 * chunk + 2, k * part : (k + 1) * part, :] = dwd[:, cut]
                stores(e)[chunk].start()
                if chunk == 0:
                    out_acc[...] = out_part
                    back_acc[...] = row_part
                    stores(e)[0].wait()
                    tick(2 * e)
                else:
                    out = (out_acc[...] + out_part).astype(BF16).astype(F32)
                    outb[...] = (gate * out).astype(BF16)
                    backb[...] = (back_acc[...] + row_part).astype(BF16)
                    grad = jnp.sum(RESIDUAL * gb[s].astype(F32) * out, 1, keepdims=True)
                    dgate[e] = jnp.broadcast_to(grad, dgate.shape[1:])
            for copy in stores(e)[2:]:
                copy.start()
            stores(e)[1].wait()
            tick(2 * e + 1)
            return carry

        lax.fori_loop(0, number, one, 0)
        for copy in stores(jnp.int32(number - 1))[2:]:
            copy.wait()
        for b in range(8):
            slot_copy(b).wait()

        def which(s):
            k = lax.rem(s, 4)
            i = jnp.where(k == 0, 1, jnp.where(k == 1, 3, jnp.where(k == 2, 2, 0)))
            return jnp.where(s < 4, 4 + i, i), i

        def comb(s):
            k = lax.rem(s, 2)
            at = pl.ds(pl.multiple_of(which(s)[0] * capp, 16), capp)
            return [
                pltpu.make_async_copy(outs_ref.at[:, at], comb_o.at[k], comb_sems.at[0, k]),
                pltpu.make_async_copy(backs_ref.at[:, at], comb_b.at[k], comb_sems.at[1, k]),
            ]

        def put(s):
            k = lax.rem(s, 2)
            r, _ = which(s)
            return [
                pltpu.make_async_copy(gst.at[k], gx_ref.at[r], part_sems.at[1, k]),
                pltpu.make_async_copy(yst.at[k], yp_ref.at[r], part_sems.at[1, 2 + k]),
            ]

        for copy in comb(jnp.int32(0)):
            copy.start()

        def join(s, carry):
            k = lax.rem(s, 2)
            r, i = which(s)

            @pl.when(s + 1 < 8)
            def _():
                for copy in comb(s + 1):
                    copy.start()

            for copy in comb(s):
                copy.wait()

            @pl.when(s >= 2)
            def _():
                put(s - 2)[1].wait()

            hots = one_hot(slots[r].astype(F32), first, number, capp)
            places = jnp.concatenate(hots, 0).astype(BF16)
            y = dot(places, comb_o[k].reshape(number * capp, width), TN).astype(BF16)
            back = dot(places, comb_b[k].reshape(number * capp, width), TN).astype(BF16)
            extra = jnp.zeros((EXPERTS, 2 * tokens), F32)
            for j in range(number):
                grads = dgate[j, pl.ds(pl.multiple_of(r * capp, 16), capp), :][:, :1]
                grad = jnp.sum(hots[j] * grads, 0, keepdims=True)
                high = grad.astype(BF16).astype(F32)
                extra = jnp.where(row_iota(extra.shape) == first + j, jnp.concatenate([high, grad - high], 1), extra)
            for q in range(2):
                yst[k, q * tokens : (q + 1) * tokens, :] = y[:, q * PIECE : (q + 1) * PIECE]
                gst[k, q * ext : q * ext + tokens, :] = back[:, q * PIECE : (q + 1) * PIECE]
            gst[k, tokens:ext, :] = extra.astype(BF16)
            gst[k, ext + tokens :, :] = jnp.zeros((EXPERTS, PIECE), BF16)
            put(s)[1].start()

            @pl.when(s < 4)
            def _():
                put(s)[0].start()
                put(s)[0].wait()
                gx.to_core(i).start()

            @pl.when(s >= 4)
            def _():
                gx.to_core(i).wait_recv()
                land[i, : gx.rows] = (land[i, : gx.rows].astype(F32) + gst[k].astype(F32)).astype(BF16)

            @pl.when((s == 4) | (s == 5))
            def _():
                gx.to_far(s - 4).start()

            @pl.when(lax.rem(s, 2) == 1)
            def _():
                tick(2 * number + s // 2)

            return carry

        lax.fori_loop(0, 8, join, 0)
        for s in range(6, 8):
            put(jnp.int32(s))[1].wait()

    slots_rows = xs_ref.shape[1]
    pl.run_scoped(
        experts,
        pltpu.VMEM((2, width, ff), BF16),
        pltpu.VMEM((2, width, ff), BF16),
        pltpu.VMEM((2, ff, width), BF16),
        pltpu.VMEM((2, slots_rows, width), BF16),
        pltpu.VMEM((2, slots_rows, width), BF16),
        pltpu.VMEM((2, slots_rows, 128), F32),
        pltpu.VMEM((6, PIECE, PIECE), BF16),
        pltpu.VMEM((slots_rows, width), F32),
        pltpu.VMEM((slots_rows, width), F32),
        pltpu.VMEM((slots_rows, width), BF16),
        pltpu.VMEM((slots_rows, width), BF16),
        pltpu.VMEM((slots_rows, width), BF16),
        pltpu.VMEM((number, slots_rows, 128), F32),
        pltpu.VMEM((2, number, capp, width), BF16),
        pltpu.VMEM((2, number, capp, width), BF16),
        pltpu.VMEM((2, 2 * ext, PIECE), BF16),
        pltpu.VMEM((2, 2 * tokens, PIECE), BF16),
        pltpu.VMEM((8, EXPERTS, tokens), BF16),
    )
    at_tick = [2 * number + 4]

    def go_on(k=1):
        for _ in range(k):
            tick(at_tick[0])
            at_tick[0] += 1

    def backward(packs, table, keys, values, keys_t, grad_q, grad_k, grad_v, acc, full_buf, ga, pack_out, wbuf, total, grad_middle, dgain, dwr, col, small, columns, cot, wo, attn, x_in, h_attn, h_ref, middle_ref, wr_ref, gains_ref, lse_ref):
        ws = GroupSum(small, small.shape[1], lands, None, sems(2), None, free, False, core, group)
        cs = GroupSum(columns, PIECE + 16, lands, None, sems(3), None, free, False, core, group)
        copies = [
            pltpu.make_async_copy(src, dst, local_sems.at[4 + k])
            for k, (src, dst) in enumerate(
                (
                    (cot_hbm, cot),
                    (wo_hbm, wo),
                    (attn_hbm, attn),
                    (packs_hbm, packs),
                    (table_hbm, table),
                    (x_hbm, x_in),
                    (h_attn_hbm, h_attn),
                    (h_hbm, h_ref),
                    (middle_hbm, middle_ref),
                    (wr_hbm, wr_ref),
                    (gains_hbm, gains_ref),
                    (lse_hbm, lse_ref),
                )
            )
        ]
        for copy in copies:
            copy.start()
        go_on(2)
        gx.over_x(go_on)
        go_on(2)
        arrived = gx.finish()
        arrived = jnp.concatenate([arrived[:ext], arrived[ext:]], 1)
        gx.release()

        for copy in copies[7:]:
            copy.wait()
        h = h_ref[...]
        gain = gains_ref[1:2]
        extra = arrived[tokens:, :]
        grad_router = extra[:, :tokens] + extra[:, tokens : 2 * tokens]
        grad_router = jnp.transpose(jnp.concatenate([grad_router, jnp.zeros((128 - EXPERTS, tokens), F32)], 0))
        logits = dot(h, wr_ref[...])
        logits = jnp.where(lane_iota(logits.shape) < EXPERTS, logits, MASKED)
        raw = jnp.exp(logits - jnp.max(logits, -1, keepdims=True))
        router = raw / jnp.sum(raw, -1, keepdims=True)
        grad_logits = (router * (grad_router - jnp.sum(router * grad_router, -1, keepdims=True))).astype(BF16)
        go_on()
        grad_h = arrived[:tokens, :] + dot(grad_logits, wr_ref[...], NT)
        normed, scale = norm_parts(middle_ref[...])
        dgain[1:2, :] = jnp.sum(grad_h * normed, 0, keepdims=True)
        for copy in copies[:3]:
            copy.wait()
        grad_mid = cot[...] + norm_back(grad_h * gain, normed, scale)
        grad_middle[...] = grad_mid
        grad_branch = (RESIDUAL * grad_mid).astype(BF16)
        for c in range(n):
            ga[c] = dot(grad_branch, wo[c], NT).astype(BF16)
        ga_exchange = (ga, ga_in, ga_send, ga_recv, local_sems.at[2], n)
        exchange_start(*ga_exchange)
        go_on()
        dwr[...] = dot(grad_logits, h, TN)[:EXPERTS]
        for r in range(8):
            at = strip(r)
            dwo = dot(attn[at], grad_branch, TN).astype(BF16)
            small[r, 0:128, :] = dwo[:, :PIECE]
            small[r, 128:256, :] = dwo[:, PIECE:]
        ws.start()
        ys.start()
        go_on()
        copies[3].wait()
        for hh in range(2):
            for c in range(n):
                kk, vv = pair_keys(packs[c, hh, :, 128:256].astype(F32))
                at = hh * half + c * rows
                keys[at : at + rows, :] = kk.astype(BF16)
                values[at : at + rows, :] = vv.astype(BF16)
                keys_t[:, at : at + rows] = jnp.transpose(kk).astype(BF16)
        grad_k[...] = jnp.zeros_like(grad_k)
        grad_v[...] = jnp.zeros_like(grad_v)
        go_on()
        ws.over_cores()
        ys.over_cores()
        go_on()
        exchange_wait(*ga_exchange)

        per = BLK // rows
        per_half = blocks // 2

        def fetch_full(b):
            return pltpu.make_async_copy(full_ref.at[b], full_buf.at[lax.rem(b, 2)], full_sems.at[lax.rem(b, 2)])

        fetch_full(jnp.int32(0)).start()
        attend_tick = at_tick[0]

        def attend(block, carry):
            late = block // per_half
            c0 = lax.rem(block, per_half) * per
            q2 = jnp.concatenate([packs[c0 + k, late, :, :128] for k in range(per)], 0)
            q2 = stack_heads((q2.astype(F32) * ATTN_SCALE).astype(BF16))
            g2 = stack_heads(jnp.concatenate([ga_in[c0 + k, pl.ds(pl.multiple_of(late * rows, rows), rows), :] for k in range(per)], 0))
            position, start = query_rows(ends_ref, block, length)
            lse = lse_ref[block]
            shift = jnp.where(start > 0, MASKED, 0.0) - lse

            @pl.when(block + 1 < blocks)
            def _():
                fetch_full(block + 1).start()

            fetch_full(block).wait()
            delta = jnp.sum(jnp.transpose(g2.astype(F32)) * full_buf[lax.rem(block, 2)], 0, keepdims=True)
            acc[...] = jnp.zeros_like(acc)

            def body(kb, whole, carry):
                at = pl.multiple_of(kb * BLK, BLK)
                scores = dot(keys[pl.ds(at, BLK), :], q2, NT)
                if whole:
                    probs = jnp.exp(scores + shift)
                else:
                    where = key_position(kb, length)
                    probs = jnp.where((where <= position) & (where >= start), jnp.exp(scores - lse), 0.0)
                grad_probs = dot(values[pl.ds(at, BLK), :], g2, NT)
                grad_scores = (probs * (grad_probs - delta)).astype(BF16)
                acc[...] += dot(keys_t[:, pl.ds(at, BLK)], grad_scores)
                grad_k[pl.ds(at, BLK), :] += dot(grad_scores, q2)
                grad_v[pl.ds(at, BLK), :] += dot(probs.astype(BF16), g2)

                if not whole:

                    @pl.when((kb == block) & ((block == per_half) | (block == per_half + 1)))
                    def _():
                        tick(attend_tick + 2 + 2 * (block - per_half))

                return carry

            block_loop(block, per_half, body, 0)
            grad_q[pl.ds(pl.multiple_of(block * BLK, BLK), BLK), :] = fold_heads(jnp.transpose(acc[...]))

            @pl.when((block == 1) | (block >= 3))
            def _():
                past = block - per_half
                late_tick = jnp.where(past < 2, 3 + 2 * past, 4 + past)
                tick(attend_tick + jnp.where(block < per_half, block // 2, late_tick))

            return carry

        lax.fori_loop(0, blocks, attend, 0)
        at_tick[0] += blocks
        copies[4].wait()
        for c in range(n):
            for hh in range(2):
                at = slice(hh * half + c * rows, hh * half + (c + 1) * rows)
                kk = grad_k[at, :]
                vv = grad_v[at, :]
                kk = kk + pltpu.roll(kk, 64, 1)
                vv = vv + pltpu.roll(vv, 64, 1)
                both = jnp.where(lane_iota(kk.shape) < 64, kk, vv)
                package = jnp.concatenate([grad_q[at, :] * ATTN_SCALE, both], -1)
                pack_out[c, hh * rows : (hh + 1) * rows, :] = turn(package, table[at, :], -1.0).astype(BF16)
        gr_exchange = (pack_out, grads_in, gr_send, gr_recv, local_sems.at[3], n)
        exchange_start(*gr_exchange)

        def fetch_w(c):
            slot = lax.rem(c, 2)
            at = pl.ds(pl.multiple_of(c * 128, 128), 128)
            return [
                pltpu.make_async_copy(weights_ref.at[1 - k, :, :, at], wbuf.at[slot, :, :, pl.ds(128 * k, 128)], w_sems.at[slot, k])
                for k in range(2)
            ]

        for copy in fetch_w(jnp.int32(0)):
            copy.start()
        go_on()
        ws.over_x()
        ys.over_x()
        go_on(2)
        total[...] = jnp.zeros_like(total)
        late_pieces[:256] = ws.finish().astype(BF16)
        ws.release()
        ffn = ys.finish()
        mixed_ref[...] = middle_ref[...] + RESIDUAL * jnp.concatenate([ffn[:tokens], ffn[tokens:]], 1)
        go_on(3)
        exchange_wait(*gr_exchange)
        copies[5].wait()
        copies[6].wait()

        columns_tick = at_tick[0]

        def finish_columns(c, carry):
            @pl.when(c + 1 < n)
            def _():
                for copy in fetch_w(c + 1):
                    copy.start()

            for copy in fetch_w(c):
                copy.wait()
            slot = lax.rem(c, 2)
            g = grads_in[c]
            col[...] = dot(h_attn[...], g, TN).astype(BF16)
            for r in range(8):
                at = pl.ds(pl.multiple_of(strip(r) * 128, 128), 128)
                columns[r, pl.ds(pl.multiple_of(c // 2 * 128, 128), 128), pl.ds(pl.multiple_of(lax.rem(c, 2) * PACK, PACK), PACK)] = col[at, :]
            for f in range(4):
                total[:, f * shard : (f + 1) * shard] += dot(g, wbuf[slot, f, :shard, :], NT)

            @pl.when(lax.rem(c, 4) == 3)
            def _():
                tick(columns_tick + c // 4)

            return carry

        lax.fori_loop(0, n, finish_columns, 0)
        at_tick[0] += n // 4
        normed, scale = norm_parts(x_in[...])
        grad_h = total[...]
        dgain[0:1, :] = jnp.sum(grad_h * normed, 0, keepdims=True)
        grad_x_ref[...] = grad_middle[...] + norm_back(grad_h * gains_ref[0:1], normed, scale)
        for r in range(8):
            at = pl.ds(pl.multiple_of(strip(r) * 128, 128), 128)
            router_rows = jnp.concatenate([dwr[q * 8 : (q + 1) * 8, at] for q in range(EXPERTS // 8)], 1)
            row = row_iota((8, 128))
            gain_rows = jnp.where(row == 0, dgain[0:1, at], jnp.where(row == 1, dgain[1:2, at], 0.0))
            gain_rows = jnp.concatenate([gain_rows, jnp.zeros((8, PIECE - 128), F32)], 1)
            columns[r, PIECE:, :] = jnp.concatenate([router_rows, gain_rows], 0).astype(BF16)
        cs.start()
        go_on()
        cs.over_cores()
        go_on(3)
        cs.over_x(go_on)
        go_on(3)
        summed = cs.finish().astype(BF16)
        late_pieces[256:] = summed[:PIECE]
        late_rest[...] = summed[PIECE:]

    f32, bf = (lambda *shape: pltpu.VMEM(shape, F32)), (lambda *shape: pltpu.VMEM(shape, BF16))
    pl.run_scoped(
        backward,
        bf(*packs_hbm.shape),
        f32(*table_hbm.shape),
        bf(length, 128),
        bf(length, 128),
        bf(128, length),
        f32(length, 128),
        f32(length, 128),
        f32(length, 128),
        f32(128, 2 * BLK),
        f32(2, 128, 2 * BLK),
        bf(n, tokens, 128),
        bf(n, tokens, PACK),
        bf(2, 4, weights_ref.shape[2], PACK),
        f32(tokens, width),
        f32(tokens, width),
        f32(8, width),
        f32(EXPERTS, width),
        bf(width, PACK),
        bf(8, 256, PIECE),
        bf(8, PIECE + 16, PIECE),
        f32(tokens, width),
        bf(*wo_hbm.shape),
        bf(*attn_hbm.shape),
        f32(tokens, width),
        bf(tokens, width),
        bf(tokens, width),
        f32(tokens, width),
        bf(*wr_hbm.shape),
        f32(*gains_hbm.shape),
        f32(*lse_hbm.shape),
    )

    def rest(t, carry):
        tick(t)
        return carry

    lax.fori_loop(at_tick[0], early, rest, 0)

    def late_source(t):
        return late_pieces.at[pl.ds(pl.multiple_of((t - early) * sub, sub), sub)]

    def late(t, carry):
        line.tick(t, late_source)
        return carry

    for t in range(1 + LAG_END):
        small_line.tick(jnp.int32(t), lambda t: late_rest)
        late(jnp.int32(early + t), 0)
    lax.fori_loop(early + 1 + LAG_END, line.count + LAG_END, late, 0)
    line.finish()
    small_line.finish()


def backward_step(ends, xs, gs, gates, w_gate, w_up, w_down, cxs, rest, diag, full, weights, packs, table, cot, wo, attn, x, h_attn, h, middle, wr, gains, lse, n, length, capp):
    tokens, width = x.shape
    number, slots_rows, _ = xs.shape
    hbm, vmem = pl.BlockSpec(memory_space=pl.ANY), pl.BlockSpec(memory_space=pltpu.VMEM)
    smem = pl.BlockSpec(memory_space=pltpu.SMEM)
    dma = lambda *k: pltpu.SemaphoreType.DMA(k)
    shaped = lambda shape, dtype=BF16: jax.ShapeDtypeStruct(shape, dtype)
    sub = PIECE // 2
    piece = (sub, PIECE)
    count = number * 12 + 3
    rest_shape = (16, PIECE)
    land_rows = max(2 * (tokens + EXPERTS), PIECE + 16)
    return pl.pallas_call(
        functools.partial(backward_kernel, n, length, capp),
        in_specs=[smem] + [hbm] * 23,
        out_specs=[hbm] * 9 + [vmem, vmem],
        out_shape=[
            shaped((count,) + piece),
            shaped((count,) + piece),
            shaped((1,) + rest_shape),
            shaped((1,) + rest_shape),
            shaped((number * 6, PIECE, PIECE)),
            shaped(xs.shape),
            shaped(xs.shape),
            shaped((8, 2 * (tokens + EXPERTS), PIECE)),
            shaped((8, 2 * tokens, PIECE)),
            shaped((tokens, width), F32),
            shaped((tokens, width), F32),
        ],
        scratch_shapes=[
            pltpu.VMEM((RING,) + piece, BF16),
            pltpu.VMEM((RING,) + piece, BF16),
            pltpu.VMEM((4,) + piece, BF16),
            pltpu.VMEM((4, land_rows, PIECE), BF16),
            pltpu.VMEM((2, land_rows, PIECE), BF16),
            pltpu.VMEM((land_rows, PIECE), BF16),
            pltpu.VMEM((4, 2 * tokens, PIECE), BF16),
            pltpu.VMEM((2, 2 * tokens, PIECE), BF16),
            pltpu.VMEM((2 * tokens, PIECE), BF16),
            pltpu.VMEM((2, 2 * tokens, PIECE), BF16),
            pltpu.VMEM((768, PIECE), BF16),
            pltpu.VMEM(rest_shape, BF16),
            pltpu.VMEM((RING,) + rest_shape, BF16),
            pltpu.VMEM((RING,) + rest_shape, BF16),
            pltpu.VMEM((4,) + rest_shape, BF16),
            pltpu.VMEM((n, tokens, 128), BF16),
            pltpu.VMEM((n, tokens, PACK), BF16),
            dma(RING),
            dma(RING),
            dma(RING),
            dma(RING),
            dma(RING),
            dma(count),
            dma(RING),
            dma(4),
            dma(n - 1),
            dma(n - 1),
            dma(n - 1),
            dma(n - 1),
            dma(4, 6, 4),
            dma(2),
            pltpu.SemaphoreType.REGULAR((3,)),
            dma(16),
            dma(2),
            dma(2, 2),
            dma(2, 6),
            dma(4),
            dma(2, 2),
            dma(2, 8),
            dma(8, RING),
        ],
        compiler_params=params(63, collective_id=0, has_side_effects=True),
        cost_estimate=cost(6e10, 1e9),
        name="backward_step",
    )(ends, xs, gs, gates, w_gate, w_up, w_down, cxs, rest, diag, full, weights, packs, table, cot, wo, attn, x, h_attn, h, middle, wr, gains, lse)


def local(
    inputs,
    cotangent,
    doc_lengths,
    routes,
    attn_gain,
    ffn_gain,
    w_query,
    key_weight,
    value_weight,
    w_out,
    w_router,
    w_gate,
    w_up,
    w_down,
):
    rows = inputs.shape[2]
    width = inputs.shape[3]
    n = lax.axis_size("ctx")
    fsdp = lax.axis_size("fsdp")
    me, mine = lax.axis_index("ctx"), lax.axis_index("fsdp")
    tokens = 2 * rows
    length = tokens * n
    experts_here = w_gate.shape[0]
    number = experts_here // 2
    capacity = 5 * tokens * TOP // (4 * EXPERTS)
    capp = -(-capacity // 16) * 16
    shard = width // fsdp
    heads = QUERY_HEADS // n
    head_lanes = heads * HEAD_DIMENSION
    copies = n // KEY_VALUE_HEADS
    bits = group_bits(fsdp)

    x = inputs.reshape(tokens, width)
    cot = cotangent.reshape(tokens, width)
    side = me % 2
    base = (side * number).astype(jnp.int32).reshape(1)
    first = (mine * experts_here + side * number).astype(jnp.int32).reshape(1)
    index = jnp.stack([side * number, (1 - side) * number]).astype(jnp.int32)
    ends = doc_lengths
    table = jnp.asarray(rotary_table(length))

    out_part = w_out.reshape(shard // head_lanes, head_lanes, width)
    if head_lanes < 128:
        out_part = jnp.pad(out_part, ((0, 0), (0, 128 - head_lanes), (0, 0)))
    merge = lambda a: a.reshape(number, -1, a.shape[-1])

    if n == 8 and fsdp == 4:
        packs, h_attn, weights, wo, wr, cxs, gains = front(
            w_query,
            key_weight,
            value_weight,
            out_part,
            jnp.transpose(w_router),
            jnp.stack([attn_gain, ffn_gain]),
            x,
            table.reshape(2, n, rows, 256),
            jnp.transpose(routes[0], (0, 2, 1)),
            cot,
            capacity,
            n,
        )
        wo, wr = wo.reshape(n, 128, width), wr.reshape(width, 128)
        packs = packs.reshape(n, 2, rows, PACK)
        lse, full, middle, h_ffn, attn, xs, gs, gates, cx_rest, diag = attend(ends, packs, cxs, wo, wr, x, gains, length, number, capp)
        own, other, own_rest, other_rest, _, _, _, _, _, grad_x, mixed = backward_step(
            ends,
            merge(xs),
            merge(gs),
            merge(gates),
            w_gate,
            w_up,
            w_down,
            cxs,
            cx_rest,
            diag,
            full,
            weights,
            packs,
            table,
            cot,
            wo,
            attn,
            x,
            h_attn,
            h_ffn,
            middle,
            wr,
            gains,
            lse,
            n,
            length,
            capp,
        )
        shapes = [w.shape for w in (w_gate, w_up, w_down)]
        outs = tail(index, own, other, own_rest, other_rest, mixed, grad_x, shapes, shard)
        return (
            outs[3].reshape(inputs.shape),
            outs[4].reshape(inputs.shape),
            outs[10].reshape(shard),
            outs[11].reshape(shard),
            outs[5],
            outs[6],
            outs[7],
            outs[8],
            jnp.transpose(outs[9]),
            outs[0],
            outs[1],
            outs[2],
        )

    else:
        own_table = lax.dynamic_slice_in_dim(table.reshape(2, n, rows, 256), me, 1, 1).reshape(tokens, 256)
        query_part = w_query.reshape(shard, n, head_lanes)
        if head_lanes < 128:
            query_part = jnp.pad(query_part, ((0, 0), (0, 0), (0, 128 - head_lanes)))
        key_part = jnp.repeat(key_weight.reshape(shard, KEY_VALUE_HEADS, HEAD_DIMENSION), copies, 1)
        value_part = jnp.repeat(value_weight.reshape(shard, KEY_VALUE_HEADS, HEAD_DIMENSION), copies, 1)
        packed = jnp.concatenate([query_part, key_part, value_part], -1).reshape(shard, n * PACK)
        padding = 2 * 16 * (shard // 32 + 1) - shard
        gains = jnp.pad(jnp.stack([attn_gain, ffn_gain]), ((0, padding - 2), (0, n * PACK - shard)))
        packed = jnp.concatenate([packed, gains], 0)
        router_part = jnp.pad(w_router, ((0, 0), (0, 128 - EXPERTS)))
        weights = lax.all_gather(packed, "fsdp", axis=0)
        gain_one = weights[:, shard, :shard].reshape(1, width).astype(F32)
        gain_two = weights[:, shard + 1, :shard].reshape(1, width).astype(F32)
        wo = lax.all_gather(out_part, "fsdp", axis=0, tiled=True)
        wr = lax.all_gather(router_part, "fsdp", axis=0, tiled=True)
        cxs = group_gather(prep(jnp.transpose(routes[0], (0, 2, 1)), cot, capacity), bits)
        packs, h_attn = qkv(x, gain_one, weights, own_table, shard, n)
        packs = lax.all_to_all(packs, "ctx", split_axis=0, concat_axis=0, tiled=True).reshape(n, 2, rows, PACK)
        attn, lse, full = attn_forward(ends, packs, length)
        attn = lax.all_to_all(attn.reshape(n, tokens, 128), "ctx", split_axis=0, concat_axis=0, tiled=True)
        middle, h_ffn = middle_step(attn, wo, x, gain_two)
        xs, gs, gates = gather_rows(first, group_gather(h_ffn, bits), cxs, jnp.transpose(wr), number, capp)
        slots = cxs[:, tokens:]
    xs, gs, gates = merge(xs), merge(gs), merge(gates)
    pieces, outs, back, dgates = expert_step(base, xs, gs, gates, w_gate, w_up, w_down)
    y_part, gx_part = combine(first, slots, outs, back, dgates, tokens, capp)
    pieces = pieces.reshape(number * 6, PIECE, PIECE)
    gx = group_reduce(gx_part, bits)
    grad_middle, dwo, grad_attn, dwr, dgain_two = home_step(gx, h_ffn, middle, cot, wr, wo, gain_two, attn)
    grad_attn = lax.all_to_all(grad_attn, "ctx", split_axis=0, concat_axis=0, tiled=True).reshape(n, 2, rows, 128)
    grads = attn_backward(ends, packs, grad_attn, lse, full, table, length)
    grads = lax.all_to_all(grads.reshape(n, tokens, PACK), "ctx", split_axis=0, concat_axis=0, tiled=True)
    dw, grad_x, dgain_one = final_step(grads, weights, h_attn, x, gain_one, grad_middle, shard)
    mixed = middle + RESIDUAL * group_reduce(y_part, bits).astype(F32)
    own = line_sum(pieces.reshape(-1, PIECE // 2, PIECE), n)
    other = swap(own, "ctx", 1)
    scatter = lambda a: lax.psum(lax.psum_scatter(a, "fsdp", scatter_dimension=0, tiled=True), "ctx").astype(F32)
    dwo = scatter(dwo)[:, :head_lanes, :].reshape(shard, width)
    small = jnp.concatenate([dwr[:, :EXPERTS], dgain_two.reshape(width, 1).astype(BF16)], 1)
    small = scatter(jnp.pad(small, ((0, 0), (0, 127 - EXPERTS))))
    dwr, dgain_two = small[:, :EXPERTS], small[:, EXPERTS]
    dw = scatter(dw).reshape(shard, n, PACK)
    dgain_one = scatter(dgain_one.reshape(width).astype(BF16))

    outs = widen(index, own, other, [w.shape for w in (w_gate, w_up, w_down)])
    fold = lambda a: a.reshape(shard, KEY_VALUE_HEADS, copies, HEAD_DIMENSION).sum(2).reshape(shard, -1)
    return (
        mixed.reshape(inputs.shape),
        grad_x.reshape(inputs.shape),
        dgain_one,
        dgain_two,
        dw[:, :, :head_lanes].reshape(shard, -1),
        fold(dw[:, :, 128:192]),
        fold(dw[:, :, 192:256]),
        dwo,
        dwr,
        outs[0],
        outs[1],
        outs[2],
    )


def solution(mesh):
    tokens = P("fsdp", None, "ctx", None)
    one, two, three = P("fsdp"), P("fsdp", None), P("fsdp", None, None)
    return jax.shard_map(
        local,
        mesh=mesh,
        in_specs=(tokens, tokens, two, tokens, one, one, two, two, two, two, two, three, three, three),
        out_specs=(tokens, tokens, one, one, two, two, two, two, two, three, three, three),
        check_vma=False,
    )
```
